32 devices in a mesh: dp: 16 (over z, y, core), tp: 2 (over x).
Axes of the slice: x: 2, y: 2, z: 4, core: 2. Of those that a mesh axis runs over, the one named last changes fastest.
Arguments:
- tokens: bfloat16 [2, 8192, 512], P(None, ('dp', 'tp')), may hold values from -6 to 6
- segment_ids: int32 [2, 8192], P(None, ('dp', 'tp')), may hold values from 0 to 95, as said below
- norm_gains: float32 [5, 512], replicated, may hold values from 0.25 to 1.75
- norm_biases: float32 [5, 512], replicated, may hold values from -2 to 2
- w_qkv: bfloat16 [2, 3, 512, 512], P(None, None, 'dp', 'tp'), may hold values from -0.25 to 0.25
- w_attn_out: bfloat16 [2, 512, 512], P(None, 'tp', 'dp'), may hold values from -3 to 3
- w_up: bfloat16 [2, 512, 2048], P(None, 'dp', 'tp'), may hold values from -0.25 to 0.25
- w_down: bfloat16 [2, 2048, 512], P(None, 'tp', 'dp'), may hold values from -0.125 to 0.125
- w_vq_in: float32 [512, 32], replicated, may hold values from -0.25 to 0.25
- w_vq_out: float32 [32, 512], replicated, may hold values from -18 to 18
- codebook: float32 [8192, 32], replicated, may hold values from -6 to 6
- cotangent: float32 [2, 8192, 512], P(None, ('dp', 'tp')), may hold values from -6 to 6
Outputs:
- decoded: float32 [2, 8192, 512], P(None, ('dp', 'tp'))
- grad_tokens: float32 [2, 8192, 512], P(None, ('dp', 'tp'))
- grad_gains: float32 [5, 512], replicated
- grad_biases: float32 [3, 512], replicated
- grad_decoder_biases: float32 [2, 512], replicated
- grad_qkv: float32 [2, 3, 512, 512], P(None, None, 'dp', 'tp')
- grad_attn_out: float32 [2, 512, 512], P(None, 'tp', 'dp')
- grad_up: float32 [2, 512, 2048], P(None, 'dp', 'tp')
- grad_down: float32 [2, 2048, 512], P(None, 'tp', 'dp')
- grad_vq_in: float32 [512, 32], replicated
- grad_vq_out: float32 [32, 512], replicated
- grad_codebook: float32 [8192, 32], replicated
The draws below stay inside these ranges and needn't reach their ends.
Inputs may be any that keep to these rules, and one draw needn't show every extreme that they name: `segment_ids`: in each micro-batch the rows form aligned groups of 512. Each group holds three sequences in order: the first ends within the group's first 256 rows, the second starts there and ends within the group's last 256 rows, the third takes the rest. Each sequence's tokens share one id, and no id appears in two groups.
All inputs are finite; a program needn't handle non-finite values.
Results may differ from the reference program's by a relative error of at most 0.018.
Values may be sent and summed in bfloat16 or wider, within the bound.
No kernel may reach another device: no remote copies, remote signals or barrier semaphores. Data moves between devices by JAX's collectives and lax.ppermute only.
A program may use at most 256 MiB of HBM per device.

```python
import jax
import jax.numpy as jnp
from jax import lax

D = 512
HEADS = 8
HEAD_DIM = 64
FF = 2048
CODES = 8192
CODE_DIM = 32
ROWS = 256
MICRO = 2
GROUP = 512
TOK_MB = 8192
N_TP = 2


def draw_segment_ids(key, part):
    key = jax.random.fold_in(key, 7)
    first_key, second_key = jax.random.split(key)
    group_count = MICRO * (TOK_MB // GROUP)
    first_end = jax.random.randint(first_key, (group_count, 1), 1, ROWS)
    second_end = GROUP - jax.random.randint(second_key, (group_count, 1), 1, ROWS)
    position = jnp.arange(GROUP, dtype=jnp.int32)[None, :]
    segment = (position >= first_end).astype(jnp.int32) + (position >= second_end).astype(jnp.int32)
    base_id = 3 * jnp.arange(group_count, dtype=jnp.int32)[:, None]
    return (segment + base_id).reshape(MICRO, TOK_MB)


def block_levels(rng, extent, pieces, least, largest):
    gain, own = 1.0, jax.random.fold_in(rng, 6)
    for dim, blocks in pieces:
        steps = jnp.exp(jax.random.uniform(jax.random.fold_in(own, dim), (blocks,), jnp.float32, least / len(pieces), largest / len(pieces)))
        gain = gain * jnp.repeat(steps, extent[dim] // blocks).reshape([-1 if axis == dim else 1 for axis in range(len(extent))])
    return gain


def bell_draw(stream_key, dims, width, most, cuts=(), held_as=jnp.bfloat16):
    entries = width * jax.random.normal(stream_key, dims, jnp.float32)
    if cuts:
        entries = entries * block_levels(stream_key, dims, cuts, -0.22, 0.18)
    return jnp.clip(entries, -most, most).astype(held_as)


def setup_inputs(seed: int = 0) -> dict:
    keys = jax.random.split(jax.random.key(seed), 13)
    tokens = bell_draw(keys[0], (MICRO, TOK_MB, D), 1.0, 6.0, ((1, 32),))
    segment_ids = draw_segment_ids(jax.random.fold_in(keys[12], 71), 0)
    norm_gains = jnp.clip(1.0 + 0.15 * jax.random.normal(keys[2], (5, D), jnp.float32), 0.25, 1.75)
    norm_biases = bell_draw(keys[3], (5, D), 0.3, 2.0, (), jnp.float32)
    w_qkv = bell_draw(keys[4], (2, 3, D, D), D ** -0.5, 0.25, ((2, 16), (3, 2)))
    w_attn_out = bell_draw(keys[5], (2, D, D), (max(1, 4 * D // (ROWS * N_TP))) ** -0.5, 3.0, ((1, 2), (2, 16)))
    w_up = bell_draw(keys[6], (2, D, FF), D ** -0.5, 0.25, ((1, 16), (2, 2)))
    w_down = bell_draw(keys[7], (2, FF, D), FF ** -0.5, 0.125, ((1, 2), (2, 16)))
    w_vq_in = bell_draw(keys[8], (D, CODE_DIM), D ** -0.5, 0.25, (), jnp.float32)
    w_vq_out = bell_draw(keys[9], (CODE_DIM, D), 3.0, 18.0, (), jnp.float32)
    codebook = bell_draw(keys[10], (CODES, CODE_DIM), 1.0, 6.0, (), jnp.float32)
    cotangent = bell_draw(keys[11], (MICRO, TOK_MB, D), 1.0, 6.0, ((1, 32),), jnp.float32)
    return dict(tokens=tokens, segment_ids=segment_ids, norm_gains=norm_gains, norm_biases=norm_biases, w_qkv=w_qkv, w_attn_out=w_attn_out, w_up=w_up, w_down=w_down, w_vq_in=w_vq_in, w_vq_out=w_vq_out, codebook=codebook, cotangent=cotangent)


@jax.custom_vjp
def low(v):
    return lax.optimization_barrier(v.astype(jnp.bfloat16)).astype(jnp.float32)

@jax.custom_vjp
def low_back(v):
    return v

def low_keep(v):
    return (low(v), None)

def low_pass(kept, grad):
    return (grad,)

def back_keep(v):
    return (v, None)

def back_low(kept, grad):
    return (low(grad),)
low.defvjp(low_keep, low_pass)
low_back.defvjp(back_keep, back_low)
highest = lax.Precision.HIGHEST
ln_eps = 1e-05
norm_eps = 1e-06
temper = 10.0
commit_weight = 64.0
gelu_coef = 0.7978845608028654
masked_score = -1e+30

def matmul(former, latter):
    return jnp.dot(former, latter, precision=highest, preferred_element_type=jnp.float32)

def layer_norm(values, norm_gain, norm_bias):
    centred = values - lax.optimization_barrier(jnp.mean(values, axis=-1, keepdims=True))
    spread = lax.optimization_barrier(jnp.mean(centred * centred, axis=-1, keepdims=True))
    return centred * lax.rsqrt(spread + ln_eps) * norm_gain + norm_bias

def gelu_tanh(values):
    return 0.5 * values * (1.0 + jnp.tanh(gelu_coef * (values + 0.044715 * values * values * values)))

def normalize(values):
    return values * lax.rsqrt(lax.optimization_barrier(jnp.sum(values * values, axis=-1, keepdims=True)) + norm_eps)

def quantize(in_rows, norm_gain, norm_bias, in_w, out_w, code_w):
    latent = normalize(matmul(layer_norm(in_rows, norm_gain, norm_bias), in_w))
    code_rows = normalize(code_w)
    logits = matmul(latent, code_rows.T) * temper
    row_max = lax.optimization_barrier(jnp.max(logits, axis=-1, keepdims=True))
    numerator = jnp.exp(logits - row_max)
    assign = numerator / lax.optimization_barrier(jnp.sum(numerator, axis=-1, keepdims=True))
    soft_code = matmul(assign, code_rows)
    offset = latent - soft_code
    vq_loss = commit_weight * 1.25 * jnp.sum(offset * offset)
    return (matmul(soft_code, out_w), vq_loss)

def block(resid, seg_rows, gains, biases, qkv_w, attn_w, up_w, down_w):
    normed = low(layer_norm(resid, gains[0], biases[0]))
    heads_in = [low_back(low(matmul(normed, qkv_w[index]))).reshape(GROUP, HEADS, HEAD_DIM).transpose(1, 0, 2) for index in range(3)]
    raw_scores = low_back(jnp.einsum('hqd,hkd->hqk', heads_in[0], heads_in[1], precision=highest))
    scores = raw_scores * HEAD_DIM ** (-0.5)
    scores = jnp.where((seg_rows[:, None] == seg_rows[None, :])[None], scores, masked_score)
    row_max = lax.optimization_barrier(jnp.max(scores, axis=-1, keepdims=True))
    numerator = jnp.exp(scores - row_max)
    prob_low = low(numerator / lax.optimization_barrier(jnp.sum(numerator, axis=-1, keepdims=True)))
    attended = jnp.einsum('hqk,hkd->hqd', prob_low, heads_in[2], precision=highest)
    attn_rows = low_back(low(attended.transpose(1, 0, 2).reshape(GROUP, D)))
    middle = resid + low_back(matmul(attn_rows, attn_w))
    normed_mid = low(layer_norm(middle, gains[1], biases[1]))
    hidden_pre = low_back(matmul(normed_mid, up_w))
    hidden = low(gelu_tanh(hidden_pre))
    return middle + low_back(matmul(hidden, down_w))

def forward(resid, seg_ids, gains, biases, qkv_w, attn_w, up_w, down_w, in_w, out_w, code_w):
    group_count = MICRO * (TOK_MB // GROUP)
    resid_groups = resid.reshape(group_count, GROUP, D)
    seg_groups = seg_ids.reshape(group_count, GROUP)

    def one_group(group_in):
        encoded = block(group_in[0], group_in[1], gains[0:2], biases[0:2], qkv_w[0], attn_w[0], up_w[0], down_w[0])
        decoder_in, vq_loss = quantize(encoded, gains[2], biases[2], in_w, out_w, code_w)
        decoded = block(decoder_in, group_in[1], gains[3:5], biases[3:5], qkv_w[1], attn_w[1], up_w[1], down_w[1])
        return (decoded, vq_loss)
    decoded, losses = lax.map(jax.checkpoint(one_group), (resid_groups, seg_groups))
    return (decoded.reshape(MICRO, TOK_MB, D), jnp.sum(losses))

def reference(tokens, segment_ids, norm_gains, norm_biases, w_qkv, w_attn_out, w_up, w_down, w_vq_in, w_vq_out, codebook, cotangent):

    def objective(resid, gains, biases, qkv_w, attn_w, up_w, down_w, in_w, out_w, code_w):
        return forward(resid, segment_ids, gains, biases, qkv_w, attn_w, up_w, down_w, in_w, out_w, code_w)
    (decoded, _), pullback = jax.vjp(objective, tokens.astype(jnp.float32), norm_gains.astype(jnp.float32), norm_biases.astype(jnp.float32), w_qkv.astype(jnp.float32), w_attn_out.astype(jnp.float32), w_up.astype(jnp.float32), w_down.astype(jnp.float32), w_vq_in.astype(jnp.float32), w_vq_out.astype(jnp.float32), codebook.astype(jnp.float32))
    grads = pullback((cotangent.astype(jnp.float32), jnp.ones((), jnp.float32)))
    return (decoded, grads[0], grads[1], grads[2][0:3], grads[2][3:5], grads[3], grads[4], grads[5], grads[6], grads[7], grads[8], grads[9])
```

```python
import functools

import jax
import jax.numpy as jnp
from jax import lax
from jax.experimental import pallas as pl
from jax.experimental.pallas import tpu as pltpu
from jax.sharding import PartitionSpec as P

HEAD_DIM = 64
MICRO = 2
bf16 = jnp.bfloat16
f32 = jnp.float32
highest = lax.Precision.HIGHEST
ln_eps = 1e-05
norm_eps = 1e-06
temper = 10.0
commit_weight = 64.0
gelu_coef = 0.7978845608028654
masked_score = -1e30
log2e = 1.4426950408889634
vmem_cap = 60 * 1024 * 1024


PLANE = ((0, 0), (0, 1), (1, 0), (1, 1))


def exchange(values, dp_xor, tp_xor, n_dp):
    pairs = [
        (d * 2 + t, (d ^ dp_xor) * 2 + (t ^ tp_xor)) for d in range(n_dp) for t in range(2)
    ]
    return lax.ppermute(values, ("dp", "tp"), pairs)


def gather_blocks(shard, n_dp):
    lines = [shard] + [exchange(shard, 4 * k, 0, n_dp) for k in range(1, 4)]
    own = jnp.stack(lines)
    quads = [own] + [exchange(own, 2 * y, x, n_dp) for y, x in PLANE[1:]]
    return quads + [exchange(quad, 1, 0, n_dp) for quad in quads]


def scatter_blocks(blocks, n_dp):
    near = [exchange(block, 1, 0, n_dp) for block in blocks[4:]]
    halves = [a.astype(f32) + b.astype(f32) for a, b in zip(blocks[:4], near)]
    total = halves[0]
    for (y, x), half in zip(PLANE[1:], halves[1:]):
        total = total + exchange(half.astype(bf16), 2 * y, x, n_dp).astype(f32)
    low = total.astype(bf16)
    result = total[0]
    for k in range(1, 4):
        result = result + exchange(low[k], 4 * k, 0, n_dp).astype(f32)
    return result


def sum_everywhere(values, n_dp):
    total = values
    for k in range(1, 4):
        total = total + exchange(values, 4 * k, 0, n_dp)
    plane = total
    for y, x in PLANE[1:]:
        plane = plane + exchange(total, 2 * y, x, n_dp)
    return plane + exchange(plane, 1, 0, n_dp)


def block_places():
    for core in range(2):
        for index, (y, x) in enumerate(PLANE):
            for k in range(4):
                yield core * 4 + index, k, k * 4 + y * 2 + core, x


def dot(a, b):
    return jnp.dot(a, b, preferred_element_type=f32)


def dot_nt(a, b, precision=None):
    return lax.dot_general(
        a, b, (((1,), (1,)), ((), ())), preferred_element_type=f32, precision=precision
    )


def dot_full(a, b):
    return jnp.dot(a, b, preferred_element_type=f32, precision=highest)


def ln_parts(x):
    centred = x - jnp.mean(x, axis=-1, keepdims=True)
    inv = lax.rsqrt(jnp.mean(centred * centred, axis=-1, keepdims=True) + ln_eps)
    return centred * inv, inv


def ln_back(grad, xhat, inv, gain):
    scaled = grad * gain
    return inv * (
        scaled
        - jnp.mean(scaled, axis=-1, keepdims=True)
        - xhat * jnp.mean(scaled * xhat, axis=-1, keepdims=True)
    )


def split2(x):
    hi = x.astype(bf16)
    return hi, (x - hi.astype(f32)).astype(bf16)


def split3(x):
    hi, _ = split2(x)
    rest = x - hi.astype(f32)
    mid = rest.astype(bf16)
    return hi, mid, (rest - mid.astype(f32)).astype(bf16)


def weight_copies(ids_ref, quad_refs, w_ref, sems):
    copies = []
    for slot, (which, k, dp_xor, tp_xor) in enumerate(block_places()):
        row = pl.multiple_of((ids_ref[0] ^ dp_xor) * 32, 32)
        copies.append(
            pltpu.make_async_copy(
                quad_refs[which].at[k],
                w_ref.at[ids_ref[1] ^ tp_xor, pl.ds(row, 32), :],
                sems.at[slot],
            )
        )
    return copies


def grad_copies(ids_ref, g_ref, quad_refs, sems):
    copies = []
    for slot, (which, k, dp_xor, tp_xor) in enumerate(block_places()):
        row = pl.multiple_of((ids_ref[0] ^ dp_xor) * 32, 32)
        copies.append(
            pltpu.make_async_copy(
                g_ref.at[ids_ref[1] ^ tp_xor, pl.ds(row, 32), :],
                quad_refs[which].at[k],
                sems.at[slot],
            )
        )
    return copies


def head_rows(ref, pair, which):
    own = ref[pl.ds(pl.multiple_of(pair * 128 + which * HEAD_DIM, HEAD_DIM), HEAD_DIM), :]
    zero = jnp.zeros_like(own)
    return jnp.concatenate([own, zero] if which == 0 else [zero, own], axis=0)


def attn_fwd_kernel(ids, x, segc, segr, gain, bias, *refs):
    quads, refs = refs[:8], refs[8:]
    x1, qs, k, v, o, qst, kt, ot, lse, w_out = refs[:10]
    w, h, vt, mask, sems, out_sem = refs[10:]
    copies = weight_copies(ids, quads, w, sems)
    for copy in copies:
        copy.start()
    xf = x[...].astype(f32)
    h[...] = (ln_parts(xf)[0] * gain[...] + bias[...]).astype(bf16)
    mask[...] = jnp.where(segc[...] == segr[...], 0.0, masked_score)
    for copy in copies:
        copy.wait()
    keep = pltpu.make_async_copy(w, w_out, out_sem)
    keep.start()
    for t in range(2):
        cols = pl.ds(t * 256, 256)
        qs[:, cols] = (dot(h[...], w[t, :, 0:256]).astype(bf16) * HEAD_DIM ** (-0.5)).astype(bf16)
        k[:, cols] = dot(h[...], w[t, :, 256:512]).astype(bf16)
        v[:, cols] = dot(h[...], w[t, :, 512:768]).astype(bf16)
    qst[...] = qs[...].T
    kt[...] = k[...].T
    vt[...] = v[...].T

    def one_pair(pair, _):
        lanes = pl.ds(pl.multiple_of(pair * 128, 128), 128)
        k_pair = k[:, lanes]
        for which in range(2):
            scores = dot(k_pair, head_rows(qst, pair, which)) + mask[...]
            top = jnp.max(scores, axis=0, keepdims=True)
            numer = jnp.exp(scores - top).astype(bf16)
            rows = pl.ds(pl.multiple_of(pair * 128 + which * HEAD_DIM, HEAD_DIM), HEAD_DIM)
            left = jnp.concatenate([vt[rows, :], jnp.ones((16, 512), bf16)], axis=0)
            both = dot(left, numer)
            total = both[HEAD_DIM : HEAD_DIM + 1, :]
            ot[rows, :] = (both[:HEAD_DIM, :] / total).astype(bf16)
            lse[pl.ds(pair * 2 + which, 1), :] = top + jnp.log(total)
        return 0

    lax.fori_loop(0, 4, one_pair, 0)
    o[...] = ot[...].T
    acc = xf
    for t in range(2):
        acc = acc + dot_nt(o[:, t * 256 : (t + 1) * 256], w[t, :, 768:1024])
    x1[...] = acc
    keep.wait()


def gelu_parts(u):
    square = u * u
    tanh = jnp.tanh(gelu_coef * u * (1.0 + 0.044715 * square))
    return 0.5 * u * (1.0 + tanh), tanh, square


def mlp_fwd_kernel(ids, x1, gain, bias, *refs):
    quads, refs = refs[:8], refs[8:]
    y, w_out = refs[:2]
    w, h2, sems, out_sem = refs[2:]
    copies = weight_copies(ids, quads, w, sems)
    for copy in copies:
        copy.start()
    h2[...] = (ln_parts(x1[...])[0] * gain[...] + bias[...]).astype(bf16)
    y[...] = x1[...]
    for copy in copies:
        copy.wait()
    keep = pltpu.make_async_copy(w, w_out, out_sem)
    keep.start()

    def one_chunk(index, _):
        t = index // 2
        col = (index % 2) * 512
        pre = dot(h2[...], w[t, :, pl.ds(pl.multiple_of(col, 512), 512)])
        hidden = gelu_parts(pre)[0].astype(bf16)
        y[...] += dot_nt(hidden, w[t, :, pl.ds(pl.multiple_of(col + 1024, 512), 512)])
        return 0

    lax.fori_loop(0, 4, one_chunk, 0)
    keep.wait()


def mlp_bwd_kernel(ids, x1, dy, gain, bias, w_hbm, *refs):
    dx1, small = refs[:2]
    quads, refs = refs[2:10], refs[10:]
    w, g, h2, h2t, dyb, dybt, dh2, w_sem, sems = refs
    load = pltpu.make_async_copy(w_hbm, w, w_sem)
    load.start()
    h2[...] = (ln_parts(x1[...])[0] * gain[...] + bias[...]).astype(bf16)
    h2t[...] = h2[...].T
    dyb[...] = dy[...].astype(bf16)
    dybt[...] = dyb[...].T
    dh2[...] = jnp.zeros_like(dh2)
    load.wait()

    def one_chunk(index, _):
        t = index // 2
        up = pl.ds(pl.multiple_of((index % 2) * 512, 512), 512)
        down = pl.ds(pl.multiple_of((index % 2) * 512 + 1024, 512), 512)
        pre = dot(h2[...], w[t, :, up])
        hidden, tanh, square = gelu_parts(pre)
        slope = 0.5 * (1.0 + tanh) + (0.5 * gelu_coef) * pre * (1.0 - tanh * tanh) * (
            1.0 + (3 * 0.044715) * square
        )
        dhidden = dot(dyb[...], w[t, :, down])
        dpre = (dhidden * slope).astype(bf16)
        g[t, :, down] = dot(dybt[...], hidden.astype(bf16)).astype(bf16)
        g[t, :, up] = dot(h2t[...], dpre).astype(bf16)
        dh2[...] += dot_nt(dpre, w[t, :, up])
        return 0

    lax.fori_loop(0, 4, one_chunk, 0)
    copies = grad_copies(ids, g, quads, sems)
    for copy in copies:
        copy.start()
    xhat, inv = ln_parts(x1[...])
    grad = dh2[...]
    small[0:1, :] = jnp.sum(grad * xhat, axis=0, keepdims=True)
    small[1:2, :] = jnp.sum(grad, axis=0, keepdims=True)
    dx1[...] = dy[...] + ln_back(grad, xhat, inv, gain[...])
    for copy in copies:
        copy.wait()


def attn_bwd_kernel(ids, x, dx1, segc, segr, gain, bias, qs, k, v, o, qst, kt, ot, lse, w_hbm, *refs):
    dx, small = refs[:2]
    quads, refs = refs[2:10], refs[10:]
    w, g, h, mask, do, dot_t, drow, dqt, dq, dk, dv, flip, w_sem, sems = refs
    load = pltpu.make_async_copy(w_hbm, w, w_sem)
    load.start()
    xf = x[...].astype(f32)
    h[...] = (ln_parts(xf)[0] * gain[...] + bias[...]).astype(bf16)
    mask[...] = jnp.where(segc[...] == segr[...], 0.0, masked_score)
    low = dx1[...].astype(bf16)
    flip[...] = low.T
    load.wait()
    for t in range(2):
        cols = pl.ds(t * 256, 256)
        do[:, cols] = dot(low, w[t, :, 768:1024]).astype(bf16)
        g[t, :, 768:1024] = dot(flip[...], o[:, cols]).astype(bf16)
    dot_t[...] = do[...].T
    for head in range(8):
        rows = pl.ds(head * HEAD_DIM, HEAD_DIM)
        drow[head : head + 1, :] = jnp.sum(
            dot_t[rows, :].astype(f32) * ot[rows, :].astype(f32), axis=0, keepdims=True
        )

    def one_pair(pair, _):
        lanes = pl.ds(pl.multiple_of(pair * 128, 128), 128)
        k_pair, v_pair = k[:, lanes], v[:, lanes]
        q_pair, do_pair = qs[:, lanes], do[:, lanes]
        dvs, dks = [], []
        for which in range(2):
            head = pl.ds(pair * 2 + which, 1)
            rows = pl.ds(pl.multiple_of(pair * 128 + which * HEAD_DIM, HEAD_DIM), HEAD_DIM)
            scores = dot(k_pair, head_rows(qst, pair, which)) + mask[...]
            probs = jnp.exp(scores - lse[head, :])
            dprobs = dot(v_pair, head_rows(dot_t, pair, which))
            dscore = (probs * (dprobs - drow[head, :])).astype(bf16)
            dvs.append(dot(probs.astype(bf16), do_pair))
            dks.append(dot(dscore, q_pair))
            dqt[rows, :] = (dot(kt[rows, :], dscore) * HEAD_DIM ** (-0.5)).astype(bf16)
        first = lax.broadcasted_iota(jnp.int32, (512, 128), 1) < HEAD_DIM
        dv[:, lanes] = jnp.where(first, dvs[0], dvs[1]).astype(bf16)
        dk[:, lanes] = jnp.where(first, dks[0], dks[1]).astype(bf16)
        return 0

    lax.fori_loop(0, 4, one_pair, 0)
    dq[...] = dqt[...].T
    flip[...] = h[...].T
    for t in range(2):
        cols = pl.ds(t * 256, 256)
        g[t, :, 0:256] = dot(flip[...], dq[:, cols]).astype(bf16)
        g[t, :, 256:512] = dot(flip[...], dk[:, cols]).astype(bf16)
        g[t, :, 512:768] = dot(flip[...], dv[:, cols]).astype(bf16)
    copies = grad_copies(ids, g, quads, sems)
    for copy in copies:
        copy.start()
    grad = jnp.zeros((512, 512), f32)
    for t in range(2):
        cols = pl.ds(t * 256, 256)
        for index, part in enumerate((dq, dk, dv)):
            grad = grad + dot_nt(part[:, cols], w[t, :, index * 256 : (index + 1) * 256])
    xhat, inv = ln_parts(xf)
    small[0:1, :] = jnp.sum(grad * xhat, axis=0, keepdims=True)
    small[1:2, :] = jnp.sum(grad, axis=0, keepdims=True)
    dx[...] = dx1[...] + ln_back(grad, xhat, inv, gain[...])
    for copy in copies:
        copy.wait()


def code_prep_kernel(book_t, stack, stack_t):
    def one_chunk(index, _):
        lanes = pl.ds(pl.multiple_of(index * 512, 512), 512)
        rows = book_t[:, lanes]
        unit = rows * lax.rsqrt(jnp.sum(rows * rows, axis=0, keepdims=True) + norm_eps)
        hi, mid, lo = split3(unit)
        stack_t[:, lanes] = jnp.concatenate([hi, mid, lo, jnp.ones((32, 512), bf16)], axis=0)
        tall = jnp.concatenate([hi, mid, lo, hi, mid, hi, jnp.zeros((64, 512), bf16)], axis=0)
        stack[lanes, :] = tall.T
        return 0

    lax.fori_loop(0, book_t.shape[1] // 512, one_chunk, 0)


def factor_stack(x):
    hi, mid, lo = split3(x)
    return jnp.concatenate([hi, hi, hi, mid, mid, lo, jnp.zeros((64, x.shape[1]), bf16)], axis=0)


def vq_fwd_kernel(e, gain, bias, in_t, out_w, stack, stack_t, u, kept, acc):
    lnv = ln_parts(e[...])[0] * gain[...] + bias[...]
    raw = dot_nt(in_t[...], lnv, highest)
    inv = lax.rsqrt(jnp.sum(raw * raw, axis=0, keepdims=True) + norm_eps)
    latent = raw * inv
    right = factor_stack(latent * (temper * log2e))
    acc[...] = jnp.zeros_like(acc)

    def one_chunk(index, _):
        codes = pl.ds(pl.multiple_of(index * 512, 512), 512)
        numer = jnp.exp2(dot(stack[codes, :], right)).astype(bf16)
        acc[...] += dot(stack_t[:, codes], numer)
        return 0

    lax.fori_loop(0, stack.shape[0] // 512, one_chunk, 0)
    total = acc[96:97, :]
    soft = (acc[0:32, :] + acc[32:64, :] + acc[64:96, :]) / total
    kept[0:32, :] = latent
    kept[32:64, :] = soft
    kept[64:65, :] = total
    kept[65:66, :] = inv
    u[...] = dot_full(soft.T, out_w[...])


def vq_bwd_kernel(ids, e, du, gain, bias, in_t, out_w, stack, stack_t, book_t, kept, *refs):
    de, small = refs[:2]
    quads, refs = refs[2:10], refs[10:]
    acc, grads, sems = refs
    xhat, inv_ln = ln_parts(e[...])
    lnv = xhat * gain[...] + bias[...]
    latent, soft = kept[0:32, :], kept[32:64, :]
    total, inv = kept[64:65, :], kept[65:66, :]
    direct = (2.0 * 1.25 * commit_weight) * (latent - soft)
    dsoft = dot_nt(out_w[...], du[...], highest) - direct
    small[32:64, :] = dot_full(soft, du[...])
    shift = jnp.sum(dsoft * soft, axis=0, keepdims=True) / total
    dsoft = dsoft / total
    right = jnp.concatenate(
        [factor_stack(latent * (temper * log2e)), factor_stack(dsoft)], axis=1
    )
    pads = jnp.zeros((64, 512), f32)

    def tall(x):
        hi, lo = split2(x)
        return jnp.concatenate([hi.astype(f32), lo.astype(f32), pads], axis=0).T.astype(bf16)

    sides = jnp.concatenate([tall(dsoft), tall(latent * temper)], axis=0)
    acc[...] = jnp.zeros_like(acc)

    def one_chunk(index, _):
        codes = pl.ds(pl.multiple_of(index * 512, 512), 512)
        both = dot(stack[codes, :], right)
        numer = jnp.exp2(both[:, :512])
        dlogit = (numer * (both[:, 512:] - shift)).astype(bf16)
        acc[...] += dot(stack_t[0:96, codes], dlogit)
        dcode = dot(jnp.concatenate([numer.astype(bf16), dlogit], axis=1), sides).T
        dcode = dcode[0:32, :] + dcode[32:64, :]
        rows = book_t[:, codes]
        scale = lax.rsqrt(jnp.sum(rows * rows, axis=0, keepdims=True) + norm_eps)
        unit = rows * scale
        grads[:, codes] = (
            scale * (dcode - unit * jnp.sum(unit * dcode, axis=0, keepdims=True))
        ).astype(bf16)
        return 0

    lax.fori_loop(0, stack.shape[0] // 512, one_chunk, 0)
    copies = []
    for slot, (which, k, dp_xor, tp_xor) in enumerate(block_places()):
        lane = pl.multiple_of(((ids[0] ^ dp_xor) * 2 + (ids[1] ^ tp_xor)) * 256, 256)
        copies.append(
            pltpu.make_async_copy(
                grads.at[:, pl.ds(lane, 256)], quads[which].at[k], sems.at[slot]
            )
        )
    for copy in copies:
        copy.start()
    dlatent = temper * (acc[0:32, :] + acc[32:64, :] + acc[64:96, :]) + direct
    draw = inv * (dlatent - latent * jnp.sum(latent * dlatent, axis=0, keepdims=True))
    small[0:32, :] = dot_full(draw, lnv)
    dln = dot_full(draw.T, in_t[...])
    small[64:65, :] = jnp.sum(dln * xhat, axis=0, keepdims=True)
    small[65:66, :] = jnp.sum(dln, axis=0, keepdims=True)
    de[...] = ln_back(dln, xhat, inv_ln, gain[...])
    for copy in copies:
        copy.wait()


def code_join_kernel(ids, *refs):
    quads, out, sems = refs[:8], refs[8], refs[9]
    copies = []
    for slot, (which, k, dp_xor, tp_xor) in enumerate(block_places()):
        lane = pl.multiple_of(((ids[0] ^ dp_xor) * 2 + (ids[1] ^ tp_xor)) * 256, 256)
        copies.append(
            pltpu.make_async_copy(quads[which].at[k], out.at[:, pl.ds(lane, 256)], sems.at[slot])
        )
    for copy in copies:
        copy.start()
    for copy in copies:
        copy.wait()


SMEM = pl.BlockSpec(memory_space=pltpu.SMEM)
VMEM = pl.BlockSpec(memory_space=pltpu.VMEM)
ANY = pl.BlockSpec(memory_space=pl.ANY)


def shaped(*pairs):
    return [jax.ShapeDtypeStruct(shape, dtype) for shape, dtype in pairs]


def call(kernel, name, in_specs, out_specs, outs, scratch, flops, moved):
    return pl.pallas_call(
        kernel,
        name=name,
        in_specs=in_specs,
        out_specs=out_specs,
        out_shape=outs,
        scratch_shapes=scratch,
        compiler_params=pltpu.CompilerParams(vmem_limit_bytes=vmem_cap),
        cost_estimate=pl.CostEstimate(flops=flops, bytes_accessed=moved, transcendentals=0),
    )


DMA = pltpu.SemaphoreType.DMA
ROWS2 = (512, 512)


def attn_fwd(ids, x, segs, gain, bias, quads):
    outs = shaped(
        (ROWS2, f32),
        *[(ROWS2, bf16)] * 7,
        ((8, 512), f32),
        ((2, 512, 1024), bf16),
    )
    scratch = [
        pltpu.VMEM((2, 512, 1024), bf16),
        pltpu.VMEM(ROWS2, bf16),
        pltpu.VMEM(ROWS2, bf16),
        pltpu.VMEM(ROWS2, f32),
        DMA((32,)),
        DMA,
    ]
    return call(
        attn_fwd_kernel,
        "attn_fwd",
        [SMEM] + [VMEM] * 5 + [ANY] * 8,
        [VMEM] * 9 + [ANY],
        outs,
        scratch,
        5 * 10**9,
        10**7,
    )(ids, x, *segs, gain, bias, *quads)


def mlp_fwd(ids, x1, gain, bias, quads):
    return call(
        mlp_fwd_kernel,
        "mlp_fwd",
        [SMEM] + [VMEM] * 3 + [ANY] * 8,
        [VMEM, ANY],
        shaped((ROWS2, f32), ((2, 512, 2048), bf16)),
        [pltpu.VMEM((2, 512, 2048), bf16), pltpu.VMEM(ROWS2, bf16), DMA((32,)), DMA],
        5 * 10**9,
        10**7,
    )(ids, x1, gain, bias, *quads)


def mlp_bwd(ids, x1, dy, gain, bias, w):
    outs = shaped((ROWS2, f32), ((8, 512), f32), *[((4, 32, 2048), bf16)] * 8)
    scratch = [
        pltpu.VMEM((2, 512, 2048), bf16),
        pltpu.VMEM((2, 512, 2048), bf16),
        *[pltpu.VMEM(ROWS2, bf16)] * 4,
        pltpu.VMEM(ROWS2, f32),
        DMA,
        DMA((32,)),
    ]
    res = call(
        mlp_bwd_kernel,
        "mlp_bwd",
        [SMEM] + [VMEM] * 4 + [ANY],
        [VMEM] * 2 + [ANY] * 8,
        outs,
        scratch,
        10**10,
        2 * 10**7,
    )(ids, x1, dy, gain, bias, w)
    return res[0], res[1], res[2:]


def attn_bwd(ids, x, dx1, segs, gain, bias, saved, w):
    outs = shaped((ROWS2, f32), ((8, 512), f32), *[((4, 32, 1024), bf16)] * 8)
    scratch = [
        pltpu.VMEM((2, 512, 1024), bf16),
        pltpu.VMEM((2, 512, 1024), bf16),
        pltpu.VMEM(ROWS2, bf16),
        pltpu.VMEM(ROWS2, f32),
        pltpu.VMEM(ROWS2, bf16),
        pltpu.VMEM(ROWS2, bf16),
        pltpu.VMEM((8, 512), f32),
        *[pltpu.VMEM(ROWS2, bf16)] * 5,
        DMA,
        DMA((32,)),
    ]
    res = call(
        attn_bwd_kernel,
        "attn_bwd",
        [SMEM] + [VMEM] * 14 + [ANY],
        [VMEM] * 2 + [ANY] * 8,
        outs,
        scratch,
        10**10,
        2 * 10**7,
    )(ids, x, dx1, *segs, gain, bias, *saved, w)
    return res[0], res[1], res[2:]


def code_prep(book_t):
    codes = book_t.shape[1]
    return call(
        code_prep_kernel,
        "code_prep",
        [VMEM],
        [VMEM] * 2,
        shaped(((codes, 256), bf16), ((128, codes), bf16)),
        [],
        10**9,
        10**7,
    )(book_t)


def vq_fwd(e, gain, bias, in_t, out_w, stack, stack_t):
    return call(
        vq_fwd_kernel,
        "vq_fwd",
        [VMEM] * 7,
        [VMEM] * 2,
        shaped((ROWS2, f32), ((72, 512), f32)),
        [pltpu.VMEM((128, 512), f32)],
        8 * 10**9,
        10**7,
    )(e, gain, bias, in_t, out_w, stack, stack_t)


def vq_bwd(ids, e, du, gain, bias, in_t, out_w, stack, stack_t, book_t, kept):
    codes = book_t.shape[1]
    outs = shaped((ROWS2, f32), ((72, 512), f32), *[((4, 32, 256), bf16)] * 8)
    res = call(
        vq_bwd_kernel,
        "vq_bwd",
        [SMEM] + [VMEM] * 10,
        [VMEM] * 2 + [ANY] * 8,
        outs,
        [pltpu.VMEM((96, 512), f32), pltpu.VMEM((32, codes), bf16), DMA((32,))],
        2 * 10**10,
        2 * 10**7,
    )(ids, e, du, gain, bias, in_t, out_w, stack, stack_t, book_t, kept)
    return res[0], res[1], res[2:]


def code_join(ids, quads, codes):
    return call(
        code_join_kernel,
        "code_join",
        [SMEM] + [ANY] * 8,
        VMEM,
        jax.ShapeDtypeStruct((32, codes), f32),
        [DMA((32,))],
        1,
        2 * 10**6,
    )(ids, *quads)


def whole_groups(
    n_dp,
    tokens,
    segment_ids,
    norm_gains,
    norm_biases,
    w_qkv,
    w_attn_out,
    w_up,
    w_down,
    w_vq_in,
    w_vq_out,
    codebook,
    cotangent,
):
    dp_at, tp_at = lax.axis_index("dp"), lax.axis_index("tp")
    ids = jnp.stack([dp_at, tp_at]).astype(jnp.int32)
    rows = tokens.shape[1]

    def mine(values):
        return lax.dynamic_index_in_dim(values, tp_at, 0, keepdims=False)

    def theirs(values):
        return lax.dynamic_index_in_dim(values, 1 - tp_at, 0, keepdims=False)

    def swap(values):
        return exchange(values, 0, 1, n_dp)

    def both_rows(own, other):
        return jnp.where(tp_at == 0, jnp.stack([own, other]), jnp.stack([other, own]))

    x = jnp.concatenate([mine(tokens), swap(theirs(tokens))], axis=0)
    seg = jnp.concatenate([mine(segment_ids), swap(theirs(segment_ids))], axis=0)
    segs = (seg[:, None], seg[None, :])
    gains = [norm_gains[i : i + 1] for i in range(5)]
    biases = [norm_biases[i : i + 1] for i in range(5)]

    attn_shards, mlp_shards = [], []
    for layer in range(2):
        attn_shards.append(
            jnp.concatenate(
                [w_qkv[layer, 0], w_qkv[layer, 1], w_qkv[layer, 2], w_attn_out[layer].T], axis=1
            )
        )
        mlp_shards.append(jnp.concatenate([w_up[layer], w_down[layer].T], axis=1))
    enc_attn = gather_blocks(attn_shards[0], n_dp)
    enc_mlp = gather_blocks(mlp_shards[0], n_dp)
    dec_attn = gather_blocks(attn_shards[1], n_dp)
    dec_mlp = gather_blocks(mlp_shards[1], n_dp)
    dy = jnp.concatenate(
        [mine(cotangent), swap(theirs(cotangent).astype(bf16)).astype(f32)], axis=0
    )

    book_t, in_t = codebook.T, w_vq_in.T
    stack, stack_t = code_prep(book_t)

    e_x1, *e_saved, e_wa = attn_fwd(ids, x, segs, gains[0], biases[0], enc_attn)
    e, e_wm = mlp_fwd(ids, e_x1, gains[1], biases[1], enc_mlp)
    u, kept = vq_fwd(e, gains[2], biases[2], in_t, w_vq_out, stack, stack_t)
    d_x1, *d_saved, d_wa = attn_fwd(ids, u, segs, gains[3], biases[3], dec_attn)
    y, d_wm = mlp_fwd(ids, d_x1, gains[4], biases[4], dec_mlp)
    decoded = both_rows(y[:rows], swap(y[rows:]))

    dx1, d_small1, d_gm = mlp_bwd(ids, d_x1, dy, gains[4], biases[4], d_wm)
    dec_mlp_grad = scatter_blocks(d_gm, n_dp)
    du, d_small0, d_ga = attn_bwd(ids, u, dx1, segs, gains[3], biases[3], d_saved, d_wa)
    dec_attn_grad = scatter_blocks(d_ga, n_dp)
    de, v_small, code_parts = vq_bwd(
        ids, e, du, gains[2], biases[2], in_t, w_vq_out, stack, stack_t, book_t, kept
    )
    code_own = scatter_blocks(code_parts, n_dp)
    mid_sum = sum_everywhere(
        jnp.concatenate([v_small[:66], d_small0[:2], d_small1[:2]], axis=0), n_dp
    )
    ex1, e_small1, e_gm = mlp_bwd(ids, e_x1, de, gains[1], biases[1], e_wm)
    enc_mlp_grad = scatter_blocks(e_gm, n_dp)
    dx, e_small0, e_ga = attn_bwd(ids, x, ex1, segs, gains[0], biases[0], e_saved, e_wa)
    enc_attn_grad = scatter_blocks(e_ga, n_dp)
    enc_sum = sum_everywhere(jnp.concatenate([e_small0[:2], e_small1[:2]], axis=0), n_dp)
    grad_tokens = both_rows(dx[:rows], swap(dx[rows:].astype(bf16)).astype(f32))
    grad_code = code_join(ids, gather_blocks(code_own, n_dp), codebook.shape[0]).T

    def parts_of(attn, mlp):
        qkv = jnp.stack([attn[:, 256 * i : 256 * (i + 1)] for i in range(3)])
        return qkv, attn[:, 768:].T, mlp[:, :1024], mlp[:, 1024:].T

    enc_parts = parts_of(enc_attn_grad, enc_mlp_grad)
    dec_parts = parts_of(dec_attn_grad, dec_mlp_grad)
    weight_grads = [jnp.stack(pair) for pair in zip(enc_parts, dec_parts)]
    gain_rows = [enc_sum[0], enc_sum[2], mid_sum[64], mid_sum[66], mid_sum[68]]
    bias_rows = [enc_sum[1], enc_sum[3], mid_sum[65], mid_sum[67], mid_sum[69]]
    return (
        decoded,
        grad_tokens,
        jnp.stack(gain_rows),
        jnp.stack(bias_rows[:3]),
        jnp.stack(bias_rows[3:]),
        *weight_grads,
        mid_sum[0:32].T,
        mid_sum[32:64],
        grad_code,
    )


def layer_norm(values, norm_gain, norm_bias):
    centred = values - jnp.mean(values, axis=-1, keepdims=True)
    spread = jnp.mean(centred * centred, axis=-1, keepdims=True)
    return centred * lax.rsqrt(spread + ln_eps) * norm_gain + norm_bias


def gelu_tanh(values):
    return (
        0.5 * values * (1.0 + jnp.tanh(gelu_coef * (values + 0.044715 * values * values * values)))
    )


def matmul(former, latter):
    return jnp.dot(former, latter, precision=highest, preferred_element_type=jnp.float32)


def normalize(values):
    return values * lax.rsqrt(jnp.sum(values * values, axis=-1, keepdims=True) + norm_eps)


def quantize(in_rows, norm_gain, norm_bias, in_w, out_w, code_w):
    latent = normalize(matmul(layer_norm(in_rows, norm_gain, norm_bias), in_w))
    code_rows = normalize(code_w)
    logits = matmul(latent, code_rows.T) * temper
    row_max = jnp.max(logits, axis=-1, keepdims=True)
    numerator = jnp.exp(logits - row_max)
    assign = numerator / jnp.sum(numerator, axis=-1, keepdims=True)
    soft_code = matmul(assign, code_rows)
    offset = latent - soft_code
    vq_loss = commit_weight * 1.25 * jnp.sum(offset * offset)
    return (matmul(soft_code, out_w), vq_loss)


def product(former, latter):
    return jnp.dot(former, latter, preferred_element_type=jnp.float32)


def product_tn(former, latter):
    return lax.dot_general(
        former, latter, (((0,), (0,)), ((), ())), preferred_element_type=jnp.float32
    )


def product_nt(former, latter):
    return lax.dot_general(
        former, latter, (((1,), (1,)), ((), ())), preferred_element_type=jnp.float32
    )


def split_heads(values):
    return values.reshape(values.shape[0], values.shape[1] // HEAD_DIM, HEAD_DIM).transpose(1, 0, 2)


def join_heads(values):
    return values.transpose(1, 0, 2).reshape(values.shape[1], values.shape[0] * HEAD_DIM)


def masked_scores(query_blk, key_h, seg_blk, seg_keys):
    scores = jnp.einsum(
        "hqd,hkd->hqk", query_blk, key_h, preferred_element_type=jnp.float32
    ) * HEAD_DIM ** (-0.5)
    return jnp.where((seg_blk[:, None] == seg_keys[None, :])[None], scores, masked_score)


def attend(query_h, key_h, value_h, seg_keys):
    block_rows = min(512, query_h.shape[1])
    block_count = query_h.shape[1] // block_rows

    def one_block(begin_row):
        query_blk = lax.dynamic_slice_in_dim(query_h, begin_row, block_rows, 1)
        seg_blk = lax.dynamic_slice_in_dim(seg_keys, begin_row, block_rows, 0)
        scores = masked_scores(query_blk, key_h, seg_blk, seg_keys)
        row_max = jnp.max(scores, axis=-1, keepdims=True)
        numerator = jnp.exp(scores - row_max)
        row_total = jnp.sum(numerator, axis=-1, keepdims=True)
        prob_low = (numerator / row_total).astype(jnp.bfloat16)
        attended = jnp.einsum("hqk,hkd->hqd", prob_low, value_h, preferred_element_type=jnp.float32)
        return (attended.astype(jnp.bfloat16), (row_max + jnp.log(row_total))[..., 0])

    starts = jnp.arange(block_count, dtype=jnp.int32) * block_rows
    attended, log_sums = lax.map(one_block, starts)
    heads_out = attended.transpose(1, 0, 2, 3).reshape(query_h.shape)
    log_sums = log_sums.transpose(1, 0, 2).reshape(query_h.shape[0], query_h.shape[1])
    return (heads_out, log_sums)


def attend_back(query_h, key_h, value_h, seg_keys, log_sums, grad_out):
    block_rows = min(512, query_h.shape[1])
    block_count = query_h.shape[1] // block_rows

    def one_block(carry, begin_row):
        grad_key, grad_value = carry
        query_blk = lax.dynamic_slice_in_dim(query_h, begin_row, block_rows, 1)
        grad_blk = lax.dynamic_slice_in_dim(grad_out, begin_row, block_rows, 1)
        lse_blk = lax.dynamic_slice_in_dim(log_sums, begin_row, block_rows, 1)
        seg_blk = lax.dynamic_slice_in_dim(seg_keys, begin_row, block_rows, 0)
        scores = masked_scores(query_blk, key_h, seg_blk, seg_keys)
        probs = jnp.exp(scores - lse_blk[..., None])
        prob_low = probs.astype(jnp.bfloat16)
        grad_value = grad_value + jnp.einsum(
            "hqk,hqd->hkd", prob_low, grad_blk, preferred_element_type=jnp.float32
        )
        grad_prob = jnp.einsum(
            "hqd,hkd->hqk", grad_blk, value_h, preferred_element_type=jnp.float32
        )
        row_dot = jnp.sum(probs * grad_prob, axis=-1, keepdims=True)
        grad_score = (probs * (grad_prob - row_dot) * HEAD_DIM ** (-0.5)).astype(jnp.bfloat16)
        grad_query = jnp.einsum(
            "hqk,hkd->hqd", grad_score, key_h, preferred_element_type=jnp.float32
        )
        grad_key = grad_key + jnp.einsum(
            "hqk,hqd->hkd", grad_score, query_blk, preferred_element_type=jnp.float32
        )
        return ((grad_key, grad_value), grad_query)

    starts = jnp.arange(block_count, dtype=jnp.int32) * block_rows
    zeros_kv = jnp.zeros(key_h.shape, jnp.float32)
    (grad_key, grad_value), grad_query = lax.scan(one_block, (zeros_kv, zeros_kv), starts)
    grad_query = grad_query.transpose(1, 0, 2, 3).reshape(query_h.shape)
    return (
        grad_query.astype(jnp.bfloat16),
        grad_key.astype(jnp.bfloat16),
        grad_value.astype(jnp.bfloat16),
    )


def spread_rows(values):
    return lax.all_gather(values, "tp", axis=0, tiled=True)


def combine_rows(partial_value):
    return lax.psum_scatter(partial_value, "tp", scatter_dimension=0, tiled=True)


def spread_grads(values):
    return lax.all_gather(values, "tp", axis=0, tiled=True)


def combine_grads(partial_value):
    return lax.psum_scatter(
        partial_value.astype(jnp.bfloat16), "tp", scatter_dimension=0, tiled=True
    ).astype(jnp.float32)


def fetch_weights(w_qkv, w_attn_out, w_up, w_down, layer):
    return (
        lax.all_gather(w_qkv[layer], "dp", axis=1, tiled=True),
        lax.all_gather(w_attn_out[layer], "dp", axis=1, tiled=True),
        lax.all_gather(w_up[layer], "dp", axis=0, tiled=True),
        lax.all_gather(w_down[layer], "dp", axis=1, tiled=True),
    )


def reduce_weight_grads(grads):
    return (
        lax.psum_scatter(
            grads[0].astype(jnp.bfloat16), "dp", scatter_dimension=1, tiled=True
        ).astype(jnp.float32),
        lax.psum_scatter(
            grads[1].astype(jnp.bfloat16), "dp", scatter_dimension=1, tiled=True
        ).astype(jnp.float32),
        lax.psum_scatter(
            grads[2].astype(jnp.bfloat16), "dp", scatter_dimension=0, tiled=True
        ).astype(jnp.float32),
        lax.psum_scatter(
            grads[3].astype(jnp.bfloat16), "dp", scatter_dimension=1, tiled=True
        ).astype(jnp.float32),
    )


def block_forward(resid_in, seg_local, gains, biases, weights):
    qkv_w, attn_w, up_w, down_w = weights
    normed = layer_norm(resid_in, gains[0], biases[0]).astype(jnp.bfloat16)
    normed_all, seg_all = (
        lax.all_gather(normed, "tp", axis=0, tiled=True),
        lax.all_gather(seg_local, "tp", axis=0, tiled=True),
    )
    query_h = split_heads(product(normed_all, qkv_w[0]).astype(jnp.bfloat16))
    key_h = split_heads(product(normed_all, qkv_w[1]).astype(jnp.bfloat16))
    value_h = split_heads(product(normed_all, qkv_w[2]).astype(jnp.bfloat16))
    heads_out, log_sums = attend(query_h, key_h, value_h, seg_all)
    attn_rows = join_heads(heads_out)
    middle = resid_in + combine_rows(product(attn_rows, attn_w))
    normed_mid = spread_rows(layer_norm(middle, gains[1], biases[1]).astype(jnp.bfloat16))
    hidden_pre = product(normed_mid, up_w)
    hidden = gelu_tanh(hidden_pre).astype(jnp.bfloat16)
    result = middle + combine_rows(product(hidden, down_w))
    kept = (
        resid_in,
        middle,
        normed_all,
        seg_all,
        query_h,
        key_h,
        value_h,
        log_sums,
        attn_rows,
        normed_mid,
        hidden_pre,
        hidden,
    )
    return (result, kept)


def block_backward(kept, gains, biases, weights, grad_result):
    (
        resid_in,
        middle,
        normed_all,
        seg_all,
        query_h,
        key_h,
        value_h,
        log_sums,
        attn_rows,
        normed_mid,
        hidden_pre,
        hidden,
    ) = kept
    qkv_w, attn_w, up_w, down_w = weights
    grad_branch = spread_grads(grad_result.astype(jnp.bfloat16))
    grad_down = product_tn(hidden, grad_branch)
    grad_hidden = product_nt(grad_branch, down_w)
    _, gelu_back = jax.vjp(gelu_tanh, hidden_pre)
    grad_pre = gelu_back(grad_hidden)[0].astype(jnp.bfloat16)
    grad_up = product_tn(normed_mid, grad_pre)
    grad_norm_mid = combine_grads(product_nt(grad_pre, up_w))
    _, norm_back_mid = jax.vjp(layer_norm, middle, gains[1], biases[1])
    grad_mid_ln, grad_gain_mid, grad_bias_mid = norm_back_mid(grad_norm_mid)
    grad_middle = grad_result + grad_mid_ln
    grad_attn_all = spread_grads(grad_middle.astype(jnp.bfloat16))
    grad_attn = product_tn(attn_rows, grad_attn_all)
    grad_heads = split_heads(product_nt(grad_attn_all, attn_w).astype(jnp.bfloat16))
    grad_query, grad_key, grad_value = attend_back(
        query_h, key_h, value_h, seg_all, log_sums, grad_heads
    )
    grad_parts = [join_heads(grad_query), join_heads(grad_key), join_heads(grad_value)]
    grad_qkv = jnp.stack([product_tn(normed_all, grad_part) for grad_part in grad_parts])
    grad_normed_part = (
        product_nt(grad_parts[0], qkv_w[0])
        + product_nt(grad_parts[1], qkv_w[1])
        + product_nt(grad_parts[2], qkv_w[2])
    )
    grad_normed = combine_grads(grad_normed_part)
    _, norm_back_in = jax.vjp(layer_norm, resid_in, gains[0], biases[0])
    grad_in_ln, grad_gain_in, grad_bias_in = norm_back_in(grad_normed)
    gain_grads = jnp.stack([grad_gain_in, grad_gain_mid])
    bias_grads = jnp.stack([grad_bias_in, grad_bias_mid])
    return (
        grad_middle + grad_in_ln,
        gain_grads,
        bias_grads,
        (grad_qkv, grad_attn, grad_up, grad_down),
    )


def local(
    tokens,
    segment_ids,
    norm_gains,
    norm_biases,
    w_qkv,
    w_attn_out,
    w_up,
    w_down,
    w_vq_in,
    w_vq_out,
    codebook,
    cotangent,
):
    gain_sum = jnp.zeros(norm_gains.shape, jnp.float32)
    bias_sum = jnp.zeros(norm_biases.shape, jnp.float32)
    vq_in_sum = jnp.zeros(w_vq_in.shape, jnp.float32)
    vq_out_sum = jnp.zeros(w_vq_out.shape, jnp.float32)
    code_sum = jnp.zeros(codebook.shape, jnp.float32)
    layer_sums = [None, None]
    outputs = []
    input_grads = []
    for micro in range(MICRO):
        resid_in = tokens[micro].astype(jnp.float32)
        seg_local = segment_ids[micro]
        enc_weights = fetch_weights(w_qkv, w_attn_out, w_up, w_down, 0)
        encoded, enc_kept = block_forward(
            resid_in, seg_local, norm_gains[0:2], norm_biases[0:2], enc_weights
        )
        (decoder_in, _), vq_back = jax.vjp(
            quantize, encoded, norm_gains[2], norm_biases[2], w_vq_in, w_vq_out, codebook
        )
        dec_weights = fetch_weights(w_qkv, w_attn_out, w_up, w_down, 1)
        decoded, dec_kept = block_forward(
            decoder_in, seg_local, norm_gains[3:5], norm_biases[3:5], dec_weights
        )
        outputs.append(decoded)
        grad_dec_in, gains_dec, biases_dec, grads_dec = block_backward(
            dec_kept, norm_gains[3:5], norm_biases[3:5], dec_weights, cotangent[micro]
        )
        grad_encoded, grad_gain_vq, grad_bias_vq, grad_in_w, grad_out_w, grad_codes = vq_back(
            (grad_dec_in, jnp.ones((), jnp.float32))
        )
        grad_input, gains_enc, biases_enc, grads_enc = block_backward(
            enc_kept, norm_gains[0:2], norm_biases[0:2], enc_weights, grad_encoded
        )
        input_grads.append(grad_input)
        gain_sum = gain_sum + jnp.concatenate([gains_enc, grad_gain_vq[None], gains_dec], axis=0)
        bias_sum = bias_sum + jnp.concatenate([biases_enc, grad_bias_vq[None], biases_dec], axis=0)
        vq_in_sum = vq_in_sum + grad_in_w
        vq_out_sum = vq_out_sum + grad_out_w
        code_sum = code_sum + grad_codes
        for layer, grads in ((0, grads_enc), (1, grads_dec)):
            reduced = reduce_weight_grads(grads)
            if layer_sums[layer] is None:
                layer_sums[layer] = reduced
            else:
                layer_sums[layer] = jax.tree.map(jnp.add, layer_sums[layer], reduced)
    gain_tot, bias_tot, vq_in_tot, vq_out_tot, code_tot = lax.psum(
        (gain_sum, bias_sum, vq_in_sum, vq_out_sum, code_sum), ("dp", "tp")
    )
    return (
        jnp.stack(outputs),
        jnp.stack(input_grads),
        gain_tot,
        bias_tot[0:3],
        bias_tot[3:5],
        jnp.stack([layer_sums[0][0], layer_sums[1][0]]),
        jnp.stack([layer_sums[0][1], layer_sums[1][1]]),
        jnp.stack([layer_sums[0][2], layer_sums[1][2]]),
        jnp.stack([layer_sums[0][3], layer_sums[1][3]]),
        vq_in_tot,
        vq_out_tot,
        code_tot,
    )


def solution(mesh):
    n_dp, n_tp = mesh.shape["dp"], mesh.shape["tp"]
    fits = n_tp == MICRO and n_dp == 16
    return jax.shard_map(
        functools.partial(whole_groups, n_dp) if fits else local,
        mesh=mesh,
        in_specs=(
            P(None, ("dp", "tp"), None),
            P(None, ("dp", "tp")),
            P(),
            P(),
            P(None, None, "dp", "tp"),
            P(None, "tp", "dp"),
            P(None, "dp", "tp"),
            P(None, "tp", "dp"),
            P(),
            P(),
            P(),
            P(None, ("dp", "tp"), None),
        ),
        out_specs=(
            P(None, ("dp", "tp"), None),
            P(None, ("dp", "tp"), None),
            P(),
            P(),
            P(),
            P(None, None, "dp", "tp"),
            P(None, "tp", "dp"),
            P(None, "dp", "tp"),
            P(None, "tp", "dp"),
            P(),
            P(),
            P(),
        ),
        check_vma=False,
    )
```

```python
import functools

import jax
import jax.numpy as jnp
from jax import lax
from jax.experimental import pallas as pl
from jax.experimental.pallas import tpu as pltpu
from jax.sharding import PartitionSpec as P

HEAD_DIM = 64
MICRO = 2
bf16 = jnp.bfloat16
f32 = jnp.float32
highest = lax.Precision.HIGHEST
ln_eps = 1e-05
norm_eps = 1e-06
temper = 10.0
commit_weight = 64.0
gelu_coef = 0.7978845608028654
masked_score = -1e30
log2e = 1.4426950408889634
vmem_cap = 60 * 1024 * 1024


PLANE = ((0, 0), (0, 1), (1, 0), (1, 1))


def exchange(values, dp_xor, tp_xor, n_dp):
    pairs = [
        (d * 2 + t, (d ^ dp_xor) * 2 + (t ^ tp_xor)) for d in range(n_dp) for t in range(2)
    ]
    return lax.ppermute(values, ("dp", "tp"), pairs)


def spread_line(shard, n_dp):
    return jnp.stack([shard] + [exchange(shard, 4 * k, 0, n_dp) for k in range(1, 4)])


def spread_plane(own, n_dp):
    quads = [own] + [exchange(own, 2 * y, x, n_dp) for y, x in PLANE[1:]]
    return quads + [exchange(quad, 1, 0, n_dp) for quad in quads]


def plane_send(lows, n_dp):
    return [exchange(low, 2 * y, x, n_dp) for (y, x), low in zip(PLANE[1:], lows)]


def line_send(lows, n_dp):
    return [exchange(low, 4 * k, 0, n_dp) for k, low in zip(range(1, 4), lows)]


def block_places():
    for core in range(2):
        for index, (y, x) in enumerate(PLANE):
            for k in range(4):
                yield core * 4 + index, k, k * 4 + y * 2 + core, x


def dot(a, b):
    return jnp.dot(a, b, preferred_element_type=f32)


def dot_nt(a, b, precision=None):
    return lax.dot_general(
        a, b, (((1,), (1,)), ((), ())), preferred_element_type=f32, precision=precision
    )


def dot_full(a, b):
    return jnp.dot(a, b, preferred_element_type=f32, precision=highest)


def ln_parts(x):
    centred = x - jnp.mean(x, axis=-1, keepdims=True)
    inv = lax.rsqrt(jnp.mean(centred * centred, axis=-1, keepdims=True) + ln_eps)
    return centred * inv, inv


def ln_back(grad, xhat, inv, gain):
    scaled = grad * gain
    return inv * (
        scaled
        - jnp.mean(scaled, axis=-1, keepdims=True)
        - xhat * jnp.mean(scaled * xhat, axis=-1, keepdims=True)
    )


def split2(x):
    hi = x.astype(bf16)
    return hi, (x - hi.astype(f32)).astype(bf16)


def split3(x):
    hi, _ = split2(x)
    rest = x - hi.astype(f32)
    mid = rest.astype(bf16)
    return hi, mid, (rest - mid.astype(f32)).astype(bf16)


def weight_copies(ids_ref, quad_refs, w_ref, sems, first):
    width = w_ref.shape[2]
    copies = []
    for slot, (which, k, dp_xor, tp_xor) in enumerate(block_places()):
        row = pl.multiple_of((ids_ref[0] ^ dp_xor) * 32, 32)
        copies.append(
            pltpu.make_async_copy(
                quad_refs[which].at[k, :, pl.ds(first, width)],
                w_ref.at[ids_ref[1] ^ tp_xor, pl.ds(row, 32), :],
                sems.at[slot],
            )
        )
    return copies


def grad_copies(ids_ref, g_ref, half_refs, sems):
    copies = []
    for slot, (which, k, dp_xor, tp_xor) in enumerate(block_places()):
        row = pl.multiple_of((ids_ref[0] ^ dp_xor) * 32, 32)
        copies.append(
            pltpu.make_async_copy(
                g_ref.at[ids_ref[1] ^ tp_xor, pl.ds(row, 32), :],
                half_refs[which // 4].at[which % 4, k],
                sems.at[slot],
            )
        )
    return copies


def head_rows(ref, pair, which):
    own = ref[pl.ds(pl.multiple_of(pair * 128 + which * HEAD_DIM, HEAD_DIM), HEAD_DIM), :]
    zero = jnp.zeros_like(own)
    return jnp.concatenate([own, zero] if which == 0 else [zero, own], axis=0)


def segment_mask(seg):
    ids = seg[...].astype(f32)
    return jnp.where(ids[:, 0:1] == ids.T[0:1, :], 0.0, masked_score)


def attn_fwd_kernel(first, ids, x, seg, gain, bias, *refs):
    quads, refs = refs[:8], refs[8:]
    x1, qs, k, v, o, qst, kt, ot, lse, w_out = refs[:10]
    w, h, vt, mask, sems, out_sem = refs[10:]
    copies = weight_copies(ids, quads, w, sems, first)
    for copy in copies:
        copy.start()
    xf = x[...].astype(f32)
    h[...] = (ln_parts(xf)[0] * gain[...] + bias[...]).astype(bf16)
    mask[...] = segment_mask(seg)
    for copy in copies:
        copy.wait()
    keep = pltpu.make_async_copy(w, w_out, out_sem)
    keep.start()
    for t in range(2):
        cols = pl.ds(t * 256, 256)
        qs[:, cols] = (dot(h[...], w[t, :, 0:256]).astype(bf16) * HEAD_DIM ** (-0.5)).astype(bf16)
        k[:, cols] = dot(h[...], w[t, :, 256:512]).astype(bf16)
        v[:, cols] = dot(h[...], w[t, :, 512:768]).astype(bf16)
    qst[...] = qs[...].T
    kt[...] = k[...].T
    vt[...] = v[...].T

    def one_pair(pair, _):
        lanes = pl.ds(pl.multiple_of(pair * 128, 128), 128)
        k_pair = k[:, lanes]
        for which in range(2):
            scores = dot(k_pair, head_rows(qst, pair, which)) + mask[...]
            top = jnp.max(scores, axis=0, keepdims=True)
            numer = jnp.exp(scores - top).astype(bf16)
            rows = pl.ds(pl.multiple_of(pair * 128 + which * HEAD_DIM, HEAD_DIM), HEAD_DIM)
            left = jnp.concatenate([vt[rows, :], jnp.ones((16, 512), bf16)], axis=0)
            both = dot(left, numer)
            total = both[HEAD_DIM : HEAD_DIM + 1, :]
            ot[rows, :] = (both[:HEAD_DIM, :] / total).astype(bf16)
            lse[pl.ds(pair * 2 + which, 1), :] = top + jnp.log(total)
        return 0

    lax.fori_loop(0, 4, one_pair, 0)
    o[...] = ot[...].T
    acc = xf
    for t in range(2):
        acc = acc + dot_nt(o[:, t * 256 : (t + 1) * 256], w[t, :, 768:1024])
    x1[...] = acc
    keep.wait()


def gelu_parts(u):
    square = u * u
    tanh = jnp.tanh(gelu_coef * u * (1.0 + 0.044715 * square))
    return 0.5 * u * (1.0 + tanh), tanh, square


def mlp_fwd_kernel(first, ids, x1, gain, bias, *refs):
    quads, refs = refs[:8], refs[8:]
    y, w_out = refs[:2]
    w, h2, sems, out_sem = refs[2:]
    copies = weight_copies(ids, quads, w, sems, first)
    for copy in copies:
        copy.start()
    h2[...] = (ln_parts(x1[...])[0] * gain[...] + bias[...]).astype(bf16)
    y[...] = x1[...]
    for copy in copies:
        copy.wait()
    keep = pltpu.make_async_copy(w, w_out, out_sem)
    keep.start()

    def one_chunk(index, _):
        t = index // 2
        col = (index % 2) * 512
        pre = dot(h2[...], w[t, :, pl.ds(pl.multiple_of(col, 512), 512)])
        hidden = gelu_parts(pre)[0].astype(bf16)
        y[...] += dot_nt(hidden, w[t, :, pl.ds(pl.multiple_of(col + 1024, 512), 512)])
        return 0

    lax.fori_loop(0, 4, one_chunk, 0)
    keep.wait()


def mlp_bwd_kernel(ids, x1, dy, gain, bias, w_hbm, *refs):
    dx1, small = refs[:2]
    halves, refs = refs[2:4], refs[4:]
    w, g, h2, h2t, dyb, dybt, dh2, w_sem, sems = refs
    load = pltpu.make_async_copy(w_hbm, w, w_sem)
    load.start()
    h2[...] = (ln_parts(x1[...])[0] * gain[...] + bias[...]).astype(bf16)
    h2t[...] = h2[...].T
    dyb[...] = dy[...].astype(bf16)
    dybt[...] = dyb[...].T
    dh2[...] = jnp.zeros_like(dh2)
    load.wait()

    def one_chunk(index, _):
        t = index // 2
        up = pl.ds(pl.multiple_of((index % 2) * 512, 512), 512)
        down = pl.ds(pl.multiple_of((index % 2) * 512 + 1024, 512), 512)
        pre = dot(h2[...], w[t, :, up])
        hidden, tanh, square = gelu_parts(pre)
        slope = 0.5 * (1.0 + tanh) + (0.5 * gelu_coef) * pre * (1.0 - tanh * tanh) * (
            1.0 + (3 * 0.044715) * square
        )
        dhidden = dot(dyb[...], w[t, :, down])
        dpre = (dhidden * slope).astype(bf16)
        g[t, :, down] = dot(dybt[...], hidden.astype(bf16)).astype(bf16)
        g[t, :, up] = dot(h2t[...], dpre).astype(bf16)
        dh2[...] += dot_nt(dpre, w[t, :, up])
        return 0

    lax.fori_loop(0, 4, one_chunk, 0)
    copies = grad_copies(ids, g, halves, sems)
    for copy in copies:
        copy.start()
    xhat, inv = ln_parts(x1[...])
    grad = dh2[...]
    small[0:1, :] = jnp.sum(grad * xhat, axis=0, keepdims=True)
    small[1:2, :] = jnp.sum(grad, axis=0, keepdims=True)
    dx1[...] = dy[...] + ln_back(grad, xhat, inv, gain[...])
    for copy in copies:
        copy.wait()


def attn_bwd_kernel(ids, x, dx1, seg, gain, bias, qs, k, v, o, qst, kt, ot, lse, w_hbm, *refs):
    dx, small = refs[:2]
    halves, refs = refs[2:4], refs[4:]
    w, g, h, mask, do, dot_t, drow, dqt, dq, dk, dv, flip, w_sem, sems = refs
    load = pltpu.make_async_copy(w_hbm, w, w_sem)
    load.start()
    xf = x[...].astype(f32)
    h[...] = (ln_parts(xf)[0] * gain[...] + bias[...]).astype(bf16)
    mask[...] = segment_mask(seg)
    low = dx1[...].astype(bf16)
    flip[...] = low.T
    load.wait()
    for t in range(2):
        cols = pl.ds(t * 256, 256)
        do[:, cols] = dot(low, w[t, :, 768:1024]).astype(bf16)
        g[t, :, 768:1024] = dot(flip[...], o[:, cols]).astype(bf16)
    dot_t[...] = do[...].T
    for head in range(8):
        rows = pl.ds(head * HEAD_DIM, HEAD_DIM)
        drow[head : head + 1, :] = jnp.sum(
            dot_t[rows, :].astype(f32) * ot[rows, :].astype(f32), axis=0, keepdims=True
        )

    def one_pair(pair, _):
        lanes = pl.ds(pl.multiple_of(pair * 128, 128), 128)
        k_pair, v_pair = k[:, lanes], v[:, lanes]
        q_pair, do_pair = qs[:, lanes], do[:, lanes]
        dvs, dks = [], []
        for which in range(2):
            head = pl.ds(pair * 2 + which, 1)
            rows = pl.ds(pl.multiple_of(pair * 128 + which * HEAD_DIM, HEAD_DIM), HEAD_DIM)
            scores = dot(k_pair, head_rows(qst, pair, which)) + mask[...]
            probs = jnp.exp(scores - lse[head, :])
            dprobs = dot(v_pair, head_rows(dot_t, pair, which))
            dscore = (probs * (dprobs - drow[head, :])).astype(bf16)
            dvs.append(dot(probs.astype(bf16), do_pair))
            dks.append(dot(dscore, q_pair))
            dqt[rows, :] = (dot(kt[rows, :], dscore) * HEAD_DIM ** (-0.5)).astype(bf16)
        first = lax.broadcasted_iota(jnp.int32, (512, 128), 1) < HEAD_DIM
        dv[:, lanes] = jnp.where(first, dvs[0], dvs[1]).astype(bf16)
        dk[:, lanes] = jnp.where(first, dks[0], dks[1]).astype(bf16)
        return 0

    lax.fori_loop(0, 4, one_pair, 0)
    dq[...] = dqt[...].T
    flip[...] = h[...].T
    for t in range(2):
        cols = pl.ds(t * 256, 256)
        g[t, :, 0:256] = dot(flip[...], dq[:, cols]).astype(bf16)
        g[t, :, 256:512] = dot(flip[...], dk[:, cols]).astype(bf16)
        g[t, :, 512:768] = dot(flip[...], dv[:, cols]).astype(bf16)
    copies = grad_copies(ids, g, halves, sems)
    for copy in copies:
        copy.start()
    grad = jnp.zeros((512, 512), f32)
    for t in range(2):
        cols = pl.ds(t * 256, 256)
        for index, part in enumerate((dq, dk, dv)):
            grad = grad + dot_nt(part[:, cols], w[t, :, index * 256 : (index + 1) * 256])
    xhat, inv = ln_parts(xf)
    small[0:1, :] = jnp.sum(grad * xhat, axis=0, keepdims=True)
    small[1:2, :] = jnp.sum(grad, axis=0, keepdims=True)
    dx[...] = dx1[...] + ln_back(grad, xhat, inv, gain[...])
    for copy in copies:
        copy.wait()


def code_prep_kernel(book_t, stack, stack_t):
    def one_chunk(index, _):
        lanes = pl.ds(pl.multiple_of(index * 512, 512), 512)
        rows = book_t[:, lanes]
        unit = rows * lax.rsqrt(jnp.sum(rows * rows, axis=0, keepdims=True) + norm_eps)
        hi, mid, lo = split3(unit)
        stack_t[:, lanes] = jnp.concatenate([hi, mid, lo, jnp.ones((32, 512), bf16)], axis=0)
        tall = jnp.concatenate([hi, mid, lo, hi, mid, hi, jnp.zeros((64, 512), bf16)], axis=0)
        stack[lanes, :] = tall.T
        return 0

    lax.fori_loop(0, book_t.shape[1] // 512, one_chunk, 0)


def factor_stack(x):
    hi, mid, lo = split3(x)
    return jnp.concatenate([hi, hi, hi, mid, mid, lo, jnp.zeros((64, x.shape[1]), bf16)], axis=0)


def vq_fwd_kernel(e, gain, bias, in_t, out_w, stack, stack_t, u, kept, acc):
    lnv = ln_parts(e[...])[0] * gain[...] + bias[...]
    raw = dot_nt(in_t[...], lnv, highest)
    inv = lax.rsqrt(jnp.sum(raw * raw, axis=0, keepdims=True) + norm_eps)
    latent = raw * inv
    right = factor_stack(latent * (temper * log2e))
    acc[...] = jnp.zeros_like(acc)

    def one_chunk(index, _):
        codes = pl.ds(pl.multiple_of(index * 512, 512), 512)
        numer = jnp.exp2(dot(stack[codes, :], right)).astype(bf16)
        acc[...] += dot(stack_t[:, codes], numer)
        return 0

    lax.fori_loop(0, stack.shape[0] // 512, one_chunk, 0)
    total = acc[96:97, :]
    soft = (acc[0:32, :] + acc[32:64, :] + acc[64:96, :]) / total
    kept[0:32, :] = latent
    kept[32:64, :] = soft
    kept[64:65, :] = total
    kept[65:66, :] = inv
    u[...] = dot_full(soft.T, out_w[...])


def vq_bwd_kernel(ids, e, du, gain, bias, in_t, out_w, stack, stack_t, book_t, kept, *refs):
    de, small, code_keep, code_send, acc, grads, sems = refs
    xhat, inv_ln = ln_parts(e[...])
    lnv = xhat * gain[...] + bias[...]
    latent, soft = kept[0:32, :], kept[32:64, :]
    total, inv = kept[64:65, :], kept[65:66, :]
    direct = (2.0 * 1.25 * commit_weight) * (latent - soft)
    dsoft = dot_nt(out_w[...], du[...], highest) - direct
    small[32:64, :] = dot_full(soft, du[...])
    shift = jnp.sum(dsoft * soft, axis=0, keepdims=True) / total
    dsoft = dsoft / total
    right = jnp.concatenate(
        [factor_stack(latent * (temper * log2e)), factor_stack(dsoft)], axis=1
    )
    pads = jnp.zeros((64, 512), f32)

    def tall(x):
        hi, lo = split2(x)
        return jnp.concatenate([hi.astype(f32), lo.astype(f32), pads], axis=0).T.astype(bf16)

    sides = jnp.concatenate([tall(dsoft), tall(latent * temper)], axis=0)
    acc[...] = jnp.zeros_like(acc)

    def one_chunk(index, _):
        codes = pl.ds(pl.multiple_of(index * 512, 512), 512)
        both = dot(stack[codes, :], right)
        numer = jnp.exp2(both[:, :512])
        dlogit = (numer * (both[:, 512:] - shift)).astype(bf16)
        acc[...] += dot(stack_t[0:96, codes], dlogit)
        dcode = dot(jnp.concatenate([numer.astype(bf16), dlogit], axis=1), sides).T
        dcode = dcode[0:32, :] + dcode[32:64, :]
        rows = book_t[:, codes]
        scale = lax.rsqrt(jnp.sum(rows * rows, axis=0, keepdims=True) + norm_eps)
        unit = rows * scale
        grads[:, codes] = (
            scale * (dcode - unit * jnp.sum(unit * dcode, axis=0, keepdims=True))
        ).astype(bf16)
        return 0

    lax.fori_loop(0, stack.shape[0] // 512, one_chunk, 0)
    half = grads.shape[1] // 2
    core = ids[0] % 2
    copies = [
        pltpu.make_async_copy(
            grads.at[:, pl.ds(pl.multiple_of(at * half, half), half)], to, sems.at[slot]
        )
        for slot, (at, to) in enumerate(((core, code_keep), (1 - core, code_send)))
    ]
    for copy in copies:
        copy.start()
    dlatent = temper * (acc[0:32, :] + acc[32:64, :] + acc[64:96, :]) + direct
    draw = inv * (dlatent - latent * jnp.sum(latent * dlatent, axis=0, keepdims=True))
    small[0:32, :] = dot_full(draw, lnv)
    dln = dot_full(draw.T, in_t[...])
    small[64:65, :] = jnp.sum(dln * xhat, axis=0, keepdims=True)
    small[65:66, :] = jnp.sum(dln, axis=0, keepdims=True)
    de[...] = ln_back(dln, xhat, inv_ln, gain[...])
    for copy in copies:
        copy.wait()


SMEM = pl.BlockSpec(memory_space=pltpu.SMEM)
VMEM = pl.BlockSpec(memory_space=pltpu.VMEM)
ANY = pl.BlockSpec(memory_space=pl.ANY)


def shaped(*pairs):
    return [jax.ShapeDtypeStruct(shape, dtype) for shape, dtype in pairs]


def call(kernel, name, in_specs, out_specs, outs, scratch, flops, moved, after=(), carry=()):
    n_in, n_extra, n_out = len(in_specs), len(after) + len(carry), len(outs)

    def body(*refs):
        first = n_in + n_extra
        kernel(*refs[:n_in], *refs[first : first + n_out], *refs[first + n_out + len(carry) :])

    made = pl.pallas_call(
        body,
        name=name,
        in_specs=in_specs + [ANY] * n_extra,
        out_specs=out_specs + [ANY] * len(carry),
        out_shape=outs + [jax.ShapeDtypeStruct(a.shape, a.dtype) for a in carry],
        scratch_shapes=scratch,
        input_output_aliases={n_in + len(after) + i: n_out + i for i in range(len(carry))},
        compiler_params=pltpu.CompilerParams(vmem_limit_bytes=vmem_cap),
        cost_estimate=pl.CostEstimate(flops=flops, bytes_accessed=moved, transcendentals=0),
    )

    def run(*args):
        res = made(*args, *after, *carry)
        return (*res[:n_out], list(res[n_out:]))

    return run


DMA = pltpu.SemaphoreType.DMA
ROWS2 = (512, 512)


def attn_fwd(ids, x, seg, gain, bias, quads, first, after=(), carry=()):
    outs = shaped(
        (ROWS2, f32),
        *[(ROWS2, bf16)] * 7,
        ((8, 512), f32),
        ((2, 512, 1024), bf16),
    )
    scratch = [
        pltpu.VMEM((2, 512, 1024), bf16),
        pltpu.VMEM(ROWS2, bf16),
        pltpu.VMEM(ROWS2, bf16),
        pltpu.VMEM(ROWS2, f32),
        DMA((32,)),
        DMA,
    ]
    return call(
        functools.partial(attn_fwd_kernel, first),
        "attn_fwd",
        [SMEM] + [VMEM] * 4 + [ANY] * 8,
        [VMEM] * 9 + [ANY],
        outs,
        scratch,
        10**10,
        10**7,
        after,
        carry,
    )(ids, x, seg, gain, bias, *quads)


def mlp_fwd(ids, x1, gain, bias, quads, first, after=(), carry=()):
    return call(
        functools.partial(mlp_fwd_kernel, first),
        "mlp_fwd",
        [SMEM] + [VMEM] * 3 + [ANY] * 8,
        [VMEM, ANY],
        shaped((ROWS2, f32), ((2, 512, 2048), bf16)),
        [pltpu.VMEM((2, 512, 2048), bf16), pltpu.VMEM(ROWS2, bf16), DMA((32,)), DMA],
        8 * 10**9,
        10**7,
        after,
        carry,
    )(ids, x1, gain, bias, *quads)


def mlp_bwd(ids, x1, dy, gain, bias, w, after=(), carry=()):
    outs = shaped((ROWS2, f32), ((8, 512), f32), *[((4, 4, 32, 2048), bf16)] * 2)
    scratch = [
        pltpu.VMEM((2, 512, 2048), bf16),
        pltpu.VMEM((2, 512, 2048), bf16),
        *[pltpu.VMEM(ROWS2, bf16)] * 4,
        pltpu.VMEM(ROWS2, f32),
        DMA,
        DMA((32,)),
    ]
    return call(
        mlp_bwd_kernel,
        "mlp_bwd",
        [SMEM] + [VMEM] * 4 + [ANY],
        [VMEM] * 2 + [ANY] * 2,
        outs,
        scratch,
        15 * 10**9,
        2 * 10**7,
        after,
        carry,
    )(ids, x1, dy, gain, bias, w)


def attn_bwd(ids, x, dx1, seg, gain, bias, saved, w, after=(), carry=()):
    outs = shaped((ROWS2, f32), ((8, 512), f32), *[((4, 4, 32, 1024), bf16)] * 2)
    scratch = [
        pltpu.VMEM((2, 512, 1024), bf16),
        pltpu.VMEM((2, 512, 1024), bf16),
        pltpu.VMEM(ROWS2, bf16),
        pltpu.VMEM(ROWS2, f32),
        pltpu.VMEM(ROWS2, bf16),
        pltpu.VMEM(ROWS2, bf16),
        pltpu.VMEM((8, 512), f32),
        *[pltpu.VMEM(ROWS2, bf16)] * 5,
        DMA,
        DMA((32,)),
    ]
    return call(
        attn_bwd_kernel,
        "attn_bwd",
        [SMEM] + [VMEM] * 13 + [ANY],
        [VMEM] * 2 + [ANY] * 2,
        outs,
        scratch,
        15 * 10**9,
        2 * 10**7,
        after,
        carry,
    )(ids, x, dx1, seg, gain, bias, *saved, w)


def code_prep(book_t, after=(), carry=()):
    codes = book_t.shape[1]
    return call(
        code_prep_kernel,
        "code_prep",
        [VMEM],
        [VMEM] * 2,
        shaped(((codes, 256), bf16), ((128, codes), bf16)),
        [],
        6 * 10**9,
        10**7,
        after,
        carry,
    )(book_t)


def vq_fwd(e, gain, bias, in_t, out_w, stack, stack_t, after=(), carry=()):
    return call(
        vq_fwd_kernel,
        "vq_fwd",
        [VMEM] * 7,
        [VMEM] * 2,
        shaped((ROWS2, f32), ((72, 512), f32)),
        [pltpu.VMEM((128, 512), f32)],
        15 * 10**9,
        10**7,
        after,
        carry,
    )(e, gain, bias, in_t, out_w, stack, stack_t)


def vq_bwd(ids, e, du, gain, bias, in_t, out_w, stack, stack_t, book_t, kept, after=(), carry=()):
    codes = book_t.shape[1]
    outs = shaped((ROWS2, f32), ((72, 512), f32), *[((32, codes // 2), bf16)] * 2)
    return call(
        vq_bwd_kernel,
        "vq_bwd",
        [SMEM] + [VMEM] * 10,
        [VMEM] * 2 + [ANY] * 2,
        outs,
        [pltpu.VMEM((96, 512), f32), pltpu.VMEM((32, codes), bf16), DMA((2,))],
        25 * 10**9,
        2 * 10**7,
        after,
        carry,
    )(ids, e, du, gain, bias, in_t, out_w, stack, stack_t, book_t, kept)


def near_kernel(ids, ins, outs):
    keep, other = ins
    outs[0][...] = keep[0].astype(f32) + other[0].astype(f32)
    for i in range(1, 4):
        outs[i][...] = (keep[i].astype(f32) + other[i].astype(f32)).astype(bf16)


def near_task(keep, other):
    shape = keep.shape[1:]
    return near_kernel, [keep, other], shaped((shape, f32), *[(shape, bf16)] * 3)


def plane_kernel(ids, ins, outs):
    for k in range(4):
        total = ins[0][k]
        for other in ins[1:]:
            total = total + other[k].astype(f32)
        outs[k][...] = total.astype(outs[k].dtype)


def plane_task(own, others):
    shape = own.shape[1:]
    return plane_kernel, [own, *others], shaped((shape, f32), *[(shape, bf16)] * 3)


def line_total(ins):
    total = ins[0][...]
    for other in ins[1:]:
        total = total + other[...].astype(f32)
    return total


def add_kernel(ids, ins, outs):
    outs[0][...] = (ins[0][...].astype(f32) + ins[1][...].astype(f32)).astype(outs[0].dtype)


def add_task(a, b):
    return add_kernel, [a, b], shaped((a.shape, a.dtype))


def tree_kernel(ids, ins, outs):
    outs[0][...] = (ins[0][...] + ins[1][...]) + (ins[2][...] + ins[3][...])


def tree_task(*arrays):
    return tree_kernel, list(arrays), shaped((arrays[0].shape, arrays[0].dtype))


def rows_kernel(ids, ins, outs):
    own, other = ins
    half = other.shape[0]
    outs[0][ids[1]] = own[0:half, :].astype(f32)
    outs[0][1 - ids[1]] = other[...].astype(f32)


def rows_task(own, other):
    return rows_kernel, [own, other], shaped(((2, *other.shape), f32))


def attn_kernel(ids, ins, outs):
    total = line_total(ins)
    for index in range(3):
        outs[0][index] = total[:, index * 256 : (index + 1) * 256]
    outs[1][...] = total[:, 768:]


def attn_task(own, others):
    return attn_kernel, [own, *others], shaped(((3, 32, 256), f32), ((32, 256), f32))


def mlp_kernel(ids, ins, outs):
    total = line_total(ins)
    outs[0][...] = total[:, :1024]
    outs[1][...] = total[:, 1024:]


def mlp_task(own, others):
    return mlp_kernel, [own, *others], shaped(*[((32, 1024), f32)] * 2)


def code_kernel(ids, ins, outs):
    core = ids[0] % 2
    low, other = ins
    half = low.shape[1]
    for at, part in ((core, low), (1 - core, other)):
        lanes = pl.ds(pl.multiple_of(at * half, half), half)
        outs[0][:, lanes] = part[...].astype(f32)


def code_task(low, other):
    return code_kernel, [low, other], shaped(((32, 2 * low.shape[1]), f32))


def run_tasks(ids, name, tasks, after=(), carry=()):
    sizes = [(len(ins), len(outs)) for _, ins, outs in tasks]
    n_in = sum(i for i, _ in sizes)

    def kernel(ids_ref, *refs):
        at_in, at_out = 0, n_in
        for (fn, _, _), (i, o) in zip(tasks, sizes):
            fn(ids_ref, refs[at_in : at_in + i], refs[at_out : at_out + o])
            at_in, at_out = at_in + i, at_out + o

    outs = [one for _, _, many in tasks for one in many]
    res = call(
        kernel, name, [SMEM] + [VMEM] * n_in, [VMEM] * len(outs), outs, [], 10**9, 10**7, after, carry
    )(ids, *[one for _, many, _ in tasks for one in many])
    split, at = [], 0
    for _, o in sizes:
        split.append(res[at : at + o])
        at += o
    return (*split, res[-1])


def whole_groups(
    n_dp,
    tokens,
    segment_ids,
    norm_gains,
    norm_biases,
    w_qkv,
    w_attn_out,
    w_up,
    w_down,
    w_vq_in,
    w_vq_out,
    codebook,
    cotangent,
):
    dp_at, tp_at = lax.axis_index("dp"), lax.axis_index("tp")
    ids = jnp.stack([dp_at, tp_at]).astype(jnp.int32)
    rows = tokens.shape[1]

    def mine(values):
        return lax.dynamic_index_in_dim(values, tp_at, 0, keepdims=False)

    def theirs(values):
        return lax.dynamic_index_in_dim(values, 1 - tp_at, 0, keepdims=False)

    def swap(values):
        return exchange(values, 0, 1, n_dp)

    marked = jnp.concatenate(
        [tokens, jnp.broadcast_to(segment_ids[..., None].astype(bf16), (MICRO, rows, 128))], axis=2
    )
    marked = jnp.concatenate([mine(marked), swap(theirs(marked))], axis=0)
    x, seg = marked[:, : tokens.shape[2]], marked[:, tokens.shape[2] :]
    gains = [norm_gains[i : i + 1] for i in range(5)]
    biases = [norm_biases[i : i + 1] for i in range(5)]

    attn_shards, mlp_shards = [], []
    for layer in range(2):
        attn_shards.append(
            jnp.concatenate(
                [w_qkv[layer, 0], w_qkv[layer, 1], w_qkv[layer, 2], w_attn_out[layer].T], axis=1
            )
        )
        mlp_shards.append(jnp.concatenate([w_up[layer], w_down[layer].T], axis=1))
    book_t, in_t = codebook.T, w_vq_in.T
    enc_attn_line = spread_line(attn_shards[0], n_dp)
    enc_mlp_line = spread_line(mlp_shards[0], n_dp)
    enc_attn = spread_plane(enc_attn_line, n_dp)
    stack, stack_t, dec_shards = code_prep(
        book_t, [enc_attn_line, enc_mlp_line], [attn_shards[1], mlp_shards[1]]
    )
    enc_mlp = spread_plane(enc_mlp_line, n_dp)
    dec_lines = [spread_line(shard, n_dp) for shard in dec_shards]

    e_x1, *e_saved, e_wa, dec_lines = attn_fwd(
        ids, x, seg, gains[0], biases[0], enc_attn, 0, carry=dec_lines
    )
    dec_attn, dec_mlp = [spread_plane(line, n_dp) for line in dec_lines]
    e, e_wm, _ = mlp_fwd(ids, e_x1, gains[1], biases[1], enc_mlp, 0)
    u, kept, (cot,) = vq_fwd(
        e, gains[2], biases[2], in_t, w_vq_out, stack, stack_t, carry=[theirs(cotangent)]
    )
    cot_other = swap(cot)
    d_x1, *d_saved, d_wa, _ = attn_fwd(ids, u, seg, gains[3], biases[3], dec_attn, 0)
    y, d_wm, _ = mlp_fwd(ids, d_x1, gains[4], biases[4], dec_mlp, 0, [cot_other])
    y_other = swap(y[rows:])
    dy = jnp.concatenate([mine(cotangent), cot_other], axis=0)

    dx1, d_small1, keep_m, send_m, _ = mlp_bwd(ids, d_x1, dy, gains[4], biases[4], d_wm)
    near_m = exchange(send_m, 1, 0, n_dp)
    du, d_small0, keep_a, send_a, (keep_m,) = attn_bwd(
        ids, u, dx1, seg, gains[3], biases[3], d_saved, d_wa, carry=[keep_m]
    )
    near_a = exchange(send_a, 1, 0, n_dp)
    (own_m, *lows_m), (decoded,), _ = run_tasks(
        ids, "sums1", [near_task(keep_m, near_m), rows_task(y, y_other)]
    )
    plane_m = plane_send(lows_m, n_dp)
    de, v_small, code_keep, code_send, (own_m, keep_a) = vq_bwd(
        ids,
        e,
        du,
        gains[2],
        biases[2],
        in_t,
        w_vq_out,
        stack,
        stack_t,
        book_t,
        kept,
        lows_m,
        [own_m, keep_a],
    )
    (own_m, *lows_m), (own_a, *lows_a), _ = run_tasks(
        ids, "sums2", [plane_task(own_m, plane_m), near_task(keep_a, near_a)]
    )
    line_m, plane_a = line_send(lows_m, n_dp), plane_send(lows_a, n_dp)
    code_near = exchange(code_send, 1, 0, n_dp)
    ex1, e_small1, keep_em, send_em, (own_m, own_a, code_keep) = mlp_bwd(
        ids,
        e_x1,
        de,
        gains[1],
        biases[1],
        e_wm,
        lows_m + lows_a,
        [own_m, own_a, code_keep],
    )
    near_em = exchange(send_em, 1, 0, n_dp)
    d_mlp, (own_a, *lows_a), (code,), _ = run_tasks(
        ids,
        "sums3",
        [mlp_task(own_m, line_m), plane_task(own_a, plane_a), add_task(code_keep, code_near)],
    )
    line_a, code_other = line_send(lows_a, n_dp), exchange(code, 0, 1, n_dp)
    dx, e_small0, keep_ea, send_ea, (own_a, keep_em) = attn_bwd(
        ids,
        x,
        ex1,
        seg,
        gains[0],
        biases[0],
        e_saved,
        e_wa,
        lows_a,
        [own_a, keep_em],
    )
    small = jnp.concatenate(
        [v_small[:66], e_small0[:2], e_small1[:2], d_small0[:2], d_small1[:2]], axis=0
    )
    near_ea = exchange(send_ea, 1, 0, n_dp)
    dx_other = swap(dx[rows:].astype(bf16))
    (own_m, *lows_m), d_attn, (code,), (keep_ea,) = run_tasks(
        ids,
        "sums4",
        [near_task(keep_em, near_em), attn_task(own_a, line_a), add_task(code, code_other)],
        carry=[keep_ea],
    )
    plane_m, code_other = plane_send(lows_m, n_dp), exchange(code, 2, 0, n_dp)
    small_other = exchange(small, 1, 0, n_dp)
    (own_a, *lows_a), (code,), (small,), (own_m,) = run_tasks(
        ids,
        "sums5",
        [near_task(keep_ea, near_ea), add_task(code, code_other), add_task(small, small_other)],
        carry=[own_m],
    )
    plane_a, code_other = plane_send(lows_a, n_dp), exchange(code, 4, 0, n_dp)
    small_other = exchange(small, 0, 1, n_dp)
    (own_m, *lows_m), (code,), (small,), (own_a,) = run_tasks(
        ids,
        "sums6",
        [plane_task(own_m, plane_m), add_task(code, code_other), add_task(small, small_other)],
        carry=[own_a],
    )
    line_m, code_other = line_send(lows_m, n_dp), exchange(code, 8, 0, n_dp)
    smalls = [exchange(small, dp_xor, 0, n_dp) for dp_xor in (2, 4, 6)]
    (own_a, *lows_a), (code,), (small,), (own_m,) = run_tasks(
        ids,
        "sums7",
        [plane_task(own_a, plane_a), add_task(code, code_other), tree_task(small, *smalls)],
        carry=[own_m],
    )
    line_a, code_other = line_send(lows_a, n_dp), exchange(code, 1, 0, n_dp)
    small_other = exchange(small, 8, 0, n_dp)
    e_mlp, e_attn, (grad_code,), (grad_tokens,), (small,), _ = run_tasks(
        ids,
        "sums8",
        [
            mlp_task(own_m, line_m),
            attn_task(own_a, line_a),
            code_task(code, code_other),
            rows_task(dx, dx_other),
            add_task(small, small_other),
        ],
    )
    qkv, out_t, up, down_t = [jnp.stack(pair) for pair in zip((*e_attn, *e_mlp), (*d_attn, *d_mlp))]
    gain_rows = [small[66], small[68], small[64], small[70], small[72]]
    bias_rows = [small[67], small[69], small[65], small[71], small[73]]
    return (
        decoded,
        grad_tokens,
        jnp.stack(gain_rows),
        jnp.stack(bias_rows[:3]),
        jnp.stack(bias_rows[3:]),
        qkv,
        out_t.transpose(0, 2, 1),
        up,
        down_t.transpose(0, 2, 1),
        small[0:32].T,
        small[32:64],
        grad_code.T,
    )


def layer_norm(values, norm_gain, norm_bias):
    centred = values - jnp.mean(values, axis=-1, keepdims=True)
    spread = jnp.mean(centred * centred, axis=-1, keepdims=True)
    return centred * lax.rsqrt(spread + ln_eps) * norm_gain + norm_bias


def gelu_tanh(values):
    return (
        0.5 * values * (1.0 + jnp.tanh(gelu_coef * (values + 0.044715 * values * values * values)))
    )


def matmul(former, latter):
    return jnp.dot(former, latter, precision=highest, preferred_element_type=jnp.float32)


def normalize(values):
    return values * lax.rsqrt(jnp.sum(values * values, axis=-1, keepdims=True) + norm_eps)


def quantize(in_rows, norm_gain, norm_bias, in_w, out_w, code_w):
    latent = normalize(matmul(layer_norm(in_rows, norm_gain, norm_bias), in_w))
    code_rows = normalize(code_w)
    logits = matmul(latent, code_rows.T) * temper
    row_max = jnp.max(logits, axis=-1, keepdims=True)
    numerator = jnp.exp(logits - row_max)
    assign = numerator / jnp.sum(numerator, axis=-1, keepdims=True)
    soft_code = matmul(assign, code_rows)
    offset = latent - soft_code
    vq_loss = commit_weight * 1.25 * jnp.sum(offset * offset)
    return (matmul(soft_code, out_w), vq_loss)


def product(former, latter):
    return jnp.dot(former, latter, preferred_element_type=jnp.float32)


def product_tn(former, latter):
    return lax.dot_general(
        former, latter, (((0,), (0,)), ((), ())), preferred_element_type=jnp.float32
    )


def product_nt(former, latter):
    return lax.dot_general(
        former, latter, (((1,), (1,)), ((), ())), preferred_element_type=jnp.float32
    )


def split_heads(values):
    return values.reshape(values.shape[0], values.shape[1] // HEAD_DIM, HEAD_DIM).transpose(1, 0, 2)


def join_heads(values):
    return values.transpose(1, 0, 2).reshape(values.shape[1], values.shape[0] * HEAD_DIM)


def masked_scores(query_blk, key_h, seg_blk, seg_keys):
    scores = jnp.einsum(
        "hqd,hkd->hqk", query_blk, key_h, preferred_element_type=jnp.float32
    ) * HEAD_DIM ** (-0.5)
    return jnp.where((seg_blk[:, None] == seg_keys[None, :])[None], scores, masked_score)


def attend(query_h, key_h, value_h, seg_keys):
    block_rows = min(512, query_h.shape[1])
    block_count = query_h.shape[1] // block_rows

    def one_block(begin_row):
        query_blk = lax.dynamic_slice_in_dim(query_h, begin_row, block_rows, 1)
        seg_blk = lax.dynamic_slice_in_dim(seg_keys, begin_row, block_rows, 0)
        scores = masked_scores(query_blk, key_h, seg_blk, seg_keys)
        row_max = jnp.max(scores, axis=-1, keepdims=True)
        numerator = jnp.exp(scores - row_max)
        row_total = jnp.sum(numerator, axis=-1, keepdims=True)
        prob_low = (numerator / row_total).astype(jnp.bfloat16)
        attended = jnp.einsum("hqk,hkd->hqd", prob_low, value_h, preferred_element_type=jnp.float32)
        return (attended.astype(jnp.bfloat16), (row_max + jnp.log(row_total))[..., 0])

    starts = jnp.arange(block_count, dtype=jnp.int32) * block_rows
    attended, log_sums = lax.map(one_block, starts)
    heads_out = attended.transpose(1, 0, 2, 3).reshape(query_h.shape)
    log_sums = log_sums.transpose(1, 0, 2).reshape(query_h.shape[0], query_h.shape[1])
    return (heads_out, log_sums)


def attend_back(query_h, key_h, value_h, seg_keys, log_sums, grad_out):
    block_rows = min(512, query_h.shape[1])
    block_count = query_h.shape[1] // block_rows

    def one_block(carry, begin_row):
        grad_key, grad_value = carry
        query_blk = lax.dynamic_slice_in_dim(query_h, begin_row, block_rows, 1)
        grad_blk = lax.dynamic_slice_in_dim(grad_out, begin_row, block_rows, 1)
        lse_blk = lax.dynamic_slice_in_dim(log_sums, begin_row, block_rows, 1)
        seg_blk = lax.dynamic_slice_in_dim(seg_keys, begin_row, block_rows, 0)
        scores = masked_scores(query_blk, key_h, seg_blk, seg_keys)
        probs = jnp.exp(scores - lse_blk[..., None])
        prob_low = probs.astype(jnp.bfloat16)
        grad_value = grad_value + jnp.einsum(
            "hqk,hqd->hkd", prob_low, grad_blk, preferred_element_type=jnp.float32
        )
        grad_prob = jnp.einsum(
            "hqd,hkd->hqk", grad_blk, value_h, preferred_element_type=jnp.float32
        )
        row_dot = jnp.sum(probs * grad_prob, axis=-1, keepdims=True)
        grad_score = (probs * (grad_prob - row_dot) * HEAD_DIM ** (-0.5)).astype(jnp.bfloat16)
        grad_query = jnp.einsum(
            "hqk,hkd->hqd", grad_score, key_h, preferred_element_type=jnp.float32
        )
        grad_key = grad_key + jnp.einsum(
            "hqk,hqd->hkd", grad_score, query_blk, preferred_element_type=jnp.float32
        )
        return ((grad_key, grad_value), grad_query)

    starts = jnp.arange(block_count, dtype=jnp.int32) * block_rows
    zeros_kv = jnp.zeros(key_h.shape, jnp.float32)
    (grad_key, grad_value), grad_query = lax.scan(one_block, (zeros_kv, zeros_kv), starts)
    grad_query = grad_query.transpose(1, 0, 2, 3).reshape(query_h.shape)
    return (
        grad_query.astype(jnp.bfloat16),
        grad_key.astype(jnp.bfloat16),
        grad_value.astype(jnp.bfloat16),
    )


def spread_rows(values):
    return lax.all_gather(values, "tp", axis=0, tiled=True)


def combine_rows(partial_value):
    return lax.psum_scatter(partial_value, "tp", scatter_dimension=0, tiled=True)


def spread_grads(values):
    return lax.all_gather(values, "tp", axis=0, tiled=True)


def combine_grads(partial_value):
    return lax.psum_scatter(
        partial_value.astype(jnp.bfloat16), "tp", scatter_dimension=0, tiled=True
    ).astype(jnp.float32)


def fetch_weights(w_qkv, w_attn_out, w_up, w_down, layer):
    return (
        lax.all_gather(w_qkv[layer], "dp", axis=1, tiled=True),
        lax.all_gather(w_attn_out[layer], "dp", axis=1, tiled=True),
        lax.all_gather(w_up[layer], "dp", axis=0, tiled=True),
        lax.all_gather(w_down[layer], "dp", axis=1, tiled=True),
    )


def reduce_weight_grads(grads):
    return (
        lax.psum_scatter(
            grads[0].astype(jnp.bfloat16), "dp", scatter_dimension=1, tiled=True
        ).astype(jnp.float32),
        lax.psum_scatter(
            grads[1].astype(jnp.bfloat16), "dp", scatter_dimension=1, tiled=True
        ).astype(jnp.float32),
        lax.psum_scatter(
            grads[2].astype(jnp.bfloat16), "dp", scatter_dimension=0, tiled=True
        ).astype(jnp.float32),
        lax.psum_scatter(
            grads[3].astype(jnp.bfloat16), "dp", scatter_dimension=1, tiled=True
        ).astype(jnp.float32),
    )


def block_forward(resid_in, seg_local, gains, biases, weights):
    qkv_w, attn_w, up_w, down_w = weights
    normed = layer_norm(resid_in, gains[0], biases[0]).astype(jnp.bfloat16)
    normed_all, seg_all = (
        lax.all_gather(normed, "tp", axis=0, tiled=True),
        lax.all_gather(seg_local, "tp", axis=0, tiled=True),
    )
    query_h = split_heads(product(normed_all, qkv_w[0]).astype(jnp.bfloat16))
    key_h = split_heads(product(normed_all, qkv_w[1]).astype(jnp.bfloat16))
    value_h = split_heads(product(normed_all, qkv_w[2]).astype(jnp.bfloat16))
    heads_out, log_sums = attend(query_h, key_h, value_h, seg_all)
    attn_rows = join_heads(heads_out)
    middle = resid_in + combine_rows(product(attn_rows, attn_w))
    normed_mid = spread_rows(layer_norm(middle, gains[1], biases[1]).astype(jnp.bfloat16))
    hidden_pre = product(normed_mid, up_w)
    hidden = gelu_tanh(hidden_pre).astype(jnp.bfloat16)
    result = middle + combine_rows(product(hidden, down_w))
    kept = (
        resid_in,
        middle,
        normed_all,
        seg_all,
        query_h,
        key_h,
        value_h,
        log_sums,
        attn_rows,
        normed_mid,
        hidden_pre,
        hidden,
    )
    return (result, kept)


def block_backward(kept, gains, biases, weights, grad_result):
    (
        resid_in,
        middle,
        normed_all,
        seg_all,
        query_h,
        key_h,
        value_h,
        log_sums,
        attn_rows,
        normed_mid,
        hidden_pre,
        hidden,
    ) = kept
    qkv_w, attn_w, up_w, down_w = weights
    grad_branch = spread_grads(grad_result.astype(jnp.bfloat16))
    grad_down = product_tn(hidden, grad_branch)
    grad_hidden = product_nt(grad_branch, down_w)
    _, gelu_back = jax.vjp(gelu_tanh, hidden_pre)
    grad_pre = gelu_back(grad_hidden)[0].astype(jnp.bfloat16)
    grad_up = product_tn(normed_mid, grad_pre)
    grad_norm_mid = combine_grads(product_nt(grad_pre, up_w))
    _, norm_back_mid = jax.vjp(layer_norm, middle, gains[1], biases[1])
    grad_mid_ln, grad_gain_mid, grad_bias_mid = norm_back_mid(grad_norm_mid)
    grad_middle = grad_result + grad_mid_ln
    grad_attn_all = spread_grads(grad_middle.astype(jnp.bfloat16))
    grad_attn = product_tn(attn_rows, grad_attn_all)
    grad_heads = split_heads(product_nt(grad_attn_all, attn_w).astype(jnp.bfloat16))
    grad_query, grad_key, grad_value = attend_back(
        query_h, key_h, value_h, seg_all, log_sums, grad_heads
    )
    grad_parts = [join_heads(grad_query), join_heads(grad_key), join_heads(grad_value)]
    grad_qkv = jnp.stack([product_tn(normed_all, grad_part) for grad_part in grad_parts])
    grad_normed_part = (
        product_nt(grad_parts[0], qkv_w[0])
        + product_nt(grad_parts[1], qkv_w[1])
        + product_nt(grad_parts[2], qkv_w[2])
    )
    grad_normed = combine_grads(grad_normed_part)
    _, norm_back_in = jax.vjp(layer_norm, resid_in, gains[0], biases[0])
    grad_in_ln, grad_gain_in, grad_bias_in = norm_back_in(grad_normed)
    gain_grads = jnp.stack([grad_gain_in, grad_gain_mid])
    bias_grads = jnp.stack([grad_bias_in, grad_bias_mid])
    return (
        grad_middle + grad_in_ln,
        gain_grads,
        bias_grads,
        (grad_qkv, grad_attn, grad_up, grad_down),
    )


def local(
    tokens,
    segment_ids,
    norm_gains,
    norm_biases,
    w_qkv,
    w_attn_out,
    w_up,
    w_down,
    w_vq_in,
    w_vq_out,
    codebook,
    cotangent,
):
    gain_sum = jnp.zeros(norm_gains.shape, jnp.float32)
    bias_sum = jnp.zeros(norm_biases.shape, jnp.float32)
    vq_in_sum = jnp.zeros(w_vq_in.shape, jnp.float32)
    vq_out_sum = jnp.zeros(w_vq_out.shape, jnp.float32)
    code_sum = jnp.zeros(codebook.shape, jnp.float32)
    layer_sums = [None, None]
    outputs = []
    input_grads = []
    for micro in range(MICRO):
        resid_in = tokens[micro].astype(jnp.float32)
        seg_local = segment_ids[micro]
        enc_weights = fetch_weights(w_qkv, w_attn_out, w_up, w_down, 0)
        encoded, enc_kept = block_forward(
            resid_in, seg_local, norm_gains[0:2], norm_biases[0:2], enc_weights
        )
        (decoder_in, _), vq_back = jax.vjp(
            quantize, encoded, norm_gains[2], norm_biases[2], w_vq_in, w_vq_out, codebook
        )
        dec_weights = fetch_weights(w_qkv, w_attn_out, w_up, w_down, 1)
        decoded, dec_kept = block_forward(
            decoder_in, seg_local, norm_gains[3:5], norm_biases[3:5], dec_weights
        )
        outputs.append(decoded)
        grad_dec_in, gains_dec, biases_dec, grads_dec = block_backward(
            dec_kept, norm_gains[3:5], norm_biases[3:5], dec_weights, cotangent[micro]
        )
        grad_encoded, grad_gain_vq, grad_bias_vq, grad_in_w, grad_out_w, grad_codes = vq_back(
            (grad_dec_in, jnp.ones((), jnp.float32))
        )
        grad_input, gains_enc, biases_enc, grads_enc = block_backward(
            enc_kept, norm_gains[0:2], norm_biases[0:2], enc_weights, grad_encoded
        )
        input_grads.append(grad_input)
        gain_sum = gain_sum + jnp.concatenate([gains_enc, grad_gain_vq[None], gains_dec], axis=0)
        bias_sum = bias_sum + jnp.concatenate([biases_enc, grad_bias_vq[None], biases_dec], axis=0)
        vq_in_sum = vq_in_sum + grad_in_w
        vq_out_sum = vq_out_sum + grad_out_w
        code_sum = code_sum + grad_codes
        for layer, grads in ((0, grads_enc), (1, grads_dec)):
            reduced = reduce_weight_grads(grads)
            if layer_sums[layer] is None:
                layer_sums[layer] = reduced
            else:
                layer_sums[layer] = jax.tree.map(jnp.add, layer_sums[layer], reduced)
    gain_tot, bias_tot, vq_in_tot, vq_out_tot, code_tot = lax.psum(
        (gain_sum, bias_sum, vq_in_sum, vq_out_sum, code_sum), ("dp", "tp")
    )
    return (
        jnp.stack(outputs),
        jnp.stack(input_grads),
        gain_tot,
        bias_tot[0:3],
        bias_tot[3:5],
        jnp.stack([layer_sums[0][0], layer_sums[1][0]]),
        jnp.stack([layer_sums[0][1], layer_sums[1][1]]),
        jnp.stack([layer_sums[0][2], layer_sums[1][2]]),
        jnp.stack([layer_sums[0][3], layer_sums[1][3]]),
        vq_in_tot,
        vq_out_tot,
        code_tot,
    )


def solution(mesh):
    n_dp, n_tp = mesh.shape["dp"], mesh.shape["tp"]
    fits = n_tp == MICRO and n_dp == 16
    return jax.shard_map(
        functools.partial(whole_groups, n_dp) if fits else local,
        mesh=mesh,
        in_specs=(
            P(None, ("dp", "tp"), None),
            P(None, ("dp", "tp")),
            P(),
            P(),
            P(None, None, "dp", "tp"),
            P(None, "tp", "dp"),
            P(None, "dp", "tp"),
            P(None, "tp", "dp"),
            P(),
            P(),
            P(),
            P(None, ("dp", "tp"), None),
        ),
        out_specs=(
            P(None, ("dp", "tp"), None),
            P(None, ("dp", "tp"), None),
            P(),
            P(),
            P(),
            P(None, None, "dp", "tp"),
            P(None, "tp", "dp"),
            P(None, "dp", "tp"),
            P(None, "tp", "dp"),
            P(),
            P(),
            P(),
        ),
        check_vma=False,
    )
```

```python
import functools

import jax
import jax.numpy as jnp
from jax import lax
from jax.experimental import pallas as pl
from jax.experimental.pallas import tpu as pltpu
from jax.sharding import PartitionSpec as P

HEAD_DIM = 64
MICRO = 2
bf16 = jnp.bfloat16
f32 = jnp.float32
highest = lax.Precision.HIGHEST
ln_eps = 1e-05
norm_eps = 1e-06
temper = 10.0
commit_weight = 64.0
gelu_coef = 0.7978845608028654
masked_score = -1e30
log2e = 1.4426950408889634
vmem_cap = 60 * 1024 * 1024


PLANE = ((0, 0), (0, 1), (1, 0), (1, 1))


def exchange(values, dp_xor, tp_xor, n_dp):
    pairs = [
        (d * 2 + t, (d ^ dp_xor) * 2 + (t ^ tp_xor)) for d in range(n_dp) for t in range(2)
    ]
    return lax.ppermute(values, ("dp", "tp"), pairs)


def spread_line(shard, n_dp):
    return jnp.stack([shard] + [exchange(shard, 4 * k, 0, n_dp) for k in range(1, 4)])


def plane_quads(own, n_dp):
    return [own] + [exchange(own, 2 * y, x, n_dp) for y, x in PLANE[1:]]


def core_quads(quads, n_dp):
    return quads + [exchange(quad, 1, 0, n_dp) for quad in quads]


def near_send(sends, n_dp):
    return [exchange(send, 1, 0, n_dp) for send in sends]


def plane_send(lows, n_dp):
    return [exchange(low, 2 * y, x, n_dp) for (y, x), low in zip(PLANE[1:], lows)]


def line_send(lows, n_dp):
    return [exchange(low, 4 * k, 0, n_dp) for k, low in zip(range(1, 4), lows)]


def block_places():
    for core in range(2):
        for index, (y, x) in enumerate(PLANE):
            for k in range(4):
                yield core * 4 + index, k, k * 4 + y * 2 + core, x


def dot(a, b):
    return jnp.dot(a, b, preferred_element_type=f32)


def dot_nt(a, b, precision=None):
    return lax.dot_general(
        a, b, (((1,), (1,)), ((), ())), preferred_element_type=f32, precision=precision
    )


def dot_full(a, b):
    return jnp.dot(a, b, preferred_element_type=f32, precision=highest)


def ln_parts(x):
    centred = x - jnp.mean(x, axis=-1, keepdims=True)
    inv = lax.rsqrt(jnp.mean(centred * centred, axis=-1, keepdims=True) + ln_eps)
    return centred * inv, inv


def ln_back(grad, xhat, inv, gain):
    scaled = grad * gain
    return inv * (
        scaled
        - jnp.mean(scaled, axis=-1, keepdims=True)
        - xhat * jnp.mean(scaled * xhat, axis=-1, keepdims=True)
    )


def split2(x):
    hi = x.astype(bf16)
    return hi, (x - hi.astype(f32)).astype(bf16)


def split3(x):
    hi, _ = split2(x)
    rest = x - hi.astype(f32)
    mid = rest.astype(bf16)
    return hi, mid, (rest - mid.astype(f32)).astype(bf16)


def weight_copies(ids_ref, quad_refs, w_ref, sems, first):
    width = w_ref.shape[2]
    copies = []
    for slot, (which, k, dp_xor, tp_xor) in enumerate(block_places()):
        row = pl.multiple_of((ids_ref[0] ^ dp_xor) * 32, 32)
        copies.append(
            pltpu.make_async_copy(
                quad_refs[which].at[k, :, pl.ds(first, width)],
                w_ref.at[ids_ref[1] ^ tp_xor, pl.ds(row, 32), :],
                sems.at[slot],
            )
        )
    return copies


def grad_copies(ids_ref, g_ref, quad_refs, sems):
    copies = []
    for slot, (which, k, dp_xor, tp_xor) in enumerate(block_places()):
        row = pl.multiple_of((ids_ref[0] ^ dp_xor) * 32, 32)
        copies.append(
            pltpu.make_async_copy(
                g_ref.at[ids_ref[1] ^ tp_xor, pl.ds(row, 32), :],
                quad_refs[which].at[k],
                sems.at[slot],
            )
        )
    return copies


def head_rows(ref, pair, which):
    own = ref[pl.ds(pl.multiple_of(pair * 128 + which * HEAD_DIM, HEAD_DIM), HEAD_DIM), :]
    zero = jnp.zeros_like(own)
    return jnp.concatenate([own, zero] if which == 0 else [zero, own], axis=0)


def segment_mask(seg):
    ids = seg[...].astype(f32)
    return jnp.where(ids[:, 0:1] == ids.T[0:1, :], 0.0, masked_score)


def attn_fwd_kernel(first, ids, x, seg, gain, bias, *refs):
    quads, refs = refs[:8], refs[8:]
    x1, qs, k, v, o, qst, kt, lse, w_out = refs[:9]
    w, h, vt, ot, mask, sems, out_sem = refs[9:]
    copies = weight_copies(ids, quads, w, sems, first)
    for copy in copies:
        copy.start()
    xf = x[...].astype(f32)
    h[...] = (ln_parts(xf)[0] * gain[...] + bias[...]).astype(bf16)
    mask[...] = segment_mask(seg)
    for copy in copies:
        copy.wait()
    keep = pltpu.make_async_copy(w, w_out, out_sem)
    keep.start()
    for t in range(2):
        cols = pl.ds(t * 256, 256)
        qs[:, cols] = (dot(h[...], w[t, :, 0:256]).astype(bf16) * HEAD_DIM ** (-0.5)).astype(bf16)
        k[:, cols] = dot(h[...], w[t, :, 256:512]).astype(bf16)
        v[:, cols] = dot(h[...], w[t, :, 512:768]).astype(bf16)
    qst[...] = qs[...].T
    kt[...] = k[...].T
    vt[...] = v[...].T

    def one_pair(pair, _):
        lanes = pl.ds(pl.multiple_of(pair * 128, 128), 128)
        k_pair = k[:, lanes]
        for which in range(2):
            scores = dot(k_pair, head_rows(qst, pair, which)) + mask[...]
            top = jnp.max(scores, axis=0, keepdims=True)
            numer = jnp.exp(scores - top).astype(bf16)
            rows = pl.ds(pl.multiple_of(pair * 128 + which * HEAD_DIM, HEAD_DIM), HEAD_DIM)
            left = jnp.concatenate([vt[rows, :], jnp.ones((16, 512), bf16)], axis=0)
            both = dot(left, numer)
            total = both[HEAD_DIM : HEAD_DIM + 1, :]
            ot[rows, :] = (both[:HEAD_DIM, :] / total).astype(bf16)
            lse[pl.ds(pair * 2 + which, 1), :] = top + jnp.log(total)
        return 0

    lax.fori_loop(0, 4, one_pair, 0)
    o[...] = ot[...].T
    acc = xf
    for t in range(2):
        acc = acc + dot_nt(o[:, t * 256 : (t + 1) * 256], w[t, :, 768:1024])
    x1[...] = acc
    keep.wait()


def gelu_parts(u):
    square = u * u
    tanh = jnp.tanh(gelu_coef * u * (1.0 + 0.044715 * square))
    return 0.5 * u * (1.0 + tanh), tanh, square


def mlp_fwd_kernel(first, ids, x1, gain, bias, *refs):
    quads, refs = refs[:8], refs[8:]
    y, theirs, w_out = refs[:3]
    w, h2, sems, out_sem = refs[3:]
    copies = weight_copies(ids, quads, w, sems, first)
    for copy in copies:
        copy.start()
    h2[...] = (ln_parts(x1[...])[0] * gain[...] + bias[...]).astype(bf16)
    y[...] = x1[...]
    for copy in copies:
        copy.wait()
    keep = pltpu.make_async_copy(w, w_out, out_sem)
    keep.start()

    def one_chunk(index, _):
        t = index // 2
        col = (index % 2) * 512
        pre = dot(h2[...], w[t, :, pl.ds(pl.multiple_of(col, 512), 512)])
        hidden = gelu_parts(pre)[0].astype(bf16)
        y[...] += dot_nt(hidden, w[t, :, pl.ds(pl.multiple_of(col + 1024, 512), 512)])
        return 0

    lax.fori_loop(0, 4, one_chunk, 0)
    theirs[...] = y[256:, :]
    keep.wait()


def mlp_bwd_kernel(split, ids, x1, gain, bias, w_hbm, *refs):
    if split:
        own, other, dx1, small = refs[:4]
        refs = refs[4:]
    else:
        dy, dx1, small = refs[:3]
        refs = refs[3:]
    halves, refs = refs[:2], refs[2:]
    w, g, h2, h2t, dyb, dybt, dh2, w_sem, sems = refs[:9]
    if split:
        dy = refs[9]
        dy[0:256, :] = own[ids[1]]
        dy[256:, :] = other[...]
    load = pltpu.make_async_copy(w_hbm, w, w_sem)
    load.start()
    h2[...] = (ln_parts(x1[...])[0] * gain[...] + bias[...]).astype(bf16)
    h2t[...] = h2[...].T
    dyb[...] = dy[...].astype(bf16)
    dybt[...] = dyb[...].T
    dh2[...] = jnp.zeros_like(dh2)
    load.wait()

    def one_chunk(index, _):
        t = index // 2
        up = pl.ds(pl.multiple_of((index % 2) * 512, 512), 512)
        down = pl.ds(pl.multiple_of((index % 2) * 512 + 1024, 512), 512)
        pre = dot(h2[...], w[t, :, up])
        hidden, tanh, square = gelu_parts(pre)
        slope = 0.5 * (1.0 + tanh) + (0.5 * gelu_coef) * pre * (1.0 - tanh * tanh) * (
            1.0 + (3 * 0.044715) * square
        )
        dhidden = dot(dyb[...], w[t, :, down])
        dpre = (dhidden * slope).astype(bf16)
        g[t, :, down] = dot(dybt[...], hidden.astype(bf16)).astype(bf16)
        g[t, :, up] = dot(h2t[...], dpre).astype(bf16)
        dh2[...] += dot_nt(dpre, w[t, :, up])
        return 0

    lax.fori_loop(0, 4, one_chunk, 0)
    copies = grad_copies(ids, g, [half.at[i] for half in halves for i in range(4)], sems)
    for copy in copies:
        copy.start()
    xhat, inv = ln_parts(x1[...])
    grad = dh2[...]
    small[0:1, :] = jnp.sum(grad * xhat, axis=0, keepdims=True)
    small[1:2, :] = jnp.sum(grad, axis=0, keepdims=True)
    dx1[...] = dy[...] + ln_back(grad, xhat, inv, gain[...])
    for copy in copies:
        copy.wait()


def pack_rows(rows):
    cut = [row[:, 128 * j : 128 * (j + 1)] for row in rows for j in range(4)]
    return jnp.concatenate(split2(jnp.concatenate(cut, axis=0)), axis=0)


def attn_bwd_kernel(with_small, ids, x, dx1, seg, gain, bias, qs, k, v, o, qst, kt, lse, w_hbm, *refs):
    if with_small:
        other_small, refs = refs[0], refs[1:]
    dx, dx_low, small = refs[:3]
    keep, sends, refs = refs[3], refs[4:8], refs[8:]
    w, g, h, mask, do, dot_t, dqt, dq, dk, dv, flip, w_sem, sems = refs
    load = pltpu.make_async_copy(w_hbm, w, w_sem)
    load.start()
    xf = x[...].astype(f32)
    h[...] = (ln_parts(xf)[0] * gain[...] + bias[...]).astype(bf16)
    mask[...] = segment_mask(seg)
    low = dx1[...].astype(bf16)
    flip[...] = low.T
    load.wait()
    for t in range(2):
        cols = pl.ds(t * 256, 256)
        do[:, cols] = dot(low, w[t, :, 768:1024]).astype(bf16)
        g[t, :, 768:1024] = dot(flip[...], o[:, cols]).astype(bf16)
    dot_t[...] = do[...].T
    def one_pair(pair, _):
        lanes = pl.ds(pl.multiple_of(pair * 128, 128), 128)
        k_pair, v_pair = k[:, lanes], v[:, lanes]
        q_pair, do_pair = qs[:, lanes], do[:, lanes]
        dvs, dks = [], []
        for which in range(2):
            head = pl.ds(pair * 2 + which, 1)
            rows = pl.ds(pl.multiple_of(pair * 128 + which * HEAD_DIM, HEAD_DIM), HEAD_DIM)
            scores = dot(k_pair, head_rows(qst, pair, which)) + mask[...]
            probs = jnp.exp(scores - lse[head, :])
            dprobs = dot(v_pair, head_rows(dot_t, pair, which))
            shift = jnp.sum(probs * dprobs, axis=0, keepdims=True)
            dscore = (probs * (dprobs - shift)).astype(bf16)
            dvs.append(dot(probs.astype(bf16), do_pair))
            dks.append(dot(dscore, q_pair))
            dqt[rows, :] = (dot(kt[rows, :], dscore) * HEAD_DIM ** (-0.5)).astype(bf16)
        first = lax.broadcasted_iota(jnp.int32, (512, 128), 1) < HEAD_DIM
        dv[:, lanes] = jnp.where(first, dvs[0], dvs[1]).astype(bf16)
        dk[:, lanes] = jnp.where(first, dks[0], dks[1]).astype(bf16)
        return 0

    lax.fori_loop(0, 4, one_pair, 0)
    dq[...] = dqt[...].T
    flip[...] = h[...].T
    for t in range(2):
        cols = pl.ds(t * 256, 256)
        g[t, :, 0:256] = dot(flip[...], dq[:, cols]).astype(bf16)
        g[t, :, 256:512] = dot(flip[...], dk[:, cols]).astype(bf16)
        g[t, :, 512:768] = dot(flip[...], dv[:, cols]).astype(bf16)
    grad = jnp.zeros((512, 512), f32)
    for t in range(2):
        cols = pl.ds(t * 256, 256)
        for index, part in enumerate((dq, dk, dv)):
            grad = grad + dot_nt(part[:, cols], w[t, :, index * 256 : (index + 1) * 256])
    xhat, inv = ln_parts(xf)
    dgain = jnp.sum(grad * xhat, axis=0, keepdims=True)
    dbias = jnp.sum(grad, axis=0, keepdims=True)
    small[0:1, :] = dgain
    small[1:2, :] = dbias
    if with_small:
        packed = pack_rows([dgain, dbias, other_small[0:1, :], other_small[1:2, :]])
        for t in range(2):
            for row in range(16):
                g[t, row * 32 : (row + 1) * 32, 1024:1152] = packed
    copies = grad_copies(ids, g, [keep.at[i] for i in range(4)] + list(sends), sems)
    for copy in copies:
        copy.start()
    total = dx1[...] + ln_back(grad, xhat, inv, gain[...])
    dx[...] = total
    dx_low[...] = total[256:, :].astype(bf16)
    for copy in copies:
        copy.wait()


def code_prep_kernel(book_t, stack, stack_t):
    def one_chunk(index, _):
        lanes = pl.ds(pl.multiple_of(index * 512, 512), 512)
        rows = book_t[:, lanes]
        unit = rows * lax.rsqrt(jnp.sum(rows * rows, axis=0, keepdims=True) + norm_eps)
        hi, mid, lo = split3(unit)
        stack_t[:, lanes] = jnp.concatenate([hi, mid, lo, jnp.ones((32, 512), bf16)], axis=0)
        tall = jnp.concatenate([hi, mid, lo, hi, mid, hi, jnp.zeros((64, 512), bf16)], axis=0)
        stack[lanes, :] = tall.T
        return 0

    lax.fori_loop(0, book_t.shape[1] // 512, one_chunk, 0)


def factor_stack(x):
    hi, mid, lo = split3(x)
    return jnp.concatenate([hi, hi, hi, mid, mid, lo, jnp.zeros((64, x.shape[1]), bf16)], axis=0)


def vq_fwd_kernel(e, gain, bias, in_t, out_w, stack, stack_t, u, kept, acc):
    lnv = ln_parts(e[...])[0] * gain[...] + bias[...]
    raw = dot_nt(in_t[...], lnv, highest)
    inv = lax.rsqrt(jnp.sum(raw * raw, axis=0, keepdims=True) + norm_eps)
    latent = raw * inv
    right = factor_stack(latent * (temper * log2e))
    acc[...] = jnp.zeros_like(acc)

    def one_chunk(index, _):
        codes = pl.ds(pl.multiple_of(index * 512, 512), 512)
        numer = jnp.exp2(dot(stack[codes, :], right)).astype(bf16)
        acc[...] += dot(stack_t[:, codes], numer)
        return 0

    lax.fori_loop(0, stack.shape[0] // 512, one_chunk, 0)
    total = acc[96:97, :]
    soft = (acc[0:32, :] + acc[32:64, :] + acc[64:96, :]) / total
    kept[0:32, :] = latent
    kept[32:64, :] = soft
    kept[64:65, :] = total
    kept[65:66, :] = inv
    u[...] = dot_full(soft.T, out_w[...])


def vq_bwd_kernel(ids, e, du, gain, bias, in_t, out_w, stack, stack_t, book_t, kept, *refs):
    small0, small1, de, code_keep, code_send, acc, grads, small, tail, sems = refs
    xhat, inv_ln = ln_parts(e[...])
    lnv = xhat * gain[...] + bias[...]
    latent, soft = kept[0:32, :], kept[32:64, :]
    total, inv = kept[64:65, :], kept[65:66, :]
    direct = (2.0 * 1.25 * commit_weight) * (latent - soft)
    dsoft = dot_nt(out_w[...], du[...], highest) - direct
    small[32:64, :] = dot_full(soft, du[...])
    shift = jnp.sum(dsoft * soft, axis=0, keepdims=True) / total
    dsoft = dsoft / total
    right = jnp.concatenate(
        [factor_stack(latent * (temper * log2e)), factor_stack(dsoft)], axis=1
    )
    pads = jnp.zeros((64, 512), f32)

    def tall(x):
        hi, lo = split2(x)
        return jnp.concatenate([hi.astype(f32), lo.astype(f32), pads], axis=0).T.astype(bf16)

    sides = jnp.concatenate([tall(dsoft), tall(latent * temper)], axis=0)
    acc[...] = jnp.zeros_like(acc)

    def one_chunk(index, _):
        codes = pl.ds(pl.multiple_of(index * 512, 512), 512)
        both = dot(stack[codes, :], right)
        numer = jnp.exp2(both[:, :512])
        dlogit = (numer * (both[:, 512:] - shift)).astype(bf16)
        acc[...] += dot(stack_t[0:96, codes], dlogit)
        dcode = dot(jnp.concatenate([numer.astype(bf16), dlogit], axis=1), sides).T
        dcode = dcode[0:32, :] + dcode[32:64, :]
        rows = book_t[:, codes]
        scale = lax.rsqrt(jnp.sum(rows * rows, axis=0, keepdims=True) + norm_eps)
        unit = rows * scale
        grads[:, codes] = (
            scale * (dcode - unit * jnp.sum(unit * dcode, axis=0, keepdims=True))
        ).astype(bf16)
        return 0

    lax.fori_loop(0, stack.shape[0] // 512, one_chunk, 0)
    dlatent = temper * (acc[0:32, :] + acc[32:64, :] + acc[64:96, :]) + direct
    draw = inv * (dlatent - latent * jnp.sum(latent * dlatent, axis=0, keepdims=True))
    small[0:32, :] = dot_full(draw, lnv)
    dln = dot_full(draw.T, in_t[...])
    small[64:65, :] = jnp.sum(dln * xhat, axis=0, keepdims=True)
    small[65:66, :] = jnp.sum(dln, axis=0, keepdims=True)
    small[66:68, :] = small0[0:2, :]
    small[68:70, :] = small1[0:2, :]
    small[70:96, :] = jnp.zeros((26, 512), f32)
    for block in range(3):
        for at, part in enumerate(split2(small[block * 32 : (block + 1) * 32, :])):
            tail[:, (at * 3 + block) * 512 : (at * 3 + block + 1) * 512] = part
    half, width = grads.shape[1] // 2, tail.shape[1]
    core = ids[0] % 2
    copies = []
    for slot, (at, to) in enumerate(((core, code_keep), (1 - core, code_send))):
        lanes = pl.ds(pl.multiple_of(at * half, half), half)
        copies += [
            pltpu.make_async_copy(grads.at[:, lanes], to.at[:, pl.ds(0, half)], sems.at[slot]),
            pltpu.make_async_copy(tail, to.at[:, pl.ds(half, width)], sems.at[slot + 2]),
        ]
    for copy in copies:
        copy.start()
    de[...] = ln_back(dln, xhat, inv_ln, gain[...])
    for copy in copies:
        copy.wait()


SMEM = pl.BlockSpec(memory_space=pltpu.SMEM)
VMEM = pl.BlockSpec(memory_space=pltpu.VMEM)
ANY = pl.BlockSpec(memory_space=pl.ANY)


def shaped(*pairs):
    return [jax.ShapeDtypeStruct(shape, dtype) for shape, dtype in pairs]


def call(kernel, name, in_specs, out_specs, outs, scratch, flops, moved, after=(), carry=()):
    n_in, n_extra, n_out = len(in_specs), len(after) + len(carry), len(outs)

    def body(*refs):
        first = n_in + n_extra
        kernel(*refs[:n_in], *refs[first : first + n_out], *refs[first + n_out + len(carry) :])

    made = pl.pallas_call(
        body,
        name=name,
        in_specs=in_specs + [ANY] * n_extra,
        out_specs=out_specs + [ANY] * len(carry),
        out_shape=outs + [jax.ShapeDtypeStruct(a.shape, a.dtype) for a in carry],
        scratch_shapes=scratch,
        input_output_aliases={n_in + len(after) + i: n_out + i for i in range(len(carry))},
        compiler_params=pltpu.CompilerParams(vmem_limit_bytes=vmem_cap),
        cost_estimate=pl.CostEstimate(flops=flops, bytes_accessed=moved, transcendentals=0),
    )

    def run(*args):
        res = made(*args, *after, *carry)
        return (*res[:n_out], list(res[n_out:]))

    return run


DMA = pltpu.SemaphoreType.DMA
ROWS2 = (512, 512)


def attn_fwd(ids, x, seg, gain, bias, quads, first, after=(), carry=()):
    outs = shaped(
        (ROWS2, f32),
        *[(ROWS2, bf16)] * 6,
        ((8, 512), f32),
        ((2, 512, 1024), bf16),
    )
    scratch = [
        pltpu.VMEM((2, 512, 1024), bf16),
        *[pltpu.VMEM(ROWS2, bf16)] * 3,
        pltpu.VMEM(ROWS2, f32),
        DMA((32,)),
        DMA,
    ]
    return call(
        functools.partial(attn_fwd_kernel, first),
        "attn_fwd",
        [SMEM] + [VMEM] * 4 + [ANY] * 8,
        [VMEM] * 8 + [ANY],
        outs,
        scratch,
        10**10,
        10**7,
        after,
        carry,
    )(ids, x, seg, gain, bias, *quads)


def mlp_fwd(ids, x1, gain, bias, quads, first, after=(), carry=()):
    return call(
        functools.partial(mlp_fwd_kernel, first),
        "mlp_fwd",
        [SMEM] + [VMEM] * 3 + [ANY] * 8,
        [VMEM] * 2 + [ANY],
        shaped((ROWS2, f32), ((256, 512), f32), ((2, 512, 2048), bf16)),
        [pltpu.VMEM((2, 512, 2048), bf16), pltpu.VMEM(ROWS2, bf16), DMA((32,)), DMA],
        8 * 10**9,
        10**7,
        after,
        carry,
    )(ids, x1, gain, bias, *quads)


def mlp_bwd(ids, x1, dys, gain, bias, w, after=(), carry=()):
    outs = shaped((ROWS2, f32), ((8, 512), f32), *[((4, 4, 32, 2048), bf16)] * 2)
    scratch = [
        pltpu.VMEM((2, 512, 2048), bf16),
        pltpu.VMEM((2, 512, 2048), bf16),
        *[pltpu.VMEM(ROWS2, bf16)] * 4,
        pltpu.VMEM(ROWS2, f32),
        DMA,
        DMA((32,)),
        *[pltpu.VMEM(ROWS2, f32)] * (len(dys) - 1),
    ]
    return call(
        functools.partial(mlp_bwd_kernel, len(dys) == 2),
        "mlp_bwd",
        [SMEM] + [VMEM] * 3 + [ANY] + [VMEM] * len(dys),
        [VMEM] * 2 + [ANY] * 2,
        outs,
        scratch,
        15 * 10**9,
        2 * 10**7,
        after,
        carry,
    )(ids, x1, gain, bias, w, *dys)


def attn_bwd(ids, x, dx1, seg, gain, bias, saved, w, other_small=(), after=(), carry=()):
    width = 1024 + 128 * len(other_small)
    outs = shaped(
        (ROWS2, f32),
        ((256, 512), bf16),
        ((8, 512), f32),
        ((4, 4, 32, width), bf16),
        *[((4, 32, width), bf16)] * 4,
    )
    scratch = [
        pltpu.VMEM((2, 512, 1024), bf16),
        pltpu.VMEM((2, 512, width), bf16),
        pltpu.VMEM(ROWS2, bf16),
        pltpu.VMEM(ROWS2, f32),
        *[pltpu.VMEM(ROWS2, bf16)] * 7,
        DMA,
        DMA((32,)),
    ]
    return call(
        functools.partial(attn_bwd_kernel, bool(other_small)),
        "attn_bwd",
        [SMEM] + [VMEM] * 12 + [ANY] + [VMEM] * len(other_small),
        [VMEM] * 3 + [ANY] * 5,
        outs,
        scratch,
        15 * 10**9,
        2 * 10**7,
        after,
        carry,
    )(ids, x, dx1, seg, gain, bias, *saved, w, *other_small)


def code_prep(book_t, after=(), carry=()):
    codes = book_t.shape[1]
    return call(
        code_prep_kernel,
        "code_prep",
        [VMEM],
        [VMEM] * 2,
        shaped(((codes, 256), bf16), ((128, codes), bf16)),
        [],
        6 * 10**9,
        10**7,
        after,
        carry,
    )(book_t)


def vq_fwd(e, gain, bias, in_t, out_w, stack, stack_t, after=(), carry=()):
    return call(
        vq_fwd_kernel,
        "vq_fwd",
        [VMEM] * 7,
        [VMEM] * 2,
        shaped((ROWS2, f32), ((72, 512), f32)),
        [pltpu.VMEM((128, 512), f32)],
        15 * 10**9,
        10**7,
        after,
        carry,
    )(e, gain, bias, in_t, out_w, stack, stack_t)


def vq_bwd(ids, e, du, gain, bias, in_t, out_w, stack, stack_t, book_t, kept, smalls, after=(), carry=()):
    codes = book_t.shape[1]
    outs = shaped((ROWS2, f32), *[((32, codes // 2 + 3072), bf16)] * 2)
    scratch = [
        pltpu.VMEM((96, 512), f32),
        pltpu.VMEM((32, codes), bf16),
        pltpu.VMEM((96, 512), f32),
        pltpu.VMEM((32, 3072), bf16),
        DMA((4,)),
    ]
    return call(
        vq_bwd_kernel,
        "vq_bwd",
        [SMEM] + [VMEM] * 12,
        [VMEM] + [ANY] * 2,
        outs,
        scratch,
        25 * 10**9,
        2 * 10**7,
        after,
        carry,
    )(ids, e, du, gain, bias, in_t, out_w, stack, stack_t, book_t, kept, *smalls)


def gate(after, carry):
    def kernel(out):
        out[...] = jnp.zeros_like(out)

    return call(kernel, "gate", [], [VMEM], shaped(((8, 128), f32)), [], 1, 1, after, carry)()[-1]


def joined(block):
    return block[0:16, 1024:].astype(f32) + block[16:32, 1024:].astype(f32)


def put_small(value, own, blocks):
    hi, lo = split2(value)
    own[0:16, 1024:] = hi.astype(f32) + lo.astype(f32)
    for block in blocks:
        block[0:16, 1024:] = hi
        block[16:32, 1024:] = lo


def near_kernel(ids, ins, outs):
    keep, others = ins[0], ins[1:]
    if len(others) == 1:
        others = [others[0].at[i] for i in range(4)]
    for i, other in enumerate(others):
        outs[i][...] = (keep[i].astype(f32) + other[...].astype(f32)).astype(outs[i].dtype)
    if keep.shape[3] == 1152:
        value = joined(keep.at[0, 0]) + joined(others[0].at[0])
        put_small(value, outs[0].at[0], [out.at[0] for out in outs[1:]])


def near_task(keep, *others):
    shape = keep.shape[1:]
    return near_kernel, [keep, *others], shaped((shape, f32), *[(shape, bf16)] * 3)


def fork_kernel(ids, ins, outs):
    keep, other = ins
    for at, (own, send, kept, sent) in enumerate(((outs[0], outs[1], (0, 2), (1, 3)), (outs[2], outs[3], (0, 1), (2, 3)))):
        cols = slice(1024 * at, 1024 * (at + 1))
        for j in range(2):
            for out, i in ((own, kept[j]), (send, sent[j])):
                total = keep[i, :, :, cols].astype(f32) + other[i, :, :, cols].astype(f32)
                out[j] = total.astype(out.dtype)


def fork_task(keep, other):
    shape = (2, *keep.shape[1:3], 1024)
    return fork_kernel, [keep, other], shaped(*[(shape, f32), (shape, bf16)] * 2)


def half_kernel(ids, ins, outs):
    own, other = ins
    for j in range(2):
        outs[j][...] = (own[j] + other[j].astype(f32)).astype(outs[j].dtype)


def half_task(own, other):
    shape = own.shape[1:]
    return half_kernel, [own, other], shaped((shape, f32), (shape, bf16))


def join_kernel(ids, ins, outs):
    for at in range(2):
        own, other = ins[2 * at : 2 * at + 2]
        for k in range(4):
            total = own[k] + other[k].astype(f32)
            outs[k][:, 1024 * at : 1024 * (at + 1)] = total.astype(outs[k].dtype)


def join_task(own_up, other_up, own_down, other_down):
    outs = shaped(((32, 2048), f32), *[((32, 2048), bf16)] * 3)
    return join_kernel, [own_up, other_up, own_down, other_down], outs


def plane_kernel(ids, ins, outs):
    for k in range(4):
        total = ins[0][k]
        for other in ins[1:]:
            total = total + other[k].astype(f32)
        outs[k][...] = total.astype(outs[k].dtype)
    if ins[0].shape[2] == 1152:
        x, y, xy = [joined(other.at[0]) for other in ins[1:]]
        put_small((ins[0][0, 0:16, 1024:] + x) + (y + xy), outs[0], outs[1:])


def plane_task(own, others):
    shape = own.shape[1:]
    return plane_kernel, [own, *others], shaped((shape, f32), *[(shape, bf16)] * 3)


def line_total(ins, width):
    total = ins[0][:, :width]
    for other in ins[1:]:
        total = total + other[:, :width].astype(f32)
    return total


def line_kernel(ids, ins, outs):
    outs[0][...] = line_total(ins, ins[0].shape[1])


def line_task(own, others):
    return line_kernel, [own, *others], shaped((own.shape, f32))


def rows_kernel(ids, ins, outs):
    own, other = ins
    half = other.shape[0]
    outs[0][ids[1]] = own[0:half, :].astype(f32)
    outs[0][1 - ids[1]] = other[...].astype(f32)


def rows_task(own, other):
    return rows_kernel, [own, other], shaped(((2, *other.shape), f32))


def small_value(ref):
    half = ref.shape[1] - 3072
    return ref[:, half : half + 1536].astype(f32) + ref[:, half + 1536 :].astype(f32)


def code_add_kernel(ids, ins, outs):
    a, b = ins
    half = a.shape[1] - 3072
    outs[0][:, :half] = (a[:, :half].astype(f32) + b[:, :half].astype(f32)).astype(bf16)
    hi, lo = split2(small_value(a) + small_value(b))
    outs[0][:, half : half + 1536] = hi
    outs[0][:, half + 1536 :] = lo


def code_add_task(a, b):
    return code_add_kernel, [a, b], shaped((a.shape, a.dtype))


def finish_kernel(ids, ins, outs):
    mlp, attn, d_mlp, d_attn, code, code_other = ins[:4], ins[4:8], *ins[8:]
    qkv, out_t, up, down_t, book, vq_in, vq_out, gains, biases, dec_biases = outs
    for layer, rows in enumerate((line_total(mlp, 2048), d_mlp[...])):
        up[layer] = rows[:, :1024]
        down_t[layer] = rows[:, 1024:]
    for layer, rows in enumerate((line_total(attn, 1024), d_attn[...])):
        for index in range(3):
            qkv[layer, index] = rows[:, index * 256 : (index + 1) * 256]
        out_t[layer] = rows[:, 768:]
    half = code.shape[1] - 3072
    core = ids[0] % 2
    for at, part in ((core, code), (1 - core, code_other)):
        lanes = pl.ds(pl.multiple_of(at * half, half), half)
        book[:, lanes] = part[:, :half].astype(f32)
    small = small_value(code)
    vq_in[...] = small[:, :512]
    vq_out[...] = small[:, 512:1024]
    rest = small[:, 1024:]
    k1, k2, k3 = [joined(other) for other in attn[1:]]
    packed = (attn[0][0:16, 1024:] + k1) + (k2 + k3)
    for row, out in enumerate((gains.at[0:1], biases.at[0:1], gains.at[1:2], biases.at[1:2])):
        for j in range(4):
            out[:, 128 * j : 128 * (j + 1)] = packed[row * 4 + j : row * 4 + j + 1, :]
    gains[2:3, :] = rest[0:1, :]
    biases[2:3, :] = rest[1:2, :]
    gains[3:4, :] = rest[2:3, :]
    dec_biases[0:1, :] = rest[3:4, :]
    gains[4:5, :] = rest[4:5, :]
    dec_biases[1:2, :] = rest[5:6, :]


def finish_task(own_m, line_m, own_a, line_a, d_mlp, d_attn, code, code_other):
    outs = shaped(
        ((2, 3, 32, 256), f32),
        ((2, 32, 256), f32),
        ((2, 32, 1024), f32),
        ((2, 32, 1024), f32),
        ((32, 2 * (code.shape[1] - 3072)), f32),
        ((32, 512), f32),
        ((32, 512), f32),
        ((5, 512), f32),
        ((3, 512), f32),
        ((2, 512), f32),
    )
    return finish_kernel, [own_m, *line_m, own_a, *line_a, d_mlp, d_attn, code, code_other], outs


def run_tasks(ids, name, tasks, after=(), carry=()):
    sizes = [(len(ins), len(outs)) for _, ins, outs in tasks]
    n_in = sum(i for i, _ in sizes)

    def kernel(ids_ref, *refs):
        at_in, at_out = 0, n_in
        for (fn, _, _), (i, o) in zip(tasks, sizes):
            fn(ids_ref, refs[at_in : at_in + i], refs[at_out : at_out + o])
            at_in, at_out = at_in + i, at_out + o

    outs = [one for _, _, many in tasks for one in many]
    res = call(
        kernel, name, [SMEM] + [VMEM] * n_in, [VMEM] * len(outs), outs, [], 10**9, 10**7, after, carry
    )(ids, *[one for _, many, _ in tasks for one in many])
    split, at = [], 0
    for _, o in sizes:
        split.append(res[at : at + o])
        at += o
    return (*split, res[-1])


def whole_groups(
    n_dp,
    tokens,
    segment_ids,
    norm_gains,
    norm_biases,
    w_qkv,
    w_attn_out,
    w_up,
    w_down,
    w_vq_in,
    w_vq_out,
    codebook,
    cotangent,
):
    dp_at, tp_at = lax.axis_index("dp"), lax.axis_index("tp")
    ids = jnp.stack([dp_at, tp_at]).astype(jnp.int32)
    rows = tokens.shape[1]

    def mine(values):
        return lax.dynamic_index_in_dim(values, tp_at, 0, keepdims=False)

    def theirs(values):
        return lax.dynamic_index_in_dim(values, 1 - tp_at, 0, keepdims=False)

    def swap(values):
        return exchange(values, 0, 1, n_dp)

    marked = jnp.concatenate(
        [tokens, jnp.broadcast_to(segment_ids[..., None].astype(bf16), (MICRO, rows, 128))], axis=2
    )
    marked = jnp.concatenate([mine(marked), swap(theirs(marked))], axis=0)
    x, seg = marked[:, : tokens.shape[2]], marked[:, tokens.shape[2] :]
    gains = [norm_gains[i : i + 1] for i in range(5)]
    biases = [norm_biases[i : i + 1] for i in range(5)]

    attn_shards, mlp_shards = [], []
    for layer in range(2):
        attn_shards.append(
            jnp.concatenate(
                [w_qkv[layer, 0], w_qkv[layer, 1], w_qkv[layer, 2], w_attn_out[layer].T], axis=1
            )
        )
        mlp_shards.append(jnp.concatenate([w_up[layer], w_down[layer].T], axis=1))
    book_t, in_t = codebook.T, w_vq_in.T
    enc_attn_line = spread_line(attn_shards[0], n_dp)
    enc_mlp_line = spread_line(mlp_shards[0], n_dp)
    dec_shard = jnp.concatenate([attn_shards[1], mlp_shards[1]], axis=1)
    enc_attn = plane_quads(enc_attn_line, n_dp)
    stack, stack_t, _ = code_prep(book_t, [enc_attn_line])
    enc_mlp_line, dec_shard = gate([*enc_attn[1:], stack_t], [enc_mlp_line, dec_shard])
    enc_mlp = plane_quads(enc_mlp_line, n_dp)
    dec_line = spread_line(dec_shard, n_dp)

    e_x1, *e_saved, e_wa, (cot,) = attn_fwd(
        ids, x, seg, gains[0], biases[0], core_quads(enc_attn, n_dp), 0, carry=[theirs(cotangent)]
    )
    *enc_mlp[1:], dec_attn_line, dec_mlp_line = gate(
        [e_x1], [*enc_mlp[1:], dec_line[:, :, :1024], dec_line[:, :, 1024:]]
    )
    dec_attn, dec_mlp = plane_quads(dec_attn_line, n_dp), plane_quads(dec_mlp_line, n_dp)
    e, _, e_wm, _ = mlp_fwd(ids, e_x1, gains[1], biases[1], core_quads(enc_mlp, n_dp), 0)
    u, kept, (cot,) = vq_fwd(
        e, gains[2], biases[2], in_t, w_vq_out, stack, stack_t, dec_attn[1:], [cot]
    )
    cot_other = swap(cot)
    d_x1, *d_saved, d_wa, _ = attn_fwd(
        ids, u, seg, gains[3], biases[3], core_quads(dec_attn, n_dp), 0
    )
    dec_mlp[1:] = gate([d_x1], dec_mlp[1:])
    y, y_theirs, d_wm, _ = mlp_fwd(
        ids, d_x1, gains[4], biases[4], core_quads(dec_mlp, n_dp), 0, [cot_other]
    )
    y_other = swap(y_theirs)

    dx1, d_small1, keep_m, send_m, _ = mlp_bwd(
        ids, d_x1, [cotangent, cot_other], gains[4], biases[4], d_wm
    )
    near_m = exchange(send_m, 1, 0, n_dp)
    du, _, d_small0, keep_a, *send_a, (keep_m,) = attn_bwd(
        ids, u, dx1, seg, gains[3], biases[3], d_saved, d_wa, carry=[keep_m]
    )
    (own_m, *lows_m), (decoded,), send_a = run_tasks(
        ids, "sums1", [near_task(keep_m, near_m), rows_task(y, y_other)], carry=send_a
    )
    plane_m, near_a = plane_send(lows_m, n_dp), near_send(send_a, n_dp)
    de, code, code_send, (own_m, keep_a) = vq_bwd(
        ids,
        e,
        du,
        gains[2],
        biases[2],
        in_t,
        w_vq_out,
        stack,
        stack_t,
        book_t,
        kept,
        [d_small0, d_small1],
        lows_m,
        [own_m, keep_a],
    )
    (own_m, *lows_m), (own_a, *lows_a), (code_send,) = run_tasks(
        ids, "sums2", [plane_task(own_m, plane_m), near_task(keep_a, *near_a)], carry=[code_send]
    )
    line_m, plane_a = line_send(lows_m, n_dp), plane_send(lows_a, n_dp)
    code_other = exchange(code_send, 1, 0, n_dp)
    (code,), _ = run_tasks(ids, "sums2b", [code_add_task(code, code_other)])
    code_other = exchange(code, 0, 1, n_dp)
    ex1, e_small1, keep_m, send_m, (own_m, own_a) = mlp_bwd(
        ids, e_x1, [de], gains[1], biases[1], e_wm, [*lows_m, *lows_a, code], [own_m, own_a]
    )
    (d_mlp,), (own_a, *lows_a), (code,), (keep_m, send_m) = run_tasks(
        ids,
        "sums3",
        [line_task(own_m, line_m), plane_task(own_a, plane_a), code_add_task(code, code_other)],
        carry=[keep_m, send_m],
    )
    line_a, near_m = line_send(lows_a, n_dp), exchange(send_m, 1, 0, n_dp)
    code_other = exchange(code, 2, 0, n_dp)
    (own_up, send_up, own_down, send_down), _ = run_tasks(
        ids, "sums3b", [fork_task(keep_m, near_m)]
    )
    other_up, other_down = exchange(send_up, 0, 1, n_dp), exchange(send_down, 2, 0, n_dp)
    dx, dx_low, _, keep_a, *send_a, (own_a, own_up, own_down) = attn_bwd(
        ids,
        x,
        ex1,
        seg,
        gains[0],
        biases[0],
        e_saved,
        e_wa,
        [e_small1],
        [*lows_a, send_up, send_down, code],
        [own_a, own_up, own_down],
    )
    (d_attn,), (code,), (own_up, send_up), (own_down, send_down), (keep_a, dx_low, *send_a) = run_tasks(
        ids,
        "sums4",
        [
            line_task(own_a, line_a),
            code_add_task(code, code_other),
            half_task(own_up, other_up),
            half_task(own_down, other_down),
        ],
        carry=[keep_a, dx_low, *send_a],
    )
    near_a, code_other = near_send(send_a, n_dp), exchange(code, 4, 0, n_dp)
    other_up, other_down = exchange(send_up, 2, 0, n_dp), exchange(send_down, 0, 1, n_dp)
    (own_a, *lows_a), (code,), (own_up, own_down, dx_low) = run_tasks(
        ids,
        "sums4b",
        [near_task(keep_a, *near_a), code_add_task(code, code_other)],
        carry=[own_up, own_down, dx_low],
    )
    plane_a, code_other = plane_send(lows_a, n_dp), exchange(code, 8, 0, n_dp)
    dx_other = swap(dx_low)
    (own_m, *lows_m), (code,), (own_a,) = run_tasks(
        ids,
        "sums5",
        [join_task(own_up, other_up, own_down, other_down), code_add_task(code, code_other)],
        lows_a,
        [own_a],
    )
    line_m, code_other = line_send(lows_m, n_dp), exchange(code, 1, 0, n_dp)
    (own_a, *lows_a), (own_m,) = run_tasks(
        ids, "sums6", [plane_task(own_a, plane_a)], lows_m, [own_m]
    )
    line_a = line_send(lows_a, n_dp)
    (qkv, out_t, up, down_t, book, vq_in, vq_out, *norms), (grad_tokens,), _ = run_tasks(
        ids,
        "finish",
        [
            finish_task(own_m, line_m, own_a, line_a, d_mlp, d_attn, code, code_other),
            rows_task(dx, dx_other),
        ],
    )
    return (
        decoded,
        grad_tokens,
        *norms,
        qkv,
        out_t.transpose(0, 2, 1),
        up,
        down_t.transpose(0, 2, 1),
        vq_in.T,
        vq_out,
        book.T,
    )


def layer_norm(values, norm_gain, norm_bias):
    centred = values - jnp.mean(values, axis=-1, keepdims=True)
    spread = jnp.mean(centred * centred, axis=-1, keepdims=True)
    return centred * lax.rsqrt(spread + ln_eps) * norm_gain + norm_bias


def gelu_tanh(values):
    return (
        0.5 * values * (1.0 + jnp.tanh(gelu_coef * (values + 0.044715 * values * values * values)))
    )


def matmul(former, latter):
    return jnp.dot(former, latter, precision=highest, preferred_element_type=jnp.float32)


def normalize(values):
    return values * lax.rsqrt(jnp.sum(values * values, axis=-1, keepdims=True) + norm_eps)


def quantize(in_rows, norm_gain, norm_bias, in_w, out_w, code_w):
    latent = normalize(matmul(layer_norm(in_rows, norm_gain, norm_bias), in_w))
    code_rows = normalize(code_w)
    logits = matmul(latent, code_rows.T) * temper
    row_max = jnp.max(logits, axis=-1, keepdims=True)
    numerator = jnp.exp(logits - row_max)
    assign = numerator / jnp.sum(numerator, axis=-1, keepdims=True)
    soft_code = matmul(assign, code_rows)
    offset = latent - soft_code
    vq_loss = commit_weight * 1.25 * jnp.sum(offset * offset)
    return (matmul(soft_code, out_w), vq_loss)


def product(former, latter):
    return jnp.dot(former, latter, preferred_element_type=jnp.float32)


def product_tn(former, latter):
    return lax.dot_general(
        former, latter, (((0,), (0,)), ((), ())), preferred_element_type=jnp.float32
    )


def product_nt(former, latter):
    return lax.dot_general(
        former, latter, (((1,), (1,)), ((), ())), preferred_element_type=jnp.float32
    )


def split_heads(values):
    return values.reshape(values.shape[0], values.shape[1] // HEAD_DIM, HEAD_DIM).transpose(1, 0, 2)


def join_heads(values):
    return values.transpose(1, 0, 2).reshape(values.shape[1], values.shape[0] * HEAD_DIM)


def masked_scores(query_blk, key_h, seg_blk, seg_keys):
    scores = jnp.einsum(
        "hqd,hkd->hqk", query_blk, key_h, preferred_element_type=jnp.float32
    ) * HEAD_DIM ** (-0.5)
    return jnp.where((seg_blk[:, None] == seg_keys[None, :])[None], scores, masked_score)


def attend(query_h, key_h, value_h, seg_keys):
    block_rows = min(512, query_h.shape[1])
    block_count = query_h.shape[1] // block_rows

    def one_block(begin_row):
        query_blk = lax.dynamic_slice_in_dim(query_h, begin_row, block_rows, 1)
        seg_blk = lax.dynamic_slice_in_dim(seg_keys, begin_row, block_rows, 0)
        scores = masked_scores(query_blk, key_h, seg_blk, seg_keys)
        row_max = jnp.max(scores, axis=-1, keepdims=True)
        numerator = jnp.exp(scores - row_max)
        row_total = jnp.sum(numerator, axis=-1, keepdims=True)
        prob_low = (numerator / row_total).astype(jnp.bfloat16)
        attended = jnp.einsum("hqk,hkd->hqd", prob_low, value_h, preferred_element_type=jnp.float32)
        return (attended.astype(jnp.bfloat16), (row_max + jnp.log(row_total))[..., 0])

    starts = jnp.arange(block_count, dtype=jnp.int32) * block_rows
    attended, log_sums = lax.map(one_block, starts)
    heads_out = attended.transpose(1, 0, 2, 3).reshape(query_h.shape)
    log_sums = log_sums.transpose(1, 0, 2).reshape(query_h.shape[0], query_h.shape[1])
    return (heads_out, log_sums)


def attend_back(query_h, key_h, value_h, seg_keys, log_sums, grad_out):
    block_rows = min(512, query_h.shape[1])
    block_count = query_h.shape[1] // block_rows

    def one_block(carry, begin_row):
        grad_key, grad_value = carry
        query_blk = lax.dynamic_slice_in_dim(query_h, begin_row, block_rows, 1)
        grad_blk = lax.dynamic_slice_in_dim(grad_out, begin_row, block_rows, 1)
        lse_blk = lax.dynamic_slice_in_dim(log_sums, begin_row, block_rows, 1)
        seg_blk = lax.dynamic_slice_in_dim(seg_keys, begin_row, block_rows, 0)
        scores = masked_scores(query_blk, key_h, seg_blk, seg_keys)
        probs = jnp.exp(scores - lse_blk[..., None])
        prob_low = probs.astype(jnp.bfloat16)
        grad_value = grad_value + jnp.einsum(
            "hqk,hqd->hkd", prob_low, grad_blk, preferred_element_type=jnp.float32
        )
        grad_prob = jnp.einsum(
            "hqd,hkd->hqk", grad_blk, value_h, preferred_element_type=jnp.float32
        )
        row_dot = jnp.sum(probs * grad_prob, axis=-1, keepdims=True)
        grad_score = (probs * (grad_prob - row_dot) * HEAD_DIM ** (-0.5)).astype(jnp.bfloat16)
        grad_query = jnp.einsum(
            "hqk,hkd->hqd", grad_score, key_h, preferred_element_type=jnp.float32
        )
        grad_key = grad_key + jnp.einsum(
            "hqk,hqd->hkd", grad_score, query_blk, preferred_element_type=jnp.float32
        )
        return ((grad_key, grad_value), grad_query)

    starts = jnp.arange(block_count, dtype=jnp.int32) * block_rows
    zeros_kv = jnp.zeros(key_h.shape, jnp.float32)
    (grad_key, grad_value), grad_query = lax.scan(one_block, (zeros_kv, zeros_kv), starts)
    grad_query = grad_query.transpose(1, 0, 2, 3).reshape(query_h.shape)
    return (
        grad_query.astype(jnp.bfloat16),
        grad_key.astype(jnp.bfloat16),
        grad_value.astype(jnp.bfloat16),
    )


def spread_rows(values):
    return lax.all_gather(values, "tp", axis=0, tiled=True)


def combine_rows(partial_value):
    return lax.psum_scatter(partial_value, "tp", scatter_dimension=0, tiled=True)


def spread_grads(values):
    return lax.all_gather(values, "tp", axis=0, tiled=True)


def combine_grads(partial_value):
    return lax.psum_scatter(
        partial_value.astype(jnp.bfloat16), "tp", scatter_dimension=0, tiled=True
    ).astype(jnp.float32)


def fetch_weights(w_qkv, w_attn_out, w_up, w_down, layer):
    return (
        lax.all_gather(w_qkv[layer], "dp", axis=1, tiled=True),
        lax.all_gather(w_attn_out[layer], "dp", axis=1, tiled=True),
        lax.all_gather(w_up[layer], "dp", axis=0, tiled=True),
        lax.all_gather(w_down[layer], "dp", axis=1, tiled=True),
    )


def reduce_weight_grads(grads):
    return (
        lax.psum_scatter(
            grads[0].astype(jnp.bfloat16), "dp", scatter_dimension=1, tiled=True
        ).astype(jnp.float32),
        lax.psum_scatter(
            grads[1].astype(jnp.bfloat16), "dp", scatter_dimension=1, tiled=True
        ).astype(jnp.float32),
        lax.psum_scatter(
            grads[2].astype(jnp.bfloat16), "dp", scatter_dimension=0, tiled=True
        ).astype(jnp.float32),
        lax.psum_scatter(
            grads[3].astype(jnp.bfloat16), "dp", scatter_dimension=1, tiled=True
        ).astype(jnp.float32),
    )


def block_forward(resid_in, seg_local, gains, biases, weights):
    qkv_w, attn_w, up_w, down_w = weights
    normed = layer_norm(resid_in, gains[0], biases[0]).astype(jnp.bfloat16)
    normed_all, seg_all = (
        lax.all_gather(normed, "tp", axis=0, tiled=True),
        lax.all_gather(seg_local, "tp", axis=0, tiled=True),
    )
    query_h = split_heads(product(normed_all, qkv_w[0]).astype(jnp.bfloat16))
    key_h = split_heads(product(normed_all, qkv_w[1]).astype(jnp.bfloat16))
    value_h = split_heads(product(normed_all, qkv_w[2]).astype(jnp.bfloat16))
    heads_out, log_sums = attend(query_h, key_h, value_h, seg_all)
    attn_rows = join_heads(heads_out)
    middle = resid_in + combine_rows(product(attn_rows, attn_w))
    normed_mid = spread_rows(layer_norm(middle, gains[1], biases[1]).astype(jnp.bfloat16))
    hidden_pre = product(normed_mid, up_w)
    hidden = gelu_tanh(hidden_pre).astype(jnp.bfloat16)
    result = middle + combine_rows(product(hidden, down_w))
    kept = (
        resid_in,
        middle,
        normed_all,
        seg_all,
        query_h,
        key_h,
        value_h,
        log_sums,
        attn_rows,
        normed_mid,
        hidden_pre,
        hidden,
    )
    return (result, kept)


def block_backward(kept, gains, biases, weights, grad_result):
    (
        resid_in,
        middle,
        normed_all,
        seg_all,
        query_h,
        key_h,
        value_h,
        log_sums,
        attn_rows,
        normed_mid,
        hidden_pre,
        hidden,
    ) = kept
    qkv_w, attn_w, up_w, down_w = weights
    grad_branch = spread_grads(grad_result.astype(jnp.bfloat16))
    grad_down = product_tn(hidden, grad_branch)
    grad_hidden = product_nt(grad_branch, down_w)
    _, gelu_back = jax.vjp(gelu_tanh, hidden_pre)
    grad_pre = gelu_back(grad_hidden)[0].astype(jnp.bfloat16)
    grad_up = product_tn(normed_mid, grad_pre)
    grad_norm_mid = combine_grads(product_nt(grad_pre, up_w))
    _, norm_back_mid = jax.vjp(layer_norm, middle, gains[1], biases[1])
    grad_mid_ln, grad_gain_mid, grad_bias_mid = norm_back_mid(grad_norm_mid)
    grad_middle = grad_result + grad_mid_ln
    grad_attn_all = spread_grads(grad_middle.astype(jnp.bfloat16))
    grad_attn = product_tn(attn_rows, grad_attn_all)
    grad_heads = split_heads(product_nt(grad_attn_all, attn_w).astype(jnp.bfloat16))
    grad_query, grad_key, grad_value = attend_back(
        query_h, key_h, value_h, seg_all, log_sums, grad_heads
    )
    grad_parts = [join_heads(grad_query), join_heads(grad_key), join_heads(grad_value)]
    grad_qkv = jnp.stack([product_tn(normed_all, grad_part) for grad_part in grad_parts])
    grad_normed_part = (
        product_nt(grad_parts[0], qkv_w[0])
        + product_nt(grad_parts[1], qkv_w[1])
        + product_nt(grad_parts[2], qkv_w[2])
    )
    grad_normed = combine_grads(grad_normed_part)
    _, norm_back_in = jax.vjp(layer_norm, resid_in, gains[0], biases[0])
    grad_in_ln, grad_gain_in, grad_bias_in = norm_back_in(grad_normed)
    gain_grads = jnp.stack([grad_gain_in, grad_gain_mid])
    bias_grads = jnp.stack([grad_bias_in, grad_bias_mid])
    return (
        grad_middle + grad_in_ln,
        gain_grads,
        bias_grads,
        (grad_qkv, grad_attn, grad_up, grad_down),
    )


def local(
    tokens,
    segment_ids,
    norm_gains,
    norm_biases,
    w_qkv,
    w_attn_out,
    w_up,
    w_down,
    w_vq_in,
    w_vq_out,
    codebook,
    cotangent,
):
    gain_sum = jnp.zeros(norm_gains.shape, jnp.float32)
    bias_sum = jnp.zeros(norm_biases.shape, jnp.float32)
    vq_in_sum = jnp.zeros(w_vq_in.shape, jnp.float32)
    vq_out_sum = jnp.zeros(w_vq_out.shape, jnp.float32)
    code_sum = jnp.zeros(codebook.shape, jnp.float32)
    layer_sums = [None, None]
    outputs = []
    input_grads = []
    for micro in range(MICRO):
        resid_in = tokens[micro].astype(jnp.float32)
        seg_local = segment_ids[micro]
        enc_weights = fetch_weights(w_qkv, w_attn_out, w_up, w_down, 0)
        encoded, enc_kept = block_forward(
            resid_in, seg_local, norm_gains[0:2], norm_biases[0:2], enc_weights
        )
        (decoder_in, _), vq_back = jax.vjp(
            quantize, encoded, norm_gains[2], norm_biases[2], w_vq_in, w_vq_out, codebook
        )
        dec_weights = fetch_weights(w_qkv, w_attn_out, w_up, w_down, 1)
        decoded, dec_kept = block_forward(
            decoder_in, seg_local, norm_gains[3:5], norm_biases[3:5], dec_weights
        )
        outputs.append(decoded)
        grad_dec_in, gains_dec, biases_dec, grads_dec = block_backward(
            dec_kept, norm_gains[3:5], norm_biases[3:5], dec_weights, cotangent[micro]
        )
        grad_encoded, grad_gain_vq, grad_bias_vq, grad_in_w, grad_out_w, grad_codes = vq_back(
            (grad_dec_in, jnp.ones((), jnp.float32))
        )
        grad_input, gains_enc, biases_enc, grads_enc = block_backward(
            enc_kept, norm_gains[0:2], norm_biases[0:2], enc_weights, grad_encoded
        )
        input_grads.append(grad_input)
        gain_sum = gain_sum + jnp.concatenate([gains_enc, grad_gain_vq[None], gains_dec], axis=0)
        bias_sum = bias_sum + jnp.concatenate([biases_enc, grad_bias_vq[None], biases_dec], axis=0)
        vq_in_sum = vq_in_sum + grad_in_w
        vq_out_sum = vq_out_sum + grad_out_w
        code_sum = code_sum + grad_codes
        for layer, grads in ((0, grads_enc), (1, grads_dec)):
            reduced = reduce_weight_grads(grads)
            if layer_sums[layer] is None:
                layer_sums[layer] = reduced
            else:
                layer_sums[layer] = jax.tree.map(jnp.add, layer_sums[layer], reduced)
    gain_tot, bias_tot, vq_in_tot, vq_out_tot, code_tot = lax.psum(
        (gain_sum, bias_sum, vq_in_sum, vq_out_sum, code_sum), ("dp", "tp")
    )
    return (
        jnp.stack(outputs),
        jnp.stack(input_grads),
        gain_tot,
        bias_tot[0:3],
        bias_tot[3:5],
        jnp.stack([layer_sums[0][0], layer_sums[1][0]]),
        jnp.stack([layer_sums[0][1], layer_sums[1][1]]),
        jnp.stack([layer_sums[0][2], layer_sums[1][2]]),
        jnp.stack([layer_sums[0][3], layer_sums[1][3]]),
        vq_in_tot,
        vq_out_tot,
        code_tot,
    )


def solution(mesh):
    n_dp, n_tp = mesh.shape["dp"], mesh.shape["tp"]
    fits = n_tp == MICRO and n_dp == 16
    return jax.shard_map(
        functools.partial(whole_groups, n_dp) if fits else local,
        mesh=mesh,
        in_specs=(
            P(None, ("dp", "tp"), None),
            P(None, ("dp", "tp")),
            P(),
            P(),
            P(None, None, "dp", "tp"),
            P(None, "tp", "dp"),
            P(None, "dp", "tp"),
            P(None, "tp", "dp"),
            P(),
            P(),
            P(),
            P(None, ("dp", "tp"), None),
        ),
        out_specs=(
            P(None, ("dp", "tp"), None),
            P(None, ("dp", "tp"), None),
            P(),
            P(),
            P(),
            P(None, None, "dp", "tp"),
            P(None, "tp", "dp"),
            P(None, "dp", "tp"),
            P(None, "tp", "dp"),
            P(),
            P(),
            P(),
        ),
        check_vma=False,
    )
```

```python
import functools

import jax
import jax.numpy as jnp
from jax import lax
from jax.experimental import pallas as pl
from jax.experimental.pallas import tpu as pltpu
from jax.sharding import PartitionSpec as P

HEAD_DIM = 64
MICRO = 2
bf16 = jnp.bfloat16
f32 = jnp.float32
highest = lax.Precision.HIGHEST
ln_eps = 1e-05
norm_eps = 1e-06
temper = 10.0
commit_weight = 64.0
gelu_coef = 0.7978845608028654
masked_score = -1e30
log2e = 1.4426950408889634
vmem_cap = 36 * 1024 * 1024


PLANE = ((0, 0), (0, 1), (1, 0), (1, 1))


def exchange(values, dp_xor, tp_xor, n_dp):
    pairs = [
        (d * 2 + t, (d ^ dp_xor) * 2 + (t ^ tp_xor)) for d in range(n_dp) for t in range(2)
    ]
    return lax.ppermute(values, ("dp", "tp"), pairs)


def spread_line(shard, n_dp):
    return jnp.stack([shard] + [exchange(shard, 4 * k, 0, n_dp) for k in range(1, 4)])


def plane_quads(own, n_dp):
    return [own] + [exchange(own, 2 * y, x, n_dp) for y, x in PLANE[1:]]


def core_quads(quads, n_dp):
    return quads + [exchange(quad, 1, 0, n_dp) for quad in quads]


def near_send(sends, n_dp):
    return [exchange(send, 1, 0, n_dp) for send in sends]


def plane_send(lows, n_dp):
    return [exchange(low, 2 * y, x, n_dp) for (y, x), low in zip(PLANE[1:], lows)]


def line_send(lows, n_dp):
    return [exchange(low, 4 * k, 0, n_dp) for k, low in zip(range(1, 4), lows)]


def block_places():
    for core in range(2):
        for index, (y, x) in enumerate(PLANE):
            for k in range(4):
                yield core * 4 + index, k, k * 4 + y * 2 + core, x


def dot(a, b):
    return jnp.dot(a, b, preferred_element_type=f32)


def dot_nt(a, b, precision=None):
    return lax.dot_general(
        a, b, (((1,), (1,)), ((), ())), preferred_element_type=f32, precision=precision
    )


def dot_full(a, b):
    return jnp.dot(a, b, preferred_element_type=f32, precision=highest)


def ln_parts(x):
    centred = x - jnp.mean(x, axis=-1, keepdims=True)
    inv = lax.rsqrt(jnp.mean(centred * centred, axis=-1, keepdims=True) + ln_eps)
    return centred * inv, inv


def ln_back(grad, xhat, inv, gain):
    scaled = grad * gain
    return inv * (
        scaled
        - jnp.mean(scaled, axis=-1, keepdims=True)
        - xhat * jnp.mean(scaled * xhat, axis=-1, keepdims=True)
    )


def split2(x):
    hi = x.astype(bf16)
    return hi, (x - hi.astype(f32)).astype(bf16)


def split3(x):
    hi, _ = split2(x)
    rest = x - hi.astype(f32)
    mid = rest.astype(bf16)
    return hi, mid, (rest - mid.astype(f32)).astype(bf16)


def weight_copies(ids_ref, quad_refs, w_ref, sems):
    copies, first = [], 0
    for at in range(0, len(quad_refs), 8):
        width = quad_refs[at].shape[2]
        for slot, (which, k, dp_xor, tp_xor) in enumerate(block_places()):
            row = pl.multiple_of((ids_ref[0] ^ dp_xor) * 32, 32)
            copies.append(
                pltpu.make_async_copy(
                    quad_refs[at + which].at[k],
                    w_ref.at[ids_ref[1] ^ tp_xor, pl.ds(row, 32), pl.ds(first, width)],
                    sems.at[at * 4 + slot],
                )
            )
        first += width
    return copies


def grad_copies(ids_ref, g_ref, quad_refs, sems):
    copies = []
    for slot, (which, k, dp_xor, tp_xor) in enumerate(block_places()):
        row = pl.multiple_of((ids_ref[0] ^ dp_xor) * 32, 32)
        copies.append(
            pltpu.make_async_copy(
                g_ref.at[ids_ref[1] ^ tp_xor, pl.ds(row, 32), :],
                quad_refs[which].at[k],
                sems.at[slot],
            )
        )
    return copies


def head_rows(ref, pair, which):
    own = ref[pl.ds(pl.multiple_of(pair * 128 + which * HEAD_DIM, HEAD_DIM), HEAD_DIM), :]
    zero = jnp.zeros_like(own)
    return jnp.concatenate([own, zero] if which == 0 else [zero, own], axis=0)


def segment_mask(own, other):
    ids = jnp.concatenate([own[:, 512:], other[:, 512:]], axis=0).astype(f32)
    return jnp.where(ids[:, 0:1] == ids.T[0:1, :], 0.0, masked_score)


def load_rows(x, own, other):
    if x is None:
        return jnp.concatenate([own[:, :512], other[:, :512]], axis=0).astype(f32)
    return x[...]


def attn_fwd_kernel(with_x, ids, own, other, gain, bias, *refs):
    x, refs = (refs[0], refs[1:]) if with_x else (None, refs)
    quads, refs = refs[:8], refs[8:]
    x1, qs, k, v, o, qst, kt, lse, w_out = refs[:9]
    w, h, vt, ot, mask, sems, out_sem = refs[9:]
    copies = weight_copies(ids, quads, w, sems)
    for copy in copies:
        copy.start()
    xf = load_rows(x, own, other)
    h[...] = (ln_parts(xf)[0] * gain[...] + bias[...]).astype(bf16)
    mask[...] = segment_mask(own, other)
    for copy in copies:
        copy.wait()
    keep = pltpu.make_async_copy(w, w_out, out_sem)
    keep.start()
    for t in range(2):
        cols = pl.ds(t * 256, 256)
        qs[:, cols] = (dot(h[...], w[t, :, 0:256]).astype(bf16) * HEAD_DIM ** (-0.5)).astype(bf16)
        k[:, cols] = dot(h[...], w[t, :, 256:512]).astype(bf16)
        v[:, cols] = dot(h[...], w[t, :, 512:768]).astype(bf16)
    qst[...] = qs[...].T
    kt[...] = k[...].T
    vt[...] = v[...].T

    def one_pair(pair, _):
        lanes = pl.ds(pl.multiple_of(pair * 128, 128), 128)
        k_pair = k[:, lanes]
        for which in range(2):
            scores = dot(k_pair, head_rows(qst, pair, which)) + mask[...]
            top = jnp.max(scores, axis=0, keepdims=True)
            numer = jnp.exp(scores - top).astype(bf16)
            rows = pl.ds(pl.multiple_of(pair * 128 + which * HEAD_DIM, HEAD_DIM), HEAD_DIM)
            left = jnp.concatenate([vt[rows, :], jnp.ones((16, 512), bf16)], axis=0)
            both = dot(left, numer)
            total = both[HEAD_DIM : HEAD_DIM + 1, :]
            ot[rows, :] = (both[:HEAD_DIM, :] / total).astype(bf16)
            lse[pl.ds(pair * 2 + which, 1), :] = top + jnp.log(total)
        return 0

    lax.fori_loop(0, 4, one_pair, 0)
    o[...] = ot[...].T
    acc = xf
    for t in range(2):
        acc = acc + dot_nt(o[:, t * 256 : (t + 1) * 256], w[t, :, 768:1024])
    x1[...] = acc
    keep.wait()


def gelu_parts(u):
    square = u * u
    tanh = jnp.tanh(gelu_coef * u * (1.0 + 0.044715 * square))
    return 0.5 * u * (1.0 + tanh), tanh, square


def mlp_fwd_kernel(n_quads, ids, x1, gain, bias, *refs):
    quads, refs = refs[:n_quads], refs[n_quads:]
    y, theirs, w_out = refs[:3]
    w, h2, sems, out_sem = refs[3:]
    copies = weight_copies(ids, quads, w, sems)
    for copy in copies:
        copy.start()
    h2[...] = (ln_parts(x1[...])[0] * gain[...] + bias[...]).astype(bf16)
    y[...] = x1[...]
    for copy in copies:
        copy.wait()
    keep = pltpu.make_async_copy(w, w_out, out_sem)
    keep.start()

    def one_chunk(index, _):
        t = index // 2
        col = (index % 2) * 512
        pre = dot(h2[...], w[t, :, pl.ds(pl.multiple_of(col, 512), 512)])
        hidden = gelu_parts(pre)[0].astype(bf16)
        y[...] += dot_nt(hidden, w[t, :, pl.ds(pl.multiple_of(col + 1024, 512), 512)])
        return 0

    lax.fori_loop(0, 4, one_chunk, 0)
    theirs[...] = y[256:, :]
    keep.wait()


def mlp_bwd_kernel(split, ids, x1, gain, bias, w_hbm, *refs):
    if split:
        own, other, dx1, small = refs[:4]
        refs = refs[4:]
    else:
        dy, dx1, small = refs[:3]
        refs = refs[3:]
    halves, refs = refs[:2], refs[2:]
    w, g, h2, h2t, dyb, dybt, dh2, w_sem, sems = refs[:9]
    if split:
        dy = refs[9]
        dy[0:256, :] = own[ids[1]]
        dy[256:, :] = other[...]
    load = pltpu.make_async_copy(w_hbm, w, w_sem)
    load.start()
    h2[...] = (ln_parts(x1[...])[0] * gain[...] + bias[...]).astype(bf16)
    h2t[...] = h2[...].T
    dyb[...] = dy[...].astype(bf16)
    dybt[...] = dyb[...].T
    dh2[...] = jnp.zeros_like(dh2)
    load.wait()

    def one_chunk(index, _):
        t = index // 2
        up = pl.ds(pl.multiple_of((index % 2) * 512, 512), 512)
        down = pl.ds(pl.multiple_of((index % 2) * 512 + 1024, 512), 512)
        pre = dot(h2[...], w[t, :, up])
        hidden, tanh, square = gelu_parts(pre)
        slope = 0.5 * (1.0 + tanh) + (0.5 * gelu_coef) * pre * (1.0 - tanh * tanh) * (
            1.0 + (3 * 0.044715) * square
        )
        dhidden = dot(dyb[...], w[t, :, down])
        dpre = (dhidden * slope).astype(bf16)
        g[t, :, down] = dot(dybt[...], hidden.astype(bf16)).astype(bf16)
        g[t, :, up] = dot(h2t[...], dpre).astype(bf16)
        dh2[...] += dot_nt(dpre, w[t, :, up])
        return 0

    lax.fori_loop(0, 4, one_chunk, 0)
    copies = grad_copies(ids, g, [half.at[i] for half in halves for i in range(4)], sems)
    for copy in copies:
        copy.start()
    xhat, inv = ln_parts(x1[...])
    grad = dh2[...]
    small[0:1, :] = jnp.sum(grad * xhat, axis=0, keepdims=True)
    small[1:2, :] = jnp.sum(grad, axis=0, keepdims=True)
    dx1[...] = dy[...] + ln_back(grad, xhat, inv, gain[...])
    for copy in copies:
        copy.wait()


def pack_rows(rows):
    cut = [row[:, 128 * j : 128 * (j + 1)] for row in rows for j in range(4)]
    return jnp.concatenate(split2(jnp.concatenate(cut, axis=0)), axis=0)


def attn_bwd_kernel(
    with_x, with_small, ids, own, other, dx1, gain, bias, qs, k, v, o, qst, kt, lse, w_hbm, *refs
):
    x, refs = (refs[0], refs[1:]) if with_x else (None, refs)
    if with_small:
        other_small, refs = refs[0], refs[1:]
    dx, dx_low, small = refs[:3]
    keep, sends, refs = refs[3], refs[4:8], refs[8:]
    w, g, h, mask, do, dot_t, dqt, dq, dk, dv, flip, w_sem, sems = refs
    load = pltpu.make_async_copy(w_hbm, w, w_sem)
    load.start()
    xf = load_rows(x, own, other)
    h[...] = (ln_parts(xf)[0] * gain[...] + bias[...]).astype(bf16)
    mask[...] = segment_mask(own, other)
    low = dx1[...].astype(bf16)
    flip[...] = low.T
    load.wait()
    for t in range(2):
        cols = pl.ds(t * 256, 256)
        do[:, cols] = dot(low, w[t, :, 768:1024]).astype(bf16)
        g[t, :, 768:1024] = dot(flip[...], o[:, cols]).astype(bf16)
    dot_t[...] = do[...].T
    def one_pair(pair, _):
        lanes = pl.ds(pl.multiple_of(pair * 128, 128), 128)
        k_pair, v_pair = k[:, lanes], v[:, lanes]
        q_pair, do_pair = qs[:, lanes], do[:, lanes]
        dvs, dks = [], []
        for which in range(2):
            head = pl.ds(pair * 2 + which, 1)
            rows = pl.ds(pl.multiple_of(pair * 128 + which * HEAD_DIM, HEAD_DIM), HEAD_DIM)
            scores = dot(k_pair, head_rows(qst, pair, which)) + mask[...]
            probs = jnp.exp(scores - lse[head, :])
            dprobs = dot(v_pair, head_rows(dot_t, pair, which))
            shift = jnp.sum(probs * dprobs, axis=0, keepdims=True)
            dscore = (probs * (dprobs - shift)).astype(bf16)
            dvs.append(dot(probs.astype(bf16), do_pair))
            dks.append(dot(dscore, q_pair))
            dqt[rows, :] = (dot(kt[rows, :], dscore) * HEAD_DIM ** (-0.5)).astype(bf16)
        first = lax.broadcasted_iota(jnp.int32, (512, 128), 1) < HEAD_DIM
        dv[:, lanes] = jnp.where(first, dvs[0], dvs[1]).astype(bf16)
        dk[:, lanes] = jnp.where(first, dks[0], dks[1]).astype(bf16)
        return 0

    lax.fori_loop(0, 4, one_pair, 0)
    dq[...] = dqt[...].T
    flip[...] = h[...].T
    for t in range(2):
        cols = pl.ds(t * 256, 256)
        g[t, :, 0:256] = dot(flip[...], dq[:, cols]).astype(bf16)
        g[t, :, 256:512] = dot(flip[...], dk[:, cols]).astype(bf16)
        g[t, :, 512:768] = dot(flip[...], dv[:, cols]).astype(bf16)
    grad = jnp.zeros((512, 512), f32)
    for t in range(2):
        cols = pl.ds(t * 256, 256)
        for index, part in enumerate((dq, dk, dv)):
            grad = grad + dot_nt(part[:, cols], w[t, :, index * 256 : (index + 1) * 256])
    xhat, inv = ln_parts(xf)
    dgain = jnp.sum(grad * xhat, axis=0, keepdims=True)
    dbias = jnp.sum(grad, axis=0, keepdims=True)
    small[0:1, :] = dgain
    small[1:2, :] = dbias
    if with_small:
        packed = pack_rows([dgain, dbias, other_small[0:1, :], other_small[1:2, :]])
        for t in range(2):
            for row in range(16):
                g[t, row * 32 : (row + 1) * 32, 1024:1152] = packed
    copies = grad_copies(ids, g, [keep.at[i] for i in range(4)] + list(sends), sems)
    for copy in copies:
        copy.start()
    total = dx1[...] + ln_back(grad, xhat, inv, gain[...])
    dx[...] = total
    dx_low[...] = total[256:, :].astype(bf16)
    for copy in copies:
        copy.wait()


def code_prep_kernel(book_t, stack, stack_t):
    def one_chunk(index, _):
        lanes = pl.ds(pl.multiple_of(index * 512, 512), 512)
        rows = book_t[:, lanes]
        unit = rows * lax.rsqrt(jnp.sum(rows * rows, axis=0, keepdims=True) + norm_eps)
        hi, mid, lo = split3(unit)
        stack_t[:, lanes] = jnp.concatenate([hi, mid, lo, jnp.ones((32, 512), bf16)], axis=0)
        tall = jnp.concatenate([hi, mid, lo, hi, mid, hi, jnp.zeros((64, 512), bf16)], axis=0)
        stack[lanes, :] = tall.T
        return 0

    lax.fori_loop(0, book_t.shape[1] // 512, one_chunk, 0)


def factor_stack(x):
    hi, mid, lo = split3(x)
    return jnp.concatenate([hi, hi, hi, mid, mid, lo, jnp.zeros((64, x.shape[1]), bf16)], axis=0)


def vq_fwd_kernel(e, gain, bias, in_t, out_w, stack, stack_t, u, kept, acc):
    lnv = ln_parts(e[...])[0] * gain[...] + bias[...]
    raw = dot_nt(in_t[...], lnv, highest)
    inv = lax.rsqrt(jnp.sum(raw * raw, axis=0, keepdims=True) + norm_eps)
    latent = raw * inv
    right = factor_stack(latent * (temper * log2e))
    acc[...] = jnp.zeros_like(acc)

    def one_chunk(index, _):
        codes = pl.ds(pl.multiple_of(index * 512, 512), 512)
        numer = jnp.exp2(dot(stack[codes, :], right)).astype(bf16)
        acc[...] += dot(stack_t[:, codes], numer)
        return 0

    lax.fori_loop(0, stack.shape[0] // 512, one_chunk, 0)
    total = acc[96:97, :]
    soft = (acc[0:32, :] + acc[32:64, :] + acc[64:96, :]) / total
    kept[0:32, :] = latent
    kept[32:64, :] = soft
    kept[64:65, :] = total
    kept[65:66, :] = inv
    u[...] = dot_full(soft.T, out_w[...])


def vq_bwd_kernel(ids, e, du, gain, bias, in_t, out_w, stack, stack_t, book_t, kept, *refs):
    small0, small1, de, code_keep, code_send, acc, grads, small, tail, sems = refs
    xhat, inv_ln = ln_parts(e[...])
    lnv = xhat * gain[...] + bias[...]
    latent, soft = kept[0:32, :], kept[32:64, :]
    total, inv = kept[64:65, :], kept[65:66, :]
    direct = (2.0 * 1.25 * commit_weight) * (latent - soft)
    dsoft = dot_nt(out_w[...], du[...], highest) - direct
    small[32:64, :] = dot_full(soft, du[...])
    shift = jnp.sum(dsoft * soft, axis=0, keepdims=True) / total
    dsoft = dsoft / total
    right = jnp.concatenate(
        [factor_stack(latent * (temper * log2e)), factor_stack(dsoft)], axis=1
    )
    pads = jnp.zeros((64, 512), f32)

    def tall(x):
        hi, lo = split2(x)
        return jnp.concatenate([hi.astype(f32), lo.astype(f32), pads], axis=0).T.astype(bf16)

    sides = jnp.concatenate([tall(dsoft), tall(latent * temper)], axis=0)
    acc[...] = jnp.zeros_like(acc)

    def one_chunk(index, _):
        codes = pl.ds(pl.multiple_of(index * 512, 512), 512)
        both = dot(stack[codes, :], right)
        numer = jnp.exp2(both[:, :512])
        dlogit = (numer * (both[:, 512:] - shift)).astype(bf16)
        acc[...] += dot(stack_t[0:96, codes], dlogit)
        dcode = dot(jnp.concatenate([numer.astype(bf16), dlogit], axis=1), sides).T
        dcode = dcode[0:32, :] + dcode[32:64, :]
        rows = book_t[:, codes]
        scale = lax.rsqrt(jnp.sum(rows * rows, axis=0, keepdims=True) + norm_eps)
        unit = rows * scale
        grads[:, codes] = (
            scale * (dcode - unit * jnp.sum(unit * dcode, axis=0, keepdims=True))
        ).astype(bf16)
        return 0

    lax.fori_loop(0, stack.shape[0] // 512, one_chunk, 0)
    dlatent = temper * (acc[0:32, :] + acc[32:64, :] + acc[64:96, :]) + direct
    draw = inv * (dlatent - latent * jnp.sum(latent * dlatent, axis=0, keepdims=True))
    small[0:32, :] = dot_full(draw, lnv)
    dln = dot_full(draw.T, in_t[...])
    small[64:65, :] = jnp.sum(dln * xhat, axis=0, keepdims=True)
    small[65:66, :] = jnp.sum(dln, axis=0, keepdims=True)
    small[66:68, :] = small0[0:2, :]
    small[68:70, :] = small1[0:2, :]
    small[70:96, :] = jnp.zeros((26, 512), f32)
    for block in range(3):
        for at, part in enumerate(split2(small[block * 32 : (block + 1) * 32, :])):
            for side in range(2):
                tail[block * 2 + side, :, at * 256 : (at + 1) * 256] = part[
                    :, side * 256 : (side + 1) * 256
                ]
    tail[6:8] = jnp.zeros((2, 32, 512), bf16)
    core, z = ids[0] % 2, ids[0] // 4
    copies = []
    for slot, (at, to) in enumerate(((core, code_keep), (1 - core, code_send))):
        for k in range(4):
            part = at * 4 + (z ^ k)
            lanes = pl.ds(pl.multiple_of(part * 1024, 1024), 1024)
            copies += [
                pltpu.make_async_copy(
                    grads.at[:, lanes], to.at[k, :, pl.ds(0, 1024)], sems.at[0, slot, k]
                ),
                pltpu.make_async_copy(
                    tail.at[part], to.at[k, :, pl.ds(1024, 512)], sems.at[1, slot, k]
                ),
            ]
    for copy in copies:
        copy.start()
    de[...] = ln_back(dln, xhat, inv_ln, gain[...])
    for copy in copies:
        copy.wait()


SMEM = pl.BlockSpec(memory_space=pltpu.SMEM)
VMEM = pl.BlockSpec(memory_space=pltpu.VMEM)
ANY = pl.BlockSpec(memory_space=pl.ANY)


def shaped(*pairs):
    return [jax.ShapeDtypeStruct(shape, dtype) for shape, dtype in pairs]


def call(kernel, name, in_specs, out_specs, outs, scratch, flops, moved, after=(), carry=()):
    n_in, n_extra, n_out = len(in_specs), len(after) + len(carry), len(outs)

    def body(*refs):
        first = n_in + n_extra
        kernel(*refs[:n_in], *refs[first : first + n_out], *refs[first + n_out + len(carry) :])

    made = pl.pallas_call(
        body,
        name=name,
        in_specs=in_specs + [ANY] * n_extra,
        out_specs=out_specs + [ANY] * len(carry),
        out_shape=outs + [jax.ShapeDtypeStruct(a.shape, a.dtype) for a in carry],
        scratch_shapes=scratch,
        input_output_aliases={n_in + len(after) + i: n_out + i for i in range(len(carry))},
        compiler_params=pltpu.CompilerParams(vmem_limit_bytes=vmem_cap),
        cost_estimate=pl.CostEstimate(flops=flops, bytes_accessed=moved, transcendentals=0),
    )

    def run(*args):
        res = made(*args, *after, *carry)
        return (*res[:n_out], list(res[n_out:]))

    return run


DMA = pltpu.SemaphoreType.DMA
ROWS2 = (512, 512)


def attn_fwd(ids, marked, xs, gain, bias, quads, after=(), carry=()):
    outs = shaped(
        (ROWS2, f32),
        *[(ROWS2, bf16)] * 6,
        ((8, 512), f32),
        ((2, 512, 1024), bf16),
    )
    scratch = [
        pltpu.VMEM((2, 512, 1024), bf16),
        *[pltpu.VMEM(ROWS2, bf16)] * 3,
        pltpu.VMEM(ROWS2, f32),
        DMA((32,)),
        DMA,
    ]
    return call(
        functools.partial(attn_fwd_kernel, bool(xs)),
        "attn_fwd",
        [SMEM] + [VMEM] * (4 + len(xs)) + [ANY] * 8,
        [VMEM] * 8 + [ANY],
        outs,
        scratch,
        10**10,
        10**7,
        after,
        carry,
    )(ids, *marked, gain, bias, *xs, *quads)


def mlp_fwd(ids, x1, gain, bias, quads, after=(), carry=()):
    return call(
        functools.partial(mlp_fwd_kernel, len(quads)),
        "mlp_fwd",
        [SMEM] + [VMEM] * 3 + [ANY] * len(quads),
        [VMEM] * 2 + [ANY],
        shaped((ROWS2, f32), ((256, 512), f32), ((2, 512, 2048), bf16)),
        [
            pltpu.VMEM((2, 512, 2048), bf16),
            pltpu.VMEM(ROWS2, bf16),
            DMA((4 * len(quads),)),
            DMA,
        ],
        8 * 10**9,
        10**7,
        after,
        carry,
    )(ids, x1, gain, bias, *quads)


def mlp_bwd(ids, x1, dys, gain, bias, w, after=(), carry=()):
    outs = shaped((ROWS2, f32), ((8, 512), f32), *[((4, 4, 32, 2048), bf16)] * 2)
    scratch = [
        pltpu.VMEM((2, 512, 2048), bf16),
        pltpu.VMEM((2, 512, 2048), bf16),
        *[pltpu.VMEM(ROWS2, bf16)] * 4,
        pltpu.VMEM(ROWS2, f32),
        DMA,
        DMA((32,)),
        *[pltpu.VMEM(ROWS2, f32)] * (len(dys) - 1),
    ]
    return call(
        functools.partial(mlp_bwd_kernel, len(dys) == 2),
        "mlp_bwd",
        [SMEM] + [VMEM] * 3 + [ANY] + [VMEM] * len(dys),
        [VMEM] * 2 + [ANY] * 2,
        outs,
        scratch,
        15 * 10**9,
        2 * 10**7,
        after,
        carry,
    )(ids, x1, gain, bias, w, *dys)


def attn_bwd(ids, marked, xs, dx1, gain, bias, saved, w, other_small=(), after=(), carry=()):
    width = 1024 + 128 * len(other_small)
    outs = shaped(
        (ROWS2, f32),
        ((256, 512), bf16),
        ((8, 512), f32),
        ((4, 4, 32, width), bf16),
        *[((4, 32, width), bf16)] * 4,
    )
    scratch = [
        pltpu.VMEM((2, 512, 1024), bf16),
        pltpu.VMEM((2, 512, width), bf16),
        pltpu.VMEM(ROWS2, bf16),
        pltpu.VMEM(ROWS2, f32),
        *[pltpu.VMEM(ROWS2, bf16)] * 7,
        DMA,
        DMA((32,)),
    ]
    return call(
        functools.partial(attn_bwd_kernel, bool(xs), bool(other_small)),
        "attn_bwd",
        [SMEM] + [VMEM] * 12 + [ANY] + [VMEM] * (len(xs) + len(other_small)),
        [VMEM] * 3 + [ANY] * 5,
        outs,
        scratch,
        15 * 10**9,
        2 * 10**7,
        after,
        carry,
    )(ids, *marked, dx1, gain, bias, *saved, w, *xs, *other_small)


def code_prep(book_t, after=(), carry=()):
    codes = book_t.shape[1]
    return call(
        code_prep_kernel,
        "code_prep",
        [VMEM],
        [VMEM] * 2,
        shaped(((codes, 256), bf16), ((128, codes), bf16)),
        [],
        6 * 10**9,
        10**7,
        after,
        carry,
    )(book_t)


def vq_fwd(e, gain, bias, in_t, out_w, stack, stack_t, after=(), carry=()):
    return call(
        vq_fwd_kernel,
        "vq_fwd",
        [VMEM] * 7,
        [VMEM] * 2,
        shaped((ROWS2, f32), ((72, 512), f32)),
        [pltpu.VMEM((128, 512), f32)],
        15 * 10**9,
        10**7,
        after,
        carry,
    )(e, gain, bias, in_t, out_w, stack, stack_t)


def vq_bwd(ids, e, du, gain, bias, in_t, out_w, stack, stack_t, book_t, kept, smalls, after=(), carry=()):
    codes = book_t.shape[1]
    outs = shaped((ROWS2, f32), *[((4, 32, 1536), bf16)] * 2)
    scratch = [
        pltpu.VMEM((96, 512), f32),
        pltpu.VMEM((32, codes), bf16),
        pltpu.VMEM((96, 512), f32),
        pltpu.VMEM((8, 32, 512), bf16),
        DMA((2, 2, 4)),
    ]
    return call(
        vq_bwd_kernel,
        "vq_bwd",
        [SMEM] + [VMEM] * 12,
        [VMEM] + [ANY] * 2,
        outs,
        scratch,
        25 * 10**9,
        2 * 10**7,
        after,
        carry,
    )(ids, e, du, gain, bias, in_t, out_w, stack, stack_t, book_t, kept, *smalls)


def gate(after, carry):
    def kernel(out):
        out[...] = jnp.zeros_like(out)

    return call(kernel, "gate", [], [VMEM], shaped(((8, 128), f32)), [], 1, 1, after, carry)()[-1]


def stack_kernel(cuts, *refs):
    shards, outs, sems = refs[:4], refs[4:-1], refs[-1]
    copies, first = [], 0
    for at, (out, width) in enumerate(zip(outs, cuts)):
        for k in range(4):
            copies.append(
                pltpu.make_async_copy(
                    shards[k].at[:, pl.ds(first, width)], out.at[k], sems.at[at, k]
                )
            )
        first += width
    for copy in copies:
        copy.start()
    for copy in copies:
        copy.wait()


def stack_lines(shards, cuts, after=()):
    return call(
        functools.partial(stack_kernel, cuts),
        "stack_lines",
        [ANY] * 4,
        [ANY] * len(cuts),
        shaped(*[((4, 32, width), bf16) for width in cuts]),
        [DMA((len(cuts), 4))],
        1,
        10**6,
        after,
    )(*shards)[:-1]


def pack_kernel(ids, qkv, out_t, up, down_t, tokens, segs, cot, attn, mlp, dec, own, other, cot_send, sem):
    send = pltpu.make_async_copy(cot.at[1 - ids[1]], cot_send, sem)
    send.start()
    for layer, (to, first) in enumerate(((attn, 0), (dec, 0))):
        for index in range(3):
            to[:, index * 256 : (index + 1) * 256] = qkv[layer, index]
        to[:, 768:1024] = out_t[layer]
    for layer, (to, first) in enumerate(((mlp, 0), (dec, 1024))):
        to[:, first : first + 1024] = up[layer]
        to[:, first + 1024 : first + 2048] = down_t[layer]
    for to, micro in ((own, ids[1]), (other, 1 - ids[1])):
        to[:, :512] = tokens[micro]
        ids_row = segs[pl.ds(micro, 1), :].astype(f32)
        to[:, 512:] = jnp.broadcast_to(ids_row, (128, 256)).T.astype(bf16)
    send.wait()


def pack(ids, qkv, out_t, up, down_t, tokens, segs, cot):
    outs = shaped(
        ((32, 1024), bf16),
        ((32, 2048), bf16),
        ((32, 3072), bf16),
        *[((256, 640), bf16)] * 2,
        ((256, 512), f32),
    )
    return call(
        pack_kernel,
        "pack",
        [SMEM] + [VMEM] * 6 + [ANY],
        [VMEM] * 5 + [ANY],
        outs,
        [DMA],
        1,
        10**6,
    )(ids, qkv, out_t, up, down_t, tokens, segs, cot)[:-1]


def joined(block):
    return block[0:16, 1024:].astype(f32) + block[16:32, 1024:].astype(f32)


def put_small(value, own, blocks):
    hi, lo = split2(value)
    own[0:16, 1024:] = hi.astype(f32) + lo.astype(f32)
    for block in blocks:
        block[0:16, 1024:] = hi
        block[16:32, 1024:] = lo


def near_kernel(ids, ins, outs):
    keep, others = ins[0], ins[1:]
    if len(others) == 1:
        others = [others[0].at[i] for i in range(4)]
    for i, other in enumerate(others):
        outs[i][...] = (keep[i].astype(f32) + other[...].astype(f32)).astype(outs[i].dtype)
    if keep.shape[3] == 1152:
        value = joined(keep.at[0, 0]) + joined(others[0].at[0])
        put_small(value, outs[0].at[0], [out.at[0] for out in outs[1:]])


def near_task(keep, *others):
    shape = keep.shape[1:]
    return near_kernel, [keep, *others], shaped((shape, f32), *[(shape, bf16)] * 3)


def fork_kernel(ids, ins, outs):
    keep, other = ins
    for at, (own, send, kept, sent) in enumerate(((outs[0], outs[1], (0, 2), (1, 3)), (outs[2], outs[3], (0, 1), (2, 3)))):
        cols = slice(1024 * at, 1024 * (at + 1))
        for j in range(2):
            for out, i in ((own, kept[j]), (send, sent[j])):
                total = keep[i, :, :, cols].astype(f32) + other[i, :, :, cols].astype(f32)
                out[j] = total.astype(out.dtype)


def fork_task(keep, other):
    shape = (2, *keep.shape[1:3], 1024)
    return fork_kernel, [keep, other], shaped(*[(shape, f32), (shape, bf16)] * 2)


def half_kernel(ids, ins, outs):
    own, other = ins
    for j in range(2):
        outs[j][...] = (own[j] + other[j].astype(f32)).astype(outs[j].dtype)


def half_task(own, other):
    shape = own.shape[1:]
    return half_kernel, [own, other], shaped((shape, f32), (shape, bf16))


def join_kernel(ids, ins, outs):
    for at in range(2):
        own, other = ins[2 * at : 2 * at + 2]
        for k in range(4):
            total = own[k] + other[k].astype(f32)
            outs[k][:, 1024 * at : 1024 * (at + 1)] = total.astype(outs[k].dtype)


def join_task(own_up, other_up, own_down, other_down):
    outs = shaped(((32, 2048), f32), *[((32, 2048), bf16)] * 3)
    return join_kernel, [own_up, other_up, own_down, other_down], outs


def plane_kernel(ids, ins, outs):
    for k in range(4):
        total = ins[0][k]
        for other in ins[1:]:
            total = total + other[k].astype(f32)
        outs[k][...] = total.astype(outs[k].dtype)
    if ins[0].shape[2] == 1152:
        x, y, xy = [joined(other.at[0]) for other in ins[1:]]
        put_small((ins[0][0, 0:16, 1024:] + x) + (y + xy), outs[0], outs[1:])


def plane_task(own, others):
    shape = own.shape[1:]
    return plane_kernel, [own, *others], shaped((shape, f32), *[(shape, bf16)] * 3)


def line_total(ins, width):
    total = ins[0][:, :width]
    for other in ins[1:]:
        total = total + other[:, :width].astype(f32)
    return total


def line_kernel(ids, ins, outs):
    outs[0][...] = line_total(ins, ins[0].shape[1])


def line_task(own, others):
    return line_kernel, [own, *others], shaped((own.shape, f32))


def rows_kernel(ids, ins, outs):
    own, other = ins
    half = other.shape[0]
    outs[0][ids[1]] = own[0:half, :].astype(f32)
    outs[0][1 - ids[1]] = other[...].astype(f32)


def rows_task(own, other):
    return rows_kernel, [own, other], shaped(((2, *other.shape), f32))


def code_small(ref):
    return ref[:, 1024:1280].astype(f32) + ref[:, 1280:1536].astype(f32)


def code_sum(refs, out):
    total, small = refs[0][:, :1024].astype(f32), code_small(refs[0])
    for ref in refs[1:]:
        total = total + ref[:, :1024].astype(f32)
        small = small + code_small(ref)
    hi, lo = split2(small)
    out[:, :1024] = total.astype(bf16)
    out[:, 1024:1280] = hi
    out[:, 1280:1536] = lo


def code_near_kernel(ids, ins, outs):
    for k in range(4):
        code_sum([ref.at[k] for ref in ins], outs[k])


def code_near_task(keep, other):
    return code_near_kernel, [keep, other], shaped(*[(keep.shape[1:], bf16)] * 4)


def code_add_kernel(ids, ins, outs):
    code_sum(ins, outs[0])


def code_add_task(*parts):
    return code_add_kernel, list(parts), shaped((parts[0].shape, bf16))


def code_line_kernel(ids, ins, outs):
    for k in range(4):
        outs[0][k] = ins[k][...]


def code_line_task(*parts):
    return code_line_kernel, list(parts), shaped(((4, *parts[0].shape), bf16))


def finish_kernel(ids, ins, outs):
    mlp, attn, d_mlp, d_attn, code, code_other = ins[:4], ins[4:8], *ins[8:]
    qkv, out_t, up, down_t, book, vq_in, vq_out, gains, biases, dec_biases, small_ref = outs
    for layer, rows in enumerate((line_total(mlp, 2048), d_mlp[...])):
        up[layer] = rows[:, :1024]
        down_t[layer] = rows[:, 1024:]
    for layer, rows in enumerate((line_total(attn, 1024), d_attn[...])):
        for index in range(3):
            qkv[layer, index] = rows[:, index * 256 : (index + 1) * 256]
        out_t[layer] = rows[:, 768:]
    core, z = ids[0] % 2, ids[0] // 4
    for at, parts in ((core, code), (1 - core, code_other)):
        for k in range(4):
            part = at * 4 + (z ^ k)
            book[:, pl.ds(pl.multiple_of(part * 1024, 1024), 1024)] = parts[k, :, :1024].astype(f32)
            small_ref[:, pl.ds(pl.multiple_of(part * 256, 256), 256)] = code_small(parts.at[k])
    small = small_ref[...]
    vq_in[...] = small[:, :512]
    vq_out[...] = small[:, 512:1024]
    rest = small[:, 1024:1536]
    k1, k2, k3 = [joined(other) for other in attn[1:]]
    packed = (attn[0][0:16, 1024:] + k1) + (k2 + k3)
    for row, out in enumerate((gains.at[0:1], biases.at[0:1], gains.at[1:2], biases.at[1:2])):
        for j in range(4):
            out[:, 128 * j : 128 * (j + 1)] = packed[row * 4 + j : row * 4 + j + 1, :]
    gains[2:3, :] = rest[0:1, :]
    biases[2:3, :] = rest[1:2, :]
    gains[3:4, :] = rest[2:3, :]
    dec_biases[0:1, :] = rest[3:4, :]
    gains[4:5, :] = rest[4:5, :]
    dec_biases[1:2, :] = rest[5:6, :]


def finish_task(own_m, line_m, own_a, line_a, d_mlp, d_attn, code, code_other):
    outs = shaped(
        ((2, 3, 32, 256), f32),
        ((2, 32, 256), f32),
        ((2, 32, 1024), f32),
        ((2, 32, 1024), f32),
        ((32, 8192), f32),
        ((32, 512), f32),
        ((32, 512), f32),
        ((5, 512), f32),
        ((3, 512), f32),
        ((2, 512), f32),
        ((32, 2048), f32),
    )
    return finish_kernel, [own_m, *line_m, own_a, *line_a, d_mlp, d_attn, code, code_other], outs


def run_tasks(ids, name, tasks, after=(), carry=()):
    sizes = [(len(ins), len(outs)) for _, ins, outs in tasks]
    n_in = sum(i for i, _ in sizes)

    def kernel(ids_ref, *refs):
        at_in, at_out = 0, n_in
        for (fn, _, _), (i, o) in zip(tasks, sizes):
            fn(ids_ref, refs[at_in : at_in + i], refs[at_out : at_out + o])
            at_in, at_out = at_in + i, at_out + o

    outs = [one for _, _, many in tasks for one in many]
    res = call(
        kernel, name, [SMEM] + [VMEM] * n_in, [VMEM] * len(outs), outs, [], 10**9, 10**7, after, carry
    )(ids, *[one for _, many, _ in tasks for one in many])
    split, at = [], 0
    for _, o in sizes:
        split.append(res[at : at + o])
        at += o
    return (*split, res[-1])


def whole_groups(
    n_dp,
    tokens,
    segment_ids,
    norm_gains,
    norm_biases,
    w_qkv,
    w_attn_out,
    w_up,
    w_down,
    w_vq_in,
    w_vq_out,
    codebook,
    cotangent,
):
    dp_at, tp_at = lax.axis_index("dp"), lax.axis_index("tp")
    ids = jnp.stack([dp_at, tp_at]).astype(jnp.int32)

    def swap(values):
        return exchange(values, 0, 1, n_dp)

    gains = [norm_gains[i : i + 1] for i in range(5)]
    biases = [norm_biases[i : i + 1] for i in range(5)]
    book_t, in_t = codebook.T, w_vq_in.T
    enc_attn_shard, enc_mlp_shard, dec_shard, own, send, cot_send = pack(
        ids,
        w_qkv,
        w_attn_out.transpose(0, 2, 1),
        w_up,
        w_down.transpose(0, 2, 1),
        tokens,
        segment_ids,
        cotangent,
    )
    marked = [own, swap(send)]

    (enc_attn_line,) = stack_lines(spread_line(enc_attn_shard, n_dp), [1024])
    enc_attn = plane_quads(enc_attn_line, n_dp)
    stack, stack_t, _ = code_prep(book_t, [enc_attn_line])
    (enc_mlp_line,) = stack_lines(
        spread_line(enc_mlp_shard, n_dp), [2048], [*enc_attn[1:], stack_t, marked[1]]
    )
    enc_attn[0], dec_shard = gate([enc_mlp_line], [enc_attn[0], dec_shard])
    enc_mlp, dec_shards = plane_quads(enc_mlp_line, n_dp), spread_line(dec_shard, n_dp)
    e_x1, *e_saved, e_wa, _ = attn_fwd(
        ids, marked, [], gains[0], biases[0], core_quads(enc_attn, n_dp)
    )
    dec_lines = stack_lines(dec_shards, [1024, 1024, 1024], [e_x1, *enc_mlp[1:]])
    enc_mlp[1:], dec_attn = gate([dec_lines[0]], enc_mlp[1:]), plane_quads(dec_lines[0], n_dp)
    e, _, e_wm, _ = mlp_fwd(ids, e_x1, gains[1], biases[1], core_quads(enc_mlp, n_dp))
    *dec_attn[1:], up_line = gate([e], [*dec_attn[1:], dec_lines[1]])
    dec_attn, dec_up = core_quads(dec_attn, n_dp), plane_quads(up_line, n_dp)
    u, kept, _ = vq_fwd(e, gains[2], biases[2], in_t, w_vq_out, stack, stack_t)
    *dec_up[1:], down_line = gate([u, *dec_attn[4:]], [*dec_up[1:], dec_lines[2]])
    dec_up, dec_down = core_quads(dec_up, n_dp), plane_quads(down_line, n_dp)
    d_x1, *d_saved, d_wa, _ = attn_fwd(ids, marked, [u], gains[3], biases[3], dec_attn)
    *dec_down[1:], cot_send = gate([d_x1, *dec_up[4:]], [*dec_down[1:], cot_send])
    cot_other = swap(cot_send)
    y, y_theirs, d_wm, _ = mlp_fwd(
        ids, d_x1, gains[4], biases[4], dec_up + core_quads(dec_down, n_dp)
    )
    y_other = swap(y_theirs)

    dx1, d_small1, keep_m, send_m, _ = mlp_bwd(
        ids, d_x1, [cotangent, cot_other], gains[4], biases[4], d_wm
    )
    near_m = exchange(send_m, 1, 0, n_dp)
    du, _, d_small0, keep_a, *send_a, (keep_m,) = attn_bwd(
        ids, marked, [u], dx1, gains[3], biases[3], d_saved, d_wa, carry=[keep_m]
    )
    (own_m, *lows_m), (decoded,), send_a = run_tasks(
        ids, "sums1", [near_task(keep_m, near_m), rows_task(y, y_other)], carry=send_a
    )
    plane_m, near_a = plane_send(lows_m, n_dp), near_send(send_a, n_dp)
    de, code, code_send, (own_m, keep_a) = vq_bwd(
        ids,
        e,
        du,
        gains[2],
        biases[2],
        in_t,
        w_vq_out,
        stack,
        stack_t,
        book_t,
        kept,
        [d_small0, d_small1],
        lows_m,
        [own_m, keep_a],
    )
    (own_m, *lows_m), (own_a, *lows_a), (code_send,) = run_tasks(
        ids, "sums2", [plane_task(own_m, plane_m), near_task(keep_a, *near_a)], carry=[code_send]
    )
    line_m, plane_a = line_send(lows_m, n_dp), plane_send(lows_a, n_dp)
    code_other = exchange(code_send, 1, 0, n_dp)
    codes, _ = run_tasks(ids, "sums2b", [code_near_task(code, code_other)])
    code, *code_others = codes[0], *line_send(codes[1:], n_dp)
    ex1, e_small1, keep_m, send_m, (own_m, own_a) = mlp_bwd(
        ids, e_x1, [de], gains[1], biases[1], e_wm, [*lows_m, *lows_a, codes[1]], [own_m, own_a]
    )
    (d_mlp,), (own_a, *lows_a), (code,), (keep_m, send_m) = run_tasks(
        ids,
        "sums3",
        [line_task(own_m, line_m), plane_task(own_a, plane_a), code_add_task(code, *code_others)],
        carry=[keep_m, send_m],
    )
    line_a, near_m = line_send(lows_a, n_dp), exchange(send_m, 1, 0, n_dp)
    code_other = exchange(code, 0, 1, n_dp)
    (own_up, send_up, own_down, send_down), _ = run_tasks(
        ids, "sums3b", [fork_task(keep_m, near_m)]
    )
    other_up, other_down = exchange(send_up, 0, 1, n_dp), exchange(send_down, 2, 0, n_dp)
    dx, dx_low, _, keep_a, *send_a, (own_a, own_up, own_down) = attn_bwd(
        ids,
        marked,
        [],
        ex1,
        gains[0],
        biases[0],
        e_saved,
        e_wa,
        [e_small1],
        [*lows_a, send_up, send_down, code],
        [own_a, own_up, own_down],
    )
    (d_attn,), (code,), (own_up, send_up), (own_down, send_down), (keep_a, dx_low, *send_a) = run_tasks(
        ids,
        "sums4",
        [
            line_task(own_a, line_a),
            code_add_task(code, code_other),
            half_task(own_up, other_up),
            half_task(own_down, other_down),
        ],
        carry=[keep_a, dx_low, *send_a],
    )
    near_a, code_other = near_send(send_a, n_dp), exchange(code, 2, 0, n_dp)
    other_up, other_down = exchange(send_up, 2, 0, n_dp), exchange(send_down, 0, 1, n_dp)
    (own_a, *lows_a), (code,), (own_up, own_down, dx_low) = run_tasks(
        ids,
        "sums4b",
        [near_task(keep_a, *near_a), code_add_task(code, code_other)],
        carry=[own_up, own_down, dx_low],
    )
    plane_a, code_others = plane_send(lows_a, n_dp), line_send([code] * 3, n_dp)
    dx_other = swap(dx_low)
    (own_m, *lows_m), (code,), (own_a,) = run_tasks(
        ids,
        "sums5",
        [join_task(own_up, other_up, own_down, other_down), code_line_task(code, *code_others)],
        lows_a,
        [own_a],
    )
    line_m, code_other = line_send(lows_m, n_dp), exchange(code, 1, 0, n_dp)
    (own_a, *lows_a), (own_m,) = run_tasks(
        ids, "sums6", [plane_task(own_a, plane_a)], lows_m, [own_m]
    )
    line_a = line_send(lows_a, n_dp)
    (qkv, out_t, up, down_t, book, vq_in, vq_out, *norms, _), (grad_tokens,), _ = run_tasks(
        ids,
        "finish",
        [
            finish_task(own_m, line_m, own_a, line_a, d_mlp, d_attn, code, code_other),
            rows_task(dx, dx_other),
        ],
    )
    return (
        decoded,
        grad_tokens,
        *norms,
        qkv,
        out_t.transpose(0, 2, 1),
        up,
        down_t.transpose(0, 2, 1),
        vq_in.T,
        vq_out,
        book.T,
    )


def layer_norm(values, norm_gain, norm_bias):
    centred = values - jnp.mean(values, axis=-1, keepdims=True)
    spread = jnp.mean(centred * centred, axis=-1, keepdims=True)
    return centred * lax.rsqrt(spread + ln_eps) * norm_gain + norm_bias


def gelu_tanh(values):
    return (
        0.5 * values * (1.0 + jnp.tanh(gelu_coef * (values + 0.044715 * values * values * values)))
    )


def matmul(former, latter):
    return jnp.dot(former, latter, precision=highest, preferred_element_type=jnp.float32)


def normalize(values):
    return values * lax.rsqrt(jnp.sum(values * values, axis=-1, keepdims=True) + norm_eps)


def quantize(in_rows, norm_gain, norm_bias, in_w, out_w, code_w):
    latent = normalize(matmul(layer_norm(in_rows, norm_gain, norm_bias), in_w))
    code_rows = normalize(code_w)
    logits = matmul(latent, code_rows.T) * temper
    row_max = jnp.max(logits, axis=-1, keepdims=True)
    numerator = jnp.exp(logits - row_max)
    assign = numerator / jnp.sum(numerator, axis=-1, keepdims=True)
    soft_code = matmul(assign, code_rows)
    offset = latent - soft_code
    vq_loss = commit_weight * 1.25 * jnp.sum(offset * offset)
    return (matmul(soft_code, out_w), vq_loss)


def product(former, latter):
    return jnp.dot(former, latter, preferred_element_type=jnp.float32)


def product_tn(former, latter):
    return lax.dot_general(
        former, latter, (((0,), (0,)), ((), ())), preferred_element_type=jnp.float32
    )


def product_nt(former, latter):
    return lax.dot_general(
        former, latter, (((1,), (1,)), ((), ())), preferred_element_type=jnp.float32
    )


def split_heads(values):
    return values.reshape(values.shape[0], values.shape[1] // HEAD_DIM, HEAD_DIM).transpose(1, 0, 2)


def join_heads(values):
    return values.transpose(1, 0, 2).reshape(values.shape[1], values.shape[0] * HEAD_DIM)


def masked_scores(query_blk, key_h, seg_blk, seg_keys):
    scores = jnp.einsum(
        "hqd,hkd->hqk", query_blk, key_h, preferred_element_type=jnp.float32
    ) * HEAD_DIM ** (-0.5)
    return jnp.where((seg_blk[:, None] == seg_keys[None, :])[None], scores, masked_score)


def attend(query_h, key_h, value_h, seg_keys):
    block_rows = min(512, query_h.shape[1])
    block_count = query_h.shape[1] // block_rows

    def one_block(begin_row):
        query_blk = lax.dynamic_slice_in_dim(query_h, begin_row, block_rows, 1)
        seg_blk = lax.dynamic_slice_in_dim(seg_keys, begin_row, block_rows, 0)
        scores = masked_scores(query_blk, key_h, seg_blk, seg_keys)
        row_max = jnp.max(scores, axis=-1, keepdims=True)
        numerator = jnp.exp(scores - row_max)
        row_total = jnp.sum(numerator, axis=-1, keepdims=True)
        prob_low = (numerator / row_total).astype(jnp.bfloat16)
        attended = jnp.einsum("hqk,hkd->hqd", prob_low, value_h, preferred_element_type=jnp.float32)
        return (attended.astype(jnp.bfloat16), (row_max + jnp.log(row_total))[..., 0])

    starts = jnp.arange(block_count, dtype=jnp.int32) * block_rows
    attended, log_sums = lax.map(one_block, starts)
    heads_out = attended.transpose(1, 0, 2, 3).reshape(query_h.shape)
    log_sums = log_sums.transpose(1, 0, 2).reshape(query_h.shape[0], query_h.shape[1])
    return (heads_out, log_sums)


def attend_back(query_h, key_h, value_h, seg_keys, log_sums, grad_out):
    block_rows = min(512, query_h.shape[1])
    block_count = query_h.shape[1] // block_rows

    def one_block(carry, begin_row):
        grad_key, grad_value = carry
        query_blk = lax.dynamic_slice_in_dim(query_h, begin_row, block_rows, 1)
        grad_blk = lax.dynamic_slice_in_dim(grad_out, begin_row, block_rows, 1)
        lse_blk = lax.dynamic_slice_in_dim(log_sums, begin_row, block_rows, 1)
        seg_blk = lax.dynamic_slice_in_dim(seg_keys, begin_row, block_rows, 0)
        scores = masked_scores(query_blk, key_h, seg_blk, seg_keys)
        probs = jnp.exp(scores - lse_blk[..., None])
        prob_low = probs.astype(jnp.bfloat16)
        grad_value = grad_value + jnp.einsum(
            "hqk,hqd->hkd", prob_low, grad_blk, preferred_element_type=jnp.float32
        )
        grad_prob = jnp.einsum(
            "hqd,hkd->hqk", grad_blk, value_h, preferred_element_type=jnp.float32
        )
        row_dot = jnp.sum(probs * grad_prob, axis=-1, keepdims=True)
        grad_score = (probs * (grad_prob - row_dot) * HEAD_DIM ** (-0.5)).astype(jnp.bfloat16)
        grad_query = jnp.einsum(
            "hqk,hkd->hqd", grad_score, key_h, preferred_element_type=jnp.float32
        )
        grad_key = grad_key + jnp.einsum(
            "hqk,hqd->hkd", grad_score, query_blk, preferred_element_type=jnp.float32
        )
        return ((grad_key, grad_value), grad_query)

    starts = jnp.arange(block_count, dtype=jnp.int32) * block_rows
    zeros_kv = jnp.zeros(key_h.shape, jnp.float32)
    (grad_key, grad_value), grad_query = lax.scan(one_block, (zeros_kv, zeros_kv), starts)
    grad_query = grad_query.transpose(1, 0, 2, 3).reshape(query_h.shape)
    return (
        grad_query.astype(jnp.bfloat16),
        grad_key.astype(jnp.bfloat16),
        grad_value.astype(jnp.bfloat16),
    )


def spread_rows(values):
    return lax.all_gather(values, "tp", axis=0, tiled=True)


def combine_rows(partial_value):
    return lax.psum_scatter(partial_value, "tp", scatter_dimension=0, tiled=True)


def spread_grads(values):
    return lax.all_gather(values, "tp", axis=0, tiled=True)


def combine_grads(partial_value):
    return lax.psum_scatter(
        partial_value.astype(jnp.bfloat16), "tp", scatter_dimension=0, tiled=True
    ).astype(jnp.float32)


def fetch_weights(w_qkv, w_attn_out, w_up, w_down, layer):
    return (
        lax.all_gather(w_qkv[layer], "dp", axis=1, tiled=True),
        lax.all_gather(w_attn_out[layer], "dp", axis=1, tiled=True),
        lax.all_gather(w_up[layer], "dp", axis=0, tiled=True),
        lax.all_gather(w_down[layer], "dp", axis=1, tiled=True),
    )


def reduce_weight_grads(grads):
    return (
        lax.psum_scatter(
            grads[0].astype(jnp.bfloat16), "dp", scatter_dimension=1, tiled=True
        ).astype(jnp.float32),
        lax.psum_scatter(
            grads[1].astype(jnp.bfloat16), "dp", scatter_dimension=1, tiled=True
        ).astype(jnp.float32),
        lax.psum_scatter(
            grads[2].astype(jnp.bfloat16), "dp", scatter_dimension=0, tiled=True
        ).astype(jnp.float32),
        lax.psum_scatter(
            grads[3].astype(jnp.bfloat16), "dp", scatter_dimension=1, tiled=True
        ).astype(jnp.float32),
    )


def block_forward(resid_in, seg_local, gains, biases, weights):
    qkv_w, attn_w, up_w, down_w = weights
    normed = layer_norm(resid_in, gains[0], biases[0]).astype(jnp.bfloat16)
    normed_all, seg_all = (
        lax.all_gather(normed, "tp", axis=0, tiled=True),
        lax.all_gather(seg_local, "tp", axis=0, tiled=True),
    )
    query_h = split_heads(product(normed_all, qkv_w[0]).astype(jnp.bfloat16))
    key_h = split_heads(product(normed_all, qkv_w[1]).astype(jnp.bfloat16))
    value_h = split_heads(product(normed_all, qkv_w[2]).astype(jnp.bfloat16))
    heads_out, log_sums = attend(query_h, key_h, value_h, seg_all)
    attn_rows = join_heads(heads_out)
    middle = resid_in + combine_rows(product(attn_rows, attn_w))
    normed_mid = spread_rows(layer_norm(middle, gains[1], biases[1]).astype(jnp.bfloat16))
    hidden_pre = product(normed_mid, up_w)
    hidden = gelu_tanh(hidden_pre).astype(jnp.bfloat16)
    result = middle + combine_rows(product(hidden, down_w))
    kept = (
        resid_in,
        middle,
        normed_all,
        seg_all,
        query_h,
        key_h,
        value_h,
        log_sums,
        attn_rows,
        normed_mid,
        hidden_pre,
        hidden,
    )
    return (result, kept)


def block_backward(kept, gains, biases, weights, grad_result):
    (
        resid_in,
        middle,
        normed_all,
        seg_all,
        query_h,
        key_h,
        value_h,
        log_sums,
        attn_rows,
        normed_mid,
        hidden_pre,
        hidden,
    ) = kept
    qkv_w, attn_w, up_w, down_w = weights
    grad_branch = spread_grads(grad_result.astype(jnp.bfloat16))
    grad_down = product_tn(hidden, grad_branch)
    grad_hidden = product_nt(grad_branch, down_w)
    _, gelu_back = jax.vjp(gelu_tanh, hidden_pre)
    grad_pre = gelu_back(grad_hidden)[0].astype(jnp.bfloat16)
    grad_up = product_tn(normed_mid, grad_pre)
    grad_norm_mid = combine_grads(product_nt(grad_pre, up_w))
    _, norm_back_mid = jax.vjp(layer_norm, middle, gains[1], biases[1])
    grad_mid_ln, grad_gain_mid, grad_bias_mid = norm_back_mid(grad_norm_mid)
    grad_middle = grad_result + grad_mid_ln
    grad_attn_all = spread_grads(grad_middle.astype(jnp.bfloat16))
    grad_attn = product_tn(attn_rows, grad_attn_all)
    grad_heads = split_heads(product_nt(grad_attn_all, attn_w).astype(jnp.bfloat16))
    grad_query, grad_key, grad_value = attend_back(
        query_h, key_h, value_h, seg_all, log_sums, grad_heads
    )
    grad_parts = [join_heads(grad_query), join_heads(grad_key), join_heads(grad_value)]
    grad_qkv = jnp.stack([product_tn(normed_all, grad_part) for grad_part in grad_parts])
    grad_normed_part = (
        product_nt(grad_parts[0], qkv_w[0])
        + product_nt(grad_parts[1], qkv_w[1])
        + product_nt(grad_parts[2], qkv_w[2])
    )
    grad_normed = combine_grads(grad_normed_part)
    _, norm_back_in = jax.vjp(layer_norm, resid_in, gains[0], biases[0])
    grad_in_ln, grad_gain_in, grad_bias_in = norm_back_in(grad_normed)
    gain_grads = jnp.stack([grad_gain_in, grad_gain_mid])
    bias_grads = jnp.stack([grad_bias_in, grad_bias_mid])
    return (
        grad_middle + grad_in_ln,
        gain_grads,
        bias_grads,
        (grad_qkv, grad_attn, grad_up, grad_down),
    )


def local(
    tokens,
    segment_ids,
    norm_gains,
    norm_biases,
    w_qkv,
    w_attn_out,
    w_up,
    w_down,
    w_vq_in,
    w_vq_out,
    codebook,
    cotangent,
):
    gain_sum = jnp.zeros(norm_gains.shape, jnp.float32)
    bias_sum = jnp.zeros(norm_biases.shape, jnp.float32)
    vq_in_sum = jnp.zeros(w_vq_in.shape, jnp.float32)
    vq_out_sum = jnp.zeros(w_vq_out.shape, jnp.float32)
    code_sum = jnp.zeros(codebook.shape, jnp.float32)
    layer_sums = [None, None]
    outputs = []
    input_grads = []
    for micro in range(MICRO):
        resid_in = tokens[micro].astype(jnp.float32)
        seg_local = segment_ids[micro]
        enc_weights = fetch_weights(w_qkv, w_attn_out, w_up, w_down, 0)
        encoded, enc_kept = block_forward(
            resid_in, seg_local, norm_gains[0:2], norm_biases[0:2], enc_weights
        )
        (decoder_in, _), vq_back = jax.vjp(
            quantize, encoded, norm_gains[2], norm_biases[2], w_vq_in, w_vq_out, codebook
        )
        dec_weights = fetch_weights(w_qkv, w_attn_out, w_up, w_down, 1)
        decoded, dec_kept = block_forward(
            decoder_in, seg_local, norm_gains[3:5], norm_biases[3:5], dec_weights
        )
        outputs.append(decoded)
        grad_dec_in, gains_dec, biases_dec, grads_dec = block_backward(
            dec_kept, norm_gains[3:5], norm_biases[3:5], dec_weights, cotangent[micro]
        )
        grad_encoded, grad_gain_vq, grad_bias_vq, grad_in_w, grad_out_w, grad_codes = vq_back(
            (grad_dec_in, jnp.ones((), jnp.float32))
        )
        grad_input, gains_enc, biases_enc, grads_enc = block_backward(
            enc_kept, norm_gains[0:2], norm_biases[0:2], enc_weights, grad_encoded
        )
        input_grads.append(grad_input)
        gain_sum = gain_sum + jnp.concatenate([gains_enc, grad_gain_vq[None], gains_dec], axis=0)
        bias_sum = bias_sum + jnp.concatenate([biases_enc, grad_bias_vq[None], biases_dec], axis=0)
        vq_in_sum = vq_in_sum + grad_in_w
        vq_out_sum = vq_out_sum + grad_out_w
        code_sum = code_sum + grad_codes
        for layer, grads in ((0, grads_enc), (1, grads_dec)):
            reduced = reduce_weight_grads(grads)
            if layer_sums[layer] is None:
                layer_sums[layer] = reduced
            else:
                layer_sums[layer] = jax.tree.map(jnp.add, layer_sums[layer], reduced)
    gain_tot, bias_tot, vq_in_tot, vq_out_tot, code_tot = lax.psum(
        (gain_sum, bias_sum, vq_in_sum, vq_out_sum, code_sum), ("dp", "tp")
    )
    return (
        jnp.stack(outputs),
        jnp.stack(input_grads),
        gain_tot,
        bias_tot[0:3],
        bias_tot[3:5],
        jnp.stack([layer_sums[0][0], layer_sums[1][0]]),
        jnp.stack([layer_sums[0][1], layer_sums[1][1]]),
        jnp.stack([layer_sums[0][2], layer_sums[1][2]]),
        jnp.stack([layer_sums[0][3], layer_sums[1][3]]),
        vq_in_tot,
        vq_out_tot,
        code_tot,
    )


def solution(mesh):
    n_dp, n_tp = mesh.shape["dp"], mesh.shape["tp"]
    fits = n_tp == MICRO and n_dp == 16
    return jax.shard_map(
        functools.partial(whole_groups, n_dp) if fits else local,
        mesh=mesh,
        in_specs=(
            P(None, ("dp", "tp"), None),
            P(None, ("dp", "tp")),
            P(),
            P(),
            P(None, None, "dp", "tp"),
            P(None, "tp", "dp"),
            P(None, "dp", "tp"),
            P(None, "tp", "dp"),
            P(),
            P(),
            P(),
            P(None, ("dp", "tp"), None),
        ),
        out_specs=(
            P(None, ("dp", "tp"), None),
            P(None, ("dp", "tp"), None),
            P(),
            P(),
            P(),
            P(None, None, "dp", "tp"),
            P(None, "tp", "dp"),
            P(None, "dp", "tp"),
            P(None, "tp", "dp"),
            P(),
            P(),
            P(),
        ),
        check_vma=False,
    )
```

```python
import functools

import jax
import jax.numpy as jnp
from jax import lax
from jax.experimental import pallas as pl
from jax.experimental.pallas import tpu as pltpu
from jax.sharding import PartitionSpec as P

HEAD_DIM = 64
MICRO = 2
bf16 = jnp.bfloat16
f32 = jnp.float32
highest = lax.Precision.HIGHEST
ln_eps = 1e-05
norm_eps = 1e-06
temper = 10.0
commit_weight = 64.0
gelu_coef = 0.7978845608028654
masked_score = -1e30
log2e = 1.4426950408889634
vmem_cap = 36 * 1024 * 1024


PLANE = ((0, 0), (0, 1), (1, 0), (1, 1))


def exchange(values, dp_xor, tp_xor, n_dp):
    pairs = [
        (d * 2 + t, (d ^ dp_xor) * 2 + (t ^ tp_xor)) for d in range(n_dp) for t in range(2)
    ]
    return lax.ppermute(values, ("dp", "tp"), pairs)


def spread_line(shard, n_dp):
    return jnp.stack([shard] + [exchange(shard, 4 * k, 0, n_dp) for k in range(1, 4)])


def plane_quads(own, n_dp):
    return [own] + [exchange(own, 2 * y, x, n_dp) for y, x in PLANE[1:]]


def plane_send(lows, n_dp):
    return [exchange(low, 2 * y, x, n_dp) for (y, x), low in zip(PLANE[1:], lows)]


def line_send(lows, n_dp):
    return [exchange(low, 4 * k, 0, n_dp) for k, low in zip(range(1, 4), lows)]


def block_places():
    for core in range(2):
        for index, (y, x) in enumerate(PLANE):
            for k in range(4):
                yield core * 4 + index, k, k * 4 + y * 2 + core, x


def dot(a, b):
    return jnp.dot(a, b, preferred_element_type=f32)


def dot_nt(a, b, precision=None):
    return lax.dot_general(
        a, b, (((1,), (1,)), ((), ())), preferred_element_type=f32, precision=precision
    )


def dot_full(a, b):
    return jnp.dot(a, b, preferred_element_type=f32, precision=highest)


def ln_parts(x):
    centred = x - jnp.mean(x, axis=-1, keepdims=True)
    inv = lax.rsqrt(jnp.mean(centred * centred, axis=-1, keepdims=True) + ln_eps)
    return centred * inv, inv


def ln_back(grad, xhat, inv, gain):
    scaled = grad * gain
    return inv * (
        scaled
        - jnp.mean(scaled, axis=-1, keepdims=True)
        - xhat * jnp.mean(scaled * xhat, axis=-1, keepdims=True)
    )


def split2(x):
    hi = x.astype(bf16)
    return hi, (x - hi.astype(f32)).astype(bf16)


def split3(x):
    hi, _ = split2(x)
    rest = x - hi.astype(f32)
    mid = rest.astype(bf16)
    return hi, mid, (rest - mid.astype(f32)).astype(bf16)


def weight_copies(ids_ref, refs, w_ref, sems, first=0):
    copies, width = [], w_ref.shape[2]
    if len(refs) == 1:
        for owner in range(32):
            copies.append(
                pltpu.make_async_copy(
                    refs[0].at[owner, :, pl.ds(first, width)],
                    w_ref.at[owner % 2, pl.ds(owner // 2 * 32, 32), :],
                    sems.at[owner],
                )
            )
        return copies
    for slot, (which, k, dp_xor, tp_xor) in enumerate(block_places()):
        row = pl.multiple_of((ids_ref[0] ^ dp_xor) * 32, 32)
        copies.append(
            pltpu.make_async_copy(
                refs[which // 4].at[which % 4, k],
                w_ref.at[ids_ref[1] ^ tp_xor, pl.ds(row, 32), :],
                sems.at[slot],
            )
        )
    return copies


def grad_copies(ids_ref, g_ref, refs, sems):
    copies = []
    if len(refs) == 1:
        for owner in range(32):
            copies.append(
                pltpu.make_async_copy(
                    g_ref.at[owner % 2, pl.ds(owner // 2 * 32, 32), :],
                    refs[0].at[owner],
                    sems.at[owner],
                )
            )
        return copies
    for slot, (which, k, dp_xor, tp_xor) in enumerate(block_places()):
        row = pl.multiple_of((ids_ref[0] ^ dp_xor) * 32, 32)
        copies.append(
            pltpu.make_async_copy(
                g_ref.at[ids_ref[1] ^ tp_xor, pl.ds(row, 32), :],
                refs[which // 4].at[which % 4, k],
                sems.at[slot],
            )
        )
    return copies


def start_all(copies):
    for copy in copies:
        copy.start()


def wait_all(copies):
    for copy in copies:
        copy.wait()


def head_rows(ref, pair, which):
    own = ref[pl.ds(pl.multiple_of(pair * 128 + which * HEAD_DIM, HEAD_DIM), HEAD_DIM), :]
    zero = jnp.zeros_like(own)
    return jnp.concatenate([own, zero] if which == 0 else [zero, own], axis=0)


def segment_mask(own, other):
    ids = jnp.concatenate([own[:, 512:], other[:, 512:]], axis=0).astype(f32)
    return jnp.where(ids[:, 0:1] == ids.T[0:1, :], 0.0, masked_score)


def load_rows(x, own, other):
    if x is None:
        return jnp.concatenate([own[:, :512], other[:, :512]], axis=0).astype(f32)
    return x[...]


def attn_fwd_kernel(with_x, n_w, ids, own, other, gain, bias, *refs):
    x, refs = (refs[0], refs[1:]) if with_x else (None, refs)
    w_refs, refs = refs[:n_w], refs[n_w:]
    x1, lse, saved, refs = refs[0], refs[1], refs[2:8], refs[8:]
    w, h, vt, ot, mask, qs, k, v, o, qst, kt, sems, out_sems = refs
    copies = weight_copies(ids, w_refs, w, sems)
    start_all(copies)
    keeps = [
        pltpu.make_async_copy(held, to, out_sems.at[at])
        for at, (held, to) in enumerate(zip((qs, k, v, o, qst, kt), saved))
    ]
    xf = load_rows(x, own, other)
    h[...] = (ln_parts(xf)[0] * gain[...] + bias[...]).astype(bf16)
    mask[...] = segment_mask(own, other)
    wait_all(copies)
    for t in range(2):
        cols = pl.ds(t * 256, 256)
        qs[:, cols] = (dot(h[...], w[t, :, 0:256]).astype(bf16) * HEAD_DIM ** (-0.5)).astype(bf16)
        k[:, cols] = dot(h[...], w[t, :, 256:512]).astype(bf16)
        v[:, cols] = dot(h[...], w[t, :, 512:768]).astype(bf16)
    qst[...] = qs[...].T
    kt[...] = k[...].T
    vt[...] = v[...].T
    for at in (0, 1, 2, 4, 5):
        keeps[at].start()

    def one_pair(pair, _):
        lanes = pl.ds(pl.multiple_of(pair * 128, 128), 128)
        k_pair = k[:, lanes]
        for which in range(2):
            scores = dot(k_pair, head_rows(qst, pair, which)) + mask[...]
            top = jnp.max(scores, axis=0, keepdims=True)
            numer = jnp.exp(scores - top).astype(bf16)
            rows = pl.ds(pl.multiple_of(pair * 128 + which * HEAD_DIM, HEAD_DIM), HEAD_DIM)
            left = jnp.concatenate([vt[rows, :], jnp.ones((16, 512), bf16)], axis=0)
            both = dot(left, numer)
            total = both[HEAD_DIM : HEAD_DIM + 1, :]
            ot[rows, :] = (both[:HEAD_DIM, :] / total).astype(bf16)
            lse[pl.ds(pair * 2 + which, 1), :] = top + jnp.log(total)
        return 0

    lax.fori_loop(0, 4, one_pair, 0)
    o[...] = ot[...].T
    keeps[3].start()
    acc = xf
    for t in range(2):
        acc = acc + dot_nt(o[:, t * 256 : (t + 1) * 256], w[t, :, 768:1024])
    x1[...] = acc
    wait_all(keeps)


def gelu_parts(u):
    square = u * u
    tanh = jnp.tanh(gelu_coef * u * (1.0 + 0.044715 * square))
    return 0.5 * u * (1.0 + tanh), tanh, square


def mlp_fwd_kernel(n_w, first, ids, x1, gain, bias, *refs):
    w_refs, refs = refs[:n_w], refs[n_w:]
    y, theirs, w, h2, sems = refs
    copies = weight_copies(ids, w_refs, w, sems, first)
    start_all(copies)
    h2[...] = (ln_parts(x1[...])[0] * gain[...] + bias[...]).astype(bf16)
    y[...] = x1[...]
    wait_all(copies)

    def one_chunk(index, _):
        t = index // 2
        col = (index % 2) * 512
        pre = dot(h2[...], w[t, :, pl.ds(pl.multiple_of(col, 512), 512)])
        hidden = gelu_parts(pre)[0].astype(bf16)
        y[...] += dot_nt(hidden, w[t, :, pl.ds(pl.multiple_of(col + 1024, 512), 512)])
        return 0

    lax.fori_loop(0, 4, one_chunk, 0)
    theirs[...] = y[256:, :]


def mlp_bwd_kernel(split, n_w, first, n_g, ids, x1, gain, bias, *refs):
    w_refs, refs = refs[:n_w], refs[n_w:]
    if split:
        own, other, refs = refs[0], refs[1], refs[2:]
    else:
        dy, refs = refs[0], refs[1:]
    dx1, small, refs = refs[0], refs[1], refs[2:]
    g_refs, refs = refs[:n_g], refs[n_g:]
    w, g, h2, h2t, dyb, dybt, dh2, w_sems, sems = refs[:9]
    loads = weight_copies(ids, w_refs, w, w_sems, first)
    start_all(loads)
    if split:
        dy = refs[9]
        dy[0:256, :] = own[ids[1]]
        dy[256:, :] = other[...]
    h2[...] = (ln_parts(x1[...])[0] * gain[...] + bias[...]).astype(bf16)
    h2t[...] = h2[...].T
    dyb[...] = dy[...].astype(bf16)
    dybt[...] = dyb[...].T
    dh2[...] = jnp.zeros_like(dh2)
    wait_all(loads)

    def one_chunk(index, _):
        t = index // 2
        up = pl.ds(pl.multiple_of((index % 2) * 512, 512), 512)
        down = pl.ds(pl.multiple_of((index % 2) * 512 + 1024, 512), 512)
        pre = dot(h2[...], w[t, :, up])
        hidden, tanh, square = gelu_parts(pre)
        slope = 0.5 * (1.0 + tanh) + (0.5 * gelu_coef) * pre * (1.0 - tanh * tanh) * (
            1.0 + (3 * 0.044715) * square
        )
        dhidden = dot(dyb[...], w[t, :, down])
        dpre = (dhidden * slope).astype(bf16)
        g[t, :, down] = dot(dybt[...], hidden.astype(bf16)).astype(bf16)
        g[t, :, up] = dot(h2t[...], dpre).astype(bf16)
        dh2[...] += dot_nt(dpre, w[t, :, up])
        return 0

    lax.fori_loop(0, 4, one_chunk, 0)
    copies = grad_copies(ids, g, g_refs, sems)
    start_all(copies)
    xhat, inv = ln_parts(x1[...])
    grad = dh2[...]
    small[0:1, :] = jnp.sum(grad * xhat, axis=0, keepdims=True)
    small[1:2, :] = jnp.sum(grad, axis=0, keepdims=True)
    dx1[...] = dy[...] + ln_back(grad, xhat, inv, gain[...])
    for copy in copies:
        copy.wait()


def pack_rows(rows):
    cut = [row[:, 128 * j : 128 * (j + 1)] for row in rows for j in range(4)]
    return jnp.concatenate(split2(jnp.concatenate(cut, axis=0)), axis=0)


def attn_bwd_kernel(with_x, with_small, n_w, n_g, ids, own, other, dx1, gain, bias, lse, *refs):
    saved, w_refs, refs = refs[:6], refs[6 : 6 + n_w], refs[6 + n_w :]
    x, refs = (refs[0], refs[1:]) if with_x else (None, refs)
    if with_small:
        other_small, refs = refs[0], refs[1:]
    dx, dx_low, small = refs[:3]
    g_refs, refs = refs[3 : 3 + n_g], refs[3 + n_g :]
    w, g, h, mask, do, dot_t, dqt, dq, dk, dv, flip = refs[:11]
    qs, k, v, o, qst, kt, w_sems, in_sems, sems = refs[11:]
    loads = weight_copies(ids, w_refs, w, w_sems)
    start_all(loads)
    takes = [
        pltpu.make_async_copy(held, to, in_sems.at[at])
        for at, (held, to) in enumerate(zip(saved, (qs, k, v, o, qst, kt)))
    ]
    start_all(takes)
    xf = load_rows(x, own, other)
    h[...] = (ln_parts(xf)[0] * gain[...] + bias[...]).astype(bf16)
    mask[...] = segment_mask(own, other)
    low = dx1[...].astype(bf16)
    flip[...] = low.T
    wait_all(loads)
    wait_all(takes)
    for t in range(2):
        cols = pl.ds(t * 256, 256)
        do[:, cols] = dot(low, w[t, :, 768:1024]).astype(bf16)
        g[t, :, 768:1024] = dot(flip[...], o[:, cols]).astype(bf16)
    dot_t[...] = do[...].T
    def one_pair(pair, _):
        lanes = pl.ds(pl.multiple_of(pair * 128, 128), 128)
        k_pair, v_pair = k[:, lanes], v[:, lanes]
        q_pair, do_pair = qs[:, lanes], do[:, lanes]
        dvs, dks = [], []
        for which in range(2):
            head = pl.ds(pair * 2 + which, 1)
            rows = pl.ds(pl.multiple_of(pair * 128 + which * HEAD_DIM, HEAD_DIM), HEAD_DIM)
            scores = dot(k_pair, head_rows(qst, pair, which)) + mask[...]
            probs = jnp.exp(scores - lse[head, :])
            dprobs = dot(v_pair, head_rows(dot_t, pair, which))
            shift = jnp.sum(probs * dprobs, axis=0, keepdims=True)
            dscore = (probs * (dprobs - shift)).astype(bf16)
            dvs.append(dot(probs.astype(bf16), do_pair))
            dks.append(dot(dscore, q_pair))
            dqt[rows, :] = (dot(kt[rows, :], dscore) * HEAD_DIM ** (-0.5)).astype(bf16)
        first = lax.broadcasted_iota(jnp.int32, (512, 128), 1) < HEAD_DIM
        dv[:, lanes] = jnp.where(first, dvs[0], dvs[1]).astype(bf16)
        dk[:, lanes] = jnp.where(first, dks[0], dks[1]).astype(bf16)
        return 0

    lax.fori_loop(0, 4, one_pair, 0)
    dq[...] = dqt[...].T
    flip[...] = h[...].T
    for t in range(2):
        cols = pl.ds(t * 256, 256)
        g[t, :, 0:256] = dot(flip[...], dq[:, cols]).astype(bf16)
        g[t, :, 256:512] = dot(flip[...], dk[:, cols]).astype(bf16)
        g[t, :, 512:768] = dot(flip[...], dv[:, cols]).astype(bf16)
    grad = jnp.zeros((512, 512), f32)
    for t in range(2):
        cols = pl.ds(t * 256, 256)
        for index, part in enumerate((dq, dk, dv)):
            grad = grad + dot_nt(part[:, cols], w[t, :, index * 256 : (index + 1) * 256])
    xhat, inv = ln_parts(xf)
    dgain = jnp.sum(grad * xhat, axis=0, keepdims=True)
    dbias = jnp.sum(grad, axis=0, keepdims=True)
    small[0:1, :] = dgain
    small[1:2, :] = dbias
    if with_small:
        packed = pack_rows([dgain, dbias, other_small[0:1, :], other_small[1:2, :]])
        for t in range(2):
            for row in range(16):
                g[t, row * 32 : (row + 1) * 32, 1024:1152] = packed
    copies = grad_copies(ids, g, g_refs, sems)
    start_all(copies)
    total = dx1[...] + ln_back(grad, xhat, inv, gain[...])
    dx[...] = total
    dx_low[...] = total[256:, :].astype(bf16)
    for copy in copies:
        copy.wait()


def code_prep_kernel(book_t, stack, stack_t):
    def one_chunk(index, _):
        lanes = pl.ds(pl.multiple_of(index * 512, 512), 512)
        rows = book_t[:, lanes]
        unit = rows * lax.rsqrt(jnp.sum(rows * rows, axis=0, keepdims=True) + norm_eps)
        hi, mid, lo = split3(unit)
        stack_t[:, lanes] = jnp.concatenate([hi, mid, lo, jnp.ones((32, 512), bf16)], axis=0)
        tall = jnp.concatenate([hi, mid, lo, hi, mid, hi, jnp.zeros((64, 512), bf16)], axis=0)
        stack[lanes, :] = tall.T
        return 0

    lax.fori_loop(0, book_t.shape[1] // 512, one_chunk, 0)


def factor_stack(x):
    hi, mid, lo = split3(x)
    return jnp.concatenate([hi, hi, hi, mid, mid, lo, jnp.zeros((64, x.shape[1]), bf16)], axis=0)


def code_loads(pairs, sems):
    loads = []
    for piece in range(4):
        group = []
        for at, (held, to, by_row) in enumerate(pairs):
            size = held.shape[0 if by_row else 1] // 4
            part = pl.ds(piece * size, size)
            place = (part, slice(None)) if by_row else (slice(None), part)
            group.append(pltpu.make_async_copy(held.at[place], to.at[place], sems.at[at, piece]))
        start_all(group)
        loads.append(group)
    return loads


def vq_fwd_kernel(
    e, gain, bias, in_t, out_w, stack_hbm, stack_t_hbm, u, kept, acc, stack, stack_t, sems
):
    loads = code_loads([(stack_hbm, stack, True), (stack_t_hbm, stack_t, False)], sems)
    lnv = ln_parts(e[...])[0] * gain[...] + bias[...]
    raw = dot_nt(in_t[...], lnv, highest)
    inv = lax.rsqrt(jnp.sum(raw * raw, axis=0, keepdims=True) + norm_eps)
    latent = raw * inv
    right = factor_stack(latent * (temper * log2e))
    acc[...] = jnp.zeros_like(acc)

    def one_chunk(index, _):
        codes = pl.ds(pl.multiple_of(index * 512, 512), 512)
        numer = jnp.exp2(dot(stack[codes, :], right)).astype(bf16)
        acc[...] += dot(stack_t[:, codes], numer)
        return 0

    chunks = stack.shape[0] // 512
    for piece, group in enumerate(loads):
        wait_all(group)
        lax.fori_loop(chunks * piece // 4, chunks * (piece + 1) // 4, one_chunk, 0)
    total = acc[96:97, :]
    soft = (acc[0:32, :] + acc[32:64, :] + acc[64:96, :]) / total
    kept[0:32, :] = latent
    kept[32:64, :] = soft
    kept[64:65, :] = total
    kept[65:66, :] = inv
    u[...] = dot_full(soft.T, out_w[...])


def vq_bwd_kernel(ids, e, du, gain, bias, in_t, out_w, stack_hbm, stack_t_hbm, book_hbm, kept, *refs):
    small0, small1, de, code_keep, code_send = refs[:5]
    acc, grads, small, tail, stack, stack_t, book_t, load_sems, sems = refs[5:]
    loads = code_loads(
        [(stack_hbm, stack, True), (stack_t_hbm, stack_t, False), (book_hbm, book_t, False)],
        load_sems,
    )
    xhat, inv_ln = ln_parts(e[...])
    lnv = xhat * gain[...] + bias[...]
    latent, soft = kept[0:32, :], kept[32:64, :]
    total, inv = kept[64:65, :], kept[65:66, :]
    direct = (2.0 * 1.25 * commit_weight) * (latent - soft)
    dsoft = dot_nt(out_w[...], du[...], highest) - direct
    small[32:64, :] = dot_full(soft, du[...])
    shift = jnp.sum(dsoft * soft, axis=0, keepdims=True) / total
    dsoft = dsoft / total
    right = jnp.concatenate(
        [factor_stack(latent * (temper * log2e)), factor_stack(dsoft)], axis=1
    )
    pads = jnp.zeros((64, 512), f32)

    def tall(x):
        hi, lo = split2(x)
        return jnp.concatenate([hi.astype(f32), lo.astype(f32), pads], axis=0).T.astype(bf16)

    sides = jnp.concatenate([tall(dsoft), tall(latent * temper)], axis=0)
    acc[...] = jnp.zeros_like(acc)

    def one_chunk(index, _):
        codes = pl.ds(pl.multiple_of(index * 512, 512), 512)
        both = dot(stack[codes, :], right)
        numer = jnp.exp2(both[:, :512])
        dlogit = (numer * (both[:, 512:] - shift)).astype(bf16)
        acc[...] += dot(stack_t[0:96, codes], dlogit)
        dcode = dot(jnp.concatenate([numer.astype(bf16), dlogit], axis=1), sides).T
        dcode = dcode[0:32, :] + dcode[32:64, :]
        rows = book_t[:, codes]
        scale = lax.rsqrt(jnp.sum(rows * rows, axis=0, keepdims=True) + norm_eps)
        unit = rows * scale
        grads[:, codes] = (
            scale * (dcode - unit * jnp.sum(unit * dcode, axis=0, keepdims=True))
        ).astype(bf16)
        return 0

    chunks = stack.shape[0] // 512
    for piece, group in enumerate(loads):
        wait_all(group)
        lax.fori_loop(chunks * piece // 4, chunks * (piece + 1) // 4, one_chunk, 0)
    dlatent = temper * (acc[0:32, :] + acc[32:64, :] + acc[64:96, :]) + direct
    draw = inv * (dlatent - latent * jnp.sum(latent * dlatent, axis=0, keepdims=True))
    small[0:32, :] = dot_full(draw, lnv)
    dln = dot_full(draw.T, in_t[...])
    small[64:65, :] = jnp.sum(dln * xhat, axis=0, keepdims=True)
    small[65:66, :] = jnp.sum(dln, axis=0, keepdims=True)
    small[66:68, :] = small0[0:2, :]
    small[68:70, :] = small1[0:2, :]
    small[70:96, :] = jnp.zeros((26, 512), f32)
    for block in range(3):
        for at, part in enumerate(split2(small[block * 32 : (block + 1) * 32, :])):
            for side in range(2):
                tail[block * 2 + side, :, at * 256 : (at + 1) * 256] = part[
                    :, side * 256 : (side + 1) * 256
                ]
    tail[6:8] = jnp.zeros((2, 32, 512), bf16)
    core, z = ids[0] % 2, ids[0] // 4
    copies = []
    for slot, (at, to) in enumerate(((core, code_keep), (1 - core, code_send))):
        for k in range(4):
            part = at * 4 + (z ^ k)
            lanes = pl.ds(pl.multiple_of(part * 1024, 1024), 1024)
            copies += [
                pltpu.make_async_copy(
                    grads.at[:, lanes], to.at[k, :, pl.ds(0, 1024)], sems.at[0, slot, k]
                ),
                pltpu.make_async_copy(
                    tail.at[part], to.at[k, :, pl.ds(1024, 512)], sems.at[1, slot, k]
                ),
            ]
    for copy in copies:
        copy.start()
    de[...] = ln_back(dln, xhat, inv_ln, gain[...])
    for copy in copies:
        copy.wait()


SMEM = pl.BlockSpec(memory_space=pltpu.SMEM)
VMEM = pl.BlockSpec(memory_space=pltpu.VMEM)
ANY = pl.BlockSpec(memory_space=pl.ANY)


def shaped(*pairs):
    return [jax.ShapeDtypeStruct(shape, dtype) for shape, dtype in pairs]


def pin(array):
    return pltpu.with_memory_space_constraint(array, pltpu.HBM)


def call(kernel, name, in_specs, out_specs, outs, scratch, flops, after=(), carry=()):
    n_in, n_extra, n_out = len(in_specs), len(after) + len(carry), len(outs)

    def body(*refs):
        first = n_in + n_extra
        kernel(*refs[:n_in], *refs[first : first + n_out], *refs[first + n_out + len(carry) :])

    made = pl.pallas_call(
        body,
        name=name,
        in_specs=in_specs + [ANY] * n_extra,
        out_specs=out_specs + [ANY] * len(carry),
        out_shape=outs + [jax.ShapeDtypeStruct(a.shape, a.dtype) for a in carry],
        scratch_shapes=scratch,
        input_output_aliases={n_in + len(after) + i: n_out + i for i in range(len(carry))},
        compiler_params=pltpu.CompilerParams(vmem_limit_bytes=vmem_cap),
        cost_estimate=pl.CostEstimate(flops=flops, bytes_accessed=10**6, transcendentals=0),
    )

    def run(*args):
        res = made(*args, *after, *carry)
        return (*res[:n_out], list(res[n_out:]))

    return run


DMA = pltpu.SemaphoreType.DMA
ROWS2 = (512, 512)


def attn_fwd(ids, marked, xs, gain, bias, w, after=(), carry=()):
    outs = shaped((ROWS2, f32), ((8, 512), f32)) + [pltpu.HBM(ROWS2, bf16)] * 6
    scratch = [
        pltpu.VMEM((2, 512, 1024), bf16),
        *[pltpu.VMEM(ROWS2, bf16)] * 3,
        pltpu.VMEM(ROWS2, f32),
        *[pltpu.VMEM(ROWS2, bf16)] * 6,
        DMA((32,)),
        DMA((6,)),
    ]
    x1, lse, *saved, carried = call(
        functools.partial(attn_fwd_kernel, bool(xs), len(w)),
        "attn_fwd",
        [SMEM] + [VMEM] * (4 + len(xs)) + [ANY] * len(w),
        [VMEM] * 2 + [ANY] * 6,
        outs,
        scratch,
        10**10,
        after,
        carry,
    )(ids, *marked, gain, bias, *xs, *map(pin, w))
    return x1, (lse, *saved), carried


def mlp_fwd(ids, x1, gain, bias, w, first=0, after=(), carry=()):
    return call(
        functools.partial(mlp_fwd_kernel, len(w), first),
        "mlp_fwd",
        [SMEM] + [VMEM] * 3 + [ANY] * len(w),
        [VMEM] * 2,
        shaped((ROWS2, f32), ((256, 512), f32)),
        [pltpu.VMEM((2, 512, 2048), bf16), pltpu.VMEM(ROWS2, bf16), DMA((32,))],
        8 * 10**9,
        after,
        carry,
    )(ids, x1, gain, bias, *map(pin, w))


def grad_shapes(split, width):
    return shaped(*([((4, 4, 32, width), bf16)] * 2 if split else [((32, 32, width), bf16)]))


def mlp_bwd(ids, x1, dys, gain, bias, w, first=0, after=(), carry=()):
    grads = grad_shapes(len(w) == 2, 2048)
    scratch = [
        pltpu.VMEM((2, 512, 2048), bf16),
        pltpu.VMEM((2, 512, 2048), bf16),
        *[pltpu.VMEM(ROWS2, bf16)] * 4,
        pltpu.VMEM(ROWS2, f32),
        DMA((32,)),
        DMA((32,)),
        *[pltpu.VMEM(ROWS2, f32)] * (len(dys) - 1),
    ]
    return call(
        functools.partial(mlp_bwd_kernel, len(dys) == 2, len(w), first, len(grads)),
        "mlp_bwd",
        [SMEM] + [VMEM] * 3 + [ANY] * len(w) + [VMEM] * len(dys),
        [VMEM] * 2 + [ANY] * len(grads),
        shaped((ROWS2, f32), ((8, 512), f32)) + grads,
        scratch,
        15 * 10**9,
        after,
        carry,
    )(ids, x1, gain, bias, *map(pin, w), *dys)


def attn_bwd(ids, marked, xs, dx1, gain, bias, saved, w, other_small=(), after=(), carry=()):
    width = 1024 + 128 * len(other_small)
    grads = grad_shapes(len(w) == 2, width)
    scratch = [
        pltpu.VMEM((2, 512, 1024), bf16),
        pltpu.VMEM((2, 512, width), bf16),
        pltpu.VMEM(ROWS2, bf16),
        pltpu.VMEM(ROWS2, f32),
        *[pltpu.VMEM(ROWS2, bf16)] * 13,
        DMA((32,)),
        DMA((6,)),
        DMA((32,)),
    ]
    return call(
        functools.partial(attn_bwd_kernel, bool(xs), bool(other_small), len(w), len(grads)),
        "attn_bwd",
        [SMEM] + [VMEM] * 6 + [ANY] * (6 + len(w)) + [VMEM] * (len(xs) + len(other_small)),
        [VMEM] * 3 + [ANY] * len(grads),
        shaped((ROWS2, f32), ((256, 512), bf16), ((8, 512), f32)) + grads,
        scratch,
        15 * 10**9,
        after,
        carry,
    )(ids, *marked, dx1, gain, bias, saved[0], *map(pin, saved[1:]), *map(pin, w), *xs, *other_small)


def code_prep(book_t, after=(), carry=()):
    codes = book_t.shape[1]
    return call(
        code_prep_kernel,
        "code_prep",
        [VMEM],
        [VMEM] * 2,
        shaped(((codes, 256), bf16), ((128, codes), bf16)),
        [],
        6 * 10**9,
        after,
        carry,
    )(book_t)


def vq_fwd(e, gain, bias, in_t, out_w, stack, stack_t, after=(), carry=()):
    return call(
        vq_fwd_kernel,
        "vq_fwd",
        [VMEM] * 5 + [ANY] * 2,
        [VMEM] * 2,
        shaped((ROWS2, f32), ((72, 512), f32)),
        [
            pltpu.VMEM((128, 512), f32),
            pltpu.VMEM(stack.shape, bf16),
            pltpu.VMEM(stack_t.shape, bf16),
            DMA((2, 4)),
        ],
        15 * 10**9,
        after,
        carry,
    )(e, gain, bias, in_t, out_w, pin(stack), pin(stack_t))


def vq_bwd(ids, e, du, gain, bias, in_t, out_w, codes, kept, smalls, after=(), carry=()):
    scratch = [
        pltpu.VMEM((96, 512), f32),
        pltpu.VMEM(codes[2].shape, bf16),
        pltpu.VMEM((96, 512), f32),
        pltpu.VMEM((8, 32, 512), bf16),
        *[pltpu.VMEM(a.shape, a.dtype) for a in codes],
        DMA((3, 4)),
        DMA((2, 2, 4)),
    ]
    return call(
        vq_bwd_kernel,
        "vq_bwd",
        [SMEM] + [VMEM] * 6 + [ANY] * 3 + [VMEM] * 3,
        [VMEM] + [ANY] * 2,
        shaped((ROWS2, f32), *[((4, 32, 1536), bf16)] * 2),
        scratch,
        25 * 10**9,
        after,
        carry,
    )(ids, e, du, gain, bias, in_t, out_w, *map(pin, codes), kept, *smalls)


def stack_kernel(cuts, *refs):
    shards, outs, sems = refs[:4], refs[4:-1], refs[-1]
    copies, first = [], 0
    for at, (out, width) in enumerate(zip(outs, cuts)):
        for k in range(4):
            copies.append(
                pltpu.make_async_copy(
                    shards[k].at[:, pl.ds(first, width)], out.at[k], sems.at[at, k]
                )
            )
        first += width
    for copy in copies:
        copy.start()
    for copy in copies:
        copy.wait()


def stack_lines(shards, cuts, after=()):
    return call(
        functools.partial(stack_kernel, cuts),
        "stack_lines",
        [ANY] * 4,
        [ANY] * len(cuts),
        shaped(*[((4, 32, width), bf16) for width in cuts]),
        [DMA((len(cuts), 4))],
        1,
        after,
    )(*shards)[:-1]


def quads_kernel(*refs):
    quads, out, sems = refs[:4], refs[4], refs[5]
    copies = [pltpu.make_async_copy(quads[i], out.at[i], sems.at[i]) for i in range(4)]
    start_all(copies)
    wait_all(copies)


def stack_quads(quads, after=(), carry=()):
    shape = (4, *quads[0].shape)
    return call(
        quads_kernel, "stack_quads", [ANY] * 4, [ANY], shaped((shape, bf16)), [DMA((4,))], 1, after, carry
    )(*quads)


def pack_kernel(ids, *refs):
    hbm, outs, (qkv, out_t, up, down_t, tokens, segs, sems) = refs[:7], refs[7:12], refs[12:]
    enc, dec, own, other, cot_send = outs
    copies = [
        pltpu.make_async_copy(held, to, sems.at[at])
        for at, (held, to) in enumerate(zip(hbm[:6], (qkv, out_t, up, down_t, tokens, segs)))
    ]
    copies.append(pltpu.make_async_copy(hbm[6].at[1 - ids[1]], cot_send, sems.at[6]))
    start_all(copies)
    wait_all(copies[:4])
    for layer, to in enumerate((enc, dec)):
        for index in range(3):
            to[:, index * 256 : (index + 1) * 256] = qkv[layer, index]
        to[:, 768:1024] = out_t[layer]
        to[:, 1024:2048] = up[layer]
        to[:, 2048:3072] = down_t[layer]
    wait_all(copies[4:6])
    for to, micro in ((own, ids[1]), (other, 1 - ids[1])):
        to[:, :512] = tokens[micro]
        ids_row = segs[pl.ds(micro, 1), :].astype(f32)
        to[:, 512:] = jnp.broadcast_to(ids_row, (128, 256)).T.astype(bf16)
    copies[6].wait()


def pack(ids, *arrays):
    return call(
        pack_kernel,
        "pack",
        [SMEM] + [ANY] * 7,
        [VMEM] * 4 + [ANY],
        shaped(*[((32, 3072), bf16)] * 2, *[((256, 640), bf16)] * 2) + [pltpu.HBM((256, 512), f32)],
        [*[pltpu.VMEM(a.shape, a.dtype) for a in arrays[:6]], DMA((7,))],
        1,
    )(ids, *map(pin, arrays))[:-1]


def joined(block):
    return block[0:16, 1024:].astype(f32) + block[16:32, 1024:].astype(f32)


def put_small(value, own, blocks):
    hi, lo = split2(value)
    own[0:16, 1024:] = hi.astype(f32) + lo.astype(f32)
    for block in blocks:
        block[0:16, 1024:] = hi
        block[16:32, 1024:] = lo


def near_kernel(ids, ins, outs):
    keep, other = ins
    for i in range(4):
        outs[i][...] = (keep[i].astype(f32) + other[i].astype(f32)).astype(outs[i].dtype)
    if keep.shape[3] == 1152:
        value = joined(keep.at[0, 0]) + joined(other.at[0, 0])
        put_small(value, outs[0].at[0], [out.at[0] for out in outs[1:]])


def near_task(keep, other):
    shape = keep.shape[1:]
    return near_kernel, [keep, other], shaped((shape, f32), *[(shape, bf16)] * 3)


def fork_kernel(ids, ins, outs):
    keep, other = ins
    for at, (own, send, kept, sent) in enumerate(((outs[0], outs[1], (0, 2), (1, 3)), (outs[2], outs[3], (0, 1), (2, 3)))):
        cols = slice(1024 * at, 1024 * (at + 1))
        for j in range(2):
            for out, i in ((own, kept[j]), (send, sent[j])):
                total = keep[i, :, :, cols].astype(f32) + other[i, :, :, cols].astype(f32)
                out[j] = total.astype(out.dtype)


def fork_task(keep, other):
    shape = (2, *keep.shape[1:3], 1024)
    return fork_kernel, [keep, other], shaped(*[(shape, f32), (shape, bf16)] * 2)


def half_kernel(ids, ins, outs):
    own, other = ins
    for j in range(2):
        outs[j][...] = (own[j] + other[j].astype(f32)).astype(outs[j].dtype)


def half_task(own, other):
    shape = own.shape[1:]
    return half_kernel, [own, other], shaped((shape, f32), (shape, bf16))


def join_kernel(ids, ins, outs):
    for at in range(2):
        own, other = ins[2 * at : 2 * at + 2]
        for k in range(4):
            total = own[k] + other[k].astype(f32)
            outs[k][:, 1024 * at : 1024 * (at + 1)] = total.astype(outs[k].dtype)


def join_task(own_up, other_up, own_down, other_down):
    outs = shaped(((32, 2048), f32), *[((32, 2048), bf16)] * 3)
    return join_kernel, [own_up, other_up, own_down, other_down], outs


def plane_kernel(ids, ins, outs):
    for k in range(4):
        total = ins[0][k]
        for other in ins[1:]:
            total = total + other[k].astype(f32)
        outs[k][...] = total.astype(outs[k].dtype)
    if ins[0].shape[2] == 1152:
        x, y, xy = [joined(other.at[0]) for other in ins[1:]]
        put_small((ins[0][0, 0:16, 1024:] + x) + (y + xy), outs[0], outs[1:])


def plane_task(own, others):
    shape = own.shape[1:]
    return plane_kernel, [own, *others], shaped((shape, f32), *[(shape, bf16)] * 3)


def line_total(ins, width):
    total = ins[0][:, :width]
    for other in ins[1:]:
        total = total + other[:, :width].astype(f32)
    return total


def rows_kernel(ids, ins, outs):
    own, other = ins
    half = other.shape[0]
    outs[0][ids[1]] = own[0:half, :].astype(f32)
    outs[0][1 - ids[1]] = other[...].astype(f32)


def rows_task(own, other):
    return rows_kernel, [own, other], shaped(((2, *other.shape), f32))


def code_small(ref):
    return ref[:, 1024:1280].astype(f32) + ref[:, 1280:1536].astype(f32)


def code_sum(refs, out):
    total, small = refs[0][:, :1024].astype(f32), code_small(refs[0])
    for ref in refs[1:]:
        total = total + ref[:, :1024].astype(f32)
        small = small + code_small(ref)
    hi, lo = split2(small)
    out[:, :1024] = total.astype(bf16)
    out[:, 1024:1280] = hi
    out[:, 1280:1536] = lo


def code_near_kernel(ids, ins, outs):
    for k in range(4):
        code_sum([ref.at[k] for ref in ins], outs[k])


def code_near_task(keep, other):
    return code_near_kernel, [keep, other], shaped(*[(keep.shape[1:], bf16)] * 4)


def code_add_kernel(ids, ins, outs):
    code_sum(ins, outs[0])


def code_add_task(*parts):
    return code_add_kernel, list(parts), shaped((parts[0].shape, bf16))


def code_line_kernel(ids, ins, outs):
    for k in range(4):
        outs[0][k] = ins[k][...]


def code_line_task(*parts):
    return code_line_kernel, list(parts), shaped(((4, *parts[0].shape), bf16))


def finish_kernel(ids, ins, outs):
    mlp, attn, d_mlp, d_attn, code, code_other = ins[:4], ins[4:8], *ins[8:]
    qkv, out_t, up, down_t, book, vq_in, vq_out, gains, biases, dec_biases, small_ref = outs
    for layer, rows in enumerate((line_total(mlp, 2048), d_mlp[...].astype(f32))):
        up[layer] = rows[:, :1024]
        down_t[layer] = rows[:, 1024:]
    for layer, rows in enumerate((line_total(attn, 1024), d_attn[...].astype(f32))):
        for index in range(3):
            qkv[layer, index] = rows[:, index * 256 : (index + 1) * 256]
        out_t[layer] = rows[:, 768:]
    core, z = ids[0] % 2, ids[0] // 4
    for at, parts in ((core, code), (1 - core, code_other)):
        for k in range(4):
            part = at * 4 + (z ^ k)
            book[:, pl.ds(pl.multiple_of(part * 1024, 1024), 1024)] = parts[k, :, :1024].astype(f32)
            small_ref[:, pl.ds(pl.multiple_of(part * 256, 256), 256)] = code_small(parts.at[k])
    small = small_ref[...]
    vq_in[...] = small[:, :512]
    vq_out[...] = small[:, 512:1024]
    rest = small[:, 1024:1536]
    k1, k2, k3 = [joined(other) for other in attn[1:]]
    packed = (attn[0][0:16, 1024:] + k1) + (k2 + k3)
    for row, out in enumerate((gains.at[0:1], biases.at[0:1], gains.at[1:2], biases.at[1:2])):
        for j in range(4):
            out[:, 128 * j : 128 * (j + 1)] = packed[row * 4 + j : row * 4 + j + 1, :]
    gains[2:3, :] = rest[0:1, :]
    biases[2:3, :] = rest[1:2, :]
    gains[3:4, :] = rest[2:3, :]
    dec_biases[0:1, :] = rest[3:4, :]
    gains[4:5, :] = rest[4:5, :]
    dec_biases[1:2, :] = rest[5:6, :]


def finish_task(own_m, line_m, own_a, line_a, d_mlp, d_attn, code, code_other):
    outs = shaped(
        ((2, 3, 32, 256), f32),
        ((2, 32, 256), f32),
        ((2, 32, 1024), f32),
        ((2, 32, 1024), f32),
        ((32, 8192), f32),
        ((32, 512), f32),
        ((32, 512), f32),
        ((5, 512), f32),
        ((3, 512), f32),
        ((2, 512), f32),
        ((32, 2048), f32),
    )
    return finish_kernel, [own_m, *line_m, own_a, *line_a, d_mlp, d_attn, code, code_other], outs


def run_tasks(ids, name, tasks, after=(), carry=()):
    sizes = [(len(ins), len(outs)) for _, ins, outs in tasks]
    n_in = sum(i for i, _ in sizes)

    def kernel(ids_ref, *refs):
        at_in, at_out = 0, n_in
        for (fn, _, _), (i, o) in zip(tasks, sizes):
            fn(ids_ref, refs[at_in : at_in + i], refs[at_out : at_out + o])
            at_in, at_out = at_in + i, at_out + o

    outs = [one for _, _, many in tasks for one in many]
    res = call(
        kernel, name, [SMEM] + [VMEM] * n_in, [VMEM] * len(outs), outs, [], 10**9, after, carry
    )(ids, *[one for _, many, _ in tasks for one in many])
    split, at = [], 0
    for _, o in sizes:
        split.append(res[at : at + o])
        at += o
    return (*split, res[-1])


def whole_groups(
    n_dp,
    tokens,
    segment_ids,
    norm_gains,
    norm_biases,
    w_qkv,
    w_attn_out,
    w_up,
    w_down,
    w_vq_in,
    w_vq_out,
    codebook,
    cotangent,
):
    dp_at, tp_at = lax.axis_index("dp"), lax.axis_index("tp")
    ids = jnp.stack([dp_at, tp_at]).astype(jnp.int32)

    def swap(values):
        return exchange(values, 0, 1, n_dp)

    gains = [norm_gains[i : i + 1] for i in range(5)]
    biases = [norm_biases[i : i + 1] for i in range(5)]
    book_t, in_t = codebook.T, w_vq_in.T
    enc_shard, dec_shard, own, send, cot_send = pack(
        ids,
        w_qkv,
        w_attn_out.transpose(0, 2, 1),
        w_up,
        w_down.transpose(0, 2, 1),
        tokens,
        segment_ids,
        cotangent,
    )
    marked = [own, swap(send)]

    attn_line, mlp_line = stack_lines(spread_line(enc_shard, n_dp), [1024, 2048])
    dec_w = [lax.all_gather(dec_shard, ("dp", "tp"))]
    stack, stack_t, _ = code_prep(book_t, [attn_line])
    codes = (stack, stack_t, book_t)
    attn_quads, (mlp_line,) = stack_quads(
        plane_quads(attn_line, n_dp), [stack_t, marked[1]], [mlp_line]
    )
    mlp_quads = plane_quads(mlp_line, n_dp)
    enc_attn = [attn_quads, exchange(attn_quads, 1, 0, n_dp)]
    e_x1, e_saved, _ = attn_fwd(ids, marked, [], gains[0], biases[0], enc_attn)
    mlp_quads, _ = stack_quads(mlp_quads, [e_x1])
    enc_mlp = [mlp_quads, exchange(mlp_quads, 1, 0, n_dp)]
    e, _, _ = mlp_fwd(ids, e_x1, gains[1], biases[1], enc_mlp)
    u, kept, _ = vq_fwd(e, gains[2], biases[2], in_t, w_vq_out, stack, stack_t)
    d_x1, d_saved, (cot_send,) = attn_fwd(
        ids, marked, [u], gains[3], biases[3], dec_w, carry=[cot_send]
    )
    cot_other = swap(cot_send)
    y, y_theirs, _ = mlp_fwd(ids, d_x1, gains[4], biases[4], dec_w, 1024)
    y_other = swap(y_theirs)

    dx1, d_small1, g_mlp, _ = mlp_bwd(
        ids, d_x1, [cotangent, cot_other], gains[4], biases[4], dec_w, 1024
    )
    d_mlp = lax.psum_scatter(g_mlp, ("dp", "tp"))
    du, _, d_small0, g_attn, _ = attn_bwd(
        ids, marked, [u], dx1, gains[3], biases[3], d_saved, dec_w
    )
    d_attn = lax.psum_scatter(g_attn, ("dp", "tp"))
    de, code, code_send, _ = vq_bwd(
        ids, e, du, gains[2], biases[2], in_t, w_vq_out, codes, kept, [d_small0, d_small1]
    )
    code_other = exchange(code_send, 1, 0, n_dp)
    code_parts, (decoded,), _ = run_tasks(
        ids, "sums2", [code_near_task(code, code_other), rows_task(y, y_other)]
    )
    code, *code_others = code_parts[0], *line_send(code_parts[1:], n_dp)
    ex1, e_small1, keep_m, send_m, _ = mlp_bwd(
        ids, e_x1, [de], gains[1], biases[1], enc_mlp, after=[code_parts[1]]
    )
    (code,), (keep_m, send_m) = run_tasks(
        ids, "sums3", [code_add_task(code, *code_others)], carry=[keep_m, send_m]
    )
    near_m, code_other = exchange(send_m, 1, 0, n_dp), exchange(code, 0, 1, n_dp)
    (own_up, send_up, own_down, send_down), (code,), _ = run_tasks(
        ids, "sums3b", [fork_task(keep_m, near_m), code_add_task(code, code_other)]
    )
    other_up, other_down = exchange(send_up, 0, 1, n_dp), exchange(send_down, 2, 0, n_dp)
    code_other = exchange(code, 2, 0, n_dp)
    dx, dx_low, _, keep_a, send_a, (own_up, own_down) = attn_bwd(
        ids,
        marked,
        [],
        ex1,
        gains[0],
        biases[0],
        e_saved,
        enc_attn,
        [e_small1],
        [send_up, send_down, code],
        [own_up, own_down],
    )
    (own_up, send_up), (own_down, send_down), (code,), (keep_a, send_a, dx_low) = run_tasks(
        ids,
        "sums4",
        [
            half_task(own_up, other_up),
            half_task(own_down, other_down),
            code_add_task(code, code_other),
        ],
        carry=[keep_a, send_a, dx_low],
    )
    near_a, code_others = exchange(send_a, 1, 0, n_dp), line_send([code] * 3, n_dp)
    other_up, other_down = exchange(send_up, 2, 0, n_dp), exchange(send_down, 0, 1, n_dp)
    (own_a, *lows_a), (code,), (own_up, own_down, dx_low) = run_tasks(
        ids,
        "sums4b",
        [near_task(keep_a, near_a), code_line_task(code, *code_others)],
        carry=[own_up, own_down, dx_low],
    )
    plane_a, code_other = plane_send(lows_a, n_dp), exchange(code, 1, 0, n_dp)
    dx_other = swap(dx_low)
    (own_m, *lows_m), (own_a,) = run_tasks(
        ids, "sums5", [join_task(own_up, other_up, own_down, other_down)], lows_a, [own_a]
    )
    line_m = line_send(lows_m, n_dp)
    (own_a, *lows_a), (grad_tokens,), (own_m,) = run_tasks(
        ids, "sums6", [plane_task(own_a, plane_a), rows_task(dx, dx_other)], lows_m, [own_m]
    )
    line_a = line_send(lows_a, n_dp)
    (qkv, out_t, up, down_t, book, vq_in, vq_out, *norms, _), _ = run_tasks(
        ids,
        "finish",
        [finish_task(own_m, line_m, own_a, line_a, d_mlp, d_attn, code, code_other)],
    )
    return (
        decoded,
        grad_tokens,
        *norms,
        qkv,
        out_t.transpose(0, 2, 1),
        up,
        down_t.transpose(0, 2, 1),
        vq_in.T,
        vq_out,
        book.T,
    )


def layer_norm(values, norm_gain, norm_bias):
    centred = values - jnp.mean(values, axis=-1, keepdims=True)
    spread = jnp.mean(centred * centred, axis=-1, keepdims=True)
    return centred * lax.rsqrt(spread + ln_eps) * norm_gain + norm_bias


def gelu_tanh(values):
    return (
        0.5 * values * (1.0 + jnp.tanh(gelu_coef * (values + 0.044715 * values * values * values)))
    )


def matmul(former, latter):
    return jnp.dot(former, latter, precision=highest, preferred_element_type=jnp.float32)


def normalize(values):
    return values * lax.rsqrt(jnp.sum(values * values, axis=-1, keepdims=True) + norm_eps)


def quantize(in_rows, norm_gain, norm_bias, in_w, out_w, code_w):
    latent = normalize(matmul(layer_norm(in_rows, norm_gain, norm_bias), in_w))
    code_rows = normalize(code_w)
    logits = matmul(latent, code_rows.T) * temper
    row_max = jnp.max(logits, axis=-1, keepdims=True)
    numerator = jnp.exp(logits - row_max)
    assign = numerator / jnp.sum(numerator, axis=-1, keepdims=True)
    soft_code = matmul(assign, code_rows)
    offset = latent - soft_code
    vq_loss = commit_weight * 1.25 * jnp.sum(offset * offset)
    return (matmul(soft_code, out_w), vq_loss)


def product(former, latter):
    return jnp.dot(former, latter, preferred_element_type=jnp.float32)


def product_tn(former, latter):
    return lax.dot_general(
        former, latter, (((0,), (0,)), ((), ())), preferred_element_type=jnp.float32
    )


def product_nt(former, latter):
    return lax.dot_general(
        former, latter, (((1,), (1,)), ((), ())), preferred_element_type=jnp.float32
    )


def split_heads(values):
    return values.reshape(values.shape[0], values.shape[1] // HEAD_DIM, HEAD_DIM).transpose(1, 0, 2)


def join_heads(values):
    return values.transpose(1, 0, 2).reshape(values.shape[1], values.shape[0] * HEAD_DIM)


def masked_scores(query_blk, key_h, seg_blk, seg_keys):
    scores = jnp.einsum(
        "hqd,hkd->hqk", query_blk, key_h, preferred_element_type=jnp.float32
    ) * HEAD_DIM ** (-0.5)
    return jnp.where((seg_blk[:, None] == seg_keys[None, :])[None], scores, masked_score)


def attend(query_h, key_h, value_h, seg_keys):
    block_rows = min(512, query_h.shape[1])
    block_count = query_h.shape[1] // block_rows

    def one_block(begin_row):
        query_blk = lax.dynamic_slice_in_dim(query_h, begin_row, block_rows, 1)
        seg_blk = lax.dynamic_slice_in_dim(seg_keys, begin_row, block_rows, 0)
        scores = masked_scores(query_blk, key_h, seg_blk, seg_keys)
        row_max = jnp.max(scores, axis=-1, keepdims=True)
        numerator = jnp.exp(scores - row_max)
        row_total = jnp.sum(numerator, axis=-1, keepdims=True)
        prob_low = (numerator / row_total).astype(jnp.bfloat16)
        attended = jnp.einsum("hqk,hkd->hqd", prob_low, value_h, preferred_element_type=jnp.float32)
        return (attended.astype(jnp.bfloat16), (row_max + jnp.log(row_total))[..., 0])

    starts = jnp.arange(block_count, dtype=jnp.int32) * block_rows
    attended, log_sums = lax.map(one_block, starts)
    heads_out = attended.transpose(1, 0, 2, 3).reshape(query_h.shape)
    log_sums = log_sums.transpose(1, 0, 2).reshape(query_h.shape[0], query_h.shape[1])
    return (heads_out, log_sums)


def attend_back(query_h, key_h, value_h, seg_keys, log_sums, grad_out):
    block_rows = min(512, query_h.shape[1])
    block_count = query_h.shape[1] // block_rows

    def one_block(carry, begin_row):
        grad_key, grad_value = carry
        query_blk = lax.dynamic_slice_in_dim(query_h, begin_row, block_rows, 1)
        grad_blk = lax.dynamic_slice_in_dim(grad_out, begin_row, block_rows, 1)
        lse_blk = lax.dynamic_slice_in_dim(log_sums, begin_row, block_rows, 1)
        seg_blk = lax.dynamic_slice_in_dim(seg_keys, begin_row, block_rows, 0)
        scores = masked_scores(query_blk, key_h, seg_blk, seg_keys)
        probs = jnp.exp(scores - lse_blk[..., None])
        prob_low = probs.astype(jnp.bfloat16)
        grad_value = grad_value + jnp.einsum(
            "hqk,hqd->hkd", prob_low, grad_blk, preferred_element_type=jnp.float32
        )
        grad_prob = jnp.einsum(
            "hqd,hkd->hqk", grad_blk, value_h, preferred_element_type=jnp.float32
        )
        row_dot = jnp.sum(probs * grad_prob, axis=-1, keepdims=True)
        grad_score = (probs * (grad_prob - row_dot) * HEAD_DIM ** (-0.5)).astype(jnp.bfloat16)
        grad_query = jnp.einsum(
            "hqk,hkd->hqd", grad_score, key_h, preferred_element_type=jnp.float32
        )
        grad_key = grad_key + jnp.einsum(
            "hqk,hqd->hkd", grad_score, query_blk, preferred_element_type=jnp.float32
        )
        return ((grad_key, grad_value), grad_query)

    starts = jnp.arange(block_count, dtype=jnp.int32) * block_rows
    zeros_kv = jnp.zeros(key_h.shape, jnp.float32)
    (grad_key, grad_value), grad_query = lax.scan(one_block, (zeros_kv, zeros_kv), starts)
    grad_query = grad_query.transpose(1, 0, 2, 3).reshape(query_h.shape)
    return (
        grad_query.astype(jnp.bfloat16),
        grad_key.astype(jnp.bfloat16),
        grad_value.astype(jnp.bfloat16),
    )


def spread_rows(values):
    return lax.all_gather(values, "tp", axis=0, tiled=True)


def combine_rows(partial_value):
    return lax.psum_scatter(partial_value, "tp", scatter_dimension=0, tiled=True)


def spread_grads(values):
    return lax.all_gather(values, "tp", axis=0, tiled=True)


def combine_grads(partial_value):
    return lax.psum_scatter(
        partial_value.astype(jnp.bfloat16), "tp", scatter_dimension=0, tiled=True
    ).astype(jnp.float32)


def fetch_weights(w_qkv, w_attn_out, w_up, w_down, layer):
    return (
        lax.all_gather(w_qkv[layer], "dp", axis=1, tiled=True),
        lax.all_gather(w_attn_out[layer], "dp", axis=1, tiled=True),
        lax.all_gather(w_up[layer], "dp", axis=0, tiled=True),
        lax.all_gather(w_down[layer], "dp", axis=1, tiled=True),
    )


def reduce_weight_grads(grads):
    return (
        lax.psum_scatter(
            grads[0].astype(jnp.bfloat16), "dp", scatter_dimension=1, tiled=True
        ).astype(jnp.float32),
        lax.psum_scatter(
            grads[1].astype(jnp.bfloat16), "dp", scatter_dimension=1, tiled=True
        ).astype(jnp.float32),
        lax.psum_scatter(
            grads[2].astype(jnp.bfloat16), "dp", scatter_dimension=0, tiled=True
        ).astype(jnp.float32),
        lax.psum_scatter(
            grads[3].astype(jnp.bfloat16), "dp", scatter_dimension=1, tiled=True
        ).astype(jnp.float32),
    )


def block_forward(resid_in, seg_local, gains, biases, weights):
    qkv_w, attn_w, up_w, down_w = weights
    normed = layer_norm(resid_in, gains[0], biases[0]).astype(jnp.bfloat16)
    normed_all, seg_all = (
        lax.all_gather(normed, "tp", axis=0, tiled=True),
        lax.all_gather(seg_local, "tp", axis=0, tiled=True),
    )
    query_h = split_heads(product(normed_all, qkv_w[0]).astype(jnp.bfloat16))
    key_h = split_heads(product(normed_all, qkv_w[1]).astype(jnp.bfloat16))
    value_h = split_heads(product(normed_all, qkv_w[2]).astype(jnp.bfloat16))
    heads_out, log_sums = attend(query_h, key_h, value_h, seg_all)
    attn_rows = join_heads(heads_out)
    middle = resid_in + combine_rows(product(attn_rows, attn_w))
    normed_mid = spread_rows(layer_norm(middle, gains[1], biases[1]).astype(jnp.bfloat16))
    hidden_pre = product(normed_mid, up_w)
    hidden = gelu_tanh(hidden_pre).astype(jnp.bfloat16)
    result = middle + combine_rows(product(hidden, down_w))
    kept = (
        resid_in,
        middle,
        normed_all,
        seg_all,
        query_h,
        key_h,
        value_h,
        log_sums,
        attn_rows,
        normed_mid,
        hidden_pre,
        hidden,
    )
    return (result, kept)


def block_backward(kept, gains, biases, weights, grad_result):
    (
        resid_in,
        middle,
        normed_all,
        seg_all,
        query_h,
        key_h,
        value_h,
        log_sums,
        attn_rows,
        normed_mid,
        hidden_pre,
        hidden,
    ) = kept
    qkv_w, attn_w, up_w, down_w = weights
    grad_branch = spread_grads(grad_result.astype(jnp.bfloat16))
    grad_down = product_tn(hidden, grad_branch)
    grad_hidden = product_nt(grad_branch, down_w)
    _, gelu_back = jax.vjp(gelu_tanh, hidden_pre)
    grad_pre = gelu_back(grad_hidden)[0].astype(jnp.bfloat16)
    grad_up = product_tn(normed_mid, grad_pre)
    grad_norm_mid = combine_grads(product_nt(grad_pre, up_w))
    _, norm_back_mid = jax.vjp(layer_norm, middle, gains[1], biases[1])
    grad_mid_ln, grad_gain_mid, grad_bias_mid = norm_back_mid(grad_norm_mid)
    grad_middle = grad_result + grad_mid_ln
    grad_attn_all = spread_grads(grad_middle.astype(jnp.bfloat16))
    grad_attn = product_tn(attn_rows, grad_attn_all)
    grad_heads = split_heads(product_nt(grad_attn_all, attn_w).astype(jnp.bfloat16))
    grad_query, grad_key, grad_value = attend_back(
        query_h, key_h, value_h, seg_all, log_sums, grad_heads
    )
    grad_parts = [join_heads(grad_query), join_heads(grad_key), join_heads(grad_value)]
    grad_qkv = jnp.stack([product_tn(normed_all, grad_part) for grad_part in grad_parts])
    grad_normed_part = (
        product_nt(grad_parts[0], qkv_w[0])
        + product_nt(grad_parts[1], qkv_w[1])
        + product_nt(grad_parts[2], qkv_w[2])
    )
    grad_normed = combine_grads(grad_normed_part)
    _, norm_back_in = jax.vjp(layer_norm, resid_in, gains[0], biases[0])
    grad_in_ln, grad_gain_in, grad_bias_in = norm_back_in(grad_normed)
    gain_grads = jnp.stack([grad_gain_in, grad_gain_mid])
    bias_grads = jnp.stack([grad_bias_in, grad_bias_mid])
    return (
        grad_middle + grad_in_ln,
        gain_grads,
        bias_grads,
        (grad_qkv, grad_attn, grad_up, grad_down),
    )


def local(
    tokens,
    segment_ids,
    norm_gains,
    norm_biases,
    w_qkv,
    w_attn_out,
    w_up,
    w_down,
    w_vq_in,
    w_vq_out,
    codebook,
    cotangent,
):
    gain_sum = jnp.zeros(norm_gains.shape, jnp.float32)
    bias_sum = jnp.zeros(norm_biases.shape, jnp.float32)
    vq_in_sum = jnp.zeros(w_vq_in.shape, jnp.float32)
    vq_out_sum = jnp.zeros(w_vq_out.shape, jnp.float32)
    code_sum = jnp.zeros(codebook.shape, jnp.float32)
    layer_sums = [None, None]
    outputs = []
    input_grads = []
    for micro in range(MICRO):
        resid_in = tokens[micro].astype(jnp.float32)
        seg_local = segment_ids[micro]
        enc_weights = fetch_weights(w_qkv, w_attn_out, w_up, w_down, 0)
        encoded, enc_kept = block_forward(
            resid_in, seg_local, norm_gains[0:2], norm_biases[0:2], enc_weights
        )
        (decoder_in, _), vq_back = jax.vjp(
            quantize, encoded, norm_gains[2], norm_biases[2], w_vq_in, w_vq_out, codebook
        )
        dec_weights = fetch_weights(w_qkv, w_attn_out, w_up, w_down, 1)
        decoded, dec_kept = block_forward(
            decoder_in, seg_local, norm_gains[3:5], norm_biases[3:5], dec_weights
        )
        outputs.append(decoded)
        grad_dec_in, gains_dec, biases_dec, grads_dec = block_backward(
            dec_kept, norm_gains[3:5], norm_biases[3:5], dec_weights, cotangent[micro]
        )
        grad_encoded, grad_gain_vq, grad_bias_vq, grad_in_w, grad_out_w, grad_codes = vq_back(
            (grad_dec_in, jnp.ones((), jnp.float32))
        )
        grad_input, gains_enc, biases_enc, grads_enc = block_backward(
            enc_kept, norm_gains[0:2], norm_biases[0:2], enc_weights, grad_encoded
        )
        input_grads.append(grad_input)
        gain_sum = gain_sum + jnp.concatenate([gains_enc, grad_gain_vq[None], gains_dec], axis=0)
        bias_sum = bias_sum + jnp.concatenate([biases_enc, grad_bias_vq[None], biases_dec], axis=0)
        vq_in_sum = vq_in_sum + grad_in_w
        vq_out_sum = vq_out_sum + grad_out_w
        code_sum = code_sum + grad_codes
        for layer, grads in ((0, grads_enc), (1, grads_dec)):
            reduced = reduce_weight_grads(grads)
            if layer_sums[layer] is None:
                layer_sums[layer] = reduced
            else:
                layer_sums[layer] = jax.tree.map(jnp.add, layer_sums[layer], reduced)
    gain_tot, bias_tot, vq_in_tot, vq_out_tot, code_tot = lax.psum(
        (gain_sum, bias_sum, vq_in_sum, vq_out_sum, code_sum), ("dp", "tp")
    )
    return (
        jnp.stack(outputs),
        jnp.stack(input_grads),
        gain_tot,
        bias_tot[0:3],
        bias_tot[3:5],
        jnp.stack([layer_sums[0][0], layer_sums[1][0]]),
        jnp.stack([layer_sums[0][1], layer_sums[1][1]]),
        jnp.stack([layer_sums[0][2], layer_sums[1][2]]),
        jnp.stack([layer_sums[0][3], layer_sums[1][3]]),
        vq_in_tot,
        vq_out_tot,
        code_tot,
    )


def solution(mesh):
    n_dp, n_tp = mesh.shape["dp"], mesh.shape["tp"]
    fits = n_tp == MICRO and n_dp == 16
    return jax.shard_map(
        functools.partial(whole_groups, n_dp) if fits else local,
        mesh=mesh,
        in_specs=(
            P(None, ("dp", "tp"), None),
            P(None, ("dp", "tp")),
            P(),
            P(),
            P(None, None, "dp", "tp"),
            P(None, "tp", "dp"),
            P(None, "dp", "tp"),
            P(None, "tp", "dp"),
            P(),
            P(),
            P(),
            P(None, ("dp", "tp"), None),
        ),
        out_specs=(
            P(None, ("dp", "tp"), None),
            P(None, ("dp", "tp"), None),
            P(),
            P(),
            P(),
            P(None, None, "dp", "tp"),
            P(None, "tp", "dp"),
            P(None, "dp", "tp"),
            P(None, "tp", "dp"),
            P(),
            P(),
            P(),
        ),
        check_vma=False,
    )
```

```python
import functools

import jax
import jax.numpy as jnp
from jax import lax
from jax.experimental import pallas as pl
from jax.experimental.pallas import tpu as pltpu
from jax.sharding import PartitionSpec as P

HEAD_DIM = 64
MICRO = 2
bf16 = jnp.bfloat16
f32 = jnp.float32
highest = lax.Precision.HIGHEST
ln_eps = 1e-05
norm_eps = 1e-06
temper = 10.0
commit_weight = 64.0
gelu_coef = 0.7978845608028654
masked_score = -1e30
log2e = 1.4426950408889634
vmem_cap = 36 * 1024 * 1024


PLANE = ((0, 0), (0, 1), (1, 0), (1, 1))


def exchange(values, dp_xor, tp_xor, n_dp):
    pairs = [
        (d * 2 + t, (d ^ dp_xor) * 2 + (t ^ tp_xor)) for d in range(n_dp) for t in range(2)
    ]
    return lax.ppermute(values, ("dp", "tp"), pairs)


def spread_line(shard, n_dp):
    return jnp.stack([shard] + [exchange(shard, 4 * k, 0, n_dp) for k in range(1, 4)])


def plane_quads(own, n_dp):
    return [own] + [exchange(own, 2 * y, x, n_dp) for y, x in PLANE[1:]]


def plane_send(lows, n_dp):
    return [exchange(low, 2 * y, x, n_dp) for (y, x), low in zip(PLANE[1:], lows)]


def line_send(lows, n_dp):
    return [exchange(low, 4 * k, 0, n_dp) for k, low in zip(range(1, 4), lows)]


def block_places():
    for core in range(2):
        for index, (y, x) in enumerate(PLANE):
            for k in range(4):
                yield core * 4 + index, k, k * 4 + y * 2 + core, x


def dot(a, b):
    return jnp.dot(a, b, preferred_element_type=f32)


def dot_nt(a, b, precision=None):
    return lax.dot_general(
        a, b, (((1,), (1,)), ((), ())), preferred_element_type=f32, precision=precision
    )


def dot_full(a, b):
    return jnp.dot(a, b, preferred_element_type=f32, precision=highest)


def ln_parts(x):
    centred = x - jnp.mean(x, axis=-1, keepdims=True)
    inv = lax.rsqrt(jnp.mean(centred * centred, axis=-1, keepdims=True) + ln_eps)
    return centred * inv, inv


def ln_back(grad, xhat, inv, gain):
    scaled = grad * gain
    return inv * (
        scaled
        - jnp.mean(scaled, axis=-1, keepdims=True)
        - xhat * jnp.mean(scaled * xhat, axis=-1, keepdims=True)
    )


def split2(x):
    hi = x.astype(bf16)
    return hi, (x - hi.astype(f32)).astype(bf16)


def split3(x):
    hi, _ = split2(x)
    rest = x - hi.astype(f32)
    mid = rest.astype(bf16)
    return hi, mid, (rest - mid.astype(f32)).astype(bf16)


def weight_copies(ids_ref, refs, w_ref, sems):
    copies, first = [], 0
    for at in range(0, len(refs), 2):
        width = refs[at].shape[3]
        for slot, (which, k, dp_xor, tp_xor) in enumerate(block_places()):
            row = pl.multiple_of((ids_ref[0] ^ dp_xor) * 32, 32)
            copies.append(
                pltpu.make_async_copy(
                    refs[at + which // 4].at[which % 4, k],
                    w_ref.at[ids_ref[1] ^ tp_xor, pl.ds(row, 32), pl.ds(first, width)],
                    sems.at[at * 16 + slot],
                )
            )
        first += width
    return copies


def grad_copies(ids_ref, g_ref, refs, sems):
    copies = []
    for slot, (which, k, dp_xor, tp_xor) in enumerate(block_places()):
        row = pl.multiple_of((ids_ref[0] ^ dp_xor) * 32, 32)
        copies.append(
            pltpu.make_async_copy(
                g_ref.at[ids_ref[1] ^ tp_xor, pl.ds(row, 32), :],
                refs[which // 4].at[which % 4, k],
                sems.at[slot],
            )
        )
    return copies


def start_all(copies):
    for copy in copies:
        copy.start()


def wait_all(copies):
    for copy in copies:
        copy.wait()


def head_rows(ref, pair, which):
    own = ref[pl.ds(pl.multiple_of(pair * 128 + which * HEAD_DIM, HEAD_DIM), HEAD_DIM), :]
    zero = jnp.zeros_like(own)
    return jnp.concatenate([own, zero] if which == 0 else [zero, own], axis=0)


def segment_mask(own, other):
    ids = jnp.concatenate([own[:, 512:640], other[:, 512:640]], axis=0).astype(f32)
    return jnp.where(ids[:, 0:1] == ids.T[0:1, :], 0.0, masked_score)


def load_rows(x, own, other):
    if x is None:
        return jnp.concatenate([own[:, :512], other[:, :512]], axis=0).astype(f32)
    return x[...]


def attn_fwd_kernel(with_x, ids, own, other, gain, bias, *refs):
    x, refs = (refs[0], refs[1:]) if with_x else (None, refs)
    w_refs, refs = refs[:2], refs[2:]
    x1, lse, saved, refs = refs[0], refs[1], refs[2:8], refs[8:]
    w, h, vt, ot, mask, qs, k, v, o, qst, kt, sems, out_sems = refs
    copies = weight_copies(ids, w_refs, w, sems)
    start_all(copies)
    keeps = [
        pltpu.make_async_copy(held, to, out_sems.at[at])
        for at, (held, to) in enumerate(zip((qs, k, v, o, qst, kt), saved))
    ]
    xf = load_rows(x, own, other)
    h[...] = (ln_parts(xf)[0] * gain[...] + bias[...]).astype(bf16)
    mask[...] = segment_mask(own, other)
    wait_all(copies)
    for t in range(2):
        cols = pl.ds(t * 256, 256)
        qs[:, cols] = (dot(h[...], w[t, :, 0:256]).astype(bf16) * HEAD_DIM ** (-0.5)).astype(bf16)
        k[:, cols] = dot(h[...], w[t, :, 256:512]).astype(bf16)
        v[:, cols] = dot(h[...], w[t, :, 512:768]).astype(bf16)
    qst[...] = qs[...].T
    kt[...] = k[...].T
    vt[...] = v[...].T
    for at in (0, 1, 2, 4, 5):
        keeps[at].start()

    def one_pair(pair, _):
        lanes = pl.ds(pl.multiple_of(pair * 128, 128), 128)
        k_pair = k[:, lanes]
        for which in range(2):
            scores = dot(k_pair, head_rows(qst, pair, which)) + mask[...]
            top = jnp.max(scores, axis=0, keepdims=True)
            numer = jnp.exp(scores - top).astype(bf16)
            rows = pl.ds(pl.multiple_of(pair * 128 + which * HEAD_DIM, HEAD_DIM), HEAD_DIM)
            left = jnp.concatenate([vt[rows, :], jnp.ones((16, 512), bf16)], axis=0)
            both = dot(left, numer)
            total = both[HEAD_DIM : HEAD_DIM + 1, :]
            ot[rows, :] = (both[:HEAD_DIM, :] / total).astype(bf16)
            lse[pl.ds(pair * 2 + which, 1), :] = top + jnp.log(total)
        return 0

    lax.fori_loop(0, 4, one_pair, 0, unroll=True)
    o[...] = ot[...].T
    keeps[3].start()
    acc = xf
    for t in range(2):
        acc = acc + dot_nt(o[:, t * 256 : (t + 1) * 256], w[t, :, 768:1024])
    x1[...] = acc
    wait_all(keeps)


def gelu_parts(u):
    square = u * u
    tanh = jnp.tanh(gelu_coef * u * (1.0 + 0.044715 * square))
    return 0.5 * u * (1.0 + tanh), tanh, square


def mlp_fwd_kernel(n_w, ids, x1, gain, bias, *refs):
    w_refs, refs = refs[:n_w], refs[n_w:]
    y, theirs, w, h2, sems = refs
    copies = weight_copies(ids, w_refs, w, sems)
    start_all(copies)
    h2[...] = (ln_parts(x1[...])[0] * gain[...] + bias[...]).astype(bf16)
    y[...] = x1[...]
    wait_all(copies)

    def one_chunk(index, _):
        t = index // 2
        col = (index % 2) * 512
        pre = dot(h2[...], w[t, :, pl.ds(pl.multiple_of(col, 512), 512)])
        hidden = gelu_parts(pre)[0].astype(bf16)
        y[...] += dot_nt(hidden, w[t, :, pl.ds(pl.multiple_of(col + 1024, 512), 512)])
        return 0

    lax.fori_loop(0, 4, one_chunk, 0, unroll=True)
    theirs[...] = y[256:, :].astype(bf16)


def mlp_bwd_kernel(split, n_w, ids, x1, gain, bias, *refs):
    w_refs, refs = refs[:n_w], refs[n_w:]
    if split:
        own, other, refs = refs[0], refs[1], refs[2:]
    else:
        dy, refs = refs[0], refs[1:]
    dx1, small, refs = refs[0], refs[1], refs[2:]
    g_refs, refs = refs[:2], refs[2:]
    w, g, h2, h2t, dyb, dybt, dh2, w_sems, sems = refs[:9]
    loads = weight_copies(ids, w_refs, w, w_sems)
    start_all(loads)
    if split:
        dy = refs[9]
        dy[0:256, :] = own[ids[1]]
        dy[256:, :] = other[:, 640:].astype(f32)
    h2[...] = (ln_parts(x1[...])[0] * gain[...] + bias[...]).astype(bf16)
    h2t[...] = h2[...].T
    dyb[...] = dy[...].astype(bf16)
    dybt[...] = dyb[...].T
    dh2[...] = jnp.zeros_like(dh2)
    wait_all(loads)

    def one_chunk(index, _):
        t = index // 2
        up = pl.ds(pl.multiple_of((index % 2) * 512, 512), 512)
        down = pl.ds(pl.multiple_of((index % 2) * 512 + 1024, 512), 512)
        pre = dot(h2[...], w[t, :, up])
        hidden, tanh, square = gelu_parts(pre)
        slope = 0.5 * (1.0 + tanh) + (0.5 * gelu_coef) * pre * (1.0 - tanh * tanh) * (
            1.0 + (3 * 0.044715) * square
        )
        dhidden = dot(dyb[...], w[t, :, down])
        dpre = (dhidden * slope).astype(bf16)
        g[t, :, down] = dot(dybt[...], hidden.astype(bf16)).astype(bf16)
        g[t, :, up] = dot(h2t[...], dpre).astype(bf16)
        dh2[...] += dot_nt(dpre, w[t, :, up])
        return 0

    lax.fori_loop(0, 4, one_chunk, 0, unroll=True)
    copies = grad_copies(ids, g, g_refs, sems)
    start_all(copies)
    xhat, inv = ln_parts(x1[...])
    grad = dh2[...]
    small[0:1, :] = jnp.sum(grad * xhat, axis=0, keepdims=True)
    small[1:2, :] = jnp.sum(grad, axis=0, keepdims=True)
    dx1[...] = dy[...] + ln_back(grad, xhat, inv, gain[...])
    for copy in copies:
        copy.wait()


def pack_rows(rows):
    cut = [row[:, 128 * j : 128 * (j + 1)] for row in rows for j in range(4)]
    return jnp.concatenate(split2(jnp.concatenate(cut, axis=0)), axis=0)


def attn_bwd_kernel(with_x, with_small, ids, own, other, dx1, gain, bias, lse, *refs):
    saved, w_refs, refs = refs[:6], refs[6:8], refs[8:]
    x, refs = (refs[0], refs[1:]) if with_x else (None, refs)
    if with_small:
        other_small, refs = refs[0], refs[1:]
    dx, dx_low, small = refs[:3]
    g_refs, refs = refs[3:5], refs[5:]
    w, g, h, mask, do, dot_t, dqt, dq, dk, dv, flip = refs[:11]
    qs, k, v, o, qst, kt, w_sems, in_sems, sems = refs[11:]
    loads = weight_copies(ids, w_refs, w, w_sems)
    start_all(loads)
    takes = [
        pltpu.make_async_copy(held, to, in_sems.at[at])
        for at, (held, to) in enumerate(zip(saved, (qs, k, v, o, qst, kt)))
    ]
    start_all(takes)
    xf = load_rows(x, own, other)
    h[...] = (ln_parts(xf)[0] * gain[...] + bias[...]).astype(bf16)
    mask[...] = segment_mask(own, other)
    low = dx1[...].astype(bf16)
    flip[...] = low.T
    wait_all(loads)
    wait_all(takes)
    for t in range(2):
        cols = pl.ds(t * 256, 256)
        do[:, cols] = dot(low, w[t, :, 768:1024]).astype(bf16)
        g[t, :, 768:1024] = dot(flip[...], o[:, cols]).astype(bf16)
    dot_t[...] = do[...].T
    def one_pair(pair, _):
        lanes = pl.ds(pl.multiple_of(pair * 128, 128), 128)
        k_pair, v_pair = k[:, lanes], v[:, lanes]
        q_pair, do_pair = qs[:, lanes], do[:, lanes]
        dvs, dks = [], []
        for which in range(2):
            head = pl.ds(pair * 2 + which, 1)
            rows = pl.ds(pl.multiple_of(pair * 128 + which * HEAD_DIM, HEAD_DIM), HEAD_DIM)
            scores = dot(k_pair, head_rows(qst, pair, which)) + mask[...]
            probs = jnp.exp(scores - lse[head, :])
            dprobs = dot(v_pair, head_rows(dot_t, pair, which))
            shift = jnp.sum(probs * dprobs, axis=0, keepdims=True)
            dscore = (probs * (dprobs - shift)).astype(bf16)
            dvs.append(dot(probs.astype(bf16), do_pair))
            dks.append(dot(dscore, q_pair))
            dqt[rows, :] = (dot(kt[rows, :], dscore) * HEAD_DIM ** (-0.5)).astype(bf16)
        first = lax.broadcasted_iota(jnp.int32, (512, 128), 1) < HEAD_DIM
        dv[:, lanes] = jnp.where(first, dvs[0], dvs[1]).astype(bf16)
        dk[:, lanes] = jnp.where(first, dks[0], dks[1]).astype(bf16)
        return 0

    lax.fori_loop(0, 4, one_pair, 0, unroll=True)
    dq[...] = dqt[...].T
    flip[...] = h[...].T
    for t in range(2):
        cols = pl.ds(t * 256, 256)
        g[t, :, 0:256] = dot(flip[...], dq[:, cols]).astype(bf16)
        g[t, :, 256:512] = dot(flip[...], dk[:, cols]).astype(bf16)
        g[t, :, 512:768] = dot(flip[...], dv[:, cols]).astype(bf16)
    grad = jnp.zeros((512, 512), f32)
    for t in range(2):
        cols = pl.ds(t * 256, 256)
        for index, part in enumerate((dq, dk, dv)):
            grad = grad + dot_nt(part[:, cols], w[t, :, index * 256 : (index + 1) * 256])
    xhat, inv = ln_parts(xf)
    dgain = jnp.sum(grad * xhat, axis=0, keepdims=True)
    dbias = jnp.sum(grad, axis=0, keepdims=True)
    small[0:1, :] = dgain
    small[1:2, :] = dbias
    if with_small:
        packed = pack_rows([dgain, dbias, other_small[0:1, :], other_small[1:2, :]])
        for t in range(2):
            for row in range(16):
                g[t, row * 32 : (row + 1) * 32, 1024:1152] = packed
    copies = grad_copies(ids, g, g_refs, sems)
    start_all(copies)
    total = dx1[...] + ln_back(grad, xhat, inv, gain[...])
    dx[...] = total
    dx_low[...] = total[256:, :].astype(bf16)
    for copy in copies:
        copy.wait()


def code_prep_kernel(book_t, stack, stack_t):
    def one_chunk(index, _):
        lanes = pl.ds(pl.multiple_of(index * 512, 512), 512)
        rows = book_t[:, lanes]
        unit = rows * lax.rsqrt(jnp.sum(rows * rows, axis=0, keepdims=True) + norm_eps)
        hi, mid, lo = split3(unit)
        stack_t[:, lanes] = jnp.concatenate([hi, mid, lo, jnp.ones((32, 512), bf16)], axis=0)
        tall = jnp.concatenate([hi, mid, lo, hi, mid, hi, jnp.zeros((64, 512), bf16)], axis=0)
        stack[lanes, :] = tall.T
        return 0

    lax.fori_loop(0, book_t.shape[1] // 512, one_chunk, 0)


def factor_stack(x):
    hi, mid, lo = split3(x)
    return jnp.concatenate([hi, hi, hi, mid, mid, lo, jnp.zeros((64, x.shape[1]), bf16)], axis=0)


def code_loads(pairs, sems):
    loads = []
    for piece in range(4):
        group = []
        for at, (held, to, by_row) in enumerate(pairs):
            size = held.shape[0 if by_row else 1] // 4
            part = pl.ds(piece * size, size)
            place = (part, slice(None)) if by_row else (slice(None), part)
            group.append(pltpu.make_async_copy(held.at[place], to.at[place], sems.at[at, piece]))
        start_all(group)
        loads.append(group)
    return loads


def vq_fwd_kernel(
    e, gain, bias, in_t, out_w, stack_hbm, stack_t_hbm, u, kept, acc, stack, stack_t, sems
):
    loads = code_loads([(stack_hbm, stack, True), (stack_t_hbm, stack_t, False)], sems)
    lnv = ln_parts(e[...])[0] * gain[...] + bias[...]
    raw = dot_nt(in_t[...], lnv, highest)
    inv = lax.rsqrt(jnp.sum(raw * raw, axis=0, keepdims=True) + norm_eps)
    latent = raw * inv
    right = factor_stack(latent * (temper * log2e))
    acc[...] = jnp.zeros_like(acc)

    def one_chunk(index, _):
        codes = pl.ds(pl.multiple_of(index * 512, 512), 512)
        numer = jnp.exp2(dot(stack[codes, :], right)).astype(bf16)
        acc[...] += dot(stack_t[:, codes], numer)
        return 0

    chunks = stack.shape[0] // 512
    for piece, group in enumerate(loads):
        wait_all(group)
        lax.fori_loop(chunks * piece // 4, chunks * (piece + 1) // 4, one_chunk, 0)
    total = acc[96:97, :]
    soft = (acc[0:32, :] + acc[32:64, :] + acc[64:96, :]) / total
    kept[0:32, :] = latent
    kept[32:64, :] = soft
    kept[64:65, :] = total
    kept[65:66, :] = inv
    u[...] = dot_full(soft.T, out_w[...])


def vq_bwd_kernel(ids, e, du, gain, bias, in_t, out_w, stack_hbm, stack_t_hbm, book_hbm, kept, *refs):
    small0, small1, de, code_keep, code_send = refs[:5]
    acc, grads, small, tail, stack, stack_t, book_t, load_sems, sems = refs[5:]
    loads = code_loads(
        [(stack_hbm, stack, True), (stack_t_hbm, stack_t, False), (book_hbm, book_t, False)],
        load_sems,
    )
    xhat, inv_ln = ln_parts(e[...])
    lnv = xhat * gain[...] + bias[...]
    latent, soft = kept[0:32, :], kept[32:64, :]
    total, inv = kept[64:65, :], kept[65:66, :]
    direct = (2.0 * 1.25 * commit_weight) * (latent - soft)
    dsoft = dot_nt(out_w[...], du[...], highest) - direct
    small[32:64, :] = dot_full(soft, du[...])
    shift = jnp.sum(dsoft * soft, axis=0, keepdims=True) / total
    dsoft = dsoft / total
    right = jnp.concatenate(
        [factor_stack(latent * (temper * log2e)), factor_stack(dsoft)], axis=1
    )
    pads = jnp.zeros((64, 512), f32)

    def tall(x):
        hi, lo = split2(x)
        return jnp.concatenate([hi.astype(f32), lo.astype(f32), pads], axis=0).T.astype(bf16)

    sides = jnp.concatenate([tall(dsoft), tall(latent * temper)], axis=0)
    acc[...] = jnp.zeros_like(acc)

    def one_chunk(index, _):
        codes = pl.ds(pl.multiple_of(index * 512, 512), 512)
        both = dot(stack[codes, :], right)
        numer = jnp.exp2(both[:, :512])
        dlogit = (numer * (both[:, 512:] - shift)).astype(bf16)
        acc[...] += dot(stack_t[0:96, codes], dlogit)
        dcode = dot(jnp.concatenate([numer.astype(bf16), dlogit], axis=1), sides).T
        dcode = dcode[0:32, :] + dcode[32:64, :]
        rows = book_t[:, codes]
        scale = lax.rsqrt(jnp.sum(rows * rows, axis=0, keepdims=True) + norm_eps)
        unit = rows * scale
        grads[:, codes] = (
            scale * (dcode - unit * jnp.sum(unit * dcode, axis=0, keepdims=True))
        ).astype(bf16)
        return 0

    chunks = stack.shape[0] // 512
    for piece, group in enumerate(loads):
        wait_all(group)
        lax.fori_loop(chunks * piece // 4, chunks * (piece + 1) // 4, one_chunk, 0)
    dlatent = temper * (acc[0:32, :] + acc[32:64, :] + acc[64:96, :]) + direct
    draw = inv * (dlatent - latent * jnp.sum(latent * dlatent, axis=0, keepdims=True))
    small[0:32, :] = dot_full(draw, lnv)
    dln = dot_full(draw.T, in_t[...])
    small[64:65, :] = jnp.sum(dln * xhat, axis=0, keepdims=True)
    small[65:66, :] = jnp.sum(dln, axis=0, keepdims=True)
    small[66:68, :] = small0[0:2, :]
    small[68:70, :] = small1[0:2, :]
    small[70:96, :] = jnp.zeros((26, 512), f32)
    for block in range(3):
        for at, part in enumerate(split2(small[block * 32 : (block + 1) * 32, :])):
            for side in range(2):
                tail[block * 2 + side, :, at * 256 : (at + 1) * 256] = part[
                    :, side * 256 : (side + 1) * 256
                ]
    tail[6:8] = jnp.zeros((2, 32, 512), bf16)
    core, z = ids[0] % 2, ids[0] // 4
    copies = []
    for slot, (at, to) in enumerate(((core, code_keep), (1 - core, code_send))):
        for k in range(4):
            part = at * 4 + (z ^ k)
            lanes = pl.ds(pl.multiple_of(part * 1024, 1024), 1024)
            copies += [
                pltpu.make_async_copy(
                    grads.at[:, lanes], to.at[k, :, pl.ds(0, 1024)], sems.at[0, slot, k]
                ),
                pltpu.make_async_copy(
                    tail.at[part], to.at[k, :, pl.ds(1024, 512)], sems.at[1, slot, k]
                ),
            ]
    for copy in copies:
        copy.start()
    de[...] = ln_back(dln, xhat, inv_ln, gain[...])
    for copy in copies:
        copy.wait()


SMEM = pl.BlockSpec(memory_space=pltpu.SMEM)
VMEM = pl.BlockSpec(memory_space=pltpu.VMEM)
ANY = pl.BlockSpec(memory_space=pl.ANY)


def shaped(*pairs):
    return [jax.ShapeDtypeStruct(shape, dtype) for shape, dtype in pairs]


def pin(array):
    return pltpu.with_memory_space_constraint(array, pltpu.HBM)


def call(kernel, name, in_specs, out_specs, outs, scratch, flops, after=(), carry=()):
    n_in, n_extra, n_out = len(in_specs), len(after) + len(carry), len(outs)

    def body(*refs):
        first = n_in + n_extra
        kernel(*refs[:n_in], *refs[first : first + n_out], *refs[first + n_out + len(carry) :])

    made = pl.pallas_call(
        body,
        name=name,
        in_specs=in_specs + [ANY] * n_extra,
        out_specs=out_specs + [ANY] * len(carry),
        out_shape=outs + [jax.ShapeDtypeStruct(a.shape, a.dtype) for a in carry],
        scratch_shapes=scratch,
        input_output_aliases={n_in + len(after) + i: n_out + i for i in range(len(carry))},
        compiler_params=pltpu.CompilerParams(vmem_limit_bytes=vmem_cap),
        cost_estimate=pl.CostEstimate(flops=flops, bytes_accessed=10**6, transcendentals=0),
    )

    def run(*args):
        res = made(*args, *after, *carry)
        return (*res[:n_out], list(res[n_out:]))

    return run


DMA = pltpu.SemaphoreType.DMA
ROWS2 = (512, 512)


def attn_fwd(ids, marked, xs, gain, bias, w, after=(), carry=()):
    outs = shaped((ROWS2, f32), ((8, 512), f32)) + [pltpu.HBM(ROWS2, bf16)] * 6
    scratch = [
        pltpu.VMEM((2, 512, 1024), bf16),
        *[pltpu.VMEM(ROWS2, bf16)] * 3,
        pltpu.VMEM(ROWS2, f32),
        *[pltpu.VMEM(ROWS2, bf16)] * 6,
        DMA((32,)),
        DMA((6,)),
    ]
    x1, lse, *saved, carried = call(
        functools.partial(attn_fwd_kernel, bool(xs)),
        "attn_fwd",
        [SMEM] + [VMEM] * (4 + len(xs)) + [ANY] * len(w),
        [VMEM] * 2 + [ANY] * 6,
        outs,
        scratch,
        10**10,
        after,
        carry,
    )(ids, *marked, gain, bias, *xs, *map(pin, w))
    return x1, (lse, *saved), carried


def mlp_fwd(ids, x1, gain, bias, w, after=(), carry=()):
    return call(
        functools.partial(mlp_fwd_kernel, len(w)),
        "mlp_fwd",
        [SMEM] + [VMEM] * 3 + [ANY] * len(w),
        [VMEM] * 2,
        shaped((ROWS2, f32), ((256, 512), bf16)),
        [pltpu.VMEM((2, 512, 2048), bf16), pltpu.VMEM(ROWS2, bf16), DMA((16 * len(w),))],
        8 * 10**9,
        after,
        carry,
    )(ids, x1, gain, bias, *map(pin, w))


def mlp_bwd(ids, x1, dys, gain, bias, w, after=(), carry=()):
    grads = shaped(*[((4, 4, 32, 2048), bf16)] * 2)
    scratch = [
        pltpu.VMEM((2, 512, 2048), bf16),
        pltpu.VMEM((2, 512, 2048), bf16),
        *[pltpu.VMEM(ROWS2, bf16)] * 4,
        pltpu.VMEM(ROWS2, f32),
        DMA((16 * len(w),)),
        DMA((32,)),
        *[pltpu.VMEM(ROWS2, f32)] * (len(dys) - 1),
    ]
    return call(
        functools.partial(mlp_bwd_kernel, len(dys) == 2, len(w)),
        "mlp_bwd",
        [SMEM] + [VMEM] * 3 + [ANY] * len(w) + [VMEM] * len(dys),
        [VMEM] * 2 + [ANY] * len(grads),
        shaped((ROWS2, f32), ((8, 512), f32)) + grads,
        scratch,
        15 * 10**9,
        after,
        carry,
    )(ids, x1, gain, bias, *map(pin, w), *dys)


def attn_bwd(ids, marked, xs, dx1, gain, bias, saved, w, other_small=(), after=(), carry=()):
    width = 1024 + 128 * len(other_small)
    grads = shaped(*[((4, 4, 32, width), bf16)] * 2)
    scratch = [
        pltpu.VMEM((2, 512, 1024), bf16),
        pltpu.VMEM((2, 512, width), bf16),
        pltpu.VMEM(ROWS2, bf16),
        pltpu.VMEM(ROWS2, f32),
        *[pltpu.VMEM(ROWS2, bf16)] * 13,
        DMA((32,)),
        DMA((6,)),
        DMA((32,)),
    ]
    return call(
        functools.partial(attn_bwd_kernel, bool(xs), bool(other_small)),
        "attn_bwd",
        [SMEM] + [VMEM] * 6 + [ANY] * (6 + len(w)) + [VMEM] * (len(xs) + len(other_small)),
        [VMEM] * 3 + [ANY] * len(grads),
        shaped((ROWS2, f32), ((256, 512), bf16), ((8, 512), f32)) + grads,
        scratch,
        15 * 10**9,
        after,
        carry,
    )(ids, *marked, dx1, gain, bias, saved[0], *map(pin, saved[1:]), *map(pin, w), *xs, *other_small)


def code_prep(book_t, after=(), carry=()):
    codes = book_t.shape[1]
    return call(
        code_prep_kernel,
        "code_prep",
        [VMEM],
        [VMEM] * 2,
        shaped(((codes, 256), bf16), ((128, codes), bf16)),
        [],
        6 * 10**9,
        after,
        carry,
    )(book_t)


def vq_fwd(e, gain, bias, in_t, out_w, stack, stack_t, after=(), carry=()):
    return call(
        vq_fwd_kernel,
        "vq_fwd",
        [VMEM] * 5 + [ANY] * 2,
        [VMEM] * 2,
        shaped((ROWS2, f32), ((72, 512), f32)),
        [
            pltpu.VMEM((128, 512), f32),
            pltpu.VMEM(stack.shape, bf16),
            pltpu.VMEM(stack_t.shape, bf16),
            DMA((2, 4)),
        ],
        15 * 10**9,
        after,
        carry,
    )(e, gain, bias, in_t, out_w, pin(stack), pin(stack_t))


def vq_bwd(ids, e, du, gain, bias, in_t, out_w, codes, kept, smalls, after=(), carry=()):
    scratch = [
        pltpu.VMEM((96, 512), f32),
        pltpu.VMEM(codes[2].shape, bf16),
        pltpu.VMEM((96, 512), f32),
        pltpu.VMEM((8, 32, 512), bf16),
        *[pltpu.VMEM(a.shape, a.dtype) for a in codes],
        DMA((3, 4)),
        DMA((2, 2, 4)),
    ]
    return call(
        vq_bwd_kernel,
        "vq_bwd",
        [SMEM] + [VMEM] * 6 + [ANY] * 3 + [VMEM] * 3,
        [VMEM] + [ANY] * 2,
        shaped((ROWS2, f32), *[((4, 32, 1536), bf16)] * 2),
        scratch,
        25 * 10**9,
        after,
        carry,
    )(ids, e, du, gain, bias, in_t, out_w, *map(pin, codes), kept, *smalls)


def lines_kernel(cuts, *refs):
    first = 0
    for out, width in zip(refs[4:], cuts):
        for k in range(4):
            out[k] = refs[k][:, first : first + width]
        first += width


def stack_lines(shards, cuts, after=(), carry=()):
    return call(
        functools.partial(lines_kernel, cuts),
        "stack_lines",
        [VMEM] * 4,
        [VMEM] * len(cuts),
        shaped(*[((4, 32, width), bf16) for width in cuts]),
        [],
        1,
        after,
        carry,
    )(*shards)


def quads_kernel(*refs):
    for i in range(4):
        refs[4][i] = refs[i][...]


def stack_quads(quads, after=(), carry=()):
    return call(
        quads_kernel,
        "stack_quads",
        [VMEM] * 4,
        [VMEM],
        shaped(((4, *quads[0].shape), bf16)),
        [],
        1,
        after,
        carry,
    )(*quads)


def pack_kernel(ids, *refs):
    hbm, (enc, dec_attn, dec_mlp, own, send), (qkv, out_t, up, down_t, tokens, segs, cot, sems) = (
        refs[:7],
        refs[7:12],
        refs[12:],
    )
    held = (qkv, out_t, up, down_t, tokens, segs, cot)
    copies = [pltpu.make_async_copy(hbm[at], held[at], sems.at[at]) for at in range(7)]
    start_all(copies)
    wait_all(copies[:4])
    for layer, (attn, mlp, first) in enumerate(((enc, enc, 1024), (dec_attn, dec_mlp, 0))):
        for index in range(3):
            attn[:, index * 256 : (index + 1) * 256] = qkv[layer, index]
        attn[:, 768:1024] = out_t[layer]
        mlp[:, first : first + 1024] = up[layer]
        mlp[:, first + 1024 : first + 2048] = down_t[layer]
    wait_all(copies[4:])
    for to, micro in ((own, ids[1]), (send, 1 - ids[1])):
        to[:, :512] = tokens[micro]
        ids_row = segs[pl.ds(micro, 1), :].astype(f32)
        to[:, 512:640] = jnp.broadcast_to(ids_row, (128, 256)).T.astype(bf16)
    send[:, 640:] = cot[1 - ids[1]].astype(bf16)


def pack(ids, *arrays):
    outs = shaped(
        ((32, 3072), bf16),
        ((32, 1024), bf16),
        ((32, 2048), bf16),
        ((256, 640), bf16),
        ((256, 1152), bf16),
    )
    return call(
        pack_kernel,
        "pack",
        [SMEM] + [ANY] * 7,
        [VMEM] * 5,
        outs,
        [*[pltpu.VMEM(a.shape, a.dtype) for a in arrays], DMA((7,))],
        1,
    )(ids, *map(pin, arrays))[:-1]


def joined(block):
    return block[0:16, 1024:].astype(f32) + block[16:32, 1024:].astype(f32)


def put_small(value, own, blocks):
    hi, lo = split2(value)
    own[0:16, 1024:] = hi.astype(f32) + lo.astype(f32)
    for block in blocks:
        block[0:16, 1024:] = hi
        block[16:32, 1024:] = lo


def near_kernel(ids, ins, outs):
    keep, other = ins
    for i in range(4):
        outs[i][...] = (keep[i].astype(f32) + other[i].astype(f32)).astype(outs[i].dtype)
    if keep.shape[3] == 1152:
        value = joined(keep.at[0, 0]) + joined(other.at[0, 0])
        put_small(value, outs[0].at[0], [out.at[0] for out in outs[1:]])


def near_task(keep, other):
    shape = keep.shape[1:]
    return near_kernel, [keep, other], shaped((shape, f32), *[(shape, bf16)] * 3)


def fork_kernel(ids, ins, outs):
    keep, other = ins
    for at, (own, send, kept, sent) in enumerate(((outs[0], outs[1], (0, 2), (1, 3)), (outs[2], outs[3], (0, 1), (2, 3)))):
        cols = slice(1024 * at, 1024 * (at + 1))
        for j in range(2):
            for out, i in ((own, kept[j]), (send, sent[j])):
                total = keep[i, :, :, cols].astype(f32) + other[i, :, :, cols].astype(f32)
                out[j] = total.astype(out.dtype)


def fork_task(keep, other):
    shape = (2, *keep.shape[1:3], 1024)
    return fork_kernel, [keep, other], shaped(*[(shape, f32), (shape, bf16)] * 2)


def half_kernel(ids, ins, outs):
    own, other = ins
    for j in range(2):
        outs[j][...] = (own[j] + other[j].astype(f32)).astype(outs[j].dtype)


def half_task(own, other):
    shape = own.shape[1:]
    return half_kernel, [own, other], shaped((shape, f32), (shape, bf16))


def join_kernel(ids, ins, outs):
    for at in range(2):
        own, other = ins[2 * at : 2 * at + 2]
        for k in range(4):
            total = own[k] + other[k].astype(f32)
            outs[k][:, 1024 * at : 1024 * (at + 1)] = total.astype(outs[k].dtype)


def join_task(own_up, other_up, own_down, other_down):
    outs = shaped(((32, 2048), f32), *[((32, 2048), bf16)] * 3)
    return join_kernel, [own_up, other_up, own_down, other_down], outs


def plane_kernel(ids, ins, outs):
    for k in range(4):
        total = ins[0][k]
        for other in ins[1:]:
            total = total + other[k].astype(f32)
        outs[k][...] = total.astype(outs[k].dtype)
    if ins[0].shape[2] == 1152:
        x, y, xy = [joined(other.at[0]) for other in ins[1:]]
        put_small((ins[0][0, 0:16, 1024:] + x) + (y + xy), outs[0], outs[1:])


def plane_task(own, others):
    shape = own.shape[1:]
    return plane_kernel, [own, *others], shaped((shape, f32), *[(shape, bf16)] * 3)


def plane_join_kernel(ids, ins, outs):
    plane_kernel(ids, ins[:4], [out.at[:, pl.ds(0, 1024)] for out in outs])
    for part, out in zip(ins[4:], outs):
        out[:, 1024:] = part[...]


def plane_join_task(own, others, *parts):
    outs = shaped(((32, 3072), f32), *[((32, 3072), bf16)] * 3)
    return plane_join_kernel, [own, *others, *parts], outs


def line_total(ins, width):
    total = ins[0][:, :width]
    for other in ins[1:]:
        total = total + other[:, :width].astype(f32)
    return total


def rows_kernel(ids, ins, outs):
    own, other = ins
    half = other.shape[0]
    outs[0][ids[1]] = own[0:half, :].astype(f32)
    outs[0][1 - ids[1]] = other[...].astype(f32)


def rows_task(own, other):
    return rows_kernel, [own, other], shaped(((2, *other.shape), f32))


def code_small(ref):
    return ref[:, 1024:1280].astype(f32) + ref[:, 1280:1536].astype(f32)


def code_sum(refs, out):
    total, small = refs[0][:, :1024].astype(f32), code_small(refs[0])
    for ref in refs[1:]:
        total = total + ref[:, :1024].astype(f32)
        small = small + code_small(ref)
    hi, lo = split2(small)
    out[:, :1024] = total.astype(bf16)
    out[:, 1024:1280] = hi
    out[:, 1280:1536] = lo


def code_near_kernel(ids, ins, outs):
    for k in range(4):
        code_sum([ref.at[k] for ref in ins], outs[k])


def code_near_task(keep, other):
    return code_near_kernel, [keep, other], shaped(*[(keep.shape[1:], bf16)] * 4)


def code_add_kernel(ids, ins, outs):
    code_sum(ins, outs[0])


def code_add_task(*parts):
    return code_add_kernel, list(parts), shaped((parts[0].shape, bf16))


def code_line_kernel(ids, ins, outs):
    for k in range(4):
        outs[0][k] = ins[k][...]


def code_line_task(*parts):
    return code_line_kernel, list(parts), shaped(((4, *parts[0].shape), bf16))


def finish_kernel(ids, ins, outs):
    mlp, attn, dec, code, code_other = ins[:4], ins[4:8], ins[8:12], *ins[12:]
    qkv, out_t, up, down_t, book, vq_in, vq_out, gains, biases, dec_biases, small_ref = outs
    both = line_total(dec, 3072)
    for layer, rows in enumerate((line_total(mlp, 2048), both[:, 1024:])):
        up[layer] = rows[:, :1024]
        down_t[layer] = rows[:, 1024:]
    for layer, rows in enumerate((line_total(attn, 1024), both[:, :1024])):
        for index in range(3):
            qkv[layer, index] = rows[:, index * 256 : (index + 1) * 256]
        out_t[layer] = rows[:, 768:]
    core, z = ids[0] % 2, ids[0] // 4
    for at, parts in ((core, code), (1 - core, code_other)):
        for k in range(4):
            part = at * 4 + (z ^ k)
            book[:, pl.ds(pl.multiple_of(part * 1024, 1024), 1024)] = parts[k, :, :1024].astype(f32)
            small_ref[:, pl.ds(pl.multiple_of(part * 256, 256), 256)] = code_small(parts.at[k])
    small = small_ref[...]
    vq_in[...] = small[:, :512]
    vq_out[...] = small[:, 512:1024]
    rest = small[:, 1024:1536]
    k1, k2, k3 = [joined(other) for other in attn[1:]]
    packed = (attn[0][0:16, 1024:] + k1) + (k2 + k3)
    for row, out in enumerate((gains.at[0:1], biases.at[0:1], gains.at[1:2], biases.at[1:2])):
        for j in range(4):
            out[:, 128 * j : 128 * (j + 1)] = packed[row * 4 + j : row * 4 + j + 1, :]
    gains[2:3, :] = rest[0:1, :]
    biases[2:3, :] = rest[1:2, :]
    gains[3:4, :] = rest[2:3, :]
    dec_biases[0:1, :] = rest[3:4, :]
    gains[4:5, :] = rest[4:5, :]
    dec_biases[1:2, :] = rest[5:6, :]


def finish_task(own_m, line_m, own_a, line_a, own_d, line_d, code, code_other):
    outs = shaped(
        ((2, 3, 32, 256), f32),
        ((2, 32, 256), f32),
        ((2, 32, 1024), f32),
        ((2, 32, 1024), f32),
        ((32, 8192), f32),
        ((32, 512), f32),
        ((32, 512), f32),
        ((5, 512), f32),
        ((3, 512), f32),
        ((2, 512), f32),
        ((32, 2048), f32),
    )
    ins = [own_m, *line_m, own_a, *line_a, own_d, *line_d, code, code_other]
    return finish_kernel, ins, outs


def run_tasks(ids, name, tasks, after=(), carry=()):
    sizes = [(len(ins), len(outs)) for _, ins, outs in tasks]
    n_in = sum(i for i, _ in sizes)

    def kernel(ids_ref, *refs):
        at_in, at_out = 0, n_in
        for (fn, _, _), (i, o) in zip(tasks, sizes):
            fn(ids_ref, refs[at_in : at_in + i], refs[at_out : at_out + o])
            at_in, at_out = at_in + i, at_out + o

    outs = [one for _, _, many in tasks for one in many]
    res = call(
        kernel, name, [SMEM] + [VMEM] * n_in, [VMEM] * len(outs), outs, [], 10**9, after, carry
    )(ids, *[one for _, many, _ in tasks for one in many])
    split, at = [], 0
    for _, o in sizes:
        split.append(res[at : at + o])
        at += o
    return (*split, res[-1])


def whole_groups(
    n_dp,
    tokens,
    segment_ids,
    norm_gains,
    norm_biases,
    w_qkv,
    w_attn_out,
    w_up,
    w_down,
    w_vq_in,
    w_vq_out,
    codebook,
    cotangent,
):
    dp_at, tp_at = lax.axis_index("dp"), lax.axis_index("tp")
    ids = jnp.stack([dp_at, tp_at]).astype(jnp.int32)

    def swap(values):
        return exchange(values, 0, 1, n_dp)

    gains = [norm_gains[i : i + 1] for i in range(5)]
    biases = [norm_biases[i : i + 1] for i in range(5)]
    book_t, in_t = codebook.T, w_vq_in.T
    enc_shard, dec_attn, dec_mlp, own, send = pack(
        ids,
        w_qkv,
        w_attn_out.transpose(0, 2, 1),
        w_up,
        w_down.transpose(0, 2, 1),
        tokens,
        segment_ids,
        cotangent,
    )
    marked = [own, swap(send)]

    attn_line, mlp_line, _ = stack_lines(spread_line(enc_shard, n_dp), [1024, 2048])
    stack, stack_t, _ = code_prep(book_t, [attn_line])
    codes = (stack, stack_t, book_t)
    enc_attn, (mlp_line, dec_attn) = stack_quads(
        plane_quads(attn_line, n_dp), [stack_t, marked[1]], [mlp_line, dec_attn]
    )
    quads, dec_attn = plane_quads(mlp_line, n_dp), spread_line(dec_attn, n_dp)
    enc_attn = [enc_attn, exchange(enc_attn, 1, 0, n_dp)]
    e_x1, e_saved, _ = attn_fwd(ids, marked, [], gains[0], biases[0], enc_attn)
    dec_attn, _ = stack_lines(dec_attn, [1024], [e_x1])
    enc_mlp, (dec_mlp,) = stack_quads(quads, [e_x1, dec_attn], [dec_mlp])
    dec_attn, dec_mlp = plane_quads(dec_attn, n_dp), spread_line(dec_mlp, n_dp)
    enc_mlp = [enc_mlp, exchange(enc_mlp, 1, 0, n_dp)]
    e, _, _ = mlp_fwd(ids, e_x1, gains[1], biases[1], enc_mlp)
    up_line, down_line, _ = stack_lines(dec_mlp, [1024, 1024], [e])
    dec_attn, (up_line,) = stack_quads(dec_attn, [e], [up_line])
    dec_attn = [dec_attn, exchange(dec_attn, 1, 0, n_dp)]
    ups = plane_quads(up_line, n_dp)
    u, kept, _ = vq_fwd(e, gains[2], biases[2], in_t, w_vq_out, stack, stack_t)
    dec_up, (down_line,) = stack_quads(ups, [u, dec_attn[1]], [down_line])
    downs, dec_up = plane_quads(down_line, n_dp), [dec_up, exchange(dec_up, 1, 0, n_dp)]
    d_x1, d_saved, _ = attn_fwd(ids, marked, [u], gains[3], biases[3], dec_attn)
    dec_down, _ = stack_quads(downs, [d_x1, dec_up[1]])
    dec_mlp = [*dec_up, dec_down, exchange(dec_down, 1, 0, n_dp)]

    dx1, d_small1, keep_m, send_m, _ = mlp_bwd(
        ids, d_x1, [cotangent, marked[1]], gains[4], biases[4], dec_mlp
    )
    near_m = exchange(send_m, 1, 0, n_dp)
    du, _, d_small0, keep_a, send_a, (keep_m,) = attn_bwd(
        ids, marked, [u], dx1, gains[3], biases[3], d_saved, dec_attn, carry=[keep_m]
    )
    (own_m, *lows_m), (send_a,) = run_tasks(
        ids, "sums1", [near_task(keep_m, near_m)], carry=[send_a]
    )
    plane_m, near_a = plane_send(lows_m, n_dp), exchange(send_a, 1, 0, n_dp)
    de, code, code_send, (own_m, keep_a) = vq_bwd(
        ids,
        e,
        du,
        gains[2],
        biases[2],
        in_t,
        w_vq_out,
        codes,
        kept,
        [d_small0, d_small1],
        lows_m,
        [own_m, keep_a],
    )
    d_mlp, (own_a, *lows_a), (code_send,) = run_tasks(
        ids, "sums2", [plane_task(own_m, plane_m), near_task(keep_a, near_a)], carry=[code_send]
    )
    plane_a, code_other = plane_send(lows_a, n_dp), exchange(code_send, 1, 0, n_dp)
    code_parts, _ = run_tasks(ids, "sums2b", [code_near_task(code, code_other)])
    code, *code_others = code_parts[0], *line_send(code_parts[1:], n_dp)
    ex1, e_small1, keep_m, send_m, (own_a,) = mlp_bwd(
        ids, e_x1, [de], gains[1], biases[1], enc_mlp, [*lows_a, code_parts[1]], [own_a]
    )
    (own_d, *lows_d), (code,), (keep_m, send_m, d_x1) = run_tasks(
        ids,
        "sums3",
        [plane_join_task(own_a, plane_a, *d_mlp), code_add_task(code, *code_others)],
        carry=[keep_m, send_m, d_x1],
    )
    near_m, code_other = exchange(send_m, 1, 0, n_dp), exchange(code, 0, 1, n_dp)
    line_d = line_send(lows_d, n_dp)
    y, y_theirs, _ = mlp_fwd(ids, d_x1, gains[4], biases[4], dec_mlp)
    (own_up, send_up, own_down, send_down), (code,), (y_theirs,) = run_tasks(
        ids,
        "sums3b",
        [fork_task(keep_m, near_m), code_add_task(code, code_other)],
        carry=[y_theirs],
    )
    other_up, other_down = exchange(send_up, 0, 1, n_dp), exchange(send_down, 2, 0, n_dp)
    code_other, y_other = exchange(code, 2, 0, n_dp), swap(y_theirs)
    dx, dx_low, _, keep_a, send_a, (own_up, own_down) = attn_bwd(
        ids,
        marked,
        [],
        ex1,
        gains[0],
        biases[0],
        e_saved,
        enc_attn,
        [e_small1],
        [send_up, send_down, code],
        [own_up, own_down],
    )
    (own_up, send_up), (own_down, send_down), (code,), (decoded,), (keep_a, send_a, dx_low) = run_tasks(
        ids,
        "sums4",
        [
            half_task(own_up, other_up),
            half_task(own_down, other_down),
            code_add_task(code, code_other),
            rows_task(y, y_other),
        ],
        line_d,
        [keep_a, send_a, dx_low],
    )
    near_a, code_others = exchange(send_a, 1, 0, n_dp), line_send([code] * 3, n_dp)
    other_up, other_down = exchange(send_up, 2, 0, n_dp), exchange(send_down, 0, 1, n_dp)
    (own_a, *lows_a), (code,), (own_up, own_down, dx_low) = run_tasks(
        ids,
        "sums4b",
        [near_task(keep_a, near_a), code_line_task(code, *code_others)],
        carry=[own_up, own_down, dx_low],
    )
    plane_a, code_other = plane_send(lows_a, n_dp), exchange(code, 1, 0, n_dp)
    dx_other = swap(dx_low)
    (own_m, *lows_m), (own_a,) = run_tasks(
        ids, "sums5", [join_task(own_up, other_up, own_down, other_down)], lows_a, [own_a]
    )
    line_m = line_send(lows_m, n_dp)
    (own_a, *lows_a), (grad_tokens,), (own_m,) = run_tasks(
        ids, "sums6", [plane_task(own_a, plane_a), rows_task(dx, dx_other)], lows_m, [own_m]
    )
    line_a = line_send(lows_a, n_dp)
    (qkv, out_t, up, down_t, book, vq_in, vq_out, *norms, _), _ = run_tasks(
        ids,
        "finish",
        [finish_task(own_m, line_m, own_a, line_a, own_d, line_d, code, code_other)],
    )
    return (
        decoded,
        grad_tokens,
        *norms,
        qkv,
        out_t.transpose(0, 2, 1),
        up,
        down_t.transpose(0, 2, 1),
        vq_in.T,
        vq_out,
        book.T,
    )


def layer_norm(values, norm_gain, norm_bias):
    centred = values - jnp.mean(values, axis=-1, keepdims=True)
    spread = jnp.mean(centred * centred, axis=-1, keepdims=True)
    return centred * lax.rsqrt(spread + ln_eps) * norm_gain + norm_bias


def gelu_tanh(values):
    return (
        0.5 * values * (1.0 + jnp.tanh(gelu_coef * (values + 0.044715 * values * values * values)))
    )


def matmul(former, latter):
    return jnp.dot(former, latter, precision=highest, preferred_element_type=jnp.float32)


def normalize(values):
    return values * lax.rsqrt(jnp.sum(values * values, axis=-1, keepdims=True) + norm_eps)


def quantize(in_rows, norm_gain, norm_bias, in_w, out_w, code_w):
    latent = normalize(matmul(layer_norm(in_rows, norm_gain, norm_bias), in_w))
    code_rows = normalize(code_w)
    logits = matmul(latent, code_rows.T) * temper
    row_max = jnp.max(logits, axis=-1, keepdims=True)
    numerator = jnp.exp(logits - row_max)
    assign = numerator / jnp.sum(numerator, axis=-1, keepdims=True)
    soft_code = matmul(assign, code_rows)
    offset = latent - soft_code
    vq_loss = commit_weight * 1.25 * jnp.sum(offset * offset)
    return (matmul(soft_code, out_w), vq_loss)


def product(former, latter):
    return jnp.dot(former, latter, preferred_element_type=jnp.float32)


def product_tn(former, latter):
    return lax.dot_general(
        former, latter, (((0,), (0,)), ((), ())), preferred_element_type=jnp.float32
    )


def product_nt(former, latter):
    return lax.dot_general(
        former, latter, (((1,), (1,)), ((), ())), preferred_element_type=jnp.float32
    )


def split_heads(values):
    return values.reshape(values.shape[0], values.shape[1] // HEAD_DIM, HEAD_DIM).transpose(1, 0, 2)


def join_heads(values):
    return values.transpose(1, 0, 2).reshape(values.shape[1], values.shape[0] * HEAD_DIM)


def masked_scores(query_blk, key_h, seg_blk, seg_keys):
    scores = jnp.einsum(
        "hqd,hkd->hqk", query_blk, key_h, preferred_element_type=jnp.float32
    ) * HEAD_DIM ** (-0.5)
    return jnp.where((seg_blk[:, None] == seg_keys[None, :])[None], scores, masked_score)


def attend(query_h, key_h, value_h, seg_keys):
    block_rows = min(512, query_h.shape[1])
    block_count = query_h.shape[1] // block_rows

    def one_block(begin_row):
        query_blk = lax.dynamic_slice_in_dim(query_h, begin_row, block_rows, 1)
        seg_blk = lax.dynamic_slice_in_dim(seg_keys, begin_row, block_rows, 0)
        scores = masked_scores(query_blk, key_h, seg_blk, seg_keys)
        row_max = jnp.max(scores, axis=-1, keepdims=True)
        numerator = jnp.exp(scores - row_max)
        row_total = jnp.sum(numerator, axis=-1, keepdims=True)
        prob_low = (numerator / row_total).astype(jnp.bfloat16)
        attended = jnp.einsum("hqk,hkd->hqd", prob_low, value_h, preferred_element_type=jnp.float32)
        return (attended.astype(jnp.bfloat16), (row_max + jnp.log(row_total))[..., 0])

    starts = jnp.arange(block_count, dtype=jnp.int32) * block_rows
    attended, log_sums = lax.map(one_block, starts)
    heads_out = attended.transpose(1, 0, 2, 3).reshape(query_h.shape)
    log_sums = log_sums.transpose(1, 0, 2).reshape(query_h.shape[0], query_h.shape[1])
    return (heads_out, log_sums)


def attend_back(query_h, key_h, value_h, seg_keys, log_sums, grad_out):
    block_rows = min(512, query_h.shape[1])
    block_count = query_h.shape[1] // block_rows

    def one_block(carry, begin_row):
        grad_key, grad_value = carry
        query_blk = lax.dynamic_slice_in_dim(query_h, begin_row, block_rows, 1)
        grad_blk = lax.dynamic_slice_in_dim(grad_out, begin_row, block_rows, 1)
        lse_blk = lax.dynamic_slice_in_dim(log_sums, begin_row, block_rows, 1)
        seg_blk = lax.dynamic_slice_in_dim(seg_keys, begin_row, block_rows, 0)
        scores = masked_scores(query_blk, key_h, seg_blk, seg_keys)
        probs = jnp.exp(scores - lse_blk[..., None])
        prob_low = probs.astype(jnp.bfloat16)
        grad_value = grad_value + jnp.einsum(
            "hqk,hqd->hkd", prob_low, grad_blk, preferred_element_type=jnp.float32
        )
        grad_prob = jnp.einsum(
            "hqd,hkd->hqk", grad_blk, value_h, preferred_element_type=jnp.float32
        )
        row_dot = jnp.sum(probs * grad_prob, axis=-1, keepdims=True)
        grad_score = (probs * (grad_prob - row_dot) * HEAD_DIM ** (-0.5)).astype(jnp.bfloat16)
        grad_query = jnp.einsum(
            "hqk,hkd->hqd", grad_score, key_h, preferred_element_type=jnp.float32
        )
        grad_key = grad_key + jnp.einsum(
            "hqk,hqd->hkd", grad_score, query_blk, preferred_element_type=jnp.float32
        )
        return ((grad_key, grad_value), grad_query)

    starts = jnp.arange(block_count, dtype=jnp.int32) * block_rows
    zeros_kv = jnp.zeros(key_h.shape, jnp.float32)
    (grad_key, grad_value), grad_query = lax.scan(one_block, (zeros_kv, zeros_kv), starts)
    grad_query = grad_query.transpose(1, 0, 2, 3).reshape(query_h.shape)
    return (
        grad_query.astype(jnp.bfloat16),
        grad_key.astype(jnp.bfloat16),
        grad_value.astype(jnp.bfloat16),
    )


def spread_rows(values):
    return lax.all_gather(values, "tp", axis=0, tiled=True)


def combine_rows(partial_value):
    return lax.psum_scatter(partial_value, "tp", scatter_dimension=0, tiled=True)


def spread_grads(values):
    return lax.all_gather(values, "tp", axis=0, tiled=True)


def combine_grads(partial_value):
    return lax.psum_scatter(
        partial_value.astype(jnp.bfloat16), "tp", scatter_dimension=0, tiled=True
    ).astype(jnp.float32)


def fetch_weights(w_qkv, w_attn_out, w_up, w_down, layer):
    return (
        lax.all_gather(w_qkv[layer], "dp", axis=1, tiled=True),
        lax.all_gather(w_attn_out[layer], "dp", axis=1, tiled=True),
        lax.all_gather(w_up[layer], "dp", axis=0, tiled=True),
        lax.all_gather(w_down[layer], "dp", axis=1, tiled=True),
    )


def reduce_weight_grads(grads):
    return (
        lax.psum_scatter(
            grads[0].astype(jnp.bfloat16), "dp", scatter_dimension=1, tiled=True
        ).astype(jnp.float32),
        lax.psum_scatter(
            grads[1].astype(jnp.bfloat16), "dp", scatter_dimension=1, tiled=True
        ).astype(jnp.float32),
        lax.psum_scatter(
            grads[2].astype(jnp.bfloat16), "dp", scatter_dimension=0, tiled=True
        ).astype(jnp.float32),
        lax.psum_scatter(
            grads[3].astype(jnp.bfloat16), "dp", scatter_dimension=1, tiled=True
        ).astype(jnp.float32),
    )


def block_forward(resid_in, seg_local, gains, biases, weights):
    qkv_w, attn_w, up_w, down_w = weights
    normed = layer_norm(resid_in, gains[0], biases[0]).astype(jnp.bfloat16)
    normed_all, seg_all = (
        lax.all_gather(normed, "tp", axis=0, tiled=True),
        lax.all_gather(seg_local, "tp", axis=0, tiled=True),
    )
    query_h = split_heads(product(normed_all, qkv_w[0]).astype(jnp.bfloat16))
    key_h = split_heads(product(normed_all, qkv_w[1]).astype(jnp.bfloat16))
    value_h = split_heads(product(normed_all, qkv_w[2]).astype(jnp.bfloat16))
    heads_out, log_sums = attend(query_h, key_h, value_h, seg_all)
    attn_rows = join_heads(heads_out)
    middle = resid_in + combine_rows(product(attn_rows, attn_w))
    normed_mid = spread_rows(layer_norm(middle, gains[1], biases[1]).astype(jnp.bfloat16))
    hidden_pre = product(normed_mid, up_w)
    hidden = gelu_tanh(hidden_pre).astype(jnp.bfloat16)
    result = middle + combine_rows(product(hidden, down_w))
    kept = (
        resid_in,
        middle,
        normed_all,
        seg_all,
        query_h,
        key_h,
        value_h,
        log_sums,
        attn_rows,
        normed_mid,
        hidden_pre,
        hidden,
    )
    return (result, kept)


def block_backward(kept, gains, biases, weights, grad_result):
    (
        resid_in,
        middle,
        normed_all,
        seg_all,
        query_h,
        key_h,
        value_h,
        log_sums,
        attn_rows,
        normed_mid,
        hidden_pre,
        hidden,
    ) = kept
    qkv_w, attn_w, up_w, down_w = weights
    grad_branch = spread_grads(grad_result.astype(jnp.bfloat16))
    grad_down = product_tn(hidden, grad_branch)
    grad_hidden = product_nt(grad_branch, down_w)
    _, gelu_back = jax.vjp(gelu_tanh, hidden_pre)
    grad_pre = gelu_back(grad_hidden)[0].astype(jnp.bfloat16)
    grad_up = product_tn(normed_mid, grad_pre)
    grad_norm_mid = combine_grads(product_nt(grad_pre, up_w))
    _, norm_back_mid = jax.vjp(layer_norm, middle, gains[1], biases[1])
    grad_mid_ln, grad_gain_mid, grad_bias_mid = norm_back_mid(grad_norm_mid)
    grad_middle = grad_result + grad_mid_ln
    grad_attn_all = spread_grads(grad_middle.astype(jnp.bfloat16))
    grad_attn = product_tn(attn_rows, grad_attn_all)
    grad_heads = split_heads(product_nt(grad_attn_all, attn_w).astype(jnp.bfloat16))
    grad_query, grad_key, grad_value = attend_back(
        query_h, key_h, value_h, seg_all, log_sums, grad_heads
    )
    grad_parts = [join_heads(grad_query), join_heads(grad_key), join_heads(grad_value)]
    grad_qkv = jnp.stack([product_tn(normed_all, grad_part) for grad_part in grad_parts])
    grad_normed_part = (
        product_nt(grad_parts[0], qkv_w[0])
        + product_nt(grad_parts[1], qkv_w[1])
        + product_nt(grad_parts[2], qkv_w[2])
    )
    grad_normed = combine_grads(grad_normed_part)
    _, norm_back_in = jax.vjp(layer_norm, resid_in, gains[0], biases[0])
    grad_in_ln, grad_gain_in, grad_bias_in = norm_back_in(grad_normed)
    gain_grads = jnp.stack([grad_gain_in, grad_gain_mid])
    bias_grads = jnp.stack([grad_bias_in, grad_bias_mid])
    return (
        grad_middle + grad_in_ln,
        gain_grads,
        bias_grads,
        (grad_qkv, grad_attn, grad_up, grad_down),
    )


def local(
    tokens,
    segment_ids,
    norm_gains,
    norm_biases,
    w_qkv,
    w_attn_out,
    w_up,
    w_down,
    w_vq_in,
    w_vq_out,
    codebook,
    cotangent,
):
    gain_sum = jnp.zeros(norm_gains.shape, jnp.float32)
    bias_sum = jnp.zeros(norm_biases.shape, jnp.float32)
    vq_in_sum = jnp.zeros(w_vq_in.shape, jnp.float32)
    vq_out_sum = jnp.zeros(w_vq_out.shape, jnp.float32)
    code_sum = jnp.zeros(codebook.shape, jnp.float32)
    layer_sums = [None, None]
    outputs = []
    input_grads = []
    for micro in range(MICRO):
        resid_in = tokens[micro].astype(jnp.float32)
        seg_local = segment_ids[micro]
        enc_weights = fetch_weights(w_qkv, w_attn_out, w_up, w_down, 0)
        encoded, enc_kept = block_forward(
            resid_in, seg_local, norm_gains[0:2], norm_biases[0:2], enc_weights
        )
        (decoder_in, _), vq_back = jax.vjp(
            quantize, encoded, norm_gains[2], norm_biases[2], w_vq_in, w_vq_out, codebook
        )
        dec_weights = fetch_weights(w_qkv, w_attn_out, w_up, w_down, 1)
        decoded, dec_kept = block_forward(
            decoder_in, seg_local, norm_gains[3:5], norm_biases[3:5], dec_weights
        )
        outputs.append(decoded)
        grad_dec_in, gains_dec, biases_dec, grads_dec = block_backward(
            dec_kept, norm_gains[3:5], norm_biases[3:5], dec_weights, cotangent[micro]
        )
        grad_encoded, grad_gain_vq, grad_bias_vq, grad_in_w, grad_out_w, grad_codes = vq_back(
            (grad_dec_in, jnp.ones((), jnp.float32))
        )
        grad_input, gains_enc, biases_enc, grads_enc = block_backward(
            enc_kept, norm_gains[0:2], norm_biases[0:2], enc_weights, grad_encoded
        )
        input_grads.append(grad_input)
        gain_sum = gain_sum + jnp.concatenate([gains_enc, grad_gain_vq[None], gains_dec], axis=0)
        bias_sum = bias_sum + jnp.concatenate([biases_enc, grad_bias_vq[None], biases_dec], axis=0)
        vq_in_sum = vq_in_sum + grad_in_w
        vq_out_sum = vq_out_sum + grad_out_w
        code_sum = code_sum + grad_codes
        for layer, grads in ((0, grads_enc), (1, grads_dec)):
            reduced = reduce_weight_grads(grads)
            if layer_sums[layer] is None:
                layer_sums[layer] = reduced
            else:
                layer_sums[layer] = jax.tree.map(jnp.add, layer_sums[layer], reduced)
    gain_tot, bias_tot, vq_in_tot, vq_out_tot, code_tot = lax.psum(
        (gain_sum, bias_sum, vq_in_sum, vq_out_sum, code_sum), ("dp", "tp")
    )
    return (
        jnp.stack(outputs),
        jnp.stack(input_grads),
        gain_tot,
        bias_tot[0:3],
        bias_tot[3:5],
        jnp.stack([layer_sums[0][0], layer_sums[1][0]]),
        jnp.stack([layer_sums[0][1], layer_sums[1][1]]),
        jnp.stack([layer_sums[0][2], layer_sums[1][2]]),
        jnp.stack([layer_sums[0][3], layer_sums[1][3]]),
        vq_in_tot,
        vq_out_tot,
        code_tot,
    )


def solution(mesh):
    n_dp, n_tp = mesh.shape["dp"], mesh.shape["tp"]
    fits = n_tp == MICRO and n_dp == 16
    return jax.shard_map(
        functools.partial(whole_groups, n_dp) if fits else local,
        mesh=mesh,
        in_specs=(
            P(None, ("dp", "tp"), None),
            P(None, ("dp", "tp")),
            P(),
            P(),
            P(None, None, "dp", "tp"),
            P(None, "tp", "dp"),
            P(None, "dp", "tp"),
            P(None, "tp", "dp"),
            P(),
            P(),
            P(),
            P(None, ("dp", "tp"), None),
        ),
        out_specs=(
            P(None, ("dp", "tp"), None),
            P(None, ("dp", "tp"), None),
            P(),
            P(),
            P(),
            P(None, None, "dp", "tp"),
            P(None, "tp", "dp"),
            P(None, "dp", "tp"),
            P(None, "tp", "dp"),
            P(),
            P(),
            P(),
        ),
        check_vma=False,
    )
```

```python
import functools

import jax
import jax.numpy as jnp
from jax import lax
from jax.experimental import pallas as pl
from jax.experimental.pallas import tpu as pltpu
from jax.sharding import PartitionSpec as P

HEAD_DIM = 64
MICRO = 2
bf16 = jnp.bfloat16
f32 = jnp.float32
highest = lax.Precision.HIGHEST
ln_eps = 1e-05
norm_eps = 1e-06
temper = 10.0
commit_weight = 64.0
gelu_coef = 0.7978845608028654
masked_score = -1e30
log2e = 1.4426950408889634
vmem_cap = 36 * 1024 * 1024


PLANE = ((0, 0), (0, 1), (1, 0), (1, 1))


def exchange(values, dp_xor, tp_xor, n_dp):
    pairs = [
        (d * 2 + t, (d ^ dp_xor) * 2 + (t ^ tp_xor)) for d in range(n_dp) for t in range(2)
    ]
    return lax.ppermute(values, ("dp", "tp"), pairs)


def plane_send(lows, n_dp):
    return [exchange(low, 2 * y, x, n_dp) for (y, x), low in zip(PLANE[1:], lows)]


def line_send(lows, n_dp):
    return [exchange(low, 4 * k, 0, n_dp) for k, low in zip(range(1, 4), lows)]


def block_places():
    for core in range(2):
        for index, (y, x) in enumerate(PLANE):
            for k in range(4):
                yield core * 4 + index, k, k * 4 + y * 2 + core, x


def dot(a, b):
    return jnp.dot(a, b, preferred_element_type=f32)


def dot_nt(a, b, precision=None):
    return lax.dot_general(
        a, b, (((1,), (1,)), ((), ())), preferred_element_type=f32, precision=precision
    )


def dot_full(a, b):
    return jnp.dot(a, b, preferred_element_type=f32, precision=highest)


def ln_parts(x):
    centred = x - jnp.mean(x, axis=-1, keepdims=True)
    inv = lax.rsqrt(jnp.mean(centred * centred, axis=-1, keepdims=True) + ln_eps)
    return centred * inv, inv


def ln_back(grad, xhat, inv, gain):
    scaled = grad * gain
    return inv * (
        scaled
        - jnp.mean(scaled, axis=-1, keepdims=True)
        - xhat * jnp.mean(scaled * xhat, axis=-1, keepdims=True)
    )


def split2(x):
    hi = x.astype(bf16)
    return hi, (x - hi.astype(f32)).astype(bf16)


def split3(x):
    hi, _ = split2(x)
    rest = x - hi.astype(f32)
    mid = rest.astype(bf16)
    return hi, mid, (rest - mid.astype(f32)).astype(bf16)


def weight_copies(w_hbm, w_ref, sems):
    return [
        pltpu.make_async_copy(
            w_hbm.at[owner], w_ref.at[owner % 2, pl.ds(owner // 2 * 32, 32), :], sems.at[owner]
        )
        for owner in range(32)
    ]


def grad_copies(ids_ref, g_ref, refs, sems):
    copies = []
    for slot, (which, k, dp_xor, tp_xor) in enumerate(block_places()):
        row = pl.multiple_of((ids_ref[0] ^ dp_xor) * 32, 32)
        copies.append(
            pltpu.make_async_copy(
                g_ref.at[ids_ref[1] ^ tp_xor, pl.ds(row, 32), :],
                refs[which // 4].at[which % 4, k],
                sems.at[slot],
            )
        )
    return copies


def start_all(copies):
    for copy in copies:
        copy.start()


def wait_all(copies):
    for copy in copies:
        copy.wait()


def head_rows(ref, pair, which):
    own = ref[pl.ds(pl.multiple_of(pair * 128 + which * HEAD_DIM, HEAD_DIM), HEAD_DIM), :]
    zero = jnp.zeros_like(own)
    return jnp.concatenate([own, zero] if which == 0 else [zero, own], axis=0)


def segment_mask(own, other):
    ids = jnp.concatenate([own[:, 512:640], other[:, 512:640]], axis=0).astype(f32)
    return jnp.where(ids[:, 0:1] == ids.T[0:1, :], 0.0, masked_score)


def load_rows(x, own, other):
    if x is None:
        return jnp.concatenate([own[:, :512], other[:, :512]], axis=0).astype(f32)
    return x[...]


def attn_fwd_kernel(with_x, ids, own, other, gain, bias, *refs):
    x, refs = (refs[0], refs[1:]) if with_x else (None, refs)
    w_hbm, refs = refs[0], refs[1:]
    x1, lse, saved, refs = refs[0], refs[1], refs[2:8], refs[8:]
    w, h, vt, ot, mask, qs, k, v, o, qst, kt, sems, out_sems = refs
    copies = weight_copies(w_hbm, w, sems)
    start_all(copies)
    keeps = [
        pltpu.make_async_copy(held, to, out_sems.at[at])
        for at, (held, to) in enumerate(zip((qs, k, v, o, qst, kt), saved))
    ]
    xf = load_rows(x, own, other)
    h[...] = (ln_parts(xf)[0] * gain[...] + bias[...]).astype(bf16)
    mask[...] = segment_mask(own, other)
    wait_all(copies)
    for t in range(2):
        cols = pl.ds(t * 256, 256)
        qs[:, cols] = (dot(h[...], w[t, :, 0:256]).astype(bf16) * HEAD_DIM ** (-0.5)).astype(bf16)
        k[:, cols] = dot(h[...], w[t, :, 256:512]).astype(bf16)
        v[:, cols] = dot(h[...], w[t, :, 512:768]).astype(bf16)
    qst[...] = qs[...].T
    kt[...] = k[...].T
    vt[...] = v[...].T
    for at in (0, 1, 2, 4, 5):
        keeps[at].start()

    def one_pair(pair, _):
        lanes = pl.ds(pl.multiple_of(pair * 128, 128), 128)
        k_pair = k[:, lanes]
        for which in range(2):
            scores = dot(k_pair, head_rows(qst, pair, which)) + mask[...]
            top = jnp.max(scores, axis=0, keepdims=True)
            numer = jnp.exp(scores - top).astype(bf16)
            rows = pl.ds(pl.multiple_of(pair * 128 + which * HEAD_DIM, HEAD_DIM), HEAD_DIM)
            left = jnp.concatenate([vt[rows, :], jnp.ones((16, 512), bf16)], axis=0)
            both = dot(left, numer)
            total = both[HEAD_DIM : HEAD_DIM + 1, :]
            ot[rows, :] = (both[:HEAD_DIM, :] / total).astype(bf16)
            lse[pl.ds(pair * 2 + which, 1), :] = top + jnp.log(total)
        return 0

    lax.fori_loop(0, 4, one_pair, 0)
    o[...] = ot[...].T
    keeps[3].start()
    acc = xf
    for t in range(2):
        acc = acc + dot_nt(o[:, t * 256 : (t + 1) * 256], w[t, :, 768:1024])
    x1[...] = acc
    wait_all(keeps)


def gelu_parts(u):
    square = u * u
    tanh = jnp.tanh(gelu_coef * u * (1.0 + 0.044715 * square))
    return 0.5 * u * (1.0 + tanh), tanh, square


def mlp_fwd_kernel(x1, gain, bias, w_hbm, y, theirs, w, h2, sems):
    copies = weight_copies(w_hbm, w, sems)
    start_all(copies)
    h2[...] = (ln_parts(x1[...])[0] * gain[...] + bias[...]).astype(bf16)
    y[...] = x1[...]
    wait_all(copies)

    def one_chunk(index, _):
        t = index // 2
        col = (index % 2) * 512
        pre = dot(h2[...], w[t, :, pl.ds(pl.multiple_of(col, 512), 512)])
        hidden = gelu_parts(pre)[0].astype(bf16)
        y[...] += dot_nt(hidden, w[t, :, pl.ds(pl.multiple_of(col + 1024, 512), 512)])
        return 0

    lax.fori_loop(0, 4, one_chunk, 0)
    theirs[...] = y[256:, :].astype(bf16)


def mlp_bwd_kernel(split, ids, x1, gain, bias, w_hbm, *refs):
    if split:
        own, other, refs = refs[0], refs[1], refs[2:]
    else:
        dy, refs = refs[0], refs[1:]
    dx1, small, refs = refs[0], refs[1], refs[2:]
    g_refs, refs = refs[:2], refs[2:]
    w, g, h2, h2t, dyb, dybt, dh2, w_sems, sems = refs[:9]
    loads = weight_copies(w_hbm, w, w_sems)
    start_all(loads)
    if split:
        dy = refs[9]
        dy[0:256, :] = own[ids[1]]
        dy[256:, :] = other[:, 640:].astype(f32)
    h2[...] = (ln_parts(x1[...])[0] * gain[...] + bias[...]).astype(bf16)
    h2t[...] = h2[...].T
    dyb[...] = dy[...].astype(bf16)
    dybt[...] = dyb[...].T
    dh2[...] = jnp.zeros_like(dh2)
    wait_all(loads)

    def one_chunk(index, _):
        t = index // 2
        up = pl.ds(pl.multiple_of((index % 2) * 512, 512), 512)
        down = pl.ds(pl.multiple_of((index % 2) * 512 + 1024, 512), 512)
        pre = dot(h2[...], w[t, :, up])
        hidden, tanh, square = gelu_parts(pre)
        slope = 0.5 * (1.0 + tanh) + (0.5 * gelu_coef) * pre * (1.0 - tanh * tanh) * (
            1.0 + (3 * 0.044715) * square
        )
        dhidden = dot(dyb[...], w[t, :, down])
        dpre = (dhidden * slope).astype(bf16)
        g[t, :, down] = dot(dybt[...], hidden.astype(bf16)).astype(bf16)
        g[t, :, up] = dot(h2t[...], dpre).astype(bf16)
        dh2[...] += dot_nt(dpre, w[t, :, up])
        return 0

    lax.fori_loop(0, 4, one_chunk, 0)
    copies = grad_copies(ids, g, g_refs, sems)
    start_all(copies)
    xhat, inv = ln_parts(x1[...])
    grad = dh2[...]
    small[0:1, :] = jnp.sum(grad * xhat, axis=0, keepdims=True)
    small[1:2, :] = jnp.sum(grad, axis=0, keepdims=True)
    dx1[...] = dy[...] + ln_back(grad, xhat, inv, gain[...])
    for copy in copies:
        copy.wait()


def pack_rows(rows):
    cut = [row[:, 128 * j : 128 * (j + 1)] for row in rows for j in range(4)]
    return jnp.concatenate(split2(jnp.concatenate(cut, axis=0)), axis=0)


def attn_bwd_kernel(with_x, with_small, ids, own, other, dx1, gain, bias, lse, *refs):
    saved, w_hbm, refs = refs[:6], refs[6], refs[7:]
    x, refs = (refs[0], refs[1:]) if with_x else (None, refs)
    if with_small:
        other_small, refs = refs[0], refs[1:]
    dx, dx_low, small = refs[:3]
    g_refs, refs = refs[3:5], refs[5:]
    w, g, h, mask, do, dot_t, dqt, dq, dk, dv, flip = refs[:11]
    qs, k, v, o, qst, kt, w_sems, in_sems, sems = refs[11:]
    loads = weight_copies(w_hbm, w, w_sems)
    start_all(loads)
    takes = [
        pltpu.make_async_copy(held, to, in_sems.at[at])
        for at, (held, to) in enumerate(zip(saved, (qs, k, v, o, qst, kt)))
    ]
    start_all(takes)
    xf = load_rows(x, own, other)
    h[...] = (ln_parts(xf)[0] * gain[...] + bias[...]).astype(bf16)
    mask[...] = segment_mask(own, other)
    low = dx1[...].astype(bf16)
    flip[...] = low.T
    wait_all(loads)
    wait_all(takes)
    for t in range(2):
        cols = pl.ds(t * 256, 256)
        do[:, cols] = dot(low, w[t, :, 768:1024]).astype(bf16)
        g[t, :, 768:1024] = dot(flip[...], o[:, cols]).astype(bf16)
    dot_t[...] = do[...].T
    def one_pair(pair, _):
        lanes = pl.ds(pl.multiple_of(pair * 128, 128), 128)
        k_pair, v_pair = k[:, lanes], v[:, lanes]
        q_pair, do_pair = qs[:, lanes], do[:, lanes]
        dvs, dks = [], []
        for which in range(2):
            head = pl.ds(pair * 2 + which, 1)
            rows = pl.ds(pl.multiple_of(pair * 128 + which * HEAD_DIM, HEAD_DIM), HEAD_DIM)
            scores = dot(k_pair, head_rows(qst, pair, which)) + mask[...]
            probs = jnp.exp(scores - lse[head, :])
            dprobs = dot(v_pair, head_rows(dot_t, pair, which))
            shift = jnp.sum(probs * dprobs, axis=0, keepdims=True)
            dscore = (probs * (dprobs - shift)).astype(bf16)
            dvs.append(dot(probs.astype(bf16), do_pair))
            dks.append(dot(dscore, q_pair))
            dqt[rows, :] = (dot(kt[rows, :], dscore) * HEAD_DIM ** (-0.5)).astype(bf16)
        first = lax.broadcasted_iota(jnp.int32, (512, 128), 1) < HEAD_DIM
        dv[:, lanes] = jnp.where(first, dvs[0], dvs[1]).astype(bf16)
        dk[:, lanes] = jnp.where(first, dks[0], dks[1]).astype(bf16)
        return 0

    lax.fori_loop(0, 4, one_pair, 0)
    dq[...] = dqt[...].T
    flip[...] = h[...].T
    for t in range(2):
        cols = pl.ds(t * 256, 256)
        g[t, :, 0:256] = dot(flip[...], dq[:, cols]).astype(bf16)
        g[t, :, 256:512] = dot(flip[...], dk[:, cols]).astype(bf16)
        g[t, :, 512:768] = dot(flip[...], dv[:, cols]).astype(bf16)
    grad = jnp.zeros((512, 512), f32)
    for t in range(2):
        cols = pl.ds(t * 256, 256)
        for index, part in enumerate((dq, dk, dv)):
            grad = grad + dot_nt(part[:, cols], w[t, :, index * 256 : (index + 1) * 256])
    xhat, inv = ln_parts(xf)
    dgain = jnp.sum(grad * xhat, axis=0, keepdims=True)
    dbias = jnp.sum(grad, axis=0, keepdims=True)
    small[0:1, :] = dgain
    small[1:2, :] = dbias
    if with_small:
        packed = pack_rows([dgain, dbias, other_small[0:1, :], other_small[1:2, :]])
        for t in range(2):
            for row in range(16):
                g[t, row * 32 : (row + 1) * 32, 1024:1152] = packed
    copies = grad_copies(ids, g, g_refs, sems)
    start_all(copies)
    total = dx1[...] + ln_back(grad, xhat, inv, gain[...])
    dx[...] = total
    dx_low[...] = total[256:, :].astype(bf16)
    for copy in copies:
        copy.wait()


def code_prep_kernel(book_t, stack, stack_t):
    def one_chunk(index, _):
        lanes = pl.ds(pl.multiple_of(index * 512, 512), 512)
        rows = book_t[:, lanes]
        unit = rows * lax.rsqrt(jnp.sum(rows * rows, axis=0, keepdims=True) + norm_eps)
        hi, mid, lo = split3(unit)
        stack_t[:, lanes] = jnp.concatenate([hi, mid, lo, jnp.ones((32, 512), bf16)], axis=0)
        tall = jnp.concatenate([hi, mid, lo, hi, mid, hi, jnp.zeros((64, 512), bf16)], axis=0)
        stack[lanes, :] = tall.T
        return 0

    lax.fori_loop(0, book_t.shape[1] // 512, one_chunk, 0)


def factor_stack(x):
    hi, mid, lo = split3(x)
    return jnp.concatenate([hi, hi, hi, mid, mid, lo, jnp.zeros((64, x.shape[1]), bf16)], axis=0)


def code_loads(pairs, sems):
    loads = []
    for piece in range(4):
        group = []
        for at, (held, to, by_row) in enumerate(pairs):
            size = held.shape[0 if by_row else 1] // 4
            part = pl.ds(piece * size, size)
            place = (part, slice(None)) if by_row else (slice(None), part)
            group.append(pltpu.make_async_copy(held.at[place], to.at[place], sems.at[at, piece]))
        start_all(group)
        loads.append(group)
    return loads


def vq_fwd_kernel(
    e, gain, bias, in_t, out_w, stack_hbm, stack_t_hbm, u, kept, acc, stack, stack_t, sems
):
    loads = code_loads([(stack_hbm, stack, True), (stack_t_hbm, stack_t, False)], sems)
    lnv = ln_parts(e[...])[0] * gain[...] + bias[...]
    raw = dot_nt(in_t[...], lnv, highest)
    inv = lax.rsqrt(jnp.sum(raw * raw, axis=0, keepdims=True) + norm_eps)
    latent = raw * inv
    right = factor_stack(latent * (temper * log2e))
    acc[...] = jnp.zeros_like(acc)

    def one_chunk(index, _):
        codes = pl.ds(pl.multiple_of(index * 512, 512), 512)
        numer = jnp.exp2(dot(stack[codes, :], right)).astype(bf16)
        acc[...] += dot(stack_t[:, codes], numer)
        return 0

    chunks = stack.shape[0] // 512
    for piece, group in enumerate(loads):
        wait_all(group)
        lax.fori_loop(chunks * piece // 4, chunks * (piece + 1) // 4, one_chunk, 0)
    total = acc[96:97, :]
    soft = (acc[0:32, :] + acc[32:64, :] + acc[64:96, :]) / total
    kept[0:32, :] = latent
    kept[32:64, :] = soft
    kept[64:65, :] = total
    kept[65:66, :] = inv
    u[...] = dot_full(soft.T, out_w[...])


def vq_bwd_kernel(ids, e, du, gain, bias, in_t, out_w, stack_hbm, stack_t_hbm, book_hbm, kept, *refs):
    small0, small1, de, code_keep, code_send = refs[:5]
    acc, grads, small, tail, stack, stack_t, book_t, load_sems, sems = refs[5:]
    loads = code_loads(
        [(stack_hbm, stack, True), (stack_t_hbm, stack_t, False), (book_hbm, book_t, False)],
        load_sems,
    )
    xhat, inv_ln = ln_parts(e[...])
    lnv = xhat * gain[...] + bias[...]
    latent, soft = kept[0:32, :], kept[32:64, :]
    total, inv = kept[64:65, :], kept[65:66, :]
    direct = (2.0 * 1.25 * commit_weight) * (latent - soft)
    dsoft = dot_nt(out_w[...], du[...], highest) - direct
    small[32:64, :] = dot_full(soft, du[...])
    shift = jnp.sum(dsoft * soft, axis=0, keepdims=True) / total
    dsoft = dsoft / total
    right = jnp.concatenate(
        [factor_stack(latent * (temper * log2e)), factor_stack(dsoft)], axis=1
    )
    pads = jnp.zeros((64, 512), f32)

    def tall(x):
        hi, lo = split2(x)
        return jnp.concatenate([hi.astype(f32), lo.astype(f32), pads], axis=0).T.astype(bf16)

    sides = jnp.concatenate([tall(dsoft), tall(latent * temper)], axis=0)
    acc[...] = jnp.zeros_like(acc)

    def one_chunk(index, _):
        codes = pl.ds(pl.multiple_of(index * 512, 512), 512)
        both = dot(stack[codes, :], right)
        numer = jnp.exp2(both[:, :512])
        dlogit = (numer * (both[:, 512:] - shift)).astype(bf16)
        acc[...] += dot(stack_t[0:96, codes], dlogit)
        dcode = dot(jnp.concatenate([numer.astype(bf16), dlogit], axis=1), sides).T
        dcode = dcode[0:32, :] + dcode[32:64, :]
        rows = book_t[:, codes]
        scale = lax.rsqrt(jnp.sum(rows * rows, axis=0, keepdims=True) + norm_eps)
        unit = rows * scale
        grads[:, codes] = (
            scale * (dcode - unit * jnp.sum(unit * dcode, axis=0, keepdims=True))
        ).astype(bf16)
        return 0

    chunks = stack.shape[0] // 512
    for piece, group in enumerate(loads):
        wait_all(group)
        lax.fori_loop(chunks * piece // 4, chunks * (piece + 1) // 4, one_chunk, 0)
    dlatent = temper * (acc[0:32, :] + acc[32:64, :] + acc[64:96, :]) + direct
    draw = inv * (dlatent - latent * jnp.sum(latent * dlatent, axis=0, keepdims=True))
    small[0:32, :] = dot_full(draw, lnv)
    dln = dot_full(draw.T, in_t[...])
    small[64:65, :] = jnp.sum(dln * xhat, axis=0, keepdims=True)
    small[65:66, :] = jnp.sum(dln, axis=0, keepdims=True)
    small[66:68, :] = small0[0:2, :]
    small[68:70, :] = small1[0:2, :]
    small[70:96, :] = jnp.zeros((26, 512), f32)
    for block in range(3):
        for at, part in enumerate(split2(small[block * 32 : (block + 1) * 32, :])):
            for side in range(2):
                tail[block * 2 + side, :, at * 256 : (at + 1) * 256] = part[
                    :, side * 256 : (side + 1) * 256
                ]
    tail[6:8] = jnp.zeros((2, 32, 512), bf16)
    core, z = ids[0] % 2, ids[0] // 4
    copies = []
    for slot, (at, to) in enumerate(((core, code_keep), (1 - core, code_send))):
        for k in range(4):
            part = at * 4 + (z ^ k)
            lanes = pl.ds(pl.multiple_of(part * 1024, 1024), 1024)
            copies += [
                pltpu.make_async_copy(
                    grads.at[:, lanes], to.at[k, :, pl.ds(0, 1024)], sems.at[0, slot, k]
                ),
                pltpu.make_async_copy(
                    tail.at[part], to.at[k, :, pl.ds(1024, 512)], sems.at[1, slot, k]
                ),
            ]
    for copy in copies:
        copy.start()
    de[...] = ln_back(dln, xhat, inv_ln, gain[...])
    for copy in copies:
        copy.wait()


SMEM = pl.BlockSpec(memory_space=pltpu.SMEM)
VMEM = pl.BlockSpec(memory_space=pltpu.VMEM)
ANY = pl.BlockSpec(memory_space=pl.ANY)


def shaped(*pairs):
    return [jax.ShapeDtypeStruct(shape, dtype) for shape, dtype in pairs]


def pin(array):
    return pltpu.with_memory_space_constraint(array, pltpu.HBM)


def call(kernel, name, in_specs, out_specs, outs, scratch, flops, after=(), carry=()):
    n_in, n_extra, n_out = len(in_specs), len(after) + len(carry), len(outs)

    def body(*refs):
        first = n_in + n_extra
        kernel(*refs[:n_in], *refs[first : first + n_out], *refs[first + n_out + len(carry) :])

    made = pl.pallas_call(
        body,
        name=name,
        in_specs=in_specs + [ANY] * n_extra,
        out_specs=out_specs + [ANY] * len(carry),
        out_shape=outs + [jax.ShapeDtypeStruct(a.shape, a.dtype) for a in carry],
        scratch_shapes=scratch,
        input_output_aliases={n_in + len(after) + i: n_out + i for i in range(len(carry))},
        compiler_params=pltpu.CompilerParams(vmem_limit_bytes=vmem_cap),
        cost_estimate=pl.CostEstimate(flops=flops, bytes_accessed=10**6, transcendentals=0),
    )

    def run(*args):
        res = made(*args, *after, *carry)
        return (*res[:n_out], list(res[n_out:]))

    return run


DMA = pltpu.SemaphoreType.DMA
ROWS2 = (512, 512)


def attn_fwd(ids, marked, xs, gain, bias, w, after=(), carry=()):
    outs = shaped((ROWS2, f32), ((8, 512), f32)) + [pltpu.HBM(ROWS2, bf16)] * 6
    scratch = [
        pltpu.VMEM((2, 512, 1024), bf16),
        *[pltpu.VMEM(ROWS2, bf16)] * 3,
        pltpu.VMEM(ROWS2, f32),
        *[pltpu.VMEM(ROWS2, bf16)] * 6,
        DMA((32,)),
        DMA((6,)),
    ]
    x1, lse, *saved, carried = call(
        functools.partial(attn_fwd_kernel, bool(xs)),
        "attn_fwd",
        [SMEM] + [VMEM] * (4 + len(xs)) + [ANY],
        [VMEM] * 2 + [ANY] * 6,
        outs,
        scratch,
        10**10,
        after,
        carry,
    )(ids, *marked, gain, bias, *xs, pin(w))
    return x1, (lse, *saved), carried


def mlp_fwd(x1, gain, bias, w, after=(), carry=()):
    return call(
        mlp_fwd_kernel,
        "mlp_fwd",
        [VMEM] * 3 + [ANY],
        [VMEM] * 2,
        shaped((ROWS2, f32), ((256, 512), bf16)),
        [pltpu.VMEM((2, 512, 2048), bf16), pltpu.VMEM(ROWS2, bf16), DMA((32,))],
        8 * 10**9,
        after,
        carry,
    )(x1, gain, bias, pin(w))


def mlp_bwd(ids, x1, dys, gain, bias, w, after=(), carry=()):
    grads = shaped(*[((4, 4, 32, 2048), bf16)] * 2)
    scratch = [
        pltpu.VMEM((2, 512, 2048), bf16),
        pltpu.VMEM((2, 512, 2048), bf16),
        *[pltpu.VMEM(ROWS2, bf16)] * 4,
        pltpu.VMEM(ROWS2, f32),
        DMA((32,)),
        DMA((32,)),
        *[pltpu.VMEM(ROWS2, f32)] * (len(dys) - 1),
    ]
    return call(
        functools.partial(mlp_bwd_kernel, len(dys) == 2),
        "mlp_bwd",
        [SMEM] + [VMEM] * 3 + [ANY] + [VMEM] * len(dys),
        [VMEM] * 2 + [ANY] * len(grads),
        shaped((ROWS2, f32), ((8, 512), f32)) + grads,
        scratch,
        15 * 10**9,
        after,
        carry,
    )(ids, x1, gain, bias, pin(w), *dys)


def attn_bwd(ids, marked, xs, dx1, gain, bias, saved, w, other_small=(), after=(), carry=()):
    width = 1024 + 128 * len(other_small)
    grads = shaped(*[((4, 4, 32, width), bf16)] * 2)
    scratch = [
        pltpu.VMEM((2, 512, 1024), bf16),
        pltpu.VMEM((2, 512, width), bf16),
        pltpu.VMEM(ROWS2, bf16),
        pltpu.VMEM(ROWS2, f32),
        *[pltpu.VMEM(ROWS2, bf16)] * 13,
        DMA((32,)),
        DMA((6,)),
        DMA((32,)),
    ]
    return call(
        functools.partial(attn_bwd_kernel, bool(xs), bool(other_small)),
        "attn_bwd",
        [SMEM] + [VMEM] * 6 + [ANY] * 7 + [VMEM] * (len(xs) + len(other_small)),
        [VMEM] * 3 + [ANY] * len(grads),
        shaped((ROWS2, f32), ((256, 512), bf16), ((8, 512), f32)) + grads,
        scratch,
        15 * 10**9,
        after,
        carry,
    )(ids, *marked, dx1, gain, bias, saved[0], *map(pin, saved[1:]), pin(w), *xs, *other_small)


def code_prep(book_t, after=(), carry=()):
    codes = book_t.shape[1]
    return call(
        code_prep_kernel,
        "code_prep",
        [VMEM],
        [VMEM] * 2,
        shaped(((codes, 256), bf16), ((128, codes), bf16)),
        [],
        6 * 10**9,
        after,
        carry,
    )(book_t)


def vq_fwd(e, gain, bias, in_t, out_w, stack, stack_t, after=(), carry=()):
    return call(
        vq_fwd_kernel,
        "vq_fwd",
        [VMEM] * 5 + [ANY] * 2,
        [VMEM] * 2,
        shaped((ROWS2, f32), ((72, 512), f32)),
        [
            pltpu.VMEM((128, 512), f32),
            pltpu.VMEM(stack.shape, bf16),
            pltpu.VMEM(stack_t.shape, bf16),
            DMA((2, 4)),
        ],
        15 * 10**9,
        after,
        carry,
    )(e, gain, bias, in_t, out_w, pin(stack), pin(stack_t))


def vq_bwd(ids, e, du, gain, bias, in_t, out_w, codes, kept, smalls, after=(), carry=()):
    scratch = [
        pltpu.VMEM((96, 512), f32),
        pltpu.VMEM(codes[2].shape, bf16),
        pltpu.VMEM((96, 512), f32),
        pltpu.VMEM((8, 32, 512), bf16),
        *[pltpu.VMEM(a.shape, a.dtype) for a in codes],
        DMA((3, 4)),
        DMA((2, 2, 4)),
    ]
    return call(
        vq_bwd_kernel,
        "vq_bwd",
        [SMEM] + [VMEM] * 6 + [ANY] * 3 + [VMEM] * 3,
        [VMEM] + [ANY] * 2,
        shaped((ROWS2, f32), *[((4, 32, 1536), bf16)] * 2),
        scratch,
        25 * 10**9,
        after,
        carry,
    )(ids, e, du, gain, bias, in_t, out_w, *map(pin, codes), kept, *smalls)


def pack_kernel(ids, *refs):
    hbm, (enc_attn, enc_mlp, dec_attn, dec_mlp, own, send), (qkv, out_t, up, down_t, tokens, segs, cot, sems) = (
        refs[:7],
        refs[7:13],
        refs[13:],
    )
    held = (qkv, out_t, up, down_t, tokens, segs, cot)
    copies = [pltpu.make_async_copy(hbm[at], held[at], sems.at[at]) for at in range(7)]
    start_all(copies)
    wait_all(copies[:4])
    for layer, (attn, mlp) in enumerate(((enc_attn, enc_mlp), (dec_attn, dec_mlp))):
        for index in range(3):
            attn[:, index * 256 : (index + 1) * 256] = qkv[layer, index]
        attn[:, 768:1024] = out_t[layer]
        mlp[:, :1024] = up[layer]
        mlp[:, 1024:] = down_t[layer]
    wait_all(copies[4:])
    for to, micro in ((own, ids[1]), (send, 1 - ids[1])):
        to[:, :512] = tokens[micro]
        ids_row = segs[pl.ds(micro, 1), :].astype(f32)
        to[:, 512:640] = jnp.broadcast_to(ids_row, (128, 256)).T.astype(bf16)
    send[:, 640:] = cot[1 - ids[1]].astype(bf16)


def pack(ids, *arrays):
    outs = shaped(
        *[((32, 1024), bf16), ((32, 2048), bf16)] * 2,
        ((256, 640), bf16),
        ((256, 1152), bf16),
    )
    return call(
        pack_kernel,
        "pack",
        [SMEM] + [ANY] * 7,
        [VMEM] * 6,
        outs,
        [*[pltpu.VMEM(a.shape, a.dtype) for a in arrays], DMA((7,))],
        1,
    )(ids, *map(pin, arrays))[:-1]


def joined(block):
    return block[0:16, 1024:].astype(f32) + block[16:32, 1024:].astype(f32)


def put_small(value, own, blocks):
    hi, lo = split2(value)
    own[0:16, 1024:] = hi.astype(f32) + lo.astype(f32)
    for block in blocks:
        block[0:16, 1024:] = hi
        block[16:32, 1024:] = lo


def near_kernel(ids, ins, outs):
    keep, other = ins
    for i in range(4):
        outs[i][...] = (keep[i].astype(f32) + other[i].astype(f32)).astype(outs[i].dtype)
    if keep.shape[3] == 1152:
        value = joined(keep.at[0, 0]) + joined(other.at[0, 0])
        put_small(value, outs[0].at[0], [out.at[0] for out in outs[1:]])


def near_task(keep, other):
    shape = keep.shape[1:]
    return near_kernel, [keep, other], shaped((shape, f32), *[(shape, bf16)] * 3)


def fork_kernel(ids, ins, outs):
    keep, other = ins
    for at, (own, send, kept, sent) in enumerate(((outs[0], outs[1], (0, 2), (1, 3)), (outs[2], outs[3], (0, 1), (2, 3)))):
        cols = slice(1024 * at, 1024 * (at + 1))
        for j in range(2):
            for out, i in ((own, kept[j]), (send, sent[j])):
                total = keep[i, :, :, cols].astype(f32) + other[i, :, :, cols].astype(f32)
                out[j] = total.astype(out.dtype)


def fork_task(keep, other):
    shape = (2, *keep.shape[1:3], 1024)
    return fork_kernel, [keep, other], shaped(*[(shape, f32), (shape, bf16)] * 2)


def half_kernel(ids, ins, outs):
    own, other = ins
    for j in range(2):
        outs[j][...] = (own[j] + other[j].astype(f32)).astype(outs[j].dtype)


def half_task(own, other):
    shape = own.shape[1:]
    return half_kernel, [own, other], shaped((shape, f32), (shape, bf16))


def join_kernel(ids, ins, outs):
    for at in range(2):
        own, other = ins[2 * at : 2 * at + 2]
        for k in range(4):
            total = own[k] + other[k].astype(f32)
            outs[k][:, 1024 * at : 1024 * (at + 1)] = total.astype(outs[k].dtype)


def join_task(own_up, other_up, own_down, other_down):
    outs = shaped(((32, 2048), f32), *[((32, 2048), bf16)] * 3)
    return join_kernel, [own_up, other_up, own_down, other_down], outs


def plane_kernel(ids, ins, outs):
    for k in range(4):
        total = ins[0][k]
        for other in ins[1:]:
            total = total + other[k].astype(f32)
        outs[k][...] = total.astype(outs[k].dtype)
    if ins[0].shape[2] == 1152:
        x, y, xy = [joined(other.at[0]) for other in ins[1:]]
        put_small((ins[0][0, 0:16, 1024:] + x) + (y + xy), outs[0], outs[1:])


def plane_task(own, others):
    shape = own.shape[1:]
    return plane_kernel, [own, *others], shaped((shape, f32), *[(shape, bf16)] * 3)


def plane_join_kernel(ids, ins, outs):
    plane_kernel(ids, ins[:4], [out.at[:, pl.ds(0, 1024)] for out in outs])
    for part, out in zip(ins[4:], outs):
        out[:, 1024:] = part[...]


def plane_join_task(own, others, *parts):
    outs = shaped(((32, 3072), f32), *[((32, 3072), bf16)] * 3)
    return plane_join_kernel, [own, *others, *parts], outs


def line_total(ins, width):
    total = ins[0][:, :width]
    for other in ins[1:]:
        total = total + other[:, :width].astype(f32)
    return total


def rows_kernel(ids, ins, outs):
    own, other = ins
    half = other.shape[0]
    outs[0][ids[1]] = own[0:half, :].astype(f32)
    outs[0][1 - ids[1]] = other[...].astype(f32)


def rows_task(own, other):
    return rows_kernel, [own, other], shaped(((2, *other.shape), f32))


def code_small(ref):
    return ref[:, 1024:1280].astype(f32) + ref[:, 1280:1536].astype(f32)


def code_sum(refs, out):
    total, small = refs[0][:, :1024].astype(f32), code_small(refs[0])
    for ref in refs[1:]:
        total = total + ref[:, :1024].astype(f32)
        small = small + code_small(ref)
    hi, lo = split2(small)
    out[:, :1024] = total.astype(bf16)
    out[:, 1024:1280] = hi
    out[:, 1280:1536] = lo


def code_near_kernel(ids, ins, outs):
    for k in range(4):
        code_sum([ref.at[k] for ref in ins], outs[k])


def code_near_task(keep, other):
    return code_near_kernel, [keep, other], shaped(*[(keep.shape[1:], bf16)] * 4)


def code_add_kernel(ids, ins, outs):
    code_sum(ins, outs[0])


def code_add_task(*parts):
    return code_add_kernel, list(parts), shaped((parts[0].shape, bf16))


def code_line_kernel(ids, ins, outs):
    for k in range(4):
        outs[0][k] = ins[k][...]


def code_line_task(*parts):
    return code_line_kernel, list(parts), shaped(((4, *parts[0].shape), bf16))


def finish_kernel(ids, ins, outs):
    mlp, attn, dec, code, code_other = ins[:4], ins[4:8], ins[8:12], *ins[12:]
    qkv, out_t, up, down_t, book, vq_in, vq_out, gains, biases, dec_biases, small_ref = outs
    both = line_total(dec, 3072)
    for layer, rows in enumerate((line_total(mlp, 2048), both[:, 1024:])):
        up[layer] = rows[:, :1024]
        down_t[layer] = rows[:, 1024:]
    for layer, rows in enumerate((line_total(attn, 1024), both[:, :1024])):
        for index in range(3):
            qkv[layer, index] = rows[:, index * 256 : (index + 1) * 256]
        out_t[layer] = rows[:, 768:]
    core, z = ids[0] % 2, ids[0] // 4
    for at, parts in ((core, code), (1 - core, code_other)):
        for k in range(4):
            part = at * 4 + (z ^ k)
            book[:, pl.ds(pl.multiple_of(part * 1024, 1024), 1024)] = parts[k, :, :1024].astype(f32)
            small_ref[:, pl.ds(pl.multiple_of(part * 256, 256), 256)] = code_small(parts.at[k])
    small = small_ref[...]
    vq_in[...] = small[:, :512]
    vq_out[...] = small[:, 512:1024]
    rest = small[:, 1024:1536]
    k1, k2, k3 = [joined(other) for other in attn[1:]]
    packed = (attn[0][0:16, 1024:] + k1) + (k2 + k3)
    for row, out in enumerate((gains.at[0:1], biases.at[0:1], gains.at[1:2], biases.at[1:2])):
        for j in range(4):
            out[:, 128 * j : 128 * (j + 1)] = packed[row * 4 + j : row * 4 + j + 1, :]
    gains[2:3, :] = rest[0:1, :]
    biases[2:3, :] = rest[1:2, :]
    gains[3:4, :] = rest[2:3, :]
    dec_biases[0:1, :] = rest[3:4, :]
    gains[4:5, :] = rest[4:5, :]
    dec_biases[1:2, :] = rest[5:6, :]


def finish_task(own_m, line_m, own_a, line_a, own_d, line_d, code, code_other):
    outs = shaped(
        ((2, 3, 32, 256), f32),
        ((2, 32, 256), f32),
        ((2, 32, 1024), f32),
        ((2, 32, 1024), f32),
        ((32, 8192), f32),
        ((32, 512), f32),
        ((32, 512), f32),
        ((5, 512), f32),
        ((3, 512), f32),
        ((2, 512), f32),
        ((32, 2048), f32),
    )
    ins = [own_m, *line_m, own_a, *line_a, own_d, *line_d, code, code_other]
    return finish_kernel, ins, outs


def run_tasks(ids, name, tasks, after=(), carry=()):
    sizes = [(len(ins), len(outs)) for _, ins, outs in tasks]
    n_in = sum(i for i, _ in sizes)

    def kernel(ids_ref, *refs):
        at_in, at_out = 0, n_in
        for (fn, _, _), (i, o) in zip(tasks, sizes):
            fn(ids_ref, refs[at_in : at_in + i], refs[at_out : at_out + o])
            at_in, at_out = at_in + i, at_out + o

    outs = [one for _, _, many in tasks for one in many]
    res = call(
        kernel, name, [SMEM] + [VMEM] * n_in, [VMEM] * len(outs), outs, [], 10**9, after, carry
    )(ids, *[one for _, many, _ in tasks for one in many])
    split, at = [], 0
    for _, o in sizes:
        split.append(res[at : at + o])
        at += o
    return (*split, res[-1])


def whole_groups(
    n_dp,
    tokens,
    segment_ids,
    norm_gains,
    norm_biases,
    w_qkv,
    w_attn_out,
    w_up,
    w_down,
    w_vq_in,
    w_vq_out,
    codebook,
    cotangent,
):
    dp_at, tp_at = lax.axis_index("dp"), lax.axis_index("tp")
    ids = jnp.stack([dp_at, tp_at]).astype(jnp.int32)

    def swap(values):
        return exchange(values, 0, 1, n_dp)

    gains = [norm_gains[i : i + 1] for i in range(5)]
    biases = [norm_biases[i : i + 1] for i in range(5)]
    book_t, in_t = codebook.T, w_vq_in.T
    *shards, own, send = pack(
        ids,
        w_qkv,
        w_attn_out.transpose(0, 2, 1),
        w_up,
        w_down.transpose(0, 2, 1),
        tokens,
        segment_ids,
        cotangent,
    )
    marked = [own, swap(send)]

    enc_attn, enc_mlp, dec_attn, dec_mlp = [
        lax.all_gather(shard, ("dp", "tp")) for shard in shards
    ]
    stack, stack_t, _ = code_prep(book_t)
    codes = (stack, stack_t, book_t)
    e_x1, e_saved, _ = attn_fwd(
        ids, marked, [], gains[0], biases[0], enc_attn, [stack_t]
    )
    e, _, _ = mlp_fwd(e_x1, gains[1], biases[1], enc_mlp)
    u, kept, _ = vq_fwd(e, gains[2], biases[2], in_t, w_vq_out, stack, stack_t)
    d_x1, d_saved, _ = attn_fwd(ids, marked, [u], gains[3], biases[3], dec_attn)

    dx1, d_small1, keep_m, send_m, _ = mlp_bwd(
        ids, d_x1, [cotangent, marked[1]], gains[4], biases[4], dec_mlp
    )
    near_m = exchange(send_m, 1, 0, n_dp)
    du, _, d_small0, keep_a, send_a, (keep_m,) = attn_bwd(
        ids, marked, [u], dx1, gains[3], biases[3], d_saved, dec_attn, carry=[keep_m]
    )
    (own_m, *lows_m), (send_a,) = run_tasks(
        ids, "sums1", [near_task(keep_m, near_m)], carry=[send_a]
    )
    plane_m, near_a = plane_send(lows_m, n_dp), exchange(send_a, 1, 0, n_dp)
    de, code, code_send, (own_m, keep_a) = vq_bwd(
        ids,
        e,
        du,
        gains[2],
        biases[2],
        in_t,
        w_vq_out,
        codes,
        kept,
        [d_small0, d_small1],
        lows_m,
        [own_m, keep_a],
    )
    d_mlp, (own_a, *lows_a), (code_send,) = run_tasks(
        ids, "sums2", [plane_task(own_m, plane_m), near_task(keep_a, near_a)], carry=[code_send]
    )
    plane_a, code_other = plane_send(lows_a, n_dp), exchange(code_send, 1, 0, n_dp)
    code_parts, _ = run_tasks(ids, "sums2b", [code_near_task(code, code_other)])
    code, *code_others = code_parts[0], *line_send(code_parts[1:], n_dp)
    ex1, e_small1, keep_m, send_m, (own_a,) = mlp_bwd(
        ids, e_x1, [de], gains[1], biases[1], enc_mlp, [*lows_a, code_parts[1]], [own_a]
    )
    (own_d, *lows_d), (code,), (keep_m, send_m, d_x1) = run_tasks(
        ids,
        "sums3",
        [plane_join_task(own_a, plane_a, *d_mlp), code_add_task(code, *code_others)],
        carry=[keep_m, send_m, d_x1],
    )
    near_m, code_other = exchange(send_m, 1, 0, n_dp), exchange(code, 0, 1, n_dp)
    line_d = line_send(lows_d, n_dp)
    y, y_theirs, _ = mlp_fwd(d_x1, gains[4], biases[4], dec_mlp)
    (own_up, send_up, own_down, send_down), (code,), (y_theirs,) = run_tasks(
        ids,
        "sums3b",
        [fork_task(keep_m, near_m), code_add_task(code, code_other)],
        carry=[y_theirs],
    )
    other_up, other_down = exchange(send_up, 0, 1, n_dp), exchange(send_down, 2, 0, n_dp)
    code_other, y_other = exchange(code, 2, 0, n_dp), swap(y_theirs)
    dx, dx_low, _, keep_a, send_a, (own_up, own_down) = attn_bwd(
        ids,
        marked,
        [],
        ex1,
        gains[0],
        biases[0],
        e_saved,
        enc_attn,
        [e_small1],
        [send_up, send_down, code],
        [own_up, own_down],
    )
    (own_up, send_up), (own_down, send_down), (code,), (decoded,), (keep_a, send_a, dx_low) = run_tasks(
        ids,
        "sums4",
        [
            half_task(own_up, other_up),
            half_task(own_down, other_down),
            code_add_task(code, code_other),
            rows_task(y, y_other),
        ],
        line_d,
        [keep_a, send_a, dx_low],
    )
    near_a, code_others = exchange(send_a, 1, 0, n_dp), line_send([code] * 3, n_dp)
    other_up, other_down = exchange(send_up, 2, 0, n_dp), exchange(send_down, 0, 1, n_dp)
    (own_a, *lows_a), (code,), (own_up, own_down, dx_low) = run_tasks(
        ids,
        "sums4b",
        [near_task(keep_a, near_a), code_line_task(code, *code_others)],
        carry=[own_up, own_down, dx_low],
    )
    plane_a, code_other = plane_send(lows_a, n_dp), exchange(code, 1, 0, n_dp)
    dx_other = swap(dx_low)
    (own_m, *lows_m), (own_a,) = run_tasks(
        ids, "sums5", [join_task(own_up, other_up, own_down, other_down)], lows_a, [own_a]
    )
    line_m = line_send(lows_m, n_dp)
    (own_a, *lows_a), (grad_tokens,), (own_m,) = run_tasks(
        ids, "sums6", [plane_task(own_a, plane_a), rows_task(dx, dx_other)], lows_m, [own_m]
    )
    line_a = line_send(lows_a, n_dp)
    (qkv, out_t, up, down_t, book, vq_in, vq_out, *norms, _), _ = run_tasks(
        ids,
        "finish",
        [finish_task(own_m, line_m, own_a, line_a, own_d, line_d, code, code_other)],
    )
    return (
        decoded,
        grad_tokens,
        *norms,
        qkv,
        out_t.transpose(0, 2, 1),
        up,
        down_t.transpose(0, 2, 1),
        vq_in.T,
        vq_out,
        book.T,
    )


def layer_norm(values, norm_gain, norm_bias):
    centred = values - jnp.mean(values, axis=-1, keepdims=True)
    spread = jnp.mean(centred * centred, axis=-1, keepdims=True)
    return centred * lax.rsqrt(spread + ln_eps) * norm_gain + norm_bias


def gelu_tanh(values):
    return (
        0.5 * values * (1.0 + jnp.tanh(gelu_coef * (values + 0.044715 * values * values * values)))
    )


def matmul(former, latter):
    return jnp.dot(former, latter, precision=highest, preferred_element_type=jnp.float32)


def normalize(values):
    return values * lax.rsqrt(jnp.sum(values * values, axis=-1, keepdims=True) + norm_eps)


def quantize(in_rows, norm_gain, norm_bias, in_w, out_w, code_w):
    latent = normalize(matmul(layer_norm(in_rows, norm_gain, norm_bias), in_w))
    code_rows = normalize(code_w)
    logits = matmul(latent, code_rows.T) * temper
    row_max = jnp.max(logits, axis=-1, keepdims=True)
    numerator = jnp.exp(logits - row_max)
    assign = numerator / jnp.sum(numerator, axis=-1, keepdims=True)
    soft_code = matmul(assign, code_rows)
    offset = latent - soft_code
    vq_loss = commit_weight * 1.25 * jnp.sum(offset * offset)
    return (matmul(soft_code, out_w), vq_loss)


def product(former, latter):
    return jnp.dot(former, latter, preferred_element_type=jnp.float32)


def product_tn(former, latter):
    return lax.dot_general(
        former, latter, (((0,), (0,)), ((), ())), preferred_element_type=jnp.float32
    )


def product_nt(former, latter):
    return lax.dot_general(
        former, latter, (((1,), (1,)), ((), ())), preferred_element_type=jnp.float32
    )


def split_heads(values):
    return values.reshape(values.shape[0], values.shape[1] // HEAD_DIM, HEAD_DIM).transpose(1, 0, 2)


def join_heads(values):
    return values.transpose(1, 0, 2).reshape(values.shape[1], values.shape[0] * HEAD_DIM)


def masked_scores(query_blk, key_h, seg_blk, seg_keys):
    scores = jnp.einsum(
        "hqd,hkd->hqk", query_blk, key_h, preferred_element_type=jnp.float32
    ) * HEAD_DIM ** (-0.5)
    return jnp.where((seg_blk[:, None] == seg_keys[None, :])[None], scores, masked_score)


def attend(query_h, key_h, value_h, seg_keys):
    block_rows = min(512, query_h.shape[1])
    block_count = query_h.shape[1] // block_rows

    def one_block(begin_row):
        query_blk = lax.dynamic_slice_in_dim(query_h, begin_row, block_rows, 1)
        seg_blk = lax.dynamic_slice_in_dim(seg_keys, begin_row, block_rows, 0)
        scores = masked_scores(query_blk, key_h, seg_blk, seg_keys)
        row_max = jnp.max(scores, axis=-1, keepdims=True)
        numerator = jnp.exp(scores - row_max)
        row_total = jnp.sum(numerator, axis=-1, keepdims=True)
        prob_low = (numerator / row_total).astype(jnp.bfloat16)
        attended = jnp.einsum("hqk,hkd->hqd", prob_low, value_h, preferred_element_type=jnp.float32)
        return (attended.astype(jnp.bfloat16), (row_max + jnp.log(row_total))[..., 0])

    starts = jnp.arange(block_count, dtype=jnp.int32) * block_rows
    attended, log_sums = lax.map(one_block, starts)
    heads_out = attended.transpose(1, 0, 2, 3).reshape(query_h.shape)
    log_sums = log_sums.transpose(1, 0, 2).reshape(query_h.shape[0], query_h.shape[1])
    return (heads_out, log_sums)


def attend_back(query_h, key_h, value_h, seg_keys, log_sums, grad_out):
    block_rows = min(512, query_h.shape[1])
    block_count = query_h.shape[1] // block_rows

    def one_block(carry, begin_row):
        grad_key, grad_value = carry
        query_blk = lax.dynamic_slice_in_dim(query_h, begin_row, block_rows, 1)
        grad_blk = lax.dynamic_slice_in_dim(grad_out, begin_row, block_rows, 1)
        lse_blk = lax.dynamic_slice_in_dim(log_sums, begin_row, block_rows, 1)
        seg_blk = lax.dynamic_slice_in_dim(seg_keys, begin_row, block_rows, 0)
        scores = masked_scores(query_blk, key_h, seg_blk, seg_keys)
        probs = jnp.exp(scores - lse_blk[..., None])
        prob_low = probs.astype(jnp.bfloat16)
        grad_value = grad_value + jnp.einsum(
            "hqk,hqd->hkd", prob_low, grad_blk, preferred_element_type=jnp.float32
        )
        grad_prob = jnp.einsum(
            "hqd,hkd->hqk", grad_blk, value_h, preferred_element_type=jnp.float32
        )
        row_dot = jnp.sum(probs * grad_prob, axis=-1, keepdims=True)
        grad_score = (probs * (grad_prob - row_dot) * HEAD_DIM ** (-0.5)).astype(jnp.bfloat16)
        grad_query = jnp.einsum(
            "hqk,hkd->hqd", grad_score, key_h, preferred_element_type=jnp.float32
        )
        grad_key = grad_key + jnp.einsum(
            "hqk,hqd->hkd", grad_score, query_blk, preferred_element_type=jnp.float32
        )
        return ((grad_key, grad_value), grad_query)

    starts = jnp.arange(block_count, dtype=jnp.int32) * block_rows
    zeros_kv = jnp.zeros(key_h.shape, jnp.float32)
    (grad_key, grad_value), grad_query = lax.scan(one_block, (zeros_kv, zeros_kv), starts)
    grad_query = grad_query.transpose(1, 0, 2, 3).reshape(query_h.shape)
    return (
        grad_query.astype(jnp.bfloat16),
        grad_key.astype(jnp.bfloat16),
        grad_value.astype(jnp.bfloat16),
    )


def spread_rows(values):
    return lax.all_gather(values, "tp", axis=0, tiled=True)


def combine_rows(partial_value):
    return lax.psum_scatter(partial_value, "tp", scatter_dimension=0, tiled=True)


def spread_grads(values):
    return lax.all_gather(values, "tp", axis=0, tiled=True)


def combine_grads(partial_value):
    return lax.psum_scatter(
        partial_value.astype(jnp.bfloat16), "tp", scatter_dimension=0, tiled=True
    ).astype(jnp.float32)


def fetch_weights(w_qkv, w_attn_out, w_up, w_down, layer):
    return (
        lax.all_gather(w_qkv[layer], "dp", axis=1, tiled=True),
        lax.all_gather(w_attn_out[layer], "dp", axis=1, tiled=True),
        lax.all_gather(w_up[layer], "dp", axis=0, tiled=True),
        lax.all_gather(w_down[layer], "dp", axis=1, tiled=True),
    )


def reduce_weight_grads(grads):
    return (
        lax.psum_scatter(
            grads[0].astype(jnp.bfloat16), "dp", scatter_dimension=1, tiled=True
        ).astype(jnp.float32),
        lax.psum_scatter(
            grads[1].astype(jnp.bfloat16), "dp", scatter_dimension=1, tiled=True
        ).astype(jnp.float32),
        lax.psum_scatter(
            grads[2].astype(jnp.bfloat16), "dp", scatter_dimension=0, tiled=True
        ).astype(jnp.float32),
        lax.psum_scatter(
            grads[3].astype(jnp.bfloat16), "dp", scatter_dimension=1, tiled=True
        ).astype(jnp.float32),
    )


def block_forward(resid_in, seg_local, gains, biases, weights):
    qkv_w, attn_w, up_w, down_w = weights
    normed = layer_norm(resid_in, gains[0], biases[0]).astype(jnp.bfloat16)
    normed_all, seg_all = (
        lax.all_gather(normed, "tp", axis=0, tiled=True),
        lax.all_gather(seg_local, "tp", axis=0, tiled=True),
    )
    query_h = split_heads(product(normed_all, qkv_w[0]).astype(jnp.bfloat16))
    key_h = split_heads(product(normed_all, qkv_w[1]).astype(jnp.bfloat16))
    value_h = split_heads(product(normed_all, qkv_w[2]).astype(jnp.bfloat16))
    heads_out, log_sums = attend(query_h, key_h, value_h, seg_all)
    attn_rows = join_heads(heads_out)
    middle = resid_in + combine_rows(product(attn_rows, attn_w))
    normed_mid = spread_rows(layer_norm(middle, gains[1], biases[1]).astype(jnp.bfloat16))
    hidden_pre = product(normed_mid, up_w)
    hidden = gelu_tanh(hidden_pre).astype(jnp.bfloat16)
    result = middle + combine_rows(product(hidden, down_w))
    kept = (
        resid_in,
        middle,
        normed_all,
        seg_all,
        query_h,
        key_h,
        value_h,
        log_sums,
        attn_rows,
        normed_mid,
        hidden_pre,
        hidden,
    )
    return (result, kept)


def block_backward(kept, gains, biases, weights, grad_result):
    (
        resid_in,
        middle,
        normed_all,
        seg_all,
        query_h,
        key_h,
        value_h,
        log_sums,
        attn_rows,
        normed_mid,
        hidden_pre,
        hidden,
    ) = kept
    qkv_w, attn_w, up_w, down_w = weights
    grad_branch = spread_grads(grad_result.astype(jnp.bfloat16))
    grad_down = product_tn(hidden, grad_branch)
    grad_hidden = product_nt(grad_branch, down_w)
    _, gelu_back = jax.vjp(gelu_tanh, hidden_pre)
    grad_pre = gelu_back(grad_hidden)[0].astype(jnp.bfloat16)
    grad_up = product_tn(normed_mid, grad_pre)
    grad_norm_mid = combine_grads(product_nt(grad_pre, up_w))
    _, norm_back_mid = jax.vjp(layer_norm, middle, gains[1], biases[1])
    grad_mid_ln, grad_gain_mid, grad_bias_mid = norm_back_mid(grad_norm_mid)
    grad_middle = grad_result + grad_mid_ln
    grad_attn_all = spread_grads(grad_middle.astype(jnp.bfloat16))
    grad_attn = product_tn(attn_rows, grad_attn_all)
    grad_heads = split_heads(product_nt(grad_attn_all, attn_w).astype(jnp.bfloat16))
    grad_query, grad_key, grad_value = attend_back(
        query_h, key_h, value_h, seg_all, log_sums, grad_heads
    )
    grad_parts = [join_heads(grad_query), join_heads(grad_key), join_heads(grad_value)]
    grad_qkv = jnp.stack([product_tn(normed_all, grad_part) for grad_part in grad_parts])
    grad_normed_part = (
        product_nt(grad_parts[0], qkv_w[0])
        + product_nt(grad_parts[1], qkv_w[1])
        + product_nt(grad_parts[2], qkv_w[2])
    )
    grad_normed = combine_grads(grad_normed_part)
    _, norm_back_in = jax.vjp(layer_norm, resid_in, gains[0], biases[0])
    grad_in_ln, grad_gain_in, grad_bias_in = norm_back_in(grad_normed)
    gain_grads = jnp.stack([grad_gain_in, grad_gain_mid])
    bias_grads = jnp.stack([grad_bias_in, grad_bias_mid])
    return (
        grad_middle + grad_in_ln,
        gain_grads,
        bias_grads,
        (grad_qkv, grad_attn, grad_up, grad_down),
    )


def local(
    tokens,
    segment_ids,
    norm_gains,
    norm_biases,
    w_qkv,
    w_attn_out,
    w_up,
    w_down,
    w_vq_in,
    w_vq_out,
    codebook,
    cotangent,
):
    gain_sum = jnp.zeros(norm_gains.shape, jnp.float32)
    bias_sum = jnp.zeros(norm_biases.shape, jnp.float32)
    vq_in_sum = jnp.zeros(w_vq_in.shape, jnp.float32)
    vq_out_sum = jnp.zeros(w_vq_out.shape, jnp.float32)
    code_sum = jnp.zeros(codebook.shape, jnp.float32)
    layer_sums = [None, None]
    outputs = []
    input_grads = []
    for micro in range(MICRO):
        resid_in = tokens[micro].astype(jnp.float32)
        seg_local = segment_ids[micro]
        enc_weights = fetch_weights(w_qkv, w_attn_out, w_up, w_down, 0)
        encoded, enc_kept = block_forward(
            resid_in, seg_local, norm_gains[0:2], norm_biases[0:2], enc_weights
        )
        (decoder_in, _), vq_back = jax.vjp(
            quantize, encoded, norm_gains[2], norm_biases[2], w_vq_in, w_vq_out, codebook
        )
        dec_weights = fetch_weights(w_qkv, w_attn_out, w_up, w_down, 1)
        decoded, dec_kept = block_forward(
            decoder_in, seg_local, norm_gains[3:5], norm_biases[3:5], dec_weights
        )
        outputs.append(decoded)
        grad_dec_in, gains_dec, biases_dec, grads_dec = block_backward(
            dec_kept, norm_gains[3:5], norm_biases[3:5], dec_weights, cotangent[micro]
        )
        grad_encoded, grad_gain_vq, grad_bias_vq, grad_in_w, grad_out_w, grad_codes = vq_back(
            (grad_dec_in, jnp.ones((), jnp.float32))
        )
        grad_input, gains_enc, biases_enc, grads_enc = block_backward(
            enc_kept, norm_gains[0:2], norm_biases[0:2], enc_weights, grad_encoded
        )
        input_grads.append(grad_input)
        gain_sum = gain_sum + jnp.concatenate([gains_enc, grad_gain_vq[None], gains_dec], axis=0)
        bias_sum = bias_sum + jnp.concatenate([biases_enc, grad_bias_vq[None], biases_dec], axis=0)
        vq_in_sum = vq_in_sum + grad_in_w
        vq_out_sum = vq_out_sum + grad_out_w
        code_sum = code_sum + grad_codes
        for layer, grads in ((0, grads_enc), (1, grads_dec)):
            reduced = reduce_weight_grads(grads)
            if layer_sums[layer] is None:
                layer_sums[layer] = reduced
            else:
                layer_sums[layer] = jax.tree.map(jnp.add, layer_sums[layer], reduced)
    gain_tot, bias_tot, vq_in_tot, vq_out_tot, code_tot = lax.psum(
        (gain_sum, bias_sum, vq_in_sum, vq_out_sum, code_sum), ("dp", "tp")
    )
    return (
        jnp.stack(outputs),
        jnp.stack(input_grads),
        gain_tot,
        bias_tot[0:3],
        bias_tot[3:5],
        jnp.stack([layer_sums[0][0], layer_sums[1][0]]),
        jnp.stack([layer_sums[0][1], layer_sums[1][1]]),
        jnp.stack([layer_sums[0][2], layer_sums[1][2]]),
        jnp.stack([layer_sums[0][3], layer_sums[1][3]]),
        vq_in_tot,
        vq_out_tot,
        code_tot,
    )


def solution(mesh):
    n_dp, n_tp = mesh.shape["dp"], mesh.shape["tp"]
    fits = n_tp == MICRO and n_dp == 16
    return jax.shard_map(
        functools.partial(whole_groups, n_dp) if fits else local,
        mesh=mesh,
        in_specs=(
            P(None, ("dp", "tp"), None),
            P(None, ("dp", "tp")),
            P(),
            P(),
            P(None, None, "dp", "tp"),
            P(None, "tp", "dp"),
            P(None, "dp", "tp"),
            P(None, "tp", "dp"),
            P(),
            P(),
            P(),
            P(None, ("dp", "tp"), None),
        ),
        out_specs=(
            P(None, ("dp", "tp"), None),
            P(None, ("dp", "tp"), None),
            P(),
            P(),
            P(),
            P(None, None, "dp", "tp"),
            P(None, "tp", "dp"),
            P(None, "dp", "tp"),
            P(None, "tp", "dp"),
            P(),
            P(),
            P(),
        ),
        check_vma=False,
    )
```

```python
import functools

import jax
import jax.numpy as jnp
from jax import lax
from jax.experimental import pallas as pl
from jax.experimental.pallas import tpu as pltpu
from jax.sharding import PartitionSpec as P

HEAD_DIM = 64
MICRO = 2
bf16 = jnp.bfloat16
f32 = jnp.float32
highest = lax.Precision.HIGHEST
ln_eps = 1e-05
norm_eps = 1e-06
temper = 10.0
commit_weight = 64.0
gelu_coef = 0.7978845608028654
masked_score = -1e30
log2e = 1.4426950408889634
vmem_cap = 36 * 1024 * 1024


PLANE = ((0, 0), (0, 1), (1, 0), (1, 1))


def exchange(values, dp_xor, tp_xor, n_dp):
    pairs = [
        (d * 2 + t, (d ^ dp_xor) * 2 + (t ^ tp_xor)) for d in range(n_dp) for t in range(2)
    ]
    return lax.ppermute(values, ("dp", "tp"), pairs)


def spread_line(shard, n_dp):
    return [shard] + [exchange(shard, 4 * k, 0, n_dp) for k in range(1, 4)]


def plane_quads(own, n_dp):
    return [own] + [exchange(own, 2 * y, x, n_dp) for y, x in PLANE[1:]]


def plane_send(lows, n_dp):
    return [exchange(low, 2 * y, x, n_dp) for (y, x), low in zip(PLANE[1:], lows)]


def line_send(lows, n_dp):
    return [exchange(low, 4 * k, 0, n_dp) for k, low in zip(range(1, 4), lows)]


def dot(a, b):
    return jnp.dot(a, b, preferred_element_type=f32)


def dot_nt(a, b, precision=None):
    return lax.dot_general(
        a, b, (((1,), (1,)), ((), ())), preferred_element_type=f32, precision=precision
    )


def dot_full(a, b):
    return jnp.dot(a, b, preferred_element_type=f32, precision=highest)


def ln_parts(x):
    centred = x - jnp.mean(x, axis=-1, keepdims=True)
    inv = lax.rsqrt(jnp.mean(centred * centred, axis=-1, keepdims=True) + ln_eps)
    return centred * inv, inv


def ln_back(grad, xhat, inv, gain):
    scaled = grad * gain
    return inv * (
        scaled
        - jnp.mean(scaled, axis=-1, keepdims=True)
        - xhat * jnp.mean(scaled * xhat, axis=-1, keepdims=True)
    )


def split2(x):
    hi = x.astype(bf16)
    return hi, (x - hi.astype(f32)).astype(bf16)


def split3(x):
    hi, _ = split2(x)
    rest = x - hi.astype(f32)
    mid = rest.astype(bf16)
    return hi, mid, (rest - mid.astype(f32)).astype(bf16)


def order_matrix(dp, inverse):
    at = lax.broadcasted_iota(jnp.int32, (512, 512), 0 if inverse else 1)
    other = lax.broadcasted_iota(jnp.int32, (512, 512), 1 if inverse else 0)
    block = at >> 5
    bits = ((block & 3) << 2) | (((block >> 2) & 1) << 1) | (block >> 3)
    return jnp.where(other == (((dp ^ bits) << 5) | (at & 31)), 1.0, 0.0).astype(bf16)


def ordered(x, matrix):
    if x.dtype == bf16:
        return dot(x, matrix)
    hi, mid, lo = split3(x)
    return (dot(hi, matrix) + dot(mid, matrix)) + dot(lo, matrix)


def w_at(refs, t, cols):
    parts = [ref[2 * y + t, :, :, cols] for ref in refs for y in range(2)]
    return jnp.concatenate([part.reshape(128, part.shape[2]) for part in parts], axis=0)


def put_grad(refs, t, cols, value):
    for core, ref in enumerate(refs):
        for y in range(2):
            rows = value[core * 256 + y * 128 : core * 256 + (y + 1) * 128]
            ref[2 * y + t, :, :, cols] = rows.reshape(4, 32, rows.shape[1])


def start_all(copies):
    for copy in copies:
        copy.start()


def wait_all(copies):
    for copy in copies:
        copy.wait()


def head_rows(ref, pair, which):
    own = ref[pl.ds(pair * 128 + which * HEAD_DIM, HEAD_DIM), :]
    zero = jnp.zeros_like(own)
    return jnp.concatenate([own, zero] if which == 0 else [zero, own], axis=0)


def segment_mask(own, other):
    ids = jnp.concatenate([own[:, 512:640], other[:, 512:640]], axis=0).astype(f32)
    return jnp.where(ids[:, 0:1] == ids.T[0:1, :], 0.0, masked_score)


def load_rows(x, own, other):
    if x is None:
        return jnp.concatenate([own[:, :512], other[:, :512]], axis=0).astype(f32)
    return x[...]


def gain_of(norms, at):
    return norms[at : at + 1, :]


def bias_of(norms, at):
    return norms[8 + at : 9 + at, :]


def attn_fwd_kernel(with_x, at, own, other, norms, w0, w1, *refs):
    x, refs = (refs[0], refs[1:]) if with_x else (None, refs)
    x1, lse, saved, refs = refs[0], refs[1], refs[2:8], refs[8:]
    h, vt, ot, mask, qs, k, v, o, qst, kt, out_sems = refs
    w = (w0, w1)
    keeps = [
        pltpu.make_async_copy(held, to, out_sems.at[i])
        for i, (held, to) in enumerate(zip((qs, k, v, o, qst, kt), saved))
    ]
    xf = load_rows(x, own, other)
    h[...] = (ln_parts(xf)[0] * gain_of(norms, at) + bias_of(norms, at)).astype(bf16)
    mask[...] = segment_mask(own, other)
    for t in range(2):
        cols = slice(t * 256, (t + 1) * 256)
        q = dot(h[...], w_at(w, t, slice(0, 256))).astype(bf16)
        qs[:, cols] = (q * HEAD_DIM ** (-0.5)).astype(bf16)
        k[:, cols] = dot(h[...], w_at(w, t, slice(256, 512))).astype(bf16)
        v[:, cols] = dot(h[...], w_at(w, t, slice(512, 768))).astype(bf16)
    qst[...] = qs[...].T
    kt[...] = k[...].T
    vt[...] = v[...].T
    for i in (0, 1, 2, 4, 5):
        keeps[i].start()
    for pair in range(4):
        k_pair = k[:, pair * 128 : (pair + 1) * 128]
        for which in range(2):
            scores = dot(k_pair, head_rows(qst, pair, which)) + mask[...]
            top = jnp.max(scores, axis=0, keepdims=True)
            numer = jnp.exp(scores - top).astype(bf16)
            rows = pl.ds(pair * 128 + which * HEAD_DIM, HEAD_DIM)
            left = jnp.concatenate([vt[rows, :], jnp.ones((16, 512), bf16)], axis=0)
            both = dot(left, numer)
            total = both[HEAD_DIM : HEAD_DIM + 1, :]
            ot[rows, :] = (both[:HEAD_DIM, :] / total).astype(bf16)
            lse[pl.ds(pair * 2 + which, 1), :] = top + jnp.log(total)
    o[...] = ot[...].T
    keeps[3].start()
    acc = xf
    for t in range(2):
        acc = acc + dot_nt(o[:, t * 256 : (t + 1) * 256], w_at(w, t, slice(768, 1024)))
    x1[...] = acc
    wait_all(keeps)


def gelu_parts(u):
    square = u * u
    tanh = jnp.tanh(gelu_coef * u * (1.0 + 0.044715 * square))
    return 0.5 * u * (1.0 + tanh), tanh, square


def mlp_halves(w):
    return (w, w, 1024) if len(w) == 2 else (w[:2], w[2:], 0)


def mlp_fwd_kernel(n_w, at, x1, norms, *refs):
    up, down, first = mlp_halves(refs[:n_w])
    y, theirs, h2 = refs[n_w:]
    h2[...] = (ln_parts(x1[...])[0] * gain_of(norms, at) + bias_of(norms, at)).astype(bf16)
    acc = x1[...]
    for t in range(2):
        for part in range(2):
            pre = dot(h2[...], w_at(up, t, slice(part * 512, (part + 1) * 512)))
            hidden = gelu_parts(pre)[0].astype(bf16)
            cols = slice(first + part * 512, first + (part + 1) * 512)
            acc = acc + dot_nt(hidden, w_at(down, t, cols))
    y[...] = acc
    theirs[...] = acc[256:, :].astype(bf16)


def mlp_bwd_kernel(split, n_w, at, ids, x1, norms, *refs):
    up, down, first = mlp_halves(refs[:n_w])
    refs = refs[n_w:]
    if split:
        own, other, refs = refs[0], refs[1], refs[2:]
    else:
        dy, refs = refs[0], refs[1:]
    dx1, small, grads = refs[0], refs[1], refs[2:4]
    h2, h2t, dyb, dybt, dh2 = refs[4:9]
    if split:
        dy = refs[9]
        dy[0:256, :] = ordered(own[ids[1]], order_matrix(ids[0], False))
        dy[256:, :] = other[:, 640:].astype(f32)
    h2[...] = (ln_parts(x1[...])[0] * gain_of(norms, at) + bias_of(norms, at)).astype(bf16)
    h2t[...] = h2[...].T
    dyb[...] = dy[...].astype(bf16)
    dybt[...] = dyb[...].T
    for t in range(2):
        for part in range(2):
            cols = slice(part * 512, (part + 1) * 512)
            down_cols = slice(first + part * 512, first + (part + 1) * 512)
            w_up = w_at(up, t, cols)
            pre = dot(h2[...], w_up)
            hidden, tanh, square = gelu_parts(pre)
            slope = 0.5 * (1.0 + tanh) + (0.5 * gelu_coef) * pre * (1.0 - tanh * tanh) * (
                1.0 + (3 * 0.044715) * square
            )
            dhidden = dot(dyb[...], w_at(down, t, down_cols))
            dpre = (dhidden * slope).astype(bf16)
            out_cols = slice(1024 + part * 512, 1024 + (part + 1) * 512)
            put_grad(grads, t, out_cols, dot(dybt[...], hidden.astype(bf16)).astype(bf16))
            put_grad(grads, t, cols, dot(h2t[...], dpre).astype(bf16))
            more = dot_nt(dpre, w_up)
            if t + part == 0:
                dh2[...] = more
            else:
                dh2[...] += more
    xhat, inv = ln_parts(x1[...])
    grad = dh2[...]
    small[0:1, :] = jnp.sum(grad * xhat, axis=0, keepdims=True)
    small[1:2, :] = jnp.sum(grad, axis=0, keepdims=True)
    dx1[...] = dy[...] + ln_back(grad, xhat, inv, gain_of(norms, at))


def pack_rows(rows):
    cut = [rows[i : i + 1, 128 * j : 128 * (j + 1)] for i in range(4) for j in range(4)]
    return jnp.concatenate(split2(jnp.concatenate(cut, axis=0)), axis=0)


def attn_bwd_kernel(with_x, with_small, at, ids, own, other, dx1, norms, lse, w0, w1, *refs):
    saved, refs = refs[:6], refs[6:]
    x, refs = (refs[0], refs[1:]) if with_x else (None, refs)
    if with_small:
        other_small, refs = refs[0], refs[1:]
    dx, dx_low, small, grads = refs[0], refs[1], refs[2], refs[3:5]
    h, mask, do, dot_t, dqt, dq, dk, dv, flip, qs, k, v, o, qst, kt, in_sems = refs[5:]
    w = (w0, w1)
    takes = [
        pltpu.make_async_copy(held, to, in_sems.at[i])
        for i, (held, to) in enumerate(zip(saved, (qs, k, v, o, qst, kt)))
    ]
    start_all(takes)
    xf = load_rows(x, own, other)
    h[...] = (ln_parts(xf)[0] * gain_of(norms, at) + bias_of(norms, at)).astype(bf16)
    mask[...] = segment_mask(own, other)
    low = dx1[...].astype(bf16)
    flip[...] = low.T
    wait_all(takes)
    for t in range(2):
        cols = slice(t * 256, (t + 1) * 256)
        do[:, cols] = dot(low, w_at(w, t, slice(768, 1024))).astype(bf16)
        put_grad(grads, t, slice(768, 1024), dot(flip[...], o[:, cols]).astype(bf16))
    dot_t[...] = do[...].T
    first = lax.broadcasted_iota(jnp.int32, (512, 128), 1) < HEAD_DIM
    for pair in range(4):
        lanes = slice(pair * 128, (pair + 1) * 128)
        dvs, dks = [], []
        for which in range(2):
            head = pair * 2 + which
            rows = pl.ds(head * HEAD_DIM, HEAD_DIM)
            scores = dot(k[:, lanes], head_rows(qst, pair, which)) + mask[...]
            probs = jnp.exp(scores - lse[head : head + 1, :])
            dprobs = dot(v[:, lanes], head_rows(dot_t, pair, which))
            shift = jnp.sum(probs * dprobs, axis=0, keepdims=True)
            dscore = (probs * (dprobs - shift)).astype(bf16)
            dvs.append(dot(probs.astype(bf16), do[:, lanes]))
            dks.append(dot(dscore, qs[:, lanes]))
            dqt[rows, :] = (dot(kt[rows, :], dscore) * HEAD_DIM ** (-0.5)).astype(bf16)
        dv[:, lanes] = jnp.where(first, dvs[0], dvs[1]).astype(bf16)
        dk[:, lanes] = jnp.where(first, dks[0], dks[1]).astype(bf16)
    dq[...] = dqt[...].T
    flip[...] = h[...].T
    grad = jnp.zeros((512, 512), f32)
    for t in range(2):
        cols = slice(t * 256, (t + 1) * 256)
        for index, part in enumerate((dq, dk, dv)):
            w_cols = slice(index * 256, (index + 1) * 256)
            put_grad(grads, t, w_cols, dot(flip[...], part[:, cols]).astype(bf16))
            grad = grad + dot_nt(part[:, cols], w_at(w, t, w_cols))
    xhat, inv = ln_parts(xf)
    small[0:1, :] = jnp.sum(grad * xhat, axis=0, keepdims=True)
    small[1:2, :] = jnp.sum(grad, axis=0, keepdims=True)
    if with_small:
        rows = jnp.concatenate([small[0:2, :], other_small[0:2, :], jnp.zeros((4, 512), f32)], axis=0)
        packed = pack_rows(ordered(rows, order_matrix(ids[0], True)))
        for out in grads:
            for i in range(4):
                for z in range(4):
                    out[i, z, :, 1024:1152] = packed
    total = dx1[...] + ln_back(grad, xhat, inv, gain_of(norms, at))
    dx[...] = total
    dx_low[...] = total[256:, :].astype(bf16)


def code_prep_kernel(book_t, stack, stack_t):
    def one_chunk(index, _):
        lanes = pl.ds(pl.multiple_of(index * 512, 512), 512)
        rows = book_t[:, lanes]
        unit = rows * lax.rsqrt(jnp.sum(rows * rows, axis=0, keepdims=True) + norm_eps)
        hi, mid, lo = split3(unit)
        stack_t[:, lanes] = jnp.concatenate([hi, mid, lo, jnp.ones((32, 512), bf16)], axis=0)
        tall = jnp.concatenate([hi, mid, lo, hi, mid, hi, jnp.zeros((64, 512), bf16)], axis=0)
        stack[lanes, :] = tall.T
        return 0

    lax.fori_loop(0, book_t.shape[1] // 512, one_chunk, 0)


def factor_stack(x):
    hi, mid, lo = split3(x)
    return jnp.concatenate([hi, hi, hi, mid, mid, lo, jnp.zeros((64, x.shape[1]), bf16)], axis=0)


def code_loads(pairs, sems):
    loads = []
    for piece in range(4):
        group = []
        for at, (held, to, by_row) in enumerate(pairs):
            size = held.shape[0 if by_row else 1] // 4
            part = pl.ds(piece * size, size)
            place = (part, slice(None)) if by_row else (slice(None), part)
            group.append(pltpu.make_async_copy(held.at[place], to.at[place], sems.at[at, piece]))
        start_all(group)
        loads.append(group)
    return loads


def vq_fwd_kernel(
    e, norms, vq_w, stack_hbm, stack_t_hbm, u, kept, acc, stack, stack_t, sems
):
    loads = code_loads([(stack_hbm, stack, True), (stack_t_hbm, stack_t, False)], sems)
    lnv = ln_parts(e[...])[0] * gain_of(norms, 2) + bias_of(norms, 2)
    raw = dot_nt(vq_w[0:32, :], lnv, highest)
    inv = lax.rsqrt(jnp.sum(raw * raw, axis=0, keepdims=True) + norm_eps)
    latent = raw * inv
    right = factor_stack(latent * (temper * log2e))
    acc[...] = jnp.zeros_like(acc)

    def one_chunk(index, _):
        codes = pl.ds(pl.multiple_of(index * 512, 512), 512)
        numer = jnp.exp2(dot(stack[codes, :], right)).astype(bf16)
        acc[...] += dot(stack_t[:, codes], numer)
        return 0

    chunks = stack.shape[0] // 512
    for piece, group in enumerate(loads):
        wait_all(group)
        lax.fori_loop(chunks * piece // 4, chunks * (piece + 1) // 4, one_chunk, 0)
    total = acc[96:97, :]
    soft = (acc[0:32, :] + acc[32:64, :] + acc[64:96, :]) / total
    kept[0:32, :] = latent
    kept[32:64, :] = soft
    kept[64:65, :] = total
    kept[65:66, :] = inv
    u[...] = dot_full(soft.T, vq_w[32:64, :])


def vq_bwd_kernel(ids, e, du, norms, vq_w, stack_hbm, stack_t_hbm, book_hbm, kept, *refs):
    small0, small1, de, code_keep, code_send = refs[:5]
    acc, grads, small, tail, stack, stack_t, book_t, load_sems, sems = refs[5:]
    loads = code_loads(
        [(stack_hbm, stack, True), (stack_t_hbm, stack_t, False), (book_hbm, book_t, False)],
        load_sems,
    )
    xhat, inv_ln = ln_parts(e[...])
    lnv = xhat * gain_of(norms, 2) + bias_of(norms, 2)
    latent, soft = kept[0:32, :], kept[32:64, :]
    total, inv = kept[64:65, :], kept[65:66, :]
    direct = (2.0 * 1.25 * commit_weight) * (latent - soft)
    dsoft = dot_nt(vq_w[32:64, :], du[...], highest) - direct
    small[32:64, :] = dot_full(soft, du[...])
    shift = jnp.sum(dsoft * soft, axis=0, keepdims=True) / total
    dsoft = dsoft / total
    right = jnp.concatenate(
        [factor_stack(latent * (temper * log2e)), factor_stack(dsoft)], axis=1
    )
    pads = jnp.zeros((64, 512), f32)

    def tall(x):
        hi, lo = split2(x)
        return jnp.concatenate([hi.astype(f32), lo.astype(f32), pads], axis=0).T.astype(bf16)

    sides = jnp.concatenate([tall(dsoft), tall(latent * temper)], axis=0)
    acc[...] = jnp.zeros_like(acc)

    def one_chunk(index, _):
        codes = pl.ds(pl.multiple_of(index * 512, 512), 512)
        both = dot(stack[codes, :], right)
        numer = jnp.exp2(both[:, :512])
        dlogit = (numer * (both[:, 512:] - shift)).astype(bf16)
        acc[...] += dot(stack_t[0:96, codes], dlogit)
        dcode = dot(jnp.concatenate([numer.astype(bf16), dlogit], axis=1), sides).T
        dcode = dcode[0:32, :] + dcode[32:64, :]
        rows = book_t[:, codes]
        scale = lax.rsqrt(jnp.sum(rows * rows, axis=0, keepdims=True) + norm_eps)
        unit = rows * scale
        grads[:, codes] = (
            scale * (dcode - unit * jnp.sum(unit * dcode, axis=0, keepdims=True))
        ).astype(bf16)
        return 0

    chunks = stack.shape[0] // 512
    for piece, group in enumerate(loads):
        wait_all(group)
        lax.fori_loop(chunks * piece // 4, chunks * (piece + 1) // 4, one_chunk, 0)
    dlatent = temper * (acc[0:32, :] + acc[32:64, :] + acc[64:96, :]) + direct
    draw = inv * (dlatent - latent * jnp.sum(latent * dlatent, axis=0, keepdims=True))
    small[0:32, :] = dot_full(draw, lnv)
    dln = dot_full(draw.T, vq_w[0:32, :])
    small[64:65, :] = jnp.sum(dln * xhat, axis=0, keepdims=True)
    small[65:66, :] = jnp.sum(dln, axis=0, keepdims=True)
    small[66:68, :] = small0[0:2, :]
    small[68:70, :] = small1[0:2, :]
    small[70:96, :] = jnp.zeros((26, 512), f32)
    small[...] = ordered(small[...], order_matrix(ids[0], True))
    for block in range(3):
        for at, part in enumerate(split2(small[block * 32 : (block + 1) * 32, :])):
            for side in range(2):
                tail[block * 2 + side, :, at * 256 : (at + 1) * 256] = part[
                    :, side * 256 : (side + 1) * 256
                ]
    tail[6:8] = jnp.zeros((2, 32, 512), bf16)
    core, z = ids[0] % 2, ids[0] // 4
    copies = []
    for slot, (at, to) in enumerate(((core, code_keep), (1 - core, code_send))):
        for k in range(4):
            part = at * 4 + (z ^ k)
            lanes = pl.ds(pl.multiple_of(part * 1024, 1024), 1024)
            copies += [
                pltpu.make_async_copy(
                    grads.at[:, lanes], to.at[k, :, pl.ds(0, 1024)], sems.at[0, slot, k]
                ),
                pltpu.make_async_copy(
                    tail.at[part], to.at[k, :, pl.ds(1024, 512)], sems.at[1, slot, k]
                ),
            ]
    for copy in copies:
        copy.start()
    de[...] = ln_back(dln, xhat, inv_ln, gain_of(norms, 2))
    for copy in copies:
        copy.wait()


SMEM = pl.BlockSpec(memory_space=pltpu.SMEM)
VMEM = pl.BlockSpec(memory_space=pltpu.VMEM)
ANY = pl.BlockSpec(memory_space=pl.ANY)


def shaped(*pairs):
    return [jax.ShapeDtypeStruct(shape, dtype) for shape, dtype in pairs]


def pin(array):
    return pltpu.with_memory_space_constraint(array, pltpu.HBM)


def call(kernel, name, in_specs, out_specs, outs, scratch, flops, after=(), carry=()):
    n_in, n_extra, n_out = len(in_specs), len(after) + len(carry), len(outs)

    def body(*refs):
        first = n_in + n_extra
        kernel(*refs[:n_in], *refs[first : first + n_out], *refs[first + n_out + len(carry) :])

    made = pl.pallas_call(
        body,
        name=name,
        in_specs=in_specs + [ANY] * n_extra,
        out_specs=out_specs + [ANY] * len(carry),
        out_shape=outs + [jax.ShapeDtypeStruct(a.shape, a.dtype) for a in carry],
        scratch_shapes=scratch,
        input_output_aliases={n_in + len(after) + i: n_out + i for i in range(len(carry))},
        compiler_params=pltpu.CompilerParams(vmem_limit_bytes=vmem_cap),
        cost_estimate=pl.CostEstimate(flops=flops, bytes_accessed=10**6, transcendentals=0),
    )

    def run(*args):
        res = made(*args, *after, *carry)
        return (*res[:n_out], list(res[n_out:]))

    return run


DMA = pltpu.SemaphoreType.DMA
ROWS2 = (512, 512)


def attn_fwd(at, marked, xs, norms, w, after=(), carry=()):
    outs = shaped((ROWS2, f32), ((8, 512), f32)) + [pltpu.HBM(ROWS2, bf16)] * 6
    scratch = [
        *[pltpu.VMEM(ROWS2, bf16)] * 3,
        pltpu.VMEM(ROWS2, f32),
        *[pltpu.VMEM(ROWS2, bf16)] * 6,
        DMA((6,)),
    ]
    x1, lse, *saved, carried = call(
        functools.partial(attn_fwd_kernel, bool(xs), at),
        "attn_fwd",
        [VMEM] * (5 + len(xs)),
        [VMEM] * 2 + [ANY] * 6,
        outs,
        scratch,
        10**10,
        after,
        carry,
    )(*marked, norms, *w, *xs)
    return x1, (lse, *saved), carried


def mlp_fwd(at, x1, norms, w, after=(), carry=()):
    return call(
        functools.partial(mlp_fwd_kernel, len(w), at),
        "mlp_fwd",
        [VMEM] * (2 + len(w)),
        [VMEM] * 2,
        shaped((ROWS2, f32), ((256, 512), bf16)),
        [pltpu.VMEM(ROWS2, bf16)],
        8 * 10**9,
        after,
        carry,
    )(x1, norms, *w)


def mlp_bwd(at, ids, x1, dys, norms, w, after=(), carry=()):
    scratch = [
        *[pltpu.VMEM(ROWS2, bf16)] * 4,
        *[pltpu.VMEM(ROWS2, f32)] * len(dys),
    ]
    return call(
        functools.partial(mlp_bwd_kernel, len(dys) == 2, len(w), at),
        "mlp_bwd",
        [SMEM] + [VMEM] * (2 + len(w) + len(dys)),
        [VMEM] * 4,
        shaped((ROWS2, f32), ((8, 512), f32), *[((4, 4, 32, 2048), bf16)] * 2),
        scratch,
        15 * 10**9,
        after,
        carry,
    )(ids, x1, norms, *w, *dys)


def attn_bwd(at, ids, marked, xs, dx1, norms, saved, w, other_small=(), after=(), carry=()):
    width = 1024 + 128 * len(other_small)
    scratch = [
        pltpu.VMEM(ROWS2, bf16),
        pltpu.VMEM(ROWS2, f32),
        *[pltpu.VMEM(ROWS2, bf16)] * 13,
        DMA((6,)),
    ]
    outs = shaped(
        (ROWS2, f32), ((256, 512), bf16), ((8, 512), f32), *[((4, 4, 32, width), bf16)] * 2
    )
    return call(
        functools.partial(attn_bwd_kernel, bool(xs), bool(other_small), at),
        "attn_bwd",
        [SMEM] + [VMEM] * 7 + [ANY] * 6 + [VMEM] * (len(xs) + len(other_small)),
        [VMEM] * 5,
        outs,
        scratch,
        15 * 10**9,
        after,
        carry,
    )(ids, *marked, dx1, norms, saved[0], *w, *map(pin, saved[1:]), *xs, *other_small)


def code_prep(book_t, after=(), carry=()):
    codes = book_t.shape[1]
    return call(
        code_prep_kernel,
        "code_prep",
        [VMEM],
        [VMEM] * 2,
        shaped(((codes, 256), bf16), ((128, codes), bf16)),
        [],
        6 * 10**9,
        after,
        carry,
    )(book_t)


def vq_fwd(e, norms, vq_w, stack, stack_t, after=(), carry=()):
    return call(
        vq_fwd_kernel,
        "vq_fwd",
        [VMEM] * 3 + [ANY] * 2,
        [VMEM] * 2,
        shaped((ROWS2, f32), ((72, 512), f32)),
        [
            pltpu.VMEM((128, 512), f32),
            pltpu.VMEM(stack.shape, bf16),
            pltpu.VMEM(stack_t.shape, bf16),
            DMA((2, 4)),
        ],
        15 * 10**9,
        after,
        carry,
    )(e, norms, vq_w, pin(stack), pin(stack_t))


def vq_bwd(ids, e, du, norms, vq_w, codes, kept, smalls, after=(), carry=()):
    scratch = [
        pltpu.VMEM((96, 512), f32),
        pltpu.VMEM(codes[2].shape, bf16),
        pltpu.VMEM((96, 512), f32),
        pltpu.VMEM((8, 32, 512), bf16),
        *[pltpu.VMEM(a.shape, a.dtype) for a in codes],
        DMA((3, 4)),
        DMA((2, 2, 4)),
    ]
    return call(
        vq_bwd_kernel,
        "vq_bwd",
        [SMEM] + [VMEM] * 4 + [ANY] * 3 + [VMEM] * 3,
        [VMEM] + [ANY] * 2,
        shaped((ROWS2, f32), *[((4, 32, 1536), bf16)] * 2),
        scratch,
        25 * 10**9,
        after,
        carry,
    )(ids, e, du, norms, vq_w, *map(pin, codes), kept, *smalls)


def lines_kernel(cuts, *refs):
    first = 0
    for out, width in zip(refs[4:], cuts):
        for k in range(4):
            out[k] = refs[k][:, first : first + width]
        first += width


def stack_lines(shards, cuts, after=(), carry=()):
    return call(
        functools.partial(lines_kernel, cuts),
        "stack_lines",
        [VMEM] * 4,
        [VMEM] * len(cuts),
        shaped(*[((4, 32, width), bf16) for width in cuts]),
        [],
        1,
        after,
        carry,
    )(*shards)


def quads_kernel(*refs):
    for i in range(4):
        refs[4][i] = refs[i][...]


def stack_quads(quads, after=(), carry=()):
    return call(
        quads_kernel,
        "stack_quads",
        [VMEM] * 4,
        [VMEM],
        shaped(((4, *quads[0].shape), bf16)),
        [],
        1,
        after,
        carry,
    )(*quads)


def pack_kernel(*refs):
    hbm, (enc, dec_attn, dec_mlp), held, sems = refs[:4], refs[4:7], refs[7:11], refs[11]
    copies = [pltpu.make_async_copy(hbm[at], held[at], sems.at[at]) for at in range(4)]
    start_all(copies)
    wait_all(copies)
    qkv, out_t, up, down_t = held
    for layer, (attn, mlp, first) in enumerate(((enc, enc, 1024), (dec_attn, dec_mlp, 0))):
        for index in range(3):
            attn[:, index * 256 : (index + 1) * 256] = qkv[layer, index]
        attn[:, 768:1024] = out_t[layer]
        mlp[:, first : first + 1024] = up[layer]
        mlp[:, first + 1024 : first + 2048] = down_t[layer]


def pack_weights(*arrays):
    return call(
        pack_kernel,
        "pack_weights",
        [ANY] * 4,
        [VMEM] * 3,
        shaped(((32, 3072), bf16), ((32, 1024), bf16), ((32, 2048), bf16)),
        [*[pltpu.VMEM(a.shape, a.dtype) for a in arrays], DMA((4,))],
        1,
    )(*map(pin, arrays))[:-1]


def rows_in_kernel(ids, *refs):
    hbm, (own, send, norms, vq_w), held, sems = refs[:7], refs[7:11], refs[11:18], refs[18]
    copies = [pltpu.make_async_copy(hbm[at], held[at], sems.at[at]) for at in range(7)]
    start_all(copies)
    matrix = order_matrix(ids[0], False)
    wait_all(copies)
    tokens, segs, cot, gains, biases, in_t, out_w = held
    for to, micro in ((send, 1 - ids[1]), (own, ids[1])):
        to[:, :512] = ordered(tokens[micro], matrix).astype(bf16)
        ids_row = segs[pl.ds(micro, 1), :].astype(f32)
        to[:, 512:640] = jnp.broadcast_to(ids_row, (128, 256)).T.astype(bf16)
    send[:, 640:] = ordered(cot[1 - ids[1]].astype(bf16), matrix).astype(bf16)
    pad = jnp.zeros((3, 512), f32)
    rows = jnp.concatenate([gains[...], pad, biases[...], pad], axis=0)
    norms[...] = ordered(rows, matrix)
    vq_w[...] = ordered(jnp.concatenate([in_t[...], out_w[...]], axis=0), matrix)


def rows_in(ids, *arrays):
    outs = shaped(
        ((256, 640), bf16), ((256, 1152), bf16), ((16, 512), f32), ((64, 512), f32)
    )
    return call(
        rows_in_kernel,
        "rows_in",
        [SMEM] + [ANY] * 7,
        [VMEM] * 4,
        outs,
        [*[pltpu.VMEM(a.shape, a.dtype) for a in arrays], DMA((7,))],
        1,
    )(ids, *map(pin, arrays))[:-1]


def joined(block):
    return block[0:16, 1024:].astype(f32) + block[16:32, 1024:].astype(f32)


def put_small(value, own, blocks):
    hi, lo = split2(value)
    own[0:16, 1024:] = hi.astype(f32) + lo.astype(f32)
    for block in blocks:
        block[0:16, 1024:] = hi
        block[16:32, 1024:] = lo


def near_kernel(ids, ins, outs):
    keep, other = ins
    for i in range(4):
        outs[i][...] = (keep[i].astype(f32) + other[i].astype(f32)).astype(outs[i].dtype)
    if keep.shape[3] == 1152:
        value = joined(keep.at[0, 0]) + joined(other.at[0, 0])
        put_small(value, outs[0].at[0], [out.at[0] for out in outs[1:]])


def near_task(keep, other):
    shape = keep.shape[1:]
    return near_kernel, [keep, other], shaped((shape, f32), *[(shape, bf16)] * 3)


def fork_kernel(ids, ins, outs):
    keep, other = ins
    for at, (own, send, kept, sent) in enumerate(((outs[0], outs[1], (0, 2), (1, 3)), (outs[2], outs[3], (0, 1), (2, 3)))):
        cols = slice(1024 * at, 1024 * (at + 1))
        for j in range(2):
            for out, i in ((own, kept[j]), (send, sent[j])):
                total = keep[i, :, :, cols].astype(f32) + other[i, :, :, cols].astype(f32)
                out[j] = total.astype(out.dtype)


def fork_task(keep, other):
    shape = (2, *keep.shape[1:3], 1024)
    return fork_kernel, [keep, other], shaped(*[(shape, f32), (shape, bf16)] * 2)


def half_kernel(ids, ins, outs):
    own, other = ins
    for j in range(2):
        outs[j][...] = (own[j] + other[j].astype(f32)).astype(outs[j].dtype)


def half_task(own, other):
    shape = own.shape[1:]
    return half_kernel, [own, other], shaped((shape, f32), (shape, bf16))


def join_kernel(ids, ins, outs):
    for at in range(2):
        own, other = ins[2 * at : 2 * at + 2]
        for k in range(4):
            total = own[k] + other[k].astype(f32)
            outs[k][:, 1024 * at : 1024 * (at + 1)] = total.astype(outs[k].dtype)


def join_task(own_up, other_up, own_down, other_down):
    outs = shaped(((32, 2048), f32), *[((32, 2048), bf16)] * 3)
    return join_kernel, [own_up, other_up, own_down, other_down], outs


def plane_kernel(ids, ins, outs):
    for k in range(4):
        total = ins[0][k]
        for other in ins[1:]:
            total = total + other[k].astype(f32)
        outs[k][...] = total.astype(outs[k].dtype)
    if ins[0].shape[2] == 1152:
        x, y, xy = [joined(other.at[0]) for other in ins[1:]]
        put_small((ins[0][0, 0:16, 1024:] + x) + (y + xy), outs[0], outs[1:])


def plane_task(own, others):
    shape = own.shape[1:]
    return plane_kernel, [own, *others], shaped((shape, f32), *[(shape, bf16)] * 3)


def plane_join_kernel(ids, ins, outs):
    plane_kernel(ids, ins[:4], [out.at[:, pl.ds(0, 1024)] for out in outs])
    for part, out in zip(ins[4:], outs):
        out[:, 1024:] = part[...]


def plane_join_task(own, others, *parts):
    outs = shaped(((32, 3072), f32), *[((32, 3072), bf16)] * 3)
    return plane_join_kernel, [own, *others, *parts], outs


def line_total(ins, width):
    total = ins[0][:, :width]
    for other in ins[1:]:
        total = total + other[:, :width].astype(f32)
    return total


def rows_kernel(ids, ins, outs):
    own, other = ins
    half = other.shape[0]
    matrix = order_matrix(ids[0], True)
    outs[0][ids[1]] = ordered(own[0:half, :], matrix)
    outs[0][1 - ids[1]] = ordered(other[...], matrix)


def rows_task(own, other):
    return rows_kernel, [own, other], shaped(((2, *other.shape), f32))


def code_small(ref):
    return ref[:, 1024:1280].astype(f32) + ref[:, 1280:1536].astype(f32)


def code_sum(refs, out):
    total, small = refs[0][:, :1024].astype(f32), code_small(refs[0])
    for ref in refs[1:]:
        total = total + ref[:, :1024].astype(f32)
        small = small + code_small(ref)
    hi, lo = split2(small)
    out[:, :1024] = total.astype(bf16)
    out[:, 1024:1280] = hi
    out[:, 1280:1536] = lo


def code_near_kernel(ids, ins, outs):
    for k in range(4):
        code_sum([ref.at[k] for ref in ins], outs[k])


def code_near_task(keep, other):
    return code_near_kernel, [keep, other], shaped(*[(keep.shape[1:], bf16)] * 4)


def code_add_kernel(ids, ins, outs):
    code_sum(ins, outs[0])


def code_add_task(*parts):
    return code_add_kernel, list(parts), shaped((parts[0].shape, bf16))


def code_line_kernel(ids, ins, outs):
    for k in range(4):
        outs[0][k] = ins[k][...]


def code_line_task(*parts):
    return code_line_kernel, list(parts), shaped(((4, *parts[0].shape), bf16))


def finish_kernel(ids, ins, outs):
    mlp, attn, dec, code, code_other = ins[:4], ins[4:8], ins[8:12], *ins[12:]
    qkv, out_t, up, down_t, book, vq_in, vq_out, gains, biases, dec_biases, small_ref = outs
    both = line_total(dec, 3072)
    for layer, rows in enumerate((line_total(mlp, 2048), both[:, 1024:])):
        up[layer] = rows[:, :1024]
        down_t[layer] = rows[:, 1024:]
    for layer, rows in enumerate((line_total(attn, 1024), both[:, :1024])):
        for index in range(3):
            qkv[layer, index] = rows[:, index * 256 : (index + 1) * 256]
        out_t[layer] = rows[:, 768:]
    core, z = ids[0] % 2, ids[0] // 4
    for at, parts in ((core, code), (1 - core, code_other)):
        for k in range(4):
            part = at * 4 + (z ^ k)
            book[:, pl.ds(pl.multiple_of(part * 1024, 1024), 1024)] = parts[k, :, :1024].astype(f32)
            small_ref[:, pl.ds(pl.multiple_of(part * 256, 256), 256)] = code_small(parts.at[k])
    small = small_ref[...]
    vq_in[...] = small[:, :512]
    vq_out[...] = small[:, 512:1024]
    rest = small[:, 1024:1536]
    k1, k2, k3 = [joined(other) for other in attn[1:]]
    packed = (attn[0][0:16, 1024:] + k1) + (k2 + k3)
    for row, out in enumerate((gains.at[0:1], biases.at[0:1], gains.at[1:2], biases.at[1:2])):
        for j in range(4):
            out[:, 128 * j : 128 * (j + 1)] = packed[row * 4 + j : row * 4 + j + 1, :]
    gains[2:3, :] = rest[0:1, :]
    biases[2:3, :] = rest[1:2, :]
    gains[3:4, :] = rest[2:3, :]
    dec_biases[0:1, :] = rest[3:4, :]
    gains[4:5, :] = rest[4:5, :]
    dec_biases[1:2, :] = rest[5:6, :]


def finish_task(own_m, line_m, own_a, line_a, own_d, line_d, code, code_other):
    outs = shaped(
        ((2, 3, 32, 256), f32),
        ((2, 32, 256), f32),
        ((2, 32, 1024), f32),
        ((2, 32, 1024), f32),
        ((32, 8192), f32),
        ((32, 512), f32),
        ((32, 512), f32),
        ((5, 512), f32),
        ((3, 512), f32),
        ((2, 512), f32),
        ((32, 2048), f32),
    )
    ins = [own_m, *line_m, own_a, *line_a, own_d, *line_d, code, code_other]
    return finish_kernel, ins, outs


def run_tasks(ids, name, tasks, after=(), carry=()):
    sizes = [(len(ins), len(outs)) for _, ins, outs in tasks]
    n_in = sum(i for i, _ in sizes)

    def kernel(ids_ref, *refs):
        at_in, at_out = 0, n_in
        for (fn, _, _), (i, o) in zip(tasks, sizes):
            fn(ids_ref, refs[at_in : at_in + i], refs[at_out : at_out + o])
            at_in, at_out = at_in + i, at_out + o

    outs = [one for _, _, many in tasks for one in many]
    res = call(
        kernel, name, [SMEM] + [VMEM] * n_in, [VMEM] * len(outs), outs, [], 10**9, after, carry
    )(ids, *[one for _, many, _ in tasks for one in many])
    split, at = [], 0
    for _, o in sizes:
        split.append(res[at : at + o])
        at += o
    return (*split, res[-1])


def whole_groups(
    n_dp,
    tokens,
    segment_ids,
    norm_gains,
    norm_biases,
    w_qkv,
    w_attn_out,
    w_up,
    w_down,
    w_vq_in,
    w_vq_out,
    codebook,
    cotangent,
):
    dp_at, tp_at = lax.axis_index("dp"), lax.axis_index("tp")
    ids = jnp.stack([dp_at, tp_at]).astype(jnp.int32)

    def swap(values):
        return exchange(values, 0, 1, n_dp)

    def core(values):
        return [values, exchange(values, 1, 0, n_dp)]

    book_t = codebook.T
    enc_shard, attn_shard, mlp_shard = pack_weights(
        w_qkv, w_attn_out.transpose(0, 2, 1), w_up, w_down.transpose(0, 2, 1)
    )
    enc_shards = spread_line(enc_shard, n_dp)
    own, send, norms, vq_w = rows_in(
        ids,
        tokens,
        segment_ids,
        cotangent,
        norm_gains,
        norm_biases,
        w_vq_in.T,
        w_vq_out,
    )
    marked = [own, swap(send)]

    attn_line, mlp_line, _ = stack_lines(enc_shards, [1024, 2048])
    stack, stack_t, _ = code_prep(book_t, [attn_line])
    codes = (stack, stack_t, book_t)
    quads, (mlp_line,) = stack_quads(
        plane_quads(attn_line, n_dp), [stack_t, marked[1]], [mlp_line]
    )
    enc_attn, quads = core(quads), plane_quads(mlp_line, n_dp)
    e_x1, e_saved, (attn_shard,) = attn_fwd(
        0, marked, [], norms, enc_attn, carry=[attn_shard]
    )
    attn_line, _ = stack_lines(spread_line(attn_shard, n_dp), [1024], [e_x1])
    quads, (mlp_shard,) = stack_quads(quads, [attn_line], [mlp_shard])
    enc_mlp, quads = core(quads), plane_quads(attn_line, n_dp)
    mlp_shards = spread_line(mlp_shard, n_dp)
    e, _, _ = mlp_fwd(1, e_x1, norms, enc_mlp)
    up_line, down_line, _ = stack_lines(mlp_shards, [1024, 1024], [e])
    quads, (up_line,) = stack_quads(quads, [e], [up_line])
    dec_attn, quads = core(quads), plane_quads(up_line, n_dp)
    u, kept, _ = vq_fwd(e, norms, vq_w, stack, stack_t)
    quads, (down_line,) = stack_quads(quads, [u, dec_attn[1]], [down_line])
    dec_up, quads = core(quads), plane_quads(down_line, n_dp)
    d_x1, d_saved, _ = attn_fwd(3, marked, [u], norms, dec_attn)
    quads, _ = stack_quads(quads, [d_x1, dec_up[1]])
    dec_mlp = dec_up + core(quads)

    dx1, d_small1, keep_m, send_m, _ = mlp_bwd(
        4, ids, d_x1, [cotangent, marked[1]], norms, dec_mlp
    )
    near_m = exchange(send_m, 1, 0, n_dp)
    du, _, d_small0, keep_a, send_a, (keep_m,) = attn_bwd(
        3, ids, marked, [u], dx1, norms, d_saved, dec_attn, carry=[keep_m]
    )
    (own_m, *lows_m), (send_a,) = run_tasks(
        ids, "sums1", [near_task(keep_m, near_m)], carry=[send_a]
    )
    plane_m, near_a = plane_send(lows_m, n_dp), exchange(send_a, 1, 0, n_dp)
    de, code, code_send, (own_m, keep_a) = vq_bwd(
        ids,
        e,
        du,
        norms,
        vq_w,
        codes,
        kept,
        [d_small0, d_small1],
        lows_m,
        [own_m, keep_a],
    )
    d_mlp, (own_a, *lows_a), (code_send,) = run_tasks(
        ids, "sums2", [plane_task(own_m, plane_m), near_task(keep_a, near_a)], carry=[code_send]
    )
    plane_a, code_other = plane_send(lows_a, n_dp), exchange(code_send, 1, 0, n_dp)
    code_parts, _ = run_tasks(ids, "sums2b", [code_near_task(code, code_other)])
    code, *code_others = code_parts[0], *line_send(code_parts[1:], n_dp)
    ex1, e_small1, keep_m, send_m, (own_a,) = mlp_bwd(
        1, ids, e_x1, [de], norms, enc_mlp, [*lows_a, code_parts[1]], [own_a]
    )
    (own_d, *lows_d), (code,), (keep_m, send_m, d_x1) = run_tasks(
        ids,
        "sums3",
        [plane_join_task(own_a, plane_a, *d_mlp), code_add_task(code, *code_others)],
        carry=[keep_m, send_m, d_x1],
    )
    near_m, code_other = exchange(send_m, 1, 0, n_dp), exchange(code, 0, 1, n_dp)
    line_d = line_send(lows_d, n_dp)
    y, y_theirs, _ = mlp_fwd(4, d_x1, norms, dec_mlp)
    (own_up, send_up, own_down, send_down), (code,), (y_theirs,) = run_tasks(
        ids,
        "sums3b",
        [fork_task(keep_m, near_m), code_add_task(code, code_other)],
        carry=[y_theirs],
    )
    other_up, other_down = exchange(send_up, 0, 1, n_dp), exchange(send_down, 2, 0, n_dp)
    code_other, y_other = exchange(code, 2, 0, n_dp), swap(y_theirs)
    dx, dx_low, _, keep_a, send_a, (own_up, own_down) = attn_bwd(
        0,
        ids,
        marked,
        [],
        ex1,
        norms,
        e_saved,
        enc_attn,
        [e_small1],
        [send_up, send_down, code],
        [own_up, own_down],
    )
    (own_up, send_up), (own_down, send_down), (code,), (decoded,), (keep_a, send_a, dx_low) = run_tasks(
        ids,
        "sums4",
        [
            half_task(own_up, other_up),
            half_task(own_down, other_down),
            code_add_task(code, code_other),
            rows_task(y, y_other),
        ],
        line_d,
        [keep_a, send_a, dx_low],
    )
    near_a, code_others = exchange(send_a, 1, 0, n_dp), line_send([code] * 3, n_dp)
    other_up, other_down = exchange(send_up, 2, 0, n_dp), exchange(send_down, 0, 1, n_dp)
    (own_a, *lows_a), (code,), (own_up, own_down, dx_low) = run_tasks(
        ids,
        "sums4b",
        [near_task(keep_a, near_a), code_line_task(code, *code_others)],
        carry=[own_up, own_down, dx_low],
    )
    plane_a, code_other = plane_send(lows_a, n_dp), exchange(code, 1, 0, n_dp)
    dx_other = swap(dx_low)
    (own_m, *lows_m), (own_a,) = run_tasks(
        ids, "sums5", [join_task(own_up, other_up, own_down, other_down)], lows_a, [own_a]
    )
    line_m = line_send(lows_m, n_dp)
    (own_a, *lows_a), (grad_tokens,), (own_m,) = run_tasks(
        ids, "sums6", [plane_task(own_a, plane_a), rows_task(dx, dx_other)], lows_m, [own_m]
    )
    line_a = line_send(lows_a, n_dp)
    (qkv, out_t, up, down_t, book, vq_in, vq_out, *norms, _), _ = run_tasks(
        ids,
        "finish",
        [finish_task(own_m, line_m, own_a, line_a, own_d, line_d, code, code_other)],
    )
    return (
        decoded,
        grad_tokens,
        *norms,
        qkv,
        out_t.transpose(0, 2, 1),
        up,
        down_t.transpose(0, 2, 1),
        vq_in.T,
        vq_out,
        book.T,
    )


def layer_norm(values, norm_gain, norm_bias):
    centred = values - jnp.mean(values, axis=-1, keepdims=True)
    spread = jnp.mean(centred * centred, axis=-1, keepdims=True)
    return centred * lax.rsqrt(spread + ln_eps) * norm_gain + norm_bias


def gelu_tanh(values):
    return (
        0.5 * values * (1.0 + jnp.tanh(gelu_coef * (values + 0.044715 * values * values * values)))
    )


def matmul(former, latter):
    return jnp.dot(former, latter, precision=highest, preferred_element_type=jnp.float32)


def normalize(values):
    return values * lax.rsqrt(jnp.sum(values * values, axis=-1, keepdims=True) + norm_eps)


def quantize(in_rows, norm_gain, norm_bias, in_w, out_w, code_w):
    latent = normalize(matmul(layer_norm(in_rows, norm_gain, norm_bias), in_w))
    code_rows = normalize(code_w)
    logits = matmul(latent, code_rows.T) * temper
    row_max = jnp.max(logits, axis=-1, keepdims=True)
    numerator = jnp.exp(logits - row_max)
    assign = numerator / jnp.sum(numerator, axis=-1, keepdims=True)
    soft_code = matmul(assign, code_rows)
    offset = latent - soft_code
    vq_loss = commit_weight * 1.25 * jnp.sum(offset * offset)
    return (matmul(soft_code, out_w), vq_loss)


def product(former, latter):
    return jnp.dot(former, latter, preferred_element_type=jnp.float32)


def product_tn(former, latter):
    return lax.dot_general(
        former, latter, (((0,), (0,)), ((), ())), preferred_element_type=jnp.float32
    )


def product_nt(former, latter):
    return lax.dot_general(
        former, latter, (((1,), (1,)), ((), ())), preferred_element_type=jnp.float32
    )


def split_heads(values):
    return values.reshape(values.shape[0], values.shape[1] // HEAD_DIM, HEAD_DIM).transpose(1, 0, 2)


def join_heads(values):
    return values.transpose(1, 0, 2).reshape(values.shape[1], values.shape[0] * HEAD_DIM)


def masked_scores(query_blk, key_h, seg_blk, seg_keys):
    scores = jnp.einsum(
        "hqd,hkd->hqk", query_blk, key_h, preferred_element_type=jnp.float32
    ) * HEAD_DIM ** (-0.5)
    return jnp.where((seg_blk[:, None] == seg_keys[None, :])[None], scores, masked_score)


def attend(query_h, key_h, value_h, seg_keys):
    block_rows = min(512, query_h.shape[1])
    block_count = query_h.shape[1] // block_rows

    def one_block(begin_row):
        query_blk = lax.dynamic_slice_in_dim(query_h, begin_row, block_rows, 1)
        seg_blk = lax.dynamic_slice_in_dim(seg_keys, begin_row, block_rows, 0)
        scores = masked_scores(query_blk, key_h, seg_blk, seg_keys)
        row_max = jnp.max(scores, axis=-1, keepdims=True)
        numerator = jnp.exp(scores - row_max)
        row_total = jnp.sum(numerator, axis=-1, keepdims=True)
        prob_low = (numerator / row_total).astype(jnp.bfloat16)
        attended = jnp.einsum("hqk,hkd->hqd", prob_low, value_h, preferred_element_type=jnp.float32)
        return (attended.astype(jnp.bfloat16), (row_max + jnp.log(row_total))[..., 0])

    starts = jnp.arange(block_count, dtype=jnp.int32) * block_rows
    attended, log_sums = lax.map(one_block, starts)
    heads_out = attended.transpose(1, 0, 2, 3).reshape(query_h.shape)
    log_sums = log_sums.transpose(1, 0, 2).reshape(query_h.shape[0], query_h.shape[1])
    return (heads_out, log_sums)


def attend_back(query_h, key_h, value_h, seg_keys, log_sums, grad_out):
    block_rows = min(512, query_h.shape[1])
    block_count = query_h.shape[1] // block_rows

    def one_block(carry, begin_row):
        grad_key, grad_value = carry
        query_blk = lax.dynamic_slice_in_dim(query_h, begin_row, block_rows, 1)
        grad_blk = lax.dynamic_slice_in_dim(grad_out, begin_row, block_rows, 1)
        lse_blk = lax.dynamic_slice_in_dim(log_sums, begin_row, block_rows, 1)
        seg_blk = lax.dynamic_slice_in_dim(seg_keys, begin_row, block_rows, 0)
        scores = masked_scores(query_blk, key_h, seg_blk, seg_keys)
        probs = jnp.exp(scores - lse_blk[..., None])
        prob_low = probs.astype(jnp.bfloat16)
        grad_value = grad_value + jnp.einsum(
            "hqk,hqd->hkd", prob_low, grad_blk, preferred_element_type=jnp.float32
        )
        grad_prob = jnp.einsum(
            "hqd,hkd->hqk", grad_blk, value_h, preferred_element_type=jnp.float32
        )
        row_dot = jnp.sum(probs * grad_prob, axis=-1, keepdims=True)
        grad_score = (probs * (grad_prob - row_dot) * HEAD_DIM ** (-0.5)).astype(jnp.bfloat16)
        grad_query = jnp.einsum(
            "hqk,hkd->hqd", grad_score, key_h, preferred_element_type=jnp.float32
        )
        grad_key = grad_key + jnp.einsum(
            "hqk,hqd->hkd", grad_score, query_blk, preferred_element_type=jnp.float32
        )
        return ((grad_key, grad_value), grad_query)

    starts = jnp.arange(block_count, dtype=jnp.int32) * block_rows
    zeros_kv = jnp.zeros(key_h.shape, jnp.float32)
    (grad_key, grad_value), grad_query = lax.scan(one_block, (zeros_kv, zeros_kv), starts)
    grad_query = grad_query.transpose(1, 0, 2, 3).reshape(query_h.shape)
    return (
        grad_query.astype(jnp.bfloat16),
        grad_key.astype(jnp.bfloat16),
        grad_value.astype(jnp.bfloat16),
    )


def spread_rows(values):
    return lax.all_gather(values, "tp", axis=0, tiled=True)


def combine_rows(partial_value):
    return lax.psum_scatter(partial_value, "tp", scatter_dimension=0, tiled=True)


def spread_grads(values):
    return lax.all_gather(values, "tp", axis=0, tiled=True)


def combine_grads(partial_value):
    return lax.psum_scatter(
        partial_value.astype(jnp.bfloat16), "tp", scatter_dimension=0, tiled=True
    ).astype(jnp.float32)


def fetch_weights(w_qkv, w_attn_out, w_up, w_down, layer):
    return (
        lax.all_gather(w_qkv[layer], "dp", axis=1, tiled=True),
        lax.all_gather(w_attn_out[layer], "dp", axis=1, tiled=True),
        lax.all_gather(w_up[layer], "dp", axis=0, tiled=True),
        lax.all_gather(w_down[layer], "dp", axis=1, tiled=True),
    )


def reduce_weight_grads(grads):
    return (
        lax.psum_scatter(
            grads[0].astype(jnp.bfloat16), "dp", scatter_dimension=1, tiled=True
        ).astype(jnp.float32),
        lax.psum_scatter(
            grads[1].astype(jnp.bfloat16), "dp", scatter_dimension=1, tiled=True
        ).astype(jnp.float32),
        lax.psum_scatter(
            grads[2].astype(jnp.bfloat16), "dp", scatter_dimension=0, tiled=True
        ).astype(jnp.float32),
        lax.psum_scatter(
            grads[3].astype(jnp.bfloat16), "dp", scatter_dimension=1, tiled=True
        ).astype(jnp.float32),
    )


def block_forward(resid_in, seg_local, gains, biases, weights):
    qkv_w, attn_w, up_w, down_w = weights
    normed = layer_norm(resid_in, gains[0], biases[0]).astype(jnp.bfloat16)
    normed_all, seg_all = (
        lax.all_gather(normed, "tp", axis=0, tiled=True),
        lax.all_gather(seg_local, "tp", axis=0, tiled=True),
    )
    query_h = split_heads(product(normed_all, qkv_w[0]).astype(jnp.bfloat16))
    key_h = split_heads(product(normed_all, qkv_w[1]).astype(jnp.bfloat16))
    value_h = split_heads(product(normed_all, qkv_w[2]).astype(jnp.bfloat16))
    heads_out, log_sums = attend(query_h, key_h, value_h, seg_all)
    attn_rows = join_heads(heads_out)
    middle = resid_in + combine_rows(product(attn_rows, attn_w))
    normed_mid = spread_rows(layer_norm(middle, gains[1], biases[1]).astype(jnp.bfloat16))
    hidden_pre = product(normed_mid, up_w)
    hidden = gelu_tanh(hidden_pre).astype(jnp.bfloat16)
    result = middle + combine_rows(product(hidden, down_w))
    kept = (
        resid_in,
        middle,
        normed_all,
        seg_all,
        query_h,
        key_h,
        value_h,
        log_sums,
        attn_rows,
        normed_mid,
        hidden_pre,
        hidden,
    )
    return (result, kept)


def block_backward(kept, gains, biases, weights, grad_result):
    (
        resid_in,
        middle,
        normed_all,
        seg_all,
        query_h,
        key_h,
        value_h,
        log_sums,
        attn_rows,
        normed_mid,
        hidden_pre,
        hidden,
    ) = kept
    qkv_w, attn_w, up_w, down_w = weights
    grad_branch = spread_grads(grad_result.astype(jnp.bfloat16))
    grad_down = product_tn(hidden, grad_branch)
    grad_hidden = product_nt(grad_branch, down_w)
    _, gelu_back = jax.vjp(gelu_tanh, hidden_pre)
    grad_pre = gelu_back(grad_hidden)[0].astype(jnp.bfloat16)
    grad_up = product_tn(normed_mid, grad_pre)
    grad_norm_mid = combine_grads(product_nt(grad_pre, up_w))
    _, norm_back_mid = jax.vjp(layer_norm, middle, gains[1], biases[1])
    grad_mid_ln, grad_gain_mid, grad_bias_mid = norm_back_mid(grad_norm_mid)
    grad_middle = grad_result + grad_mid_ln
    grad_attn_all = spread_grads(grad_middle.astype(jnp.bfloat16))
    grad_attn = product_tn(attn_rows, grad_attn_all)
    grad_heads = split_heads(product_nt(grad_attn_all, attn_w).astype(jnp.bfloat16))
    grad_query, grad_key, grad_value = attend_back(
        query_h, key_h, value_h, seg_all, log_sums, grad_heads
    )
    grad_parts = [join_heads(grad_query), join_heads(grad_key), join_heads(grad_value)]
    grad_qkv = jnp.stack([product_tn(normed_all, grad_part) for grad_part in grad_parts])
    grad_normed_part = (
        product_nt(grad_parts[0], qkv_w[0])
        + product_nt(grad_parts[1], qkv_w[1])
        + product_nt(grad_parts[2], qkv_w[2])
    )
    grad_normed = combine_grads(grad_normed_part)
    _, norm_back_in = jax.vjp(layer_norm, resid_in, gains[0], biases[0])
    grad_in_ln, grad_gain_in, grad_bias_in = norm_back_in(grad_normed)
    gain_grads = jnp.stack([grad_gain_in, grad_gain_mid])
    bias_grads = jnp.stack([grad_bias_in, grad_bias_mid])
    return (
        grad_middle + grad_in_ln,
        gain_grads,
        bias_grads,
        (grad_qkv, grad_attn, grad_up, grad_down),
    )


def local(
    tokens,
    segment_ids,
    norm_gains,
    norm_biases,
    w_qkv,
    w_attn_out,
    w_up,
    w_down,
    w_vq_in,
    w_vq_out,
    codebook,
    cotangent,
):
    gain_sum = jnp.zeros(norm_gains.shape, jnp.float32)
    bias_sum = jnp.zeros(norm_biases.shape, jnp.float32)
    vq_in_sum = jnp.zeros(w_vq_in.shape, jnp.float32)
    vq_out_sum = jnp.zeros(w_vq_out.shape, jnp.float32)
    code_sum = jnp.zeros(codebook.shape, jnp.float32)
    layer_sums = [None, None]
    outputs = []
    input_grads = []
    for micro in range(MICRO):
        resid_in = tokens[micro].astype(jnp.float32)
        seg_local = segment_ids[micro]
        enc_weights = fetch_weights(w_qkv, w_attn_out, w_up, w_down, 0)
        encoded, enc_kept = block_forward(
            resid_in, seg_local, norm_gains[0:2], norm_biases[0:2], enc_weights
        )
        (decoder_in, _), vq_back = jax.vjp(
            quantize, encoded, norm_gains[2], norm_biases[2], w_vq_in, w_vq_out, codebook
        )
        dec_weights = fetch_weights(w_qkv, w_attn_out, w_up, w_down, 1)
        decoded, dec_kept = block_forward(
            decoder_in, seg_local, norm_gains[3:5], norm_biases[3:5], dec_weights
        )
        outputs.append(decoded)
        grad_dec_in, gains_dec, biases_dec, grads_dec = block_backward(
            dec_kept, norm_gains[3:5], norm_biases[3:5], dec_weights, cotangent[micro]
        )
        grad_encoded, grad_gain_vq, grad_bias_vq, grad_in_w, grad_out_w, grad_codes = vq_back(
            (grad_dec_in, jnp.ones((), jnp.float32))
        )
        grad_input, gains_enc, biases_enc, grads_enc = block_backward(
            enc_kept, norm_gains[0:2], norm_biases[0:2], enc_weights, grad_encoded
        )
        input_grads.append(grad_input)
        gain_sum = gain_sum + jnp.concatenate([gains_enc, grad_gain_vq[None], gains_dec], axis=0)
        bias_sum = bias_sum + jnp.concatenate([biases_enc, grad_bias_vq[None], biases_dec], axis=0)
        vq_in_sum = vq_in_sum + grad_in_w
        vq_out_sum = vq_out_sum + grad_out_w
        code_sum = code_sum + grad_codes
        for layer, grads in ((0, grads_enc), (1, grads_dec)):
            reduced = reduce_weight_grads(grads)
            if layer_sums[layer] is None:
                layer_sums[layer] = reduced
            else:
                layer_sums[layer] = jax.tree.map(jnp.add, layer_sums[layer], reduced)
    gain_tot, bias_tot, vq_in_tot, vq_out_tot, code_tot = lax.psum(
        (gain_sum, bias_sum, vq_in_sum, vq_out_sum, code_sum), ("dp", "tp")
    )
    return (
        jnp.stack(outputs),
        jnp.stack(input_grads),
        gain_tot,
        bias_tot[0:3],
        bias_tot[3:5],
        jnp.stack([layer_sums[0][0], layer_sums[1][0]]),
        jnp.stack([layer_sums[0][1], layer_sums[1][1]]),
        jnp.stack([layer_sums[0][2], layer_sums[1][2]]),
        jnp.stack([layer_sums[0][3], layer_sums[1][3]]),
        vq_in_tot,
        vq_out_tot,
        code_tot,
    )


def solution(mesh):
    n_dp, n_tp = mesh.shape["dp"], mesh.shape["tp"]
    fits = n_tp == MICRO and n_dp == 16
    return jax.shard_map(
        functools.partial(whole_groups, n_dp) if fits else local,
        mesh=mesh,
        in_specs=(
            P(None, ("dp", "tp"), None),
            P(None, ("dp", "tp")),
            P(),
            P(),
            P(None, None, "dp", "tp"),
            P(None, "tp", "dp"),
            P(None, "dp", "tp"),
            P(None, "tp", "dp"),
            P(),
            P(),
            P(),
            P(None, ("dp", "tp"), None),
        ),
        out_specs=(
            P(None, ("dp", "tp"), None),
            P(None, ("dp", "tp"), None),
            P(),
            P(),
            P(),
            P(None, None, "dp", "tp"),
            P(None, "tp", "dp"),
            P(None, "dp", "tp"),
            P(None, "tp", "dp"),
            P(),
            P(),
            P(),
        ),
        check_vma=False,
    )
```

```python
import functools

import jax
import jax.numpy as jnp
from jax import lax
from jax.experimental import pallas as pl
from jax.experimental.pallas import tpu as pltpu
from jax.sharding import PartitionSpec as P

HEAD_DIM = 64
MICRO = 2
bf16 = jnp.bfloat16
f32 = jnp.float32
highest = lax.Precision.HIGHEST
ln_eps = 1e-05
norm_eps = 1e-06
temper = 10.0
commit_weight = 64.0
gelu_coef = 0.7978845608028654
masked_score = -1e30
log2e = 1.4426950408889634
vmem_cap = 36 * 1024 * 1024


PLANE = ((0, 0), (0, 1), (1, 0), (1, 1))


def exchange(values, dp_xor, tp_xor, n_dp):
    pairs = [
        (d * 2 + t, (d ^ dp_xor) * 2 + (t ^ tp_xor)) for d in range(n_dp) for t in range(2)
    ]
    return lax.ppermute(values, ("dp", "tp"), pairs)


def spread_line(shard, n_dp):
    return [shard] + [exchange(shard, 4 * k, 0, n_dp) for k in range(1, 4)]


def plane_quads(own, n_dp):
    return [own] + [exchange(own, 2 * y, x, n_dp) for y, x in PLANE[1:]]


def plane_send(lows, n_dp):
    return [exchange(low, 2 * y, x, n_dp) for (y, x), low in zip(PLANE[1:], lows)]


def line_send(lows, n_dp):
    return [exchange(low, 4 * k, 0, n_dp) for k, low in zip(range(1, 4), lows)]


def dot(a, b):
    return jnp.dot(a, b, preferred_element_type=f32)


def dot_nt(a, b, precision=None):
    return lax.dot_general(
        a, b, (((1,), (1,)), ((), ())), preferred_element_type=f32, precision=precision
    )


def dot_full(a, b):
    return jnp.dot(a, b, preferred_element_type=f32, precision=highest)


def ln_parts(x):
    centred = x - jnp.mean(x, axis=-1, keepdims=True)
    inv = lax.rsqrt(jnp.mean(centred * centred, axis=-1, keepdims=True) + ln_eps)
    return centred * inv, inv


def ln_back(grad, xhat, inv, gain):
    scaled = grad * gain
    return inv * (
        scaled
        - jnp.mean(scaled, axis=-1, keepdims=True)
        - xhat * jnp.mean(scaled * xhat, axis=-1, keepdims=True)
    )


def split2(x):
    hi = x.astype(bf16)
    return hi, (x - hi.astype(f32)).astype(bf16)


def split3(x):
    hi, _ = split2(x)
    rest = x - hi.astype(f32)
    mid = rest.astype(bf16)
    return hi, mid, (rest - mid.astype(f32)).astype(bf16)


def order_matrix(dp, inverse):
    at = lax.broadcasted_iota(jnp.int32, (512, 512), 0 if inverse else 1)
    other = lax.broadcasted_iota(jnp.int32, (512, 512), 1 if inverse else 0)
    block = at >> 5
    bits = ((block & 3) << 2) | (((block >> 2) & 1) << 1) | (block >> 3)
    return jnp.where(other == (((dp ^ bits) << 5) | (at & 31)), 1.0, 0.0).astype(bf16)


def ordered(x, matrix):
    if x.dtype == bf16:
        return dot(x, matrix)
    hi, mid, lo = split3(x)
    return (dot(hi, matrix) + dot(mid, matrix)) + dot(lo, matrix)


def w_at(refs, t, cols):
    parts = [ref[2 * y + t, :, :, cols] for ref in refs for y in range(2)]
    return jnp.concatenate([part.reshape(128, part.shape[2]) for part in parts], axis=0)


def w_of_all(ref, ids, t, cols):
    parts = []
    for place in range(16):
        dp_xor = (place & 3) * 4 + ((place >> 2) & 1) * 2 + (place >> 3)
        parts.append(ref[(ids[0] ^ dp_xor) * 2 + (ids[1] ^ t), :, cols])
    return jnp.concatenate(parts, axis=0)


def put_grad(refs, t, cols, value):
    for core, ref in enumerate(refs):
        for y in range(2):
            rows = value[core * 256 + y * 128 : core * 256 + (y + 1) * 128]
            ref[2 * y + t, :, :, cols] = rows.reshape(4, 32, rows.shape[1])


def start_all(copies):
    for copy in copies:
        copy.start()


def wait_all(copies):
    for copy in copies:
        copy.wait()


def head_rows(ref, pair, which):
    own = ref[pl.ds(pair * 128 + which * HEAD_DIM, HEAD_DIM), :]
    zero = jnp.zeros_like(own)
    return jnp.concatenate([own, zero] if which == 0 else [zero, own], axis=0)


def segment_mask(own, other):
    ids = jnp.concatenate([own[:, 512:640], other[:, 512:640]], axis=0).astype(f32)
    return jnp.where(ids[:, 0:1] == ids.T[0:1, :], 0.0, masked_score)


def load_rows(x, own, other):
    if x is None:
        return jnp.concatenate([own[:, :512], other[:, :512]], axis=0).astype(f32)
    return x[...]


def gain_of(norms, at):
    return norms[at : at + 1, :]


def bias_of(norms, at):
    return norms[8 + at : 9 + at, :]


def attn_fwd_kernel(with_x, at, own, other, norms, w0, w1, *refs):
    x, refs = (refs[0], refs[1:]) if with_x else (None, refs)
    x1, lse, saved, refs = refs[0], refs[1], refs[2:8], refs[8:]
    h, vt, ot, mask, qs, k, v, o, qst, kt, out_sems = refs
    w = (w0, w1)
    keeps = [
        pltpu.make_async_copy(held, to, out_sems.at[i])
        for i, (held, to) in enumerate(zip((qs, k, v, o, qst, kt), saved))
    ]
    xf = load_rows(x, own, other)
    h[...] = (ln_parts(xf)[0] * gain_of(norms, at) + bias_of(norms, at)).astype(bf16)
    mask[...] = segment_mask(own, other)
    for t in range(2):
        cols = slice(t * 256, (t + 1) * 256)
        q = dot(h[...], w_at(w, t, slice(0, 256))).astype(bf16)
        qs[:, cols] = (q * HEAD_DIM ** (-0.5)).astype(bf16)
        k[:, cols] = dot(h[...], w_at(w, t, slice(256, 512))).astype(bf16)
        v[:, cols] = dot(h[...], w_at(w, t, slice(512, 768))).astype(bf16)
    qst[...] = qs[...].T
    kt[...] = k[...].T
    vt[...] = v[...].T
    for i in (0, 1, 2, 4, 5):
        keeps[i].start()
    for pair in range(4):
        k_pair = k[:, pair * 128 : (pair + 1) * 128]
        for which in range(2):
            scores = dot(k_pair, head_rows(qst, pair, which)) + mask[...]
            top = jnp.max(scores, axis=0, keepdims=True)
            numer = jnp.exp(scores - top).astype(bf16)
            rows = pl.ds(pair * 128 + which * HEAD_DIM, HEAD_DIM)
            left = jnp.concatenate([vt[rows, :], jnp.ones((16, 512), bf16)], axis=0)
            both = dot(left, numer)
            total = both[HEAD_DIM : HEAD_DIM + 1, :]
            ot[rows, :] = (both[:HEAD_DIM, :] / total).astype(bf16)
            lse[pl.ds(pair * 2 + which, 1), :] = top + jnp.log(total)
    o[...] = ot[...].T
    keeps[3].start()
    acc = xf
    for t in range(2):
        acc = acc + dot_nt(o[:, t * 256 : (t + 1) * 256], w_at(w, t, slice(768, 1024)))
    x1[...] = acc
    wait_all(keeps)


def gelu_parts(u):
    square = u * u
    tanh = jnp.tanh(gelu_coef * u * (1.0 + 0.044715 * square))
    return 0.5 * u * (1.0 + tanh), tanh, square


def mlp_weights(refs, ids):
    def weights(first):
        def take(t, part):
            cols = slice(first + part * 512, first + (part + 1) * 512)
            return w_at(refs, t, cols) if len(refs) == 2 else w_of_all(refs[0], ids, t, cols)

        return take

    return weights(0), weights(1024)


def mlp_fwd_kernel(n_w, at, ids, x1, norms, *refs):
    up, down = mlp_weights(refs[:n_w], ids)
    y, theirs, h2 = refs[n_w:]
    h2[...] = (ln_parts(x1[...])[0] * gain_of(norms, at) + bias_of(norms, at)).astype(bf16)
    acc = x1[...]
    for t in range(2):
        for part in range(2):
            hidden = gelu_parts(dot(h2[...], up(t, part)))[0].astype(bf16)
            acc = acc + dot_nt(hidden, down(t, part))
    y[...] = acc
    theirs[...] = acc[256:, :].astype(bf16)


def mlp_bwd_kernel(split, n_w, at, ids, x1, norms, *refs):
    up, down = mlp_weights(refs[:n_w], ids)
    refs = refs[n_w:]
    if split:
        own, other, refs = refs[0], refs[1], refs[2:]
    else:
        dy, refs = refs[0], refs[1:]
    dx1, small, grads = refs[0], refs[1], refs[2:4]
    h2, h2t, dyb, dybt, dh2 = refs[4:9]
    if split:
        dy = refs[9]
        dy[0:256, :] = ordered(own[ids[1]], order_matrix(ids[0], False))
        dy[256:, :] = other[:, 640:].astype(f32)
    h2[...] = (ln_parts(x1[...])[0] * gain_of(norms, at) + bias_of(norms, at)).astype(bf16)
    h2t[...] = h2[...].T
    dyb[...] = dy[...].astype(bf16)
    dybt[...] = dyb[...].T
    for t in range(2):
        for part in range(2):
            cols = slice(part * 512, (part + 1) * 512)
            w_up = up(t, part)
            pre = dot(h2[...], w_up)
            hidden, tanh, square = gelu_parts(pre)
            slope = 0.5 * (1.0 + tanh) + (0.5 * gelu_coef) * pre * (1.0 - tanh * tanh) * (
                1.0 + (3 * 0.044715) * square
            )
            dhidden = dot(dyb[...], down(t, part))
            dpre = (dhidden * slope).astype(bf16)
            out_cols = slice(1024 + part * 512, 1024 + (part + 1) * 512)
            put_grad(grads, t, out_cols, dot(dybt[...], hidden.astype(bf16)).astype(bf16))
            put_grad(grads, t, cols, dot(h2t[...], dpre).astype(bf16))
            more = dot_nt(dpre, w_up)
            if t + part == 0:
                dh2[...] = more
            else:
                dh2[...] += more
    xhat, inv = ln_parts(x1[...])
    grad = dh2[...]
    small[0:1, :] = jnp.sum(grad * xhat, axis=0, keepdims=True)
    small[1:2, :] = jnp.sum(grad, axis=0, keepdims=True)
    dx1[...] = dy[...] + ln_back(grad, xhat, inv, gain_of(norms, at))


def pack_rows(rows):
    cut = [rows[i : i + 1, 128 * j : 128 * (j + 1)] for i in range(4) for j in range(4)]
    return jnp.concatenate(split2(jnp.concatenate(cut, axis=0)), axis=0)


def attn_bwd_kernel(with_x, with_small, at, ids, own, other, dx1, norms, lse, w0, w1, *refs):
    saved, refs = refs[:6], refs[6:]
    x, refs = (refs[0], refs[1:]) if with_x else (None, refs)
    if with_small:
        other_small, refs = refs[0], refs[1:]
    dx, dx_low, small, grads = refs[0], refs[1], refs[2], refs[3:5]
    h, mask, do, dot_t, dqt, dq, dk, dv, flip, qs, k, v, o, qst, kt, in_sems = refs[5:]
    w = (w0, w1)
    takes = [
        pltpu.make_async_copy(held, to, in_sems.at[i])
        for i, (held, to) in enumerate(zip(saved, (qs, k, v, o, qst, kt)))
    ]
    start_all(takes)
    xf = load_rows(x, own, other)
    h[...] = (ln_parts(xf)[0] * gain_of(norms, at) + bias_of(norms, at)).astype(bf16)
    mask[...] = segment_mask(own, other)
    low = dx1[...].astype(bf16)
    flip[...] = low.T
    wait_all(takes)
    for t in range(2):
        cols = slice(t * 256, (t + 1) * 256)
        do[:, cols] = dot(low, w_at(w, t, slice(768, 1024))).astype(bf16)
        put_grad(grads, t, slice(768, 1024), dot(flip[...], o[:, cols]).astype(bf16))
    dot_t[...] = do[...].T
    first = lax.broadcasted_iota(jnp.int32, (512, 128), 1) < HEAD_DIM
    for pair in range(4):
        lanes = slice(pair * 128, (pair + 1) * 128)
        dvs, dks = [], []
        for which in range(2):
            head = pair * 2 + which
            rows = pl.ds(head * HEAD_DIM, HEAD_DIM)
            scores = dot(k[:, lanes], head_rows(qst, pair, which)) + mask[...]
            probs = jnp.exp(scores - lse[head : head + 1, :])
            dprobs = dot(v[:, lanes], head_rows(dot_t, pair, which))
            shift = jnp.sum(probs * dprobs, axis=0, keepdims=True)
            dscore = (probs * (dprobs - shift)).astype(bf16)
            dvs.append(dot(probs.astype(bf16), do[:, lanes]))
            dks.append(dot(dscore, qs[:, lanes]))
            dqt[rows, :] = (dot(kt[rows, :], dscore) * HEAD_DIM ** (-0.5)).astype(bf16)
        dv[:, lanes] = jnp.where(first, dvs[0], dvs[1]).astype(bf16)
        dk[:, lanes] = jnp.where(first, dks[0], dks[1]).astype(bf16)
    dq[...] = dqt[...].T
    flip[...] = h[...].T
    grad = jnp.zeros((512, 512), f32)
    for t in range(2):
        cols = slice(t * 256, (t + 1) * 256)
        for index, part in enumerate((dq, dk, dv)):
            w_cols = slice(index * 256, (index + 1) * 256)
            put_grad(grads, t, w_cols, dot(flip[...], part[:, cols]).astype(bf16))
            grad = grad + dot_nt(part[:, cols], w_at(w, t, w_cols))
    xhat, inv = ln_parts(xf)
    small[0:1, :] = jnp.sum(grad * xhat, axis=0, keepdims=True)
    small[1:2, :] = jnp.sum(grad, axis=0, keepdims=True)
    if with_small:
        rows = jnp.concatenate([small[0:2, :], other_small[0:2, :], jnp.zeros((4, 512), f32)], axis=0)
        packed = pack_rows(ordered(rows, order_matrix(ids[0], True)))
        for out in grads:
            for i in range(4):
                for z in range(4):
                    out[i, z, :, 1024:1152] = packed
    total = dx1[...] + ln_back(grad, xhat, inv, gain_of(norms, at))
    dx[...] = total
    dx_low[...] = total[256:, :].astype(bf16)


def code_prep_kernel(book_t, stack, stack_t):
    def one_chunk(index, _):
        lanes = pl.ds(pl.multiple_of(index * 512, 512), 512)
        rows = book_t[:, lanes]
        unit = rows * lax.rsqrt(jnp.sum(rows * rows, axis=0, keepdims=True) + norm_eps)
        hi, mid, lo = split3(unit)
        stack_t[:, lanes] = jnp.concatenate([hi, mid, lo, jnp.ones((32, 512), bf16)], axis=0)
        tall = jnp.concatenate([hi, mid, lo, hi, mid, hi, jnp.zeros((64, 512), bf16)], axis=0)
        stack[lanes, :] = tall.T
        return 0

    lax.fori_loop(0, book_t.shape[1] // 512, one_chunk, 0)


def factor_stack(x):
    hi, mid, lo = split3(x)
    return jnp.concatenate([hi, hi, hi, mid, mid, lo, jnp.zeros((64, x.shape[1]), bf16)], axis=0)


def code_loads(pairs, sems):
    loads = []
    for piece in range(4):
        group = []
        for at, (held, to, by_row) in enumerate(pairs):
            size = held.shape[0 if by_row else 1] // 4
            part = pl.ds(piece * size, size)
            place = (part, slice(None)) if by_row else (slice(None), part)
            group.append(pltpu.make_async_copy(held.at[place], to.at[place], sems.at[at, piece]))
        start_all(group)
        loads.append(group)
    return loads


def vq_fwd_kernel(
    e, norms, vq_w, stack_hbm, stack_t_hbm, u, kept, acc, stack, stack_t, sems
):
    loads = code_loads([(stack_hbm, stack, True), (stack_t_hbm, stack_t, False)], sems)
    lnv = ln_parts(e[...])[0] * gain_of(norms, 2) + bias_of(norms, 2)
    raw = dot_nt(vq_w[0:32, :], lnv, highest)
    inv = lax.rsqrt(jnp.sum(raw * raw, axis=0, keepdims=True) + norm_eps)
    latent = raw * inv
    right = factor_stack(latent * (temper * log2e))
    chunks = stack.shape[0] // 2048
    for piece, group in enumerate(loads):
        wait_all(group)
        for part in range(piece * chunks // 4, (piece + 1) * chunks // 4):
            numers = []
            for index in range(4 * part, 4 * part + 4):
                codes = slice(index * 512, (index + 1) * 512)
                numers.append(jnp.exp2(dot(stack[codes, :], right)).astype(bf16))
            sums = dot(
                stack_t[:, part * 2048 : (part + 1) * 2048], jnp.concatenate(numers, axis=0)
            )
            if part == 0:
                acc[...] = sums
            else:
                acc[...] += sums
    total = acc[96:97, :]
    soft = (acc[0:32, :] + acc[32:64, :] + acc[64:96, :]) / total
    kept[0:32, :] = latent
    kept[32:64, :] = soft
    kept[64:65, :] = total
    kept[65:66, :] = inv
    u[...] = dot_full(soft.T, vq_w[32:64, :])


def vq_bwd_kernel(ids, e, du, norms, vq_w, stack_hbm, stack_t_hbm, book_hbm, kept, *refs):
    small0, small1, de, code_keep, code_send = refs[:5]
    acc, grads, small, tail, stack, stack_t, book_t, load_sems, sems = refs[5:]
    loads = code_loads(
        [(stack_hbm, stack, True), (stack_t_hbm, stack_t, False), (book_hbm, book_t, False)],
        load_sems,
    )
    xhat, inv_ln = ln_parts(e[...])
    lnv = xhat * gain_of(norms, 2) + bias_of(norms, 2)
    latent, soft = kept[0:32, :], kept[32:64, :]
    total, inv = kept[64:65, :], kept[65:66, :]
    direct = (2.0 * 1.25 * commit_weight) * (latent - soft)
    dsoft = dot_nt(vq_w[32:64, :], du[...], highest) - direct
    small[32:64, :] = dot_full(soft, du[...])
    shift = jnp.sum(dsoft * soft, axis=0, keepdims=True) / total
    dsoft = dsoft / total
    right = jnp.concatenate(
        [factor_stack(latent * (temper * log2e)), factor_stack(dsoft)], axis=1
    )
    pads = jnp.zeros((64, 512), f32)

    def tall(x):
        hi, lo = split2(x)
        return jnp.concatenate([hi.astype(f32), lo.astype(f32), pads], axis=0).T.astype(bf16)

    sides = jnp.concatenate([tall(dsoft), tall(latent * temper)], axis=0)
    chunks = stack.shape[0] // 2048
    for piece, group in enumerate(loads):
        wait_all(group)
        for part in range(piece * chunks // 4, (piece + 1) * chunks // 4):
            dlogits = []
            for index in range(4 * part, 4 * part + 4):
                codes = slice(index * 512, (index + 1) * 512)
                both = dot(stack[codes, :], right)
                numer = jnp.exp2(both[:, :512])
                dlogit = (numer * (both[:, 512:] - shift)).astype(bf16)
                dlogits.append(dlogit)
                sums = jnp.concatenate([numer.astype(bf16), dlogit], axis=1)
                dcode = dot(sums, sides).T
                dcode = dcode[0:32, :] + dcode[32:64, :]
                rows = book_t[:, codes]
                scale = lax.rsqrt(jnp.sum(rows * rows, axis=0, keepdims=True) + norm_eps)
                unit = rows * scale
                grads[:, codes] = (
                    scale * (dcode - unit * jnp.sum(unit * dcode, axis=0, keepdims=True))
                ).astype(bf16)
            sums = dot(
                stack_t[0:96, part * 2048 : (part + 1) * 2048], jnp.concatenate(dlogits, axis=0)
            )
            if part == 0:
                acc[...] = sums
            else:
                acc[...] += sums
    dlatent = temper * (acc[0:32, :] + acc[32:64, :] + acc[64:96, :]) + direct
    draw = inv * (dlatent - latent * jnp.sum(latent * dlatent, axis=0, keepdims=True))
    small[0:32, :] = dot_full(draw, lnv)
    dln = dot_full(draw.T, vq_w[0:32, :])
    small[64:65, :] = jnp.sum(dln * xhat, axis=0, keepdims=True)
    small[65:66, :] = jnp.sum(dln, axis=0, keepdims=True)
    small[66:68, :] = small0[0:2, :]
    small[68:70, :] = small1[0:2, :]
    small[70:96, :] = jnp.zeros((26, 512), f32)
    small[...] = ordered(small[...], order_matrix(ids[0], True))
    for block in range(3):
        for at, part in enumerate(split2(small[block * 32 : (block + 1) * 32, :])):
            for side in range(2):
                tail[block * 2 + side, :, at * 256 : (at + 1) * 256] = part[
                    :, side * 256 : (side + 1) * 256
                ]
    tail[6:8] = jnp.zeros((2, 32, 512), bf16)
    core, z = ids[0] % 2, ids[0] // 4
    copies = []
    for slot, (at, to) in enumerate(((core, code_keep), (1 - core, code_send))):
        for k in range(4):
            part = at * 4 + (z ^ k)
            lanes = pl.ds(pl.multiple_of(part * 1024, 1024), 1024)
            copies += [
                pltpu.make_async_copy(
                    grads.at[:, lanes], to.at[k, :, pl.ds(0, 1024)], sems.at[0, slot, k]
                ),
                pltpu.make_async_copy(
                    tail.at[part], to.at[k, :, pl.ds(1024, 512)], sems.at[1, slot, k]
                ),
            ]
    for copy in copies:
        copy.start()
    de[...] = ln_back(dln, xhat, inv_ln, gain_of(norms, 2))
    for copy in copies:
        copy.wait()


SMEM = pl.BlockSpec(memory_space=pltpu.SMEM)
VMEM = pl.BlockSpec(memory_space=pltpu.VMEM)
ANY = pl.BlockSpec(memory_space=pl.ANY)


def shaped(*pairs):
    return [jax.ShapeDtypeStruct(shape, dtype) for shape, dtype in pairs]


def pin(array):
    return pltpu.with_memory_space_constraint(array, pltpu.HBM)


def call(kernel, name, in_specs, out_specs, outs, scratch, flops, after=(), carry=()):
    n_in, n_extra, n_out = len(in_specs), len(after) + len(carry), len(outs)

    def body(*refs):
        first = n_in + n_extra
        kernel(*refs[:n_in], *refs[first : first + n_out], *refs[first + n_out + len(carry) :])

    made = pl.pallas_call(
        body,
        name=name,
        in_specs=in_specs + [ANY] * n_extra,
        out_specs=out_specs + [ANY] * len(carry),
        out_shape=outs + [jax.ShapeDtypeStruct(a.shape, a.dtype) for a in carry],
        scratch_shapes=scratch,
        input_output_aliases={n_in + len(after) + i: n_out + i for i in range(len(carry))},
        compiler_params=pltpu.CompilerParams(vmem_limit_bytes=vmem_cap),
        cost_estimate=pl.CostEstimate(flops=flops, bytes_accessed=10**6, transcendentals=0),
    )

    def run(*args):
        res = made(*args, *after, *carry)
        return (*res[:n_out], list(res[n_out:]))

    return run


DMA = pltpu.SemaphoreType.DMA
ROWS2 = (512, 512)


def attn_fwd(at, marked, xs, norms, w, after=(), carry=()):
    outs = shaped((ROWS2, f32), ((8, 512), f32)) + [pltpu.HBM(ROWS2, bf16)] * 6
    scratch = [
        *[pltpu.VMEM(ROWS2, bf16)] * 3,
        pltpu.VMEM(ROWS2, f32),
        *[pltpu.VMEM(ROWS2, bf16)] * 6,
        DMA((6,)),
    ]
    x1, lse, *saved, carried = call(
        functools.partial(attn_fwd_kernel, bool(xs), at),
        "attn_fwd",
        [VMEM] * (5 + len(xs)),
        [VMEM] * 2 + [ANY] * 6,
        outs,
        scratch,
        10**10,
        after,
        carry,
    )(*marked, norms, *w, *xs)
    return x1, (lse, *saved), carried


def mlp_fwd(at, ids, x1, norms, w, after=(), carry=()):
    return call(
        functools.partial(mlp_fwd_kernel, len(w), at),
        "mlp_fwd",
        [SMEM] + [VMEM] * (2 + len(w)),
        [VMEM] * 2,
        shaped((ROWS2, f32), ((256, 512), bf16)),
        [pltpu.VMEM(ROWS2, bf16)],
        8 * 10**9,
        after,
        carry,
    )(ids, x1, norms, *w)


def mlp_bwd(at, ids, x1, dys, norms, w, after=(), carry=()):
    scratch = [
        *[pltpu.VMEM(ROWS2, bf16)] * 4,
        *[pltpu.VMEM(ROWS2, f32)] * len(dys),
    ]
    return call(
        functools.partial(mlp_bwd_kernel, len(dys) == 2, len(w), at),
        "mlp_bwd",
        [SMEM] + [VMEM] * (2 + len(w) + len(dys)),
        [VMEM] * 4,
        shaped((ROWS2, f32), ((8, 512), f32), *[((4, 4, 32, 2048), bf16)] * 2),
        scratch,
        15 * 10**9,
        after,
        carry,
    )(ids, x1, norms, *w, *dys)


def attn_bwd(at, ids, marked, xs, dx1, norms, saved, w, other_small=(), after=(), carry=()):
    width = 1024 + 128 * len(other_small)
    scratch = [
        pltpu.VMEM(ROWS2, bf16),
        pltpu.VMEM(ROWS2, f32),
        *[pltpu.VMEM(ROWS2, bf16)] * 13,
        DMA((6,)),
    ]
    outs = shaped(
        (ROWS2, f32), ((256, 512), bf16), ((8, 512), f32), *[((4, 4, 32, width), bf16)] * 2
    )
    return call(
        functools.partial(attn_bwd_kernel, bool(xs), bool(other_small), at),
        "attn_bwd",
        [SMEM] + [VMEM] * 7 + [ANY] * 6 + [VMEM] * (len(xs) + len(other_small)),
        [VMEM] * 5,
        outs,
        scratch,
        15 * 10**9,
        after,
        carry,
    )(ids, *marked, dx1, norms, saved[0], *w, *map(pin, saved[1:]), *xs, *other_small)


def code_prep(book_t, after=(), carry=()):
    codes = book_t.shape[1]
    return call(
        code_prep_kernel,
        "code_prep",
        [VMEM],
        [VMEM] * 2,
        shaped(((codes, 256), bf16), ((128, codes), bf16)),
        [],
        6 * 10**9,
        after,
        carry,
    )(book_t)


def vq_fwd(e, norms, vq_w, stack, stack_t, after=(), carry=()):
    return call(
        vq_fwd_kernel,
        "vq_fwd",
        [VMEM] * 3 + [ANY] * 2,
        [VMEM] * 2,
        shaped((ROWS2, f32), ((72, 512), f32)),
        [
            pltpu.VMEM((128, 512), f32),
            pltpu.VMEM(stack.shape, bf16),
            pltpu.VMEM(stack_t.shape, bf16),
            DMA((2, 4)),
        ],
        15 * 10**9,
        after,
        carry,
    )(e, norms, vq_w, pin(stack), pin(stack_t))


def vq_bwd(ids, e, du, norms, vq_w, codes, kept, smalls, after=(), carry=()):
    scratch = [
        pltpu.VMEM((96, 512), f32),
        pltpu.VMEM(codes[2].shape, bf16),
        pltpu.VMEM((96, 512), f32),
        pltpu.VMEM((8, 32, 512), bf16),
        *[pltpu.VMEM(a.shape, a.dtype) for a in codes],
        DMA((3, 4)),
        DMA((2, 2, 4)),
    ]
    return call(
        vq_bwd_kernel,
        "vq_bwd",
        [SMEM] + [VMEM] * 4 + [ANY] * 3 + [VMEM] * 3,
        [VMEM] + [ANY] * 2,
        shaped((ROWS2, f32), *[((4, 32, 1536), bf16)] * 2),
        scratch,
        25 * 10**9,
        after,
        carry,
    )(ids, e, du, norms, vq_w, *map(pin, codes), kept, *smalls)


def lines_kernel(cuts, *refs):
    first = 0
    for out, width in zip(refs[4:], cuts):
        for k in range(4):
            out[k] = refs[k][:, first : first + width]
        first += width


def stack_lines(shards, cuts, after=(), carry=()):
    return call(
        functools.partial(lines_kernel, cuts),
        "stack_lines",
        [VMEM] * 4,
        [VMEM] * len(cuts),
        shaped(*[((4, 32, width), bf16) for width in cuts]),
        [],
        1,
        after,
        carry,
    )(*shards)


def quads_kernel(*refs):
    for i in range(4):
        refs[4][i] = refs[i][...]


def stack_quads(quads, after=(), carry=()):
    return call(
        quads_kernel,
        "stack_quads",
        [VMEM] * 4,
        [VMEM],
        shaped(((4, *quads[0].shape), bf16)),
        [],
        1,
        after,
        carry,
    )(*quads)


def pack_kernel(*refs):
    hbm, (enc, dec_attn, dec_mlp), held, sems = refs[:4], refs[4:7], refs[7:11], refs[11]
    copies = [pltpu.make_async_copy(hbm[at], held[at], sems.at[at]) for at in range(4)]
    start_all(copies)
    wait_all(copies)
    qkv, out_t, up, down_t = held
    for layer, (attn, mlp, first) in enumerate(((enc, enc, 1024), (dec_attn, dec_mlp, 0))):
        for index in range(3):
            attn[:, index * 256 : (index + 1) * 256] = qkv[layer, index]
        attn[:, 768:1024] = out_t[layer]
        mlp[:, first : first + 1024] = up[layer]
        mlp[:, first + 1024 : first + 2048] = down_t[layer]


def pack_weights(*arrays):
    return call(
        pack_kernel,
        "pack_weights",
        [ANY] * 4,
        [VMEM] * 3,
        shaped(((32, 3072), bf16), ((32, 1024), bf16), ((32, 2048), bf16)),
        [*[pltpu.VMEM(a.shape, a.dtype) for a in arrays], DMA((4,))],
        1,
    )(*map(pin, arrays))[:-1]


def rows_in_kernel(ids, *refs):
    hbm, (own, send, norms, vq_w), held, sems = refs[:7], refs[7:11], refs[11:18], refs[18]
    copies = [pltpu.make_async_copy(hbm[at], held[at], sems.at[at]) for at in range(7)]
    start_all(copies)
    matrix = order_matrix(ids[0], False)
    wait_all(copies)
    tokens, segs, cot, gains, biases, in_t, out_w = held
    for to, micro in ((send, 1 - ids[1]), (own, ids[1])):
        to[:, :512] = ordered(tokens[micro], matrix).astype(bf16)
        ids_row = segs[pl.ds(micro, 1), :].astype(f32)
        to[:, 512:640] = jnp.broadcast_to(ids_row, (128, 256)).T.astype(bf16)
    send[:, 640:] = ordered(cot[1 - ids[1]].astype(bf16), matrix).astype(bf16)
    pad = jnp.zeros((3, 512), f32)
    rows = jnp.concatenate([gains[...], pad, biases[...], pad], axis=0)
    norms[...] = ordered(rows, matrix)
    vq_w[...] = ordered(jnp.concatenate([in_t[...], out_w[...]], axis=0), matrix)


def rows_in(ids, *arrays):
    outs = shaped(
        ((256, 640), bf16), ((256, 1152), bf16), ((16, 512), f32), ((64, 512), f32)
    )
    return call(
        rows_in_kernel,
        "rows_in",
        [SMEM] + [ANY] * 7,
        [VMEM] * 4,
        outs,
        [*[pltpu.VMEM(a.shape, a.dtype) for a in arrays], DMA((7,))],
        1,
    )(ids, *map(pin, arrays))[:-1]


def joined(block):
    return block[0:16, 1024:].astype(f32) + block[16:32, 1024:].astype(f32)


def put_small(value, own, blocks):
    hi, lo = split2(value)
    own[0:16, 1024:] = hi.astype(f32) + lo.astype(f32)
    for block in blocks:
        block[0:16, 1024:] = hi
        block[16:32, 1024:] = lo


def near_kernel(ids, ins, outs):
    keep, other = ins
    for i in range(4):
        outs[i][...] = (keep[i].astype(f32) + other[i].astype(f32)).astype(outs[i].dtype)
    if keep.shape[3] == 1152:
        value = joined(keep.at[0, 0]) + joined(other.at[0, 0])
        put_small(value, outs[0].at[0], [out.at[0] for out in outs[1:]])


def near_task(keep, other):
    shape = keep.shape[1:]
    return near_kernel, [keep, other], shaped((shape, f32), *[(shape, bf16)] * 3)


def put_code(ref, first, code):
    for i in range(3):
        ref[first + i] = code[:, 1024 * i : 1024 * (i + 1)]


def get_code(ref, first):
    return jnp.concatenate([ref[first + i] for i in range(3)], axis=1)


def put_rows(ref, first, rows):
    for i in range(4):
        ref[first + i, :, :512] = rows[i * 32 : (i + 1) * 32, :]
        ref[first + i, :, 512:] = rows[128 + i * 32 : 128 + (i + 1) * 32, :]


def get_rows(ref, first):
    parts = [ref[first + i, :, :512] for i in range(4)] + [ref[first + i, :, 512:] for i in range(4)]
    return jnp.concatenate(parts, axis=0)


def code_sum(a, b):
    done = []
    for first in range(0, a.shape[1], 1536):
        total = a[:, first : first + 1024].astype(f32) + b[:, first : first + 1024].astype(f32)
        small = [
            x[:, first + 1024 : first + 1280].astype(f32) + x[:, first + 1280 : first + 1536].astype(f32)
            for x in (a, b)
        ]
        done += [total.astype(bf16), *split2(small[0] + small[1])]
    return jnp.concatenate(done, axis=1)


def fork_kernel(ids, ins, outs):
    keep, other, code, code_other, rows = ins
    own_up, to_x, own_down, to_y, code_out = outs
    for at, (own, send, kept, sent) in enumerate(
        ((own_up, to_x, (0, 2), (1, 3)), (own_down, to_y, (0, 1), (2, 3)))
    ):
        cols = slice(1024 * at, 1024 * (at + 1))
        for j in range(2):
            own[j] = keep[kept[j], :, :, cols].astype(f32) + other[kept[j], :, :, cols].astype(f32)
            total = keep[sent[j], :, :, cols].astype(f32) + other[sent[j], :, :, cols].astype(f32)
            send[4 * j : 4 * (j + 1)] = total.astype(bf16)
    swapped = jnp.concatenate([code_other[:, 1536:], code_other[:, :1536]], axis=1)
    code_out[...] = code_sum(code[...], swapped)
    put_code(to_x, 8, code_out)
    put_rows(to_x, 11, rows)


def fork_task(keep, other, code, code_other, rows):
    outs = shaped(
        ((2, 4, 32, 1024), f32),
        ((15, 32, 1024), bf16),
        ((2, 4, 32, 1024), f32),
        ((8, 32, 1024), bf16),
        (code.shape, bf16),
    )
    return fork_kernel, [keep, other, code, code_other, rows], outs


def half_kernel(ids, ins, outs):
    own_up, from_x, own_down, from_y, code, dx_low = ins
    up, to_y, down, to_x, code_out, rows = outs
    for own, other, kept, send in ((own_up, from_x, up, to_y), (own_down, from_y, down, to_x)):
        kept[...] = own[0] + other[0:4].astype(f32)
        send[0:4] = (own[1] + other[4:8].astype(f32)).astype(bf16)
    code_out[...] = code_sum(code[...], get_code(from_x, 8))
    put_code(to_y, 4, code_out)
    put_rows(to_x, 4, dx_low)
    rows[...] = get_rows(from_x, 11)


def half_task(own_up, from_x, own_down, from_y, code, dx_low):
    outs = shaped(
        ((4, 32, 1024), f32),
        ((7, 32, 1024), bf16),
        ((4, 32, 1024), f32),
        ((8, 32, 1024), bf16),
        (code.shape, bf16),
        (dx_low.shape, bf16),
    )
    return half_kernel, [own_up, from_x, own_down, from_y, code, dx_low], outs


def join_kernel(ids, ins, outs):
    own_up, from_y, own_down, from_x, code = ins
    kept, send, code_out, rows = outs
    for at, (own, other) in enumerate(((own_up, from_y), (own_down, from_x))):
        cols = slice(1024 * at, 1024 * (at + 1))
        for k in range(2):
            kept[k, :, cols] = own[k] + other[k].astype(f32)
            send[k, :, cols] = (own[2 + k] + other[2 + k].astype(f32)).astype(bf16)
    code_out[...] = code_sum(code[...], get_code(from_y, 4))
    rows[...] = get_rows(from_x, 4)


def join_task(own_up, from_y, own_down, from_x, code):
    outs = shaped(
        ((2, 32, 2048), f32), ((2, 32, 2048), bf16), (code.shape, bf16), ((256, 512), bf16)
    )
    return join_kernel, [own_up, from_y, own_down, from_x, code], outs


def line_step_kernel(ids, ins, outs):
    kept, other = ins
    outs[0][...] = kept[0] + other[0].astype(f32)
    outs[1][...] = (kept[1] + other[1].astype(f32)).astype(bf16)


def line_step_task(kept, other):
    shape = kept.shape[1:]
    return line_step_kernel, [kept, other], shaped((shape, f32), (shape, bf16))


def plane_kernel(ids, ins, outs):
    for k in range(4):
        total = ins[0][k]
        for other in ins[1:]:
            total = total + other[k].astype(f32)
        outs[k][...] = total.astype(outs[k].dtype)
    if ins[0].shape[2] == 1152:
        x, y, xy = [joined(other.at[0]) for other in ins[1:]]
        put_small((ins[0][0, 0:16, 1024:] + x) + (y + xy), outs[0], outs[1:])


def plane_task(own, others):
    shape = own.shape[1:]
    return plane_kernel, [own, *others], shaped((shape, f32), *[(shape, bf16)] * 3)


def plane_join_kernel(ids, ins, outs):
    plane_kernel(ids, ins[:4], [out.at[:, pl.ds(0, 1024)] for out in outs])
    for part, out in zip(ins[4:], outs):
        out[:, 1024:] = part[...]


def plane_join_task(own, others, *parts):
    outs = shaped(((32, 3072), f32), *[((32, 3072), bf16)] * 3)
    return plane_join_kernel, [own, *others, *parts], outs


def line_total(ins, width):
    total = ins[0][:, :width]
    for other in ins[1:]:
        total = total + other[:, :width].astype(f32)
    return total


def rows_kernel(ids, ins, outs):
    own, other = ins
    half = other.shape[0]
    matrix = order_matrix(ids[0], True)
    outs[0][ids[1]] = ordered(own[0:half, :], matrix)
    outs[0][1 - ids[1]] = ordered(other[...], matrix)


def rows_task(own, other):
    return rows_kernel, [own, other], shaped(((2, *other.shape), f32))


def code_near_kernel(ids, ins, outs):
    keep, other = ins
    for at, out in enumerate(outs):
        for i in range(2):
            out[:, 1536 * i : 1536 * (i + 1)] = code_sum(keep[2 * at + i], other[2 * at + i])


def code_near_task(keep, other):
    return code_near_kernel, [keep, other], shaped(*[((32, 3072), bf16)] * 2)


def code_add_kernel(ids, ins, outs):
    outs[0][...] = code_sum(ins[0][...], ins[1][...])


def code_add_task(a, b):
    return code_add_kernel, [a, b], shaped((a.shape, bf16))


def code_pair_kernel(ids, ins, outs):
    for at, part in enumerate(ins):
        outs[0][:, 3072 * at : 3072 * (at + 1)] = part[...]


def code_pair_task(a, b):
    return code_pair_kernel, [a, b], shaped(((32, 6144), bf16))


def finish_kernel(ids, ins, outs):
    mlp, attn, dec, code, code_other = ins[:2], ins[2:6], ins[6:10], *ins[10:]
    qkv, out_t, up, down_t, book, vq_in, vq_out, gains, biases, dec_biases, small_ref = outs
    both = line_total(dec, 3072)
    for layer, rows in enumerate((line_total(mlp, 2048), both[:, 1024:])):
        up[layer] = rows[:, :1024]
        down_t[layer] = rows[:, 1024:]
    for layer, rows in enumerate((line_total(attn, 1024), both[:, :1024])):
        for index in range(3):
            qkv[layer, index] = rows[:, index * 256 : (index + 1) * 256]
        out_t[layer] = rows[:, 768:]
    core, z = ids[0] % 2, ids[0] // 4
    for at, parts in ((core, code), (1 - core, code_other)):
        for k in range(4):
            part = at * 4 + (z ^ k)
            held = parts[:, 1536 * k : 1536 * (k + 1)].astype(f32)
            book[:, pl.ds(pl.multiple_of(part * 1024, 1024), 1024)] = held[:, :1024]
            small_ref[:, pl.ds(pl.multiple_of(part * 256, 256), 256)] = (
                held[:, 1024:1280] + held[:, 1280:1536]
            )
    small = small_ref[...]
    vq_in[...] = small[:, :512]
    vq_out[...] = small[:, 512:1024]
    rest = small[:, 1024:1536]
    k1, k2, k3 = [joined(other) for other in attn[1:]]
    packed = (attn[0][0:16, 1024:] + k1) + (k2 + k3)
    for row, out in enumerate((gains.at[0:1], biases.at[0:1], gains.at[1:2], biases.at[1:2])):
        for j in range(4):
            out[:, 128 * j : 128 * (j + 1)] = packed[row * 4 + j : row * 4 + j + 1, :]
    gains[2:3, :] = rest[0:1, :]
    biases[2:3, :] = rest[1:2, :]
    gains[3:4, :] = rest[2:3, :]
    dec_biases[0:1, :] = rest[3:4, :]
    gains[4:5, :] = rest[4:5, :]
    dec_biases[1:2, :] = rest[5:6, :]


def finish_task(own_m, other_m, own_a, line_a, own_d, line_d, code, code_other):
    outs = shaped(
        ((2, 3, 32, 256), f32),
        ((2, 32, 256), f32),
        ((2, 32, 1024), f32),
        ((2, 32, 1024), f32),
        ((32, 8192), f32),
        ((32, 512), f32),
        ((32, 512), f32),
        ((5, 512), f32),
        ((3, 512), f32),
        ((2, 512), f32),
        ((32, 2048), f32),
    )
    ins = [own_m, other_m, own_a, *line_a, own_d, *line_d, code, code_other]
    return finish_kernel, ins, outs


def run_tasks(ids, name, tasks, after=(), carry=()):
    sizes = [(len(ins), len(outs)) for _, ins, outs in tasks]
    n_in = sum(i for i, _ in sizes)

    def kernel(ids_ref, *refs):
        at_in, at_out = 0, n_in
        for (fn, _, _), (i, o) in zip(tasks, sizes):
            fn(ids_ref, refs[at_in : at_in + i], refs[at_out : at_out + o])
            at_in, at_out = at_in + i, at_out + o

    outs = [one for _, _, many in tasks for one in many]
    res = call(
        kernel, name, [SMEM] + [VMEM] * n_in, [VMEM] * len(outs), outs, [], 10**9, after, carry
    )(ids, *[one for _, many, _ in tasks for one in many])
    split, at = [], 0
    for _, o in sizes:
        split.append(res[at : at + o])
        at += o
    return (*split, res[-1])


def whole_groups(
    n_dp,
    tokens,
    segment_ids,
    norm_gains,
    norm_biases,
    w_qkv,
    w_attn_out,
    w_up,
    w_down,
    w_vq_in,
    w_vq_out,
    codebook,
    cotangent,
):
    dp_at, tp_at = lax.axis_index("dp"), lax.axis_index("tp")
    ids = jnp.stack([dp_at, tp_at]).astype(jnp.int32)

    def swap(values):
        return exchange(values, 0, 1, n_dp)

    def core(values):
        return [values, exchange(values, 1, 0, n_dp)]

    book_t = codebook.T
    enc_shard, attn_shard, mlp_shard = pack_weights(
        w_qkv, w_attn_out.transpose(0, 2, 1), w_up, w_down.transpose(0, 2, 1)
    )
    enc_shards = spread_line(enc_shard, n_dp)
    own, send, norms, vq_w = rows_in(
        ids,
        tokens,
        segment_ids,
        cotangent,
        norm_gains,
        norm_biases,
        w_vq_in.T,
        w_vq_out,
    )
    marked = [own, swap(send)]

    dec_mlp = [lax.all_gather(mlp_shard, ("dp", "tp"))]
    attn_line, mlp_line, _ = stack_lines(enc_shards, [1024, 2048])
    stack, stack_t, _ = code_prep(book_t, [attn_line])
    codes = (stack, stack_t, book_t)
    quads, (mlp_line,) = stack_quads(
        plane_quads(attn_line, n_dp), [stack_t, marked[1]], [mlp_line]
    )
    enc_attn, quads = core(quads), plane_quads(mlp_line, n_dp)
    e_x1, e_saved, (attn_shard,) = attn_fwd(
        0, marked, [], norms, enc_attn, carry=[attn_shard]
    )
    attn_line, _ = stack_lines(spread_line(attn_shard, n_dp), [1024], [e_x1])
    quads, _ = stack_quads(quads, [attn_line])
    enc_mlp, quads = core(quads), plane_quads(attn_line, n_dp)
    e, _, _ = mlp_fwd(1, ids, e_x1, norms, enc_mlp)
    quads, _ = stack_quads(quads, [e])
    dec_attn = core(quads)
    u, kept, _ = vq_fwd(e, norms, vq_w, stack, stack_t)
    d_x1, d_saved, _ = attn_fwd(3, marked, [u], norms, dec_attn)

    dx1, d_small1, keep_m, send_m, _ = mlp_bwd(
        4, ids, d_x1, [cotangent, marked[1]], norms, dec_mlp
    )
    near_m = exchange(send_m, 1, 0, n_dp)
    du, _, d_small0, keep_a, send_a, (keep_m,) = attn_bwd(
        3, ids, marked, [u], dx1, norms, d_saved, dec_attn, carry=[keep_m]
    )
    (own_m, *lows_m), (send_a,) = run_tasks(
        ids, "sums1", [near_task(keep_m, near_m)], carry=[send_a]
    )
    plane_m, near_a = plane_send(lows_m, n_dp), exchange(send_a, 1, 0, n_dp)
    de, code, code_send, (own_m, keep_a) = vq_bwd(
        ids,
        e,
        du,
        norms,
        vq_w,
        codes,
        kept,
        [d_small0, d_small1],
        lows_m,
        [own_m, keep_a],
    )
    d_mlp, (own_a, *lows_a), (code, code_send) = run_tasks(
        ids,
        "sums2",
        [plane_task(own_m, plane_m), near_task(keep_a, near_a)],
        carry=[code, code_send],
    )
    plane_a, code_other = plane_send(lows_a, n_dp), exchange(code_send, 1, 0, n_dp)
    (code, code_send), _ = run_tasks(ids, "sums2b", [code_near_task(code, code_other)])
    code_other = exchange(code_send, 8, 0, n_dp)
    ex1, e_small1, keep_m, send_m, (own_a, code) = mlp_bwd(
        1, ids, e_x1, [de], norms, enc_mlp, [*lows_a, code_send], [own_a, code]
    )
    (own_d, *lows_d), (code,), (keep_m, send_m, d_x1) = run_tasks(
        ids,
        "sums3",
        [plane_join_task(own_a, plane_a, *d_mlp), code_add_task(code, code_other)],
        carry=[keep_m, send_m, d_x1],
    )
    near_m, code_other = exchange(send_m, 1, 0, n_dp), exchange(code, 4, 0, n_dp)
    line_d = line_send(lows_d, n_dp)
    y, y_theirs, _ = mlp_fwd(4, ids, d_x1, norms, dec_mlp)
    (own_up, to_x, own_down, to_y, code), _ = run_tasks(
        ids, "sums3b", [fork_task(keep_m, near_m, code, code_other, y_theirs)]
    )
    from_x, from_y = exchange(to_x, 0, 1, n_dp), exchange(to_y, 2, 0, n_dp)
    dx, dx_low, _, keep_a, send_a, (own_up, own_down, code) = attn_bwd(
        0,
        ids,
        marked,
        [],
        ex1,
        norms,
        e_saved,
        enc_attn,
        [e_small1],
        [to_x, to_y],
        [own_up, own_down, code],
    )
    (own_up, to_y, own_down, to_x, code, y_other), (keep_a, send_a) = run_tasks(
        ids,
        "sums4",
        [half_task(own_up, from_x, own_down, from_y, code, dx_low)],
        line_d,
        [keep_a, send_a],
    )
    near_a = exchange(send_a, 1, 0, n_dp)
    from_y, from_x = exchange(to_y, 2, 0, n_dp), exchange(to_x, 0, 1, n_dp)
    (own_a, *lows_a), (own_up, own_down, code) = run_tasks(
        ids, "sums4b", [near_task(keep_a, near_a)], carry=[own_up, own_down, code]
    )
    plane_a = plane_send(lows_a, n_dp)
    (own_m, send_m, code, dx_other), (own_a,) = run_tasks(
        ids, "sums5", [join_task(own_up, from_y, own_down, from_x, code)], lows_a, [own_a]
    )
    other_m, code_other = exchange(send_m, 8, 0, n_dp), exchange(code, 8, 0, n_dp)
    (decoded,), (grad_tokens,), (own_a,) = run_tasks(
        ids,
        "rows_out",
        [rows_task(y, y_other), rows_task(dx, dx_other)],
        [send_m, code],
        [own_a],
    )
    (own_a, *lows_a), (own_m, send_m), (code,), _ = run_tasks(
        ids,
        "sums6",
        [
            plane_task(own_a, plane_a),
            line_step_task(own_m, other_m),
            code_pair_task(code, code_other),
        ],
    )
    line_a, other_m = line_send(lows_a, n_dp), exchange(send_m, 4, 0, n_dp)
    code_other = exchange(code, 1, 0, n_dp)
    (qkv, out_t, up, down_t, book, vq_in, vq_out, *norm_grads, _), _ = run_tasks(
        ids,
        "finish",
        [finish_task(own_m, other_m, own_a, line_a, own_d, line_d, code, code_other)],
    )
    return (
        decoded,
        grad_tokens,
        *norm_grads,
        qkv,
        out_t.transpose(0, 2, 1),
        up,
        down_t.transpose(0, 2, 1),
        vq_in.T,
        vq_out,
        book.T,
    )


def layer_norm(values, norm_gain, norm_bias):
    centred = values - jnp.mean(values, axis=-1, keepdims=True)
    spread = jnp.mean(centred * centred, axis=-1, keepdims=True)
    return centred * lax.rsqrt(spread + ln_eps) * norm_gain + norm_bias


def gelu_tanh(values):
    return (
        0.5 * values * (1.0 + jnp.tanh(gelu_coef * (values + 0.044715 * values * values * values)))
    )


def matmul(former, latter):
    return jnp.dot(former, latter, precision=highest, preferred_element_type=jnp.float32)


def normalize(values):
    return values * lax.rsqrt(jnp.sum(values * values, axis=-1, keepdims=True) + norm_eps)


def quantize(in_rows, norm_gain, norm_bias, in_w, out_w, code_w):
    latent = normalize(matmul(layer_norm(in_rows, norm_gain, norm_bias), in_w))
    code_rows = normalize(code_w)
    logits = matmul(latent, code_rows.T) * temper
    row_max = jnp.max(logits, axis=-1, keepdims=True)
    numerator = jnp.exp(logits - row_max)
    assign = numerator / jnp.sum(numerator, axis=-1, keepdims=True)
    soft_code = matmul(assign, code_rows)
    offset = latent - soft_code
    vq_loss = commit_weight * 1.25 * jnp.sum(offset * offset)
    return (matmul(soft_code, out_w), vq_loss)


def product(former, latter):
    return jnp.dot(former, latter, preferred_element_type=jnp.float32)


def product_tn(former, latter):
    return lax.dot_general(
        former, latter, (((0,), (0,)), ((), ())), preferred_element_type=jnp.float32
    )


def product_nt(former, latter):
    return lax.dot_general(
        former, latter, (((1,), (1,)), ((), ())), preferred_element_type=jnp.float32
    )


def split_heads(values):
    return values.reshape(values.shape[0], values.shape[1] // HEAD_DIM, HEAD_DIM).transpose(1, 0, 2)


def join_heads(values):
    return values.transpose(1, 0, 2).reshape(values.shape[1], values.shape[0] * HEAD_DIM)


def masked_scores(query_blk, key_h, seg_blk, seg_keys):
    scores = jnp.einsum(
        "hqd,hkd->hqk", query_blk, key_h, preferred_element_type=jnp.float32
    ) * HEAD_DIM ** (-0.5)
    return jnp.where((seg_blk[:, None] == seg_keys[None, :])[None], scores, masked_score)


def attend(query_h, key_h, value_h, seg_keys):
    block_rows = min(512, query_h.shape[1])
    block_count = query_h.shape[1] // block_rows

    def one_block(begin_row):
        query_blk = lax.dynamic_slice_in_dim(query_h, begin_row, block_rows, 1)
        seg_blk = lax.dynamic_slice_in_dim(seg_keys, begin_row, block_rows, 0)
        scores = masked_scores(query_blk, key_h, seg_blk, seg_keys)
        row_max = jnp.max(scores, axis=-1, keepdims=True)
        numerator = jnp.exp(scores - row_max)
        row_total = jnp.sum(numerator, axis=-1, keepdims=True)
        prob_low = (numerator / row_total).astype(jnp.bfloat16)
        attended = jnp.einsum("hqk,hkd->hqd", prob_low, value_h, preferred_element_type=jnp.float32)
        return (attended.astype(jnp.bfloat16), (row_max + jnp.log(row_total))[..., 0])

    starts = jnp.arange(block_count, dtype=jnp.int32) * block_rows
    attended, log_sums = lax.map(one_block, starts)
    heads_out = attended.transpose(1, 0, 2, 3).reshape(query_h.shape)
    log_sums = log_sums.transpose(1, 0, 2).reshape(query_h.shape[0], query_h.shape[1])
    return (heads_out, log_sums)


def attend_back(query_h, key_h, value_h, seg_keys, log_sums, grad_out):
    block_rows = min(512, query_h.shape[1])
    block_count = query_h.shape[1] // block_rows

    def one_block(carry, begin_row):
        grad_key, grad_value = carry
        query_blk = lax.dynamic_slice_in_dim(query_h, begin_row, block_rows, 1)
        grad_blk = lax.dynamic_slice_in_dim(grad_out, begin_row, block_rows, 1)
        lse_blk = lax.dynamic_slice_in_dim(log_sums, begin_row, block_rows, 1)
        seg_blk = lax.dynamic_slice_in_dim(seg_keys, begin_row, block_rows, 0)
        scores = masked_scores(query_blk, key_h, seg_blk, seg_keys)
        probs = jnp.exp(scores - lse_blk[..., None])
        prob_low = probs.astype(jnp.bfloat16)
        grad_value = grad_value + jnp.einsum(
            "hqk,hqd->hkd", prob_low, grad_blk, preferred_element_type=jnp.float32
        )
        grad_prob = jnp.einsum(
            "hqd,hkd->hqk", grad_blk, value_h, preferred_element_type=jnp.float32
        )
        row_dot = jnp.sum(probs * grad_prob, axis=-1, keepdims=True)
        grad_score = (probs * (grad_prob - row_dot) * HEAD_DIM ** (-0.5)).astype(jnp.bfloat16)
        grad_query = jnp.einsum(
            "hqk,hkd->hqd", grad_score, key_h, preferred_element_type=jnp.float32
        )
        grad_key = grad_key + jnp.einsum(
            "hqk,hqd->hkd", grad_score, query_blk, preferred_element_type=jnp.float32
        )
        return ((grad_key, grad_value), grad_query)

    starts = jnp.arange(block_count, dtype=jnp.int32) * block_rows
    zeros_kv = jnp.zeros(key_h.shape, jnp.float32)
    (grad_key, grad_value), grad_query = lax.scan(one_block, (zeros_kv, zeros_kv), starts)
    grad_query = grad_query.transpose(1, 0, 2, 3).reshape(query_h.shape)
    return (
        grad_query.astype(jnp.bfloat16),
        grad_key.astype(jnp.bfloat16),
        grad_value.astype(jnp.bfloat16),
    )


def spread_rows(values):
    return lax.all_gather(values, "tp", axis=0, tiled=True)


def combine_rows(partial_value):
    return lax.psum_scatter(partial_value, "tp", scatter_dimension=0, tiled=True)


def spread_grads(values):
    return lax.all_gather(values, "tp", axis=0, tiled=True)


def combine_grads(partial_value):
    return lax.psum_scatter(
        partial_value.astype(jnp.bfloat16), "tp", scatter_dimension=0, tiled=True
    ).astype(jnp.float32)


def fetch_weights(w_qkv, w_attn_out, w_up, w_down, layer):
    return (
        lax.all_gather(w_qkv[layer], "dp", axis=1, tiled=True),
        lax.all_gather(w_attn_out[layer], "dp", axis=1, tiled=True),
        lax.all_gather(w_up[layer], "dp", axis=0, tiled=True),
        lax.all_gather(w_down[layer], "dp", axis=1, tiled=True),
    )


def reduce_weight_grads(grads):
    return (
        lax.psum_scatter(
            grads[0].astype(jnp.bfloat16), "dp", scatter_dimension=1, tiled=True
        ).astype(jnp.float32),
        lax.psum_scatter(
            grads[1].astype(jnp.bfloat16), "dp", scatter_dimension=1, tiled=True
        ).astype(jnp.float32),
        lax.psum_scatter(
            grads[2].astype(jnp.bfloat16), "dp", scatter_dimension=0, tiled=True
        ).astype(jnp.float32),
        lax.psum_scatter(
            grads[3].astype(jnp.bfloat16), "dp", scatter_dimension=1, tiled=True
        ).astype(jnp.float32),
    )


def block_forward(resid_in, seg_local, gains, biases, weights):
    qkv_w, attn_w, up_w, down_w = weights
    normed = layer_norm(resid_in, gains[0], biases[0]).astype(jnp.bfloat16)
    normed_all, seg_all = (
        lax.all_gather(normed, "tp", axis=0, tiled=True),
        lax.all_gather(seg_local, "tp", axis=0, tiled=True),
    )
    query_h = split_heads(product(normed_all, qkv_w[0]).astype(jnp.bfloat16))
    key_h = split_heads(product(normed_all, qkv_w[1]).astype(jnp.bfloat16))
    value_h = split_heads(product(normed_all, qkv_w[2]).astype(jnp.bfloat16))
    heads_out, log_sums = attend(query_h, key_h, value_h, seg_all)
    attn_rows = join_heads(heads_out)
    middle = resid_in + combine_rows(product(attn_rows, attn_w))
    normed_mid = spread_rows(layer_norm(middle, gains[1], biases[1]).astype(jnp.bfloat16))
    hidden_pre = product(normed_mid, up_w)
    hidden = gelu_tanh(hidden_pre).astype(jnp.bfloat16)
    result = middle + combine_rows(product(hidden, down_w))
    kept = (
        resid_in,
        middle,
        normed_all,
        seg_all,
        query_h,
        key_h,
        value_h,
        log_sums,
        attn_rows,
        normed_mid,
        hidden_pre,
        hidden,
    )
    return (result, kept)


def block_backward(kept, gains, biases, weights, grad_result):
    (
        resid_in,
        middle,
        normed_all,
        seg_all,
        query_h,
        key_h,
        value_h,
        log_sums,
        attn_rows,
        normed_mid,
        hidden_pre,
        hidden,
    ) = kept
    qkv_w, attn_w, up_w, down_w = weights
    grad_branch = spread_grads(grad_result.astype(jnp.bfloat16))
    grad_down = product_tn(hidden, grad_branch)
    grad_hidden = product_nt(grad_branch, down_w)
    _, gelu_back = jax.vjp(gelu_tanh, hidden_pre)
    grad_pre = gelu_back(grad_hidden)[0].astype(jnp.bfloat16)
    grad_up = product_tn(normed_mid, grad_pre)
    grad_norm_mid = combine_grads(product_nt(grad_pre, up_w))
    _, norm_back_mid = jax.vjp(layer_norm, middle, gains[1], biases[1])
    grad_mid_ln, grad_gain_mid, grad_bias_mid = norm_back_mid(grad_norm_mid)
    grad_middle = grad_result + grad_mid_ln
    grad_attn_all = spread_grads(grad_middle.astype(jnp.bfloat16))
    grad_attn = product_tn(attn_rows, grad_attn_all)
    grad_heads = split_heads(product_nt(grad_attn_all, attn_w).astype(jnp.bfloat16))
    grad_query, grad_key, grad_value = attend_back(
        query_h, key_h, value_h, seg_all, log_sums, grad_heads
    )
    grad_parts = [join_heads(grad_query), join_heads(grad_key), join_heads(grad_value)]
    grad_qkv = jnp.stack([product_tn(normed_all, grad_part) for grad_part in grad_parts])
    grad_normed_part = (
        product_nt(grad_parts[0], qkv_w[0])
        + product_nt(grad_parts[1], qkv_w[1])
        + product_nt(grad_parts[2], qkv_w[2])
    )
    grad_normed = combine_grads(grad_normed_part)
    _, norm_back_in = jax.vjp(layer_norm, resid_in, gains[0], biases[0])
    grad_in_ln, grad_gain_in, grad_bias_in = norm_back_in(grad_normed)
    gain_grads = jnp.stack([grad_gain_in, grad_gain_mid])
    bias_grads = jnp.stack([grad_bias_in, grad_bias_mid])
    return (
        grad_middle + grad_in_ln,
        gain_grads,
        bias_grads,
        (grad_qkv, grad_attn, grad_up, grad_down),
    )


def local(
    tokens,
    segment_ids,
    norm_gains,
    norm_biases,
    w_qkv,
    w_attn_out,
    w_up,
    w_down,
    w_vq_in,
    w_vq_out,
    codebook,
    cotangent,
):
    gain_sum = jnp.zeros(norm_gains.shape, jnp.float32)
    bias_sum = jnp.zeros(norm_biases.shape, jnp.float32)
    vq_in_sum = jnp.zeros(w_vq_in.shape, jnp.float32)
    vq_out_sum = jnp.zeros(w_vq_out.shape, jnp.float32)
    code_sum = jnp.zeros(codebook.shape, jnp.float32)
    layer_sums = [None, None]
    outputs = []
    input_grads = []
    for micro in range(MICRO):
        resid_in = tokens[micro].astype(jnp.float32)
        seg_local = segment_ids[micro]
        enc_weights = fetch_weights(w_qkv, w_attn_out, w_up, w_down, 0)
        encoded, enc_kept = block_forward(
            resid_in, seg_local, norm_gains[0:2], norm_biases[0:2], enc_weights
        )
        (decoder_in, _), vq_back = jax.vjp(
            quantize, encoded, norm_gains[2], norm_biases[2], w_vq_in, w_vq_out, codebook
        )
        dec_weights = fetch_weights(w_qkv, w_attn_out, w_up, w_down, 1)
        decoded, dec_kept = block_forward(
            decoder_in, seg_local, norm_gains[3:5], norm_biases[3:5], dec_weights
        )
        outputs.append(decoded)
        grad_dec_in, gains_dec, biases_dec, grads_dec = block_backward(
            dec_kept, norm_gains[3:5], norm_biases[3:5], dec_weights, cotangent[micro]
        )
        grad_encoded, grad_gain_vq, grad_bias_vq, grad_in_w, grad_out_w, grad_codes = vq_back(
            (grad_dec_in, jnp.ones((), jnp.float32))
        )
        grad_input, gains_enc, biases_enc, grads_enc = block_backward(
            enc_kept, norm_gains[0:2], norm_biases[0:2], enc_weights, grad_encoded
        )
        input_grads.append(grad_input)
        gain_sum = gain_sum + jnp.concatenate([gains_enc, grad_gain_vq[None], gains_dec], axis=0)
        bias_sum = bias_sum + jnp.concatenate([biases_enc, grad_bias_vq[None], biases_dec], axis=0)
        vq_in_sum = vq_in_sum + grad_in_w
        vq_out_sum = vq_out_sum + grad_out_w
        code_sum = code_sum + grad_codes
        for layer, grads in ((0, grads_enc), (1, grads_dec)):
            reduced = reduce_weight_grads(grads)
            if layer_sums[layer] is None:
                layer_sums[layer] = reduced
            else:
                layer_sums[layer] = jax.tree.map(jnp.add, layer_sums[layer], reduced)
    gain_tot, bias_tot, vq_in_tot, vq_out_tot, code_tot = lax.psum(
        (gain_sum, bias_sum, vq_in_sum, vq_out_sum, code_sum), ("dp", "tp")
    )
    return (
        jnp.stack(outputs),
        jnp.stack(input_grads),
        gain_tot,
        bias_tot[0:3],
        bias_tot[3:5],
        jnp.stack([layer_sums[0][0], layer_sums[1][0]]),
        jnp.stack([layer_sums[0][1], layer_sums[1][1]]),
        jnp.stack([layer_sums[0][2], layer_sums[1][2]]),
        jnp.stack([layer_sums[0][3], layer_sums[1][3]]),
        vq_in_tot,
        vq_out_tot,
        code_tot,
    )


def solution(mesh):
    n_dp, n_tp = mesh.shape["dp"], mesh.shape["tp"]
    fits = n_tp == MICRO and n_dp == 16
    return jax.shard_map(
        functools.partial(whole_groups, n_dp) if fits else local,
        mesh=mesh,
        in_specs=(
            P(None, ("dp", "tp"), None),
            P(None, ("dp", "tp")),
            P(),
            P(),
            P(None, None, "dp", "tp"),
            P(None, "tp", "dp"),
            P(None, "dp", "tp"),
            P(None, "tp", "dp"),
            P(),
            P(),
            P(),
            P(None, ("dp", "tp"), None),
        ),
        out_specs=(
            P(None, ("dp", "tp"), None),
            P(None, ("dp", "tp"), None),
            P(),
            P(),
            P(),
            P(None, None, "dp", "tp"),
            P(None, "tp", "dp"),
            P(None, "dp", "tp"),
            P(None, "tp", "dp"),
            P(),
            P(),
            P(),
        ),
        check_vma=False,
    )
```

```python
import functools

import jax
import jax.numpy as jnp
from jax import lax
from jax.experimental import pallas as pl
from jax.experimental.pallas import tpu as pltpu
from jax.sharding import PartitionSpec as P

HEAD_DIM = 64
MICRO = 2
bf16 = jnp.bfloat16
f32 = jnp.float32
highest = lax.Precision.HIGHEST
ln_eps = 1e-05
norm_eps = 1e-06
temper = 10.0
commit_weight = 64.0
gelu_coef = 0.7978845608028654
masked_score = -1e30
log2e = 1.4426950408889634
vmem_cap = 36 * 1024 * 1024


PLANE = ((0, 0), (0, 1), (1, 0), (1, 1))


def exchange(values, dp_xor, tp_xor, n_dp):
    pairs = [
        (d * 2 + t, (d ^ dp_xor) * 2 + (t ^ tp_xor)) for d in range(n_dp) for t in range(2)
    ]
    return lax.ppermute(values, ("dp", "tp"), pairs)


def spread_line(shard, n_dp):
    return [shard] + [exchange(shard, 4 * k, 0, n_dp) for k in range(1, 4)]


def plane_quads(own, n_dp):
    return [own] + [exchange(own, 2 * y, x, n_dp) for y, x in PLANE[1:]]


def plane_send(lows, n_dp):
    return [exchange(low, 2 * y, x, n_dp) for (y, x), low in zip(PLANE[1:], lows)]


def line_send(lows, n_dp):
    return [exchange(low, 4 * k, 0, n_dp) for k, low in zip(range(1, 4), lows)]


def dot(a, b):
    return jnp.dot(a, b, preferred_element_type=f32)


def dot_nt(a, b, precision=None):
    return lax.dot_general(
        a, b, (((1,), (1,)), ((), ())), preferred_element_type=f32, precision=precision
    )


def dot_full(a, b):
    return jnp.dot(a, b, preferred_element_type=f32, precision=highest)


def ln_parts(x):
    centred = x - jnp.mean(x, axis=-1, keepdims=True)
    inv = lax.rsqrt(jnp.mean(centred * centred, axis=-1, keepdims=True) + ln_eps)
    return centred * inv, inv


def ln_back(grad, xhat, inv, gain):
    scaled = grad * gain
    return inv * (
        scaled
        - jnp.mean(scaled, axis=-1, keepdims=True)
        - xhat * jnp.mean(scaled * xhat, axis=-1, keepdims=True)
    )


def split2(x):
    hi = x.astype(bf16)
    return hi, (x - hi.astype(f32)).astype(bf16)


def split3(x):
    hi, _ = split2(x)
    rest = x - hi.astype(f32)
    mid = rest.astype(bf16)
    return hi, mid, (rest - mid.astype(f32)).astype(bf16)


def order_matrix(dp, inverse):
    at = lax.broadcasted_iota(jnp.int32, (512, 512), 0 if inverse else 1)
    other = lax.broadcasted_iota(jnp.int32, (512, 512), 1 if inverse else 0)
    block = at >> 5
    bits = ((block & 3) << 2) | (((block >> 2) & 1) << 1) | (block >> 3)
    return jnp.where(other == (((dp ^ bits) << 5) | (at & 31)), 1.0, 0.0).astype(bf16)


def ordered(x, matrix):
    if x.dtype == bf16:
        return dot(x, matrix)
    hi, mid, lo = split3(x)
    return (dot(hi, matrix) + dot(mid, matrix)) + dot(lo, matrix)


QUADS, PAIRS_X, PAIRS_Y = 0, 1, 2


def w_at(form, refs, t, cols):
    parts = []
    for core in range(2):
        for y in range(2):
            if form == QUADS:
                part = refs[core][2 * y + t, :, :, cols]
            elif form == PAIRS_X:
                part = refs[2 * core + y][t, :, :, cols]
            else:
                part = refs[2 * core + t][y, :, :, cols]
            parts.append(part.reshape(128, part.shape[2]))
    return jnp.concatenate(parts, axis=0)


def put_grad(refs, t, cols, value):
    for core, ref in enumerate(refs):
        for y in range(2):
            rows = value[core * 256 + y * 128 : core * 256 + (y + 1) * 128]
            ref[2 * y + t, :, :, cols] = rows.reshape(4, 32, rows.shape[1])


def start_all(copies):
    for copy in copies:
        copy.start()


def wait_all(copies):
    for copy in copies:
        copy.wait()


def head_rows(ref, pair, which):
    own = ref[pl.ds(pair * 128 + which * HEAD_DIM, HEAD_DIM), :]
    zero = jnp.zeros_like(own)
    return jnp.concatenate([own, zero] if which == 0 else [zero, own], axis=0)


def segment_mask(own, other):
    ids = jnp.concatenate([own[:, 512:640], other[:, 512:640]], axis=0).astype(f32)
    return jnp.where(ids[:, 0:1] == ids.T[0:1, :], 0.0, masked_score)


def load_rows(x, own, other):
    if x is None:
        return jnp.concatenate([own[:, :512], other[:, :512]], axis=0).astype(f32)
    return x[...]


def gain_of(norms, at):
    return norms[at : at + 1, :]


def bias_of(norms, at):
    return norms[8 + at : 9 + at, :]


def attn_fwd_kernel(with_x, form, n_w, at, own, other, norms, *refs):
    w, refs = refs[:n_w], refs[n_w:]
    x, refs = (refs[0], refs[1:]) if with_x else (None, refs)
    x1, lse, saved, refs = refs[0], refs[1], refs[2:8], refs[8:]
    h, vt, ot, mask, qs, k, v, o, qst, kt, out_sems = refs
    keeps = [
        pltpu.make_async_copy(held, to, out_sems.at[i])
        for i, (held, to) in enumerate(zip((qs, k, v, o, qst, kt), saved))
    ]
    xf = load_rows(x, own, other)
    h[...] = (ln_parts(xf)[0] * gain_of(norms, at) + bias_of(norms, at)).astype(bf16)
    mask[...] = segment_mask(own, other)
    for t in range(2):
        cols = slice(t * 256, (t + 1) * 256)
        q = dot(h[...], w_at(form, w, t, slice(0, 256))).astype(bf16)
        qs[:, cols] = (q * HEAD_DIM ** (-0.5)).astype(bf16)
        k[:, cols] = dot(h[...], w_at(form, w, t, slice(256, 512))).astype(bf16)
        v[:, cols] = dot(h[...], w_at(form, w, t, slice(512, 768))).astype(bf16)
    qst[...] = qs[...].T
    kt[...] = k[...].T
    vt[...] = v[...].T
    for i in (0, 1, 2, 4, 5):
        keeps[i].start()
    for pair in range(4):
        k_pair = k[:, pair * 128 : (pair + 1) * 128]
        for which in range(2):
            scores = dot(k_pair, head_rows(qst, pair, which)) + mask[...]
            top = jnp.max(scores, axis=0, keepdims=True)
            numer = jnp.exp(scores - top).astype(bf16)
            rows = pl.ds(pair * 128 + which * HEAD_DIM, HEAD_DIM)
            left = jnp.concatenate([vt[rows, :], jnp.ones((16, 512), bf16)], axis=0)
            both = dot(left, numer)
            total = both[HEAD_DIM : HEAD_DIM + 1, :]
            ot[rows, :] = (both[:HEAD_DIM, :] / total).astype(bf16)
            lse[pl.ds(pair * 2 + which, 1), :] = top + jnp.log(total)
    o[...] = ot[...].T
    keeps[3].start()
    acc = xf
    for t in range(2):
        acc = acc + dot_nt(o[:, t * 256 : (t + 1) * 256], w_at(form, w, t, slice(768, 1024)))
    x1[...] = acc
    wait_all(keeps)


def gelu_parts(u):
    square = u * u
    tanh = jnp.tanh(gelu_coef * u * (1.0 + 0.044715 * square))
    return 0.5 * u * (1.0 + tanh), tanh, square


def mlp_weights(forms, refs):
    split = len(forms) == 2

    def weights(at):
        held = refs[4 * at : 4 * at + 4] if split else refs
        first = 0 if split else 1024 * at

        def take(t, part):
            return w_at(forms[at * split], held, t, slice(first + part * 512, first + (part + 1) * 512))

        return take

    return weights(0), weights(1)


def mlp_fwd_kernel(forms, n_w, at, x1, norms, *refs):
    up, down = mlp_weights(forms, refs[:n_w])
    y, theirs, h2 = refs[n_w:]
    h2[...] = (ln_parts(x1[...])[0] * gain_of(norms, at) + bias_of(norms, at)).astype(bf16)
    acc = x1[...]
    for t in range(2):
        for part in range(2):
            hidden = gelu_parts(dot(h2[...], up(t, part)))[0].astype(bf16)
            acc = acc + dot_nt(hidden, down(t, part))
    y[...] = acc
    theirs[...] = acc[256:, :]


def mlp_bwd_kernel(split, forms, n_w, at, ids, x1, norms, *refs):
    up, down = mlp_weights(forms, refs[:n_w])
    refs = refs[n_w:]
    if split:
        own, other, refs = refs[0], refs[1], refs[2:]
    else:
        dy, refs = refs[0], refs[1:]
    dx1, small, grads = refs[0], refs[1], refs[2:4]
    h2, h2t, dyb, dybt, dh2 = refs[4:9]
    if split:
        dy = refs[9]
        dy[0:256, :] = ordered(own[ids[1]], order_matrix(ids[0], False))
        dy[256:, :] = other[:, 640:].astype(f32)
    h2[...] = (ln_parts(x1[...])[0] * gain_of(norms, at) + bias_of(norms, at)).astype(bf16)
    h2t[...] = h2[...].T
    dyb[...] = dy[...].astype(bf16)
    dybt[...] = dyb[...].T
    for t in range(2):
        for part in range(2):
            cols = slice(part * 512, (part + 1) * 512)
            w_up = up(t, part)
            pre = dot(h2[...], w_up)
            hidden, tanh, square = gelu_parts(pre)
            slope = 0.5 * (1.0 + tanh) + (0.5 * gelu_coef) * pre * (1.0 - tanh * tanh) * (
                1.0 + (3 * 0.044715) * square
            )
            dhidden = dot(dyb[...], down(t, part))
            dpre = (dhidden * slope).astype(bf16)
            out_cols = slice(1024 + part * 512, 1024 + (part + 1) * 512)
            put_grad(grads, t, out_cols, dot(dybt[...], hidden.astype(bf16)).astype(bf16))
            put_grad(grads, t, cols, dot(h2t[...], dpre).astype(bf16))
            more = dot_nt(dpre, w_up)
            if t + part == 0:
                dh2[...] = more
            else:
                dh2[...] += more
    xhat, inv = ln_parts(x1[...])
    grad = dh2[...]
    small[0:1, :] = jnp.sum(grad * xhat, axis=0, keepdims=True)
    small[1:2, :] = jnp.sum(grad, axis=0, keepdims=True)
    dx1[...] = dy[...] + ln_back(grad, xhat, inv, gain_of(norms, at))


def pack_rows(rows):
    cut = [rows[i : i + 1, 128 * j : 128 * (j + 1)] for i in range(4) for j in range(4)]
    return jnp.concatenate(split2(jnp.concatenate(cut, axis=0)), axis=0)


def attn_bwd_kernel(with_x, with_small, form, n_w, at, ids, own, other, dx1, norms, lse, *refs):
    w, saved, refs = refs[:n_w], refs[n_w : n_w + 6], refs[n_w + 6 :]
    x, refs = (refs[0], refs[1:]) if with_x else (None, refs)
    if with_small:
        other_small, refs = refs[0], refs[1:]
    dx, dx_low, small, grads = refs[0], refs[1], refs[2], refs[3:5]
    h, mask, do, dot_t, dqt, dq, dk, dv, flip, qs, k, v, o, qst, kt, in_sems = refs[5:]
    takes = [
        pltpu.make_async_copy(held, to, in_sems.at[i])
        for i, (held, to) in enumerate(zip(saved, (qs, k, v, o, qst, kt)))
    ]
    start_all(takes)
    xf = load_rows(x, own, other)
    h[...] = (ln_parts(xf)[0] * gain_of(norms, at) + bias_of(norms, at)).astype(bf16)
    mask[...] = segment_mask(own, other)
    low = dx1[...].astype(bf16)
    flip[...] = low.T
    wait_all(takes)
    for t in range(2):
        cols = slice(t * 256, (t + 1) * 256)
        do[:, cols] = dot(low, w_at(form, w, t, slice(768, 1024))).astype(bf16)
        put_grad(grads, t, slice(768, 1024), dot(flip[...], o[:, cols]).astype(bf16))
    dot_t[...] = do[...].T
    first = lax.broadcasted_iota(jnp.int32, (512, 128), 1) < HEAD_DIM
    for pair in range(4):
        lanes = slice(pair * 128, (pair + 1) * 128)
        dvs, dks = [], []
        for which in range(2):
            head = pair * 2 + which
            rows = pl.ds(head * HEAD_DIM, HEAD_DIM)
            scores = dot(k[:, lanes], head_rows(qst, pair, which)) + mask[...]
            probs = jnp.exp(scores - lse[head : head + 1, :])
            dprobs = dot(v[:, lanes], head_rows(dot_t, pair, which))
            shift = jnp.sum(probs * dprobs, axis=0, keepdims=True)
            dscore = (probs * (dprobs - shift)).astype(bf16)
            dvs.append(dot(probs.astype(bf16), do[:, lanes]))
            dks.append(dot(dscore, qs[:, lanes]))
            dqt[rows, :] = (dot(kt[rows, :], dscore) * HEAD_DIM ** (-0.5)).astype(bf16)
        dv[:, lanes] = jnp.where(first, dvs[0], dvs[1]).astype(bf16)
        dk[:, lanes] = jnp.where(first, dks[0], dks[1]).astype(bf16)
    dq[...] = dqt[...].T
    flip[...] = h[...].T
    grad = jnp.zeros((512, 512), f32)
    for t in range(2):
        cols = slice(t * 256, (t + 1) * 256)
        for index, part in enumerate((dq, dk, dv)):
            w_cols = slice(index * 256, (index + 1) * 256)
            put_grad(grads, t, w_cols, dot(flip[...], part[:, cols]).astype(bf16))
            grad = grad + dot_nt(part[:, cols], w_at(form, w, t, w_cols))
    xhat, inv = ln_parts(xf)
    small[0:1, :] = jnp.sum(grad * xhat, axis=0, keepdims=True)
    small[1:2, :] = jnp.sum(grad, axis=0, keepdims=True)
    if with_small:
        rows = jnp.concatenate([small[0:2, :], other_small[0:2, :], jnp.zeros((4, 512), f32)], axis=0)
        packed = pack_rows(ordered(rows, order_matrix(ids[0], True)))
        for out in grads:
            for i in range(4):
                for z in range(4):
                    out[i, z, :, 1024:1152] = packed
    total = dx1[...] + ln_back(grad, xhat, inv, gain_of(norms, at))
    dx[...] = total
    dx_low[...] = total[256:, :].astype(bf16)


def code_prep_kernel(book_t, stack, stack_t):
    def one_chunk(index, _):
        lanes = pl.ds(pl.multiple_of(index * 512, 512), 512)
        rows = book_t[:, lanes]
        unit = rows * lax.rsqrt(jnp.sum(rows * rows, axis=0, keepdims=True) + norm_eps)
        hi, mid, lo = split3(unit)
        stack_t[:, lanes] = jnp.concatenate([hi, mid, lo, jnp.ones((32, 512), bf16)], axis=0)
        tall = jnp.concatenate([hi, mid, lo, hi, mid, hi, jnp.zeros((64, 512), bf16)], axis=0)
        stack[lanes, :] = tall.T
        return 0

    lax.fori_loop(0, book_t.shape[1] // 512, one_chunk, 0)


def factor_stack(x):
    hi, mid, lo = split3(x)
    return jnp.concatenate([hi, hi, hi, mid, mid, lo, jnp.zeros((64, x.shape[1]), bf16)], axis=0)


def code_loads(pairs, sems):
    loads = []
    for piece in range(4):
        group = []
        for at, (held, to, by_row) in enumerate(pairs):
            size = held.shape[0 if by_row else 1] // 4
            part = pl.ds(piece * size, size)
            place = (part, slice(None)) if by_row else (slice(None), part)
            group.append(pltpu.make_async_copy(held.at[place], to.at[place], sems.at[at, piece]))
        start_all(group)
        loads.append(group)
    return loads


def vq_fwd_kernel(
    e, norms, vq_w, stack_hbm, stack_t_hbm, u, kept, acc, stack, stack_t, sems
):
    loads = code_loads([(stack_hbm, stack, True), (stack_t_hbm, stack_t, False)], sems)
    lnv = ln_parts(e[...])[0] * gain_of(norms, 2) + bias_of(norms, 2)
    raw = dot_nt(vq_w[0:32, :], lnv, highest)
    inv = lax.rsqrt(jnp.sum(raw * raw, axis=0, keepdims=True) + norm_eps)
    latent = raw * inv
    right = factor_stack(latent * (temper * log2e))
    chunks = stack.shape[0] // 2048
    for piece, group in enumerate(loads):
        wait_all(group)
        for part in range(piece * chunks // 4, (piece + 1) * chunks // 4):
            numers = []
            for index in range(4 * part, 4 * part + 4):
                codes = slice(index * 512, (index + 1) * 512)
                numers.append(jnp.exp2(dot(stack[codes, :], right)).astype(bf16))
            sums = dot(
                stack_t[:, part * 2048 : (part + 1) * 2048], jnp.concatenate(numers, axis=0)
            )
            if part == 0:
                acc[...] = sums
            else:
                acc[...] += sums
    total = acc[96:97, :]
    soft = (acc[0:32, :] + acc[32:64, :] + acc[64:96, :]) / total
    kept[0:32, :] = latent
    kept[32:64, :] = soft
    kept[64:65, :] = total
    kept[65:66, :] = inv
    u[...] = dot_full(soft.T, vq_w[32:64, :])


def vq_bwd_kernel(ids, e, du, norms, vq_w, stack_hbm, stack_t_hbm, book_hbm, kept, *refs):
    small0, small1, de, code_keep, code_send = refs[:5]
    acc, grads, small, tail, stack, stack_t, book_t, load_sems, sems = refs[5:]
    loads = code_loads(
        [(stack_hbm, stack, True), (stack_t_hbm, stack_t, False), (book_hbm, book_t, False)],
        load_sems,
    )
    xhat, inv_ln = ln_parts(e[...])
    lnv = xhat * gain_of(norms, 2) + bias_of(norms, 2)
    latent, soft = kept[0:32, :], kept[32:64, :]
    total, inv = kept[64:65, :], kept[65:66, :]
    direct = (2.0 * 1.25 * commit_weight) * (latent - soft)
    dsoft = dot_nt(vq_w[32:64, :], du[...], highest) - direct
    small[32:64, :] = dot_full(soft, du[...])
    shift = jnp.sum(dsoft * soft, axis=0, keepdims=True) / total
    dsoft = dsoft / total
    right = jnp.concatenate(
        [factor_stack(latent * (temper * log2e)), factor_stack(dsoft)], axis=1
    )
    pads = jnp.zeros((64, 512), f32)

    def tall(x):
        hi, lo = split2(x)
        return jnp.concatenate([hi.astype(f32), lo.astype(f32), pads], axis=0).T.astype(bf16)

    sides = jnp.concatenate([tall(dsoft), tall(latent * temper)], axis=0)
    chunks = stack.shape[0] // 2048
    for piece, group in enumerate(loads):
        wait_all(group)
        for part in range(piece * chunks // 4, (piece + 1) * chunks // 4):
            dlogits = []
            for index in range(4 * part, 4 * part + 4):
                codes = slice(index * 512, (index + 1) * 512)
                both = dot(stack[codes, :], right)
                numer = jnp.exp2(both[:, :512])
                dlogit = (numer * (both[:, 512:] - shift)).astype(bf16)
                dlogits.append(dlogit)
                sums = jnp.concatenate([numer.astype(bf16), dlogit], axis=1)
                dcode = dot(sums, sides).T
                dcode = dcode[0:32, :] + dcode[32:64, :]
                rows = book_t[:, codes]
                scale = lax.rsqrt(jnp.sum(rows * rows, axis=0, keepdims=True) + norm_eps)
                unit = rows * scale
                grads[:, codes] = (
                    scale * (dcode - unit * jnp.sum(unit * dcode, axis=0, keepdims=True))
                ).astype(bf16)
            sums = dot(
                stack_t[0:96, part * 2048 : (part + 1) * 2048], jnp.concatenate(dlogits, axis=0)
            )
            if part == 0:
                acc[...] = sums
            else:
                acc[...] += sums
    dlatent = temper * (acc[0:32, :] + acc[32:64, :] + acc[64:96, :]) + direct
    draw = inv * (dlatent - latent * jnp.sum(latent * dlatent, axis=0, keepdims=True))
    small[0:32, :] = dot_full(draw, lnv)
    dln = dot_full(draw.T, vq_w[0:32, :])
    small[64:65, :] = jnp.sum(dln * xhat, axis=0, keepdims=True)
    small[65:66, :] = jnp.sum(dln, axis=0, keepdims=True)
    small[66:68, :] = small0[0:2, :]
    small[68:70, :] = small1[0:2, :]
    small[70:96, :] = jnp.zeros((26, 512), f32)
    small[...] = ordered(small[...], order_matrix(ids[0], True))
    for block in range(3):
        for at, part in enumerate(split2(small[block * 32 : (block + 1) * 32, :])):
            for side in range(2):
                tail[block * 2 + side, :, at * 256 : (at + 1) * 256] = part[
                    :, side * 256 : (side + 1) * 256
                ]
    tail[6:8] = jnp.zeros((2, 32, 512), bf16)
    core, z = ids[0] % 2, ids[0] // 4
    copies = []
    for slot, (at, to) in enumerate(((core, code_keep), (1 - core, code_send))):
        for k in range(4):
            part = at * 4 + (z ^ k)
            lanes = pl.ds(pl.multiple_of(part * 1024, 1024), 1024)
            copies += [
                pltpu.make_async_copy(
                    grads.at[:, lanes], to.at[k, :, pl.ds(0, 1024)], sems.at[0, slot, k]
                ),
                pltpu.make_async_copy(
                    tail.at[part], to.at[k, :, pl.ds(1024, 512)], sems.at[1, slot, k]
                ),
            ]
    for copy in copies:
        copy.start()
    de[...] = ln_back(dln, xhat, inv_ln, gain_of(norms, 2))
    for copy in copies:
        copy.wait()


SMEM = pl.BlockSpec(memory_space=pltpu.SMEM)
VMEM = pl.BlockSpec(memory_space=pltpu.VMEM)
ANY = pl.BlockSpec(memory_space=pl.ANY)


def shaped(*pairs):
    return [jax.ShapeDtypeStruct(shape, dtype) for shape, dtype in pairs]


def pin(array):
    return pltpu.with_memory_space_constraint(array, pltpu.HBM)


def call(kernel, name, in_specs, out_specs, outs, scratch, flops, after=(), carry=()):
    n_in, n_extra, n_out = len(in_specs), len(after) + len(carry), len(outs)

    def body(*refs):
        first = n_in + n_extra
        kernel(*refs[:n_in], *refs[first : first + n_out], *refs[first + n_out + len(carry) :])

    made = pl.pallas_call(
        body,
        name=name,
        in_specs=in_specs + [ANY] * n_extra,
        out_specs=out_specs + [ANY] * len(carry),
        out_shape=outs + [jax.ShapeDtypeStruct(a.shape, a.dtype) for a in carry],
        scratch_shapes=scratch,
        input_output_aliases={n_in + len(after) + i: n_out + i for i in range(len(carry))},
        compiler_params=pltpu.CompilerParams(vmem_limit_bytes=vmem_cap),
        cost_estimate=pl.CostEstimate(flops=flops, bytes_accessed=10**6, transcendentals=0),
    )

    def run(*args):
        res = made(*args, *after, *carry)
        return (*res[:n_out], list(res[n_out:]))

    return run


DMA = pltpu.SemaphoreType.DMA
ROWS2 = (512, 512)


def attn_fwd(at, marked, xs, norms, w, after=(), carry=()):
    outs = shaped((ROWS2, f32), ((8, 512), f32)) + [pltpu.HBM(ROWS2, bf16)] * 6
    scratch = [
        *[pltpu.VMEM(ROWS2, bf16)] * 3,
        pltpu.VMEM(ROWS2, f32),
        *[pltpu.VMEM(ROWS2, bf16)] * 6,
        DMA((6,)),
    ]
    x1, lse, *saved, carried = call(
        functools.partial(attn_fwd_kernel, bool(xs), w[0], len(w[1]), at),
        "attn_fwd",
        [VMEM] * (3 + len(w[1]) + len(xs)),
        [VMEM] * 2 + [ANY] * 6,
        outs,
        scratch,
        10**10,
        after,
        carry,
    )(*marked, norms, *w[1], *xs)
    return x1, (lse, *saved), carried


def mlp_fwd(at, x1, norms, ws, after=(), carry=()):
    arrays = [array for _, held in ws for array in held]
    return call(
        functools.partial(mlp_fwd_kernel, [form for form, _ in ws], len(arrays), at),
        "mlp_fwd",
        [VMEM] * (2 + len(arrays)),
        [VMEM] * 2,
        shaped((ROWS2, f32), ((256, 512), f32)),
        [pltpu.VMEM(ROWS2, bf16)],
        8 * 10**9,
        after,
        carry,
    )(x1, norms, *arrays)


def mlp_bwd(at, ids, x1, dys, norms, ws, after=(), carry=()):
    arrays = [array for _, held in ws for array in held]
    scratch = [
        *[pltpu.VMEM(ROWS2, bf16)] * 4,
        *[pltpu.VMEM(ROWS2, f32)] * len(dys),
    ]
    return call(
        functools.partial(
            mlp_bwd_kernel, len(dys) == 2, [form for form, _ in ws], len(arrays), at
        ),
        "mlp_bwd",
        [SMEM] + [VMEM] * (2 + len(arrays) + len(dys)),
        [VMEM] * 4,
        shaped((ROWS2, f32), ((8, 512), f32), *[((4, 4, 32, 2048), bf16)] * 2),
        scratch,
        15 * 10**9,
        after,
        carry,
    )(ids, x1, norms, *arrays, *dys)


def attn_bwd(at, ids, marked, xs, dx1, norms, saved, w, other_small=(), after=(), carry=()):
    width = 1024 + 128 * len(other_small)
    scratch = [
        pltpu.VMEM(ROWS2, bf16),
        pltpu.VMEM(ROWS2, f32),
        *[pltpu.VMEM(ROWS2, bf16)] * 13,
        DMA((6,)),
    ]
    outs = shaped(
        (ROWS2, f32), ((256, 512), bf16), ((8, 512), f32), *[((4, 4, 32, width), bf16)] * 2
    )
    return call(
        functools.partial(attn_bwd_kernel, bool(xs), bool(other_small), w[0], len(w[1]), at),
        "attn_bwd",
        [SMEM]
        + [VMEM] * (5 + len(w[1]))
        + [ANY] * 6
        + [VMEM] * (len(xs) + len(other_small)),
        [VMEM] * 5,
        outs,
        scratch,
        15 * 10**9,
        after,
        carry,
    )(ids, *marked, dx1, norms, saved[0], *w[1], *map(pin, saved[1:]), *xs, *other_small)


def code_prep(book_t, after=(), carry=()):
    codes = book_t.shape[1]
    return call(
        code_prep_kernel,
        "code_prep",
        [VMEM],
        [VMEM] * 2,
        shaped(((codes, 256), bf16), ((128, codes), bf16)),
        [],
        6 * 10**9,
        after,
        carry,
    )(book_t)


def vq_fwd(e, norms, vq_w, stack, stack_t, after=(), carry=()):
    return call(
        vq_fwd_kernel,
        "vq_fwd",
        [VMEM] * 3 + [ANY] * 2,
        [VMEM] * 2,
        shaped((ROWS2, f32), ((72, 512), f32)),
        [
            pltpu.VMEM((128, 512), f32),
            pltpu.VMEM(stack.shape, bf16),
            pltpu.VMEM(stack_t.shape, bf16),
            DMA((2, 4)),
        ],
        15 * 10**9,
        after,
        carry,
    )(e, norms, vq_w, pin(stack), pin(stack_t))


def vq_bwd(ids, e, du, norms, vq_w, codes, kept, smalls, after=(), carry=()):
    scratch = [
        pltpu.VMEM((96, 512), f32),
        pltpu.VMEM(codes[2].shape, bf16),
        pltpu.VMEM((96, 512), f32),
        pltpu.VMEM((8, 32, 512), bf16),
        *[pltpu.VMEM(a.shape, a.dtype) for a in codes],
        DMA((3, 4)),
        DMA((2, 2, 4)),
    ]
    return call(
        vq_bwd_kernel,
        "vq_bwd",
        [SMEM] + [VMEM] * 4 + [ANY] * 3 + [VMEM] * 3,
        [VMEM] + [ANY] * 2,
        shaped((ROWS2, f32), *[((4, 32, 1536), bf16)] * 2),
        scratch,
        25 * 10**9,
        after,
        carry,
    )(ids, e, du, norms, vq_w, *map(pin, codes), kept, *smalls)


def lines_kernel(cuts, *refs):
    first = 0
    for out, width in zip(refs[4:], cuts):
        for k in range(4):
            out[k] = refs[k][:, first : first + width]
        first += width


def stack_lines(shards, cuts, after=(), carry=()):
    return call(
        functools.partial(lines_kernel, cuts),
        "stack_lines",
        [VMEM] * 4,
        [VMEM] * len(cuts),
        shaped(*[((4, 32, width), bf16) for width in cuts]),
        [],
        1,
        after,
        carry,
    )(*shards)


def quads_kernel(*refs):
    for i in range(4):
        refs[4][i] = refs[i][...]


def stack_quads(quads, after=(), carry=()):
    return call(
        quads_kernel,
        "stack_quads",
        [VMEM] * 4,
        [VMEM],
        shaped(((4, *quads[0].shape), bf16)),
        [],
        1,
        after,
        carry,
    )(*quads)


def pack_kernel(*refs):
    hbm, outs, held, sems = refs[:4], refs[4:6], refs[6:10], refs[10]
    copies = [pltpu.make_async_copy(hbm[at], held[at], sems.at[at]) for at in range(4)]
    start_all(copies)
    wait_all(copies)
    qkv, out_t, up, down_t = held
    for layer, out in enumerate(outs):
        for index in range(3):
            out[:, index * 256 : (index + 1) * 256] = qkv[layer, index]
        out[:, 768:1024] = out_t[layer]
        out[:, 1024:2048] = up[layer]
        out[:, 2048:] = down_t[layer]


def pack_weights(*arrays):
    return call(
        pack_kernel,
        "pack_weights",
        [ANY] * 4,
        [VMEM] * 2,
        shaped(*[((32, 3072), bf16)] * 2),
        [*[pltpu.VMEM(a.shape, a.dtype) for a in arrays], DMA((4,))],
        1,
    )(*map(pin, arrays))[:-1]


def pairs_kernel(*refs):
    count = len(refs) // 3
    for at in range(count):
        refs[2 * count + at][0] = refs[2 * at][...]
        refs[2 * count + at][1] = refs[2 * at + 1][...]


def stack_pairs(pairs, after=(), carry=()):
    return call(
        pairs_kernel,
        "stack_pairs",
        [VMEM] * (2 * len(pairs)),
        [VMEM] * len(pairs),
        shaped(*[((2, *a.shape), bf16) for a, _ in pairs]),
        [],
        1,
        after,
        carry,
    )(*[array for pair in pairs for array in pair])


def gate(after, carry):
    def kernel(out):
        out[...] = jnp.zeros_like(out)

    return call(kernel, "gate", [], [VMEM], shaped(((8, 128), f32)), [], 1, after, carry)()[-1]


def rows_in_kernel(ids, *refs):
    hbm, (own, send, norms, vq_w), held, sems = refs[:7], refs[7:11], refs[11:18], refs[18]
    copies = [pltpu.make_async_copy(hbm[at], held[at], sems.at[at]) for at in range(7)]
    start_all(copies)
    matrix = order_matrix(ids[0], False)
    wait_all(copies)
    tokens, segs, cot, gains, biases, in_t, out_w = held
    for to, micro in ((send, 1 - ids[1]), (own, ids[1])):
        to[:, :512] = ordered(tokens[micro], matrix).astype(bf16)
        ids_row = segs[pl.ds(micro, 1), :].astype(f32)
        to[:, 512:640] = jnp.broadcast_to(ids_row, (128, 256)).T.astype(bf16)
    send[:, 640:] = ordered(cot[1 - ids[1]].astype(bf16), matrix).astype(bf16)
    pad = jnp.zeros((3, 512), f32)
    rows = jnp.concatenate([gains[...], pad, biases[...], pad], axis=0)
    norms[...] = ordered(rows, matrix)
    vq_w[...] = ordered(jnp.concatenate([in_t[...], out_w[...]], axis=0), matrix)


def rows_in(ids, *arrays):
    outs = shaped(
        ((256, 640), bf16), ((256, 1152), bf16), ((16, 512), f32), ((64, 512), f32)
    )
    return call(
        rows_in_kernel,
        "rows_in",
        [SMEM] + [ANY] * 7,
        [VMEM] * 4,
        outs,
        [*[pltpu.VMEM(a.shape, a.dtype) for a in arrays], DMA((7,))],
        1,
    )(ids, *map(pin, arrays))[:-1]


def joined(block):
    return block[0:16, 1024:].astype(f32) + block[16:32, 1024:].astype(f32)


def put_small(value, own, blocks):
    hi, lo = split2(value)
    own[0:16, 1024:] = hi.astype(f32) + lo.astype(f32)
    for block in blocks:
        block[0:16, 1024:] = hi
        block[16:32, 1024:] = lo


def near_kernel(ids, ins, outs):
    keep, other = ins
    for i in range(4):
        outs[i][...] = (keep[i].astype(f32) + other[i].astype(f32)).astype(outs[i].dtype)
    if keep.shape[3] == 1152:
        value = joined(keep.at[0, 0]) + joined(other.at[0, 0])
        put_small(value, outs[0].at[0], [out.at[0] for out in outs[1:]])


def near_task(keep, other):
    shape = keep.shape[1:]
    return near_kernel, [keep, other], shaped((shape, f32), *[(shape, bf16)] * 3)


def put_code(ref, first, code):
    for i in range(3):
        ref[first + i] = code[:, 1024 * i : 1024 * (i + 1)]


def get_code(ref, first):
    return jnp.concatenate([ref[first + i] for i in range(3)], axis=1)


def put_rows(ref, first, rows):
    for i in range(4):
        ref[first + i, :, :512] = rows[i * 32 : (i + 1) * 32, :]
        ref[first + i, :, 512:] = rows[128 + i * 32 : 128 + (i + 1) * 32, :]


def get_rows(ref, first):
    parts = [ref[first + i, :, :512] for i in range(4)] + [ref[first + i, :, 512:] for i in range(4)]
    return jnp.concatenate(parts, axis=0)


def code_sum(a, b):
    done = []
    for first in range(0, a.shape[1], 1536):
        total = a[:, first : first + 1024].astype(f32) + b[:, first : first + 1024].astype(f32)
        small = [
            x[:, first + 1024 : first + 1280].astype(f32) + x[:, first + 1280 : first + 1536].astype(f32)
            for x in (a, b)
        ]
        done += [total.astype(bf16), *split2(small[0] + small[1])]
    return jnp.concatenate(done, axis=1)


def fork_kernel(ids, ins, outs):
    keep, other, code, code_other = ins
    own_up, to_x, own_down, to_y, code_out = outs
    for at, (own, send, kept, sent) in enumerate(
        ((own_up, to_x, (0, 2), (1, 3)), (own_down, to_y, (0, 1), (2, 3)))
    ):
        cols = slice(1024 * at, 1024 * (at + 1))
        for j in range(2):
            own[j] = keep[kept[j], :, :, cols].astype(f32) + other[kept[j], :, :, cols].astype(f32)
            total = keep[sent[j], :, :, cols].astype(f32) + other[sent[j], :, :, cols].astype(f32)
            send[4 * j : 4 * (j + 1)] = total.astype(bf16)
    swapped = jnp.concatenate([code_other[:, 1536:], code_other[:, :1536]], axis=1)
    code_out[...] = code_sum(code[...], swapped)
    put_code(to_y, 8, code_out)


def fork_task(keep, other, code, code_other):
    outs = shaped(
        ((2, 4, 32, 1024), f32),
        ((8, 32, 1024), bf16),
        ((2, 4, 32, 1024), f32),
        ((11, 32, 1024), bf16),
        (code.shape, bf16),
    )
    return fork_kernel, [keep, other, code, code_other], outs


def half_kernel(ids, ins, outs):
    own_up, from_x, own_down, from_y, code, dx_low = ins
    up, to_y, down, to_x, code_out = outs
    for own, other, kept, send in ((own_up, from_x, up, to_y), (own_down, from_y, down, to_x)):
        kept[...] = own[0] + other[0:4].astype(f32)
        send[0:4] = (own[1] + other[4:8].astype(f32)).astype(bf16)
    code_out[...] = code_sum(code[...], get_code(from_y, 8))
    put_code(to_x, 4, code_out)
    put_rows(to_x, 7, dx_low)


def half_task(own_up, from_x, own_down, from_y, code, dx_low):
    outs = shaped(
        ((4, 32, 1024), f32),
        ((4, 32, 1024), bf16),
        ((4, 32, 1024), f32),
        ((11, 32, 1024), bf16),
        (code.shape, bf16),
    )
    return half_kernel, [own_up, from_x, own_down, from_y, code, dx_low], outs


def join_kernel(ids, ins, outs):
    own_up, from_y, own_down, from_x, code = ins
    kept, send, code_out, rows = outs
    for at, (own, other) in enumerate(((own_up, from_y), (own_down, from_x))):
        cols = slice(1024 * at, 1024 * (at + 1))
        for k in range(2):
            kept[k, :, cols] = own[2 * k] + other[2 * k].astype(f32)
            send[k, :, cols] = (own[2 * k + 1] + other[2 * k + 1].astype(f32)).astype(bf16)
    code_out[...] = code_sum(code[...], get_code(from_x, 4))
    rows[...] = get_rows(from_x, 7)


def join_task(own_up, from_y, own_down, from_x, code):
    outs = shaped(
        ((2, 32, 2048), f32), ((2, 32, 2048), bf16), (code.shape, bf16), ((256, 512), bf16)
    )
    return join_kernel, [own_up, from_y, own_down, from_x, code], outs


def line_step_kernel(ids, ins, outs):
    kept, other = ins
    outs[0][...] = kept[0] + other[0].astype(f32)
    outs[1][...] = (kept[1] + other[1].astype(f32)).astype(bf16)


def line_step_task(kept, other):
    shape = kept.shape[1:]
    return line_step_kernel, [kept, other], shaped((shape, f32), (shape, bf16))


def plane_kernel(ids, ins, outs):
    for k in range(4):
        total = ins[0][k]
        for other in ins[1:]:
            total = total + other[k].astype(f32)
        outs[k][...] = total.astype(outs[k].dtype)
    if ins[0].shape[2] == 1152:
        x, y, xy = [joined(other.at[0]) for other in ins[1:]]
        put_small((ins[0][0, 0:16, 1024:] + x) + (y + xy), outs[0], outs[1:])


def plane_task(own, others):
    shape = own.shape[1:]
    return plane_kernel, [own, *others], shaped((shape, f32), *[(shape, bf16)] * 3)


def plane_join_kernel(ids, ins, outs):
    plane_kernel(ids, ins[:4], [out.at[:, pl.ds(0, 1024)] for out in outs])
    for part, out in zip(ins[4:], outs):
        out[:, 1024:] = part[...]


def plane_join_task(own, others, *parts):
    outs = shaped(((32, 3072), f32), *[((32, 3072), bf16)] * 3)
    return plane_join_kernel, [own, *others, *parts], outs


def line_total(ins, width):
    total = ins[0][:, :width]
    for other in ins[1:]:
        total = total + other[:, :width].astype(f32)
    return total


def rows_kernel(ids, ins, outs):
    own, other = ins
    half = other.shape[0]
    matrix = order_matrix(ids[0], True)
    outs[0][ids[1]] = ordered(own[0:half, :], matrix)
    outs[0][1 - ids[1]] = ordered(other[...], matrix)


def rows_task(own, other):
    return rows_kernel, [own, other], shaped(((2, *other.shape), f32))


def code_near_kernel(ids, ins, outs):
    keep, other = ins
    for at, out in enumerate(outs):
        for i in range(2):
            out[:, 1536 * i : 1536 * (i + 1)] = code_sum(keep[2 * at + i], other[2 * at + i])


def code_near_task(keep, other):
    return code_near_kernel, [keep, other], shaped(*[((32, 3072), bf16)] * 2)


def code_add_kernel(ids, ins, outs):
    outs[0][...] = code_sum(ins[0][...], ins[1][...])


def code_add_task(a, b):
    return code_add_kernel, [a, b], shaped((a.shape, bf16))


def code_pair_kernel(ids, ins, outs):
    for at, part in enumerate(ins):
        outs[0][:, 3072 * at : 3072 * (at + 1)] = part[...]


def code_pair_task(a, b):
    return code_pair_kernel, [a, b], shaped(((32, 6144), bf16))


def finish_kernel(ids, ins, outs):
    mlp, attn, dec, code, code_other = ins[:2], ins[2:6], ins[6:10], *ins[10:]
    qkv, out_t, up, down_t, book, vq_in, vq_out, gains, biases, dec_biases, small_ref = outs
    both = line_total(dec, 3072)
    for layer, rows in enumerate((line_total(mlp, 2048), both[:, 1024:])):
        up[layer] = rows[:, :1024]
        down_t[layer] = rows[:, 1024:]
    for layer, rows in enumerate((line_total(attn, 1024), both[:, :1024])):
        for index in range(3):
            qkv[layer, index] = rows[:, index * 256 : (index + 1) * 256]
        out_t[layer] = rows[:, 768:]
    core, z = ids[0] % 2, ids[0] // 4
    for at, parts in ((core, code), (1 - core, code_other)):
        for k in range(4):
            part = at * 4 + (z ^ k)
            held = parts[:, 1536 * k : 1536 * (k + 1)].astype(f32)
            book[:, pl.ds(pl.multiple_of(part * 1024, 1024), 1024)] = held[:, :1024]
            small_ref[:, pl.ds(pl.multiple_of(part * 256, 256), 256)] = (
                held[:, 1024:1280] + held[:, 1280:1536]
            )
    small = small_ref[...]
    vq_in[...] = small[:, :512]
    vq_out[...] = small[:, 512:1024]
    rest = small[:, 1024:1536]
    k1, k2, k3 = [joined(other) for other in attn[1:]]
    packed = (attn[0][0:16, 1024:] + k1) + (k2 + k3)
    for row, out in enumerate((gains.at[0:1], biases.at[0:1], gains.at[1:2], biases.at[1:2])):
        for j in range(4):
            out[:, 128 * j : 128 * (j + 1)] = packed[row * 4 + j : row * 4 + j + 1, :]
    gains[2:3, :] = rest[0:1, :]
    biases[2:3, :] = rest[1:2, :]
    gains[3:4, :] = rest[2:3, :]
    dec_biases[0:1, :] = rest[3:4, :]
    gains[4:5, :] = rest[4:5, :]
    dec_biases[1:2, :] = rest[5:6, :]


def finish_task(own_m, other_m, own_a, line_a, own_d, line_d, code, code_other):
    outs = shaped(
        ((2, 3, 32, 256), f32),
        ((2, 32, 256), f32),
        ((2, 32, 1024), f32),
        ((2, 32, 1024), f32),
        ((32, 8192), f32),
        ((32, 512), f32),
        ((32, 512), f32),
        ((5, 512), f32),
        ((3, 512), f32),
        ((2, 512), f32),
        ((32, 2048), f32),
    )
    ins = [own_m, other_m, own_a, *line_a, own_d, *line_d, code, code_other]
    return finish_kernel, ins, outs


def run_tasks(ids, name, tasks, after=(), carry=()):
    sizes = [(len(ins), len(outs)) for _, ins, outs in tasks]
    n_in = sum(i for i, _ in sizes)

    def kernel(ids_ref, *refs):
        at_in, at_out = 0, n_in
        for (fn, _, _), (i, o) in zip(tasks, sizes):
            fn(ids_ref, refs[at_in : at_in + i], refs[at_out : at_out + o])
            at_in, at_out = at_in + i, at_out + o

    outs = [one for _, _, many in tasks for one in many]
    res = call(
        kernel, name, [SMEM] + [VMEM] * n_in, [VMEM] * len(outs), outs, [], 10**9, after, carry
    )(ids, *[one for _, many, _ in tasks for one in many])
    split, at = [], 0
    for _, o in sizes:
        split.append(res[at : at + o])
        at += o
    return (*split, res[-1])


def whole_groups(
    n_dp,
    tokens,
    segment_ids,
    norm_gains,
    norm_biases,
    w_qkv,
    w_attn_out,
    w_up,
    w_down,
    w_vq_in,
    w_vq_out,
    codebook,
    cotangent,
):
    dp_at, tp_at = lax.axis_index("dp"), lax.axis_index("tp")
    ids = jnp.stack([dp_at, tp_at]).astype(jnp.int32)

    def swap(values):
        return exchange(values, 0, 1, n_dp)

    def core(values):
        return [values, exchange(values, 1, 0, n_dp)]

    book_t = codebook.T
    enc_shard, dec_shard = pack_weights(
        w_qkv, w_attn_out.transpose(0, 2, 1), w_up, w_down.transpose(0, 2, 1)
    )
    enc_shards = spread_line(enc_shard, n_dp)
    own, send, norms, vq_w = rows_in(
        ids,
        tokens,
        segment_ids,
        cotangent,
        norm_gains,
        norm_biases,
        w_vq_in.T,
        w_vq_out,
    )
    marked = [own, swap(send)]

    attn_line, mlp_line, _ = stack_lines(enc_shards, [1024, 2048])
    stack, stack_t, _ = code_prep(book_t, [attn_line])
    codes = (stack, stack_t, book_t)
    quads, (mlp_line,) = stack_quads(
        plane_quads(attn_line, n_dp), [stack_t, marked[1]], [mlp_line]
    )
    enc_attn, quads = (QUADS, core(quads)), plane_quads(mlp_line, n_dp)
    e_x1, e_saved, (dec_shard,) = attn_fwd(
        0, marked, [], norms, enc_attn, carry=[dec_shard]
    )
    attn_line, up_line, down_line, _ = stack_lines(
        spread_line(dec_shard, n_dp), [1024] * 3, [e_x1]
    )
    quads, _ = stack_quads(quads, [attn_line])
    enc_mlp = [(QUADS, core(quads))]
    along_x, along_y = exchange(attn_line, 0, 1, n_dp), exchange(up_line, 2, 0, n_dp)
    e, _, _ = mlp_fwd(1, e_x1, norms, enc_mlp)
    attn_0, up_0, (down_line,) = stack_pairs(
        [(attn_line, along_x), (up_line, along_y)], [e], [down_line]
    )
    attn_1, up_1 = exchange(attn_0, 2, 0, n_dp), exchange(up_0, 0, 1, n_dp)
    along_x = exchange(down_line, 0, 1, n_dp)
    attn_0, up_0 = core(attn_0), core(up_0)
    u, kept, _ = vq_fwd(e, norms, vq_w, stack, stack_t)
    down_0, (attn_1, up_1) = stack_pairs(
        [(down_line, along_x)], [u, attn_0[1], up_0[1]], [attn_1, up_1]
    )
    down_1, attn_1 = exchange(down_0, 2, 0, n_dp), core(attn_1)
    dec_attn = (PAIRS_X, [attn_0[0], attn_1[0], attn_0[1], attn_1[1]])
    d_x1, d_saved, _ = attn_fwd(3, marked, [u], norms, dec_attn)
    down_1, down_0, up_1 = gate([d_x1], [down_1, down_0, up_1])
    down_0, down_1, up_1 = core(down_0), core(down_1), core(up_1)
    dec_mlp = [
        (PAIRS_Y, [up_0[0], up_1[0], up_0[1], up_1[1]]),
        (PAIRS_X, [down_0[0], down_1[0], down_0[1], down_1[1]]),
    ]

    dx1, d_small1, keep_m, send_m, _ = mlp_bwd(
        4, ids, d_x1, [cotangent, marked[1]], norms, dec_mlp
    )
    y, y_theirs, _ = mlp_fwd(4, d_x1, norms, dec_mlp, [keep_m])
    near_m, y_other = exchange(send_m, 1, 0, n_dp), swap(y_theirs)
    du, _, d_small0, keep_a, send_a, (keep_m,) = attn_bwd(
        3, ids, marked, [u], dx1, norms, d_saved, dec_attn, after=[y_theirs], carry=[keep_m]
    )
    (own_m, *lows_m), (send_a,) = run_tasks(
        ids, "sums1", [near_task(keep_m, near_m)], [y_other], [send_a]
    )
    plane_m, near_a = plane_send(lows_m, n_dp), exchange(send_a, 1, 0, n_dp)
    de, code, code_send, (own_m, keep_a) = vq_bwd(
        ids,
        e,
        du,
        norms,
        vq_w,
        codes,
        kept,
        [d_small0, d_small1],
        lows_m,
        [own_m, keep_a],
    )
    d_mlp, (own_a, *lows_a), (code, code_send) = run_tasks(
        ids,
        "sums2",
        [plane_task(own_m, plane_m), near_task(keep_a, near_a)],
        carry=[code, code_send],
    )
    plane_a, code_other = plane_send(lows_a, n_dp), exchange(code_send, 1, 0, n_dp)
    (code, code_send), _ = run_tasks(ids, "sums2b", [code_near_task(code, code_other)])
    code_other = exchange(code_send, 8, 0, n_dp)
    ex1, e_small1, keep_m, send_m, (own_a, code) = mlp_bwd(
        1, ids, e_x1, [de], norms, enc_mlp, [*lows_a, code_send], [own_a, code]
    )
    (own_d, *lows_d), (code,), (keep_m, send_m) = run_tasks(
        ids,
        "sums3",
        [plane_join_task(own_a, plane_a, *d_mlp), code_add_task(code, code_other)],
        carry=[keep_m, send_m],
    )
    near_m, code_other = exchange(send_m, 1, 0, n_dp), exchange(code, 4, 0, n_dp)
    line_d = line_send(lows_d, n_dp)
    (own_up, to_x, own_down, to_y, code), _ = run_tasks(
        ids, "sums3b", [fork_task(keep_m, near_m, code, code_other)]
    )
    from_x, from_y = exchange(to_x, 0, 1, n_dp), exchange(to_y, 2, 0, n_dp)
    dx, dx_low, _, keep_a, send_a, (own_up, own_down, code) = attn_bwd(
        0,
        ids,
        marked,
        [],
        ex1,
        norms,
        e_saved,
        enc_attn,
        [e_small1],
        [to_x, to_y],
        [own_up, own_down, code],
    )
    (own_up, to_y, own_down, to_x, code), (keep_a, send_a) = run_tasks(
        ids,
        "sums4",
        [half_task(own_up, from_x, own_down, from_y, code, dx_low)],
        line_d,
        [keep_a, send_a],
    )
    near_a = exchange(send_a, 1, 0, n_dp)
    from_y, from_x = exchange(to_y, 2, 0, n_dp), exchange(to_x, 0, 1, n_dp)
    (own_a, *lows_a), (own_up, own_down, code) = run_tasks(
        ids, "sums4b", [near_task(keep_a, near_a)], carry=[own_up, own_down, code]
    )
    plane_a = plane_send(lows_a, n_dp)
    (own_m, send_m, code, dx_other), (own_a,) = run_tasks(
        ids, "sums5", [join_task(own_up, from_y, own_down, from_x, code)], lows_a, [own_a]
    )
    other_m, code_other = exchange(send_m, 4, 0, n_dp), exchange(code, 8, 0, n_dp)
    (decoded,), (grad_tokens,), (own_a,) = run_tasks(
        ids,
        "rows_out",
        [rows_task(y, y_other), rows_task(dx, dx_other)],
        [send_m, code],
        [own_a],
    )
    (own_a, *lows_a), (own_m, send_m), (code,), _ = run_tasks(
        ids,
        "sums6",
        [
            plane_task(own_a, plane_a),
            line_step_task(own_m, other_m),
            code_pair_task(code, code_other),
        ],
    )
    line_a, other_m = line_send(lows_a, n_dp), exchange(send_m, 8, 0, n_dp)
    code_other = exchange(code, 1, 0, n_dp)
    (qkv, out_t, up, down_t, book, vq_in, vq_out, *norm_grads, _), _ = run_tasks(
        ids,
        "finish",
        [finish_task(own_m, other_m, own_a, line_a, own_d, line_d, code, code_other)],
    )
    return (
        decoded,
        grad_tokens,
        *norm_grads,
        qkv,
        out_t.transpose(0, 2, 1),
        up,
        down_t.transpose(0, 2, 1),
        vq_in.T,
        vq_out,
        book.T,
    )


def layer_norm(values, norm_gain, norm_bias):
    centred = values - jnp.mean(values, axis=-1, keepdims=True)
    spread = jnp.mean(centred * centred, axis=-1, keepdims=True)
    return centred * lax.rsqrt(spread + ln_eps) * norm_gain + norm_bias


def gelu_tanh(values):
    return (
        0.5 * values * (1.0 + jnp.tanh(gelu_coef * (values + 0.044715 * values * values * values)))
    )


def matmul(former, latter):
    return jnp.dot(former, latter, precision=highest, preferred_element_type=jnp.float32)


def normalize(values):
    return values * lax.rsqrt(jnp.sum(values * values, axis=-1, keepdims=True) + norm_eps)


def quantize(in_rows, norm_gain, norm_bias, in_w, out_w, code_w):
    latent = normalize(matmul(layer_norm(in_rows, norm_gain, norm_bias), in_w))
    code_rows = normalize(code_w)
    logits = matmul(latent, code_rows.T) * temper
    row_max = jnp.max(logits, axis=-1, keepdims=True)
    numerator = jnp.exp(logits - row_max)
    assign = numerator / jnp.sum(numerator, axis=-1, keepdims=True)
    soft_code = matmul(assign, code_rows)
    offset = latent - soft_code
    vq_loss = commit_weight * 1.25 * jnp.sum(offset * offset)
    return (matmul(soft_code, out_w), vq_loss)


def product(former, latter):
    return jnp.dot(former, latter, preferred_element_type=jnp.float32)


def product_tn(former, latter):
    return lax.dot_general(
        former, latter, (((0,), (0,)), ((), ())), preferred_element_type=jnp.float32
    )


def product_nt(former, latter):
    return lax.dot_general(
        former, latter, (((1,), (1,)), ((), ())), preferred_element_type=jnp.float32
    )


def split_heads(values):
    return values.reshape(values.shape[0], values.shape[1] // HEAD_DIM, HEAD_DIM).transpose(1, 0, 2)


def join_heads(values):
    return values.transpose(1, 0, 2).reshape(values.shape[1], values.shape[0] * HEAD_DIM)


def masked_scores(query_blk, key_h, seg_blk, seg_keys):
    scores = jnp.einsum(
        "hqd,hkd->hqk", query_blk, key_h, preferred_element_type=jnp.float32
    ) * HEAD_DIM ** (-0.5)
    return jnp.where((seg_blk[:, None] == seg_keys[None, :])[None], scores, masked_score)


def attend(query_h, key_h, value_h, seg_keys):
    block_rows = min(512, query_h.shape[1])
    block_count = query_h.shape[1] // block_rows

    def one_block(begin_row):
        query_blk = lax.dynamic_slice_in_dim(query_h, begin_row, block_rows, 1)
        seg_blk = lax.dynamic_slice_in_dim(seg_keys, begin_row, block_rows, 0)
        scores = masked_scores(query_blk, key_h, seg_blk, seg_keys)
        row_max = jnp.max(scores, axis=-1, keepdims=True)
        numerator = jnp.exp(scores - row_max)
        row_total = jnp.sum(numerator, axis=-1, keepdims=True)
        prob_low = (numerator / row_total).astype(jnp.bfloat16)
        attended = jnp.einsum("hqk,hkd->hqd", prob_low, value_h, preferred_element_type=jnp.float32)
        return (attended.astype(jnp.bfloat16), (row_max + jnp.log(row_total))[..., 0])

    starts = jnp.arange(block_count, dtype=jnp.int32) * block_rows
    attended, log_sums = lax.map(one_block, starts)
    heads_out = attended.transpose(1, 0, 2, 3).reshape(query_h.shape)
    log_sums = log_sums.transpose(1, 0, 2).reshape(query_h.shape[0], query_h.shape[1])
    return (heads_out, log_sums)


def attend_back(query_h, key_h, value_h, seg_keys, log_sums, grad_out):
    block_rows = min(512, query_h.shape[1])
    block_count = query_h.shape[1] // block_rows

    def one_block(carry, begin_row):
        grad_key, grad_value = carry
        query_blk = lax.dynamic_slice_in_dim(query_h, begin_row, block_rows, 1)
        grad_blk = lax.dynamic_slice_in_dim(grad_out, begin_row, block_rows, 1)
        lse_blk = lax.dynamic_slice_in_dim(log_sums, begin_row, block_rows, 1)
        seg_blk = lax.dynamic_slice_in_dim(seg_keys, begin_row, block_rows, 0)
        scores = masked_scores(query_blk, key_h, seg_blk, seg_keys)
        probs = jnp.exp(scores - lse_blk[..., None])
        prob_low = probs.astype(jnp.bfloat16)
        grad_value = grad_value + jnp.einsum(
            "hqk,hqd->hkd", prob_low, grad_blk, preferred_element_type=jnp.float32
        )
        grad_prob = jnp.einsum(
            "hqd,hkd->hqk", grad_blk, value_h, preferred_element_type=jnp.float32
        )
        row_dot = jnp.sum(probs * grad_prob, axis=-1, keepdims=True)
        grad_score = (probs * (grad_prob - row_dot) * HEAD_DIM ** (-0.5)).astype(jnp.bfloat16)
        grad_query = jnp.einsum(
            "hqk,hkd->hqd", grad_score, key_h, preferred_element_type=jnp.float32
        )
        grad_key = grad_key + jnp.einsum(
            "hqk,hqd->hkd", grad_score, query_blk, preferred_element_type=jnp.float32
        )
        return ((grad_key, grad_value), grad_query)

    starts = jnp.arange(block_count, dtype=jnp.int32) * block_rows
    zeros_kv = jnp.zeros(key_h.shape, jnp.float32)
    (grad_key, grad_value), grad_query = lax.scan(one_block, (zeros_kv, zeros_kv), starts)
    grad_query = grad_query.transpose(1, 0, 2, 3).reshape(query_h.shape)
    return (
        grad_query.astype(jnp.bfloat16),
        grad_key.astype(jnp.bfloat16),
        grad_value.astype(jnp.bfloat16),
    )


def spread_rows(values):
    return lax.all_gather(values, "tp", axis=0, tiled=True)


def combine_rows(partial_value):
    return lax.psum_scatter(partial_value, "tp", scatter_dimension=0, tiled=True)


def spread_grads(values):
    return lax.all_gather(values, "tp", axis=0, tiled=True)


def combine_grads(partial_value):
    return lax.psum_scatter(
        partial_value.astype(jnp.bfloat16), "tp", scatter_dimension=0, tiled=True
    ).astype(jnp.float32)


def fetch_weights(w_qkv, w_attn_out, w_up, w_down, layer):
    return (
        lax.all_gather(w_qkv[layer], "dp", axis=1, tiled=True),
        lax.all_gather(w_attn_out[layer], "dp", axis=1, tiled=True),
        lax.all_gather(w_up[layer], "dp", axis=0, tiled=True),
        lax.all_gather(w_down[layer], "dp", axis=1, tiled=True),
    )


def reduce_weight_grads(grads):
    return (
        lax.psum_scatter(
            grads[0].astype(jnp.bfloat16), "dp", scatter_dimension=1, tiled=True
        ).astype(jnp.float32),
        lax.psum_scatter(
            grads[1].astype(jnp.bfloat16), "dp", scatter_dimension=1, tiled=True
        ).astype(jnp.float32),
        lax.psum_scatter(
            grads[2].astype(jnp.bfloat16), "dp", scatter_dimension=0, tiled=True
        ).astype(jnp.float32),
        lax.psum_scatter(
            grads[3].astype(jnp.bfloat16), "dp", scatter_dimension=1, tiled=True
        ).astype(jnp.float32),
    )


def block_forward(resid_in, seg_local, gains, biases, weights):
    qkv_w, attn_w, up_w, down_w = weights
    normed = layer_norm(resid_in, gains[0], biases[0]).astype(jnp.bfloat16)
    normed_all, seg_all = (
        lax.all_gather(normed, "tp", axis=0, tiled=True),
        lax.all_gather(seg_local, "tp", axis=0, tiled=True),
    )
    query_h = split_heads(product(normed_all, qkv_w[0]).astype(jnp.bfloat16))
    key_h = split_heads(product(normed_all, qkv_w[1]).astype(jnp.bfloat16))
    value_h = split_heads(product(normed_all, qkv_w[2]).astype(jnp.bfloat16))
    heads_out, log_sums = attend(query_h, key_h, value_h, seg_all)
    attn_rows = join_heads(heads_out)
    middle = resid_in + combine_rows(product(attn_rows, attn_w))
    normed_mid = spread_rows(layer_norm(middle, gains[1], biases[1]).astype(jnp.bfloat16))
    hidden_pre = product(normed_mid, up_w)
    hidden = gelu_tanh(hidden_pre).astype(jnp.bfloat16)
    result = middle + combine_rows(product(hidden, down_w))
    kept = (
        resid_in,
        middle,
        normed_all,
        seg_all,
        query_h,
        key_h,
        value_h,
        log_sums,
        attn_rows,
        normed_mid,
        hidden_pre,
        hidden,
    )
    return (result, kept)


def block_backward(kept, gains, biases, weights, grad_result):
    (
        resid_in,
        middle,
        normed_all,
        seg_all,
        query_h,
        key_h,
        value_h,
        log_sums,
        attn_rows,
        normed_mid,
        hidden_pre,
        hidden,
    ) = kept
    qkv_w, attn_w, up_w, down_w = weights
    grad_branch = spread_grads(grad_result.astype(jnp.bfloat16))
    grad_down = product_tn(hidden, grad_branch)
    grad_hidden = product_nt(grad_branch, down_w)
    _, gelu_back = jax.vjp(gelu_tanh, hidden_pre)
    grad_pre = gelu_back(grad_hidden)[0].astype(jnp.bfloat16)
    grad_up = product_tn(normed_mid, grad_pre)
    grad_norm_mid = combine_grads(product_nt(grad_pre, up_w))
    _, norm_back_mid = jax.vjp(layer_norm, middle, gains[1], biases[1])
    grad_mid_ln, grad_gain_mid, grad_bias_mid = norm_back_mid(grad_norm_mid)
    grad_middle = grad_result + grad_mid_ln
    grad_attn_all = spread_grads(grad_middle.astype(jnp.bfloat16))
    grad_attn = product_tn(attn_rows, grad_attn_all)
    grad_heads = split_heads(product_nt(grad_attn_all, attn_w).astype(jnp.bfloat16))
    grad_query, grad_key, grad_value = attend_back(
        query_h, key_h, value_h, seg_all, log_sums, grad_heads
    )
    grad_parts = [join_heads(grad_query), join_heads(grad_key), join_heads(grad_value)]
    grad_qkv = jnp.stack([product_tn(normed_all, grad_part) for grad_part in grad_parts])
    grad_normed_part = (
        product_nt(grad_parts[0], qkv_w[0])
        + product_nt(grad_parts[1], qkv_w[1])
        + product_nt(grad_parts[2], qkv_w[2])
    )
    grad_normed = combine_grads(grad_normed_part)
    _, norm_back_in = jax.vjp(layer_norm, resid_in, gains[0], biases[0])
    grad_in_ln, grad_gain_in, grad_bias_in = norm_back_in(grad_normed)
    gain_grads = jnp.stack([grad_gain_in, grad_gain_mid])
    bias_grads = jnp.stack([grad_bias_in, grad_bias_mid])
    return (
        grad_middle + grad_in_ln,
        gain_grads,
        bias_grads,
        (grad_qkv, grad_attn, grad_up, grad_down),
    )


def local(
    tokens,
    segment_ids,
    norm_gains,
    norm_biases,
    w_qkv,
    w_attn_out,
    w_up,
    w_down,
    w_vq_in,
    w_vq_out,
    codebook,
    cotangent,
):
    gain_sum = jnp.zeros(norm_gains.shape, jnp.float32)
    bias_sum = jnp.zeros(norm_biases.shape, jnp.float32)
    vq_in_sum = jnp.zeros(w_vq_in.shape, jnp.float32)
    vq_out_sum = jnp.zeros(w_vq_out.shape, jnp.float32)
    code_sum = jnp.zeros(codebook.shape, jnp.float32)
    layer_sums = [None, None]
    outputs = []
    input_grads = []
    for micro in range(MICRO):
        resid_in = tokens[micro].astype(jnp.float32)
        seg_local = segment_ids[micro]
        enc_weights = fetch_weights(w_qkv, w_attn_out, w_up, w_down, 0)
        encoded, enc_kept = block_forward(
            resid_in, seg_local, norm_gains[0:2], norm_biases[0:2], enc_weights
        )
        (decoder_in, _), vq_back = jax.vjp(
            quantize, encoded, norm_gains[2], norm_biases[2], w_vq_in, w_vq_out, codebook
        )
        dec_weights = fetch_weights(w_qkv, w_attn_out, w_up, w_down, 1)
        decoded, dec_kept = block_forward(
            decoder_in, seg_local, norm_gains[3:5], norm_biases[3:5], dec_weights
        )
        outputs.append(decoded)
        grad_dec_in, gains_dec, biases_dec, grads_dec = block_backward(
            dec_kept, norm_gains[3:5], norm_biases[3:5], dec_weights, cotangent[micro]
        )
        grad_encoded, grad_gain_vq, grad_bias_vq, grad_in_w, grad_out_w, grad_codes = vq_back(
            (grad_dec_in, jnp.ones((), jnp.float32))
        )
        grad_input, gains_enc, biases_enc, grads_enc = block_backward(
            enc_kept, norm_gains[0:2], norm_biases[0:2], enc_weights, grad_encoded
        )
        input_grads.append(grad_input)
        gain_sum = gain_sum + jnp.concatenate([gains_enc, grad_gain_vq[None], gains_dec], axis=0)
        bias_sum = bias_sum + jnp.concatenate([biases_enc, grad_bias_vq[None], biases_dec], axis=0)
        vq_in_sum = vq_in_sum + grad_in_w
        vq_out_sum = vq_out_sum + grad_out_w
        code_sum = code_sum + grad_codes
        for layer, grads in ((0, grads_enc), (1, grads_dec)):
            reduced = reduce_weight_grads(grads)
            if layer_sums[layer] is None:
                layer_sums[layer] = reduced
            else:
                layer_sums[layer] = jax.tree.map(jnp.add, layer_sums[layer], reduced)
    gain_tot, bias_tot, vq_in_tot, vq_out_tot, code_tot = lax.psum(
        (gain_sum, bias_sum, vq_in_sum, vq_out_sum, code_sum), ("dp", "tp")
    )
    return (
        jnp.stack(outputs),
        jnp.stack(input_grads),
        gain_tot,
        bias_tot[0:3],
        bias_tot[3:5],
        jnp.stack([layer_sums[0][0], layer_sums[1][0]]),
        jnp.stack([layer_sums[0][1], layer_sums[1][1]]),
        jnp.stack([layer_sums[0][2], layer_sums[1][2]]),
        jnp.stack([layer_sums[0][3], layer_sums[1][3]]),
        vq_in_tot,
        vq_out_tot,
        code_tot,
    )


def solution(mesh):
    n_dp, n_tp = mesh.shape["dp"], mesh.shape["tp"]
    fits = n_tp == MICRO and n_dp == 16
    return jax.shard_map(
        functools.partial(whole_groups, n_dp) if fits else local,
        mesh=mesh,
        in_specs=(
            P(None, ("dp", "tp"), None),
            P(None, ("dp", "tp")),
            P(),
            P(),
            P(None, None, "dp", "tp"),
            P(None, "tp", "dp"),
            P(None, "dp", "tp"),
            P(None, "tp", "dp"),
            P(),
            P(),
            P(),
            P(None, ("dp", "tp"), None),
        ),
        out_specs=(
            P(None, ("dp", "tp"), None),
            P(None, ("dp", "tp"), None),
            P(),
            P(),
            P(),
            P(None, None, "dp", "tp"),
            P(None, "tp", "dp"),
            P(None, "dp", "tp"),
            P(None, "tp", "dp"),
            P(),
            P(),
            P(),
        ),
        check_vma=False,
    )
```

```python
import functools

import jax
import jax.numpy as jnp
from jax import lax
from jax.experimental import pallas as pl
from jax.experimental.pallas import tpu as pltpu
from jax.sharding import PartitionSpec as P

HEAD_DIM = 64
MICRO = 2
bf16 = jnp.bfloat16
f32 = jnp.float32
highest = lax.Precision.HIGHEST
ln_eps = 1e-05
norm_eps = 1e-06
temper = 10.0
commit_weight = 64.0
gelu_coef = 0.7978845608028654
masked_score = -1e30
log2e = 1.4426950408889634
vmem_cap = 34 * 1024 * 1024


PLANE = ((0, 0), (0, 1), (1, 0), (1, 1))


def exchange(values, dp_xor, tp_xor, n_dp):
    pairs = [
        (d * 2 + t, (d ^ dp_xor) * 2 + (t ^ tp_xor)) for d in range(n_dp) for t in range(2)
    ]
    return lax.ppermute(values, ("dp", "tp"), pairs)


def spread_line(shard, n_dp):
    return [shard] + [exchange(shard, 4 * k, 0, n_dp) for k in range(1, 4)]


def plane_send(lows, n_dp):
    return [exchange(low, 2 * y, x, n_dp) for (y, x), low in zip(PLANE[1:], lows)]


def line_send(lows, n_dp):
    return [exchange(low, 4 * k, 0, n_dp) for k, low in zip(range(1, 4), lows)]


def dot(a, b):
    return jnp.dot(a, b, preferred_element_type=f32)


def dot_nt(a, b, precision=None):
    return lax.dot_general(
        a, b, (((1,), (1,)), ((), ())), preferred_element_type=f32, precision=precision
    )


def dot_full(a, b):
    return jnp.dot(a, b, preferred_element_type=f32, precision=highest)


def ln_parts(x):
    centred = x - jnp.mean(x, axis=-1, keepdims=True)
    inv = lax.rsqrt(jnp.mean(centred * centred, axis=-1, keepdims=True) + ln_eps)
    return centred * inv, inv


def ln_back(grad, xhat, inv, gain):
    scaled = grad * gain
    return inv * (
        scaled
        - jnp.mean(scaled, axis=-1, keepdims=True)
        - xhat * jnp.mean(scaled * xhat, axis=-1, keepdims=True)
    )


def split2(x):
    hi = x.astype(bf16)
    return hi, (x - hi.astype(f32)).astype(bf16)


def split3(x):
    hi, _ = split2(x)
    rest = x - hi.astype(f32)
    mid = rest.astype(bf16)
    return hi, mid, (rest - mid.astype(f32)).astype(bf16)


def order_matrix(dp, inverse):
    at = lax.broadcasted_iota(jnp.int32, (512, 512), 0 if inverse else 1)
    other = lax.broadcasted_iota(jnp.int32, (512, 512), 1 if inverse else 0)
    block = at >> 5
    bits = ((block & 3) << 2) | (((block >> 2) & 1) << 1) | (block >> 3)
    return jnp.where(other == (((dp ^ bits) << 5) | (at & 31)), 1.0, 0.0).astype(bf16)


def ordered(x, matrix):
    if x.dtype == bf16:
        return dot(x, matrix)
    hi, mid, lo = split3(x)
    return (dot(hi, matrix) + dot(mid, matrix)) + dot(lo, matrix)


def w_at(a, b, t, first, width):
    parts = []
    for core in range(2):
        for y in range(2):
            if first < 1536:
                part = a[2 * core + y][t, :, :, first : first + width]
            else:
                part = b[2 * core + t][y, :, :, first - 1536 : first - 1536 + width]
            parts.append(part.reshape(128, width))
    return jnp.concatenate(parts, axis=0)


def put_grad(refs, t, cols, value):
    for core, ref in enumerate(refs):
        for y in range(2):
            rows = value[core * 256 + y * 128 : core * 256 + (y + 1) * 128]
            ref[2 * y + t, :, :, cols] = rows.reshape(4, 32, rows.shape[1])


def start_all(copies):
    for copy in copies:
        copy.start()


def wait_all(copies):
    for copy in copies:
        copy.wait()


def head_rows(ref, pair, which):
    own = ref[pl.ds(pair * 128 + which * HEAD_DIM, HEAD_DIM), :]
    zero = jnp.zeros_like(own)
    return jnp.concatenate([own, zero] if which == 0 else [zero, own], axis=0)


def segment_mask(own, other):
    ids = jnp.concatenate([own[:, 512:640], other[:, 512:640]], axis=0).astype(f32)
    return jnp.where(ids[:, 0:1] == ids.T[0:1, :], 0.0, masked_score)


def load_rows(x, own, other):
    if x is None:
        return jnp.concatenate([own[:, :512], other[:, :512]], axis=0).astype(f32)
    return x[...]


def gain_of(norms, at):
    return norms[at : at + 1, :]


def bias_of(norms, at):
    return norms[8 + at : 9 + at, :]


def attn_fwd_kernel(with_x, at, own, other, norms, *refs):
    w, refs = refs[:4], refs[4:]
    x, refs = (refs[0], refs[1:]) if with_x else (None, refs)
    x1, lse, saved, refs = refs[0], refs[1], refs[2:8], refs[8:]
    h, vt, ot, mask, qs, k, v, o, qst, kt, out_sems = refs
    keeps = [
        pltpu.make_async_copy(held, to, out_sems.at[i])
        for i, (held, to) in enumerate(zip((qs, k, v, o, qst, kt), saved))
    ]
    xf = load_rows(x, own, other)
    h[...] = (ln_parts(xf)[0] * gain_of(norms, at) + bias_of(norms, at)).astype(bf16)
    mask[...] = segment_mask(own, other)
    for t in range(2):
        cols = slice(t * 256, (t + 1) * 256)
        q = dot(h[...], w_at(w, None, t, 0, 256)).astype(bf16)
        qs[:, cols] = (q * HEAD_DIM ** (-0.5)).astype(bf16)
        k[:, cols] = dot(h[...], w_at(w, None, t, 256, 256)).astype(bf16)
        v[:, cols] = dot(h[...], w_at(w, None, t, 512, 256)).astype(bf16)
    qst[...] = qs[...].T
    kt[...] = k[...].T
    vt[...] = v[...].T
    for i in (0, 1, 2, 4, 5):
        keeps[i].start()
    for pair in range(4):
        k_pair = k[:, pair * 128 : (pair + 1) * 128]
        for which in range(2):
            scores = dot(k_pair, head_rows(qst, pair, which)) + mask[...]
            top = jnp.max(scores, axis=0, keepdims=True)
            numer = jnp.exp(scores - top).astype(bf16)
            rows = pl.ds(pair * 128 + which * HEAD_DIM, HEAD_DIM)
            left = jnp.concatenate([vt[rows, :], jnp.ones((16, 512), bf16)], axis=0)
            both = dot(left, numer)
            total = both[HEAD_DIM : HEAD_DIM + 1, :]
            ot[rows, :] = (both[:HEAD_DIM, :] / total).astype(bf16)
            lse[pl.ds(pair * 2 + which, 1), :] = top + jnp.log(total)
    o[...] = ot[...].T
    keeps[3].start()
    acc = xf
    for t in range(2):
        acc = acc + dot_nt(o[:, t * 256 : (t + 1) * 256], w_at(w, None, t, 768, 256))
    x1[...] = acc
    wait_all(keeps)


def gelu_parts(u):
    square = u * u
    tanh = jnp.tanh(gelu_coef * u * (1.0 + 0.044715 * square))
    return 0.5 * u * (1.0 + tanh), tanh, square


def mlp_weights(w):
    def up(t, part):
        return w_at(w[:4], w[4:], t, 1024 + part * 512, 512)

    def down(t, part):
        return w_at(w[:4], w[4:], t, 2048 + part * 512, 512)

    return up, down


def mlp_rows(at, x, norms, w, h2):
    up, down = mlp_weights(w)
    h2[...] = (ln_parts(x)[0] * gain_of(norms, at) + bias_of(norms, at)).astype(bf16)
    for t in range(2):
        for part in range(2):
            hidden = gelu_parts(dot(h2[...], up(t, part)))[0].astype(bf16)
            x = x + dot_nt(hidden, down(t, part))
    return x


def mlp_fwd_kernel(at, x1, norms, *refs):
    w, (y, theirs, h2) = refs[:8], refs[8:]
    rows = mlp_rows(at, x1[...], norms, w, h2)
    y[...] = rows
    theirs[...] = rows[256:, :]


def mlp_bwd_kernel(split, at, ids, x1, norms, *refs):
    up, down = mlp_weights(refs[:8])
    refs = refs[8:]
    if split:
        own, other, refs = refs[0], refs[1], refs[2:]
    else:
        dy, refs = refs[0], refs[1:]
    dx1, small, grads = refs[0], refs[1], refs[2:4]
    h2, h2t, dyb, dybt, dh2 = refs[4:9]
    if split:
        dy = refs[9]
        dy[0:256, :] = ordered(own[ids[1]], order_matrix(ids[0], False))
        dy[256:, :] = other[:, 640:].astype(f32)
    h2[...] = (ln_parts(x1[...])[0] * gain_of(norms, at) + bias_of(norms, at)).astype(bf16)
    h2t[...] = h2[...].T
    dyb[...] = dy[...].astype(bf16)
    dybt[...] = dyb[...].T
    for t in range(2):
        for part in range(2):
            cols = slice(part * 512, (part + 1) * 512)
            w_up = up(t, part)
            pre = dot(h2[...], w_up)
            hidden, tanh, square = gelu_parts(pre)
            slope = 0.5 * (1.0 + tanh) + (0.5 * gelu_coef) * pre * (1.0 - tanh * tanh) * (
                1.0 + (3 * 0.044715) * square
            )
            dhidden = dot(dyb[...], down(t, part))
            dpre = (dhidden * slope).astype(bf16)
            out_cols = slice(1024 + part * 512, 1024 + (part + 1) * 512)
            put_grad(grads, t, out_cols, dot(dybt[...], hidden.astype(bf16)).astype(bf16))
            put_grad(grads, t, cols, dot(h2t[...], dpre).astype(bf16))
            more = dot_nt(dpre, w_up)
            if t + part == 0:
                dh2[...] = more
            else:
                dh2[...] += more
    xhat, inv = ln_parts(x1[...])
    grad = dh2[...]
    small[0:1, :] = jnp.sum(grad * xhat, axis=0, keepdims=True)
    small[1:2, :] = jnp.sum(grad, axis=0, keepdims=True)
    dx1[...] = dy[...] + ln_back(grad, xhat, inv, gain_of(norms, at))


def pack_rows(rows):
    cut = [rows[i : i + 1, 128 * j : 128 * (j + 1)] for i in range(4) for j in range(4)]
    return jnp.concatenate(split2(jnp.concatenate(cut, axis=0)), axis=0)


def attn_bwd_kernel(with_x, with_small, at, ids, own, other, dx1, norms, lse, *refs):
    w, saved, refs = refs[:4], refs[4:10], refs[10:]
    x, refs = (refs[0], refs[1:]) if with_x else (None, refs)
    if with_small:
        other_small, refs = refs[0], refs[1:]
    dx, dx_low, small, grads = refs[0], refs[1], refs[2], refs[3:5]
    h, mask, do, dot_t, dqt, dq, dk, dv, flip, qs, k, v, o, qst, kt, in_sems = refs[5:]
    takes = [
        pltpu.make_async_copy(held, to, in_sems.at[i])
        for i, (held, to) in enumerate(zip(saved, (qs, k, v, o, qst, kt)))
    ]
    start_all(takes)
    xf = load_rows(x, own, other)
    h[...] = (ln_parts(xf)[0] * gain_of(norms, at) + bias_of(norms, at)).astype(bf16)
    mask[...] = segment_mask(own, other)
    low = dx1[...].astype(bf16)
    flip[...] = low.T
    wait_all(takes)
    for t in range(2):
        cols = slice(t * 256, (t + 1) * 256)
        do[:, cols] = dot(low, w_at(w, None, t, 768, 256)).astype(bf16)
        put_grad(grads, t, slice(768, 1024), dot(flip[...], o[:, cols]).astype(bf16))
    dot_t[...] = do[...].T
    first = lax.broadcasted_iota(jnp.int32, (512, 128), 1) < HEAD_DIM
    for pair in range(4):
        lanes = slice(pair * 128, (pair + 1) * 128)
        dvs, dks = [], []
        for which in range(2):
            head = pair * 2 + which
            rows = pl.ds(head * HEAD_DIM, HEAD_DIM)
            scores = dot(k[:, lanes], head_rows(qst, pair, which)) + mask[...]
            probs = jnp.exp(scores - lse[head : head + 1, :])
            dprobs = dot(v[:, lanes], head_rows(dot_t, pair, which))
            shift = jnp.sum(probs * dprobs, axis=0, keepdims=True)
            dscore = (probs * (dprobs - shift)).astype(bf16)
            dvs.append(dot(probs.astype(bf16), do[:, lanes]))
            dks.append(dot(dscore, qs[:, lanes]))
            dqt[rows, :] = (dot(kt[rows, :], dscore) * HEAD_DIM ** (-0.5)).astype(bf16)
        dv[:, lanes] = jnp.where(first, dvs[0], dvs[1]).astype(bf16)
        dk[:, lanes] = jnp.where(first, dks[0], dks[1]).astype(bf16)
    dq[...] = dqt[...].T
    flip[...] = h[...].T
    grad = jnp.zeros((512, 512), f32)
    for t in range(2):
        cols = slice(t * 256, (t + 1) * 256)
        for index, part in enumerate((dq, dk, dv)):
            w_cols = slice(index * 256, (index + 1) * 256)
            put_grad(grads, t, w_cols, dot(flip[...], part[:, cols]).astype(bf16))
            grad = grad + dot_nt(part[:, cols], w_at(w, None, t, index * 256, 256))
    xhat, inv = ln_parts(xf)
    small[0:1, :] = jnp.sum(grad * xhat, axis=0, keepdims=True)
    small[1:2, :] = jnp.sum(grad, axis=0, keepdims=True)
    if with_small:
        rows = jnp.concatenate([small[0:2, :], other_small[0:2, :], jnp.zeros((4, 512), f32)], axis=0)
        packed = pack_rows(ordered(rows, order_matrix(ids[0], True)))
        for out in grads:
            for i in range(4):
                for z in range(4):
                    out[i, z, :, 1024:1152] = packed
    total = dx1[...] + ln_back(grad, xhat, inv, gain_of(norms, at))
    dx[...] = total
    dx_low[...] = total[256:, :].astype(bf16)


def code_prep_kernel(book_t, stack, stack_t):
    def one_chunk(index, _):
        lanes = pl.ds(pl.multiple_of(index * 512, 512), 512)
        rows = book_t[:, lanes]
        unit = rows * lax.rsqrt(jnp.sum(rows * rows, axis=0, keepdims=True) + norm_eps)
        hi, mid, lo = split3(unit)
        stack_t[:, lanes] = jnp.concatenate([hi, mid, lo, jnp.ones((32, 512), bf16)], axis=0)
        tall = jnp.concatenate([hi, mid, lo, hi, mid, hi, jnp.zeros((64, 512), bf16)], axis=0)
        stack[lanes, :] = tall.T
        return 0

    lax.fori_loop(0, book_t.shape[1] // 512, one_chunk, 0)


def factor_stack(x):
    hi, mid, lo = split3(x)
    return jnp.concatenate([hi, hi, hi, mid, mid, lo, jnp.zeros((64, x.shape[1]), bf16)], axis=0)


def code_loads(pairs, sems):
    loads = []
    for piece in range(4):
        group = []
        for at, (held, to, by_row) in enumerate(pairs):
            size = held.shape[0 if by_row else 1] // 4
            part = pl.ds(piece * size, size)
            place = (part, slice(None)) if by_row else (slice(None), part)
            group.append(pltpu.make_async_copy(held.at[place], to.at[place], sems.at[at, piece]))
        start_all(group)
        loads.append(group)
    return loads


def mlp_vq_kernel(x1, norms, vq_w, stack_hbm, stack_t_hbm, *refs):
    w, (e, u, kept, h2, acc, stack, stack_t, sems) = refs[:8], refs[8:]
    loads = code_loads([(stack_hbm, stack, True), (stack_t_hbm, stack_t, False)], sems)
    e[...] = mlp_rows(1, x1[...], norms, w, h2)
    lnv = ln_parts(e[...])[0] * gain_of(norms, 2) + bias_of(norms, 2)
    raw = dot_nt(vq_w[0:32, :], lnv, highest)
    inv = lax.rsqrt(jnp.sum(raw * raw, axis=0, keepdims=True) + norm_eps)
    latent = raw * inv
    right = factor_stack(latent * (temper * log2e))
    chunks = stack.shape[0] // 2048
    for piece, group in enumerate(loads):
        wait_all(group)
        for part in range(piece * chunks // 4, (piece + 1) * chunks // 4):
            numers = []
            for index in range(4 * part, 4 * part + 4):
                codes = slice(index * 512, (index + 1) * 512)
                numers.append(jnp.exp2(dot(stack[codes, :], right)).astype(bf16))
            sums = dot(
                stack_t[:, part * 2048 : (part + 1) * 2048], jnp.concatenate(numers, axis=0)
            )
            if part == 0:
                acc[...] = sums
            else:
                acc[...] += sums
    total = acc[96:97, :]
    soft = (acc[0:32, :] + acc[32:64, :] + acc[64:96, :]) / total
    kept[0:32, :] = latent
    kept[32:64, :] = soft
    kept[64:65, :] = total
    kept[65:66, :] = inv
    u[...] = dot_full(soft.T, vq_w[32:64, :])


def vq_bwd_kernel(ids, e, du, norms, vq_w, stack_hbm, stack_t_hbm, book_hbm, kept, *refs):
    small0, small1, de, code_keep, code_send = refs[:5]
    acc, grads, small, tail, stack, stack_t, book_t, load_sems, sems = refs[5:]
    loads = code_loads(
        [(stack_hbm, stack, True), (stack_t_hbm, stack_t, False), (book_hbm, book_t, False)],
        load_sems,
    )
    xhat, inv_ln = ln_parts(e[...])
    lnv = xhat * gain_of(norms, 2) + bias_of(norms, 2)
    latent, soft = kept[0:32, :], kept[32:64, :]
    total, inv = kept[64:65, :], kept[65:66, :]
    direct = (2.0 * 1.25 * commit_weight) * (latent - soft)
    dsoft = dot_nt(vq_w[32:64, :], du[...], highest) - direct
    small[32:64, :] = dot_full(soft, du[...])
    shift = jnp.sum(dsoft * soft, axis=0, keepdims=True) / total
    dsoft = dsoft / total
    right = jnp.concatenate(
        [factor_stack(latent * (temper * log2e)), factor_stack(dsoft)], axis=1
    )
    pads = jnp.zeros((64, 512), f32)

    def tall(x):
        hi, lo = split2(x)
        return jnp.concatenate([hi.astype(f32), lo.astype(f32), pads], axis=0).T.astype(bf16)

    sides = jnp.concatenate([tall(dsoft), tall(latent * temper)], axis=0)
    chunks = stack.shape[0] // 2048
    for piece, group in enumerate(loads):
        wait_all(group)
        for part in range(piece * chunks // 4, (piece + 1) * chunks // 4):
            dlogits = []
            for index in range(4 * part, 4 * part + 4):
                codes = slice(index * 512, (index + 1) * 512)
                both = dot(stack[codes, :], right)
                numer = jnp.exp2(both[:, :512])
                dlogit = (numer * (both[:, 512:] - shift)).astype(bf16)
                dlogits.append(dlogit)
                sums = jnp.concatenate([numer.astype(bf16), dlogit], axis=1)
                dcode = dot(sums, sides).T
                dcode = dcode[0:32, :] + dcode[32:64, :]
                rows = book_t[:, codes]
                scale = lax.rsqrt(jnp.sum(rows * rows, axis=0, keepdims=True) + norm_eps)
                unit = rows * scale
                grads[:, codes] = (
                    scale * (dcode - unit * jnp.sum(unit * dcode, axis=0, keepdims=True))
                ).astype(bf16)
            sums = dot(
                stack_t[0:96, part * 2048 : (part + 1) * 2048], jnp.concatenate(dlogits, axis=0)
            )
            if part == 0:
                acc[...] = sums
            else:
                acc[...] += sums
    dlatent = temper * (acc[0:32, :] + acc[32:64, :] + acc[64:96, :]) + direct
    draw = inv * (dlatent - latent * jnp.sum(latent * dlatent, axis=0, keepdims=True))
    small[0:32, :] = dot_full(draw, lnv)
    dln = dot_full(draw.T, vq_w[0:32, :])
    small[64:65, :] = jnp.sum(dln * xhat, axis=0, keepdims=True)
    small[65:66, :] = jnp.sum(dln, axis=0, keepdims=True)
    small[66:68, :] = small0[0:2, :]
    small[68:70, :] = small1[0:2, :]
    small[70:96, :] = jnp.zeros((26, 512), f32)
    small[...] = ordered(small[...], order_matrix(ids[0], True))
    for block in range(3):
        for at, part in enumerate(split2(small[block * 32 : (block + 1) * 32, :])):
            for side in range(2):
                tail[block * 2 + side, :, at * 256 : (at + 1) * 256] = part[
                    :, side * 256 : (side + 1) * 256
                ]
    tail[6:8] = jnp.zeros((2, 32, 512), bf16)
    core, z = ids[0] % 2, ids[0] // 4
    copies = []
    for slot, (at, to) in enumerate(((core, code_keep), (1 - core, code_send))):
        for k in range(4):
            part = at * 4 + (z ^ k)
            lanes = pl.ds(pl.multiple_of(part * 1024, 1024), 1024)
            copies += [
                pltpu.make_async_copy(
                    grads.at[:, lanes], to.at[k, :, pl.ds(0, 1024)], sems.at[0, slot, k]
                ),
                pltpu.make_async_copy(
                    tail.at[part], to.at[k, :, pl.ds(1024, 512)], sems.at[1, slot, k]
                ),
            ]
    for copy in copies:
        copy.start()
    de[...] = ln_back(dln, xhat, inv_ln, gain_of(norms, 2))
    for copy in copies:
        copy.wait()


SMEM = pl.BlockSpec(memory_space=pltpu.SMEM)
VMEM = pl.BlockSpec(memory_space=pltpu.VMEM)
ANY = pl.BlockSpec(memory_space=pl.ANY)


def shaped(*pairs):
    return [jax.ShapeDtypeStruct(shape, dtype) for shape, dtype in pairs]


def pin(array):
    return pltpu.with_memory_space_constraint(array, pltpu.HBM)


def call(kernel, name, in_specs, out_specs, outs, scratch, flops, after=(), carry=()):
    n_in, n_extra, n_out = len(in_specs), len(after) + len(carry), len(outs)

    def body(*refs):
        first = n_in + n_extra
        kernel(*refs[:n_in], *refs[first : first + n_out], *refs[first + n_out + len(carry) :])

    made = pl.pallas_call(
        body,
        name=name,
        in_specs=in_specs + [ANY] * n_extra,
        out_specs=out_specs + [ANY] * len(carry),
        out_shape=outs + [jax.ShapeDtypeStruct(a.shape, a.dtype) for a in carry],
        scratch_shapes=scratch,
        input_output_aliases={n_in + len(after) + i: n_out + i for i in range(len(carry))},
        compiler_params=pltpu.CompilerParams(vmem_limit_bytes=vmem_cap),
        cost_estimate=pl.CostEstimate(flops=flops, bytes_accessed=10**6, transcendentals=0),
    )

    def run(*args):
        res = made(*args, *after, *carry)
        return (*res[:n_out], list(res[n_out:]))

    return run


DMA = pltpu.SemaphoreType.DMA
ROWS2 = (512, 512)


def attn_fwd(at, marked, xs, norms, w, after=(), carry=()):
    outs = shaped((ROWS2, f32), ((8, 512), f32)) + [pltpu.HBM(ROWS2, bf16)] * 6
    scratch = [
        *[pltpu.VMEM(ROWS2, bf16)] * 3,
        pltpu.VMEM(ROWS2, f32),
        *[pltpu.VMEM(ROWS2, bf16)] * 6,
        DMA((6,)),
    ]
    x1, lse, *saved, carried = call(
        functools.partial(attn_fwd_kernel, bool(xs), at),
        "attn_fwd",
        [VMEM] * (7 + len(xs)),
        [VMEM] * 2 + [ANY] * 6,
        outs,
        scratch,
        10**10,
        after,
        carry,
    )(*marked, norms, *w[:4], *xs)
    return x1, (lse, *saved), carried


def mlp_fwd(at, x1, norms, w, after=(), carry=()):
    return call(
        functools.partial(mlp_fwd_kernel, at),
        "mlp_fwd",
        [VMEM] * 10,
        [VMEM] * 2,
        shaped((ROWS2, f32), ((256, 512), f32)),
        [pltpu.VMEM(ROWS2, bf16)],
        8 * 10**9,
        after,
        carry,
    )(x1, norms, *w)


def mlp_bwd(at, ids, x1, dys, norms, w, after=(), carry=()):
    scratch = [
        *[pltpu.VMEM(ROWS2, bf16)] * 4,
        *[pltpu.VMEM(ROWS2, f32)] * len(dys),
    ]
    return call(
        functools.partial(mlp_bwd_kernel, len(dys) == 2, at),
        "mlp_bwd",
        [SMEM] + [VMEM] * (10 + len(dys)),
        [VMEM] * 4,
        shaped((ROWS2, f32), ((8, 512), f32), *[((4, 4, 32, 2048), bf16)] * 2),
        scratch,
        15 * 10**9,
        after,
        carry,
    )(ids, x1, norms, *w, *dys)


def attn_bwd(at, ids, marked, xs, dx1, norms, saved, w, other_small=(), after=(), carry=()):
    width = 1024 + 128 * len(other_small)
    scratch = [
        pltpu.VMEM(ROWS2, bf16),
        pltpu.VMEM(ROWS2, f32),
        *[pltpu.VMEM(ROWS2, bf16)] * 13,
        DMA((6,)),
    ]
    outs = shaped(
        (ROWS2, f32), ((256, 512), bf16), ((8, 512), f32), *[((4, 4, 32, width), bf16)] * 2
    )
    return call(
        functools.partial(attn_bwd_kernel, bool(xs), bool(other_small), at),
        "attn_bwd",
        [SMEM]
        + [VMEM] * 9
        + [ANY] * 6
        + [VMEM] * (len(xs) + len(other_small)),
        [VMEM] * 5,
        outs,
        scratch,
        15 * 10**9,
        after,
        carry,
    )(ids, *marked, dx1, norms, saved[0], *w[:4], *map(pin, saved[1:]), *xs, *other_small)


def code_prep(book_t, after=(), carry=()):
    codes = book_t.shape[1]
    return call(
        code_prep_kernel,
        "code_prep",
        [VMEM],
        [VMEM] * 2,
        shaped(((codes, 256), bf16), ((128, codes), bf16)),
        [],
        6 * 10**9,
        after,
        carry,
    )(book_t)


def mlp_vq(x1, norms, vq_w, stack, stack_t, w, after=(), carry=()):
    return call(
        mlp_vq_kernel,
        "mlp_vq",
        [VMEM] * 3 + [ANY] * 2 + [VMEM] * 8,
        [VMEM] * 3,
        shaped((ROWS2, f32), (ROWS2, f32), ((72, 512), f32)),
        [
            pltpu.VMEM(ROWS2, bf16),
            pltpu.VMEM((128, 512), f32),
            pltpu.VMEM(stack.shape, bf16),
            pltpu.VMEM(stack_t.shape, bf16),
            DMA((2, 4)),
        ],
        25 * 10**9,
        after,
        carry,
    )(x1, norms, vq_w, pin(stack), pin(stack_t), *w)


def vq_bwd(ids, e, du, norms, vq_w, codes, kept, smalls, after=(), carry=()):
    scratch = [
        pltpu.VMEM((96, 512), f32),
        pltpu.VMEM(codes[2].shape, bf16),
        pltpu.VMEM((96, 512), f32),
        pltpu.VMEM((8, 32, 512), bf16),
        *[pltpu.VMEM(a.shape, a.dtype) for a in codes],
        DMA((3, 4)),
        DMA((2, 2, 4)),
    ]
    return call(
        vq_bwd_kernel,
        "vq_bwd",
        [SMEM] + [VMEM] * 4 + [ANY] * 3 + [VMEM] * 3,
        [VMEM] + [ANY] * 2,
        shaped((ROWS2, f32), *[((4, 32, 1536), bf16)] * 2),
        scratch,
        25 * 10**9,
        after,
        carry,
    )(ids, e, du, norms, vq_w, *map(pin, codes), kept, *smalls)


def lines_kernel(cuts, *refs):
    first = 0
    for out, width in zip(refs[4:], cuts):
        for k in range(4):
            out[k] = refs[k][:, first : first + width]
        first += width


def stack_lines(shards, cuts, after=(), carry=()):
    return call(
        functools.partial(lines_kernel, cuts),
        "stack_lines",
        [VMEM] * 4,
        [VMEM] * len(cuts),
        shaped(*[((4, 32, width), bf16) for width in cuts]),
        [],
        1,
        after,
        carry,
    )(*shards)


def pack_kernel(*refs):
    hbm, outs, held, sems = refs[:4], refs[4:6], refs[6:10], refs[10]
    copies = [pltpu.make_async_copy(hbm[at], held[at], sems.at[at]) for at in range(4)]
    start_all(copies)
    wait_all(copies)
    qkv, out_t, up, down_t = held
    for layer, out in enumerate(outs):
        for index in range(3):
            out[:, index * 256 : (index + 1) * 256] = qkv[layer, index]
        out[:, 768:1024] = out_t[layer]
        out[:, 1024:2048] = up[layer]
        out[:, 2048:] = down_t[layer]


def pack_weights(*arrays):
    return call(
        pack_kernel,
        "pack_weights",
        [ANY] * 4,
        [VMEM] * 2,
        shaped(*[((32, 3072), bf16)] * 2),
        [*[pltpu.VMEM(a.shape, a.dtype) for a in arrays], DMA((4,))],
        1,
    )(*map(pin, arrays))[:-1]


def pairs_kernel(*refs):
    count = len(refs) // 3
    for at in range(count):
        refs[2 * count + at][0] = refs[2 * at][...]
        refs[2 * count + at][1] = refs[2 * at + 1][...]


def stack_pairs(pairs, after=(), carry=()):
    return call(
        pairs_kernel,
        "stack_pairs",
        [VMEM] * (2 * len(pairs)),
        [VMEM] * len(pairs),
        shaped(*[((2, *a.shape), bf16) for a, _ in pairs]),
        [],
        1,
        after,
        carry,
    )(*[array for pair in pairs for array in pair])


def gate(after, carry):
    def kernel(out):
        out[...] = jnp.zeros_like(out)

    return call(kernel, "gate", [], [VMEM], shaped(((8, 128), f32)), [], 1, after, carry)()[-1]


def rows_in_kernel(ids, *refs):
    hbm, (own, send, norms, vq_w), held, sems = refs[:7], refs[7:11], refs[11:18], refs[18]
    copies = [pltpu.make_async_copy(hbm[at], held[at], sems.at[at]) for at in range(7)]
    start_all(copies)
    matrix = order_matrix(ids[0], False)
    wait_all(copies)
    tokens, segs, cot, gains, biases, in_t, out_w = held
    for to, micro in ((send, 1 - ids[1]), (own, ids[1])):
        to[:, :512] = ordered(tokens[micro], matrix).astype(bf16)
        ids_row = segs[pl.ds(micro, 1), :].astype(f32)
        to[:, 512:640] = jnp.broadcast_to(ids_row, (128, 256)).T.astype(bf16)
    send[:, 640:] = ordered(cot[1 - ids[1]].astype(bf16), matrix).astype(bf16)
    pad = jnp.zeros((3, 512), f32)
    rows = jnp.concatenate([gains[...], pad, biases[...], pad], axis=0)
    norms[...] = ordered(rows, matrix)
    vq_w[...] = ordered(jnp.concatenate([in_t[...], out_w[...]], axis=0), matrix)


def rows_in(ids, *arrays):
    outs = shaped(
        ((256, 640), bf16), ((256, 1152), bf16), ((16, 512), f32), ((64, 512), f32)
    )
    return call(
        rows_in_kernel,
        "rows_in",
        [SMEM] + [ANY] * 7,
        [VMEM] * 4,
        outs,
        [*[pltpu.VMEM(a.shape, a.dtype) for a in arrays], DMA((7,))],
        1,
    )(ids, *map(pin, arrays))[:-1]


def joined(block):
    return block[0:16, 1024:].astype(f32) + block[16:32, 1024:].astype(f32)


def put_small(value, own, blocks):
    hi, lo = split2(value)
    own[0:16, 1024:] = hi.astype(f32) + lo.astype(f32)
    for block in blocks:
        block[0:16, 1024:] = hi
        block[16:32, 1024:] = lo


def near_kernel(ids, ins, outs):
    keep, other = ins
    for i in range(4):
        outs[i][...] = (keep[i].astype(f32) + other[i].astype(f32)).astype(outs[i].dtype)
    if keep.shape[3] == 1152:
        value = joined(keep.at[0, 0]) + joined(other.at[0, 0])
        put_small(value, outs[0].at[0], [out.at[0] for out in outs[1:]])


def near_task(keep, other):
    shape = keep.shape[1:]
    return near_kernel, [keep, other], shaped((shape, f32), *[(shape, bf16)] * 3)


def put_code(ref, first, code):
    for i in range(3):
        ref[first + i] = code[:, 1024 * i : 1024 * (i + 1)]


def get_code(ref, first):
    return jnp.concatenate([ref[first + i] for i in range(3)], axis=1)


def put_rows(ref, first, rows):
    for i in range(4):
        ref[first + i, :, :512] = rows[i * 32 : (i + 1) * 32, :]
        ref[first + i, :, 512:] = rows[128 + i * 32 : 128 + (i + 1) * 32, :]


def get_rows(ref, first):
    parts = [ref[first + i, :, :512] for i in range(4)] + [ref[first + i, :, 512:] for i in range(4)]
    return jnp.concatenate(parts, axis=0)


def code_sum(a, b):
    done = []
    for first in range(0, a.shape[1], 1536):
        total = a[:, first : first + 1024].astype(f32) + b[:, first : first + 1024].astype(f32)
        small = [
            x[:, first + 1024 : first + 1280].astype(f32) + x[:, first + 1280 : first + 1536].astype(f32)
            for x in (a, b)
        ]
        done += [total.astype(bf16), *split2(small[0] + small[1])]
    return jnp.concatenate(done, axis=1)


def fork_kernel(ids, ins, outs):
    keep, other, code, code_other = ins
    own_up, to_x, own_down, to_y, code_out = outs
    for at, (own, send, kept, sent) in enumerate(
        ((own_up, to_x, (0, 2), (1, 3)), (own_down, to_y, (0, 1), (2, 3)))
    ):
        cols = slice(1024 * at, 1024 * (at + 1))
        for j in range(2):
            own[j] = keep[kept[j], :, :, cols].astype(f32) + other[kept[j], :, :, cols].astype(f32)
            total = keep[sent[j], :, :, cols].astype(f32) + other[sent[j], :, :, cols].astype(f32)
            send[4 * j : 4 * (j + 1)] = total.astype(bf16)
    swapped = jnp.concatenate([code_other[:, 1536:], code_other[:, :1536]], axis=1)
    code_out[...] = code_sum(code[...], swapped)
    put_code(to_x, 8, code_out)


def fork_task(keep, other, code, code_other):
    outs = shaped(
        ((2, 4, 32, 1024), f32),
        ((11, 32, 1024), bf16),
        ((2, 4, 32, 1024), f32),
        ((8, 32, 1024), bf16),
        (code.shape, bf16),
    )
    return fork_kernel, [keep, other, code, code_other], outs


def half_kernel(ids, ins, outs):
    own_up, from_x, own_down, from_y, code, dx_low = ins
    up, to_y, down, to_x, code_out = outs
    for own, other, kept, send in ((own_up, from_x, up, to_y), (own_down, from_y, down, to_x)):
        kept[...] = own[0] + other[0:4].astype(f32)
        send[0:4] = (own[1] + other[4:8].astype(f32)).astype(bf16)
    code_out[...] = code_sum(code[...], get_code(from_x, 8))
    put_code(to_y, 4, code_out)
    put_rows(to_x, 4, dx_low)


def half_task(own_up, from_x, own_down, from_y, code, dx_low):
    outs = shaped(
        ((4, 32, 1024), f32),
        ((7, 32, 1024), bf16),
        ((4, 32, 1024), f32),
        ((8, 32, 1024), bf16),
        (code.shape, bf16),
    )
    return half_kernel, [own_up, from_x, own_down, from_y, code, dx_low], outs


def join_kernel(ids, ins, outs):
    own_up, from_y, own_down, from_x, code = ins
    kept, send, code_out, rows = outs
    for at, (own, other) in enumerate(((own_up, from_y), (own_down, from_x))):
        cols = slice(1024 * at, 1024 * (at + 1))
        for k in range(2):
            kept[k, :, cols] = own[2 * k] + other[2 * k].astype(f32)
            send[k, :, cols] = (own[2 * k + 1] + other[2 * k + 1].astype(f32)).astype(bf16)
    code_out[...] = code_sum(code[...], get_code(from_y, 4))
    rows[...] = get_rows(from_x, 4)


def join_task(own_up, from_y, own_down, from_x, code):
    outs = shaped(
        ((2, 32, 2048), f32), ((2, 32, 2048), bf16), (code.shape, bf16), ((256, 512), bf16)
    )
    return join_kernel, [own_up, from_y, own_down, from_x, code], outs


def line_step_kernel(ids, ins, outs):
    kept, other = ins
    outs[0][...] = kept[0] + other[0].astype(f32)
    outs[1][...] = (kept[1] + other[1].astype(f32)).astype(bf16)


def line_step_task(kept, other):
    shape = kept.shape[1:]
    return line_step_kernel, [kept, other], shaped((shape, f32), (shape, bf16))


def plane_kernel(ids, ins, outs):
    for k in range(4):
        total = ins[0][k]
        for other in ins[1:]:
            total = total + other[k].astype(f32)
        outs[k][...] = total.astype(outs[k].dtype)
    if ins[0].shape[2] == 1152:
        x, y, xy = [joined(other.at[0]) for other in ins[1:]]
        put_small((ins[0][0, 0:16, 1024:] + x) + (y + xy), outs[0], outs[1:])


def plane_task(own, others):
    shape = own.shape[1:]
    return plane_kernel, [own, *others], shaped((shape, f32), *[(shape, bf16)] * 3)


def plane_join_kernel(ids, ins, outs):
    plane_kernel(ids, ins[:4], [out.at[:, pl.ds(0, 1024)] for out in outs])
    for part, out in zip(ins[4:], outs):
        out[:, 1024:] = part[...]


def plane_join_task(own, others, *parts):
    outs = shaped(((32, 3072), f32), *[((32, 3072), bf16)] * 3)
    return plane_join_kernel, [own, *others, *parts], outs


def line_total(ins, width):
    total = ins[0][:, :width]
    for other in ins[1:]:
        total = total + other[:, :width].astype(f32)
    return total


def rows_kernel(ids, ins, outs):
    own, other = ins
    half = other.shape[0]
    matrix = order_matrix(ids[0], True)
    outs[0][ids[1]] = ordered(own[0:half, :], matrix)
    outs[0][1 - ids[1]] = ordered(other[...], matrix)


def rows_task(own, other):
    return rows_kernel, [own, other], shaped(((2, *other.shape), f32))


def code_near_kernel(ids, ins, outs):
    keep, other = ins
    for at, out in enumerate(outs):
        for i in range(2):
            out[:, 1536 * i : 1536 * (i + 1)] = code_sum(keep[2 * at + i], other[2 * at + i])


def code_near_task(keep, other):
    return code_near_kernel, [keep, other], shaped(*[((32, 3072), bf16)] * 2)


def code_add_kernel(ids, ins, outs):
    outs[0][...] = code_sum(ins[0][...], ins[1][...])


def code_add_task(a, b):
    return code_add_kernel, [a, b], shaped((a.shape, bf16))


def code_pair_kernel(ids, ins, outs):
    for at, part in enumerate(ins):
        outs[0][:, 3072 * at : 3072 * (at + 1)] = part[...]


def code_pair_task(a, b):
    return code_pair_kernel, [a, b], shaped(((32, 6144), bf16))


def finish_kernel(ids, ins, outs):
    mlp, attn, dec, code, code_other = ins[:2], ins[2:6], ins[6:10], *ins[10:]
    qkv, out_t, up, down_t, book, vq_in, vq_out, gains, biases, dec_biases, small_ref = outs
    both = line_total(dec, 3072)
    for layer, rows in enumerate((line_total(mlp, 2048), both[:, 1024:])):
        up[layer] = rows[:, :1024]
        down_t[layer] = rows[:, 1024:]
    for layer, rows in enumerate((line_total(attn, 1024), both[:, :1024])):
        for index in range(3):
            qkv[layer, index] = rows[:, index * 256 : (index + 1) * 256]
        out_t[layer] = rows[:, 768:]
    core, z = ids[0] % 2, ids[0] // 4
    for at, parts in ((core, code), (1 - core, code_other)):
        for k in range(4):
            part = at * 4 + (z ^ k)
            held = parts[:, 1536 * k : 1536 * (k + 1)].astype(f32)
            book[:, pl.ds(pl.multiple_of(part * 1024, 1024), 1024)] = held[:, :1024]
            small_ref[:, pl.ds(pl.multiple_of(part * 256, 256), 256)] = (
                held[:, 1024:1280] + held[:, 1280:1536]
            )
    small = small_ref[...]
    vq_in[...] = small[:, :512]
    vq_out[...] = small[:, 512:1024]
    rest = small[:, 1024:1536]
    k1, k2, k3 = [joined(other) for other in attn[1:]]
    packed = (attn[0][0:16, 1024:] + k1) + (k2 + k3)
    for row, out in enumerate((gains.at[0:1], biases.at[0:1], gains.at[1:2], biases.at[1:2])):
        for j in range(4):
            out[:, 128 * j : 128 * (j + 1)] = packed[row * 4 + j : row * 4 + j + 1, :]
    gains[2:3, :] = rest[0:1, :]
    biases[2:3, :] = rest[1:2, :]
    gains[3:4, :] = rest[2:3, :]
    dec_biases[0:1, :] = rest[3:4, :]
    gains[4:5, :] = rest[4:5, :]
    dec_biases[1:2, :] = rest[5:6, :]


def finish_task(own_m, other_m, own_a, line_a, own_d, line_d, code, code_other):
    outs = shaped(
        ((2, 3, 32, 256), f32),
        ((2, 32, 256), f32),
        ((2, 32, 1024), f32),
        ((2, 32, 1024), f32),
        ((32, 8192), f32),
        ((32, 512), f32),
        ((32, 512), f32),
        ((5, 512), f32),
        ((3, 512), f32),
        ((2, 512), f32),
        ((32, 2048), f32),
    )
    ins = [own_m, other_m, own_a, *line_a, own_d, *line_d, code, code_other]
    return finish_kernel, ins, outs


def run_tasks(ids, name, tasks, after=(), carry=()):
    sizes = [(len(ins), len(outs)) for _, ins, outs in tasks]
    n_in = sum(i for i, _ in sizes)

    def kernel(ids_ref, *refs):
        at_in, at_out = 0, n_in
        for (fn, _, _), (i, o) in zip(tasks, sizes):
            fn(ids_ref, refs[at_in : at_in + i], refs[at_out : at_out + o])
            at_in, at_out = at_in + i, at_out + o

    outs = [one for _, _, many in tasks for one in many]
    res = call(
        kernel, name, [SMEM] + [VMEM] * n_in, [VMEM] * len(outs), outs, [], 10**9, after, carry
    )(ids, *[one for _, many, _ in tasks for one in many])
    split, at = [], 0
    for _, o in sizes:
        split.append(res[at : at + o])
        at += o
    return (*split, res[-1])


def whole_groups(
    n_dp,
    tokens,
    segment_ids,
    norm_gains,
    norm_biases,
    w_qkv,
    w_attn_out,
    w_up,
    w_down,
    w_vq_in,
    w_vq_out,
    codebook,
    cotangent,
):
    dp_at, tp_at = lax.axis_index("dp"), lax.axis_index("tp")
    ids = jnp.stack([dp_at, tp_at]).astype(jnp.int32)

    def swap(values):
        return exchange(values, 0, 1, n_dp)

    def core(values):
        return [values, exchange(values, 1, 0, n_dp)]

    book_t = codebook.T
    enc_shard, dec_shard = pack_weights(
        w_qkv, w_attn_out.transpose(0, 2, 1), w_up, w_down.transpose(0, 2, 1)
    )
    enc_shards = spread_line(enc_shard, n_dp)
    own, send, norms, vq_w = rows_in(
        ids,
        tokens,
        segment_ids,
        cotangent,
        norm_gains,
        norm_biases,
        w_vq_in.T,
        w_vq_out,
    )
    marked = [own, swap(send)]

    line_a, line_b, (dec_shard,) = stack_lines(enc_shards, [1536] * 2, carry=[dec_shard])
    along_x, along_y = exchange(line_a, 0, 1, n_dp), exchange(line_b, 2, 0, n_dp)
    dec_shards = spread_line(dec_shard, n_dp)
    stack, stack_t, _ = code_prep(book_t, [line_a])
    codes = (stack, stack_t, book_t)
    a_0, b_0, _ = stack_pairs([(line_a, along_x), (line_b, along_y)], [stack_t, marked[1]])
    a_1, b_1 = exchange(a_0, 2, 0, n_dp), exchange(b_0, 0, 1, n_dp)
    line_a, line_b, _ = stack_lines(dec_shards, [1536] * 2, [a_1, b_1])
    enc_w = [a_0, a_1, exchange(a_0, 1, 0, n_dp), exchange(a_1, 1, 0, n_dp)]
    enc_w += [b_0, b_1, exchange(b_0, 1, 0, n_dp), exchange(b_1, 1, 0, n_dp)]
    along_x, along_y = exchange(line_a, 0, 1, n_dp), exchange(line_b, 2, 0, n_dp)
    e_x1, e_saved, _ = attn_fwd(0, marked, [], norms, enc_w)
    a_0, b_0, _ = stack_pairs([(line_a, along_x), (line_b, along_y)], [e_x1])
    a_1, b_1 = exchange(a_0, 2, 0, n_dp), exchange(b_0, 0, 1, n_dp)
    dec_w = [a_0, exchange(a_0, 1, 0, n_dp), b_0, exchange(b_0, 1, 0, n_dp)]
    e, u, kept, _ = mlp_vq(e_x1, norms, vq_w, stack, stack_t, enc_w, [a_0, b_0])
    a_1, b_1 = gate([u], [a_1, b_1])
    a_1, b_1 = core(a_1), core(b_1)
    dec_w = [dec_w[0], a_1[0], dec_w[1], a_1[1], dec_w[2], b_1[0], dec_w[3], b_1[1]]
    d_x1, d_saved, _ = attn_fwd(3, marked, [u], norms, dec_w)

    dx1, d_small1, keep_m, send_m, _ = mlp_bwd(
        4, ids, d_x1, [cotangent, marked[1]], norms, dec_w
    )
    y, y_theirs, _ = mlp_fwd(4, d_x1, norms, dec_w, [keep_m])
    near_m, y_other = exchange(send_m, 1, 0, n_dp), swap(y_theirs)
    du, _, d_small0, keep_a, send_a, (keep_m,) = attn_bwd(
        3, ids, marked, [u], dx1, norms, d_saved, dec_w, after=[y_theirs], carry=[keep_m]
    )
    (own_m, *lows_m), (send_a,) = run_tasks(
        ids, "sums1", [near_task(keep_m, near_m)], [y_other], [send_a]
    )
    plane_m, near_a = plane_send(lows_m, n_dp), exchange(send_a, 1, 0, n_dp)
    de, code, code_send, (own_m, keep_a) = vq_bwd(
        ids,
        e,
        du,
        norms,
        vq_w,
        codes,
        kept,
        [d_small0, d_small1],
        lows_m,
        [own_m, keep_a],
    )
    d_mlp, (own_a, *lows_a), (code, code_send) = run_tasks(
        ids,
        "sums2",
        [plane_task(own_m, plane_m), near_task(keep_a, near_a)],
        carry=[code, code_send],
    )
    plane_a, code_other = plane_send(lows_a, n_dp), exchange(code_send, 1, 0, n_dp)
    (code, code_send), _ = run_tasks(ids, "sums2b", [code_near_task(code, code_other)])
    code_other = exchange(code_send, 8, 0, n_dp)
    ex1, e_small1, keep_m, send_m, (own_a, code) = mlp_bwd(
        1, ids, e_x1, [de], norms, enc_w, [*lows_a, code_send], [own_a, code]
    )
    (own_d, *lows_d), (code,), (keep_m, send_m) = run_tasks(
        ids,
        "sums3",
        [plane_join_task(own_a, plane_a, *d_mlp), code_add_task(code, code_other)],
        carry=[keep_m, send_m],
    )
    near_m, code_other = exchange(send_m, 1, 0, n_dp), exchange(code, 4, 0, n_dp)
    (own_up, to_x, own_down, to_y, code), lows_d = run_tasks(
        ids, "sums3b", [fork_task(keep_m, near_m, code, code_other)], carry=lows_d
    )
    line_d = line_send(lows_d, n_dp)
    from_x, from_y = exchange(to_x, 0, 1, n_dp), exchange(to_y, 2, 0, n_dp)
    dx, dx_low, _, keep_a, send_a, (own_up, own_down, code) = attn_bwd(
        0,
        ids,
        marked,
        [],
        ex1,
        norms,
        e_saved,
        enc_w,
        [e_small1],
        [to_x, to_y],
        [own_up, own_down, code],
    )
    (own_up, to_y, own_down, to_x, code), (keep_a, send_a) = run_tasks(
        ids,
        "sums4",
        [half_task(own_up, from_x, own_down, from_y, code, dx_low)],
        line_d,
        [keep_a, send_a],
    )
    near_a = exchange(send_a, 1, 0, n_dp)
    from_y, from_x = exchange(to_y, 2, 0, n_dp), exchange(to_x, 0, 1, n_dp)
    (own_a, *lows_a), (own_up, own_down, code) = run_tasks(
        ids, "sums4b", [near_task(keep_a, near_a)], carry=[own_up, own_down, code]
    )
    plane_a = plane_send(lows_a, n_dp)
    (own_m, send_m, code, dx_other), (own_a,) = run_tasks(
        ids, "sums5", [join_task(own_up, from_y, own_down, from_x, code)], lows_a, [own_a]
    )
    other_m, code_other = exchange(send_m, 4, 0, n_dp), exchange(code, 8, 0, n_dp)
    (decoded,), (grad_tokens,), (own_a,) = run_tasks(
        ids,
        "rows_out",
        [rows_task(y, y_other), rows_task(dx, dx_other)],
        [send_m, code],
        [own_a],
    )
    (own_a, *lows_a), (own_m, send_m), (code,), _ = run_tasks(
        ids,
        "sums6",
        [
            plane_task(own_a, plane_a),
            line_step_task(own_m, other_m),
            code_pair_task(code, code_other),
        ],
    )
    line_a, other_m = line_send(lows_a, n_dp), exchange(send_m, 8, 0, n_dp)
    code_other = exchange(code, 1, 0, n_dp)
    (qkv, out_t, up, down_t, book, vq_in, vq_out, *norm_grads, _), _ = run_tasks(
        ids,
        "finish",
        [finish_task(own_m, other_m, own_a, line_a, own_d, line_d, code, code_other)],
    )
    return (
        decoded,
        grad_tokens,
        *norm_grads,
        qkv,
        out_t.transpose(0, 2, 1),
        up,
        down_t.transpose(0, 2, 1),
        vq_in.T,
        vq_out,
        book.T,
    )


def layer_norm(values, norm_gain, norm_bias):
    centred = values - jnp.mean(values, axis=-1, keepdims=True)
    spread = jnp.mean(centred * centred, axis=-1, keepdims=True)
    return centred * lax.rsqrt(spread + ln_eps) * norm_gain + norm_bias


def gelu_tanh(values):
    return (
        0.5 * values * (1.0 + jnp.tanh(gelu_coef * (values + 0.044715 * values * values * values)))
    )


def matmul(former, latter):
    return jnp.dot(former, latter, precision=highest, preferred_element_type=jnp.float32)


def normalize(values):
    return values * lax.rsqrt(jnp.sum(values * values, axis=-1, keepdims=True) + norm_eps)


def quantize(in_rows, norm_gain, norm_bias, in_w, out_w, code_w):
    latent = normalize(matmul(layer_norm(in_rows, norm_gain, norm_bias), in_w))
    code_rows = normalize(code_w)
    logits = matmul(latent, code_rows.T) * temper
    row_max = jnp.max(logits, axis=-1, keepdims=True)
    numerator = jnp.exp(logits - row_max)
    assign = numerator / jnp.sum(numerator, axis=-1, keepdims=True)
    soft_code = matmul(assign, code_rows)
    offset = latent - soft_code
    vq_loss = commit_weight * 1.25 * jnp.sum(offset * offset)
    return (matmul(soft_code, out_w), vq_loss)


def product(former, latter):
    return jnp.dot(former, latter, preferred_element_type=jnp.float32)


def product_tn(former, latter):
    return lax.dot_general(
        former, latter, (((0,), (0,)), ((), ())), preferred_element_type=jnp.float32
    )


def product_nt(former, latter):
    return lax.dot_general(
        former, latter, (((1,), (1,)), ((), ())), preferred_element_type=jnp.float32
    )


def split_heads(values):
    return values.reshape(values.shape[0], values.shape[1] // HEAD_DIM, HEAD_DIM).transpose(1, 0, 2)


def join_heads(values):
    return values.transpose(1, 0, 2).reshape(values.shape[1], values.shape[0] * HEAD_DIM)


def masked_scores(query_blk, key_h, seg_blk, seg_keys):
    scores = jnp.einsum(
        "hqd,hkd->hqk", query_blk, key_h, preferred_element_type=jnp.float32
    ) * HEAD_DIM ** (-0.5)
    return jnp.where((seg_blk[:, None] == seg_keys[None, :])[None], scores, masked_score)


def attend(query_h, key_h, value_h, seg_keys):
    block_rows = min(512, query_h.shape[1])
    block_count = query_h.shape[1] // block_rows

    def one_block(begin_row):
        query_blk = lax.dynamic_slice_in_dim(query_h, begin_row, block_rows, 1)
        seg_blk = lax.dynamic_slice_in_dim(seg_keys, begin_row, block_rows, 0)
        scores = masked_scores(query_blk, key_h, seg_blk, seg_keys)
        row_max = jnp.max(scores, axis=-1, keepdims=True)
        numerator = jnp.exp(scores - row_max)
        row_total = jnp.sum(numerator, axis=-1, keepdims=True)
        prob_low = (numerator / row_total).astype(jnp.bfloat16)
        attended = jnp.einsum("hqk,hkd->hqd", prob_low, value_h, preferred_element_type=jnp.float32)
        return (attended.astype(jnp.bfloat16), (row_max + jnp.log(row_total))[..., 0])

    starts = jnp.arange(block_count, dtype=jnp.int32) * block_rows
    attended, log_sums = lax.map(one_block, starts)
    heads_out = attended.transpose(1, 0, 2, 3).reshape(query_h.shape)
    log_sums = log_sums.transpose(1, 0, 2).reshape(query_h.shape[0], query_h.shape[1])
    return (heads_out, log_sums)


def attend_back(query_h, key_h, value_h, seg_keys, log_sums, grad_out):
    block_rows = min(512, query_h.shape[1])
    block_count = query_h.shape[1] // block_rows

    def one_block(carry, begin_row):
        grad_key, grad_value = carry
        query_blk = lax.dynamic_slice_in_dim(query_h, begin_row, block_rows, 1)
        grad_blk = lax.dynamic_slice_in_dim(grad_out, begin_row, block_rows, 1)
        lse_blk = lax.dynamic_slice_in_dim(log_sums, begin_row, block_rows, 1)
        seg_blk = lax.dynamic_slice_in_dim(seg_keys, begin_row, block_rows, 0)
        scores = masked_scores(query_blk, key_h, seg_blk, seg_keys)
        probs = jnp.exp(scores - lse_blk[..., None])
        prob_low = probs.astype(jnp.bfloat16)
        grad_value = grad_value + jnp.einsum(
            "hqk,hqd->hkd", prob_low, grad_blk, preferred_element_type=jnp.float32
        )
        grad_prob = jnp.einsum(
            "hqd,hkd->hqk", grad_blk, value_h, preferred_element_type=jnp.float32
        )
        row_dot = jnp.sum(probs * grad_prob, axis=-1, keepdims=True)
        grad_score = (probs * (grad_prob - row_dot) * HEAD_DIM ** (-0.5)).astype(jnp.bfloat16)
        grad_query = jnp.einsum(
            "hqk,hkd->hqd", grad_score, key_h, preferred_element_type=jnp.float32
        )
        grad_key = grad_key + jnp.einsum(
            "hqk,hqd->hkd", grad_score, query_blk, preferred_element_type=jnp.float32
        )
        return ((grad_key, grad_value), grad_query)

    starts = jnp.arange(block_count, dtype=jnp.int32) * block_rows
    zeros_kv = jnp.zeros(key_h.shape, jnp.float32)
    (grad_key, grad_value), grad_query = lax.scan(one_block, (zeros_kv, zeros_kv), starts)
    grad_query = grad_query.transpose(1, 0, 2, 3).reshape(query_h.shape)
    return (
        grad_query.astype(jnp.bfloat16),
        grad_key.astype(jnp.bfloat16),
        grad_value.astype(jnp.bfloat16),
    )


def spread_rows(values):
    return lax.all_gather(values, "tp", axis=0, tiled=True)


def combine_rows(partial_value):
    return lax.psum_scatter(partial_value, "tp", scatter_dimension=0, tiled=True)


def spread_grads(values):
    return lax.all_gather(values, "tp", axis=0, tiled=True)


def combine_grads(partial_value):
    return lax.psum_scatter(
        partial_value.astype(jnp.bfloat16), "tp", scatter_dimension=0, tiled=True
    ).astype(jnp.float32)


def fetch_weights(w_qkv, w_attn_out, w_up, w_down, layer):
    return (
        lax.all_gather(w_qkv[layer], "dp", axis=1, tiled=True),
        lax.all_gather(w_attn_out[layer], "dp", axis=1, tiled=True),
        lax.all_gather(w_up[layer], "dp", axis=0, tiled=True),
        lax.all_gather(w_down[layer], "dp", axis=1, tiled=True),
    )


def reduce_weight_grads(grads):
    return (
        lax.psum_scatter(
            grads[0].astype(jnp.bfloat16), "dp", scatter_dimension=1, tiled=True
        ).astype(jnp.float32),
        lax.psum_scatter(
            grads[1].astype(jnp.bfloat16), "dp", scatter_dimension=1, tiled=True
        ).astype(jnp.float32),
        lax.psum_scatter(
            grads[2].astype(jnp.bfloat16), "dp", scatter_dimension=0, tiled=True
        ).astype(jnp.float32),
        lax.psum_scatter(
            grads[3].astype(jnp.bfloat16), "dp", scatter_dimension=1, tiled=True
        ).astype(jnp.float32),
    )


def block_forward(resid_in, seg_local, gains, biases, weights):
    qkv_w, attn_w, up_w, down_w = weights
    normed = layer_norm(resid_in, gains[0], biases[0]).astype(jnp.bfloat16)
    normed_all, seg_all = (
        lax.all_gather(normed, "tp", axis=0, tiled=True),
        lax.all_gather(seg_local, "tp", axis=0, tiled=True),
    )
    query_h = split_heads(product(normed_all, qkv_w[0]).astype(jnp.bfloat16))
    key_h = split_heads(product(normed_all, qkv_w[1]).astype(jnp.bfloat16))
    value_h = split_heads(product(normed_all, qkv_w[2]).astype(jnp.bfloat16))
    heads_out, log_sums = attend(query_h, key_h, value_h, seg_all)
    attn_rows = join_heads(heads_out)
    middle = resid_in + combine_rows(product(attn_rows, attn_w))
    normed_mid = spread_rows(layer_norm(middle, gains[1], biases[1]).astype(jnp.bfloat16))
    hidden_pre = product(normed_mid, up_w)
    hidden = gelu_tanh(hidden_pre).astype(jnp.bfloat16)
    result = middle + combine_rows(product(hidden, down_w))
    kept = (
        resid_in,
        middle,
        normed_all,
        seg_all,
        query_h,
        key_h,
        value_h,
        log_sums,
        attn_rows,
        normed_mid,
        hidden_pre,
        hidden,
    )
    return (result, kept)


def block_backward(kept, gains, biases, weights, grad_result):
    (
        resid_in,
        middle,
        normed_all,
        seg_all,
        query_h,
        key_h,
        value_h,
        log_sums,
        attn_rows,
        normed_mid,
        hidden_pre,
        hidden,
    ) = kept
    qkv_w, attn_w, up_w, down_w = weights
    grad_branch = spread_grads(grad_result.astype(jnp.bfloat16))
    grad_down = product_tn(hidden, grad_branch)
    grad_hidden = product_nt(grad_branch, down_w)
    _, gelu_back = jax.vjp(gelu_tanh, hidden_pre)
    grad_pre = gelu_back(grad_hidden)[0].astype(jnp.bfloat16)
    grad_up = product_tn(normed_mid, grad_pre)
    grad_norm_mid = combine_grads(product_nt(grad_pre, up_w))
    _, norm_back_mid = jax.vjp(layer_norm, middle, gains[1], biases[1])
    grad_mid_ln, grad_gain_mid, grad_bias_mid = norm_back_mid(grad_norm_mid)
    grad_middle = grad_result + grad_mid_ln
    grad_attn_all = spread_grads(grad_middle.astype(jnp.bfloat16))
    grad_attn = product_tn(attn_rows, grad_attn_all)
    grad_heads = split_heads(product_nt(grad_attn_all, attn_w).astype(jnp.bfloat16))
    grad_query, grad_key, grad_value = attend_back(
        query_h, key_h, value_h, seg_all, log_sums, grad_heads
    )
    grad_parts = [join_heads(grad_query), join_heads(grad_key), join_heads(grad_value)]
    grad_qkv = jnp.stack([product_tn(normed_all, grad_part) for grad_part in grad_parts])
    grad_normed_part = (
        product_nt(grad_parts[0], qkv_w[0])
        + product_nt(grad_parts[1], qkv_w[1])
        + product_nt(grad_parts[2], qkv_w[2])
    )
    grad_normed = combine_grads(grad_normed_part)
    _, norm_back_in = jax.vjp(layer_norm, resid_in, gains[0], biases[0])
    grad_in_ln, grad_gain_in, grad_bias_in = norm_back_in(grad_normed)
    gain_grads = jnp.stack([grad_gain_in, grad_gain_mid])
    bias_grads = jnp.stack([grad_bias_in, grad_bias_mid])
    return (
        grad_middle + grad_in_ln,
        gain_grads,
        bias_grads,
        (grad_qkv, grad_attn, grad_up, grad_down),
    )


def local(
    tokens,
    segment_ids,
    norm_gains,
    norm_biases,
    w_qkv,
    w_attn_out,
    w_up,
    w_down,
    w_vq_in,
    w_vq_out,
    codebook,
    cotangent,
):
    gain_sum = jnp.zeros(norm_gains.shape, jnp.float32)
    bias_sum = jnp.zeros(norm_biases.shape, jnp.float32)
    vq_in_sum = jnp.zeros(w_vq_in.shape, jnp.float32)
    vq_out_sum = jnp.zeros(w_vq_out.shape, jnp.float32)
    code_sum = jnp.zeros(codebook.shape, jnp.float32)
    layer_sums = [None, None]
    outputs = []
    input_grads = []
    for micro in range(MICRO):
        resid_in = tokens[micro].astype(jnp.float32)
        seg_local = segment_ids[micro]
        enc_weights = fetch_weights(w_qkv, w_attn_out, w_up, w_down, 0)
        encoded, enc_kept = block_forward(
            resid_in, seg_local, norm_gains[0:2], norm_biases[0:2], enc_weights
        )
        (decoder_in, _), vq_back = jax.vjp(
            quantize, encoded, norm_gains[2], norm_biases[2], w_vq_in, w_vq_out, codebook
        )
        dec_weights = fetch_weights(w_qkv, w_attn_out, w_up, w_down, 1)
        decoded, dec_kept = block_forward(
            decoder_in, seg_local, norm_gains[3:5], norm_biases[3:5], dec_weights
        )
        outputs.append(decoded)
        grad_dec_in, gains_dec, biases_dec, grads_dec = block_backward(
            dec_kept, norm_gains[3:5], norm_biases[3:5], dec_weights, cotangent[micro]
        )
        grad_encoded, grad_gain_vq, grad_bias_vq, grad_in_w, grad_out_w, grad_codes = vq_back(
            (grad_dec_in, jnp.ones((), jnp.float32))
        )
        grad_input, gains_enc, biases_enc, grads_enc = block_backward(
            enc_kept, norm_gains[0:2], norm_biases[0:2], enc_weights, grad_encoded
        )
        input_grads.append(grad_input)
        gain_sum = gain_sum + jnp.concatenate([gains_enc, grad_gain_vq[None], gains_dec], axis=0)
        bias_sum = bias_sum + jnp.concatenate([biases_enc, grad_bias_vq[None], biases_dec], axis=0)
        vq_in_sum = vq_in_sum + grad_in_w
        vq_out_sum = vq_out_sum + grad_out_w
        code_sum = code_sum + grad_codes
        for layer, grads in ((0, grads_enc), (1, grads_dec)):
            reduced = reduce_weight_grads(grads)
            if layer_sums[layer] is None:
                layer_sums[layer] = reduced
            else:
                layer_sums[layer] = jax.tree.map(jnp.add, layer_sums[layer], reduced)
    gain_tot, bias_tot, vq_in_tot, vq_out_tot, code_tot = lax.psum(
        (gain_sum, bias_sum, vq_in_sum, vq_out_sum, code_sum), ("dp", "tp")
    )
    return (
        jnp.stack(outputs),
        jnp.stack(input_grads),
        gain_tot,
        bias_tot[0:3],
        bias_tot[3:5],
        jnp.stack([layer_sums[0][0], layer_sums[1][0]]),
        jnp.stack([layer_sums[0][1], layer_sums[1][1]]),
        jnp.stack([layer_sums[0][2], layer_sums[1][2]]),
        jnp.stack([layer_sums[0][3], layer_sums[1][3]]),
        vq_in_tot,
        vq_out_tot,
        code_tot,
    )


def solution(mesh):
    n_dp, n_tp = mesh.shape["dp"], mesh.shape["tp"]
    fits = n_tp == MICRO and n_dp == 16
    return jax.shard_map(
        functools.partial(whole_groups, n_dp) if fits else local,
        mesh=mesh,
        in_specs=(
            P(None, ("dp", "tp"), None),
            P(None, ("dp", "tp")),
            P(),
            P(),
            P(None, None, "dp", "tp"),
            P(None, "tp", "dp"),
            P(None, "dp", "tp"),
            P(None, "tp", "dp"),
            P(),
            P(),
            P(),
            P(None, ("dp", "tp"), None),
        ),
        out_specs=(
            P(None, ("dp", "tp"), None),
            P(None, ("dp", "tp"), None),
            P(),
            P(),
            P(),
            P(None, None, "dp", "tp"),
            P(None, "tp", "dp"),
            P(None, "dp", "tp"),
            P(None, "tp", "dp"),
            P(),
            P(),
            P(),
        ),
        check_vma=False,
    )
```

```python
import functools

import jax
import jax.numpy as jnp
from jax import lax
from jax.experimental import pallas as pl
from jax.experimental.pallas import tpu as pltpu
from jax.sharding import PartitionSpec as P

HEAD_DIM = 64
MICRO = 2
bf16 = jnp.bfloat16
f32 = jnp.float32
highest = lax.Precision.HIGHEST
ln_eps = 1e-05
norm_eps = 1e-06
temper = 10.0
commit_weight = 64.0
gelu_coef = 0.7978845608028654
masked_score = -1e30
log2e = 1.4426950408889634
vmem_cap = 26 * 1024 * 1024


PLANE = ((0, 0), (0, 1), (1, 0), (1, 1))


def exchange(values, dp_xor, tp_xor, n_dp):
    pairs = [
        (d * 2 + t, (d ^ dp_xor) * 2 + (t ^ tp_xor)) for d in range(n_dp) for t in range(2)
    ]
    return lax.ppermute(values, ("dp", "tp"), pairs)


def spread_line(shard, n_dp):
    return [shard] + [exchange(shard, 4 * k, 0, n_dp) for k in range(1, 4)]


def plane_send(lows, n_dp):
    return [exchange(low, 2 * y, x, n_dp) for (y, x), low in zip(PLANE[1:], lows)]


def line_send(lows, n_dp):
    return [exchange(low, 4 * k, 0, n_dp) for k, low in zip(range(1, 4), lows)]


def dot(a, b):
    return jnp.dot(a, b, preferred_element_type=f32)


def dot_nt(a, b, precision=None):
    return lax.dot_general(
        a, b, (((1,), (1,)), ((), ())), preferred_element_type=f32, precision=precision
    )


def dot_full(a, b):
    return jnp.dot(a, b, preferred_element_type=f32, precision=highest)


def ln_parts(x):
    centred = x - jnp.mean(x, axis=-1, keepdims=True)
    inv = lax.rsqrt(jnp.mean(centred * centred, axis=-1, keepdims=True) + ln_eps)
    return centred * inv, inv


def ln_back(grad, xhat, inv, gain):
    scaled = grad * gain
    return inv * (
        scaled
        - jnp.mean(scaled, axis=-1, keepdims=True)
        - xhat * jnp.mean(scaled * xhat, axis=-1, keepdims=True)
    )


def split2(x):
    hi = x.astype(bf16)
    return hi, (x - hi.astype(f32)).astype(bf16)


def split3(x):
    hi, _ = split2(x)
    rest = x - hi.astype(f32)
    mid = rest.astype(bf16)
    return hi, mid, (rest - mid.astype(f32)).astype(bf16)


def order_matrix(dp, inverse):
    at = lax.broadcasted_iota(jnp.int32, (512, 512), 0 if inverse else 1)
    other = lax.broadcasted_iota(jnp.int32, (512, 512), 1 if inverse else 0)
    block = at >> 5
    bits = ((block & 3) << 2) | (((block >> 2) & 1) << 1) | (block >> 3)
    return jnp.where(other == (((dp ^ bits) << 5) | (at & 31)), 1.0, 0.0).astype(bf16)


def ordered(x, matrix):
    if x.dtype == bf16:
        return dot(x, matrix)
    hi, mid, lo = split3(x)
    return (dot(hi, matrix) + dot(mid, matrix)) + dot(lo, matrix)


def w_at(a, b, t, first, width):
    parts = []
    for core in range(2):
        for y in range(2):
            if first < 1536:
                part = a[2 * core + y][t, :, :, first : first + width]
            else:
                part = b[2 * core + t][y, :, :, first - 1536 : first - 1536 + width]
            parts.append(part.reshape(128, width))
    return jnp.concatenate(parts, axis=0)


def put_grad(refs, t, cols, value):
    for core, ref in enumerate(refs):
        for y in range(2):
            rows = value[core * 256 + y * 128 : core * 256 + (y + 1) * 128]
            ref[2 * y + t, :, :, cols] = rows.reshape(4, 32, rows.shape[1])


def start_all(copies):
    for copy in copies:
        copy.start()


def wait_all(copies):
    for copy in copies:
        copy.wait()


def head_rows(ref, pair, which):
    own = ref[pl.ds(pair * 128 + which * HEAD_DIM, HEAD_DIM), :]
    zero = jnp.zeros_like(own)
    return jnp.concatenate([own, zero] if which == 0 else [zero, own], axis=0)


def segment_mask(own, other):
    ids = jnp.concatenate([own[:, 512:640], other[:, 512:640]], axis=0).astype(f32)
    return jnp.where(ids[:, 0:1] == ids.T[0:1, :], 0.0, masked_score)


def load_rows(x, own, other):
    if x is None:
        return jnp.concatenate([own[:, :512], other[:, :512]], axis=0).astype(f32)
    return x[...]


def gain_of(norms, at):
    return norms[at : at + 1, :]


def bias_of(norms, at):
    return norms[8 + at : 9 + at, :]


def attn_fwd_kernel(with_x, at, own, other, norms, *refs):
    w, refs = refs[:4], refs[4:]
    x, refs = (refs[0], refs[1:]) if with_x else (None, refs)
    x1, lse, saved, refs = refs[0], refs[1], refs[2:8], refs[8:]
    h, vt, ot, mask, qs, k, v, o, qst, kt, out_sems = refs
    keeps = [
        pltpu.make_async_copy(held, to, out_sems.at[i])
        for i, (held, to) in enumerate(zip((qs, k, v, o, qst, kt), saved))
    ]
    xf = load_rows(x, own, other)
    h[...] = (ln_parts(xf)[0] * gain_of(norms, at) + bias_of(norms, at)).astype(bf16)
    mask[...] = segment_mask(own, other)
    for t in range(2):
        cols = slice(t * 256, (t + 1) * 256)
        q = dot(h[...], w_at(w, None, t, 0, 256)).astype(bf16)
        qs[:, cols] = (q * HEAD_DIM ** (-0.5)).astype(bf16)
        k[:, cols] = dot(h[...], w_at(w, None, t, 256, 256)).astype(bf16)
        v[:, cols] = dot(h[...], w_at(w, None, t, 512, 256)).astype(bf16)
    qst[...] = qs[...].T
    kt[...] = k[...].T
    vt[...] = v[...].T
    for i in (0, 1, 2, 4, 5):
        keeps[i].start()
    for pair in range(4):
        k_pair = k[:, pair * 128 : (pair + 1) * 128]
        for which in range(2):
            scores = dot(k_pair, head_rows(qst, pair, which)) + mask[...]
            top = jnp.max(scores, axis=0, keepdims=True)
            numer = jnp.exp(scores - top).astype(bf16)
            rows = pl.ds(pair * 128 + which * HEAD_DIM, HEAD_DIM)
            left = jnp.concatenate([vt[rows, :], jnp.ones((16, 512), bf16)], axis=0)
            both = dot(left, numer)
            total = both[HEAD_DIM : HEAD_DIM + 1, :]
            ot[rows, :] = (both[:HEAD_DIM, :] / total).astype(bf16)
            lse[pl.ds(pair * 2 + which, 1), :] = top + jnp.log(total)
    o[...] = ot[...].T
    keeps[3].start()
    acc = xf
    for t in range(2):
        acc = acc + dot_nt(o[:, t * 256 : (t + 1) * 256], w_at(w, None, t, 768, 256))
    x1[...] = acc
    wait_all(keeps)


def gelu_parts(u):
    square = u * u
    tanh = jnp.tanh(gelu_coef * u * (1.0 + 0.044715 * square))
    return 0.5 * u * (1.0 + tanh), tanh, square


def mlp_weights(w):
    def up(t, part):
        return w_at(w[:4], w[4:], t, 1024 + part * 512, 512)

    def down(t, part):
        return w_at(w[:4], w[4:], t, 2048 + part * 512, 512)

    return up, down


def mlp_rows(at, x, norms, w, h2):
    up, down = mlp_weights(w)
    h2[...] = (ln_parts(x)[0] * gain_of(norms, at) + bias_of(norms, at)).astype(bf16)
    for t in range(2):
        for part in range(2):
            hidden = gelu_parts(dot(h2[...], up(t, part)))[0].astype(bf16)
            x = x + dot_nt(hidden, down(t, part))
    return x


def mlp_fwd_kernel(at, x1, norms, *refs):
    w, (y, theirs, h2) = refs[:8], refs[8:]
    rows = mlp_rows(at, x1[...], norms, w, h2)
    y[...] = rows
    theirs[...] = rows[256:, :]


def mlp_bwd_kernel(split, at, ids, x1, norms, *refs):
    up, down = mlp_weights(refs[:8])
    refs = refs[8:]
    if split:
        own, other, refs = refs[0], refs[1], refs[2:]
    else:
        dy, refs = refs[0], refs[1:]
    dx1, small, grads = refs[0], refs[1], refs[2:4]
    h2, h2t, dyb, dybt, dh2 = refs[4:9]
    if split:
        dy = refs[9]
        dy[0:256, :] = ordered(own[ids[1]], order_matrix(ids[0], False))
        dy[256:, :] = other[:, 640:].astype(f32)
    h2[...] = (ln_parts(x1[...])[0] * gain_of(norms, at) + bias_of(norms, at)).astype(bf16)
    h2t[...] = h2[...].T
    dyb[...] = dy[...].astype(bf16)
    dybt[...] = dyb[...].T
    for t in range(2):
        for part in range(2):
            cols = slice(part * 512, (part + 1) * 512)
            w_up = up(t, part)
            pre = dot(h2[...], w_up)
            hidden, tanh, square = gelu_parts(pre)
            slope = 0.5 * (1.0 + tanh) + (0.5 * gelu_coef) * pre * (1.0 - tanh * tanh) * (
                1.0 + (3 * 0.044715) * square
            )
            dhidden = dot(dyb[...], down(t, part))
            dpre = (dhidden * slope).astype(bf16)
            out_cols = slice(1024 + part * 512, 1024 + (part + 1) * 512)
            put_grad(grads, t, out_cols, dot(dybt[...], hidden.astype(bf16)).astype(bf16))
            put_grad(grads, t, cols, dot(h2t[...], dpre).astype(bf16))
            more = dot_nt(dpre, w_up)
            if t + part == 0:
                dh2[...] = more
            else:
                dh2[...] += more
    xhat, inv = ln_parts(x1[...])
    grad = dh2[...]
    small[0:1, :] = jnp.sum(grad * xhat, axis=0, keepdims=True)
    small[1:2, :] = jnp.sum(grad, axis=0, keepdims=True)
    dx1[...] = dy[...] + ln_back(grad, xhat, inv, gain_of(norms, at))


def heads_back(low, w, saved, lse, mask, put_out, scratch):
    qs, k, v, o, qst, kt = saved
    flip, do, dot_t, dqt, dq, dk, dv = scratch
    flip[...] = low.T
    for t in range(2):
        cols = slice(t * 256, (t + 1) * 256)
        do[:, cols] = dot(low, w_at(w, None, t, 768, 256)).astype(bf16)
        put_out(t, dot(flip[...], o[:, cols]).astype(bf16))
    dot_t[...] = do[...].T
    first = lax.broadcasted_iota(jnp.int32, (512, 128), 1) < HEAD_DIM
    for pair in range(4):
        lanes = slice(pair * 128, (pair + 1) * 128)
        dvs, dks = [], []
        for which in range(2):
            head = pair * 2 + which
            rows = pl.ds(head * HEAD_DIM, HEAD_DIM)
            scores = dot(k[:, lanes], head_rows(qst, pair, which)) + mask[...]
            probs = jnp.exp(scores - lse[head : head + 1, :])
            dprobs = dot(v[:, lanes], head_rows(dot_t, pair, which))
            shift = jnp.sum(probs * dprobs, axis=0, keepdims=True)
            dscore = (probs * (dprobs - shift)).astype(bf16)
            dvs.append(dot(probs.astype(bf16), do[:, lanes]))
            dks.append(dot(dscore, qs[:, lanes]))
            dqt[rows, :] = (dot(kt[rows, :], dscore) * HEAD_DIM ** (-0.5)).astype(bf16)
        dv[:, lanes] = jnp.where(first, dvs[0], dvs[1]).astype(bf16)
        dk[:, lanes] = jnp.where(first, dks[0], dks[1]).astype(bf16)
    dq[...] = dqt[...].T


def rows_back(at, xf, norms, w, parts, small, grads, h, flip):
    h[...] = (ln_parts(xf)[0] * gain_of(norms, at) + bias_of(norms, at)).astype(bf16)
    flip[...] = h[...].T
    grad = jnp.zeros((512, 512), f32)
    for t in range(2):
        cols = slice(t * 256, (t + 1) * 256)
        for index, part in enumerate(parts):
            w_cols = slice(index * 256, (index + 1) * 256)
            put_grad(grads, t, w_cols, dot(flip[...], part[:, cols]).astype(bf16))
            grad = grad + dot_nt(part[:, cols], w_at(w, None, t, index * 256, 256))
    xhat, inv = ln_parts(xf)
    small[0:1, :] = jnp.sum(grad * xhat, axis=0, keepdims=True)
    small[1:2, :] = jnp.sum(grad, axis=0, keepdims=True)
    return ln_back(grad, xhat, inv, gain_of(norms, at))


def take_saved(saved, held, sems):
    copies = [
        pltpu.make_async_copy(a, b, sems.at[i]) for i, (a, b) in enumerate(zip(saved, held))
    ]
    start_all(copies)
    return copies


def attn_bwd_kernel(at, own, other, dx1, norms, lse, *refs):
    w, saved, x, refs = refs[:4], refs[4:10], refs[10], refs[11:]
    dx, small, grads = refs[0], refs[1], refs[2:4]
    mask, h, held, scratch, sems = refs[4], refs[5], refs[6:12], refs[12:19], refs[19]
    copies = take_saved(saved, held, sems)
    mask[...] = segment_mask(own, other)
    low = dx1[...].astype(bf16)
    wait_all(copies)

    def put_out(t, value):
        put_grad(grads, t, slice(768, 1024), value)

    heads_back(low, w, held, lse, mask, put_out, scratch)
    dx[...] = dx1[...] + rows_back(
        at, x[...], norms, w, scratch[4:], small, grads, h, scratch[0]
    )


def heads_bwd_kernel(own, other, dx1, lse, *refs):
    w, saved, refs = refs[:4], refs[4:10], refs[10:]
    parts, grads, mask, held = refs[:3], refs[3:5], refs[5], refs[6:12]
    scratch, sems = (*refs[12:16], *parts), refs[16]
    copies = take_saved(saved, held, sems)
    mask[...] = segment_mask(own, other)
    low = dx1[...].astype(bf16)
    wait_all(copies)

    def put_out(t, value):
        put_grad(grads, t, slice(0, 256), value)

    heads_back(low, w, held, lse, mask, put_out, scratch)


def rows_bwd_kernel(at, ids, own, other, dx1, norms, dq, dk, dv, out_0, out_1, other_small, *refs):
    w, (dx, dx_low), grads, (small, h, flip) = refs[:4], refs[4:6], refs[6:8], refs[8:]
    total = dx1[...] + rows_back(
        at, load_rows(None, own, other), norms, w, (dq, dk, dv), small, grads, h, flip
    )
    dx[...] = total
    dx_low[...] = total[256:, :].astype(bf16)
    rows = jnp.concatenate([small[0:2, :], other_small[0:2, :], jnp.zeros((4, 512), f32)], axis=0)
    packed = pack_rows(ordered(rows, order_matrix(ids[0], True)))
    for grad, part in zip(grads, (out_0, out_1)):
        for i in range(4):
            for z in range(4):
                grad[i, z, :, 768:1024] = part[i, z]
                grad[i, z, :, 1024:1152] = packed


def pack_rows(rows):
    cut = [rows[i : i + 1, 128 * j : 128 * (j + 1)] for i in range(4) for j in range(4)]
    return jnp.concatenate(split2(jnp.concatenate(cut, axis=0)), axis=0)


def code_prep_kernel(book_t, stack, stack_t):
    def one_chunk(index, _):
        lanes = pl.ds(pl.multiple_of(index * 512, 512), 512)
        rows = book_t[:, lanes]
        unit = rows * lax.rsqrt(jnp.sum(rows * rows, axis=0, keepdims=True) + norm_eps)
        hi, mid, lo = split3(unit)
        stack_t[:, lanes] = jnp.concatenate([hi, mid, lo, jnp.ones((32, 512), bf16)], axis=0)
        tall = jnp.concatenate([hi, mid, lo, hi, mid, hi, jnp.zeros((64, 512), bf16)], axis=0)
        stack[lanes, :] = tall.T
        return 0

    lax.fori_loop(0, book_t.shape[1] // 512, one_chunk, 0)


def factor_stack(x):
    hi, mid, lo = split3(x)
    return jnp.concatenate([hi, hi, hi, mid, mid, lo, jnp.zeros((64, x.shape[1]), bf16)], axis=0)


def code_loads(pairs, sems):
    loads = []
    for piece in range(4):
        group = []
        for at, (held, to, by_row) in enumerate(pairs):
            size = held.shape[0 if by_row else 1] // 4
            part = pl.ds(piece * size, size)
            place = (part, slice(None)) if by_row else (slice(None), part)
            group.append(pltpu.make_async_copy(held.at[place], to.at[place], sems.at[at, piece]))
        start_all(group)
        loads.append(group)
    return loads


def mlp_vq_kernel(x1, norms, vq_w, stack_hbm, stack_t_hbm, *refs):
    w, (e, u, kept, h2, acc, stack, stack_t, sems) = refs[:8], refs[8:]
    loads = code_loads([(stack_hbm, stack, True), (stack_t_hbm, stack_t, False)], sems)
    e[...] = mlp_rows(1, x1[...], norms, w, h2)
    lnv = ln_parts(e[...])[0] * gain_of(norms, 2) + bias_of(norms, 2)
    raw = dot_nt(vq_w[0:32, :], lnv, highest)
    inv = lax.rsqrt(jnp.sum(raw * raw, axis=0, keepdims=True) + norm_eps)
    latent = raw * inv
    right = factor_stack(latent * (temper * log2e))
    chunks = stack.shape[0] // 2048
    for piece, group in enumerate(loads):
        wait_all(group)
        for part in range(piece * chunks // 4, (piece + 1) * chunks // 4):
            numers = []
            for index in range(4 * part, 4 * part + 4):
                codes = slice(index * 512, (index + 1) * 512)
                numers.append(jnp.exp2(dot(stack[codes, :], right)).astype(bf16))
            sums = dot(
                stack_t[:, part * 2048 : (part + 1) * 2048], jnp.concatenate(numers, axis=0)
            )
            if part == 0:
                acc[...] = sums
            else:
                acc[...] += sums
    total = acc[96:97, :]
    soft = (acc[0:32, :] + acc[32:64, :] + acc[64:96, :]) / total
    kept[0:32, :] = latent
    kept[32:64, :] = soft
    kept[64:65, :] = total
    kept[65:66, :] = inv
    u[...] = dot_full(soft.T, vq_w[32:64, :])


def vq_bwd_kernel(ids, e, du, norms, vq_w, stack_hbm, stack_t_hbm, book_hbm, kept, *refs):
    small0, small1, de, code_keep, code_send = refs[:5]
    acc, grads, small, tail, stack, stack_t, book_t, load_sems, sems = refs[5:]
    loads = code_loads(
        [(stack_hbm, stack, True), (stack_t_hbm, stack_t, False), (book_hbm, book_t, False)],
        load_sems,
    )
    xhat, inv_ln = ln_parts(e[...])
    lnv = xhat * gain_of(norms, 2) + bias_of(norms, 2)
    latent, soft = kept[0:32, :], kept[32:64, :]
    total, inv = kept[64:65, :], kept[65:66, :]
    direct = (2.0 * 1.25 * commit_weight) * (latent - soft)
    dsoft = dot_nt(vq_w[32:64, :], du[...], highest) - direct
    small[32:64, :] = dot_full(soft, du[...])
    shift = jnp.sum(dsoft * soft, axis=0, keepdims=True) / total
    dsoft = dsoft / total
    right = jnp.concatenate(
        [factor_stack(latent * (temper * log2e)), factor_stack(dsoft)], axis=1
    )
    pads = jnp.zeros((64, 512), f32)

    def tall(x):
        hi, lo = split2(x)
        return jnp.concatenate([hi.astype(f32), lo.astype(f32), pads], axis=0).T.astype(bf16)

    sides = jnp.concatenate([tall(dsoft), tall(latent * temper)], axis=0)
    chunks = stack.shape[0] // 2048
    for piece, group in enumerate(loads):
        wait_all(group)
        for part in range(piece * chunks // 4, (piece + 1) * chunks // 4):
            dlogits = []
            for index in range(4 * part, 4 * part + 4):
                codes = slice(index * 512, (index + 1) * 512)
                both = dot(stack[codes, :], right)
                numer = jnp.exp2(both[:, :512])
                dlogit = (numer * (both[:, 512:] - shift)).astype(bf16)
                dlogits.append(dlogit)
                sums = jnp.concatenate([numer.astype(bf16), dlogit], axis=1)
                dcode = dot(sums, sides).T
                dcode = dcode[0:32, :] + dcode[32:64, :]
                rows = book_t[:, codes]
                scale = lax.rsqrt(jnp.sum(rows * rows, axis=0, keepdims=True) + norm_eps)
                unit = rows * scale
                grads[:, codes] = (
                    scale * (dcode - unit * jnp.sum(unit * dcode, axis=0, keepdims=True))
                ).astype(bf16)
            sums = dot(
                stack_t[0:96, part * 2048 : (part + 1) * 2048], jnp.concatenate(dlogits, axis=0)
            )
            if part == 0:
                acc[...] = sums
            else:
                acc[...] += sums
    dlatent = temper * (acc[0:32, :] + acc[32:64, :] + acc[64:96, :]) + direct
    draw = inv * (dlatent - latent * jnp.sum(latent * dlatent, axis=0, keepdims=True))
    small[0:32, :] = dot_full(draw, lnv)
    dln = dot_full(draw.T, vq_w[0:32, :])
    small[64:65, :] = jnp.sum(dln * xhat, axis=0, keepdims=True)
    small[65:66, :] = jnp.sum(dln, axis=0, keepdims=True)
    small[66:68, :] = small0[0:2, :]
    small[68:70, :] = small1[0:2, :]
    small[70:96, :] = jnp.zeros((26, 512), f32)
    small[...] = ordered(small[...], order_matrix(ids[0], True))
    for block in range(3):
        for at, part in enumerate(split2(small[block * 32 : (block + 1) * 32, :])):
            for side in range(2):
                tail[block * 2 + side, :, at * 256 : (at + 1) * 256] = part[
                    :, side * 256 : (side + 1) * 256
                ]
    tail[6:8] = jnp.zeros((2, 32, 512), bf16)
    core, z = ids[0] % 2, ids[0] // 4
    copies = []
    for slot, (at, to) in enumerate(((core, code_keep), (1 - core, code_send))):
        for k in range(4):
            part = at * 4 + (z ^ k)
            lanes = pl.ds(pl.multiple_of(part * 1024, 1024), 1024)
            copies += [
                pltpu.make_async_copy(
                    grads.at[:, lanes], to.at[k, :, pl.ds(0, 1024)], sems.at[0, slot, k]
                ),
                pltpu.make_async_copy(
                    tail.at[part], to.at[k, :, pl.ds(1024, 512)], sems.at[1, slot, k]
                ),
            ]
    for copy in copies:
        copy.start()
    de[...] = ln_back(dln, xhat, inv_ln, gain_of(norms, 2))
    for copy in copies:
        copy.wait()


SMEM = pl.BlockSpec(memory_space=pltpu.SMEM)
VMEM = pl.BlockSpec(memory_space=pltpu.VMEM)
ANY = pl.BlockSpec(memory_space=pl.ANY)


def shaped(*pairs):
    return [jax.ShapeDtypeStruct(shape, dtype) for shape, dtype in pairs]


def pin(array):
    return pltpu.with_memory_space_constraint(array, pltpu.HBM)


def call(kernel, name, in_specs, out_specs, outs, scratch, flops, after=(), carry=()):
    n_in, n_extra, n_out = len(in_specs), len(after) + len(carry), len(outs)

    def body(*refs):
        first = n_in + n_extra
        kernel(*refs[:n_in], *refs[first : first + n_out], *refs[first + n_out + len(carry) :])

    made = pl.pallas_call(
        body,
        name=name,
        in_specs=in_specs + [ANY] * n_extra,
        out_specs=out_specs + [ANY] * len(carry),
        out_shape=outs + [jax.ShapeDtypeStruct(a.shape, a.dtype) for a in carry],
        scratch_shapes=scratch,
        input_output_aliases={n_in + len(after) + i: n_out + i for i in range(len(carry))},
        compiler_params=pltpu.CompilerParams(vmem_limit_bytes=vmem_cap),
        cost_estimate=pl.CostEstimate(flops=flops, bytes_accessed=10**6, transcendentals=0),
    )

    def run(*args):
        res = made(*args, *after, *carry)
        return (*res[:n_out], list(res[n_out:]))

    return run


DMA = pltpu.SemaphoreType.DMA
ROWS2 = (512, 512)


def attn_fwd(at, marked, xs, norms, w, after=(), carry=()):
    outs = shaped((ROWS2, f32), ((8, 512), f32)) + [pltpu.HBM(ROWS2, bf16)] * 6
    scratch = [
        *[pltpu.VMEM(ROWS2, bf16)] * 3,
        pltpu.VMEM(ROWS2, f32),
        *[pltpu.VMEM(ROWS2, bf16)] * 6,
        DMA((6,)),
    ]
    x1, lse, *saved, carried = call(
        functools.partial(attn_fwd_kernel, bool(xs), at),
        "attn_fwd",
        [VMEM] * (7 + len(xs)),
        [VMEM] * 2 + [ANY] * 6,
        outs,
        scratch,
        10**10,
        after,
        carry,
    )(*marked, norms, *w[:4], *xs)
    return x1, (lse, *saved), carried


def mlp_fwd(at, x1, norms, w, after=(), carry=()):
    return call(
        functools.partial(mlp_fwd_kernel, at),
        "mlp_fwd",
        [VMEM] * 10,
        [VMEM] * 2,
        shaped((ROWS2, f32), ((256, 512), f32)),
        [pltpu.VMEM(ROWS2, bf16)],
        8 * 10**9,
        after,
        carry,
    )(x1, norms, *w)


def mlp_bwd(at, ids, x1, dys, norms, w, after=(), carry=()):
    scratch = [
        *[pltpu.VMEM(ROWS2, bf16)] * 4,
        *[pltpu.VMEM(ROWS2, f32)] * len(dys),
    ]
    return call(
        functools.partial(mlp_bwd_kernel, len(dys) == 2, at),
        "mlp_bwd",
        [SMEM] + [VMEM] * (10 + len(dys)),
        [VMEM] * 4,
        shaped((ROWS2, f32), ((8, 512), f32), *[((4, 4, 32, 2048), bf16)] * 2),
        scratch,
        15 * 10**9,
        after,
        carry,
    )(ids, x1, norms, *w, *dys)


def attn_bwd(at, marked, x, dx1, norms, saved, w, after=(), carry=()):
    scratch = [pltpu.VMEM(ROWS2, f32), *[pltpu.VMEM(ROWS2, bf16)] * 14, DMA((6,))]
    outs = shaped((ROWS2, f32), ((8, 512), f32), *[((4, 4, 32, 1024), bf16)] * 2)
    return call(
        functools.partial(attn_bwd_kernel, at),
        "attn_bwd",
        [VMEM] * 9 + [ANY] * 6 + [VMEM],
        [VMEM] * 4,
        outs,
        scratch,
        15 * 10**9,
        after,
        carry,
    )(*marked, dx1, norms, saved[0], *w[:4], *map(pin, saved[1:]), x)


def heads_bwd(marked, dx1, saved, w, after=(), carry=()):
    scratch = [pltpu.VMEM(ROWS2, f32), *[pltpu.VMEM(ROWS2, bf16)] * 10, DMA((6,))]
    outs = shaped(*[(ROWS2, bf16)] * 3, *[((4, 4, 32, 256), bf16)] * 2)
    return call(
        heads_bwd_kernel,
        "heads_bwd",
        [VMEM] * 8 + [ANY] * 6,
        [VMEM] * 5,
        outs,
        scratch,
        10 * 10**9,
        after,
        carry,
    )(*marked, dx1, saved[0], *w[:4], *map(pin, saved[1:]))


def rows_bwd(at, ids, marked, dx1, norms, parts, other_small, w, after=(), carry=()):
    scratch = [pltpu.VMEM((8, 512), f32), *[pltpu.VMEM(ROWS2, bf16)] * 2]
    outs = shaped((ROWS2, f32), ((256, 512), bf16), *[((4, 4, 32, 1152), bf16)] * 2)
    return call(
        functools.partial(rows_bwd_kernel, at),
        "rows_bwd",
        [SMEM] + [VMEM] * 14,
        [VMEM] * 4,
        outs,
        scratch,
        5 * 10**9,
        after,
        carry,
    )(ids, *marked, dx1, norms, *parts, other_small, *w[:4])


def code_prep(book_t, after=(), carry=()):
    codes = book_t.shape[1]
    return call(
        code_prep_kernel,
        "code_prep",
        [VMEM],
        [VMEM] * 2,
        shaped(((codes, 256), bf16), ((128, codes), bf16)),
        [],
        6 * 10**9,
        after,
        carry,
    )(book_t)


def mlp_vq(x1, norms, vq_w, stack, stack_t, w, after=(), carry=()):
    return call(
        mlp_vq_kernel,
        "mlp_vq",
        [VMEM] * 3 + [ANY] * 2 + [VMEM] * 8,
        [VMEM] * 3,
        shaped((ROWS2, f32), (ROWS2, f32), ((72, 512), f32)),
        [
            pltpu.VMEM(ROWS2, bf16),
            pltpu.VMEM((128, 512), f32),
            pltpu.VMEM(stack.shape, bf16),
            pltpu.VMEM(stack_t.shape, bf16),
            DMA((2, 4)),
        ],
        25 * 10**9,
        after,
        carry,
    )(x1, norms, vq_w, pin(stack), pin(stack_t), *w)


def vq_bwd(ids, e, du, norms, vq_w, codes, kept, smalls, after=(), carry=()):
    scratch = [
        pltpu.VMEM((96, 512), f32),
        pltpu.VMEM(codes[2].shape, bf16),
        pltpu.VMEM((96, 512), f32),
        pltpu.VMEM((8, 32, 512), bf16),
        *[pltpu.VMEM(a.shape, a.dtype) for a in codes],
        DMA((3, 4)),
        DMA((2, 2, 4)),
    ]
    return call(
        vq_bwd_kernel,
        "vq_bwd",
        [SMEM] + [VMEM] * 4 + [ANY] * 3 + [VMEM] * 3,
        [VMEM] + [ANY] * 2,
        shaped((ROWS2, f32), *[((4, 32, 1536), bf16)] * 2),
        scratch,
        25 * 10**9,
        after,
        carry,
    )(ids, e, du, norms, vq_w, *map(pin, codes), kept, *smalls)


def lines_kernel(cuts, *refs):
    first = 0
    for out, width in zip(refs[4:], cuts):
        for k in range(4):
            out[k] = refs[k][:, first : first + width]
        first += width


def stack_lines(shards, cuts, after=(), carry=()):
    return call(
        functools.partial(lines_kernel, cuts),
        "stack_lines",
        [VMEM] * 4,
        [VMEM] * len(cuts),
        shaped(*[((4, 32, width), bf16) for width in cuts]),
        [],
        1,
        after,
        carry,
    )(*shards)


def pack_kernel(*refs):
    hbm, outs, held, sems = refs[:4], refs[4:6], refs[6:10], refs[10]
    copies = [pltpu.make_async_copy(hbm[at], held[at], sems.at[at]) for at in range(4)]
    start_all(copies)
    wait_all(copies)
    qkv, out_t, up, down_t = held
    for layer, out in enumerate(outs):
        for index in range(3):
            out[:, index * 256 : (index + 1) * 256] = qkv[layer, index]
        out[:, 768:1024] = out_t[layer]
        out[:, 1024:2048] = up[layer]
        out[:, 2048:] = down_t[layer]


def pack_weights(*arrays):
    return call(
        pack_kernel,
        "pack_weights",
        [ANY] * 4,
        [VMEM] * 2,
        shaped(*[((32, 3072), bf16)] * 2),
        [*[pltpu.VMEM(a.shape, a.dtype) for a in arrays], DMA((4,))],
        1,
    )(*map(pin, arrays))[:-1]


def pairs_kernel(*refs):
    count = len(refs) // 3
    for at in range(count):
        refs[2 * count + at][0] = refs[2 * at][...]
        refs[2 * count + at][1] = refs[2 * at + 1][...]


def stack_pairs(pairs, after=(), carry=()):
    return call(
        pairs_kernel,
        "stack_pairs",
        [VMEM] * (2 * len(pairs)),
        [VMEM] * len(pairs),
        shaped(*[((2, *a.shape), bf16) for a, _ in pairs]),
        [],
        1,
        after,
        carry,
    )(*[array for pair in pairs for array in pair])


def gate(after, carry):
    def kernel(out):
        out[...] = jnp.zeros_like(out)

    return call(kernel, "gate", [], [VMEM], shaped(((8, 128), f32)), [], 1, after, carry)()[-1]


def rows_in_kernel(ids, *refs):
    hbm, (own, send, norms, vq_w), held, sems = refs[:7], refs[7:11], refs[11:18], refs[18]
    copies = [pltpu.make_async_copy(hbm[at], held[at], sems.at[at]) for at in range(7)]
    start_all(copies)
    matrix = order_matrix(ids[0], False)
    wait_all(copies)
    tokens, segs, cot, gains, biases, in_t, out_w = held
    for to, micro in ((send, 1 - ids[1]), (own, ids[1])):
        to[:, :512] = ordered(tokens[micro], matrix).astype(bf16)
        ids_row = segs[pl.ds(micro, 1), :].astype(f32)
        to[:, 512:640] = jnp.broadcast_to(ids_row, (128, 256)).T.astype(bf16)
    send[:, 640:] = ordered(cot[1 - ids[1]].astype(bf16), matrix).astype(bf16)
    pad = jnp.zeros((3, 512), f32)
    rows = jnp.concatenate([gains[...], pad, biases[...], pad], axis=0)
    norms[...] = ordered(rows, matrix)
    vq_w[...] = ordered(jnp.concatenate([in_t[...], out_w[...]], axis=0), matrix)


def rows_in(ids, *arrays):
    outs = shaped(
        ((256, 640), bf16), ((256, 1152), bf16), ((16, 512), f32), ((64, 512), f32)
    )
    return call(
        rows_in_kernel,
        "rows_in",
        [SMEM] + [ANY] * 7,
        [VMEM] * 4,
        outs,
        [*[pltpu.VMEM(a.shape, a.dtype) for a in arrays], DMA((7,))],
        1,
    )(ids, *map(pin, arrays))[:-1]


def joined(block):
    return block[0:16, 1024:].astype(f32) + block[16:32, 1024:].astype(f32)


def put_small(value, own, blocks):
    hi, lo = split2(value)
    own[0:16, 1024:] = hi.astype(f32) + lo.astype(f32)
    for block in blocks:
        block[0:16, 1024:] = hi
        block[16:32, 1024:] = lo


def near_kernel(ids, ins, outs):
    keep, other = ins
    for i in range(4):
        outs[i][...] = (keep[i].astype(f32) + other[i].astype(f32)).astype(outs[i].dtype)
    if keep.shape[3] == 1152:
        value = joined(keep.at[0, 0]) + joined(other.at[0, 0])
        put_small(value, outs[0].at[0], [out.at[0] for out in outs[1:]])


def near_task(keep, other):
    shape = keep.shape[1:]
    return near_kernel, [keep, other], shaped((shape, f32), *[(shape, bf16)] * 3)


def put_code(ref, first, code):
    for i in range(3):
        ref[first + i] = code[:, 1024 * i : 1024 * (i + 1)]


def get_code(ref, first):
    return jnp.concatenate([ref[first + i] for i in range(3)], axis=1)


def put_rows(ref, first, rows):
    for i in range(4):
        ref[first + i, :, :512] = rows[i * 32 : (i + 1) * 32, :]
        ref[first + i, :, 512:] = rows[128 + i * 32 : 128 + (i + 1) * 32, :]


def get_rows(ref, first):
    parts = [ref[first + i, :, :512] for i in range(4)] + [ref[first + i, :, 512:] for i in range(4)]
    return jnp.concatenate(parts, axis=0)


def code_sum(a, b):
    done = []
    for first in range(0, a.shape[1], 1536):
        total = a[:, first : first + 1024].astype(f32) + b[:, first : first + 1024].astype(f32)
        small = [
            x[:, first + 1024 : first + 1280].astype(f32) + x[:, first + 1280 : first + 1536].astype(f32)
            for x in (a, b)
        ]
        done += [total.astype(bf16), *split2(small[0] + small[1])]
    return jnp.concatenate(done, axis=1)


def fork_kernel(ids, ins, outs):
    keep, other, code, code_other = ins
    own_up, to_x, own_down, to_y, code_out = outs
    for at, (own, send, kept, sent) in enumerate(
        ((own_up, to_x, (0, 2), (1, 3)), (own_down, to_y, (0, 1), (2, 3)))
    ):
        cols = slice(1024 * at, 1024 * (at + 1))
        for j in range(2):
            own[j] = keep[kept[j], :, :, cols].astype(f32) + other[kept[j], :, :, cols].astype(f32)
            total = keep[sent[j], :, :, cols].astype(f32) + other[sent[j], :, :, cols].astype(f32)
            send[4 * j : 4 * (j + 1)] = total.astype(bf16)
    swapped = jnp.concatenate([code_other[:, 1536:], code_other[:, :1536]], axis=1)
    code_out[...] = code_sum(code[...], swapped)
    put_code(to_x, 8, code_out)


def fork_task(keep, other, code, code_other):
    outs = shaped(
        ((2, 4, 32, 1024), f32),
        ((11, 32, 1024), bf16),
        ((2, 4, 32, 1024), f32),
        ((8, 32, 1024), bf16),
        (code.shape, bf16),
    )
    return fork_kernel, [keep, other, code, code_other], outs


def half_kernel(ids, ins, outs):
    own_up, from_x, own_down, from_y, code, dx_low = ins
    up, to_y, down, to_x, code_out = outs
    for own, other, kept, send in ((own_up, from_x, up, to_y), (own_down, from_y, down, to_x)):
        kept[...] = own[0] + other[0:4].astype(f32)
        send[0:4] = (own[1] + other[4:8].astype(f32)).astype(bf16)
    code_out[...] = code_sum(code[...], get_code(from_x, 8))
    put_code(to_y, 4, code_out)
    put_rows(to_x, 4, dx_low)


def half_task(own_up, from_x, own_down, from_y, code, dx_low):
    outs = shaped(
        ((4, 32, 1024), f32),
        ((7, 32, 1024), bf16),
        ((4, 32, 1024), f32),
        ((8, 32, 1024), bf16),
        (code.shape, bf16),
    )
    return half_kernel, [own_up, from_x, own_down, from_y, code, dx_low], outs


def join_kernel(ids, ins, outs):
    own_up, from_y, own_down, from_x, code = ins
    kept, send, code_out, rows = outs
    for at, (own, other) in enumerate(((own_up, from_y), (own_down, from_x))):
        cols = slice(1024 * at, 1024 * (at + 1))
        for k in range(2):
            kept[k, :, cols] = own[2 * k] + other[2 * k].astype(f32)
            send[k, :, cols] = (own[2 * k + 1] + other[2 * k + 1].astype(f32)).astype(bf16)
    code_out[...] = code_sum(code[...], get_code(from_y, 4))
    rows[...] = get_rows(from_x, 4)


def join_task(own_up, from_y, own_down, from_x, code):
    outs = shaped(
        ((2, 32, 2048), f32), ((2, 32, 2048), bf16), (code.shape, bf16), ((256, 512), bf16)
    )
    return join_kernel, [own_up, from_y, own_down, from_x, code], outs


def line_step_kernel(ids, ins, outs):
    kept, other = ins
    outs[0][...] = kept[0] + other[0].astype(f32)
    outs[1][...] = (kept[1] + other[1].astype(f32)).astype(bf16)


def line_step_task(kept, other):
    shape = kept.shape[1:]
    return line_step_kernel, [kept, other], shaped((shape, f32), (shape, bf16))


def plane_kernel(ids, ins, outs):
    for k in range(4):
        total = ins[0][k]
        for other in ins[1:]:
            total = total + other[k].astype(f32)
        outs[k][...] = total.astype(outs[k].dtype)
    if ins[0].shape[2] == 1152:
        x, y, xy = [joined(other.at[0]) for other in ins[1:]]
        put_small((ins[0][0, 0:16, 1024:] + x) + (y + xy), outs[0], outs[1:])


def plane_task(own, others):
    shape = own.shape[1:]
    return plane_kernel, [own, *others], shaped((shape, f32), *[(shape, bf16)] * 3)


def plane_join_kernel(ids, ins, outs):
    own, others, m_own, m_lows = ins[0], ins[1:4], ins[4], ins[5:]
    kept, send = outs
    for k in range(4):
        total = own[k]
        for other in others:
            total = total + other[k].astype(f32)
        rest = m_own if k == 0 else m_lows[k - 1]
        to = send if k % 2 else kept
        to[k // 2, :, :1024] = total.astype(to.dtype)
        to[k // 2, :, 1024:] = rest[...].astype(to.dtype)


def plane_join_task(own, others, *parts):
    outs = shaped(((2, 32, 3072), f32), ((2, 32, 3072), bf16))
    return plane_join_kernel, [own, *others, *parts], outs


def line_total(ins, width):
    total = ins[0][:, :width]
    for other in ins[1:]:
        total = total + other[:, :width].astype(f32)
    return total


def rows_kernel(ids, ins, outs):
    own, other = ins
    half = other.shape[0]
    matrix = order_matrix(ids[0], True)
    outs[0][ids[1]] = ordered(own[0:half, :], matrix)
    outs[0][1 - ids[1]] = ordered(other[...], matrix)


def rows_task(own, other):
    return rows_kernel, [own, other], shaped(((2, *other.shape), f32))


def code_near_kernel(ids, ins, outs):
    keep, other = ins
    for at, out in enumerate(outs):
        for i in range(2):
            out[:, 1536 * i : 1536 * (i + 1)] = code_sum(keep[2 * at + i], other[2 * at + i])


def code_near_task(keep, other):
    return code_near_kernel, [keep, other], shaped(*[((32, 3072), bf16)] * 2)


def code_add_kernel(ids, ins, outs):
    outs[0][...] = code_sum(ins[0][...], ins[1][...])


def code_add_task(a, b):
    return code_add_kernel, [a, b], shaped((a.shape, bf16))


def code_pair_kernel(ids, ins, outs):
    for at, part in enumerate(ins):
        outs[0][:, 3072 * at : 3072 * (at + 1)] = part[...]


def code_pair_task(a, b):
    return code_pair_kernel, [a, b], shaped(((32, 6144), bf16))


def finish_kernel(ids, ins, outs):
    mlp, attn, dec, code, code_other = ins[:2], ins[2:6], ins[6:8], *ins[8:]
    qkv, out_t, up, down_t, book, vq_in, vq_out, gains, biases, dec_biases, small_ref = outs
    both = line_total(dec, 3072)
    for layer, rows in enumerate((line_total(mlp, 2048), both[:, 1024:])):
        up[layer] = rows[:, :1024]
        down_t[layer] = rows[:, 1024:]
    for layer, rows in enumerate((line_total(attn, 1024), both[:, :1024])):
        for index in range(3):
            qkv[layer, index] = rows[:, index * 256 : (index + 1) * 256]
        out_t[layer] = rows[:, 768:]
    core, z = ids[0] % 2, ids[0] // 4
    for at, parts in ((core, code), (1 - core, code_other)):
        for k in range(4):
            part = at * 4 + (z ^ k)
            held = parts[:, 1536 * k : 1536 * (k + 1)].astype(f32)
            book[:, pl.ds(pl.multiple_of(part * 1024, 1024), 1024)] = held[:, :1024]
            small_ref[:, pl.ds(pl.multiple_of(part * 256, 256), 256)] = (
                held[:, 1024:1280] + held[:, 1280:1536]
            )
    small = small_ref[...]
    vq_in[...] = small[:, :512]
    vq_out[...] = small[:, 512:1024]
    rest = small[:, 1024:1536]
    k1, k2, k3 = [joined(other) for other in attn[1:]]
    packed = (attn[0][0:16, 1024:] + k1) + (k2 + k3)
    for row, out in enumerate((gains.at[0:1], biases.at[0:1], gains.at[1:2], biases.at[1:2])):
        for j in range(4):
            out[:, 128 * j : 128 * (j + 1)] = packed[row * 4 + j : row * 4 + j + 1, :]
    gains[2:3, :] = rest[0:1, :]
    biases[2:3, :] = rest[1:2, :]
    gains[3:4, :] = rest[2:3, :]
    dec_biases[0:1, :] = rest[3:4, :]
    gains[4:5, :] = rest[4:5, :]
    dec_biases[1:2, :] = rest[5:6, :]


def finish_task(own_m, other_m, own_a, line_a, own_d, other_d, code, code_other):
    outs = shaped(
        ((2, 3, 32, 256), f32),
        ((2, 32, 256), f32),
        ((2, 32, 1024), f32),
        ((2, 32, 1024), f32),
        ((32, 8192), f32),
        ((32, 512), f32),
        ((32, 512), f32),
        ((5, 512), f32),
        ((3, 512), f32),
        ((2, 512), f32),
        ((32, 2048), f32),
    )
    ins = [own_m, other_m, own_a, *line_a, own_d, other_d, code, code_other]
    return finish_kernel, ins, outs


def run_tasks(ids, name, tasks, after=(), carry=()):
    sizes = [(len(ins), len(outs)) for _, ins, outs in tasks]
    n_in = sum(i for i, _ in sizes)

    def kernel(ids_ref, *refs):
        at_in, at_out = 0, n_in
        for (fn, _, _), (i, o) in zip(tasks, sizes):
            fn(ids_ref, refs[at_in : at_in + i], refs[at_out : at_out + o])
            at_in, at_out = at_in + i, at_out + o

    outs = [one for _, _, many in tasks for one in many]
    res = call(
        kernel, name, [SMEM] + [VMEM] * n_in, [VMEM] * len(outs), outs, [], 10**9, after, carry
    )(ids, *[one for _, many, _ in tasks for one in many])
    split, at = [], 0
    for _, o in sizes:
        split.append(res[at : at + o])
        at += o
    return (*split, res[-1])


def whole_groups(
    n_dp,
    tokens,
    segment_ids,
    norm_gains,
    norm_biases,
    w_qkv,
    w_attn_out,
    w_up,
    w_down,
    w_vq_in,
    w_vq_out,
    codebook,
    cotangent,
):
    dp_at, tp_at = lax.axis_index("dp"), lax.axis_index("tp")
    ids = jnp.stack([dp_at, tp_at]).astype(jnp.int32)

    def swap(values):
        return exchange(values, 0, 1, n_dp)

    def core(values):
        return [values, exchange(values, 1, 0, n_dp)]

    book_t = codebook.T
    enc_shard, dec_shard = pack_weights(
        w_qkv, w_attn_out.transpose(0, 2, 1), w_up, w_down.transpose(0, 2, 1)
    )
    enc_shards = spread_line(enc_shard, n_dp)
    own, send, norms, vq_w = rows_in(
        ids,
        tokens,
        segment_ids,
        cotangent,
        norm_gains,
        norm_biases,
        w_vq_in.T,
        w_vq_out,
    )
    marked = [own, swap(send)]

    line_a, line_b, (dec_shard,) = stack_lines(enc_shards, [1536] * 2, carry=[dec_shard])
    along_x, along_y = exchange(line_a, 0, 1, n_dp), exchange(line_b, 2, 0, n_dp)
    dec_shards = spread_line(dec_shard, n_dp)
    stack, stack_t, _ = code_prep(book_t, [line_a])
    codes = (stack, stack_t, book_t)
    a_0, b_0, _ = stack_pairs([(line_a, along_x), (line_b, along_y)], [stack_t, marked[1]])
    a_1, b_1 = exchange(a_0, 2, 0, n_dp), exchange(b_0, 0, 1, n_dp)
    line_a, line_b, (a_0, b_0) = stack_lines(dec_shards, [1536] * 2, [a_1, b_1], [a_0, b_0])
    enc_w = [a_0, a_1, exchange(a_0, 1, 0, n_dp), exchange(a_1, 1, 0, n_dp)]
    enc_w += [b_0, b_1, exchange(b_0, 1, 0, n_dp), exchange(b_1, 1, 0, n_dp)]
    along_x, along_y = exchange(line_a, 0, 1, n_dp), exchange(line_b, 2, 0, n_dp)
    e_x1, e_saved, _ = attn_fwd(0, marked, [], norms, enc_w)
    a_0, b_0, _ = stack_pairs([(line_a, along_x), (line_b, along_y)], [e_x1])
    a_1, b_1 = exchange(a_0, 2, 0, n_dp), exchange(b_0, 0, 1, n_dp)
    dec_w = [a_0, exchange(a_0, 1, 0, n_dp), b_0, exchange(b_0, 1, 0, n_dp)]
    e, u, kept, _ = mlp_vq(e_x1, norms, vq_w, stack, stack_t, enc_w, [a_0, b_0])
    a_1, b_1 = gate([u], [a_1, b_1])
    a_1, b_1 = core(a_1), core(b_1)
    dec_w = [dec_w[0], a_1[0], dec_w[1], a_1[1], dec_w[2], b_1[0], dec_w[3], b_1[1]]
    d_x1, d_saved, _ = attn_fwd(3, marked, [u], norms, dec_w)

    dx1, d_small1, keep_m, send_m, _ = mlp_bwd(
        4, ids, d_x1, [cotangent, marked[1]], norms, dec_w
    )
    y, y_theirs, _ = mlp_fwd(4, d_x1, norms, dec_w, [keep_m])
    near_m, y_other = exchange(send_m, 1, 0, n_dp), swap(y_theirs)
    du, d_small0, keep_a, send_a, (keep_m,) = attn_bwd(
        3, marked, u, dx1, norms, d_saved, dec_w, [y_theirs], [keep_m]
    )
    (own_m, *lows_m), (send_a,) = run_tasks(
        ids, "sums1", [near_task(keep_m, near_m)], [y_other], [send_a]
    )
    plane_m, near_a = plane_send(lows_m, n_dp), exchange(send_a, 1, 0, n_dp)
    de, code, code_send, (own_m, keep_a) = vq_bwd(
        ids,
        e,
        du,
        norms,
        vq_w,
        codes,
        kept,
        [d_small0, d_small1],
        lows_m,
        [own_m, keep_a],
    )
    d_mlp, (own_a, *lows_a), (code, code_send) = run_tasks(
        ids,
        "sums2",
        [plane_task(own_m, plane_m), near_task(keep_a, near_a)],
        carry=[code, code_send],
    )
    plane_a, code_other = plane_send(lows_a, n_dp), exchange(code_send, 1, 0, n_dp)
    (code, code_send), _ = run_tasks(ids, "sums2b", [code_near_task(code, code_other)])
    code_other = exchange(code_send, 8, 0, n_dp)
    ex1, e_small1, keep_m, send_m, (own_a, code) = mlp_bwd(
        1, ids, e_x1, [de], norms, enc_w, [*lows_a, code_send], [own_a, code]
    )
    (own_d, send_d), (code,), (keep_m, send_m) = run_tasks(
        ids,
        "sums3",
        [plane_join_task(own_a, plane_a, *d_mlp), code_add_task(code, code_other)],
        carry=[keep_m, send_m],
    )
    near_m, code_other = exchange(send_m, 1, 0, n_dp), exchange(code, 4, 0, n_dp)
    other_d = exchange(send_d, 4, 0, n_dp)
    *parts, _ = heads_bwd(marked, ex1, e_saved, enc_w, [send_d, code])
    (own_up, to_x, own_down, to_y, code), (own_d, send_d), _ = run_tasks(
        ids,
        "sums3b",
        [fork_task(keep_m, near_m, code, code_other), line_step_task(own_d, other_d)],
        [parts[0]],
    )
    from_x, from_y = exchange(to_x, 0, 1, n_dp), exchange(to_y, 2, 0, n_dp)
    other_d = exchange(send_d, 8, 0, n_dp)
    dx, dx_low, keep_a, send_a, (own_up, own_down, code, own_d) = rows_bwd(
        0,
        ids,
        marked,
        ex1,
        norms,
        parts,
        e_small1,
        enc_w,
        [to_x, to_y],
        [own_up, own_down, code, own_d],
    )
    (own_up, to_y, own_down, to_x, code), (keep_a, send_a) = run_tasks(
        ids,
        "sums4",
        [half_task(own_up, from_x, own_down, from_y, code, dx_low)],
        [other_d],
        [keep_a, send_a],
    )
    near_a = exchange(send_a, 1, 0, n_dp)
    from_y, from_x = exchange(to_y, 2, 0, n_dp), exchange(to_x, 0, 1, n_dp)
    (own_a, *lows_a), (own_up, own_down, code) = run_tasks(
        ids, "sums4b", [near_task(keep_a, near_a)], carry=[own_up, own_down, code]
    )
    plane_a = plane_send(lows_a, n_dp)
    (own_m, send_m, code, dx_other), (own_a,) = run_tasks(
        ids, "sums5", [join_task(own_up, from_y, own_down, from_x, code)], lows_a, [own_a]
    )
    other_m, code_other = exchange(send_m, 4, 0, n_dp), exchange(code, 8, 0, n_dp)
    (decoded,), (grad_tokens,), (own_a,) = run_tasks(
        ids,
        "rows_out",
        [rows_task(y, y_other), rows_task(dx, dx_other)],
        [send_m, code],
        [own_a],
    )
    (own_a, *lows_a), (own_m, send_m), (code,), _ = run_tasks(
        ids,
        "sums6",
        [
            plane_task(own_a, plane_a),
            line_step_task(own_m, other_m),
            code_pair_task(code, code_other),
        ],
    )
    line_a, other_m = line_send(lows_a, n_dp), exchange(send_m, 8, 0, n_dp)
    code_other = exchange(code, 1, 0, n_dp)
    (qkv, out_t, up, down_t, book, vq_in, vq_out, *norm_grads, _), _ = run_tasks(
        ids,
        "finish",
        [finish_task(own_m, other_m, own_a, line_a, own_d, other_d, code, code_other)],
    )
    return (
        decoded,
        grad_tokens,
        *norm_grads,
        qkv,
        out_t.transpose(0, 2, 1),
        up,
        down_t.transpose(0, 2, 1),
        vq_in.T,
        vq_out,
        book.T,
    )


def layer_norm(values, norm_gain, norm_bias):
    centred = values - jnp.mean(values, axis=-1, keepdims=True)
    spread = jnp.mean(centred * centred, axis=-1, keepdims=True)
    return centred * lax.rsqrt(spread + ln_eps) * norm_gain + norm_bias


def gelu_tanh(values):
    return (
        0.5 * values * (1.0 + jnp.tanh(gelu_coef * (values + 0.044715 * values * values * values)))
    )


def matmul(former, latter):
    return jnp.dot(former, latter, precision=highest, preferred_element_type=jnp.float32)


def normalize(values):
    return values * lax.rsqrt(jnp.sum(values * values, axis=-1, keepdims=True) + norm_eps)


def quantize(in_rows, norm_gain, norm_bias, in_w, out_w, code_w):
    latent = normalize(matmul(layer_norm(in_rows, norm_gain, norm_bias), in_w))
    code_rows = normalize(code_w)
    logits = matmul(latent, code_rows.T) * temper
    row_max = jnp.max(logits, axis=-1, keepdims=True)
    numerator = jnp.exp(logits - row_max)
    assign = numerator / jnp.sum(numerator, axis=-1, keepdims=True)
    soft_code = matmul(assign, code_rows)
    offset = latent - soft_code
    vq_loss = commit_weight * 1.25 * jnp.sum(offset * offset)
    return (matmul(soft_code, out_w), vq_loss)


def product(former, latter):
    return jnp.dot(former, latter, preferred_element_type=jnp.float32)


def product_tn(former, latter):
    return lax.dot_general(
        former, latter, (((0,), (0,)), ((), ())), preferred_element_type=jnp.float32
    )


def product_nt(former, latter):
    return lax.dot_general(
        former, latter, (((1,), (1,)), ((), ())), preferred_element_type=jnp.float32
    )


def split_heads(values):
    return values.reshape(values.shape[0], values.shape[1] // HEAD_DIM, HEAD_DIM).transpose(1, 0, 2)


def join_heads(values):
    return values.transpose(1, 0, 2).reshape(values.shape[1], values.shape[0] * HEAD_DIM)


def masked_scores(query_blk, key_h, seg_blk, seg_keys):
    scores = jnp.einsum(
        "hqd,hkd->hqk", query_blk, key_h, preferred_element_type=jnp.float32
    ) * HEAD_DIM ** (-0.5)
    return jnp.where((seg_blk[:, None] == seg_keys[None, :])[None], scores, masked_score)


def attend(query_h, key_h, value_h, seg_keys):
    block_rows = min(512, query_h.shape[1])
    block_count = query_h.shape[1] // block_rows

    def one_block(begin_row):
        query_blk = lax.dynamic_slice_in_dim(query_h, begin_row, block_rows, 1)
        seg_blk = lax.dynamic_slice_in_dim(seg_keys, begin_row, block_rows, 0)
        scores = masked_scores(query_blk, key_h, seg_blk, seg_keys)
        row_max = jnp.max(scores, axis=-1, keepdims=True)
        numerator = jnp.exp(scores - row_max)
        row_total = jnp.sum(numerator, axis=-1, keepdims=True)
        prob_low = (numerator / row_total).astype(jnp.bfloat16)
        attended = jnp.einsum("hqk,hkd->hqd", prob_low, value_h, preferred_element_type=jnp.float32)
        return (attended.astype(jnp.bfloat16), (row_max + jnp.log(row_total))[..., 0])

    starts = jnp.arange(block_count, dtype=jnp.int32) * block_rows
    attended, log_sums = lax.map(one_block, starts)
    heads_out = attended.transpose(1, 0, 2, 3).reshape(query_h.shape)
    log_sums = log_sums.transpose(1, 0, 2).reshape(query_h.shape[0], query_h.shape[1])
    return (heads_out, log_sums)


def attend_back(query_h, key_h, value_h, seg_keys, log_sums, grad_out):
    block_rows = min(512, query_h.shape[1])
    block_count = query_h.shape[1] // block_rows

    def one_block(carry, begin_row):
        grad_key, grad_value = carry
        query_blk = lax.dynamic_slice_in_dim(query_h, begin_row, block_rows, 1)
        grad_blk = lax.dynamic_slice_in_dim(grad_out, begin_row, block_rows, 1)
        lse_blk = lax.dynamic_slice_in_dim(log_sums, begin_row, block_rows, 1)
        seg_blk = lax.dynamic_slice_in_dim(seg_keys, begin_row, block_rows, 0)
        scores = masked_scores(query_blk, key_h, seg_blk, seg_keys)
        probs = jnp.exp(scores - lse_blk[..., None])
        prob_low = probs.astype(jnp.bfloat16)
        grad_value = grad_value + jnp.einsum(
            "hqk,hqd->hkd", prob_low, grad_blk, preferred_element_type=jnp.float32
        )
        grad_prob = jnp.einsum(
            "hqd,hkd->hqk", grad_blk, value_h, preferred_element_type=jnp.float32
        )
        row_dot = jnp.sum(probs * grad_prob, axis=-1, keepdims=True)
        grad_score = (probs * (grad_prob - row_dot) * HEAD_DIM ** (-0.5)).astype(jnp.bfloat16)
        grad_query = jnp.einsum(
            "hqk,hkd->hqd", grad_score, key_h, preferred_element_type=jnp.float32
        )
        grad_key = grad_key + jnp.einsum(
            "hqk,hqd->hkd", grad_score, query_blk, preferred_element_type=jnp.float32
        )
        return ((grad_key, grad_value), grad_query)

    starts = jnp.arange(block_count, dtype=jnp.int32) * block_rows
    zeros_kv = jnp.zeros(key_h.shape, jnp.float32)
    (grad_key, grad_value), grad_query = lax.scan(one_block, (zeros_kv, zeros_kv), starts)
    grad_query = grad_query.transpose(1, 0, 2, 3).reshape(query_h.shape)
    return (
        grad_query.astype(jnp.bfloat16),
        grad_key.astype(jnp.bfloat16),
        grad_value.astype(jnp.bfloat16),
    )


def spread_rows(values):
    return lax.all_gather(values, "tp", axis=0, tiled=True)


def combine_rows(partial_value):
    return lax.psum_scatter(partial_value, "tp", scatter_dimension=0, tiled=True)


def spread_grads(values):
    return lax.all_gather(values, "tp", axis=0, tiled=True)


def combine_grads(partial_value):
    return lax.psum_scatter(
        partial_value.astype(jnp.bfloat16), "tp", scatter_dimension=0, tiled=True
    ).astype(jnp.float32)


def fetch_weights(w_qkv, w_attn_out, w_up, w_down, layer):
    return (
        lax.all_gather(w_qkv[layer], "dp", axis=1, tiled=True),
        lax.all_gather(w_attn_out[layer], "dp", axis=1, tiled=True),
        lax.all_gather(w_up[layer], "dp", axis=0, tiled=True),
        lax.all_gather(w_down[layer], "dp", axis=1, tiled=True),
    )


def reduce_weight_grads(grads):
    return (
        lax.psum_scatter(
            grads[0].astype(jnp.bfloat16), "dp", scatter_dimension=1, tiled=True
        ).astype(jnp.float32),
        lax.psum_scatter(
            grads[1].astype(jnp.bfloat16), "dp", scatter_dimension=1, tiled=True
        ).astype(jnp.float32),
        lax.psum_scatter(
            grads[2].astype(jnp.bfloat16), "dp", scatter_dimension=0, tiled=True
        ).astype(jnp.float32),
        lax.psum_scatter(
            grads[3].astype(jnp.bfloat16), "dp", scatter_dimension=1, tiled=True
        ).astype(jnp.float32),
    )


def block_forward(resid_in, seg_local, gains, biases, weights):
    qkv_w, attn_w, up_w, down_w = weights
    normed = layer_norm(resid_in, gains[0], biases[0]).astype(jnp.bfloat16)
    normed_all, seg_all = (
        lax.all_gather(normed, "tp", axis=0, tiled=True),
        lax.all_gather(seg_local, "tp", axis=0, tiled=True),
    )
    query_h = split_heads(product(normed_all, qkv_w[0]).astype(jnp.bfloat16))
    key_h = split_heads(product(normed_all, qkv_w[1]).astype(jnp.bfloat16))
    value_h = split_heads(product(normed_all, qkv_w[2]).astype(jnp.bfloat16))
    heads_out, log_sums = attend(query_h, key_h, value_h, seg_all)
    attn_rows = join_heads(heads_out)
    middle = resid_in + combine_rows(product(attn_rows, attn_w))
    normed_mid = spread_rows(layer_norm(middle, gains[1], biases[1]).astype(jnp.bfloat16))
    hidden_pre = product(normed_mid, up_w)
    hidden = gelu_tanh(hidden_pre).astype(jnp.bfloat16)
    result = middle + combine_rows(product(hidden, down_w))
    kept = (
        resid_in,
        middle,
        normed_all,
        seg_all,
        query_h,
        key_h,
        value_h,
        log_sums,
        attn_rows,
        normed_mid,
        hidden_pre,
        hidden,
    )
    return (result, kept)


def block_backward(kept, gains, biases, weights, grad_result):
    (
        resid_in,
        middle,
        normed_all,
        seg_all,
        query_h,
        key_h,
        value_h,
        log_sums,
        attn_rows,
        normed_mid,
        hidden_pre,
        hidden,
    ) = kept
    qkv_w, attn_w, up_w, down_w = weights
    grad_branch = spread_grads(grad_result.astype(jnp.bfloat16))
    grad_down = product_tn(hidden, grad_branch)
    grad_hidden = product_nt(grad_branch, down_w)
    _, gelu_back = jax.vjp(gelu_tanh, hidden_pre)
    grad_pre = gelu_back(grad_hidden)[0].astype(jnp.bfloat16)
    grad_up = product_tn(normed_mid, grad_pre)
    grad_norm_mid = combine_grads(product_nt(grad_pre, up_w))
    _, norm_back_mid = jax.vjp(layer_norm, middle, gains[1], biases[1])
    grad_mid_ln, grad_gain_mid, grad_bias_mid = norm_back_mid(grad_norm_mid)
    grad_middle = grad_result + grad_mid_ln
    grad_attn_all = spread_grads(grad_middle.astype(jnp.bfloat16))
    grad_attn = product_tn(attn_rows, grad_attn_all)
    grad_heads = split_heads(product_nt(grad_attn_all, attn_w).astype(jnp.bfloat16))
    grad_query, grad_key, grad_value = attend_back(
        query_h, key_h, value_h, seg_all, log_sums, grad_heads
    )
    grad_parts = [join_heads(grad_query), join_heads(grad_key), join_heads(grad_value)]
    grad_qkv = jnp.stack([product_tn(normed_all, grad_part) for grad_part in grad_parts])
    grad_normed_part = (
        product_nt(grad_parts[0], qkv_w[0])
        + product_nt(grad_parts[1], qkv_w[1])
        + product_nt(grad_parts[2], qkv_w[2])
    )
    grad_normed = combine_grads(grad_normed_part)
    _, norm_back_in = jax.vjp(layer_norm, resid_in, gains[0], biases[0])
    grad_in_ln, grad_gain_in, grad_bias_in = norm_back_in(grad_normed)
    gain_grads = jnp.stack([grad_gain_in, grad_gain_mid])
    bias_grads = jnp.stack([grad_bias_in, grad_bias_mid])
    return (
        grad_middle + grad_in_ln,
        gain_grads,
        bias_grads,
        (grad_qkv, grad_attn, grad_up, grad_down),
    )


def local(
    tokens,
    segment_ids,
    norm_gains,
    norm_biases,
    w_qkv,
    w_attn_out,
    w_up,
    w_down,
    w_vq_in,
    w_vq_out,
    codebook,
    cotangent,
):
    gain_sum = jnp.zeros(norm_gains.shape, jnp.float32)
    bias_sum = jnp.zeros(norm_biases.shape, jnp.float32)
    vq_in_sum = jnp.zeros(w_vq_in.shape, jnp.float32)
    vq_out_sum = jnp.zeros(w_vq_out.shape, jnp.float32)
    code_sum = jnp.zeros(codebook.shape, jnp.float32)
    layer_sums = [None, None]
    outputs = []
    input_grads = []
    for micro in range(MICRO):
        resid_in = tokens[micro].astype(jnp.float32)
        seg_local = segment_ids[micro]
        enc_weights = fetch_weights(w_qkv, w_attn_out, w_up, w_down, 0)
        encoded, enc_kept = block_forward(
            resid_in, seg_local, norm_gains[0:2], norm_biases[0:2], enc_weights
        )
        (decoder_in, _), vq_back = jax.vjp(
            quantize, encoded, norm_gains[2], norm_biases[2], w_vq_in, w_vq_out, codebook
        )
        dec_weights = fetch_weights(w_qkv, w_attn_out, w_up, w_down, 1)
        decoded, dec_kept = block_forward(
            decoder_in, seg_local, norm_gains[3:5], norm_biases[3:5], dec_weights
        )
        outputs.append(decoded)
        grad_dec_in, gains_dec, biases_dec, grads_dec = block_backward(
            dec_kept, norm_gains[3:5], norm_biases[3:5], dec_weights, cotangent[micro]
        )
        grad_encoded, grad_gain_vq, grad_bias_vq, grad_in_w, grad_out_w, grad_codes = vq_back(
            (grad_dec_in, jnp.ones((), jnp.float32))
        )
        grad_input, gains_enc, biases_enc, grads_enc = block_backward(
            enc_kept, norm_gains[0:2], norm_biases[0:2], enc_weights, grad_encoded
        )
        input_grads.append(grad_input)
        gain_sum = gain_sum + jnp.concatenate([gains_enc, grad_gain_vq[None], gains_dec], axis=0)
        bias_sum = bias_sum + jnp.concatenate([biases_enc, grad_bias_vq[None], biases_dec], axis=0)
        vq_in_sum = vq_in_sum + grad_in_w
        vq_out_sum = vq_out_sum + grad_out_w
        code_sum = code_sum + grad_codes
        for layer, grads in ((0, grads_enc), (1, grads_dec)):
            reduced = reduce_weight_grads(grads)
            if layer_sums[layer] is None:
                layer_sums[layer] = reduced
            else:
                layer_sums[layer] = jax.tree.map(jnp.add, layer_sums[layer], reduced)
    gain_tot, bias_tot, vq_in_tot, vq_out_tot, code_tot = lax.psum(
        (gain_sum, bias_sum, vq_in_sum, vq_out_sum, code_sum), ("dp", "tp")
    )
    return (
        jnp.stack(outputs),
        jnp.stack(input_grads),
        gain_tot,
        bias_tot[0:3],
        bias_tot[3:5],
        jnp.stack([layer_sums[0][0], layer_sums[1][0]]),
        jnp.stack([layer_sums[0][1], layer_sums[1][1]]),
        jnp.stack([layer_sums[0][2], layer_sums[1][2]]),
        jnp.stack([layer_sums[0][3], layer_sums[1][3]]),
        vq_in_tot,
        vq_out_tot,
        code_tot,
    )


def solution(mesh):
    n_dp, n_tp = mesh.shape["dp"], mesh.shape["tp"]
    fits = n_tp == MICRO and n_dp == 16
    return jax.shard_map(
        functools.partial(whole_groups, n_dp) if fits else local,
        mesh=mesh,
        in_specs=(
            P(None, ("dp", "tp"), None),
            P(None, ("dp", "tp")),
            P(),
            P(),
            P(None, None, "dp", "tp"),
            P(None, "tp", "dp"),
            P(None, "dp", "tp"),
            P(None, "tp", "dp"),
            P(),
            P(),
            P(),
            P(None, ("dp", "tp"), None),
        ),
        out_specs=(
            P(None, ("dp", "tp"), None),
            P(None, ("dp", "tp"), None),
            P(),
            P(),
            P(),
            P(None, None, "dp", "tp"),
            P(None, "tp", "dp"),
            P(None, "dp", "tp"),
            P(None, "tp", "dp"),
            P(),
            P(),
            P(),
        ),
        check_vma=False,
    )
```

```python
import functools

import jax
import jax.numpy as jnp
from jax import lax
from jax.experimental import pallas as pl
from jax.experimental.pallas import tpu as pltpu
from jax.sharding import PartitionSpec as P

HEAD_DIM = 64
MICRO = 2
bf16 = jnp.bfloat16
f32 = jnp.float32
highest = lax.Precision.HIGHEST
ln_eps = 1e-05
norm_eps = 1e-06
temper = 10.0
commit_weight = 64.0
gelu_coef = 0.7978845608028654
masked_score = -1e30
log2e = 1.4426950408889634
vmem_cap = 26 * 1024 * 1024


PLANE = ((0, 0), (0, 1), (1, 0), (1, 1))


def exchange(values, dp_xor, tp_xor, n_dp):
    pairs = [
        (d * 2 + t, (d ^ dp_xor) * 2 + (t ^ tp_xor)) for d in range(n_dp) for t in range(2)
    ]
    return lax.ppermute(values, ("dp", "tp"), pairs)


def spread_line(shard, n_dp):
    return [shard] + [exchange(shard, 4 * k, 0, n_dp) for k in range(1, 4)]


def plane_send(lows, n_dp):
    return [exchange(low, 2 * y, x, n_dp) for (y, x), low in zip(PLANE[1:], lows)]


def line_send(lows, n_dp):
    return [exchange(low, 4 * k, 0, n_dp) for k, low in zip(range(1, 4), lows)]


def dot(a, b):
    return jnp.dot(a, b, preferred_element_type=f32)


def dot_nt(a, b, precision=None):
    return lax.dot_general(
        a, b, (((1,), (1,)), ((), ())), preferred_element_type=f32, precision=precision
    )


def dot_full(a, b):
    return jnp.dot(a, b, preferred_element_type=f32, precision=highest)


def ln_parts(x):
    centred = x - jnp.mean(x, axis=-1, keepdims=True)
    inv = lax.rsqrt(jnp.mean(centred * centred, axis=-1, keepdims=True) + ln_eps)
    return centred * inv, inv


def ln_back(grad, xhat, inv, gain):
    scaled = grad * gain
    return inv * (
        scaled
        - jnp.mean(scaled, axis=-1, keepdims=True)
        - xhat * jnp.mean(scaled * xhat, axis=-1, keepdims=True)
    )


def split2(x):
    hi = x.astype(bf16)
    return hi, (x - hi.astype(f32)).astype(bf16)


def split3(x):
    hi, _ = split2(x)
    rest = x - hi.astype(f32)
    mid = rest.astype(bf16)
    return hi, mid, (rest - mid.astype(f32)).astype(bf16)


def order_matrix(dp, inverse):
    at = lax.broadcasted_iota(jnp.int32, (512, 512), 0 if inverse else 1)
    other = lax.broadcasted_iota(jnp.int32, (512, 512), 1 if inverse else 0)
    block = at >> 5
    bits = ((block & 3) << 2) | (((block >> 2) & 1) << 1) | (block >> 3)
    return jnp.where(other == (((dp ^ bits) << 5) | (at & 31)), 1.0, 0.0).astype(bf16)


def ordered(x, matrix):
    if x.dtype == bf16:
        return dot(x, matrix)
    hi, mid, lo = split3(x)
    return (dot(hi, matrix) + dot(mid, matrix)) + dot(lo, matrix)


def w_at(a, b, t, first, width):
    parts = []
    for core in range(2):
        for y in range(2):
            if first < 1536:
                part = a[2 * core + y][t, :, :, first : first + width]
            else:
                part = b[2 * core + t][y, :, :, first - 1536 : first - 1536 + width]
            parts.append(part.reshape(128, width))
    return jnp.concatenate(parts, axis=0)


def put_grad(refs, t, cols, value):
    for core, ref in enumerate(refs):
        for y in range(2):
            rows = value[core * 256 + y * 128 : core * 256 + (y + 1) * 128]
            ref[2 * y + t, :, :, cols] = rows.reshape(4, 32, rows.shape[1])


def start_all(copies):
    for copy in copies:
        copy.start()


def wait_all(copies):
    for copy in copies:
        copy.wait()


def head_rows(ref, pair, which):
    own = ref[pl.ds(pair * 128 + which * HEAD_DIM, HEAD_DIM), :]
    zero = jnp.zeros_like(own)
    return jnp.concatenate([own, zero] if which == 0 else [zero, own], axis=0)


def segment_mask(own, other):
    ids = jnp.concatenate([own[:, 512:640], other[:, 512:640]], axis=0).astype(f32)
    return jnp.where(ids[:, 0:1] == ids.T[0:1, :], 0.0, masked_score)


def load_rows(x, own, other):
    if x is None:
        return jnp.concatenate([own[:, :512], other[:, :512]], axis=0).astype(f32)
    return x[...]


def gain_of(norms, at):
    return norms[at : at + 1, :]


def bias_of(norms, at):
    return norms[8 + at : 9 + at, :]


def attn_fwd_kernel(with_x, at, own, other, norms, *refs):
    w, refs = refs[:4], refs[4:]
    x, refs = (refs[0], refs[1:]) if with_x else (None, refs)
    x1, lse, saved, refs = refs[0], refs[1], refs[2:8], refs[8:]
    h, vt, ot, mask, qs, k, v, o, qst, kt, out_sems = refs
    keeps = [
        pltpu.make_async_copy(held, to, out_sems.at[i])
        for i, (held, to) in enumerate(zip((qs, k, v, o, qst, kt), saved))
    ]
    xf = load_rows(x, own, other)
    h[...] = (ln_parts(xf)[0] * gain_of(norms, at) + bias_of(norms, at)).astype(bf16)
    mask[...] = segment_mask(own, other)
    for t in range(2):
        cols = slice(t * 256, (t + 1) * 256)
        q = dot(h[...], w_at(w, None, t, 0, 256)).astype(bf16)
        qs[:, cols] = (q * HEAD_DIM ** (-0.5)).astype(bf16)
        k[:, cols] = dot(h[...], w_at(w, None, t, 256, 256)).astype(bf16)
        v[:, cols] = dot(h[...], w_at(w, None, t, 512, 256)).astype(bf16)
    qst[...] = qs[...].T
    kt[...] = k[...].T
    vt[...] = v[...].T
    for i in (0, 1, 2, 4, 5):
        keeps[i].start()
    for pair in range(4):
        k_pair = k[:, pair * 128 : (pair + 1) * 128]
        for which in range(2):
            scores = dot(k_pair, head_rows(qst, pair, which)) + mask[...]
            top = jnp.max(scores, axis=0, keepdims=True)
            numer = jnp.exp(scores - top).astype(bf16)
            rows = pl.ds(pair * 128 + which * HEAD_DIM, HEAD_DIM)
            left = jnp.concatenate([vt[rows, :], jnp.ones((16, 512), bf16)], axis=0)
            both = dot(left, numer)
            total = both[HEAD_DIM : HEAD_DIM + 1, :]
            ot[rows, :] = (both[:HEAD_DIM, :] / total).astype(bf16)
            lse[pl.ds(pair * 2 + which, 1), :] = top + jnp.log(total)
    o[...] = ot[...].T
    keeps[3].start()
    acc = xf
    for t in range(2):
        acc = acc + dot_nt(o[:, t * 256 : (t + 1) * 256], w_at(w, None, t, 768, 256))
    x1[...] = acc
    wait_all(keeps)


def gelu_parts(u):
    square = u * u
    tanh = jnp.tanh(gelu_coef * u * (1.0 + 0.044715 * square))
    return 0.5 * u * (1.0 + tanh), tanh, square


def mlp_weights(w):
    def up(t, part):
        return w_at(w[:4], w[4:], t, 1024 + part * 512, 512)

    def down(t, part):
        return w_at(w[:4], w[4:], t, 2048 + part * 512, 512)

    return up, down


def mlp_rows(at, x, norms, w, h2):
    up, down = mlp_weights(w)
    h2[...] = (ln_parts(x)[0] * gain_of(norms, at) + bias_of(norms, at)).astype(bf16)
    for t in range(2):
        for part in range(2):
            hidden = gelu_parts(dot(h2[...], up(t, part)))[0].astype(bf16)
            x = x + dot_nt(hidden, down(t, part))
    return x


def mlp_bwd_kernel(split, at, ids, x1, norms, *refs):
    up, down = mlp_weights(refs[:8])
    refs = refs[8:]
    if split:
        own, other, refs = refs[0], refs[1], refs[2:]
    else:
        dy, refs = refs[0], refs[1:]
    dx1, small, grads = refs[0], refs[1], refs[2:4]
    h2, h2t, dyb, dybt, dh2 = refs[4:9]
    if split:
        dy = refs[9]
        dy[0:256, :] = ordered(own[ids[1]], order_matrix(ids[0], False))
        dy[256:, :] = other[:, 640:].astype(f32)
    h2[...] = (ln_parts(x1[...])[0] * gain_of(norms, at) + bias_of(norms, at)).astype(bf16)
    h2t[...] = h2[...].T
    dyb[...] = dy[...].astype(bf16)
    dybt[...] = dyb[...].T
    for t in range(2):
        for part in range(2):
            cols = slice(part * 512, (part + 1) * 512)
            w_up = up(t, part)
            pre = dot(h2[...], w_up)
            hidden, tanh, square = gelu_parts(pre)
            slope = 0.5 * (1.0 + tanh) + (0.5 * gelu_coef) * pre * (1.0 - tanh * tanh) * (
                1.0 + (3 * 0.044715) * square
            )
            dhidden = dot(dyb[...], down(t, part))
            dpre = (dhidden * slope).astype(bf16)
            out_cols = slice(1024 + part * 512, 1024 + (part + 1) * 512)
            put_grad(grads, t, out_cols, dot(dybt[...], hidden.astype(bf16)).astype(bf16))
            put_grad(grads, t, cols, dot(h2t[...], dpre).astype(bf16))
            more = dot_nt(dpre, w_up)
            if t + part == 0:
                dh2[...] = more
            else:
                dh2[...] += more
    xhat, inv = ln_parts(x1[...])
    grad = dh2[...]
    small[0:1, :] = jnp.sum(grad * xhat, axis=0, keepdims=True)
    small[1:2, :] = jnp.sum(grad, axis=0, keepdims=True)
    dx1[...] = dy[...] + ln_back(grad, xhat, inv, gain_of(norms, at))


def heads_back(low, w, saved, lse, mask, put_out, scratch):
    qs, k, v, o, qst, kt = saved
    flip, do, dot_t, dqt, dq, dk, dv = scratch
    flip[...] = low.T
    for t in range(2):
        cols = slice(t * 256, (t + 1) * 256)
        do[:, cols] = dot(low, w_at(w, None, t, 768, 256)).astype(bf16)
        put_out(t, dot(flip[...], o[:, cols]).astype(bf16))
    dot_t[...] = do[...].T
    first = lax.broadcasted_iota(jnp.int32, (512, 128), 1) < HEAD_DIM
    for pair in range(4):
        lanes = slice(pair * 128, (pair + 1) * 128)
        dvs, dks = [], []
        for which in range(2):
            head = pair * 2 + which
            rows = pl.ds(head * HEAD_DIM, HEAD_DIM)
            scores = dot(k[:, lanes], head_rows(qst, pair, which)) + mask[...]
            probs = jnp.exp(scores - lse[head : head + 1, :])
            dprobs = dot(v[:, lanes], head_rows(dot_t, pair, which))
            shift = jnp.sum(probs * dprobs, axis=0, keepdims=True)
            dscore = (probs * (dprobs - shift)).astype(bf16)
            dvs.append(dot(probs.astype(bf16), do[:, lanes]))
            dks.append(dot(dscore, qs[:, lanes]))
            dqt[rows, :] = (dot(kt[rows, :], dscore) * HEAD_DIM ** (-0.5)).astype(bf16)
        dv[:, lanes] = jnp.where(first, dvs[0], dvs[1]).astype(bf16)
        dk[:, lanes] = jnp.where(first, dks[0], dks[1]).astype(bf16)
    dq[...] = dqt[...].T


def rows_back(at, xf, norms, w, parts, small, grads, h, flip):
    h[...] = (ln_parts(xf)[0] * gain_of(norms, at) + bias_of(norms, at)).astype(bf16)
    flip[...] = h[...].T
    grad = jnp.zeros((512, 512), f32)
    for t in range(2):
        cols = slice(t * 256, (t + 1) * 256)
        for index, part in enumerate(parts):
            w_cols = slice(index * 256, (index + 1) * 256)
            put_grad(grads, t, w_cols, dot(flip[...], part[:, cols]).astype(bf16))
            grad = grad + dot_nt(part[:, cols], w_at(w, None, t, index * 256, 256))
    xhat, inv = ln_parts(xf)
    small[0:1, :] = jnp.sum(grad * xhat, axis=0, keepdims=True)
    small[1:2, :] = jnp.sum(grad, axis=0, keepdims=True)
    return ln_back(grad, xhat, inv, gain_of(norms, at))


def take_saved(saved, held, sems):
    copies = [
        pltpu.make_async_copy(a, b, sems.at[i]) for i, (a, b) in enumerate(zip(saved, held))
    ]
    start_all(copies)
    return copies


def attn_bwd_kernel(at, own, other, dx1, norms, lse, *refs):
    w, saved, x, refs = refs[:4], refs[4:10], refs[10], refs[11:]
    dx, small, grads = refs[0], refs[1], refs[2:4]
    mask, h, held, scratch, sems = refs[4], refs[5], refs[6:12], refs[12:19], refs[19]
    copies = take_saved(saved, held, sems)
    mask[...] = segment_mask(own, other)
    low = dx1[...].astype(bf16)
    wait_all(copies)

    def put_out(t, value):
        put_grad(grads, t, slice(768, 1024), value)

    heads_back(low, w, held, lse, mask, put_out, scratch)
    dx[...] = dx1[...] + rows_back(
        at, x[...], norms, w, scratch[4:], small, grads, h, scratch[0]
    )


def heads_bwd_kernel(own, other, dx1, lse, *refs):
    w, saved, refs = refs[:4], refs[4:10], refs[10:]
    parts, grads, mask, held = refs[:3], refs[3:5], refs[5], refs[6:12]
    scratch, sems = (*refs[12:16], *parts), refs[16]
    copies = take_saved(saved, held, sems)
    mask[...] = segment_mask(own, other)
    low = dx1[...].astype(bf16)
    wait_all(copies)

    def put_out(t, value):
        put_grad(grads, t, slice(0, 256), value)

    heads_back(low, w, held, lse, mask, put_out, scratch)


def rows_bwd_kernel(
    ids, own, other, dx1, norms, dq, dk, dv, out_0, out_1, other_small, d_x1, *refs
):
    w, d_w, (dx, dx_low, y, y_low), grads, (small, h, flip) = (
        refs[:4],
        refs[4:12],
        refs[12:16],
        refs[16:18],
        refs[18:],
    )
    total = dx1[...] + rows_back(
        0, load_rows(None, own, other), norms, w, (dq, dk, dv), small, grads, h, flip
    )
    dx[...] = total[:256, :]
    dx_low[...] = total[256:, :].astype(bf16)
    rows = jnp.concatenate([small[0:2, :], other_small[0:2, :], jnp.zeros((4, 512), f32)], axis=0)
    packed = pack_rows(ordered(rows, order_matrix(ids[0], True)))
    for grad, part in zip(grads, (out_0, out_1)):
        for i in range(4):
            for z in range(4):
                grad[i, z, :, 768:1024] = part[i, z]
                grad[i, z, :, 1024:1152] = packed
    rows = mlp_rows(4, d_x1[...], norms, d_w, h)
    y[...] = rows[:256, :]
    y_low[...] = rows[256:, :].astype(bf16)


def pack_rows(rows):
    cut = [rows[i : i + 1, 128 * j : 128 * (j + 1)] for i in range(4) for j in range(4)]
    return jnp.concatenate(split2(jnp.concatenate(cut, axis=0)), axis=0)


def code_prep_kernel(book_t, stack, stack_t):
    def one_chunk(index, _):
        lanes = pl.ds(pl.multiple_of(index * 512, 512), 512)
        rows = book_t[:, lanes]
        unit = rows * lax.rsqrt(jnp.sum(rows * rows, axis=0, keepdims=True) + norm_eps)
        hi, mid, lo = split3(unit)
        stack_t[:, lanes] = jnp.concatenate([hi, mid, lo, jnp.ones((32, 512), bf16)], axis=0)
        tall = jnp.concatenate([hi, mid, lo, hi, mid, hi, jnp.zeros((64, 512), bf16)], axis=0)
        stack[lanes, :] = tall.T
        return 0

    lax.fori_loop(0, book_t.shape[1] // 512, one_chunk, 0)


def factor_stack(x):
    hi, mid, lo = split3(x)
    return jnp.concatenate([hi, hi, hi, mid, mid, lo, jnp.zeros((64, x.shape[1]), bf16)], axis=0)


def code_loads(pairs, sems):
    loads = []
    for piece in range(4):
        group = []
        for at, (held, to, by_row) in enumerate(pairs):
            size = held.shape[0 if by_row else 1] // 4
            part = pl.ds(piece * size, size)
            place = (part, slice(None)) if by_row else (slice(None), part)
            group.append(pltpu.make_async_copy(held.at[place], to.at[place], sems.at[at, piece]))
        start_all(group)
        loads.append(group)
    return loads


def mlp_vq_kernel(x1, norms, vq_w, stack_hbm, stack_t_hbm, *refs):
    w, (e, u, kept, h2, acc, stack, stack_t, sems) = refs[:8], refs[8:]
    loads = code_loads([(stack_hbm, stack, True), (stack_t_hbm, stack_t, False)], sems)
    e[...] = mlp_rows(1, x1[...], norms, w, h2)
    lnv = ln_parts(e[...])[0] * gain_of(norms, 2) + bias_of(norms, 2)
    raw = dot_nt(vq_w[0:32, :], lnv, highest)
    inv = lax.rsqrt(jnp.sum(raw * raw, axis=0, keepdims=True) + norm_eps)
    latent = raw * inv
    right = factor_stack(latent * (temper * log2e))
    chunks = stack.shape[0] // 2048
    for piece, group in enumerate(loads):
        wait_all(group)
        for part in range(piece * chunks // 4, (piece + 1) * chunks // 4):
            numers = []
            for index in range(4 * part, 4 * part + 4):
                codes = slice(index * 512, (index + 1) * 512)
                numers.append(jnp.exp2(dot(stack[codes, :], right)).astype(bf16))
            sums = dot(
                stack_t[:, part * 2048 : (part + 1) * 2048], jnp.concatenate(numers, axis=0)
            )
            if part == 0:
                acc[...] = sums
            else:
                acc[...] += sums
    total = acc[96:97, :]
    soft = (acc[0:32, :] + acc[32:64, :] + acc[64:96, :]) / total
    kept[0:32, :] = latent
    kept[32:64, :] = soft
    kept[64:65, :] = total
    kept[65:66, :] = inv
    u[...] = dot_full(soft.T, vq_w[32:64, :])


def vq_bwd_kernel(ids, e, du, norms, vq_w, stack_hbm, stack_t_hbm, book_hbm, kept, *refs):
    small0, small1, de, code_keep, code_send = refs[:5]
    acc, grads, small, tail, stack, stack_t, book_t, load_sems, sems = refs[5:]
    loads = code_loads(
        [(stack_hbm, stack, True), (stack_t_hbm, stack_t, False), (book_hbm, book_t, False)],
        load_sems,
    )
    xhat, inv_ln = ln_parts(e[...])
    lnv = xhat * gain_of(norms, 2) + bias_of(norms, 2)
    latent, soft = kept[0:32, :], kept[32:64, :]
    total, inv = kept[64:65, :], kept[65:66, :]
    direct = (2.0 * 1.25 * commit_weight) * (latent - soft)
    dsoft = dot_nt(vq_w[32:64, :], du[...], highest) - direct
    small[32:64, :] = dot_full(soft, du[...])
    shift = jnp.sum(dsoft * soft, axis=0, keepdims=True) / total
    dsoft = dsoft / total
    right = jnp.concatenate(
        [factor_stack(latent * (temper * log2e)), factor_stack(dsoft)], axis=1
    )
    pads = jnp.zeros((64, 512), f32)

    def tall(x):
        hi, lo = split2(x)
        return jnp.concatenate([hi.astype(f32), lo.astype(f32), pads], axis=0).T.astype(bf16)

    sides = jnp.concatenate([tall(dsoft), tall(latent * temper)], axis=0)
    chunks = stack.shape[0] // 2048
    for piece, group in enumerate(loads):
        wait_all(group)
        for part in range(piece * chunks // 4, (piece + 1) * chunks // 4):
            dlogits = []
            for index in range(4 * part, 4 * part + 4):
                codes = slice(index * 512, (index + 1) * 512)
                both = dot(stack[codes, :], right)
                numer = jnp.exp2(both[:, :512])
                dlogit = (numer * (both[:, 512:] - shift)).astype(bf16)
                dlogits.append(dlogit)
                sums = jnp.concatenate([numer.astype(bf16), dlogit], axis=1)
                dcode = dot(sums, sides).T
                dcode = dcode[0:32, :] + dcode[32:64, :]
                rows = book_t[:, codes]
                scale = lax.rsqrt(jnp.sum(rows * rows, axis=0, keepdims=True) + norm_eps)
                unit = rows * scale
                grads[:, codes] = (
                    scale * (dcode - unit * jnp.sum(unit * dcode, axis=0, keepdims=True))
                ).astype(bf16)
            sums = dot(
                stack_t[0:96, part * 2048 : (part + 1) * 2048], jnp.concatenate(dlogits, axis=0)
            )
            if part == 0:
                acc[...] = sums
            else:
                acc[...] += sums
    dlatent = temper * (acc[0:32, :] + acc[32:64, :] + acc[64:96, :]) + direct
    draw = inv * (dlatent - latent * jnp.sum(latent * dlatent, axis=0, keepdims=True))
    small[0:32, :] = dot_full(draw, lnv)
    dln = dot_full(draw.T, vq_w[0:32, :])
    small[64:65, :] = jnp.sum(dln * xhat, axis=0, keepdims=True)
    small[65:66, :] = jnp.sum(dln, axis=0, keepdims=True)
    small[66:68, :] = small0[0:2, :]
    small[68:70, :] = small1[0:2, :]
    small[70:96, :] = jnp.zeros((26, 512), f32)
    small[...] = ordered(small[...], order_matrix(ids[0], True))
    for block in range(3):
        for at, part in enumerate(split2(small[block * 32 : (block + 1) * 32, :])):
            for side in range(2):
                tail[block * 2 + side, :, at * 256 : (at + 1) * 256] = part[
                    :, side * 256 : (side + 1) * 256
                ]
    tail[6:8] = jnp.zeros((2, 32, 512), bf16)
    core, z = ids[0] % 2, ids[0] // 4
    copies = []
    for slot, (at, to) in enumerate(((core, code_keep), (1 - core, code_send))):
        for k in range(4):
            part = at * 4 + (z ^ k)
            lanes = pl.ds(pl.multiple_of(part * 1024, 1024), 1024)
            copies += [
                pltpu.make_async_copy(
                    grads.at[:, lanes], to.at[k, :, pl.ds(0, 1024)], sems.at[0, slot, k]
                ),
                pltpu.make_async_copy(
                    tail.at[part], to.at[k, :, pl.ds(1024, 512)], sems.at[1, slot, k]
                ),
            ]
    for copy in copies:
        copy.start()
    de[...] = ln_back(dln, xhat, inv_ln, gain_of(norms, 2))
    for copy in copies:
        copy.wait()


SMEM = pl.BlockSpec(memory_space=pltpu.SMEM)
VMEM = pl.BlockSpec(memory_space=pltpu.VMEM)
ANY = pl.BlockSpec(memory_space=pl.ANY)


def shaped(*pairs):
    return [jax.ShapeDtypeStruct(shape, dtype) for shape, dtype in pairs]


def pin(array):
    return pltpu.with_memory_space_constraint(array, pltpu.HBM)


def call(kernel, name, in_specs, out_specs, outs, scratch, flops, after=(), carry=()):
    n_in, n_extra, n_out = len(in_specs), len(after) + len(carry), len(outs)

    def body(*refs):
        first = n_in + n_extra
        kernel(*refs[:n_in], *refs[first : first + n_out], *refs[first + n_out + len(carry) :])

    made = pl.pallas_call(
        body,
        name=name,
        in_specs=in_specs + [ANY] * n_extra,
        out_specs=out_specs + [ANY] * len(carry),
        out_shape=outs + [jax.ShapeDtypeStruct(a.shape, a.dtype) for a in carry],
        scratch_shapes=scratch,
        input_output_aliases={n_in + len(after) + i: n_out + i for i in range(len(carry))},
        compiler_params=pltpu.CompilerParams(vmem_limit_bytes=vmem_cap),
        cost_estimate=pl.CostEstimate(flops=flops, bytes_accessed=10**6, transcendentals=0),
    )

    def run(*args):
        res = made(*args, *after, *carry)
        return (*res[:n_out], list(res[n_out:]))

    return run


DMA = pltpu.SemaphoreType.DMA
ROWS2 = (512, 512)


def attn_fwd(at, marked, xs, norms, w, after=(), carry=()):
    outs = shaped((ROWS2, f32), ((8, 512), f32)) + [pltpu.HBM(ROWS2, bf16)] * 6
    scratch = [
        *[pltpu.VMEM(ROWS2, bf16)] * 3,
        pltpu.VMEM(ROWS2, f32),
        *[pltpu.VMEM(ROWS2, bf16)] * 6,
        DMA((6,)),
    ]
    x1, lse, *saved, carried = call(
        functools.partial(attn_fwd_kernel, bool(xs), at),
        "attn_fwd",
        [VMEM] * (7 + len(xs)),
        [VMEM] * 2 + [ANY] * 6,
        outs,
        scratch,
        10**10,
        after,
        carry,
    )(*marked, norms, *w[:4], *xs)
    return x1, (lse, *saved), carried


def mlp_bwd(at, ids, x1, dys, norms, w, after=(), carry=()):
    scratch = [
        *[pltpu.VMEM(ROWS2, bf16)] * 4,
        *[pltpu.VMEM(ROWS2, f32)] * len(dys),
    ]
    return call(
        functools.partial(mlp_bwd_kernel, len(dys) == 2, at),
        "mlp_bwd",
        [SMEM] + [VMEM] * (10 + len(dys)),
        [VMEM] * 4,
        shaped((ROWS2, f32), ((8, 512), f32), *[((4, 4, 32, 2048), bf16)] * 2),
        scratch,
        15 * 10**9,
        after,
        carry,
    )(ids, x1, norms, *w, *dys)


def attn_bwd(at, marked, x, dx1, norms, saved, w, after=(), carry=()):
    scratch = [pltpu.VMEM(ROWS2, f32), *[pltpu.VMEM(ROWS2, bf16)] * 14, DMA((6,))]
    outs = shaped((ROWS2, f32), ((8, 512), f32), *[((4, 4, 32, 1024), bf16)] * 2)
    return call(
        functools.partial(attn_bwd_kernel, at),
        "attn_bwd",
        [VMEM] * 9 + [ANY] * 6 + [VMEM],
        [VMEM] * 4,
        outs,
        scratch,
        15 * 10**9,
        after,
        carry,
    )(*marked, dx1, norms, saved[0], *w[:4], *map(pin, saved[1:]), x)


def heads_bwd(marked, dx1, saved, w, after=(), carry=()):
    scratch = [pltpu.VMEM(ROWS2, f32), *[pltpu.VMEM(ROWS2, bf16)] * 10, DMA((6,))]
    outs = shaped(*[(ROWS2, bf16)] * 3, *[((4, 4, 32, 256), bf16)] * 2)
    return call(
        heads_bwd_kernel,
        "heads_bwd",
        [VMEM] * 8 + [ANY] * 6,
        [VMEM] * 5,
        outs,
        scratch,
        10 * 10**9,
        after,
        carry,
    )(*marked, dx1, saved[0], *w[:4], *map(pin, saved[1:]))


def rows_bwd(ids, marked, dx1, norms, parts, other_small, d_x1, w, d_w, after=(), carry=()):
    scratch = [pltpu.VMEM((8, 512), f32), *[pltpu.VMEM(ROWS2, bf16)] * 2]
    outs = shaped(*[((256, 512), f32), ((256, 512), bf16)] * 2, *[((4, 4, 32, 1152), bf16)] * 2)
    return call(
        rows_bwd_kernel,
        "rows_bwd",
        [SMEM] + [VMEM] * 23,
        [VMEM] * 6,
        outs,
        scratch,
        10 * 10**9,
        after,
        carry,
    )(ids, *marked, dx1, norms, *parts, other_small, d_x1, *w[:4], *d_w)


def code_prep(book_t, after=(), carry=()):
    codes = book_t.shape[1]
    return call(
        code_prep_kernel,
        "code_prep",
        [VMEM],
        [VMEM] * 2,
        shaped(((codes, 256), bf16), ((128, codes), bf16)),
        [],
        6 * 10**9,
        after,
        carry,
    )(book_t)


def mlp_vq(x1, norms, vq_w, stack, stack_t, w, after=(), carry=()):
    return call(
        mlp_vq_kernel,
        "mlp_vq",
        [VMEM] * 3 + [ANY] * 2 + [VMEM] * 8,
        [VMEM] * 3,
        shaped((ROWS2, f32), (ROWS2, f32), ((72, 512), f32)),
        [
            pltpu.VMEM(ROWS2, bf16),
            pltpu.VMEM((128, 512), f32),
            pltpu.VMEM(stack.shape, bf16),
            pltpu.VMEM(stack_t.shape, bf16),
            DMA((2, 4)),
        ],
        25 * 10**9,
        after,
        carry,
    )(x1, norms, vq_w, pin(stack), pin(stack_t), *w)


def vq_bwd(ids, e, du, norms, vq_w, codes, kept, smalls, after=(), carry=()):
    scratch = [
        pltpu.VMEM((96, 512), f32),
        pltpu.VMEM(codes[2].shape, bf16),
        pltpu.VMEM((96, 512), f32),
        pltpu.VMEM((8, 32, 512), bf16),
        *[pltpu.VMEM(a.shape, a.dtype) for a in codes],
        DMA((3, 4)),
        DMA((2, 2, 4)),
    ]
    return call(
        vq_bwd_kernel,
        "vq_bwd",
        [SMEM] + [VMEM] * 4 + [ANY] * 3 + [VMEM] * 3,
        [VMEM] + [ANY] * 2,
        shaped((ROWS2, f32), *[((4, 32, 1536), bf16)] * 2),
        scratch,
        25 * 10**9,
        after,
        carry,
    )(ids, e, du, norms, vq_w, *map(pin, codes), kept, *smalls)


def lines_kernel(cuts, *refs):
    first = 0
    for out, width in zip(refs[4:], cuts):
        for k in range(4):
            out[k] = refs[k][:, first : first + width]
        first += width


def stack_lines(shards, cuts, after=(), carry=()):
    return call(
        functools.partial(lines_kernel, cuts),
        "stack_lines",
        [VMEM] * 4,
        [VMEM] * len(cuts),
        shaped(*[((4, 32, width), bf16) for width in cuts]),
        [],
        1,
        after,
        carry,
    )(*shards)


def pack_kernel(*refs):
    hbm, outs, held, sems = refs[:4], refs[4:6], refs[6:10], refs[10]
    copies = [pltpu.make_async_copy(hbm[at], held[at], sems.at[at]) for at in range(4)]
    start_all(copies)
    wait_all(copies)
    qkv, out_t, up, down_t = held
    for layer, out in enumerate(outs):
        for index in range(3):
            out[:, index * 256 : (index + 1) * 256] = qkv[layer, index]
        out[:, 768:1024] = out_t[layer]
        out[:, 1024:2048] = up[layer]
        out[:, 2048:] = down_t[layer]


def pack_weights(*arrays):
    return call(
        pack_kernel,
        "pack_weights",
        [ANY] * 4,
        [VMEM] * 2,
        shaped(*[((32, 3072), bf16)] * 2),
        [*[pltpu.VMEM(a.shape, a.dtype) for a in arrays], DMA((4,))],
        1,
    )(*map(pin, arrays))[:-1]


def pairs_kernel(*refs):
    count = len(refs) // 3
    for at in range(count):
        refs[2 * count + at][0] = refs[2 * at][...]
        refs[2 * count + at][1] = refs[2 * at + 1][...]


def stack_pairs(pairs, after=(), carry=()):
    return call(
        pairs_kernel,
        "stack_pairs",
        [VMEM] * (2 * len(pairs)),
        [VMEM] * len(pairs),
        shaped(*[((2, *a.shape), bf16) for a, _ in pairs]),
        [],
        1,
        after,
        carry,
    )(*[array for pair in pairs for array in pair])


def gate(after, carry):
    def kernel(out):
        out[...] = jnp.zeros_like(out)

    return call(kernel, "gate", [], [VMEM], shaped(((8, 128), f32)), [], 1, after, carry)()[-1]


def rows_in_kernel(ids, *refs):
    hbm, (own, send, norms, vq_w), held, sems = refs[:7], refs[7:11], refs[11:18], refs[18]
    copies = [pltpu.make_async_copy(hbm[at], held[at], sems.at[at]) for at in range(7)]
    start_all(copies)
    matrix = order_matrix(ids[0], False)
    wait_all(copies)
    tokens, segs, cot, gains, biases, in_t, out_w = held
    for to, micro in ((send, 1 - ids[1]), (own, ids[1])):
        to[:, :512] = ordered(tokens[micro], matrix).astype(bf16)
        ids_row = segs[pl.ds(micro, 1), :].astype(f32)
        to[:, 512:640] = jnp.broadcast_to(ids_row, (128, 256)).T.astype(bf16)
    send[:, 640:] = ordered(cot[1 - ids[1]].astype(bf16), matrix).astype(bf16)
    pad = jnp.zeros((3, 512), f32)
    rows = jnp.concatenate([gains[...], pad, biases[...], pad], axis=0)
    norms[...] = ordered(rows, matrix)
    vq_w[...] = ordered(jnp.concatenate([in_t[...], out_w[...]], axis=0), matrix)


def rows_in(ids, *arrays):
    outs = shaped(
        ((256, 640), bf16), ((256, 1152), bf16), ((16, 512), f32), ((64, 512), f32)
    )
    return call(
        rows_in_kernel,
        "rows_in",
        [SMEM] + [ANY] * 7,
        [VMEM] * 4,
        outs,
        [*[pltpu.VMEM(a.shape, a.dtype) for a in arrays], DMA((7,))],
        1,
    )(ids, *map(pin, arrays))[:-1]


def joined(block):
    return block[0:16, 1024:].astype(f32) + block[16:32, 1024:].astype(f32)


def put_small(value, own, blocks):
    hi, lo = split2(value)
    own[0:16, 1024:] = hi.astype(f32) + lo.astype(f32)
    for block in blocks:
        block[0:16, 1024:] = hi
        block[16:32, 1024:] = lo


def near_kernel(ids, ins, outs):
    keep, other = ins
    for i in range(4):
        outs[i][...] = (keep[i].astype(f32) + other[i].astype(f32)).astype(outs[i].dtype)
    if keep.shape[3] == 1152:
        value = joined(keep.at[0, 0]) + joined(other.at[0, 0])
        put_small(value, outs[0].at[0], [out.at[0] for out in outs[1:]])


def near_task(keep, other):
    shape = keep.shape[1:]
    return near_kernel, [keep, other], shaped((shape, f32), *[(shape, bf16)] * 3)


def put_code(ref, first, code):
    for i in range(3):
        ref[first + i] = code[:, 1024 * i : 1024 * (i + 1)]


def get_code(ref, first):
    return jnp.concatenate([ref[first + i] for i in range(3)], axis=1)


def swapped(code):
    return jnp.concatenate([code[:, 1536:], code[:, :1536]], axis=1)


def code_sum(a, b):
    done = []
    for first in range(0, a.shape[1], 1536):
        total = a[:, first : first + 1024].astype(f32) + b[:, first : first + 1024].astype(f32)
        small = [
            x[:, first + 1024 : first + 1280].astype(f32) + x[:, first + 1280 : first + 1536].astype(f32)
            for x in (a, b)
        ]
        done += [total.astype(bf16), *split2(small[0] + small[1])]
    return jnp.concatenate(done, axis=1)


def fork_kernel(ids, ins, outs):
    keep, other, code, code_other = ins
    own_up, to_x, own_down, to_y, code_out = outs
    for at, (own, send, kept, sent) in enumerate(
        ((own_up, to_x, (0, 2), (1, 3)), (own_down, to_y, (0, 1), (2, 3)))
    ):
        cols = slice(1024 * at, 1024 * (at + 1))
        for j in range(2):
            own[j] = keep[kept[j], :, :, cols].astype(f32) + other[kept[j], :, :, cols].astype(f32)
            total = keep[sent[j], :, :, cols].astype(f32) + other[sent[j], :, :, cols].astype(f32)
            send[4 * j : 4 * (j + 1)] = total.astype(bf16)
    code_out[...] = code_sum(code[...], code_other[...])
    put_code(to_x, 8, code_out)


def fork_task(keep, other, code, code_other):
    outs = shaped(
        ((2, 4, 32, 1024), f32),
        ((11, 32, 1024), bf16),
        ((2, 4, 32, 1024), f32),
        ((8, 32, 1024), bf16),
        (code.shape, bf16),
    )
    return fork_kernel, [keep, other, code, code_other], outs


def half_kernel(ids, ins, outs):
    own_up, from_x, own_down, from_y, code = ins
    up, to_y, down, to_x, code_out = outs
    for own, other, kept, send in ((own_up, from_x, up, to_y), (own_down, from_y, down, to_x)):
        kept[...] = own[0] + other[0:4].astype(f32)
        send[0:4] = (own[1] + other[4:8].astype(f32)).astype(bf16)
    code_out[...] = code_sum(code[...], get_code(from_x, 8))


def half_task(own_up, from_x, own_down, from_y, code):
    outs = shaped(*[((4, 32, 1024), f32), ((4, 32, 1024), bf16)] * 2, (code.shape, bf16))
    return half_kernel, [own_up, from_x, own_down, from_y, code], outs


def join_kernel(ids, ins, outs):
    own_up, from_y, own_down, from_x = ins
    kept, send = outs
    for at, (own, other) in enumerate(((own_up, from_y), (own_down, from_x))):
        cols = slice(1024 * at, 1024 * (at + 1))
        for k in range(2):
            kept[k, :, cols] = own[2 * k] + other[2 * k].astype(f32)
            send[k, :, cols] = (own[2 * k + 1] + other[2 * k + 1].astype(f32)).astype(bf16)


def join_task(own_up, from_y, own_down, from_x):
    outs = shaped(((2, 32, 2048), f32), ((2, 32, 2048), bf16))
    return join_kernel, [own_up, from_y, own_down, from_x], outs


def line_step_kernel(ids, ins, outs):
    kept, other = ins
    outs[0][...] = kept[0] + other[0].astype(f32)
    outs[1][...] = (kept[1] + other[1].astype(f32)).astype(bf16)


def line_step_task(kept, other):
    shape = kept.shape[1:]
    return line_step_kernel, [kept, other], shaped((shape, f32), (shape, bf16))


def plane_kernel(ids, ins, outs):
    for k in range(4):
        total = ins[0][k]
        for other in ins[1:]:
            total = total + other[k].astype(f32)
        outs[k][...] = total.astype(outs[k].dtype)
    if ins[0].shape[2] == 1152:
        x, y, xy = [joined(other.at[0]) for other in ins[1:]]
        put_small((ins[0][0, 0:16, 1024:] + x) + (y + xy), outs[0], outs[1:])


def plane_line_kernel(ids, ins, outs):
    kept, send = outs
    for k in range(4):
        total = ins[0][k]
        for other in ins[1:]:
            total = total + other[k].astype(f32)
        to = send if k % 2 else kept
        to[k // 2] = total.astype(to.dtype)
    x, y, xy = [joined(other.at[0]) for other in ins[1:]]
    put_small((ins[0][0, 0:16, 1024:] + x) + (y + xy), kept.at[0], [send.at[0]])


def plane_line_task(own, others):
    outs = shaped(((2, 32, 1152), f32), ((2, 32, 1152), bf16))
    return plane_line_kernel, [own, *others], outs


def small_step_kernel(ids, ins, outs):
    kept, other = ins
    line_step_kernel(ids, ins, outs)
    put_small(kept[0, 0:16, 1024:] + joined(other.at[0]), outs[0], [outs[1]])


def small_step_task(kept, other):
    shape = kept.shape[1:]
    return small_step_kernel, [kept, other], shaped((shape, f32), (shape, bf16))


def plane_task(own, others):
    shape = own.shape[1:]
    return plane_kernel, [own, *others], shaped((shape, f32), *[(shape, bf16)] * 3)


def plane_join_kernel(ids, ins, outs):
    own, others, m_own, m_lows = ins[0], ins[1:4], ins[4], ins[5:]
    kept, send = outs
    for k in range(4):
        total = own[k]
        for other in others:
            total = total + other[k].astype(f32)
        rest = m_own if k == 0 else m_lows[k - 1]
        to = send if k % 2 else kept
        to[k // 2, :, :1024] = total.astype(to.dtype)
        to[k // 2, :, 1024:] = rest[...].astype(to.dtype)


def plane_join_task(own, others, *parts):
    outs = shaped(((2, 32, 3072), f32), ((2, 32, 3072), bf16))
    return plane_join_kernel, [own, *others, *parts], outs


def line_total(ins, width):
    total = ins[0][:, :width]
    for other in ins[1:]:
        total = total + other[:, :width].astype(f32)
    return total


def rows_out_kernel(ids, ins, outs):
    y, y_low, dx, dx_low = ins
    matrix = order_matrix(ids[0], True)
    outs[0][...] = ordered(y[...], matrix)
    outs[1][...] = ordered(dx[...], matrix)
    outs[2][0:256, :] = y_low[...]
    outs[2][256:, :] = dx_low[...]


def rows_out_task(y, y_low, dx, dx_low):
    outs = shaped((y.shape, f32), (dx.shape, f32), (ROWS2, bf16))
    return rows_out_kernel, [y, y_low, dx, dx_low], outs


def rows_kernel(ids, ins, outs):
    y, dx, others = ins
    moved = ordered(others[...], order_matrix(ids[0], True))
    for at, (out, own) in enumerate(zip(outs, (y, dx))):
        out[ids[1]] = own[...]
        out[1 - ids[1]] = moved[256 * at : 256 * (at + 1), :]


def rows_task(y, dx, others):
    return rows_kernel, [y, dx, others], shaped(*[((2, 256, 512), f32)] * 2)


def code_near_kernel(ids, ins, outs):
    keep, other = ins
    for at, out in enumerate(outs):
        for i in range(2):
            out[:, 1536 * i : 1536 * (i + 1)] = code_sum(keep[2 * at + i], other[2 * at + i])


def code_near_task(keep, other):
    return code_near_kernel, [keep, other], shaped(*[((32, 3072), bf16)] * 2)


def code_add_kernel(ids, ins, outs):
    outs[0][...] = code_sum(ins[0][...], ins[1][...])


def code_turn_kernel(ids, ins, outs):
    outs[0][...] = code_sum(ins[0][...], swapped(ins[1][...]))


def code_turn_task(a, b):
    return code_turn_kernel, [a, b], shaped((a.shape, bf16))


def code_add_task(a, b):
    return code_add_kernel, [a, b], shaped((a.shape, bf16))


def code_pair_kernel(ids, ins, outs):
    for at, part in enumerate(ins):
        outs[0][:, 3072 * at : 3072 * (at + 1)] = part[...]


def code_pair_task(a, b):
    return code_pair_kernel, [a, b], shaped(((32, 6144), bf16))


def finish_kernel(ids, ins, outs):
    mlp, attn, dec, code, code_other = ins[:2], ins[2:4], ins[4:6], *ins[6:]
    qkv, out_t, up, down_t, book, vq_in, vq_out, gains, biases, dec_biases, small_ref = outs
    both = line_total(dec, 3072)
    for layer, rows in enumerate((line_total(mlp, 2048), both[:, 1024:])):
        up[layer] = rows[:, :1024]
        down_t[layer] = rows[:, 1024:]
    for layer, rows in enumerate((line_total(attn, 1024), both[:, :1024])):
        for index in range(3):
            qkv[layer, index] = rows[:, index * 256 : (index + 1) * 256]
        out_t[layer] = rows[:, 768:]
    core, z = ids[0] % 2, ids[0] // 4
    for at, parts in ((core, code), (1 - core, code_other)):
        for k in range(4):
            part = at * 4 + (z ^ k)
            held = parts[:, 1536 * k : 1536 * (k + 1)].astype(f32)
            book[:, pl.ds(pl.multiple_of(part * 1024, 1024), 1024)] = held[:, :1024]
            small_ref[:, pl.ds(pl.multiple_of(part * 256, 256), 256)] = (
                held[:, 1024:1280] + held[:, 1280:1536]
            )
    small = small_ref[...]
    vq_in[...] = small[:, :512]
    vq_out[...] = small[:, 512:1024]
    rest = small[:, 1024:1536]
    packed = attn[0][0:16, 1024:] + joined(attn[1])
    for row, out in enumerate((gains.at[0:1], biases.at[0:1], gains.at[1:2], biases.at[1:2])):
        for j in range(4):
            out[:, 128 * j : 128 * (j + 1)] = packed[row * 4 + j : row * 4 + j + 1, :]
    gains[2:3, :] = rest[0:1, :]
    biases[2:3, :] = rest[1:2, :]
    gains[3:4, :] = rest[2:3, :]
    dec_biases[0:1, :] = rest[3:4, :]
    gains[4:5, :] = rest[4:5, :]
    dec_biases[1:2, :] = rest[5:6, :]


def finish_task(own_m, other_m, own_a, other_a, own_d, other_d, code, code_other):
    outs = shaped(
        ((2, 3, 32, 256), f32),
        ((2, 32, 256), f32),
        ((2, 32, 1024), f32),
        ((2, 32, 1024), f32),
        ((32, 8192), f32),
        ((32, 512), f32),
        ((32, 512), f32),
        ((5, 512), f32),
        ((3, 512), f32),
        ((2, 512), f32),
        ((32, 2048), f32),
    )
    ins = [own_m, other_m, own_a, other_a, own_d, other_d, code, code_other]
    return finish_kernel, ins, outs


def run_tasks(ids, name, tasks, after=(), carry=()):
    sizes = [(len(ins), len(outs)) for _, ins, outs in tasks]
    n_in = sum(i for i, _ in sizes)

    def kernel(ids_ref, *refs):
        at_in, at_out = 0, n_in
        for (fn, _, _), (i, o) in zip(tasks, sizes):
            fn(ids_ref, refs[at_in : at_in + i], refs[at_out : at_out + o])
            at_in, at_out = at_in + i, at_out + o

    outs = [one for _, _, many in tasks for one in many]
    res = call(
        kernel, name, [SMEM] + [VMEM] * n_in, [VMEM] * len(outs), outs, [], 10**9, after, carry
    )(ids, *[one for _, many, _ in tasks for one in many])
    split, at = [], 0
    for _, o in sizes:
        split.append(res[at : at + o])
        at += o
    return (*split, res[-1])


def whole_groups(
    n_dp,
    tokens,
    segment_ids,
    norm_gains,
    norm_biases,
    w_qkv,
    w_attn_out,
    w_up,
    w_down,
    w_vq_in,
    w_vq_out,
    codebook,
    cotangent,
):
    dp_at, tp_at = lax.axis_index("dp"), lax.axis_index("tp")
    ids = jnp.stack([dp_at, tp_at]).astype(jnp.int32)

    def swap(values):
        return exchange(values, 0, 1, n_dp)

    def core(values):
        return [values, exchange(values, 1, 0, n_dp)]

    book_t = codebook.T
    enc_shard, dec_shard = pack_weights(
        w_qkv, w_attn_out.transpose(0, 2, 1), w_up, w_down.transpose(0, 2, 1)
    )
    enc_shards = spread_line(enc_shard, n_dp)
    own, send, norms, vq_w = rows_in(
        ids,
        tokens,
        segment_ids,
        cotangent,
        norm_gains,
        norm_biases,
        w_vq_in.T,
        w_vq_out,
    )
    marked = [own, swap(send)]

    line_a, line_b, (dec_shard,) = stack_lines(enc_shards, [1536] * 2, carry=[dec_shard])
    along_x, along_y = exchange(line_a, 0, 1, n_dp), exchange(line_b, 2, 0, n_dp)
    dec_shards = spread_line(dec_shard, n_dp)
    stack, stack_t, _ = code_prep(book_t, [line_a])
    codes = (stack, stack_t, book_t)
    a_0, b_0, _ = stack_pairs([(line_a, along_x), (line_b, along_y)], [stack_t, marked[1]])
    a_1, b_1 = exchange(a_0, 2, 0, n_dp), exchange(b_0, 0, 1, n_dp)
    line_a, line_b, (a_0, b_0) = stack_lines(dec_shards, [1536] * 2, [a_1, b_1], [a_0, b_0])
    enc_w = [a_0, a_1, exchange(a_0, 1, 0, n_dp), exchange(a_1, 1, 0, n_dp)]
    enc_w += [b_0, b_1, exchange(b_0, 1, 0, n_dp), exchange(b_1, 1, 0, n_dp)]
    along_x, along_y = exchange(line_a, 0, 1, n_dp), exchange(line_b, 2, 0, n_dp)
    e_x1, e_saved, _ = attn_fwd(0, marked, [], norms, enc_w)
    a_0, b_0, _ = stack_pairs([(line_a, along_x), (line_b, along_y)], [e_x1])
    a_1, b_1 = exchange(a_0, 2, 0, n_dp), exchange(b_0, 0, 1, n_dp)
    dec_w = [a_0, exchange(a_0, 1, 0, n_dp), b_0, exchange(b_0, 1, 0, n_dp)]
    e, u, kept, _ = mlp_vq(e_x1, norms, vq_w, stack, stack_t, enc_w, [a_0, b_0])
    a_1, b_1 = gate([u], [a_1, b_1])
    a_1, b_1 = core(a_1), core(b_1)
    dec_w = [dec_w[0], a_1[0], dec_w[1], a_1[1], dec_w[2], b_1[0], dec_w[3], b_1[1]]
    d_x1, d_saved, _ = attn_fwd(3, marked, [u], norms, dec_w)

    dx1, d_small1, keep_m, send_m, _ = mlp_bwd(
        4, ids, d_x1, [cotangent, marked[1]], norms, dec_w
    )
    near_m = exchange(send_m, 1, 0, n_dp)
    du, d_small0, keep_a, send_a, (keep_m,) = attn_bwd(
        3, marked, u, dx1, norms, d_saved, dec_w, carry=[keep_m]
    )
    (own_m, *lows_m), (send_a,) = run_tasks(
        ids, "sums1", [near_task(keep_m, near_m)], carry=[send_a]
    )
    plane_m, near_a = plane_send(lows_m, n_dp), exchange(send_a, 1, 0, n_dp)
    de, code, code_send, (own_m, keep_a) = vq_bwd(
        ids,
        e,
        du,
        norms,
        vq_w,
        codes,
        kept,
        [d_small0, d_small1],
        lows_m,
        [own_m, keep_a],
    )
    d_mlp, (own_a, *lows_a), (code, code_send) = run_tasks(
        ids,
        "sums2",
        [plane_task(own_m, plane_m), near_task(keep_a, near_a)],
        carry=[code, code_send],
    )
    plane_a, code_other = plane_send(lows_a, n_dp), exchange(code_send, 1, 0, n_dp)
    (code, code_send), _ = run_tasks(ids, "sums2b", [code_near_task(code, code_other)])
    code_other = exchange(code_send, 8, 0, n_dp)
    ex1, e_small1, keep_m, send_m, (own_a, code) = mlp_bwd(
        1, ids, e_x1, [de], norms, enc_w, [*lows_a, code_send], [own_a, code]
    )
    (own_d, send_d), (code,), (keep_m, send_m) = run_tasks(
        ids,
        "sums3",
        [plane_join_task(own_a, plane_a, *d_mlp), code_add_task(code, code_other)],
        carry=[keep_m, send_m],
    )
    near_m, code_other = exchange(send_m, 1, 0, n_dp), exchange(code, 2, 0, n_dp)
    other_d = exchange(send_d, 4, 0, n_dp)
    *parts, _ = heads_bwd(marked, ex1, e_saved, enc_w, [send_d, code])
    (own_up, to_x, own_down, to_y, code), (own_d, send_d), _ = run_tasks(
        ids,
        "sums3b",
        [fork_task(keep_m, near_m, code, code_other), line_step_task(own_d, other_d)],
        [parts[0]],
    )
    from_x, from_y = exchange(to_x, 0, 1, n_dp), exchange(to_y, 2, 0, n_dp)
    other_d = exchange(send_d, 8, 0, n_dp)
    dx, dx_low, y, y_low, keep_a, send_a, (own_up, own_down, code, own_d) = rows_bwd(
        ids,
        marked,
        ex1,
        norms,
        parts,
        e_small1,
        d_x1,
        enc_w,
        dec_w,
        [to_x, to_y],
        [own_up, own_down, code, own_d],
    )
    (own_up, to_y, own_down, to_x, code), (keep_a, send_a) = run_tasks(
        ids,
        "sums4",
        [half_task(own_up, from_x, own_down, from_y, code)],
        [other_d],
        [keep_a, send_a],
    )
    near_a, code_other = exchange(send_a, 1, 0, n_dp), exchange(code, 4, 0, n_dp)
    from_y, from_x = exchange(to_y, 2, 0, n_dp), exchange(to_x, 0, 1, n_dp)
    (own_a, *lows_a), (code,), (own_up, own_down) = run_tasks(
        ids,
        "sums4b",
        [near_task(keep_a, near_a), code_turn_task(code, code_other)],
        carry=[own_up, own_down],
    )
    plane_a = plane_send(lows_a, n_dp)
    (own_m, send_m), (own_a, code) = run_tasks(
        ids, "sums5", [join_task(own_up, from_y, own_down, from_x)], lows_a, [own_a, code]
    )
    other_m, code_other = exchange(send_m, 4, 0, n_dp), exchange(code, 8, 0, n_dp)
    (y, dx, rows), (own_a,) = run_tasks(
        ids, "rows_out", [rows_out_task(y, y_low, dx, dx_low)], [send_m, code], [own_a]
    )
    (own_a, send_a), (own_m, send_m), (code,), (rows,) = run_tasks(
        ids,
        "sums6",
        [
            plane_line_task(own_a, plane_a),
            line_step_task(own_m, other_m),
            code_pair_task(code, code_other),
        ],
        carry=[rows],
    )
    other_a, other_m = exchange(send_a, 4, 0, n_dp), exchange(send_m, 8, 0, n_dp)
    code_other, rows = exchange(code, 1, 0, n_dp), swap(rows)
    (own_a, send_a), _ = run_tasks(ids, "sums7", [small_step_task(own_a, other_a)])
    other_a = exchange(send_a, 8, 0, n_dp)
    (qkv, out_t, up, down_t, book, vq_in, vq_out, *norm_grads, _), (decoded, grad_tokens), _ = (
        run_tasks(
            ids,
            "finish",
            [
                finish_task(own_m, other_m, own_a, other_a, own_d, other_d, code, code_other),
                rows_task(y, dx, rows),
            ],
        )
    )
    return (
        decoded,
        grad_tokens,
        *norm_grads,
        qkv,
        out_t.transpose(0, 2, 1),
        up,
        down_t.transpose(0, 2, 1),
        vq_in.T,
        vq_out,
        book.T,
    )


def layer_norm(values, norm_gain, norm_bias):
    centred = values - jnp.mean(values, axis=-1, keepdims=True)
    spread = jnp.mean(centred * centred, axis=-1, keepdims=True)
    return centred * lax.rsqrt(spread + ln_eps) * norm_gain + norm_bias


def gelu_tanh(values):
    return (
        0.5 * values * (1.0 + jnp.tanh(gelu_coef * (values + 0.044715 * values * values * values)))
    )


def matmul(former, latter):
    return jnp.dot(former, latter, precision=highest, preferred_element_type=jnp.float32)


def normalize(values):
    return values * lax.rsqrt(jnp.sum(values * values, axis=-1, keepdims=True) + norm_eps)


def quantize(in_rows, norm_gain, norm_bias, in_w, out_w, code_w):
    latent = normalize(matmul(layer_norm(in_rows, norm_gain, norm_bias), in_w))
    code_rows = normalize(code_w)
    logits = matmul(latent, code_rows.T) * temper
    row_max = jnp.max(logits, axis=-1, keepdims=True)
    numerator = jnp.exp(logits - row_max)
    assign = numerator / jnp.sum(numerator, axis=-1, keepdims=True)
    soft_code = matmul(assign, code_rows)
    offset = latent - soft_code
    vq_loss = commit_weight * 1.25 * jnp.sum(offset * offset)
    return (matmul(soft_code, out_w), vq_loss)


def product(former, latter):
    return jnp.dot(former, latter, preferred_element_type=jnp.float32)


def product_tn(former, latter):
    return lax.dot_general(
        former, latter, (((0,), (0,)), ((), ())), preferred_element_type=jnp.float32
    )


def product_nt(former, latter):
    return lax.dot_general(
        former, latter, (((1,), (1,)), ((), ())), preferred_element_type=jnp.float32
    )


def split_heads(values):
    return values.reshape(values.shape[0], values.shape[1] // HEAD_DIM, HEAD_DIM).transpose(1, 0, 2)


def join_heads(values):
    return values.transpose(1, 0, 2).reshape(values.shape[1], values.shape[0] * HEAD_DIM)


def masked_scores(query_blk, key_h, seg_blk, seg_keys):
    scores = jnp.einsum(
        "hqd,hkd->hqk", query_blk, key_h, preferred_element_type=jnp.float32
    ) * HEAD_DIM ** (-0.5)
    return jnp.where((seg_blk[:, None] == seg_keys[None, :])[None], scores, masked_score)


def attend(query_h, key_h, value_h, seg_keys):
    block_rows = min(512, query_h.shape[1])
    block_count = query_h.shape[1] // block_rows

    def one_block(begin_row):
        query_blk = lax.dynamic_slice_in_dim(query_h, begin_row, block_rows, 1)
        seg_blk = lax.dynamic_slice_in_dim(seg_keys, begin_row, block_rows, 0)
        scores = masked_scores(query_blk, key_h, seg_blk, seg_keys)
        row_max = jnp.max(scores, axis=-1, keepdims=True)
        numerator = jnp.exp(scores - row_max)
        row_total = jnp.sum(numerator, axis=-1, keepdims=True)
        prob_low = (numerator / row_total).astype(jnp.bfloat16)
        attended = jnp.einsum("hqk,hkd->hqd", prob_low, value_h, preferred_element_type=jnp.float32)
        return (attended.astype(jnp.bfloat16), (row_max + jnp.log(row_total))[..., 0])

    starts = jnp.arange(block_count, dtype=jnp.int32) * block_rows
    attended, log_sums = lax.map(one_block, starts)
    heads_out = attended.transpose(1, 0, 2, 3).reshape(query_h.shape)
    log_sums = log_sums.transpose(1, 0, 2).reshape(query_h.shape[0], query_h.shape[1])
    return (heads_out, log_sums)


def attend_back(query_h, key_h, value_h, seg_keys, log_sums, grad_out):
    block_rows = min(512, query_h.shape[1])
    block_count = query_h.shape[1] // block_rows

    def one_block(carry, begin_row):
        grad_key, grad_value = carry
        query_blk = lax.dynamic_slice_in_dim(query_h, begin_row, block_rows, 1)
        grad_blk = lax.dynamic_slice_in_dim(grad_out, begin_row, block_rows, 1)
        lse_blk = lax.dynamic_slice_in_dim(log_sums, begin_row, block_rows, 1)
        seg_blk = lax.dynamic_slice_in_dim(seg_keys, begin_row, block_rows, 0)
        scores = masked_scores(query_blk, key_h, seg_blk, seg_keys)
        probs = jnp.exp(scores - lse_blk[..., None])
        prob_low = probs.astype(jnp.bfloat16)
        grad_value = grad_value + jnp.einsum(
            "hqk,hqd->hkd", prob_low, grad_blk, preferred_element_type=jnp.float32
        )
        grad_prob = jnp.einsum(
            "hqd,hkd->hqk", grad_blk, value_h, preferred_element_type=jnp.float32
        )
        row_dot = jnp.sum(probs * grad_prob, axis=-1, keepdims=True)
        grad_score = (probs * (grad_prob - row_dot) * HEAD_DIM ** (-0.5)).astype(jnp.bfloat16)
        grad_query = jnp.einsum(
            "hqk,hkd->hqd", grad_score, key_h, preferred_element_type=jnp.float32
        )
        grad_key = grad_key + jnp.einsum(
            "hqk,hqd->hkd", grad_score, query_blk, preferred_element_type=jnp.float32
        )
        return ((grad_key, grad_value), grad_query)

    starts = jnp.arange(block_count, dtype=jnp.int32) * block_rows
    zeros_kv = jnp.zeros(key_h.shape, jnp.float32)
    (grad_key, grad_value), grad_query = lax.scan(one_block, (zeros_kv, zeros_kv), starts)
    grad_query = grad_query.transpose(1, 0, 2, 3).reshape(query_h.shape)
    return (
        grad_query.astype(jnp.bfloat16),
        grad_key.astype(jnp.bfloat16),
        grad_value.astype(jnp.bfloat16),
    )


def spread_rows(values):
    return lax.all_gather(values, "tp", axis=0, tiled=True)


def combine_rows(partial_value):
    return lax.psum_scatter(partial_value, "tp", scatter_dimension=0, tiled=True)


def spread_grads(values):
    return lax.all_gather(values, "tp", axis=0, tiled=True)


def combine_grads(partial_value):
    return lax.psum_scatter(
        partial_value.astype(jnp.bfloat16), "tp", scatter_dimension=0, tiled=True
    ).astype(jnp.float32)


def fetch_weights(w_qkv, w_attn_out, w_up, w_down, layer):
    return (
        lax.all_gather(w_qkv[layer], "dp", axis=1, tiled=True),
        lax.all_gather(w_attn_out[layer], "dp", axis=1, tiled=True),
        lax.all_gather(w_up[layer], "dp", axis=0, tiled=True),
        lax.all_gather(w_down[layer], "dp", axis=1, tiled=True),
    )


def reduce_weight_grads(grads):
    return (
        lax.psum_scatter(
            grads[0].astype(jnp.bfloat16), "dp", scatter_dimension=1, tiled=True
        ).astype(jnp.float32),
        lax.psum_scatter(
            grads[1].astype(jnp.bfloat16), "dp", scatter_dimension=1, tiled=True
        ).astype(jnp.float32),
        lax.psum_scatter(
            grads[2].astype(jnp.bfloat16), "dp", scatter_dimension=0, tiled=True
        ).astype(jnp.float32),
        lax.psum_scatter(
            grads[3].astype(jnp.bfloat16), "dp", scatter_dimension=1, tiled=True
        ).astype(jnp.float32),
    )


def block_forward(resid_in, seg_local, gains, biases, weights):
    qkv_w, attn_w, up_w, down_w = weights
    normed = layer_norm(resid_in, gains[0], biases[0]).astype(jnp.bfloat16)
    normed_all, seg_all = (
        lax.all_gather(normed, "tp", axis=0, tiled=True),
        lax.all_gather(seg_local, "tp", axis=0, tiled=True),
    )
    query_h = split_heads(product(normed_all, qkv_w[0]).astype(jnp.bfloat16))
    key_h = split_heads(product(normed_all, qkv_w[1]).astype(jnp.bfloat16))
    value_h = split_heads(product(normed_all, qkv_w[2]).astype(jnp.bfloat16))
    heads_out, log_sums = attend(query_h, key_h, value_h, seg_all)
    attn_rows = join_heads(heads_out)
    middle = resid_in + combine_rows(product(attn_rows, attn_w))
    normed_mid = spread_rows(layer_norm(middle, gains[1], biases[1]).astype(jnp.bfloat16))
    hidden_pre = product(normed_mid, up_w)
    hidden = gelu_tanh(hidden_pre).astype(jnp.bfloat16)
    result = middle + combine_rows(product(hidden, down_w))
    kept = (
        resid_in,
        middle,
        normed_all,
        seg_all,
        query_h,
        key_h,
        value_h,
        log_sums,
        attn_rows,
        normed_mid,
        hidden_pre,
        hidden,
    )
    return (result, kept)


def block_backward(kept, gains, biases, weights, grad_result):
    (
        resid_in,
        middle,
        normed_all,
        seg_all,
        query_h,
        key_h,
        value_h,
        log_sums,
        attn_rows,
        normed_mid,
        hidden_pre,
        hidden,
    ) = kept
    qkv_w, attn_w, up_w, down_w = weights
    grad_branch = spread_grads(grad_result.astype(jnp.bfloat16))
    grad_down = product_tn(hidden, grad_branch)
    grad_hidden = product_nt(grad_branch, down_w)
    _, gelu_back = jax.vjp(gelu_tanh, hidden_pre)
    grad_pre = gelu_back(grad_hidden)[0].astype(jnp.bfloat16)
    grad_up = product_tn(normed_mid, grad_pre)
    grad_norm_mid = combine_grads(product_nt(grad_pre, up_w))
    _, norm_back_mid = jax.vjp(layer_norm, middle, gains[1], biases[1])
    grad_mid_ln, grad_gain_mid, grad_bias_mid = norm_back_mid(grad_norm_mid)
    grad_middle = grad_result + grad_mid_ln
    grad_attn_all = spread_grads(grad_middle.astype(jnp.bfloat16))
    grad_attn = product_tn(attn_rows, grad_attn_all)
    grad_heads = split_heads(product_nt(grad_attn_all, attn_w).astype(jnp.bfloat16))
    grad_query, grad_key, grad_value = attend_back(
        query_h, key_h, value_h, seg_all, log_sums, grad_heads
    )
    grad_parts = [join_heads(grad_query), join_heads(grad_key), join_heads(grad_value)]
    grad_qkv = jnp.stack([product_tn(normed_all, grad_part) for grad_part in grad_parts])
    grad_normed_part = (
        product_nt(grad_parts[0], qkv_w[0])
        + product_nt(grad_parts[1], qkv_w[1])
        + product_nt(grad_parts[2], qkv_w[2])
    )
    grad_normed = combine_grads(grad_normed_part)
    _, norm_back_in = jax.vjp(layer_norm, resid_in, gains[0], biases[0])
    grad_in_ln, grad_gain_in, grad_bias_in = norm_back_in(grad_normed)
    gain_grads = jnp.stack([grad_gain_in, grad_gain_mid])
    bias_grads = jnp.stack([grad_bias_in, grad_bias_mid])
    return (
        grad_middle + grad_in_ln,
        gain_grads,
        bias_grads,
        (grad_qkv, grad_attn, grad_up, grad_down),
    )


def local(
    tokens,
    segment_ids,
    norm_gains,
    norm_biases,
    w_qkv,
    w_attn_out,
    w_up,
    w_down,
    w_vq_in,
    w_vq_out,
    codebook,
    cotangent,
):
    gain_sum = jnp.zeros(norm_gains.shape, jnp.float32)
    bias_sum = jnp.zeros(norm_biases.shape, jnp.float32)
    vq_in_sum = jnp.zeros(w_vq_in.shape, jnp.float32)
    vq_out_sum = jnp.zeros(w_vq_out.shape, jnp.float32)
    code_sum = jnp.zeros(codebook.shape, jnp.float32)
    layer_sums = [None, None]
    outputs = []
    input_grads = []
    for micro in range(MICRO):
        resid_in = tokens[micro].astype(jnp.float32)
        seg_local = segment_ids[micro]
        enc_weights = fetch_weights(w_qkv, w_attn_out, w_up, w_down, 0)
        encoded, enc_kept = block_forward(
            resid_in, seg_local, norm_gains[0:2], norm_biases[0:2], enc_weights
        )
        (decoder_in, _), vq_back = jax.vjp(
            quantize, encoded, norm_gains[2], norm_biases[2], w_vq_in, w_vq_out, codebook
        )
        dec_weights = fetch_weights(w_qkv, w_attn_out, w_up, w_down, 1)
        decoded, dec_kept = block_forward(
            decoder_in, seg_local, norm_gains[3:5], norm_biases[3:5], dec_weights
        )
        outputs.append(decoded)
        grad_dec_in, gains_dec, biases_dec, grads_dec = block_backward(
            dec_kept, norm_gains[3:5], norm_biases[3:5], dec_weights, cotangent[micro]
        )
        grad_encoded, grad_gain_vq, grad_bias_vq, grad_in_w, grad_out_w, grad_codes = vq_back(
            (grad_dec_in, jnp.ones((), jnp.float32))
        )
        grad_input, gains_enc, biases_enc, grads_enc = block_backward(
            enc_kept, norm_gains[0:2], norm_biases[0:2], enc_weights, grad_encoded
        )
        input_grads.append(grad_input)
        gain_sum = gain_sum + jnp.concatenate([gains_enc, grad_gain_vq[None], gains_dec], axis=0)
        bias_sum = bias_sum + jnp.concatenate([biases_enc, grad_bias_vq[None], biases_dec], axis=0)
        vq_in_sum = vq_in_sum + grad_in_w
        vq_out_sum = vq_out_sum + grad_out_w
        code_sum = code_sum + grad_codes
        for layer, grads in ((0, grads_enc), (1, grads_dec)):
            reduced = reduce_weight_grads(grads)
            if layer_sums[layer] is None:
                layer_sums[layer] = reduced
            else:
                layer_sums[layer] = jax.tree.map(jnp.add, layer_sums[layer], reduced)
    gain_tot, bias_tot, vq_in_tot, vq_out_tot, code_tot = lax.psum(
        (gain_sum, bias_sum, vq_in_sum, vq_out_sum, code_sum), ("dp", "tp")
    )
    return (
        jnp.stack(outputs),
        jnp.stack(input_grads),
        gain_tot,
        bias_tot[0:3],
        bias_tot[3:5],
        jnp.stack([layer_sums[0][0], layer_sums[1][0]]),
        jnp.stack([layer_sums[0][1], layer_sums[1][1]]),
        jnp.stack([layer_sums[0][2], layer_sums[1][2]]),
        jnp.stack([layer_sums[0][3], layer_sums[1][3]]),
        vq_in_tot,
        vq_out_tot,
        code_tot,
    )


def solution(mesh):
    n_dp, n_tp = mesh.shape["dp"], mesh.shape["tp"]
    fits = n_tp == MICRO and n_dp == 16
    return jax.shard_map(
        functools.partial(whole_groups, n_dp) if fits else local,
        mesh=mesh,
        in_specs=(
            P(None, ("dp", "tp"), None),
            P(None, ("dp", "tp")),
            P(),
            P(),
            P(None, None, "dp", "tp"),
            P(None, "tp", "dp"),
            P(None, "dp", "tp"),
            P(None, "tp", "dp"),
            P(),
            P(),
            P(),
            P(None, ("dp", "tp"), None),
        ),
        out_specs=(
            P(None, ("dp", "tp"), None),
            P(None, ("dp", "tp"), None),
            P(),
            P(),
            P(),
            P(None, None, "dp", "tp"),
            P(None, "tp", "dp"),
            P(None, "dp", "tp"),
            P(None, "tp", "dp"),
            P(),
            P(),
            P(),
        ),
        check_vma=False,
    )
```

```python
import functools

import jax
import jax.numpy as jnp
from jax import lax
from jax.experimental import pallas as pl
from jax.experimental.pallas import tpu as pltpu
from jax.sharding import PartitionSpec as P

HEAD_DIM = 64
MICRO = 2
bf16 = jnp.bfloat16
f32 = jnp.float32
highest = lax.Precision.HIGHEST
ln_eps = 1e-05
norm_eps = 1e-06
temper = 10.0
commit_weight = 64.0
gelu_coef = 0.7978845608028654
masked_score = -1e30
log2e = 1.4426950408889634
vmem_cap = 26 * 1024 * 1024


PLANE = ((0, 0), (0, 1), (1, 0), (1, 1))


def exchange(values, dp_xor, tp_xor, n_dp):
    pairs = [
        (d * 2 + t, (d ^ dp_xor) * 2 + (t ^ tp_xor)) for d in range(n_dp) for t in range(2)
    ]
    return lax.ppermute(values, ("dp", "tp"), pairs)


def spread_line(shard, n_dp):
    return [shard] + [exchange(shard, 4 * k, 0, n_dp) for k in range(1, 4)]


def plane_send(lows, n_dp):
    return [exchange(low, 2 * y, x, n_dp) for (y, x), low in zip(PLANE[1:], lows)]


def line_send(lows, n_dp):
    return [exchange(low, 4 * k, 0, n_dp) for k, low in zip(range(1, 4), lows)]


def dot(a, b):
    return jnp.dot(a, b, preferred_element_type=f32)


def dot_nt(a, b, precision=None):
    return lax.dot_general(
        a, b, (((1,), (1,)), ((), ())), preferred_element_type=f32, precision=precision
    )


def dot_full(a, b):
    return jnp.dot(a, b, preferred_element_type=f32, precision=highest)


def ln_parts(x):
    centred = x - jnp.mean(x, axis=-1, keepdims=True)
    inv = lax.rsqrt(jnp.mean(centred * centred, axis=-1, keepdims=True) + ln_eps)
    return centred * inv, inv


def ln_back(grad, xhat, inv, gain):
    scaled = grad * gain
    return inv * (
        scaled
        - jnp.mean(scaled, axis=-1, keepdims=True)
        - xhat * jnp.mean(scaled * xhat, axis=-1, keepdims=True)
    )


def split2(x):
    hi = x.astype(bf16)
    return hi, (x - hi.astype(f32)).astype(bf16)


def split3(x):
    hi, _ = split2(x)
    rest = x - hi.astype(f32)
    mid = rest.astype(bf16)
    return hi, mid, (rest - mid.astype(f32)).astype(bf16)


def order_matrix(dp, inverse):
    at = lax.broadcasted_iota(jnp.int32, (512, 512), 0 if inverse else 1)
    other = lax.broadcasted_iota(jnp.int32, (512, 512), 1 if inverse else 0)
    block = at >> 5
    bits = ((block & 3) << 2) | (((block >> 2) & 1) << 1) | (block >> 3)
    return jnp.where(other == (((dp ^ bits) << 5) | (at & 31)), 1.0, 0.0).astype(bf16)


def ordered(x, matrix):
    if x.dtype == bf16:
        return dot(x, matrix)
    hi, mid, lo = split3(x)
    return (dot(hi, matrix) + dot(mid, matrix)) + dot(lo, matrix)


def w_at(a, b, t, first, width):
    parts = []
    for core in range(2):
        for y in range(2):
            if first < 1536:
                part = a[2 * core + y][t, :, :, first : first + width]
            else:
                part = b[2 * core + t][y, :, :, first - 1536 : first - 1536 + width]
            parts.append(part.reshape(128, width))
    return jnp.concatenate(parts, axis=0)


def put_grad(refs, t, cols, value):
    for core, ref in enumerate(refs):
        for y in range(2):
            rows = value[core * 256 + y * 128 : core * 256 + (y + 1) * 128]
            ref[2 * y + t, :, :, cols] = rows.reshape(4, 32, rows.shape[1])


def start_all(copies):
    for copy in copies:
        copy.start()


def wait_all(copies):
    for copy in copies:
        copy.wait()


def head_rows(ref, pair, which):
    own = ref[pl.ds(pair * 128 + which * HEAD_DIM, HEAD_DIM), :]
    zero = jnp.zeros_like(own)
    return jnp.concatenate([own, zero] if which == 0 else [zero, own], axis=0)


def segment_mask(own, other):
    ids = jnp.concatenate([own[:, 512:640], other[:, 512:640]], axis=0).astype(f32)
    return jnp.where(ids[:, 0:1] == ids.T[0:1, :], 0.0, masked_score)


def load_rows(x, own, other):
    if x is None:
        return jnp.concatenate([own[:, :512], other[:, :512]], axis=0).astype(f32)
    return x[...]


def gain_of(norms, at):
    return norms[at : at + 1, :]


def bias_of(norms, at):
    return norms[8 + at : 9 + at, :]


def attn_fwd_kernel(with_x, at, own, other, norms, *refs):
    w, refs = refs[:4], refs[4:]
    x, refs = (refs[0], refs[1:]) if with_x else (None, refs)
    x1, lse, saved, refs = refs[0], refs[1], refs[2:8], refs[8:]
    h, vt, ot, mask, qs, k, v, o, qst, kt, out_sems = refs
    keeps = [
        pltpu.make_async_copy(held, to, out_sems.at[i])
        for i, (held, to) in enumerate(zip((qs, k, v, o, qst, kt), saved))
    ]
    xf = load_rows(x, own, other)
    h[...] = (ln_parts(xf)[0] * gain_of(norms, at) + bias_of(norms, at)).astype(bf16)
    mask[...] = segment_mask(own, other)
    for t in range(2):
        cols = slice(t * 256, (t + 1) * 256)
        q = dot(h[...], w_at(w, None, t, 0, 256)).astype(bf16)
        qs[:, cols] = (q * HEAD_DIM ** (-0.5)).astype(bf16)
        k[:, cols] = dot(h[...], w_at(w, None, t, 256, 256)).astype(bf16)
        v[:, cols] = dot(h[...], w_at(w, None, t, 512, 256)).astype(bf16)
    qst[...] = qs[...].T
    kt[...] = k[...].T
    vt[...] = v[...].T
    for i in (0, 1, 2, 4, 5):
        keeps[i].start()
    for pair in range(4):
        k_pair = k[:, pair * 128 : (pair + 1) * 128]
        for which in range(2):
            scores = dot(k_pair, head_rows(qst, pair, which)) + mask[...]
            top = jnp.max(scores, axis=0, keepdims=True)
            numer = jnp.exp(scores - top).astype(bf16)
            rows = pl.ds(pair * 128 + which * HEAD_DIM, HEAD_DIM)
            left = jnp.concatenate([vt[rows, :], jnp.ones((16, 512), bf16)], axis=0)
            both = dot(left, numer)
            total = both[HEAD_DIM : HEAD_DIM + 1, :]
            ot[rows, :] = (both[:HEAD_DIM, :] / total).astype(bf16)
            lse[pl.ds(pair * 2 + which, 1), :] = top + jnp.log(total)
    o[...] = ot[...].T
    keeps[3].start()
    acc = xf
    for t in range(2):
        acc = acc + dot_nt(o[:, t * 256 : (t + 1) * 256], w_at(w, None, t, 768, 256))
    x1[...] = acc
    wait_all(keeps)


def gelu_parts(u):
    square = u * u
    tanh = jnp.tanh(gelu_coef * u * (1.0 + 0.044715 * square))
    return 0.5 * u * (1.0 + tanh), tanh, square


def mlp_weights(w):
    def up(t, part):
        return w_at(w[:4], w[4:], t, 1024 + part * 512, 512)

    def down(t, part):
        return w_at(w[:4], w[4:], t, 2048 + part * 512, 512)

    return up, down


def mlp_rows(at, x, norms, w, h2):
    up, down = mlp_weights(w)
    h2[...] = (ln_parts(x)[0] * gain_of(norms, at) + bias_of(norms, at)).astype(bf16)
    for t in range(2):
        for part in range(2):
            hidden = gelu_parts(dot(h2[...], up(t, part)))[0].astype(bf16)
            x = x + dot_nt(hidden, down(t, part))
    return x


def mlp_bwd_kernel(split, at, ids, x1, norms, *refs):
    up, down = mlp_weights(refs[:8])
    refs = refs[8:]
    if split:
        own, other, refs = refs[0], refs[1], refs[2:]
    else:
        dy, refs = refs[0], refs[1:]
    dx1, small, grads = refs[0], refs[1], refs[2:4]
    h2, h2t, dyb, dybt, dh2 = refs[4:9]
    if split:
        dy = refs[9]
        dy[0:256, :] = ordered(own[ids[1]], order_matrix(ids[0], False))
        dy[256:, :] = other[:, 640:].astype(f32)
    h2[...] = (ln_parts(x1[...])[0] * gain_of(norms, at) + bias_of(norms, at)).astype(bf16)
    h2t[...] = h2[...].T
    dyb[...] = dy[...].astype(bf16)
    dybt[...] = dyb[...].T
    for t in range(2):
        for part in range(2):
            cols = slice(part * 512, (part + 1) * 512)
            w_up = up(t, part)
            pre = dot(h2[...], w_up)
            hidden, tanh, square = gelu_parts(pre)
            slope = 0.5 * (1.0 + tanh) + (0.5 * gelu_coef) * pre * (1.0 - tanh * tanh) * (
                1.0 + (3 * 0.044715) * square
            )
            dhidden = dot(dyb[...], down(t, part))
            dpre = (dhidden * slope).astype(bf16)
            out_cols = slice(1024 + part * 512, 1024 + (part + 1) * 512)
            put_grad(grads, t, out_cols, dot(dybt[...], hidden.astype(bf16)).astype(bf16))
            put_grad(grads, t, cols, dot(h2t[...], dpre).astype(bf16))
            more = dot_nt(dpre, w_up)
            if t + part == 0:
                dh2[...] = more
            else:
                dh2[...] += more
    xhat, inv = ln_parts(x1[...])
    grad = dh2[...]
    small[0:1, :] = jnp.sum(grad * xhat, axis=0, keepdims=True)
    small[1:2, :] = jnp.sum(grad, axis=0, keepdims=True)
    dx1[...] = dy[...] + ln_back(grad, xhat, inv, gain_of(norms, at))


def heads_back(low, w, saved, lse, mask, put_out, scratch):
    qs, k, v, o, qst, kt = saved
    flip, do, dot_t, dqt, dq, dk, dv = scratch
    flip[...] = low.T
    for t in range(2):
        cols = slice(t * 256, (t + 1) * 256)
        do[:, cols] = dot(low, w_at(w, None, t, 768, 256)).astype(bf16)
        put_out(t, dot(flip[...], o[:, cols]).astype(bf16))
    dot_t[...] = do[...].T
    first = lax.broadcasted_iota(jnp.int32, (512, 128), 1) < HEAD_DIM
    for pair in range(4):
        lanes = slice(pair * 128, (pair + 1) * 128)
        dvs, dks = [], []
        for which in range(2):
            head = pair * 2 + which
            rows = pl.ds(head * HEAD_DIM, HEAD_DIM)
            scores = dot(k[:, lanes], head_rows(qst, pair, which)) + mask[...]
            probs = jnp.exp(scores - lse[head : head + 1, :])
            dprobs = dot(v[:, lanes], head_rows(dot_t, pair, which))
            shift = jnp.sum(probs * dprobs, axis=0, keepdims=True)
            dscore = (probs * (dprobs - shift)).astype(bf16)
            dvs.append(dot(probs.astype(bf16), do[:, lanes]))
            dks.append(dot(dscore, qs[:, lanes]))
            dqt[rows, :] = (dot(kt[rows, :], dscore) * HEAD_DIM ** (-0.5)).astype(bf16)
        dv[:, lanes] = jnp.where(first, dvs[0], dvs[1]).astype(bf16)
        dk[:, lanes] = jnp.where(first, dks[0], dks[1]).astype(bf16)
    dq[...] = dqt[...].T


def rows_back(at, xf, norms, w, parts, small, grads, h, flip):
    h[...] = (ln_parts(xf)[0] * gain_of(norms, at) + bias_of(norms, at)).astype(bf16)
    flip[...] = h[...].T
    grad = jnp.zeros((512, 512), f32)
    for t in range(2):
        cols = slice(t * 256, (t + 1) * 256)
        for index, part in enumerate(parts):
            w_cols = slice(index * 256, (index + 1) * 256)
            put_grad(grads, t, w_cols, dot(flip[...], part[:, cols]).astype(bf16))
            grad = grad + dot_nt(part[:, cols], w_at(w, None, t, index * 256, 256))
    xhat, inv = ln_parts(xf)
    small[0:1, :] = jnp.sum(grad * xhat, axis=0, keepdims=True)
    small[1:2, :] = jnp.sum(grad, axis=0, keepdims=True)
    return ln_back(grad, xhat, inv, gain_of(norms, at))


def take_saved(saved, held, sems):
    copies = [
        pltpu.make_async_copy(a, b, sems.at[i]) for i, (a, b) in enumerate(zip(saved, held))
    ]
    start_all(copies)
    return copies


def attn_bwd_kernel(at, own, other, dx1, norms, lse, *refs):
    w, saved, x, refs = refs[:4], refs[4:10], refs[10], refs[11:]
    dx, small, grads = refs[0], refs[1], refs[2:4]
    mask, h, held, scratch, sems = refs[4], refs[5], refs[6:12], refs[12:19], refs[19]
    copies = take_saved(saved, held, sems)
    mask[...] = segment_mask(own, other)
    low = dx1[...].astype(bf16)
    wait_all(copies)

    def put_out(t, value):
        put_grad(grads, t, slice(768, 1024), value)

    heads_back(low, w, held, lse, mask, put_out, scratch)
    dx[...] = dx1[...] + rows_back(
        at, x[...], norms, w, scratch[4:], small, grads, h, scratch[0]
    )


def heads_bwd_kernel(own, other, dx1, lse, *refs):
    w, saved, refs = refs[:4], refs[4:10], refs[10:]
    parts, grads, mask, held = refs[:3], refs[3:5], refs[5], refs[6:12]
    scratch, sems = (*refs[12:16], *parts), refs[16]
    copies = take_saved(saved, held, sems)
    mask[...] = segment_mask(own, other)
    low = dx1[...].astype(bf16)
    wait_all(copies)

    def put_out(t, value):
        put_grad(grads, t, slice(0, 256), value)

    heads_back(low, w, held, lse, mask, put_out, scratch)


def rows_bwd_kernel(
    ids, own, other, dx1, norms, dq, dk, dv, out_0, out_1, other_small, d_x1, *refs
):
    w, d_w, (dx, dx_low, y, y_low), grads, (small, h, flip) = (
        refs[:4],
        refs[4:12],
        refs[12:16],
        refs[16:18],
        refs[18:],
    )
    total = dx1[...] + rows_back(
        0, load_rows(None, own, other), norms, w, (dq, dk, dv), small, grads, h, flip
    )
    dx[...] = total[:256, :]
    dx_low[...] = total[256:, :].astype(bf16)
    rows = jnp.concatenate([small[0:2, :], other_small[0:2, :], jnp.zeros((4, 512), f32)], axis=0)
    packed = pack_rows(ordered(rows, order_matrix(ids[0], True)))
    for grad, part in zip(grads, (out_0, out_1)):
        for i in range(4):
            for z in range(4):
                grad[i, z, :, 768:1024] = part[i, z]
                grad[i, z, :, 1024:1152] = packed
    rows = mlp_rows(4, d_x1[...], norms, d_w, h)
    y[...] = rows[:256, :]
    y_low[...] = rows[256:, :].astype(bf16)


def pack_rows(rows):
    cut = [rows[i : i + 1, 128 * j : 128 * (j + 1)] for i in range(4) for j in range(4)]
    return jnp.concatenate(split2(jnp.concatenate(cut, axis=0)), axis=0)


def code_prep_kernel(book_t, stack, stack_t):
    def one_chunk(index, _):
        lanes = pl.ds(pl.multiple_of(index * 512, 512), 512)
        rows = book_t[:, lanes]
        unit = rows * lax.rsqrt(jnp.sum(rows * rows, axis=0, keepdims=True) + norm_eps)
        hi, mid, lo = split3(unit)
        stack_t[:, lanes] = jnp.concatenate([hi, mid, lo, jnp.ones((32, 512), bf16)], axis=0)
        tall = jnp.concatenate([hi, mid, lo, hi, mid, hi, jnp.zeros((64, 512), bf16)], axis=0)
        stack[lanes, :] = tall.T
        return 0

    lax.fori_loop(0, book_t.shape[1] // 512, one_chunk, 0)


def factor_stack(x):
    hi, mid, lo = split3(x)
    return jnp.concatenate([hi, hi, hi, mid, mid, lo, jnp.zeros((64, x.shape[1]), bf16)], axis=0)


def code_loads(pairs, sems):
    loads = []
    for piece in range(4):
        group = []
        for at, (held, to, by_row) in enumerate(pairs):
            size = held.shape[0 if by_row else 1] // 4
            part = pl.ds(piece * size, size)
            place = (part, slice(None)) if by_row else (slice(None), part)
            group.append(pltpu.make_async_copy(held.at[place], to.at[place], sems.at[at, piece]))
        start_all(group)
        loads.append(group)
    return loads


def mlp_vq_kernel(x1, norms, vq_w, stack_hbm, stack_t_hbm, *refs):
    w, (e, u, kept, numer_hbm, h2, acc, stack, stack_t, numer, sems, out_sems) = refs[:8], refs[8:]
    loads = code_loads([(stack_hbm, stack, True), (stack_t_hbm, stack_t, False)], sems)
    e[...] = mlp_rows(1, x1[...], norms, w, h2)
    lnv = ln_parts(e[...])[0] * gain_of(norms, 2) + bias_of(norms, 2)
    raw = dot_nt(vq_w[0:32, :], lnv, highest)
    inv = lax.rsqrt(jnp.sum(raw * raw, axis=0, keepdims=True) + norm_eps)
    latent = raw * inv
    right = factor_stack(latent * (temper * log2e))
    chunks, keeps = stack.shape[0] // 2048, []
    for piece, group in enumerate(loads):
        wait_all(group)
        for part in range(piece * chunks // 4, (piece + 1) * chunks // 4):
            numers = []
            for index in range(4 * part, 4 * part + 4):
                codes = slice(index * 512, (index + 1) * 512)
                numers.append(jnp.exp2(dot(stack[codes, :], right)).astype(bf16))
            if part > 1:
                keeps[part - 2].wait()
            keeps.append(
                pltpu.make_async_copy(
                    numer.at[part % 2],
                    numer_hbm.at[pl.ds(part * 2048, 2048), :],
                    out_sems.at[part % 2],
                )
            )
            numer[part % 2] = jnp.concatenate(numers, axis=0)
            keeps[part].start()
            sums = dot(stack_t[:, part * 2048 : (part + 1) * 2048], numer[part % 2])
            if part == 0:
                acc[...] = sums
            else:
                acc[...] += sums
    total = acc[96:97, :]
    soft = (acc[0:32, :] + acc[32:64, :] + acc[64:96, :]) / total
    kept[0:32, :] = latent
    kept[32:64, :] = soft
    kept[64:65, :] = total
    kept[65:66, :] = inv
    u[...] = dot_full(soft.T, vq_w[32:64, :])
    wait_all(keeps[-2:])


def vq_bwd_kernel(
    ids, e, du, norms, vq_w, stack_hbm, stack_t_hbm, book_hbm, numer_hbm, kept, *refs
):
    small0, small1, de, code_keep, code_send = refs[:5]
    acc, grads, small, tail, stack, stack_t, book_t, numer, load_sems, sems = refs[5:]
    loads = code_loads(
        [
            (stack_hbm, stack, True),
            (numer_hbm, numer, True),
            (stack_t_hbm, stack_t, False),
            (book_hbm, book_t, False),
        ],
        load_sems,
    )
    xhat, inv_ln = ln_parts(e[...])
    lnv = xhat * gain_of(norms, 2) + bias_of(norms, 2)
    latent, soft = kept[0:32, :], kept[32:64, :]
    total, inv = kept[64:65, :], kept[65:66, :]
    direct = (2.0 * 1.25 * commit_weight) * (latent - soft)
    dsoft = dot_nt(vq_w[32:64, :], du[...], highest) - direct
    small[32:64, :] = dot_full(soft, du[...])
    shift = jnp.sum(dsoft * soft, axis=0, keepdims=True) / total
    dsoft = dsoft / total
    right = factor_stack(dsoft)
    pads = jnp.zeros((64, 512), f32)

    def tall(x):
        hi, lo = split2(x)
        return jnp.concatenate([hi.astype(f32), lo.astype(f32), pads], axis=0).T.astype(bf16)

    sides = jnp.concatenate([tall(dsoft), tall(latent * temper)], axis=0)
    chunks = stack.shape[0] // 2048
    for piece, group in enumerate(loads):
        wait_all(group)
        for part in range(piece * chunks // 4, (piece + 1) * chunks // 4):
            dlogits = []
            for index in range(4 * part, 4 * part + 4):
                codes = slice(index * 512, (index + 1) * 512)
                held = numer[codes, :]
                dlogit = (held.astype(f32) * (dot(stack[codes, :], right) - shift)).astype(bf16)
                dlogits.append(dlogit)
                sums = jnp.concatenate([held, dlogit], axis=1)
                dcode = dot(sums, sides).T
                dcode = dcode[0:32, :] + dcode[32:64, :]
                rows = book_t[:, codes]
                scale = lax.rsqrt(jnp.sum(rows * rows, axis=0, keepdims=True) + norm_eps)
                unit = rows * scale
                grads[:, codes] = (
                    scale * (dcode - unit * jnp.sum(unit * dcode, axis=0, keepdims=True))
                ).astype(bf16)
            sums = dot(
                stack_t[0:96, part * 2048 : (part + 1) * 2048], jnp.concatenate(dlogits, axis=0)
            )
            if part == 0:
                acc[...] = sums
            else:
                acc[...] += sums
    dlatent = temper * (acc[0:32, :] + acc[32:64, :] + acc[64:96, :]) + direct
    draw = inv * (dlatent - latent * jnp.sum(latent * dlatent, axis=0, keepdims=True))
    small[0:32, :] = dot_full(draw, lnv)
    dln = dot_full(draw.T, vq_w[0:32, :])
    small[64:65, :] = jnp.sum(dln * xhat, axis=0, keepdims=True)
    small[65:66, :] = jnp.sum(dln, axis=0, keepdims=True)
    small[66:68, :] = small0[0:2, :]
    small[68:70, :] = small1[0:2, :]
    small[70:96, :] = jnp.zeros((26, 512), f32)
    small[...] = ordered(small[...], order_matrix(ids[0], True))
    for block in range(3):
        for at, part in enumerate(split2(small[block * 32 : (block + 1) * 32, :])):
            for side in range(2):
                tail[block * 2 + side, :, at * 256 : (at + 1) * 256] = part[
                    :, side * 256 : (side + 1) * 256
                ]
    tail[6:8] = jnp.zeros((2, 32, 512), bf16)
    core, z = ids[0] % 2, ids[0] // 4
    copies = []
    for slot, (at, to) in enumerate(((core, code_keep), (1 - core, code_send))):
        for k in range(4):
            part = at * 4 + (z ^ k)
            lanes = pl.ds(pl.multiple_of(part * 1024, 1024), 1024)
            copies += [
                pltpu.make_async_copy(
                    grads.at[:, lanes], to.at[k, :, pl.ds(0, 1024)], sems.at[0, slot, k]
                ),
                pltpu.make_async_copy(
                    tail.at[part], to.at[k, :, pl.ds(1024, 512)], sems.at[1, slot, k]
                ),
            ]
    for copy in copies:
        copy.start()
    de[...] = ln_back(dln, xhat, inv_ln, gain_of(norms, 2))
    for copy in copies:
        copy.wait()


SMEM = pl.BlockSpec(memory_space=pltpu.SMEM)
VMEM = pl.BlockSpec(memory_space=pltpu.VMEM)
ANY = pl.BlockSpec(memory_space=pl.ANY)


def shaped(*pairs):
    return [jax.ShapeDtypeStruct(shape, dtype) for shape, dtype in pairs]


def pin(array):
    return pltpu.with_memory_space_constraint(array, pltpu.HBM)


def call(kernel, name, in_specs, out_specs, outs, scratch, flops, after=(), carry=()):
    n_in, n_extra, n_out = len(in_specs), len(after) + len(carry), len(outs)

    def body(*refs):
        first = n_in + n_extra
        kernel(*refs[:n_in], *refs[first : first + n_out], *refs[first + n_out + len(carry) :])

    made = pl.pallas_call(
        body,
        name=name,
        in_specs=in_specs + [ANY] * n_extra,
        out_specs=out_specs + [ANY] * len(carry),
        out_shape=outs + [jax.ShapeDtypeStruct(a.shape, a.dtype) for a in carry],
        scratch_shapes=scratch,
        input_output_aliases={n_in + len(after) + i: n_out + i for i in range(len(carry))},
        compiler_params=pltpu.CompilerParams(vmem_limit_bytes=vmem_cap),
        cost_estimate=pl.CostEstimate(flops=flops, bytes_accessed=10**6, transcendentals=0),
    )

    def run(*args):
        res = made(*args, *after, *carry)
        return (*res[:n_out], list(res[n_out:]))

    return run


DMA = pltpu.SemaphoreType.DMA
ROWS2 = (512, 512)


def attn_fwd(at, marked, xs, norms, w, after=(), carry=()):
    outs = shaped((ROWS2, f32), ((8, 512), f32)) + [pltpu.HBM(ROWS2, bf16)] * 6
    scratch = [
        *[pltpu.VMEM(ROWS2, bf16)] * 3,
        pltpu.VMEM(ROWS2, f32),
        *[pltpu.VMEM(ROWS2, bf16)] * 6,
        DMA((6,)),
    ]
    x1, lse, *saved, carried = call(
        functools.partial(attn_fwd_kernel, bool(xs), at),
        "attn_fwd",
        [VMEM] * (7 + len(xs)),
        [VMEM] * 2 + [ANY] * 6,
        outs,
        scratch,
        10**10,
        after,
        carry,
    )(*marked, norms, *w[:4], *xs)
    return x1, (lse, *saved), carried


def mlp_bwd(at, ids, x1, dys, norms, w, after=(), carry=()):
    scratch = [
        *[pltpu.VMEM(ROWS2, bf16)] * 4,
        *[pltpu.VMEM(ROWS2, f32)] * len(dys),
    ]
    return call(
        functools.partial(mlp_bwd_kernel, len(dys) == 2, at),
        "mlp_bwd",
        [SMEM] + [VMEM] * (10 + len(dys)),
        [VMEM] * 4,
        shaped((ROWS2, f32), ((8, 512), f32), *[((4, 4, 32, 2048), bf16)] * 2),
        scratch,
        15 * 10**9,
        after,
        carry,
    )(ids, x1, norms, *w, *dys)


def attn_bwd(at, marked, x, dx1, norms, saved, w, after=(), carry=()):
    scratch = [pltpu.VMEM(ROWS2, f32), *[pltpu.VMEM(ROWS2, bf16)] * 14, DMA((6,))]
    outs = shaped((ROWS2, f32), ((8, 512), f32), *[((4, 4, 32, 1024), bf16)] * 2)
    return call(
        functools.partial(attn_bwd_kernel, at),
        "attn_bwd",
        [VMEM] * 9 + [ANY] * 6 + [VMEM],
        [VMEM] * 4,
        outs,
        scratch,
        15 * 10**9,
        after,
        carry,
    )(*marked, dx1, norms, saved[0], *w[:4], *map(pin, saved[1:]), x)


def heads_bwd(marked, dx1, saved, w, after=(), carry=()):
    scratch = [pltpu.VMEM(ROWS2, f32), *[pltpu.VMEM(ROWS2, bf16)] * 10, DMA((6,))]
    outs = shaped(*[(ROWS2, bf16)] * 3, *[((4, 4, 32, 256), bf16)] * 2)
    return call(
        heads_bwd_kernel,
        "heads_bwd",
        [VMEM] * 8 + [ANY] * 6,
        [VMEM] * 5,
        outs,
        scratch,
        10 * 10**9,
        after,
        carry,
    )(*marked, dx1, saved[0], *w[:4], *map(pin, saved[1:]))


def rows_bwd(ids, marked, dx1, norms, parts, other_small, d_x1, w, d_w, after=(), carry=()):
    scratch = [pltpu.VMEM((8, 512), f32), *[pltpu.VMEM(ROWS2, bf16)] * 2]
    outs = shaped(*[((256, 512), f32), ((256, 512), bf16)] * 2, *[((4, 4, 32, 1152), bf16)] * 2)
    return call(
        rows_bwd_kernel,
        "rows_bwd",
        [SMEM] + [VMEM] * 23,
        [VMEM] * 6,
        outs,
        scratch,
        10 * 10**9,
        after,
        carry,
    )(ids, *marked, dx1, norms, *parts, other_small, d_x1, *w[:4], *d_w)


def code_prep(book_t, after=(), carry=()):
    codes = book_t.shape[1]
    return call(
        code_prep_kernel,
        "code_prep",
        [VMEM],
        [VMEM] * 2,
        shaped(((codes, 256), bf16), ((128, codes), bf16)),
        [],
        6 * 10**9,
        after,
        carry,
    )(book_t)


def mlp_vq(x1, norms, vq_w, stack, stack_t, w, after=(), carry=()):
    return call(
        mlp_vq_kernel,
        "mlp_vq",
        [VMEM] * 3 + [ANY] * 2 + [VMEM] * 8,
        [VMEM] * 3 + [ANY],
        shaped((ROWS2, f32), (ROWS2, f32), ((72, 512), f32))
        + [pltpu.HBM((stack.shape[0], 512), bf16)],
        [
            pltpu.VMEM(ROWS2, bf16),
            pltpu.VMEM((128, 512), f32),
            pltpu.VMEM(stack.shape, bf16),
            pltpu.VMEM(stack_t.shape, bf16),
            pltpu.VMEM((2, 2048, 512), bf16),
            DMA((2, 4)),
            DMA((2,)),
        ],
        25 * 10**9,
        after,
        carry,
    )(x1, norms, vq_w, pin(stack), pin(stack_t), *w)


def vq_bwd(ids, e, du, norms, vq_w, codes, kept, smalls, after=(), carry=()):
    scratch = [
        pltpu.VMEM((96, 512), f32),
        pltpu.VMEM(codes[2].shape, bf16),
        pltpu.VMEM((96, 512), f32),
        pltpu.VMEM((8, 32, 512), bf16),
        *[pltpu.VMEM(a.shape, a.dtype) for a in codes],
        DMA((4, 4)),
        DMA((2, 2, 4)),
    ]
    return call(
        vq_bwd_kernel,
        "vq_bwd",
        [SMEM] + [VMEM] * 4 + [ANY] * 4 + [VMEM] * 3,
        [VMEM] + [ANY] * 2,
        shaped((ROWS2, f32), *[((4, 32, 1536), bf16)] * 2),
        scratch,
        25 * 10**9,
        after,
        carry,
    )(ids, e, du, norms, vq_w, *map(pin, codes), kept, *smalls)


def lines_kernel(cuts, *refs):
    first = 0
    for out, width in zip(refs[4:], cuts):
        for k in range(4):
            out[k] = refs[k][:, first : first + width]
        first += width


def stack_lines(shards, cuts, after=(), carry=()):
    return call(
        functools.partial(lines_kernel, cuts),
        "stack_lines",
        [VMEM] * 4,
        [VMEM] * len(cuts),
        shaped(*[((4, 32, width), bf16) for width in cuts]),
        [],
        1,
        after,
        carry,
    )(*shards)


def pack_kernel(*refs):
    hbm, outs, held, sems = refs[:4], refs[4:6], refs[6:10], refs[10]
    copies = [pltpu.make_async_copy(hbm[at], held[at], sems.at[at]) for at in range(4)]
    start_all(copies)
    wait_all(copies)
    qkv, out_t, up, down_t = held
    for layer, out in enumerate(outs):
        for index in range(3):
            out[:, index * 256 : (index + 1) * 256] = qkv[layer, index]
        out[:, 768:1024] = out_t[layer]
        out[:, 1024:2048] = up[layer]
        out[:, 2048:] = down_t[layer]


def pack_weights(*arrays):
    return call(
        pack_kernel,
        "pack_weights",
        [ANY] * 4,
        [VMEM] * 2,
        shaped(*[((32, 3072), bf16)] * 2),
        [*[pltpu.VMEM(a.shape, a.dtype) for a in arrays], DMA((4,))],
        1,
    )(*map(pin, arrays))[:-1]


def pairs_kernel(*refs):
    count = len(refs) // 3
    for at in range(count):
        refs[2 * count + at][0] = refs[2 * at][...]
        refs[2 * count + at][1] = refs[2 * at + 1][...]


def stack_pairs(pairs, after=(), carry=()):
    return call(
        pairs_kernel,
        "stack_pairs",
        [VMEM] * (2 * len(pairs)),
        [VMEM] * len(pairs),
        shaped(*[((2, *a.shape), bf16) for a, _ in pairs]),
        [],
        1,
        after,
        carry,
    )(*[array for pair in pairs for array in pair])


def gate(after, carry):
    def kernel(out):
        out[...] = jnp.zeros_like(out)

    return call(kernel, "gate", [], [VMEM], shaped(((8, 128), f32)), [], 1, after, carry)()[-1]


def rows_in_kernel(ids, *refs):
    hbm, (own, send, norms, vq_w), held, sems = refs[:7], refs[7:11], refs[11:18], refs[18]
    copies = [pltpu.make_async_copy(hbm[at], held[at], sems.at[at]) for at in range(7)]
    start_all(copies)
    matrix = order_matrix(ids[0], False)
    wait_all(copies)
    tokens, segs, cot, gains, biases, in_t, out_w = held
    for to, micro in ((send, 1 - ids[1]), (own, ids[1])):
        to[:, :512] = ordered(tokens[micro], matrix).astype(bf16)
        ids_row = segs[pl.ds(micro, 1), :].astype(f32)
        to[:, 512:640] = jnp.broadcast_to(ids_row, (128, 256)).T.astype(bf16)
    send[:, 640:] = ordered(cot[1 - ids[1]].astype(bf16), matrix).astype(bf16)
    pad = jnp.zeros((3, 512), f32)
    rows = jnp.concatenate([gains[...], pad, biases[...], pad], axis=0)
    norms[...] = ordered(rows, matrix)
    vq_w[...] = ordered(jnp.concatenate([in_t[...], out_w[...]], axis=0), matrix)


def rows_in(ids, *arrays):
    outs = shaped(
        ((256, 640), bf16), ((256, 1152), bf16), ((16, 512), f32), ((64, 512), f32)
    )
    return call(
        rows_in_kernel,
        "rows_in",
        [SMEM] + [ANY] * 7,
        [VMEM] * 4,
        outs,
        [*[pltpu.VMEM(a.shape, a.dtype) for a in arrays], DMA((7,))],
        1,
    )(ids, *map(pin, arrays))[:-1]


def joined(block):
    return block[0:16, 1024:].astype(f32) + block[16:32, 1024:].astype(f32)


def put_small(value, own, blocks):
    hi, lo = split2(value)
    own[0:16, 1024:] = hi.astype(f32) + lo.astype(f32)
    for block in blocks:
        block[0:16, 1024:] = hi
        block[16:32, 1024:] = lo


def near_kernel(ids, ins, outs):
    keep, other = ins
    for i in range(4):
        outs[i][...] = (keep[i].astype(f32) + other[i].astype(f32)).astype(outs[i].dtype)
    if keep.shape[3] == 1152:
        value = joined(keep.at[0, 0]) + joined(other.at[0, 0])
        put_small(value, outs[0].at[0], [out.at[0] for out in outs[1:]])


def near_task(keep, other):
    shape = keep.shape[1:]
    return near_kernel, [keep, other], shaped((shape, f32), *[(shape, bf16)] * 3)


def put_code(ref, first, code):
    for i in range(3):
        ref[first + i] = code[:, 1024 * i : 1024 * (i + 1)]


def get_code(ref, first):
    return jnp.concatenate([ref[first + i] for i in range(3)], axis=1)


def swapped(code):
    return jnp.concatenate([code[:, 1536:], code[:, :1536]], axis=1)


def code_sum(a, b):
    done = []
    for first in range(0, a.shape[1], 1536):
        total = a[:, first : first + 1024].astype(f32) + b[:, first : first + 1024].astype(f32)
        small = [
            x[:, first + 1024 : first + 1280].astype(f32) + x[:, first + 1280 : first + 1536].astype(f32)
            for x in (a, b)
        ]
        done += [total.astype(bf16), *split2(small[0] + small[1])]
    return jnp.concatenate(done, axis=1)


def fork_kernel(ids, ins, outs):
    keep, other, code, code_other = ins
    own_up, to_x, own_down, to_y, code_out = outs
    for at, (own, send, kept, sent) in enumerate(
        ((own_up, to_x, (0, 2), (1, 3)), (own_down, to_y, (0, 1), (2, 3)))
    ):
        cols = slice(1024 * at, 1024 * (at + 1))
        for j in range(2):
            own[j] = keep[kept[j], :, :, cols].astype(f32) + other[kept[j], :, :, cols].astype(f32)
            total = keep[sent[j], :, :, cols].astype(f32) + other[sent[j], :, :, cols].astype(f32)
            send[4 * j : 4 * (j + 1)] = total.astype(bf16)
    code_out[...] = code_sum(code[...], code_other[...])


def fork_task(keep, other, code, code_other):
    outs = shaped(
        ((2, 4, 32, 1024), f32),
        ((8, 32, 1024), bf16),
        ((2, 4, 32, 1024), f32),
        ((8, 32, 1024), bf16),
        (code.shape, bf16),
    )
    return fork_kernel, [keep, other, code, code_other], outs


def half_kernel(ids, ins, outs):
    own_up, from_x, own_down, from_y, code, code_other = ins
    up, to_y, down, to_x, code_out = outs
    for own, other, kept, send in ((own_up, from_x, up, to_y), (own_down, from_y, down, to_x)):
        kept[...] = own[0] + other[0:4].astype(f32)
        send[0:4] = (own[1] + other[4:8].astype(f32)).astype(bf16)
    code_out[...] = code_sum(code[...], swapped(code_other[...]))
    put_code(to_x, 4, code_out)


def half_task(own_up, from_x, own_down, from_y, code, code_other):
    outs = shaped(
        ((4, 32, 1024), f32),
        ((4, 32, 1024), bf16),
        ((4, 32, 1024), f32),
        ((7, 32, 1024), bf16),
        (code.shape, bf16),
    )
    return half_kernel, [own_up, from_x, own_down, from_y, code, code_other], outs


def join_kernel(ids, ins, outs):
    own_up, from_y, own_down, from_x, code = ins
    kept, send, code_out = outs
    code_out[...] = code_sum(code[...], get_code(from_x, 4))
    for at, (own, other) in enumerate(((own_up, from_y), (own_down, from_x))):
        cols = slice(1024 * at, 1024 * (at + 1))
        for k in range(2):
            kept[k, :, cols] = own[2 * k] + other[2 * k].astype(f32)
            send[k, :, cols] = (own[2 * k + 1] + other[2 * k + 1].astype(f32)).astype(bf16)


def join_task(own_up, from_y, own_down, from_x, code):
    outs = shaped(((2, 32, 2048), f32), ((2, 32, 2048), bf16), (code.shape, bf16))
    return join_kernel, [own_up, from_y, own_down, from_x, code], outs


def line_step_kernel(ids, ins, outs):
    kept, other = ins
    outs[0][...] = kept[0] + other[0].astype(f32)
    outs[1][...] = (kept[1] + other[1].astype(f32)).astype(bf16)


def line_step_task(kept, other):
    shape = kept.shape[1:]
    return line_step_kernel, [kept, other], shaped((shape, f32), (shape, bf16))


def plane_kernel(ids, ins, outs):
    for k in range(4):
        total = ins[0][k]
        for other in ins[1:]:
            total = total + other[k].astype(f32)
        outs[k][...] = total.astype(outs[k].dtype)
    if ins[0].shape[2] == 1152:
        x, y, xy = [joined(other.at[0]) for other in ins[1:]]
        put_small((ins[0][0, 0:16, 1024:] + x) + (y + xy), outs[0], outs[1:])


def plane_line_kernel(ids, ins, outs):
    kept, send = outs
    for k in range(4):
        total = ins[0][k]
        for other in ins[1:]:
            total = total + other[k].astype(f32)
        to = send if k % 2 else kept
        to[k // 2] = total.astype(to.dtype)
    x, y, xy = [joined(other.at[0]) for other in ins[1:]]
    put_small((ins[0][0, 0:16, 1024:] + x) + (y + xy), kept.at[0], [send.at[0]])


def plane_line_task(own, others):
    outs = shaped(((2, 32, 1152), f32), ((2, 32, 1152), bf16))
    return plane_line_kernel, [own, *others], outs


def small_step_kernel(ids, ins, outs):
    kept, other = ins
    line_step_kernel(ids, ins, outs)
    put_small(kept[0, 0:16, 1024:] + joined(other.at[0]), outs[0], [outs[1]])


def small_step_task(kept, other):
    shape = kept.shape[1:]
    return small_step_kernel, [kept, other], shaped((shape, f32), (shape, bf16))


def plane_task(own, others):
    shape = own.shape[1:]
    return plane_kernel, [own, *others], shaped((shape, f32), *[(shape, bf16)] * 3)


def plane_part_kernel(ids, ins, outs):
    outs[0][...] = ins[0][...] + ins[1][...].astype(f32) + ins[2][...].astype(f32)


def plane_part_task(own, a, b):
    return plane_part_kernel, [own, a, b], shaped((own.shape, f32))


def plane_join_kernel(ids, ins, outs):
    own, others, m_own, m_lows = ins[0], ins[1:4], ins[4], ins[5:]
    kept, send = outs
    for k in range(4):
        total = own[k]
        for other in others:
            total = total + other[k].astype(f32)
        rest = m_own if k == 0 else m_lows[k - 1]
        to = send if k % 2 else kept
        to[k // 2, :, :1024] = total.astype(to.dtype)
        to[k // 2, :, 1024:] = rest[...].astype(to.dtype)


def plane_join_task(own, others, *parts):
    outs = shaped(((2, 32, 3072), f32), ((2, 32, 3072), bf16))
    return plane_join_kernel, [own, *others, *parts], outs


def line_total(ins, width):
    total = ins[0][:, :width]
    for other in ins[1:]:
        total = total + other[:, :width].astype(f32)
    return total


def rows_out_kernel(ids, ins, outs):
    y, y_low, dx, dx_low = ins
    matrix = order_matrix(ids[0], True)
    outs[0][...] = ordered(y[...], matrix)
    outs[1][...] = ordered(dx[...], matrix)
    outs[2][0:256, :] = y_low[...]
    outs[2][256:, :] = dx_low[...]


def rows_out_task(y, y_low, dx, dx_low):
    outs = shaped((y.shape, f32), (dx.shape, f32), (ROWS2, bf16))
    return rows_out_kernel, [y, y_low, dx, dx_low], outs


def rows_kernel(ids, ins, outs):
    y, dx, others = ins
    moved = ordered(others[...], order_matrix(ids[0], True))
    for at, (out, own) in enumerate(zip(outs, (y, dx))):
        out[ids[1]] = own[...]
        out[1 - ids[1]] = moved[256 * at : 256 * (at + 1), :]


def rows_task(y, dx, others):
    return rows_kernel, [y, dx, others], shaped(*[((2, 256, 512), f32)] * 2)


def code_near_kernel(ids, ins, outs):
    keep, other = ins
    for at, out in enumerate(outs):
        for i in range(2):
            out[:, 1536 * i : 1536 * (i + 1)] = code_sum(keep[2 * at + i], other[2 * at + i])


def code_near_task(keep, other):
    return code_near_kernel, [keep, other], shaped(*[((32, 3072), bf16)] * 2)


def code_add_kernel(ids, ins, outs):
    outs[0][...] = code_sum(ins[0][...], ins[1][...])


def code_add_task(a, b):
    return code_add_kernel, [a, b], shaped((a.shape, bf16))


def code_pair_kernel(ids, ins, outs):
    for at, part in enumerate(ins):
        outs[0][:, 3072 * at : 3072 * (at + 1)] = part[...]


def code_pair_task(a, b):
    return code_pair_kernel, [a, b], shaped(((32, 6144), bf16))


def finish_kernel(ids, ins, outs):
    mlp, attn, dec, code, code_other = ins[:2], ins[2:4], ins[4:6], *ins[6:]
    qkv, out_t, up, down_t, book, vq_in, vq_out, gains, biases, dec_biases, small_ref = outs
    both = line_total(dec, 3072)
    for layer, rows in enumerate((line_total(mlp, 2048), both[:, 1024:])):
        up[layer] = rows[:, :1024]
        down_t[layer] = rows[:, 1024:]
    for layer, rows in enumerate((line_total(attn, 1024), both[:, :1024])):
        for index in range(3):
            qkv[layer, index] = rows[:, index * 256 : (index + 1) * 256]
        out_t[layer] = rows[:, 768:]
    core, z = ids[0] % 2, ids[0] // 4
    for at, parts in ((core, code), (1 - core, code_other)):
        for k in range(4):
            part = at * 4 + (z ^ k)
            held = parts[:, 1536 * k : 1536 * (k + 1)].astype(f32)
            book[:, pl.ds(pl.multiple_of(part * 1024, 1024), 1024)] = held[:, :1024]
            small_ref[:, pl.ds(pl.multiple_of(part * 256, 256), 256)] = (
                held[:, 1024:1280] + held[:, 1280:1536]
            )
    small = small_ref[...]
    vq_in[...] = small[:, :512]
    vq_out[...] = small[:, 512:1024]
    rest = small[:, 1024:1536]
    packed = attn[0][0:16, 1024:] + joined(attn[1])
    for row, out in enumerate((gains.at[0:1], biases.at[0:1], gains.at[1:2], biases.at[1:2])):
        for j in range(4):
            out[:, 128 * j : 128 * (j + 1)] = packed[row * 4 + j : row * 4 + j + 1, :]
    gains[2:3, :] = rest[0:1, :]
    biases[2:3, :] = rest[1:2, :]
    gains[3:4, :] = rest[2:3, :]
    dec_biases[0:1, :] = rest[3:4, :]
    gains[4:5, :] = rest[4:5, :]
    dec_biases[1:2, :] = rest[5:6, :]


def finish_task(own_m, other_m, own_a, other_a, own_d, other_d, code, code_other):
    outs = shaped(
        ((2, 3, 32, 256), f32),
        ((2, 32, 256), f32),
        ((2, 32, 1024), f32),
        ((2, 32, 1024), f32),
        ((32, 8192), f32),
        ((32, 512), f32),
        ((32, 512), f32),
        ((5, 512), f32),
        ((3, 512), f32),
        ((2, 512), f32),
        ((32, 2048), f32),
    )
    ins = [own_m, other_m, own_a, other_a, own_d, other_d, code, code_other]
    return finish_kernel, ins, outs


def run_tasks(ids, name, tasks, after=(), carry=()):
    sizes = [(len(ins), len(outs)) for _, ins, outs in tasks]
    n_in = sum(i for i, _ in sizes)

    def kernel(ids_ref, *refs):
        at_in, at_out = 0, n_in
        for (fn, _, _), (i, o) in zip(tasks, sizes):
            fn(ids_ref, refs[at_in : at_in + i], refs[at_out : at_out + o])
            at_in, at_out = at_in + i, at_out + o

    outs = [one for _, _, many in tasks for one in many]
    res = call(
        kernel, name, [SMEM] + [VMEM] * n_in, [VMEM] * len(outs), outs, [], 10**9, after, carry
    )(ids, *[one for _, many, _ in tasks for one in many])
    split, at = [], 0
    for _, o in sizes:
        split.append(res[at : at + o])
        at += o
    return (*split, res[-1])


def whole_groups(
    n_dp,
    tokens,
    segment_ids,
    norm_gains,
    norm_biases,
    w_qkv,
    w_attn_out,
    w_up,
    w_down,
    w_vq_in,
    w_vq_out,
    codebook,
    cotangent,
):
    dp_at, tp_at = lax.axis_index("dp"), lax.axis_index("tp")
    ids = jnp.stack([dp_at, tp_at]).astype(jnp.int32)

    def swap(values):
        return exchange(values, 0, 1, n_dp)

    def core(values):
        return [values, exchange(values, 1, 0, n_dp)]

    book_t = codebook.T
    enc_shard, dec_shard = pack_weights(
        w_qkv, w_attn_out.transpose(0, 2, 1), w_up, w_down.transpose(0, 2, 1)
    )
    enc_shards = spread_line(enc_shard, n_dp)
    own, send, norms, vq_w = rows_in(
        ids,
        tokens,
        segment_ids,
        cotangent,
        norm_gains,
        norm_biases,
        w_vq_in.T,
        w_vq_out,
    )
    marked = [own, swap(send)]

    line_a, line_b, (dec_shard,) = stack_lines(enc_shards, [1536] * 2, carry=[dec_shard])
    along_x, along_y = exchange(line_a, 0, 1, n_dp), exchange(line_b, 2, 0, n_dp)
    dec_shards = spread_line(dec_shard, n_dp)
    stack, stack_t, _ = code_prep(book_t, [line_a])
    codes = (stack, stack_t, book_t)
    a_0, b_0, _ = stack_pairs([(line_a, along_x), (line_b, along_y)], [stack_t, marked[1]])
    a_1, b_1 = exchange(a_0, 2, 0, n_dp), exchange(b_0, 0, 1, n_dp)
    line_a, line_b, (a_0, b_0) = stack_lines(dec_shards, [1536] * 2, [a_1, b_1], [a_0, b_0])
    enc_w = [a_0, a_1, exchange(a_0, 1, 0, n_dp), exchange(a_1, 1, 0, n_dp)]
    enc_w += [b_0, b_1, exchange(b_0, 1, 0, n_dp), exchange(b_1, 1, 0, n_dp)]
    along_x, along_y = exchange(line_a, 0, 1, n_dp), exchange(line_b, 2, 0, n_dp)
    e_x1, e_saved, _ = attn_fwd(0, marked, [], norms, enc_w)
    a_0, b_0, _ = stack_pairs([(line_a, along_x), (line_b, along_y)], [e_x1])
    a_1, b_1 = exchange(a_0, 2, 0, n_dp), exchange(b_0, 0, 1, n_dp)
    dec_w = [a_0, exchange(a_0, 1, 0, n_dp), b_0, exchange(b_0, 1, 0, n_dp)]
    e, u, kept, numer, _ = mlp_vq(e_x1, norms, vq_w, stack, stack_t, enc_w, [a_0, b_0])
    a_1, b_1 = gate([u], [a_1, b_1])
    a_1, b_1 = core(a_1), core(b_1)
    dec_w = [dec_w[0], a_1[0], dec_w[1], a_1[1], dec_w[2], b_1[0], dec_w[3], b_1[1]]
    d_x1, d_saved, _ = attn_fwd(3, marked, [u], norms, dec_w)

    dx1, d_small1, keep_m, send_m, _ = mlp_bwd(
        4, ids, d_x1, [cotangent, marked[1]], norms, dec_w
    )
    near_m = exchange(send_m, 1, 0, n_dp)
    du, d_small0, keep_a, send_a, (keep_m,) = attn_bwd(
        3, marked, u, dx1, norms, d_saved, dec_w, carry=[keep_m]
    )
    (own_m, *lows_m), (send_a,) = run_tasks(
        ids, "sums1", [near_task(keep_m, near_m)], carry=[send_a]
    )
    from_x, from_y = exchange(lows_m[0], 0, 1, n_dp), exchange(lows_m[1], 2, 0, n_dp)
    near_a = exchange(send_a, 1, 0, n_dp)
    de, code, code_send, (own_m, keep_a, low_m) = vq_bwd(
        ids,
        e,
        du,
        norms,
        vq_w,
        [*codes, numer],
        kept,
        [d_small0, d_small1],
        lows_m[:2],
        [own_m, keep_a, lows_m[2]],
    )
    (own_m,), (own_a, *lows_a), (code, code_send) = run_tasks(
        ids,
        "sums2",
        [plane_part_task(own_m, from_x, from_y), near_task(keep_a, near_a)],
        carry=[code, code_send],
    )
    from_xy, code_other = exchange(low_m, 2, 1, n_dp), exchange(code_send, 1, 0, n_dp)
    (code, code_send), _ = run_tasks(ids, "sums2b", [code_near_task(code, code_other)])
    code_other = exchange(code_send, 8, 0, n_dp)
    ex1, e_small1, keep_m, send_m, (own_m, own_a, code, *lows_a) = mlp_bwd(
        1, ids, e_x1, [de], norms, enc_w, [low_m, code_send], [own_m, own_a, code, *lows_a]
    )
    d_mlp, (code,), (keep_m, send_m, own_a, *lows_a) = run_tasks(
        ids,
        "sums3",
        [plane_task(own_m, [from_xy]), code_add_task(code, code_other)],
        carry=[keep_m, send_m, own_a, *lows_a],
    )
    near_m, code_other = exchange(send_m, 1, 0, n_dp), exchange(code, 2, 0, n_dp)
    plane_a = plane_send(lows_a, n_dp)
    *parts, (own_a,) = heads_bwd(marked, ex1, e_saved, enc_w, [*lows_a, code], [own_a])
    (own_up, to_x, own_down, to_y, code), (own_d, send_d), _ = run_tasks(
        ids,
        "sums3b",
        [fork_task(keep_m, near_m, code, code_other), plane_join_task(own_a, plane_a, *d_mlp)],
        [parts[0]],
    )
    other_d, code_other = exchange(send_d, 4, 0, n_dp), exchange(code, 4, 0, n_dp)
    from_y, from_x = exchange(to_y, 2, 0, n_dp), exchange(to_x, 0, 1, n_dp)
    dx, dx_low, y, y_low, keep_a, send_a, (own_up, own_down, code, own_d) = rows_bwd(
        ids,
        marked,
        ex1,
        norms,
        parts,
        e_small1,
        d_x1,
        enc_w,
        dec_w,
        [to_x, to_y, send_d],
        [own_up, own_down, code, own_d],
    )
    (own_up, to_y, own_down, to_x, code), (own_d, send_d), (keep_a, send_a) = run_tasks(
        ids,
        "sums4",
        [
            half_task(own_up, from_x, own_down, from_y, code, code_other),
            line_step_task(own_d, other_d),
        ],
        carry=[keep_a, send_a],
    )
    near_a, other_d = exchange(send_a, 1, 0, n_dp), exchange(send_d, 8, 0, n_dp)
    from_y, from_x = exchange(to_y, 2, 0, n_dp), exchange(to_x, 0, 1, n_dp)
    (own_a, *lows_a), (own_up, own_down, code) = run_tasks(
        ids, "sums4b", [near_task(keep_a, near_a)], carry=[own_up, own_down, code]
    )
    plane_a = plane_send(lows_a, n_dp)
    (own_m, send_m, code), (own_a,) = run_tasks(
        ids,
        "sums5",
        [join_task(own_up, from_y, own_down, from_x, code)],
        [*lows_a, other_d],
        [own_a],
    )
    other_m, code_other = exchange(send_m, 4, 0, n_dp), exchange(code, 8, 0, n_dp)
    (y, dx, rows), (own_a,) = run_tasks(
        ids, "rows_out", [rows_out_task(y, y_low, dx, dx_low)], [send_m, code], [own_a]
    )
    (own_a, send_a), (own_m, send_m), (code,), (rows,) = run_tasks(
        ids,
        "sums6",
        [
            plane_line_task(own_a, plane_a),
            line_step_task(own_m, other_m),
            code_pair_task(code, code_other),
        ],
        carry=[rows],
    )
    other_a, other_m = exchange(send_a, 4, 0, n_dp), exchange(send_m, 8, 0, n_dp)
    code_other, rows = exchange(code, 1, 0, n_dp), swap(rows)
    (own_a, send_a), _ = run_tasks(ids, "sums7", [small_step_task(own_a, other_a)])
    other_a = exchange(send_a, 8, 0, n_dp)
    (decoded, grad_tokens), _ = run_tasks(ids, "rows_done", [rows_task(y, dx, rows)], [send_a])
    (qkv, out_t, up, down_t, book, vq_in, vq_out, *norm_grads, _), _ = run_tasks(
        ids,
        "finish",
        [finish_task(own_m, other_m, own_a, other_a, own_d, other_d, code, code_other)],
    )
    return (
        decoded,
        grad_tokens,
        *norm_grads,
        qkv,
        out_t.transpose(0, 2, 1),
        up,
        down_t.transpose(0, 2, 1),
        vq_in.T,
        vq_out,
        book.T,
    )


def layer_norm(values, norm_gain, norm_bias):
    centred = values - jnp.mean(values, axis=-1, keepdims=True)
    spread = jnp.mean(centred * centred, axis=-1, keepdims=True)
    return centred * lax.rsqrt(spread + ln_eps) * norm_gain + norm_bias


def gelu_tanh(values):
    return (
        0.5 * values * (1.0 + jnp.tanh(gelu_coef * (values + 0.044715 * values * values * values)))
    )


def matmul(former, latter):
    return jnp.dot(former, latter, precision=highest, preferred_element_type=jnp.float32)


def normalize(values):
    return values * lax.rsqrt(jnp.sum(values * values, axis=-1, keepdims=True) + norm_eps)


def quantize(in_rows, norm_gain, norm_bias, in_w, out_w, code_w):
    latent = normalize(matmul(layer_norm(in_rows, norm_gain, norm_bias), in_w))
    code_rows = normalize(code_w)
    logits = matmul(latent, code_rows.T) * temper
    row_max = jnp.max(logits, axis=-1, keepdims=True)
    numerator = jnp.exp(logits - row_max)
    assign = numerator / jnp.sum(numerator, axis=-1, keepdims=True)
    soft_code = matmul(assign, code_rows)
    offset = latent - soft_code
    vq_loss = commit_weight * 1.25 * jnp.sum(offset * offset)
    return (matmul(soft_code, out_w), vq_loss)


def product(former, latter):
    return jnp.dot(former, latter, preferred_element_type=jnp.float32)


def product_tn(former, latter):
    return lax.dot_general(
        former, latter, (((0,), (0,)), ((), ())), preferred_element_type=jnp.float32
    )


def product_nt(former, latter):
    return lax.dot_general(
        former, latter, (((1,), (1,)), ((), ())), preferred_element_type=jnp.float32
    )


def split_heads(values):
    return values.reshape(values.shape[0], values.shape[1] // HEAD_DIM, HEAD_DIM).transpose(1, 0, 2)


def join_heads(values):
    return values.transpose(1, 0, 2).reshape(values.shape[1], values.shape[0] * HEAD_DIM)


def masked_scores(query_blk, key_h, seg_blk, seg_keys):
    scores = jnp.einsum(
        "hqd,hkd->hqk", query_blk, key_h, preferred_element_type=jnp.float32
    ) * HEAD_DIM ** (-0.5)
    return jnp.where((seg_blk[:, None] == seg_keys[None, :])[None], scores, masked_score)


def attend(query_h, key_h, value_h, seg_keys):
    block_rows = min(512, query_h.shape[1])
    block_count = query_h.shape[1] // block_rows

    def one_block(begin_row):
        query_blk = lax.dynamic_slice_in_dim(query_h, begin_row, block_rows, 1)
        seg_blk = lax.dynamic_slice_in_dim(seg_keys, begin_row, block_rows, 0)
        scores = masked_scores(query_blk, key_h, seg_blk, seg_keys)
        row_max = jnp.max(scores, axis=-1, keepdims=True)
        numerator = jnp.exp(scores - row_max)
        row_total = jnp.sum(numerator, axis=-1, keepdims=True)
        prob_low = (numerator / row_total).astype(jnp.bfloat16)
        attended = jnp.einsum("hqk,hkd->hqd", prob_low, value_h, preferred_element_type=jnp.float32)
        return (attended.astype(jnp.bfloat16), (row_max + jnp.log(row_total))[..., 0])

    starts = jnp.arange(block_count, dtype=jnp.int32) * block_rows
    attended, log_sums = lax.map(one_block, starts)
    heads_out = attended.transpose(1, 0, 2, 3).reshape(query_h.shape)
    log_sums = log_sums.transpose(1, 0, 2).reshape(query_h.shape[0], query_h.shape[1])
    return (heads_out, log_sums)


def attend_back(query_h, key_h, value_h, seg_keys, log_sums, grad_out):
    block_rows = min(512, query_h.shape[1])
    block_count = query_h.shape[1] // block_rows

    def one_block(carry, begin_row):
        grad_key, grad_value = carry
        query_blk = lax.dynamic_slice_in_dim(query_h, begin_row, block_rows, 1)
        grad_blk = lax.dynamic_slice_in_dim(grad_out, begin_row, block_rows, 1)
        lse_blk = lax.dynamic_slice_in_dim(log_sums, begin_row, block_rows, 1)
        seg_blk = lax.dynamic_slice_in_dim(seg_keys, begin_row, block_rows, 0)
        scores = masked_scores(query_blk, key_h, seg_blk, seg_keys)
        probs = jnp.exp(scores - lse_blk[..., None])
        prob_low = probs.astype(jnp.bfloat16)
        grad_value = grad_value + jnp.einsum(
            "hqk,hqd->hkd", prob_low, grad_blk, preferred_element_type=jnp.float32
        )
        grad_prob = jnp.einsum(
            "hqd,hkd->hqk", grad_blk, value_h, preferred_element_type=jnp.float32
        )
        row_dot = jnp.sum(probs * grad_prob, axis=-1, keepdims=True)
        grad_score = (probs * (grad_prob - row_dot) * HEAD_DIM ** (-0.5)).astype(jnp.bfloat16)
        grad_query = jnp.einsum(
            "hqk,hkd->hqd", grad_score, key_h, preferred_element_type=jnp.float32
        )
        grad_key = grad_key + jnp.einsum(
            "hqk,hqd->hkd", grad_score, query_blk, preferred_element_type=jnp.float32
        )
        return ((grad_key, grad_value), grad_query)

    starts = jnp.arange(block_count, dtype=jnp.int32) * block_rows
    zeros_kv = jnp.zeros(key_h.shape, jnp.float32)
    (grad_key, grad_value), grad_query = lax.scan(one_block, (zeros_kv, zeros_kv), starts)
    grad_query = grad_query.transpose(1, 0, 2, 3).reshape(query_h.shape)
    return (
        grad_query.astype(jnp.bfloat16),
        grad_key.astype(jnp.bfloat16),
        grad_value.astype(jnp.bfloat16),
    )


def spread_rows(values):
    return lax.all_gather(values, "tp", axis=0, tiled=True)


def combine_rows(partial_value):
    return lax.psum_scatter(partial_value, "tp", scatter_dimension=0, tiled=True)


def spread_grads(values):
    return lax.all_gather(values, "tp", axis=0, tiled=True)


def combine_grads(partial_value):
    return lax.psum_scatter(
        partial_value.astype(jnp.bfloat16), "tp", scatter_dimension=0, tiled=True
    ).astype(jnp.float32)


def fetch_weights(w_qkv, w_attn_out, w_up, w_down, layer):
    return (
        lax.all_gather(w_qkv[layer], "dp", axis=1, tiled=True),
        lax.all_gather(w_attn_out[layer], "dp", axis=1, tiled=True),
        lax.all_gather(w_up[layer], "dp", axis=0, tiled=True),
        lax.all_gather(w_down[layer], "dp", axis=1, tiled=True),
    )


def reduce_weight_grads(grads):
    return (
        lax.psum_scatter(
            grads[0].astype(jnp.bfloat16), "dp", scatter_dimension=1, tiled=True
        ).astype(jnp.float32),
        lax.psum_scatter(
            grads[1].astype(jnp.bfloat16), "dp", scatter_dimension=1, tiled=True
        ).astype(jnp.float32),
        lax.psum_scatter(
            grads[2].astype(jnp.bfloat16), "dp", scatter_dimension=0, tiled=True
        ).astype(jnp.float32),
        lax.psum_scatter(
            grads[3].astype(jnp.bfloat16), "dp", scatter_dimension=1, tiled=True
        ).astype(jnp.float32),
    )


def block_forward(resid_in, seg_local, gains, biases, weights):
    qkv_w, attn_w, up_w, down_w = weights
    normed = layer_norm(resid_in, gains[0], biases[0]).astype(jnp.bfloat16)
    normed_all, seg_all = (
        lax.all_gather(normed, "tp", axis=0, tiled=True),
        lax.all_gather(seg_local, "tp", axis=0, tiled=True),
    )
    query_h = split_heads(product(normed_all, qkv_w[0]).astype(jnp.bfloat16))
    key_h = split_heads(product(normed_all, qkv_w[1]).astype(jnp.bfloat16))
    value_h = split_heads(product(normed_all, qkv_w[2]).astype(jnp.bfloat16))
    heads_out, log_sums = attend(query_h, key_h, value_h, seg_all)
    attn_rows = join_heads(heads_out)
    middle = resid_in + combine_rows(product(attn_rows, attn_w))
    normed_mid = spread_rows(layer_norm(middle, gains[1], biases[1]).astype(jnp.bfloat16))
    hidden_pre = product(normed_mid, up_w)
    hidden = gelu_tanh(hidden_pre).astype(jnp.bfloat16)
    result = middle + combine_rows(product(hidden, down_w))
    kept = (
        resid_in,
        middle,
        normed_all,
        seg_all,
        query_h,
        key_h,
        value_h,
        log_sums,
        attn_rows,
        normed_mid,
        hidden_pre,
        hidden,
    )
    return (result, kept)


def block_backward(kept, gains, biases, weights, grad_result):
    (
        resid_in,
        middle,
        normed_all,
        seg_all,
        query_h,
        key_h,
        value_h,
        log_sums,
        attn_rows,
        normed_mid,
        hidden_pre,
        hidden,
    ) = kept
    qkv_w, attn_w, up_w, down_w = weights
    grad_branch = spread_grads(grad_result.astype(jnp.bfloat16))
    grad_down = product_tn(hidden, grad_branch)
    grad_hidden = product_nt(grad_branch, down_w)
    _, gelu_back = jax.vjp(gelu_tanh, hidden_pre)
    grad_pre = gelu_back(grad_hidden)[0].astype(jnp.bfloat16)
    grad_up = product_tn(normed_mid, grad_pre)
    grad_norm_mid = combine_grads(product_nt(grad_pre, up_w))
    _, norm_back_mid = jax.vjp(layer_norm, middle, gains[1], biases[1])
    grad_mid_ln, grad_gain_mid, grad_bias_mid = norm_back_mid(grad_norm_mid)
    grad_middle = grad_result + grad_mid_ln
    grad_attn_all = spread_grads(grad_middle.astype(jnp.bfloat16))
    grad_attn = product_tn(attn_rows, grad_attn_all)
    grad_heads = split_heads(product_nt(grad_attn_all, attn_w).astype(jnp.bfloat16))
    grad_query, grad_key, grad_value = attend_back(
        query_h, key_h, value_h, seg_all, log_sums, grad_heads
    )
    grad_parts = [join_heads(grad_query), join_heads(grad_key), join_heads(grad_value)]
    grad_qkv = jnp.stack([product_tn(normed_all, grad_part) for grad_part in grad_parts])
    grad_normed_part = (
        product_nt(grad_parts[0], qkv_w[0])
        + product_nt(grad_parts[1], qkv_w[1])
        + product_nt(grad_parts[2], qkv_w[2])
    )
    grad_normed = combine_grads(grad_normed_part)
    _, norm_back_in = jax.vjp(layer_norm, resid_in, gains[0], biases[0])
    grad_in_ln, grad_gain_in, grad_bias_in = norm_back_in(grad_normed)
    gain_grads = jnp.stack([grad_gain_in, grad_gain_mid])
    bias_grads = jnp.stack([grad_bias_in, grad_bias_mid])
    return (
        grad_middle + grad_in_ln,
        gain_grads,
        bias_grads,
        (grad_qkv, grad_attn, grad_up, grad_down),
    )


def local(
    tokens,
    segment_ids,
    norm_gains,
    norm_biases,
    w_qkv,
    w_attn_out,
    w_up,
    w_down,
    w_vq_in,
    w_vq_out,
    codebook,
    cotangent,
):
    gain_sum = jnp.zeros(norm_gains.shape, jnp.float32)
    bias_sum = jnp.zeros(norm_biases.shape, jnp.float32)
    vq_in_sum = jnp.zeros(w_vq_in.shape, jnp.float32)
    vq_out_sum = jnp.zeros(w_vq_out.shape, jnp.float32)
    code_sum = jnp.zeros(codebook.shape, jnp.float32)
    layer_sums = [None, None]
    outputs = []
    input_grads = []
    for micro in range(MICRO):
        resid_in = tokens[micro].astype(jnp.float32)
        seg_local = segment_ids[micro]
        enc_weights = fetch_weights(w_qkv, w_attn_out, w_up, w_down, 0)
        encoded, enc_kept = block_forward(
            resid_in, seg_local, norm_gains[0:2], norm_biases[0:2], enc_weights
        )
        (decoder_in, _), vq_back = jax.vjp(
            quantize, encoded, norm_gains[2], norm_biases[2], w_vq_in, w_vq_out, codebook
        )
        dec_weights = fetch_weights(w_qkv, w_attn_out, w_up, w_down, 1)
        decoded, dec_kept = block_forward(
            decoder_in, seg_local, norm_gains[3:5], norm_biases[3:5], dec_weights
        )
        outputs.append(decoded)
        grad_dec_in, gains_dec, biases_dec, grads_dec = block_backward(
            dec_kept, norm_gains[3:5], norm_biases[3:5], dec_weights, cotangent[micro]
        )
        grad_encoded, grad_gain_vq, grad_bias_vq, grad_in_w, grad_out_w, grad_codes = vq_back(
            (grad_dec_in, jnp.ones((), jnp.float32))
        )
        grad_input, gains_enc, biases_enc, grads_enc = block_backward(
            enc_kept, norm_gains[0:2], norm_biases[0:2], enc_weights, grad_encoded
        )
        input_grads.append(grad_input)
        gain_sum = gain_sum + jnp.concatenate([gains_enc, grad_gain_vq[None], gains_dec], axis=0)
        bias_sum = bias_sum + jnp.concatenate([biases_enc, grad_bias_vq[None], biases_dec], axis=0)
        vq_in_sum = vq_in_sum + grad_in_w
        vq_out_sum = vq_out_sum + grad_out_w
        code_sum = code_sum + grad_codes
        for layer, grads in ((0, grads_enc), (1, grads_dec)):
            reduced = reduce_weight_grads(grads)
            if layer_sums[layer] is None:
                layer_sums[layer] = reduced
            else:
                layer_sums[layer] = jax.tree.map(jnp.add, layer_sums[layer], reduced)
    gain_tot, bias_tot, vq_in_tot, vq_out_tot, code_tot = lax.psum(
        (gain_sum, bias_sum, vq_in_sum, vq_out_sum, code_sum), ("dp", "tp")
    )
    return (
        jnp.stack(outputs),
        jnp.stack(input_grads),
        gain_tot,
        bias_tot[0:3],
        bias_tot[3:5],
        jnp.stack([layer_sums[0][0], layer_sums[1][0]]),
        jnp.stack([layer_sums[0][1], layer_sums[1][1]]),
        jnp.stack([layer_sums[0][2], layer_sums[1][2]]),
        jnp.stack([layer_sums[0][3], layer_sums[1][3]]),
        vq_in_tot,
        vq_out_tot,
        code_tot,
    )


def solution(mesh):
    n_dp, n_tp = mesh.shape["dp"], mesh.shape["tp"]
    fits = n_tp == MICRO and n_dp == 16
    return jax.shard_map(
        functools.partial(whole_groups, n_dp) if fits else local,
        mesh=mesh,
        in_specs=(
            P(None, ("dp", "tp"), None),
            P(None, ("dp", "tp")),
            P(),
            P(),
            P(None, None, "dp", "tp"),
            P(None, "tp", "dp"),
            P(None, "dp", "tp"),
            P(None, "tp", "dp"),
            P(),
            P(),
            P(),
            P(None, ("dp", "tp"), None),
        ),
        out_specs=(
            P(None, ("dp", "tp"), None),
            P(None, ("dp", "tp"), None),
            P(),
            P(),
            P(),
            P(None, None, "dp", "tp"),
            P(None, "tp", "dp"),
            P(None, "dp", "tp"),
            P(None, "tp", "dp"),
            P(),
            P(),
            P(),
        ),
        check_vma=False,
    )
```

```python
import functools

import jax
import jax.numpy as jnp
from jax import lax
from jax.experimental import pallas as pl
from jax.experimental.pallas import tpu as pltpu
from jax.sharding import PartitionSpec as P

HEAD_DIM = 64
MICRO = 2
bf16 = jnp.bfloat16
f32 = jnp.float32
highest = lax.Precision.HIGHEST
ln_eps = 1e-05
norm_eps = 1e-06
temper = 10.0
commit_weight = 64.0
gelu_coef = 0.7978845608028654
masked_score = -1e30
log2e = 1.4426950408889634
vmem_cap = 26 * 1024 * 1024


PLANE = ((0, 0), (0, 1), (1, 0), (1, 1))


def exchange(values, dp_xor, tp_xor, n_dp):
    pairs = [
        (d * 2 + t, (d ^ dp_xor) * 2 + (t ^ tp_xor)) for d in range(n_dp) for t in range(2)
    ]
    return lax.ppermute(values, ("dp", "tp"), pairs)


def spread_line(shard, n_dp):
    return [shard] + [exchange(shard, 4 * k, 0, n_dp) for k in range(1, 4)]


def plane_send(lows, n_dp):
    return [exchange(low, 2 * y, x, n_dp) for (y, x), low in zip(PLANE[1:], lows)]


def line_send(lows, n_dp):
    return [exchange(low, 4 * k, 0, n_dp) for k, low in zip(range(1, 4), lows)]


def dot(a, b):
    return jnp.dot(a, b, preferred_element_type=f32)


def dot_nt(a, b, precision=None):
    return lax.dot_general(
        a, b, (((1,), (1,)), ((), ())), preferred_element_type=f32, precision=precision
    )


def dot_full(a, b):
    return jnp.dot(a, b, preferred_element_type=f32, precision=highest)


def ln_parts(x):
    centred = x - jnp.mean(x, axis=-1, keepdims=True)
    inv = lax.rsqrt(jnp.mean(centred * centred, axis=-1, keepdims=True) + ln_eps)
    return centred * inv, inv


def ln_back(grad, xhat, inv, gain):
    scaled = grad * gain
    return inv * (
        scaled
        - jnp.mean(scaled, axis=-1, keepdims=True)
        - xhat * jnp.mean(scaled * xhat, axis=-1, keepdims=True)
    )


def split2(x):
    hi = x.astype(bf16)
    return hi, (x - hi.astype(f32)).astype(bf16)


def split3(x):
    hi, _ = split2(x)
    rest = x - hi.astype(f32)
    mid = rest.astype(bf16)
    return hi, mid, (rest - mid.astype(f32)).astype(bf16)


def order_matrix(dp, inverse):
    at = lax.broadcasted_iota(jnp.int32, (512, 512), 0 if inverse else 1)
    other = lax.broadcasted_iota(jnp.int32, (512, 512), 1 if inverse else 0)
    block = at >> 5
    bits = ((block & 3) << 2) | (((block >> 2) & 1) << 1) | (block >> 3)
    return jnp.where(other == (((dp ^ bits) << 5) | (at & 31)), 1.0, 0.0).astype(bf16)


def ordered(x, matrix):
    if x.dtype == bf16:
        return dot(x, matrix)
    hi, mid, lo = split3(x)
    return (dot(hi, matrix) + dot(mid, matrix)) + dot(lo, matrix)


def w_at(a, b, t, first, width):
    parts = []
    for core in range(2):
        for y in range(2):
            if first < 1536:
                part = a[2 * core + y][t, :, :, first : first + width]
            else:
                part = b[2 * core + t][y, :, :, first - 1536 : first - 1536 + width]
            parts.append(part.reshape(128, width))
    return jnp.concatenate(parts, axis=0)


def put_grad(refs, t, cols, value):
    for core, ref in enumerate(refs):
        for y in range(2):
            rows = value[core * 256 + y * 128 : core * 256 + (y + 1) * 128]
            ref[2 * y + t, :, :, cols] = rows.reshape(4, 32, rows.shape[1])


def start_all(copies):
    for copy in copies:
        copy.start()


def wait_all(copies):
    for copy in copies:
        copy.wait()


def head_rows(ref, pair, which):
    own = ref[pl.ds(pair * 128 + which * HEAD_DIM, HEAD_DIM), :]
    zero = jnp.zeros_like(own)
    return jnp.concatenate([own, zero] if which == 0 else [zero, own], axis=0)


def segment_mask(own, other):
    ids = jnp.concatenate([own[:, 512:640], other[:, 512:640]], axis=0).astype(f32)
    return jnp.where(ids[:, 0:1] == ids.T[0:1, :], 0.0, masked_score)


def load_rows(x, own, other):
    if x is None:
        return jnp.concatenate([own[:, :512], other[:, :512]], axis=0).astype(f32)
    return x[...]


def gain_of(norms, at):
    return norms[at : at + 1, :]


def bias_of(norms, at):
    return norms[8 + at : 9 + at, :]


def attn_fwd_kernel(with_x, at, own, other, norms, *refs):
    w, refs = refs[:4], refs[4:]
    x, refs = (refs[0], refs[1:]) if with_x else (None, refs)
    x1, lse, saved, refs = refs[0], refs[1], refs[2:8], refs[8:]
    h, vt, ot, mask, qs, k, v, o, qst, kt, out_sems = refs
    keeps = [
        pltpu.make_async_copy(held, to, out_sems.at[i])
        for i, (held, to) in enumerate(zip((qs, k, v, o, qst, kt), saved))
    ]
    xf = load_rows(x, own, other)
    h[...] = (ln_parts(xf)[0] * gain_of(norms, at) + bias_of(norms, at)).astype(bf16)
    mask[...] = segment_mask(own, other)
    for t in range(2):
        cols = slice(t * 256, (t + 1) * 256)
        q = dot(h[...], w_at(w, None, t, 0, 256)).astype(bf16)
        qs[:, cols] = (q * HEAD_DIM ** (-0.5)).astype(bf16)
        k[:, cols] = dot(h[...], w_at(w, None, t, 256, 256)).astype(bf16)
        v[:, cols] = dot(h[...], w_at(w, None, t, 512, 256)).astype(bf16)
    qst[...] = qs[...].T
    kt[...] = k[...].T
    vt[...] = v[...].T
    for i in (0, 1, 2, 4, 5):
        keeps[i].start()
    for pair in range(4):
        k_pair = k[:, pair * 128 : (pair + 1) * 128]
        for which in range(2):
            scores = dot(k_pair, head_rows(qst, pair, which)) + mask[...]
            top = jnp.max(scores, axis=0, keepdims=True)
            numer = jnp.exp(scores - top).astype(bf16)
            rows = pl.ds(pair * 128 + which * HEAD_DIM, HEAD_DIM)
            left = jnp.concatenate([vt[rows, :], jnp.ones((16, 512), bf16)], axis=0)
            both = dot(left, numer)
            total = both[HEAD_DIM : HEAD_DIM + 1, :]
            ot[rows, :] = (both[:HEAD_DIM, :] / total).astype(bf16)
            lse[pl.ds(pair * 2 + which, 1), :] = top + jnp.log(total)
    o[...] = ot[...].T
    keeps[3].start()
    acc = xf
    for t in range(2):
        acc = acc + dot_nt(o[:, t * 256 : (t + 1) * 256], w_at(w, None, t, 768, 256))
    x1[...] = acc
    wait_all(keeps)


def gelu_parts(u):
    square = u * u
    tanh = jnp.tanh(gelu_coef * u * (1.0 + 0.044715 * square))
    return 0.5 * u * (1.0 + tanh), tanh, square


def mlp_weights(w):
    def up(t, part):
        return w_at(w[:4], w[4:], t, 1024 + part * 512, 512)

    def down(t, part):
        return w_at(w[:4], w[4:], t, 2048 + part * 512, 512)

    return up, down


def mlp_rows(at, x, norms, w, h2):
    up, down = mlp_weights(w)
    h2[...] = (ln_parts(x)[0] * gain_of(norms, at) + bias_of(norms, at)).astype(bf16)
    for t in range(2):
        for part in range(2):
            hidden = gelu_parts(dot(h2[...], up(t, part)))[0].astype(bf16)
            x = x + dot_nt(hidden, down(t, part))
    return x


def mlp_bwd_kernel(split, at, ids, x1, norms, *refs):
    up, down = mlp_weights(refs[:8])
    refs = refs[8:]
    if split:
        own, other, refs = refs[0], refs[1], refs[2:]
    else:
        dy, refs = refs[0], refs[1:]
    dx1, small, grads = refs[0], refs[1], refs[2:4]
    h2, h2t, dyb, dybt, dh2 = refs[4:9]
    if split:
        dy = refs[9]
        dy[0:256, :] = ordered(own[ids[1]], order_matrix(ids[0], False))
        dy[256:, :] = other[:, 640:].astype(f32)
    h2[...] = (ln_parts(x1[...])[0] * gain_of(norms, at) + bias_of(norms, at)).astype(bf16)
    h2t[...] = h2[...].T
    dyb[...] = dy[...].astype(bf16)
    dybt[...] = dyb[...].T
    for t in range(2):
        for part in range(2):
            cols = slice(part * 512, (part + 1) * 512)
            w_up = up(t, part)
            pre = dot(h2[...], w_up)
            hidden, tanh, square = gelu_parts(pre)
            slope = 0.5 * (1.0 + tanh) + (0.5 * gelu_coef) * pre * (1.0 - tanh * tanh) * (
                1.0 + (3 * 0.044715) * square
            )
            dhidden = dot(dyb[...], down(t, part))
            dpre = (dhidden * slope).astype(bf16)
            out_cols = slice(1024 + part * 512, 1024 + (part + 1) * 512)
            put_grad(grads, t, out_cols, dot(dybt[...], hidden.astype(bf16)).astype(bf16))
            put_grad(grads, t, cols, dot(h2t[...], dpre).astype(bf16))
            more = dot_nt(dpre, w_up)
            if t + part == 0:
                dh2[...] = more
            else:
                dh2[...] += more
    xhat, inv = ln_parts(x1[...])
    grad = dh2[...]
    small[0:1, :] = jnp.sum(grad * xhat, axis=0, keepdims=True)
    small[1:2, :] = jnp.sum(grad, axis=0, keepdims=True)
    dx1[...] = dy[...] + ln_back(grad, xhat, inv, gain_of(norms, at))


def heads_back(low, w, saved, lse, mask, put_out, scratch):
    qs, k, v, o, qst, kt = saved
    flip, do, dot_t, dqt, dq, dk, dv = scratch
    flip[...] = low.T
    for t in range(2):
        cols = slice(t * 256, (t + 1) * 256)
        do[:, cols] = dot(low, w_at(w, None, t, 768, 256)).astype(bf16)
        put_out(t, dot(flip[...], o[:, cols]).astype(bf16))
    dot_t[...] = do[...].T
    first = lax.broadcasted_iota(jnp.int32, (512, 128), 1) < HEAD_DIM
    for pair in range(4):
        lanes = slice(pair * 128, (pair + 1) * 128)
        dvs, dks = [], []
        for which in range(2):
            head = pair * 2 + which
            rows = pl.ds(head * HEAD_DIM, HEAD_DIM)
            scores = dot(k[:, lanes], head_rows(qst, pair, which)) + mask[...]
            probs = jnp.exp(scores - lse[head : head + 1, :])
            dprobs = dot(v[:, lanes], head_rows(dot_t, pair, which))
            shift = jnp.sum(probs * dprobs, axis=0, keepdims=True)
            dscore = (probs * (dprobs - shift)).astype(bf16)
            dvs.append(dot(probs.astype(bf16), do[:, lanes]))
            dks.append(dot(dscore, qs[:, lanes]))
            dqt[rows, :] = (dot(kt[rows, :], dscore) * HEAD_DIM ** (-0.5)).astype(bf16)
        dv[:, lanes] = jnp.where(first, dvs[0], dvs[1]).astype(bf16)
        dk[:, lanes] = jnp.where(first, dks[0], dks[1]).astype(bf16)
    dq[...] = dqt[...].T


def rows_back(at, xf, norms, w, parts, small, grads, h, flip):
    h[...] = (ln_parts(xf)[0] * gain_of(norms, at) + bias_of(norms, at)).astype(bf16)
    flip[...] = h[...].T
    grad = jnp.zeros((512, 512), f32)
    for t in range(2):
        cols = slice(t * 256, (t + 1) * 256)
        for index, part in enumerate(parts):
            w_cols = slice(index * 256, (index + 1) * 256)
            put_grad(grads, t, w_cols, dot(flip[...], part[:, cols]).astype(bf16))
            grad = grad + dot_nt(part[:, cols], w_at(w, None, t, index * 256, 256))
    xhat, inv = ln_parts(xf)
    small[0:1, :] = jnp.sum(grad * xhat, axis=0, keepdims=True)
    small[1:2, :] = jnp.sum(grad, axis=0, keepdims=True)
    return ln_back(grad, xhat, inv, gain_of(norms, at))


def take_saved(saved, held, sems):
    copies = [
        pltpu.make_async_copy(a, b, sems.at[i]) for i, (a, b) in enumerate(zip(saved, held))
    ]
    start_all(copies)
    return copies


def attn_bwd_kernel(at, own, other, dx1, norms, lse, *refs):
    w, saved, x, refs = refs[:4], refs[4:10], refs[10], refs[11:]
    dx, small, grads = refs[0], refs[1], refs[2:4]
    mask, h, held, scratch, sems = refs[4], refs[5], refs[6:12], refs[12:19], refs[19]
    copies = take_saved(saved, held, sems)
    mask[...] = segment_mask(own, other)
    low = dx1[...].astype(bf16)
    wait_all(copies)

    def put_out(t, value):
        put_grad(grads, t, slice(768, 1024), value)

    heads_back(low, w, held, lse, mask, put_out, scratch)
    dx[...] = dx1[...] + rows_back(
        at, x[...], norms, w, scratch[4:], small, grads, h, scratch[0]
    )


def heads_bwd_kernel(own, other, dx1, lse, *refs):
    w, saved, refs = refs[:4], refs[4:10], refs[10:]
    parts, grads, mask, held = refs[:3], refs[3:5], refs[5], refs[6:12]
    scratch, sems = (*refs[12:16], *parts), refs[16]
    copies = take_saved(saved, held, sems)
    mask[...] = segment_mask(own, other)
    low = dx1[...].astype(bf16)
    wait_all(copies)

    def put_out(t, value):
        put_grad(grads, t, slice(0, 256), value)

    heads_back(low, w, held, lse, mask, put_out, scratch)


def rows_bwd_kernel(
    ids, own, other, dx1, norms, dq, dk, dv, out_0, out_1, other_small, d_x1, *refs
):
    w, d_w, (dx, dx_low, y, y_low), grads, (small, h, flip) = (
        refs[:4],
        refs[4:12],
        refs[12:16],
        refs[16:18],
        refs[18:],
    )
    total = dx1[...] + rows_back(
        0, load_rows(None, own, other), norms, w, (dq, dk, dv), small, grads, h, flip
    )
    dx[...] = total[:256, :]
    dx_low[...] = total[256:, :].astype(bf16)
    rows = jnp.concatenate([small[0:2, :], other_small[0:2, :], jnp.zeros((4, 512), f32)], axis=0)
    packed = pack_rows(ordered(rows, order_matrix(ids[0], True)))
    for grad, part in zip(grads, (out_0, out_1)):
        for i in range(4):
            for z in range(4):
                grad[i, z, :, 768:1024] = part[i, z]
                grad[i, z, :, 1024:1152] = packed
    rows = mlp_rows(4, d_x1[...], norms, d_w, h)
    y[...] = rows[:256, :]
    y_low[...] = rows[256:, :].astype(bf16)


def pack_rows(rows):
    cut = [rows[i : i + 1, 128 * j : 128 * (j + 1)] for i in range(4) for j in range(4)]
    return jnp.concatenate(split2(jnp.concatenate(cut, axis=0)), axis=0)


def code_prep_kernel(book_t, stack, stack_t):
    def one_chunk(index, _):
        lanes = pl.ds(pl.multiple_of(index * 512, 512), 512)
        rows = book_t[:, lanes]
        unit = rows * lax.rsqrt(jnp.sum(rows * rows, axis=0, keepdims=True) + norm_eps)
        hi, mid, lo = split3(unit)
        stack_t[:, lanes] = jnp.concatenate([hi, mid, lo, jnp.ones((32, 512), bf16)], axis=0)
        tall = jnp.concatenate([hi, mid, lo, hi, mid, hi, jnp.zeros((64, 512), bf16)], axis=0)
        stack[lanes, :] = tall.T
        return 0

    lax.fori_loop(0, book_t.shape[1] // 512, one_chunk, 0)


def factor_stack(x):
    hi, mid, lo = split3(x)
    return jnp.concatenate([hi, hi, hi, mid, mid, lo, jnp.zeros((64, x.shape[1]), bf16)], axis=0)


def code_loads(pairs, sems):
    loads = []
    for piece in range(4):
        group = []
        for at, (held, to, by_row) in enumerate(pairs):
            size = held.shape[0 if by_row else 1] // 4
            part = pl.ds(piece * size, size)
            place = (part, slice(None)) if by_row else (slice(None), part)
            group.append(pltpu.make_async_copy(held.at[place], to.at[place], sems.at[at, piece]))
        start_all(group)
        loads.append(group)
    return loads


def mlp_vq_kernel(x1, norms, vq_w, stack_hbm, stack_t_hbm, *refs):
    w, (e, u, kept, numer_hbm, h2, acc, stack, stack_t, numer, sems, out_sems) = refs[:8], refs[8:]
    loads = code_loads([(stack_hbm, stack, True), (stack_t_hbm, stack_t, False)], sems)
    e[...] = mlp_rows(1, x1[...], norms, w, h2)
    lnv = ln_parts(e[...])[0] * gain_of(norms, 2) + bias_of(norms, 2)
    raw = dot_nt(vq_w[0:32, :], lnv, highest)
    inv = lax.rsqrt(jnp.sum(raw * raw, axis=0, keepdims=True) + norm_eps)
    latent = raw * inv
    right = factor_stack(latent * (temper * log2e))
    chunks, keeps = stack.shape[0] // 2048, []
    for piece, group in enumerate(loads):
        wait_all(group)
        for part in range(piece * chunks // 4, (piece + 1) * chunks // 4):
            numers = []
            for index in range(4 * part, 4 * part + 4):
                codes = slice(index * 512, (index + 1) * 512)
                numers.append(jnp.exp2(dot(stack[codes, :], right)).astype(bf16))
            if part > 1:
                keeps[part - 2].wait()
            keeps.append(
                pltpu.make_async_copy(
                    numer.at[part % 2],
                    numer_hbm.at[pl.ds(part * 2048, 2048), :],
                    out_sems.at[part % 2],
                )
            )
            numer[part % 2] = jnp.concatenate(numers, axis=0)
            keeps[part].start()
            sums = dot(stack_t[:, part * 2048 : (part + 1) * 2048], numer[part % 2])
            if part == 0:
                acc[...] = sums
            else:
                acc[...] += sums
    total = acc[96:97, :]
    soft = (acc[0:32, :] + acc[32:64, :] + acc[64:96, :]) / total
    kept[0:32, :] = latent
    kept[32:64, :] = soft
    kept[64:65, :] = total
    kept[65:66, :] = inv
    u[...] = dot_full(soft.T, vq_w[32:64, :])
    wait_all(keeps[-2:])


def vq_bwd_kernel(
    ids, e, du, norms, vq_w, stack_hbm, stack_t_hbm, book_hbm, numer_hbm, kept, *refs
):
    small0, small1, de, code_keep, code_send = refs[:5]
    acc, grads, small, tail, stack, stack_t, book_t, numer, load_sems, sems = refs[5:]
    loads = code_loads(
        [
            (stack_hbm, stack, True),
            (numer_hbm, numer, True),
            (stack_t_hbm, stack_t, False),
            (book_hbm, book_t, False),
        ],
        load_sems,
    )
    xhat, inv_ln = ln_parts(e[...])
    lnv = xhat * gain_of(norms, 2) + bias_of(norms, 2)
    latent, soft = kept[0:32, :], kept[32:64, :]
    total, inv = kept[64:65, :], kept[65:66, :]
    direct = (2.0 * 1.25 * commit_weight) * (latent - soft)
    dsoft = dot_nt(vq_w[32:64, :], du[...], highest) - direct
    small[32:64, :] = dot_full(soft, du[...])
    shift = jnp.sum(dsoft * soft, axis=0, keepdims=True) / total
    dsoft = dsoft / total
    right = factor_stack(dsoft)
    pads = jnp.zeros((64, 512), f32)

    def tall(x):
        hi, lo = split2(x)
        return jnp.concatenate([hi.astype(f32), lo.astype(f32), pads], axis=0).T.astype(bf16)

    sides = jnp.concatenate([tall(dsoft), tall(latent * temper)], axis=0)
    chunks = stack.shape[0] // 2048
    for piece, group in enumerate(loads):
        wait_all(group)
        for part in range(piece * chunks // 4, (piece + 1) * chunks // 4):
            dlogits = []
            for index in range(4 * part, 4 * part + 4):
                codes = slice(index * 512, (index + 1) * 512)
                held = numer[codes, :]
                dlogit = (held.astype(f32) * (dot(stack[codes, :], right) - shift)).astype(bf16)
                dlogits.append(dlogit)
                sums = jnp.concatenate([held, dlogit], axis=1)
                dcode = dot(sums, sides).T
                dcode = dcode[0:32, :] + dcode[32:64, :]
                rows = book_t[:, codes]
                scale = lax.rsqrt(jnp.sum(rows * rows, axis=0, keepdims=True) + norm_eps)
                unit = rows * scale
                grads[:, codes] = (
                    scale * (dcode - unit * jnp.sum(unit * dcode, axis=0, keepdims=True))
                ).astype(bf16)
            sums = dot(
                stack_t[0:96, part * 2048 : (part + 1) * 2048], jnp.concatenate(dlogits, axis=0)
            )
            if part == 0:
                acc[...] = sums
            else:
                acc[...] += sums
    dlatent = temper * (acc[0:32, :] + acc[32:64, :] + acc[64:96, :]) + direct
    draw = inv * (dlatent - latent * jnp.sum(latent * dlatent, axis=0, keepdims=True))
    small[0:32, :] = dot_full(draw, lnv)
    dln = dot_full(draw.T, vq_w[0:32, :])
    small[64:65, :] = jnp.sum(dln * xhat, axis=0, keepdims=True)
    small[65:66, :] = jnp.sum(dln, axis=0, keepdims=True)
    small[66:68, :] = small0[0:2, :]
    small[68:70, :] = small1[0:2, :]
    small[70:96, :] = jnp.zeros((26, 512), f32)
    small[...] = ordered(small[...], order_matrix(ids[0], True))
    for block in range(3):
        for at, part in enumerate(split2(small[block * 32 : (block + 1) * 32, :])):
            for side in range(2):
                tail[block * 2 + side, :, at * 256 : (at + 1) * 256] = part[
                    :, side * 256 : (side + 1) * 256
                ]
    tail[6:8] = jnp.zeros((2, 32, 512), bf16)
    core, z = ids[0] % 2, ids[0] // 4
    copies = []
    for slot, (at, to) in enumerate(((core, code_keep), (1 - core, code_send))):
        for k in range(4):
            part = at * 4 + (z ^ k)
            lanes = pl.ds(pl.multiple_of(part * 1024, 1024), 1024)
            copies += [
                pltpu.make_async_copy(
                    grads.at[:, lanes], to.at[k, :, pl.ds(0, 1024)], sems.at[0, slot, k]
                ),
                pltpu.make_async_copy(
                    tail.at[part], to.at[k, :, pl.ds(1024, 512)], sems.at[1, slot, k]
                ),
            ]
    for copy in copies:
        copy.start()
    de[...] = ln_back(dln, xhat, inv_ln, gain_of(norms, 2))
    for copy in copies:
        copy.wait()


SMEM = pl.BlockSpec(memory_space=pltpu.SMEM)
VMEM = pl.BlockSpec(memory_space=pltpu.VMEM)
ANY = pl.BlockSpec(memory_space=pl.ANY)


def shaped(*pairs):
    return [jax.ShapeDtypeStruct(shape, dtype) for shape, dtype in pairs]


def pin(array):
    return pltpu.with_memory_space_constraint(array, pltpu.HBM)


def call(kernel, name, in_specs, out_specs, outs, scratch, flops, after=(), carry=()):
    n_in, n_extra, n_out = len(in_specs), len(after) + len(carry), len(outs)

    def body(*refs):
        first = n_in + n_extra
        kernel(*refs[:n_in], *refs[first : first + n_out], *refs[first + n_out + len(carry) :])

    made = pl.pallas_call(
        body,
        name=name,
        in_specs=in_specs + [ANY] * n_extra,
        out_specs=out_specs + [ANY] * len(carry),
        out_shape=outs + [jax.ShapeDtypeStruct(a.shape, a.dtype) for a in carry],
        scratch_shapes=scratch,
        input_output_aliases={n_in + len(after) + i: n_out + i for i in range(len(carry))},
        compiler_params=pltpu.CompilerParams(vmem_limit_bytes=vmem_cap),
        cost_estimate=pl.CostEstimate(flops=flops, bytes_accessed=10**6, transcendentals=0),
    )

    def run(*args):
        res = made(*args, *after, *carry)
        return (*res[:n_out], list(res[n_out:]))

    return run


DMA = pltpu.SemaphoreType.DMA
ROWS2 = (512, 512)


def attn_fwd(at, marked, xs, norms, w, after=(), carry=()):
    outs = shaped((ROWS2, f32), ((8, 512), f32)) + [pltpu.HBM(ROWS2, bf16)] * 6
    scratch = [
        *[pltpu.VMEM(ROWS2, bf16)] * 3,
        pltpu.VMEM(ROWS2, f32),
        *[pltpu.VMEM(ROWS2, bf16)] * 6,
        DMA((6,)),
    ]
    x1, lse, *saved, carried = call(
        functools.partial(attn_fwd_kernel, bool(xs), at),
        "attn_fwd",
        [VMEM] * (7 + len(xs)),
        [VMEM] * 2 + [ANY] * 6,
        outs,
        scratch,
        10**10,
        after,
        carry,
    )(*marked, norms, *w[:4], *xs)
    return x1, (lse, *saved), carried


def mlp_bwd(at, ids, x1, dys, norms, w, after=(), carry=()):
    scratch = [
        *[pltpu.VMEM(ROWS2, bf16)] * 4,
        *[pltpu.VMEM(ROWS2, f32)] * len(dys),
    ]
    return call(
        functools.partial(mlp_bwd_kernel, len(dys) == 2, at),
        "mlp_bwd",
        [SMEM] + [VMEM] * (10 + len(dys)),
        [VMEM] * 4,
        shaped((ROWS2, f32), ((8, 512), f32), *[((4, 4, 32, 2048), bf16)] * 2),
        scratch,
        15 * 10**9,
        after,
        carry,
    )(ids, x1, norms, *w, *dys)


def attn_bwd(at, marked, x, dx1, norms, saved, w, after=(), carry=()):
    scratch = [pltpu.VMEM(ROWS2, f32), *[pltpu.VMEM(ROWS2, bf16)] * 14, DMA((6,))]
    outs = shaped((ROWS2, f32), ((8, 512), f32), *[((4, 4, 32, 1024), bf16)] * 2)
    return call(
        functools.partial(attn_bwd_kernel, at),
        "attn_bwd",
        [VMEM] * 9 + [ANY] * 6 + [VMEM],
        [VMEM] * 4,
        outs,
        scratch,
        15 * 10**9,
        after,
        carry,
    )(*marked, dx1, norms, saved[0], *w[:4], *map(pin, saved[1:]), x)


def heads_bwd(marked, dx1, saved, w, after=(), carry=()):
    scratch = [pltpu.VMEM(ROWS2, f32), *[pltpu.VMEM(ROWS2, bf16)] * 10, DMA((6,))]
    outs = shaped(*[(ROWS2, bf16)] * 3, *[((4, 4, 32, 256), bf16)] * 2)
    return call(
        heads_bwd_kernel,
        "heads_bwd",
        [VMEM] * 8 + [ANY] * 6,
        [VMEM] * 5,
        outs,
        scratch,
        10 * 10**9,
        after,
        carry,
    )(*marked, dx1, saved[0], *w[:4], *map(pin, saved[1:]))


def rows_bwd(ids, marked, dx1, norms, parts, other_small, d_x1, w, d_w, after=(), carry=()):
    scratch = [pltpu.VMEM((8, 512), f32), *[pltpu.VMEM(ROWS2, bf16)] * 2]
    outs = shaped(*[((256, 512), f32), ((256, 512), bf16)] * 2, *[((4, 4, 32, 1152), bf16)] * 2)
    return call(
        rows_bwd_kernel,
        "rows_bwd",
        [SMEM] + [VMEM] * 23,
        [VMEM] * 6,
        outs,
        scratch,
        10 * 10**9,
        after,
        carry,
    )(ids, *marked, dx1, norms, *parts, other_small, d_x1, *w[:4], *d_w)


def code_prep(book_t, after=(), carry=()):
    codes = book_t.shape[1]
    return call(
        code_prep_kernel,
        "code_prep",
        [VMEM],
        [VMEM] * 2,
        shaped(((codes, 256), bf16), ((128, codes), bf16)),
        [],
        6 * 10**9,
        after,
        carry,
    )(book_t)


def mlp_vq(x1, norms, vq_w, stack, stack_t, w, after=(), carry=()):
    return call(
        mlp_vq_kernel,
        "mlp_vq",
        [VMEM] * 3 + [ANY] * 2 + [VMEM] * 8,
        [VMEM] * 3 + [ANY],
        shaped((ROWS2, f32), (ROWS2, f32), ((72, 512), f32))
        + [pltpu.HBM((stack.shape[0], 512), bf16)],
        [
            pltpu.VMEM(ROWS2, bf16),
            pltpu.VMEM((128, 512), f32),
            pltpu.VMEM(stack.shape, bf16),
            pltpu.VMEM(stack_t.shape, bf16),
            pltpu.VMEM((2, 2048, 512), bf16),
            DMA((2, 4)),
            DMA((2,)),
        ],
        25 * 10**9,
        after,
        carry,
    )(x1, norms, vq_w, pin(stack), pin(stack_t), *w)


def vq_bwd(ids, e, du, norms, vq_w, codes, kept, smalls, after=(), carry=()):
    scratch = [
        pltpu.VMEM((96, 512), f32),
        pltpu.VMEM(codes[2].shape, bf16),
        pltpu.VMEM((96, 512), f32),
        pltpu.VMEM((8, 32, 512), bf16),
        *[pltpu.VMEM(a.shape, a.dtype) for a in codes],
        DMA((4, 4)),
        DMA((2, 2, 4)),
    ]
    return call(
        vq_bwd_kernel,
        "vq_bwd",
        [SMEM] + [VMEM] * 4 + [ANY] * 4 + [VMEM] * 3,
        [VMEM] + [ANY] * 2,
        shaped((ROWS2, f32), *[((4, 32, 1536), bf16)] * 2),
        scratch,
        25 * 10**9,
        after,
        carry,
    )(ids, e, du, norms, vq_w, *map(pin, codes), kept, *smalls)


def lines_kernel(cuts, *refs):
    first = 0
    for out, width in zip(refs[4:], cuts):
        for k in range(4):
            out[k] = refs[k][:, first : first + width]
        first += width


def stack_lines(shards, cuts, after=(), carry=()):
    return call(
        functools.partial(lines_kernel, cuts),
        "stack_lines",
        [VMEM] * 4,
        [VMEM] * len(cuts),
        shaped(*[((4, 32, width), bf16) for width in cuts]),
        [],
        1,
        after,
        carry,
    )(*shards)


def pack_kernel(*refs):
    hbm, outs, held, sems = refs[:4], refs[4:6], refs[6:10], refs[10]
    copies = [pltpu.make_async_copy(hbm[at], held[at], sems.at[at]) for at in range(4)]
    start_all(copies)
    wait_all(copies)
    qkv, out_t, up, down_t = held
    for layer, out in enumerate(outs):
        for index in range(3):
            out[:, index * 256 : (index + 1) * 256] = qkv[layer, index]
        out[:, 768:1024] = out_t[layer]
        out[:, 1024:2048] = up[layer]
        out[:, 2048:] = down_t[layer]


def pack_weights(*arrays):
    return call(
        pack_kernel,
        "pack_weights",
        [ANY] * 4,
        [VMEM] * 2,
        shaped(*[((32, 3072), bf16)] * 2),
        [*[pltpu.VMEM(a.shape, a.dtype) for a in arrays], DMA((4,))],
        1,
    )(*map(pin, arrays))[:-1]


def pairs_kernel(*refs):
    count = len(refs) // 3
    for at in range(count):
        refs[2 * count + at][0] = refs[2 * at][...]
        refs[2 * count + at][1] = refs[2 * at + 1][...]


def stack_pairs(pairs, after=(), carry=()):
    return call(
        pairs_kernel,
        "stack_pairs",
        [VMEM] * (2 * len(pairs)),
        [VMEM] * len(pairs),
        shaped(*[((2, *a.shape), bf16) for a, _ in pairs]),
        [],
        1,
        after,
        carry,
    )(*[array for pair in pairs for array in pair])


def gate(after, carry):
    def kernel(out):
        out[...] = jnp.zeros_like(out)

    return call(kernel, "gate", [], [VMEM], shaped(((8, 128), f32)), [], 1, after, carry)()[-1]


def rows_in_kernel(ids, *refs):
    hbm, (own, send, norms, vq_w), held, sems = refs[:7], refs[7:11], refs[11:18], refs[18]
    copies = [pltpu.make_async_copy(hbm[at], held[at], sems.at[at]) for at in range(7)]
    start_all(copies)
    matrix = order_matrix(ids[0], False)
    wait_all(copies)
    tokens, segs, cot, gains, biases, in_t, out_w = held
    for to, micro in ((send, 1 - ids[1]), (own, ids[1])):
        to[:, :512] = ordered(tokens[micro], matrix).astype(bf16)
        ids_row = segs[pl.ds(micro, 1), :].astype(f32)
        to[:, 512:640] = jnp.broadcast_to(ids_row, (128, 256)).T.astype(bf16)
    send[:, 640:] = ordered(cot[1 - ids[1]].astype(bf16), matrix).astype(bf16)
    pad = jnp.zeros((3, 512), f32)
    rows = jnp.concatenate([gains[...], pad, biases[...], pad], axis=0)
    norms[...] = ordered(rows, matrix)
    vq_w[...] = ordered(jnp.concatenate([in_t[...], out_w[...]], axis=0), matrix)


def rows_in(ids, *arrays):
    outs = shaped(
        ((256, 640), bf16), ((256, 1152), bf16), ((16, 512), f32), ((64, 512), f32)
    )
    return call(
        rows_in_kernel,
        "rows_in",
        [SMEM] + [ANY] * 7,
        [VMEM] * 4,
        outs,
        [*[pltpu.VMEM(a.shape, a.dtype) for a in arrays], DMA((7,))],
        1,
    )(ids, *map(pin, arrays))[:-1]


def joined(block):
    return block[0:16, 1024:].astype(f32) + block[16:32, 1024:].astype(f32)


def put_small(value, own, blocks):
    hi, lo = split2(value)
    own[0:16, 1024:] = hi.astype(f32) + lo.astype(f32)
    for block in blocks:
        block[0:16, 1024:] = hi
        block[16:32, 1024:] = lo


def near_kernel(ids, ins, outs):
    keep, other = ins
    for i in range(4):
        outs[i][...] = (keep[i].astype(f32) + other[i].astype(f32)).astype(outs[i].dtype)
    if keep.shape[3] == 1152:
        value = joined(keep.at[0, 0]) + joined(other.at[0, 0])
        put_small(value, outs[0].at[0], [out.at[0] for out in outs[1:]])


def near_task(keep, other):
    shape = keep.shape[1:]
    return near_kernel, [keep, other], shaped((shape, f32), *[(shape, bf16)] * 3)


def put_code(ref, first, code):
    for i in range(3):
        ref[first + i] = code[:, 1024 * i : 1024 * (i + 1)]


def get_code(ref, first):
    return jnp.concatenate([ref[first + i] for i in range(3)], axis=1)


def swapped(code):
    return jnp.concatenate([code[:, 1536:], code[:, :1536]], axis=1)


def code_sum(a, b):
    done = []
    for first in range(0, a.shape[1], 1536):
        total = a[:, first : first + 1024].astype(f32) + b[:, first : first + 1024].astype(f32)
        small = [
            x[:, first + 1024 : first + 1280].astype(f32) + x[:, first + 1280 : first + 1536].astype(f32)
            for x in (a, b)
        ]
        done += [total.astype(bf16), *split2(small[0] + small[1])]
    return jnp.concatenate(done, axis=1)


def fork_kernel(ids, ins, outs):
    keep, other = ins
    own_a, to_x, own_b, to_y = outs
    half = keep.shape[3] // 2
    for at, (own, send, kept, sent) in enumerate(
        ((own_a, to_x, (0, 2), (1, 3)), (own_b, to_y, (0, 1), (2, 3)))
    ):
        cols = slice(half * at, half * (at + 1))
        for j in range(2):
            own[j] = keep[kept[j], :, :, cols].astype(f32) + other[kept[j], :, :, cols].astype(f32)
            total = keep[sent[j], :, :, cols].astype(f32) + other[sent[j], :, :, cols].astype(f32)
            send[4 * j : 4 * (j + 1)] = total.astype(bf16)


def fork_task(keep, other):
    half = keep.shape[3] // 2
    outs = shaped(*[((2, 4, 32, half), f32), ((8, 32, half), bf16)] * 2)
    return fork_kernel, [keep, other], outs


def half_kernel(ids, ins, outs):
    own_a, from_x, own_b, from_y = ins[:4]
    kept_a, to_y, kept_b, to_x = outs[:4]
    for own, other, kept, send in (
        (own_a, from_x, kept_a, to_y),
        (own_b, from_y, kept_b, to_x),
    ):
        kept[...] = own[0] + other[0:4].astype(f32)
        send[0:4] = (own[1] + other[4:8].astype(f32)).astype(bf16)
    if len(ins) == 6:
        code, code_other = ins[4:]
        outs[4][...] = code_sum(code[...], swapped(code_other[...]))
        put_code(to_x, 4, outs[4])


def half_task(own_a, from_x, own_b, from_y, *codes):
    width = own_a.shape[3]
    outs = shaped(
        ((4, 32, width), f32),
        ((4, 32, width), bf16),
        ((4, 32, width), f32),
        ((7 if codes else 4, 32, width), bf16),
        *[(code.shape, bf16) for code in codes[:1]],
    )
    return half_kernel, [own_a, from_x, own_b, from_y, *codes], outs


def join_kernel(ids, ins, outs):
    kept, send = outs[:2]
    width = ins[0].shape[2]
    for at, (own, other) in enumerate((ins[0:2], ins[2:4])):
        cols = slice(width * at, width * (at + 1))
        for k in range(2):
            kept[k, :, cols] = own[2 * k] + other[2 * k].astype(f32)
            send[k, :, cols] = (own[2 * k + 1] + other[2 * k + 1].astype(f32)).astype(bf16)
    if len(ins) == 5:
        outs[2][...] = code_sum(ins[4][...], get_code(ins[3], 4))


def join_task(own_a, from_y, own_b, from_x, *codes):
    width = 2 * own_a.shape[2]
    outs = shaped(
        ((2, 32, width), f32),
        ((2, 32, width), bf16),
        *[(code.shape, bf16) for code in codes],
    )
    return join_kernel, [own_a, from_y, own_b, from_x, *codes], outs


def line_step_kernel(ids, ins, outs):
    kept, other = ins
    outs[0][...] = kept[0] + other[0].astype(f32)
    outs[1][...] = (kept[1] + other[1].astype(f32)).astype(bf16)


def line_step_task(kept, other):
    shape = kept.shape[1:]
    return line_step_kernel, [kept, other], shaped((shape, f32), (shape, bf16))


def plane_line_kernel(ids, ins, outs):
    kept, send = outs
    for k in range(4):
        total = ins[0][k]
        for other in ins[1:]:
            total = total + other[k].astype(f32)
        to = send if k % 2 else kept
        to[k // 2] = total.astype(to.dtype)
    x, y, xy = [joined(other.at[0]) for other in ins[1:]]
    put_small((ins[0][0, 0:16, 1024:] + x) + (y + xy), kept.at[0], [send.at[0]])


def plane_line_task(own, others):
    outs = shaped(((2, 32, 1152), f32), ((2, 32, 1152), bf16))
    return plane_line_kernel, [own, *others], outs


def small_step_kernel(ids, ins, outs):
    kept, other = ins
    line_step_kernel(ids, ins, outs)
    put_small(kept[0, 0:16, 1024:] + joined(other.at[0]), outs[0], [outs[1]])


def small_step_task(kept, other):
    shape = kept.shape[1:]
    return small_step_kernel, [kept, other], shaped((shape, f32), (shape, bf16))


def line_total(ins, width):
    total = ins[0][:, :width]
    for other in ins[1:]:
        total = total + other[:, :width].astype(f32)
    return total


def rows_out_kernel(ids, ins, outs):
    y, y_low, dx, dx_low = ins
    matrix = order_matrix(ids[0], True)
    outs[0][...] = ordered(y[...], matrix)
    outs[1][...] = ordered(dx[...], matrix)
    outs[2][0:256, :] = y_low[...]
    outs[2][256:, :] = dx_low[...]


def rows_out_task(y, y_low, dx, dx_low):
    outs = shaped((y.shape, f32), (dx.shape, f32), (ROWS2, bf16))
    return rows_out_kernel, [y, y_low, dx, dx_low], outs


def rows_kernel(ids, ins, outs):
    y, dx, others = ins
    moved = ordered(others[...], order_matrix(ids[0], True))
    for at, (out, own) in enumerate(zip(outs, (y, dx))):
        out[ids[1]] = own[...]
        out[1 - ids[1]] = moved[256 * at : 256 * (at + 1), :]


def rows_task(y, dx, others):
    return rows_kernel, [y, dx, others], shaped(*[((2, 256, 512), f32)] * 2)


def code_near_kernel(ids, ins, outs):
    keep, other = ins
    for at, out in enumerate(outs):
        for i in range(2):
            out[:, 1536 * i : 1536 * (i + 1)] = code_sum(keep[2 * at + i], other[2 * at + i])


def code_near_task(keep, other):
    return code_near_kernel, [keep, other], shaped(*[((32, 3072), bf16)] * 2)


def code_add_kernel(ids, ins, outs):
    outs[0][...] = code_sum(ins[0][...], ins[1][...])


def code_add_task(a, b):
    return code_add_kernel, [a, b], shaped((a.shape, bf16))


def code_pair_kernel(ids, ins, outs):
    for at, part in enumerate(ins):
        outs[0][:, 3072 * at : 3072 * (at + 1)] = part[...]


def code_pair_task(a, b):
    return code_pair_kernel, [a, b], shaped(((32, 6144), bf16))


def finish_kernel(ids, ins, outs):
    mlp, attn, d_mlp, d_attn, code, code_other = ins[:2], ins[2:4], ins[4:6], ins[6:8], *ins[8:]
    qkv, out_t, up, down_t, book, vq_in, vq_out, gains, biases, dec_biases, small_ref = outs
    for layer, rows in enumerate((line_total(mlp, 2048), line_total(d_mlp, 2048))):
        up[layer] = rows[:, :1024]
        down_t[layer] = rows[:, 1024:]
    for layer, rows in enumerate((line_total(attn, 1024), line_total(d_attn, 1024))):
        for index in range(3):
            qkv[layer, index] = rows[:, index * 256 : (index + 1) * 256]
        out_t[layer] = rows[:, 768:]
    core, z = ids[0] % 2, ids[0] // 4
    for at, parts in ((core, code), (1 - core, code_other)):
        for k in range(4):
            part = at * 4 + (z ^ k)
            held = parts[:, 1536 * k : 1536 * (k + 1)].astype(f32)
            book[:, pl.ds(pl.multiple_of(part * 1024, 1024), 1024)] = held[:, :1024]
            small_ref[:, pl.ds(pl.multiple_of(part * 256, 256), 256)] = (
                held[:, 1024:1280] + held[:, 1280:1536]
            )
    small = small_ref[...]
    vq_in[...] = small[:, :512]
    vq_out[...] = small[:, 512:1024]
    rest = small[:, 1024:1536]
    packed = attn[0][0:16, 1024:] + joined(attn[1])
    for row, out in enumerate((gains.at[0:1], biases.at[0:1], gains.at[1:2], biases.at[1:2])):
        for j in range(4):
            out[:, 128 * j : 128 * (j + 1)] = packed[row * 4 + j : row * 4 + j + 1, :]
    gains[2:3, :] = rest[0:1, :]
    biases[2:3, :] = rest[1:2, :]
    gains[3:4, :] = rest[2:3, :]
    dec_biases[0:1, :] = rest[3:4, :]
    gains[4:5, :] = rest[4:5, :]
    dec_biases[1:2, :] = rest[5:6, :]


def finish_task(mlp, attn, d_mlp, d_attn, code, code_other):
    outs = shaped(
        ((2, 3, 32, 256), f32),
        ((2, 32, 256), f32),
        ((2, 32, 1024), f32),
        ((2, 32, 1024), f32),
        ((32, 8192), f32),
        ((32, 512), f32),
        ((32, 512), f32),
        ((5, 512), f32),
        ((3, 512), f32),
        ((2, 512), f32),
        ((32, 2048), f32),
    )
    ins = [*mlp, *attn, *d_mlp, *d_attn, code, code_other]
    return finish_kernel, ins, outs


def run_tasks(ids, name, tasks, after=(), carry=()):
    sizes = [(len(ins), len(outs)) for _, ins, outs in tasks]
    n_in = sum(i for i, _ in sizes)

    def kernel(ids_ref, *refs):
        at_in, at_out = 0, n_in
        for (fn, _, _), (i, o) in zip(tasks, sizes):
            fn(ids_ref, refs[at_in : at_in + i], refs[at_out : at_out + o])
            at_in, at_out = at_in + i, at_out + o

    outs = [one for _, _, many in tasks for one in many]
    res = call(
        kernel, name, [SMEM] + [VMEM] * n_in, [VMEM] * len(outs), outs, [], 10**9, after, carry
    )(ids, *[one for _, many, _ in tasks for one in many])
    split, at = [], 0
    for _, o in sizes:
        split.append(res[at : at + o])
        at += o
    return (*split, res[-1])


def whole_groups(
    n_dp,
    tokens,
    segment_ids,
    norm_gains,
    norm_biases,
    w_qkv,
    w_attn_out,
    w_up,
    w_down,
    w_vq_in,
    w_vq_out,
    codebook,
    cotangent,
):
    dp_at, tp_at = lax.axis_index("dp"), lax.axis_index("tp")
    ids = jnp.stack([dp_at, tp_at]).astype(jnp.int32)

    def swap(values):
        return exchange(values, 0, 1, n_dp)

    def core(values):
        return [values, exchange(values, 1, 0, n_dp)]

    book_t = codebook.T
    enc_shard, dec_shard = pack_weights(
        w_qkv, w_attn_out.transpose(0, 2, 1), w_up, w_down.transpose(0, 2, 1)
    )
    enc_shards = spread_line(enc_shard, n_dp)
    own, send, norms, vq_w = rows_in(
        ids,
        tokens,
        segment_ids,
        cotangent,
        norm_gains,
        norm_biases,
        w_vq_in.T,
        w_vq_out,
    )
    marked = [own, swap(send)]

    line_a, line_b, (dec_shard,) = stack_lines(enc_shards, [1536] * 2, carry=[dec_shard])
    along_x, along_y = exchange(line_a, 0, 1, n_dp), exchange(line_b, 2, 0, n_dp)
    dec_shards = spread_line(dec_shard, n_dp)
    stack, stack_t, _ = code_prep(book_t, [line_a])
    codes = (stack, stack_t, book_t)
    a_0, b_0, _ = stack_pairs([(line_a, along_x), (line_b, along_y)], [stack_t, marked[1]])
    a_1, b_1 = exchange(a_0, 2, 0, n_dp), exchange(b_0, 0, 1, n_dp)
    line_a, line_b, (a_0, b_0) = stack_lines(dec_shards, [1536] * 2, [a_1, b_1], [a_0, b_0])
    enc_w = [a_0, a_1, exchange(a_0, 1, 0, n_dp), exchange(a_1, 1, 0, n_dp)]
    enc_w += [b_0, b_1, exchange(b_0, 1, 0, n_dp), exchange(b_1, 1, 0, n_dp)]
    along_x, along_y = exchange(line_a, 0, 1, n_dp), exchange(line_b, 2, 0, n_dp)
    e_x1, e_saved, _ = attn_fwd(0, marked, [], norms, enc_w)
    a_0, b_0, _ = stack_pairs([(line_a, along_x), (line_b, along_y)], [e_x1])
    a_1, b_1 = exchange(a_0, 2, 0, n_dp), exchange(b_0, 0, 1, n_dp)
    dec_w = [a_0, exchange(a_0, 1, 0, n_dp), b_0, exchange(b_0, 1, 0, n_dp)]
    e, u, kept, numer, _ = mlp_vq(e_x1, norms, vq_w, stack, stack_t, enc_w, [a_0, b_0])
    a_1, b_1 = gate([u], [a_1, b_1])
    a_1, b_1 = core(a_1), core(b_1)
    dec_w = [dec_w[0], a_1[0], dec_w[1], a_1[1], dec_w[2], b_1[0], dec_w[3], b_1[1]]
    d_x1, d_saved, _ = attn_fwd(3, marked, [u], norms, dec_w)

    dx1, d_small1, keep_m, send_m, _ = mlp_bwd(
        4, ids, d_x1, [cotangent, marked[1]], norms, dec_w
    )
    near_m = exchange(send_m, 1, 0, n_dp)
    du, d_small0, keep_a, send_a, (keep_m,) = attn_bwd(
        3, marked, u, dx1, norms, d_saved, dec_w, carry=[keep_m]
    )
    (m_a, to_x, m_b, to_y), (send_a,) = run_tasks(
        ids, "sums1", [fork_task(keep_m, near_m)], carry=[send_a]
    )
    from_x, from_y = exchange(to_x, 0, 1, n_dp), exchange(to_y, 2, 0, n_dp)
    near_a = exchange(send_a, 1, 0, n_dp)
    de, code, code_send, (m_a, m_b, keep_a) = vq_bwd(
        ids,
        e,
        du,
        norms,
        vq_w,
        [*codes, numer],
        kept,
        [d_small0, d_small1],
        [to_x, to_y],
        [m_a, m_b, keep_a],
    )
    (m_a, m_y, m_b, m_x), (a_a, to_x, a_b, to_y), (code, code_send) = run_tasks(
        ids,
        "sums2",
        [half_task(m_a, from_x, m_b, from_y), fork_task(keep_a, near_a)],
        carry=[code, code_send],
    )
    code_other = exchange(code_send, 1, 0, n_dp)
    from_m_y, from_m_x = exchange(m_y, 2, 0, n_dp), exchange(m_x, 0, 1, n_dp)
    from_x, from_y = exchange(to_x, 0, 1, n_dp), exchange(to_y, 2, 0, n_dp)
    (code, code_send), _ = run_tasks(ids, "sums2b", [code_near_task(code, code_other)])
    code_other = exchange(code_send, 8, 0, n_dp)
    ex1, e_small1, keep_m, send_m, (m_a, m_b, a_a, a_b, code) = mlp_bwd(
        1,
        ids,
        e_x1,
        [de],
        norms,
        enc_w,
        [m_y, m_x, to_x, to_y, code_send],
        [m_a, m_b, a_a, a_b, code],
    )
    (own_dm, send_dm), (a_a, to_y, a_b, to_x), (code,), (keep_m, send_m) = run_tasks(
        ids,
        "sums3",
        [
            join_task(m_a, from_m_y, m_b, from_m_x),
            half_task(a_a, from_x, a_b, from_y),
            code_add_task(code, code_other),
        ],
        carry=[keep_m, send_m],
    )
    near_m, code_other = exchange(send_m, 1, 0, n_dp), exchange(code, 2, 0, n_dp)
    from_y, from_x = exchange(to_y, 2, 0, n_dp), exchange(to_x, 0, 1, n_dp)
    other_dm = exchange(send_dm, 4, 0, n_dp)
    *parts, (a_a, a_b, own_dm) = heads_bwd(
        marked, ex1, e_saved, enc_w, [to_x, to_y, send_dm, code], [a_a, a_b, own_dm]
    )
    (m_a, to_x, m_b, to_y), (code,), (own_da, send_da), (own_dm, send_dm), _ = run_tasks(
        ids,
        "sums3b",
        [
            fork_task(keep_m, near_m),
            code_add_task(code, code_other),
            join_task(a_a, from_y, a_b, from_x),
            line_step_task(own_dm, other_dm),
        ],
        [parts[0]],
    )
    other_da, other_dm = exchange(send_da, 4, 0, n_dp), exchange(send_dm, 8, 0, n_dp)
    code_other = exchange(code, 4, 0, n_dp)
    from_y, from_x = exchange(to_y, 2, 0, n_dp), exchange(to_x, 0, 1, n_dp)
    dx, dx_low, y, y_low, keep_a, send_a, (m_a, m_b, own_dm, own_da) = rows_bwd(
        ids,
        marked,
        ex1,
        norms,
        parts,
        e_small1,
        d_x1,
        enc_w,
        dec_w,
        [to_x, to_y, send_da, send_dm, code],
        [m_a, m_b, own_dm, own_da],
    )
    (m_a, to_y, m_b, to_x, code), (own_da, send_da), (keep_a, send_a) = run_tasks(
        ids,
        "sums4",
        [
            half_task(m_a, from_x, m_b, from_y, code, code_other),
            line_step_task(own_da, other_da),
        ],
        [other_dm],
        [keep_a, send_a],
    )
    near_a, other_da = exchange(send_a, 1, 0, n_dp), exchange(send_da, 8, 0, n_dp)
    from_y, from_x = exchange(to_y, 2, 0, n_dp), exchange(to_x, 0, 1, n_dp)
    (own_a, *lows_a), (m_a, m_b, code) = run_tasks(
        ids, "sums4b", [near_task(keep_a, near_a)], [other_da], [m_a, m_b, code]
    )
    plane_a = plane_send(lows_a, n_dp)
    (own_m, send_m, code), (own_a,) = run_tasks(
        ids,
        "sums5",
        [join_task(m_a, from_y, m_b, from_x, code)],
        lows_a,
        [own_a],
    )
    other_m, code_other = exchange(send_m, 4, 0, n_dp), exchange(code, 8, 0, n_dp)
    (y, dx, rows), (own_a,) = run_tasks(
        ids, "rows_out", [rows_out_task(y, y_low, dx, dx_low)], [send_m, code], [own_a]
    )
    (own_a, send_a), (own_m, send_m), (code,), (rows,) = run_tasks(
        ids,
        "sums6",
        [
            plane_line_task(own_a, plane_a),
            line_step_task(own_m, other_m),
            code_pair_task(code, code_other),
        ],
        carry=[rows],
    )
    other_a, other_m = exchange(send_a, 4, 0, n_dp), exchange(send_m, 8, 0, n_dp)
    code_other, rows = exchange(code, 1, 0, n_dp), swap(rows)
    (own_a, send_a), _ = run_tasks(ids, "sums7", [small_step_task(own_a, other_a)])
    other_a = exchange(send_a, 8, 0, n_dp)
    (decoded, grad_tokens), _ = run_tasks(ids, "rows_done", [rows_task(y, dx, rows)], [send_a])
    (qkv, out_t, up, down_t, book, vq_in, vq_out, *norm_grads, _), _ = run_tasks(
        ids,
        "finish",
        [
            finish_task(
                (own_m, other_m),
                (own_a, other_a),
                (own_dm, other_dm),
                (own_da, other_da),
                code,
                code_other,
            )
        ],
        [decoded],
    )
    return (
        decoded,
        grad_tokens,
        *norm_grads,
        qkv,
        out_t.transpose(0, 2, 1),
        up,
        down_t.transpose(0, 2, 1),
        vq_in.T,
        vq_out,
        book.T,
    )


def layer_norm(values, norm_gain, norm_bias):
    centred = values - jnp.mean(values, axis=-1, keepdims=True)
    spread = jnp.mean(centred * centred, axis=-1, keepdims=True)
    return centred * lax.rsqrt(spread + ln_eps) * norm_gain + norm_bias


def gelu_tanh(values):
    return (
        0.5 * values * (1.0 + jnp.tanh(gelu_coef * (values + 0.044715 * values * values * values)))
    )


def matmul(former, latter):
    return jnp.dot(former, latter, precision=highest, preferred_element_type=jnp.float32)


def normalize(values):
    return values * lax.rsqrt(jnp.sum(values * values, axis=-1, keepdims=True) + norm_eps)


def quantize(in_rows, norm_gain, norm_bias, in_w, out_w, code_w):
    latent = normalize(matmul(layer_norm(in_rows, norm_gain, norm_bias), in_w))
    code_rows = normalize(code_w)
    logits = matmul(latent, code_rows.T) * temper
    row_max = jnp.max(logits, axis=-1, keepdims=True)
    numerator = jnp.exp(logits - row_max)
    assign = numerator / jnp.sum(numerator, axis=-1, keepdims=True)
    soft_code = matmul(assign, code_rows)
    offset = latent - soft_code
    vq_loss = commit_weight * 1.25 * jnp.sum(offset * offset)
    return (matmul(soft_code, out_w), vq_loss)


def product(former, latter):
    return jnp.dot(former, latter, preferred_element_type=jnp.float32)


def product_tn(former, latter):
    return lax.dot_general(
        former, latter, (((0,), (0,)), ((), ())), preferred_element_type=jnp.float32
    )


def product_nt(former, latter):
    return lax.dot_general(
        former, latter, (((1,), (1,)), ((), ())), preferred_element_type=jnp.float32
    )


def split_heads(values):
    return values.reshape(values.shape[0], values.shape[1] // HEAD_DIM, HEAD_DIM).transpose(1, 0, 2)


def join_heads(values):
    return values.transpose(1, 0, 2).reshape(values.shape[1], values.shape[0] * HEAD_DIM)


def masked_scores(query_blk, key_h, seg_blk, seg_keys):
    scores = jnp.einsum(
        "hqd,hkd->hqk", query_blk, key_h, preferred_element_type=jnp.float32
    ) * HEAD_DIM ** (-0.5)
    return jnp.where((seg_blk[:, None] == seg_keys[None, :])[None], scores, masked_score)


def attend(query_h, key_h, value_h, seg_keys):
    block_rows = min(512, query_h.shape[1])
    block_count = query_h.shape[1] // block_rows

    def one_block(begin_row):
        query_blk = lax.dynamic_slice_in_dim(query_h, begin_row, block_rows, 1)
        seg_blk = lax.dynamic_slice_in_dim(seg_keys, begin_row, block_rows, 0)
        scores = masked_scores(query_blk, key_h, seg_blk, seg_keys)
        row_max = jnp.max(scores, axis=-1, keepdims=True)
        numerator = jnp.exp(scores - row_max)
        row_total = jnp.sum(numerator, axis=-1, keepdims=True)
        prob_low = (numerator / row_total).astype(jnp.bfloat16)
        attended = jnp.einsum("hqk,hkd->hqd", prob_low, value_h, preferred_element_type=jnp.float32)
        return (attended.astype(jnp.bfloat16), (row_max + jnp.log(row_total))[..., 0])

    starts = jnp.arange(block_count, dtype=jnp.int32) * block_rows
    attended, log_sums = lax.map(one_block, starts)
    heads_out = attended.transpose(1, 0, 2, 3).reshape(query_h.shape)
    log_sums = log_sums.transpose(1, 0, 2).reshape(query_h.shape[0], query_h.shape[1])
    return (heads_out, log_sums)


def attend_back(query_h, key_h, value_h, seg_keys, log_sums, grad_out):
    block_rows = min(512, query_h.shape[1])
    block_count = query_h.shape[1] // block_rows

    def one_block(carry, begin_row):
        grad_key, grad_value = carry
        query_blk = lax.dynamic_slice_in_dim(query_h, begin_row, block_rows, 1)
        grad_blk = lax.dynamic_slice_in_dim(grad_out, begin_row, block_rows, 1)
        lse_blk = lax.dynamic_slice_in_dim(log_sums, begin_row, block_rows, 1)
        seg_blk = lax.dynamic_slice_in_dim(seg_keys, begin_row, block_rows, 0)
        scores = masked_scores(query_blk, key_h, seg_blk, seg_keys)
        probs = jnp.exp(scores - lse_blk[..., None])
        prob_low = probs.astype(jnp.bfloat16)
        grad_value = grad_value + jnp.einsum(
            "hqk,hqd->hkd", prob_low, grad_blk, preferred_element_type=jnp.float32
        )
        grad_prob = jnp.einsum(
            "hqd,hkd->hqk", grad_blk, value_h, preferred_element_type=jnp.float32
        )
        row_dot = jnp.sum(probs * grad_prob, axis=-1, keepdims=True)
        grad_score = (probs * (grad_prob - row_dot) * HEAD_DIM ** (-0.5)).astype(jnp.bfloat16)
        grad_query = jnp.einsum(
            "hqk,hkd->hqd", grad_score, key_h, preferred_element_type=jnp.float32
        )
        grad_key = grad_key + jnp.einsum(
            "hqk,hqd->hkd", grad_score, query_blk, preferred_element_type=jnp.float32
        )
        return ((grad_key, grad_value), grad_query)

    starts = jnp.arange(block_count, dtype=jnp.int32) * block_rows
    zeros_kv = jnp.zeros(key_h.shape, jnp.float32)
    (grad_key, grad_value), grad_query = lax.scan(one_block, (zeros_kv, zeros_kv), starts)
    grad_query = grad_query.transpose(1, 0, 2, 3).reshape(query_h.shape)
    return (
        grad_query.astype(jnp.bfloat16),
        grad_key.astype(jnp.bfloat16),
        grad_value.astype(jnp.bfloat16),
    )


def spread_rows(values):
    return lax.all_gather(values, "tp", axis=0, tiled=True)


def combine_rows(partial_value):
    return lax.psum_scatter(partial_value, "tp", scatter_dimension=0, tiled=True)


def spread_grads(values):
    return lax.all_gather(values, "tp", axis=0, tiled=True)


def combine_grads(partial_value):
    return lax.psum_scatter(
        partial_value.astype(jnp.bfloat16), "tp", scatter_dimension=0, tiled=True
    ).astype(jnp.float32)


def fetch_weights(w_qkv, w_attn_out, w_up, w_down, layer):
    return (
        lax.all_gather(w_qkv[layer], "dp", axis=1, tiled=True),
        lax.all_gather(w_attn_out[layer], "dp", axis=1, tiled=True),
        lax.all_gather(w_up[layer], "dp", axis=0, tiled=True),
        lax.all_gather(w_down[layer], "dp", axis=1, tiled=True),
    )


def reduce_weight_grads(grads):
    return (
        lax.psum_scatter(
            grads[0].astype(jnp.bfloat16), "dp", scatter_dimension=1, tiled=True
        ).astype(jnp.float32),
        lax.psum_scatter(
            grads[1].astype(jnp.bfloat16), "dp", scatter_dimension=1, tiled=True
        ).astype(jnp.float32),
        lax.psum_scatter(
            grads[2].astype(jnp.bfloat16), "dp", scatter_dimension=0, tiled=True
        ).astype(jnp.float32),
        lax.psum_scatter(
            grads[3].astype(jnp.bfloat16), "dp", scatter_dimension=1, tiled=True
        ).astype(jnp.float32),
    )


def block_forward(resid_in, seg_local, gains, biases, weights):
    qkv_w, attn_w, up_w, down_w = weights
    normed = layer_norm(resid_in, gains[0], biases[0]).astype(jnp.bfloat16)
    normed_all, seg_all = (
        lax.all_gather(normed, "tp", axis=0, tiled=True),
        lax.all_gather(seg_local, "tp", axis=0, tiled=True),
    )
    query_h = split_heads(product(normed_all, qkv_w[0]).astype(jnp.bfloat16))
    key_h = split_heads(product(normed_all, qkv_w[1]).astype(jnp.bfloat16))
    value_h = split_heads(product(normed_all, qkv_w[2]).astype(jnp.bfloat16))
    heads_out, log_sums = attend(query_h, key_h, value_h, seg_all)
    attn_rows = join_heads(heads_out)
    middle = resid_in + combine_rows(product(attn_rows, attn_w))
    normed_mid = spread_rows(layer_norm(middle, gains[1], biases[1]).astype(jnp.bfloat16))
    hidden_pre = product(normed_mid, up_w)
    hidden = gelu_tanh(hidden_pre).astype(jnp.bfloat16)
    result = middle + combine_rows(product(hidden, down_w))
    kept = (
        resid_in,
        middle,
        normed_all,
        seg_all,
        query_h,
        key_h,
        value_h,
        log_sums,
        attn_rows,
        normed_mid,
        hidden_pre,
        hidden,
    )
    return (result, kept)


def block_backward(kept, gains, biases, weights, grad_result):
    (
        resid_in,
        middle,
        normed_all,
        seg_all,
        query_h,
        key_h,
        value_h,
        log_sums,
        attn_rows,
        normed_mid,
        hidden_pre,
        hidden,
    ) = kept
    qkv_w, attn_w, up_w, down_w = weights
    grad_branch = spread_grads(grad_result.astype(jnp.bfloat16))
    grad_down = product_tn(hidden, grad_branch)
    grad_hidden = product_nt(grad_branch, down_w)
    _, gelu_back = jax.vjp(gelu_tanh, hidden_pre)
    grad_pre = gelu_back(grad_hidden)[0].astype(jnp.bfloat16)
    grad_up = product_tn(normed_mid, grad_pre)
    grad_norm_mid = combine_grads(product_nt(grad_pre, up_w))
    _, norm_back_mid = jax.vjp(layer_norm, middle, gains[1], biases[1])
    grad_mid_ln, grad_gain_mid, grad_bias_mid = norm_back_mid(grad_norm_mid)
    grad_middle = grad_result + grad_mid_ln
    grad_attn_all = spread_grads(grad_middle.astype(jnp.bfloat16))
    grad_attn = product_tn(attn_rows, grad_attn_all)
    grad_heads = split_heads(product_nt(grad_attn_all, attn_w).astype(jnp.bfloat16))
    grad_query, grad_key, grad_value = attend_back(
        query_h, key_h, value_h, seg_all, log_sums, grad_heads
    )
    grad_parts = [join_heads(grad_query), join_heads(grad_key), join_heads(grad_value)]
    grad_qkv = jnp.stack([product_tn(normed_all, grad_part) for grad_part in grad_parts])
    grad_normed_part = (
        product_nt(grad_parts[0], qkv_w[0])
        + product_nt(grad_parts[1], qkv_w[1])
        + product_nt(grad_parts[2], qkv_w[2])
    )
    grad_normed = combine_grads(grad_normed_part)
    _, norm_back_in = jax.vjp(layer_norm, resid_in, gains[0], biases[0])
    grad_in_ln, grad_gain_in, grad_bias_in = norm_back_in(grad_normed)
    gain_grads = jnp.stack([grad_gain_in, grad_gain_mid])
    bias_grads = jnp.stack([grad_bias_in, grad_bias_mid])
    return (
        grad_middle + grad_in_ln,
        gain_grads,
        bias_grads,
        (grad_qkv, grad_attn, grad_up, grad_down),
    )


def local(
    tokens,
    segment_ids,
    norm_gains,
    norm_biases,
    w_qkv,
    w_attn_out,
    w_up,
    w_down,
    w_vq_in,
    w_vq_out,
    codebook,
    cotangent,
):
    gain_sum = jnp.zeros(norm_gains.shape, jnp.float32)
    bias_sum = jnp.zeros(norm_biases.shape, jnp.float32)
    vq_in_sum = jnp.zeros(w_vq_in.shape, jnp.float32)
    vq_out_sum = jnp.zeros(w_vq_out.shape, jnp.float32)
    code_sum = jnp.zeros(codebook.shape, jnp.float32)
    layer_sums = [None, None]
    outputs = []
    input_grads = []
    for micro in range(MICRO):
        resid_in = tokens[micro].astype(jnp.float32)
        seg_local = segment_ids[micro]
        enc_weights = fetch_weights(w_qkv, w_attn_out, w_up, w_down, 0)
        encoded, enc_kept = block_forward(
            resid_in, seg_local, norm_gains[0:2], norm_biases[0:2], enc_weights
        )
        (decoder_in, _), vq_back = jax.vjp(
            quantize, encoded, norm_gains[2], norm_biases[2], w_vq_in, w_vq_out, codebook
        )
        dec_weights = fetch_weights(w_qkv, w_attn_out, w_up, w_down, 1)
        decoded, dec_kept = block_forward(
            decoder_in, seg_local, norm_gains[3:5], norm_biases[3:5], dec_weights
        )
        outputs.append(decoded)
        grad_dec_in, gains_dec, biases_dec, grads_dec = block_backward(
            dec_kept, norm_gains[3:5], norm_biases[3:5], dec_weights, cotangent[micro]
        )
        grad_encoded, grad_gain_vq, grad_bias_vq, grad_in_w, grad_out_w, grad_codes = vq_back(
            (grad_dec_in, jnp.ones((), jnp.float32))
        )
        grad_input, gains_enc, biases_enc, grads_enc = block_backward(
            enc_kept, norm_gains[0:2], norm_biases[0:2], enc_weights, grad_encoded
        )
        input_grads.append(grad_input)
        gain_sum = gain_sum + jnp.concatenate([gains_enc, grad_gain_vq[None], gains_dec], axis=0)
        bias_sum = bias_sum + jnp.concatenate([biases_enc, grad_bias_vq[None], biases_dec], axis=0)
        vq_in_sum = vq_in_sum + grad_in_w
        vq_out_sum = vq_out_sum + grad_out_w
        code_sum = code_sum + grad_codes
        for layer, grads in ((0, grads_enc), (1, grads_dec)):
            reduced = reduce_weight_grads(grads)
            if layer_sums[layer] is None:
                layer_sums[layer] = reduced
            else:
                layer_sums[layer] = jax.tree.map(jnp.add, layer_sums[layer], reduced)
    gain_tot, bias_tot, vq_in_tot, vq_out_tot, code_tot = lax.psum(
        (gain_sum, bias_sum, vq_in_sum, vq_out_sum, code_sum), ("dp", "tp")
    )
    return (
        jnp.stack(outputs),
        jnp.stack(input_grads),
        gain_tot,
        bias_tot[0:3],
        bias_tot[3:5],
        jnp.stack([layer_sums[0][0], layer_sums[1][0]]),
        jnp.stack([layer_sums[0][1], layer_sums[1][1]]),
        jnp.stack([layer_sums[0][2], layer_sums[1][2]]),
        jnp.stack([layer_sums[0][3], layer_sums[1][3]]),
        vq_in_tot,
        vq_out_tot,
        code_tot,
    )


def solution(mesh):
    n_dp, n_tp = mesh.shape["dp"], mesh.shape["tp"]
    fits = n_tp == MICRO and n_dp == 16
    return jax.shard_map(
        functools.partial(whole_groups, n_dp) if fits else local,
        mesh=mesh,
        in_specs=(
            P(None, ("dp", "tp"), None),
            P(None, ("dp", "tp")),
            P(),
            P(),
            P(None, None, "dp", "tp"),
            P(None, "tp", "dp"),
            P(None, "dp", "tp"),
            P(None, "tp", "dp"),
            P(),
            P(),
            P(),
            P(None, ("dp", "tp"), None),
        ),
        out_specs=(
            P(None, ("dp", "tp"), None),
            P(None, ("dp", "tp"), None),
            P(),
            P(),
            P(),
            P(None, None, "dp", "tp"),
            P(None, "tp", "dp"),
            P(None, "dp", "tp"),
            P(None, "tp", "dp"),
            P(),
            P(),
            P(),
        ),
        check_vma=False,
    )
```

```python
import functools

import jax
import jax.numpy as jnp
from jax import lax
from jax.experimental import pallas as pl
from jax.experimental.pallas import tpu as pltpu
from jax.sharding import PartitionSpec as P

HEAD_DIM = 64
MICRO = 2
bf16 = jnp.bfloat16
f32 = jnp.float32
highest = lax.Precision.HIGHEST
ln_eps = 1e-05
norm_eps = 1e-06
temper = 10.0
commit_weight = 64.0
gelu_coef = 0.7978845608028654
masked_score = -1e30
log2e = 1.4426950408889634
vmem_cap = 26 * 1024 * 1024


PLANE = ((0, 0), (0, 1), (1, 0), (1, 1))


def exchange(values, dp_xor, tp_xor, n_dp):
    pairs = [
        (d * 2 + t, (d ^ dp_xor) * 2 + (t ^ tp_xor)) for d in range(n_dp) for t in range(2)
    ]
    return lax.ppermute(values, ("dp", "tp"), pairs)


def spread_line(shard, n_dp):
    return [shard] + [exchange(shard, 4 * k, 0, n_dp) for k in range(1, 4)]


def plane_send(lows, n_dp):
    return [exchange(low, 2 * y, x, n_dp) for (y, x), low in zip(PLANE[1:], lows)]


def line_send(lows, n_dp):
    return [exchange(low, 4 * k, 0, n_dp) for k, low in zip(range(1, 4), lows)]


def dot(a, b):
    return jnp.dot(a, b, preferred_element_type=f32)


def dot_nt(a, b, precision=None):
    return lax.dot_general(
        a, b, (((1,), (1,)), ((), ())), preferred_element_type=f32, precision=precision
    )


def dot_full(a, b):
    return jnp.dot(a, b, preferred_element_type=f32, precision=highest)


def ln_parts(x):
    centred = x - jnp.mean(x, axis=-1, keepdims=True)
    inv = lax.rsqrt(jnp.mean(centred * centred, axis=-1, keepdims=True) + ln_eps)
    return centred * inv, inv


def ln_back(grad, xhat, inv, gain):
    scaled = grad * gain
    return inv * (
        scaled
        - jnp.mean(scaled, axis=-1, keepdims=True)
        - xhat * jnp.mean(scaled * xhat, axis=-1, keepdims=True)
    )


def split2(x):
    hi = x.astype(bf16)
    return hi, (x - hi.astype(f32)).astype(bf16)


def split3(x):
    hi, _ = split2(x)
    rest = x - hi.astype(f32)
    mid = rest.astype(bf16)
    return hi, mid, (rest - mid.astype(f32)).astype(bf16)


def order_matrix(dp, inverse):
    at = lax.broadcasted_iota(jnp.int32, (512, 512), 0 if inverse else 1)
    other = lax.broadcasted_iota(jnp.int32, (512, 512), 1 if inverse else 0)
    block = at >> 5
    bits = ((block & 3) << 2) | (((block >> 2) & 1) << 1) | (block >> 3)
    return jnp.where(other == (((dp ^ bits) << 5) | (at & 31)), 1.0, 0.0).astype(bf16)


def ordered(x, matrix):
    if x.dtype == bf16:
        return dot(x, matrix)
    hi, mid, lo = split3(x)
    return (dot(hi, matrix) + dot(mid, matrix)) + dot(lo, matrix)


def w_at(a, b, t, first, width):
    parts = []
    for core in range(2):
        for y in range(2):
            if first < 1536:
                part = a[2 * core + y][t, :, :, first : first + width]
            else:
                part = b[2 * core + t][y, :, :, first - 1536 : first - 1536 + width]
            parts.append(part.reshape(128, width))
    return jnp.concatenate(parts, axis=0)


def put_grad(refs, t, cols, value):
    for core, ref in enumerate(refs):
        for y in range(2):
            rows = value[core * 256 + y * 128 : core * 256 + (y + 1) * 128]
            ref[2 * y + t, :, :, cols] = rows.reshape(4, 32, rows.shape[1])


def start_all(copies):
    for copy in copies:
        copy.start()


def wait_all(copies):
    for copy in copies:
        copy.wait()


def head_rows(ref, pair, which):
    own = ref[pl.ds(pair * 128 + which * HEAD_DIM, HEAD_DIM), :]
    zero = jnp.zeros_like(own)
    return jnp.concatenate([own, zero] if which == 0 else [zero, own], axis=0)


def segment_mask(own, other):
    ids = jnp.concatenate([own[:, 512:640], other[:, 512:640]], axis=0).astype(f32)
    return jnp.where(ids[:, 0:1] == ids.T[0:1, :], 0.0, masked_score)


def load_rows(x, own, other):
    if x is None:
        return jnp.concatenate([own[:, :512], other[:, :512]], axis=0).astype(f32)
    return x[...]


def gain_of(norms, at):
    return norms[at : at + 1, :]


def bias_of(norms, at):
    return norms[8 + at : 9 + at, :]


def attn_fwd_kernel(with_x, at, own, other, norms, *refs):
    w, refs = refs[:4], refs[4:]
    x, refs = (refs[0], refs[1:]) if with_x else (None, refs)
    x1, lse, saved, refs = refs[0], refs[1], refs[2:8], refs[8:]
    h, vt, ot, mask, qs, k, v, o, qst, kt, out_sems = refs
    keeps = [
        pltpu.make_async_copy(held, to, out_sems.at[i])
        for i, (held, to) in enumerate(zip((qs, k, v, o, qst, kt), saved))
    ]
    xf = load_rows(x, own, other)
    h[...] = (ln_parts(xf)[0] * gain_of(norms, at) + bias_of(norms, at)).astype(bf16)
    mask[...] = segment_mask(own, other)
    for t in range(2):
        cols = slice(t * 256, (t + 1) * 256)
        q = dot(h[...], w_at(w, None, t, 0, 256)).astype(bf16)
        qs[:, cols] = (q * HEAD_DIM ** (-0.5)).astype(bf16)
        k[:, cols] = dot(h[...], w_at(w, None, t, 256, 256)).astype(bf16)
        v[:, cols] = dot(h[...], w_at(w, None, t, 512, 256)).astype(bf16)
    qst[...] = qs[...].T
    kt[...] = k[...].T
    vt[...] = v[...].T
    for i in (0, 1, 2, 4, 5):
        keeps[i].start()
    for pair in range(4):
        k_pair = k[:, pair * 128 : (pair + 1) * 128]
        for which in range(2):
            scores = dot(k_pair, head_rows(qst, pair, which)) + mask[...]
            top = jnp.max(scores, axis=0, keepdims=True)
            numer = jnp.exp(scores - top).astype(bf16)
            rows = pl.ds(pair * 128 + which * HEAD_DIM, HEAD_DIM)
            left = jnp.concatenate([vt[rows, :], jnp.ones((16, 512), bf16)], axis=0)
            both = dot(left, numer)
            total = both[HEAD_DIM : HEAD_DIM + 1, :]
            ot[rows, :] = (both[:HEAD_DIM, :] / total).astype(bf16)
            lse[pl.ds(pair * 2 + which, 1), :] = top + jnp.log(total)
    o[...] = ot[...].T
    keeps[3].start()
    acc = xf
    for t in range(2):
        acc = acc + dot_nt(o[:, t * 256 : (t + 1) * 256], w_at(w, None, t, 768, 256))
    x1[...] = acc
    wait_all(keeps)


def gelu_parts(u):
    square = u * u
    tanh = jnp.tanh(gelu_coef * u * (1.0 + 0.044715 * square))
    return 0.5 * u * (1.0 + tanh), tanh, square


def mlp_weights(w):
    def up(t, part):
        return w_at(w[:4], w[4:], t, 1024 + part * 512, 512)

    def down(t, part):
        return w_at(w[:4], w[4:], t, 2048 + part * 512, 512)

    return up, down


def mlp_rows(at, x, norms, w, h2):
    up, down = mlp_weights(w)
    h2[...] = (ln_parts(x)[0] * gain_of(norms, at) + bias_of(norms, at)).astype(bf16)
    for t in range(2):
        for part in range(2):
            hidden = gelu_parts(dot(h2[...], up(t, part)))[0].astype(bf16)
            x = x + dot_nt(hidden, down(t, part))
    return x


def mlp_bwd_kernel(split, at, ids, x1, norms, *refs):
    up, down = mlp_weights(refs[:8])
    refs = refs[8:]
    if split:
        own, other, refs = refs[0], refs[1], refs[2:]
    else:
        dy, refs = refs[0], refs[1:]
    dx1, small, grads = refs[0], refs[1], refs[2:4]
    h2, h2t, dyb, dybt, dh2 = refs[4:9]
    if split:
        dy = refs[9]
        dy[0:256, :] = ordered(own[ids[1]], order_matrix(ids[0], False))
        dy[256:, :] = other[:, 640:].astype(f32)
    h2[...] = (ln_parts(x1[...])[0] * gain_of(norms, at) + bias_of(norms, at)).astype(bf16)
    h2t[...] = h2[...].T
    dyb[...] = dy[...].astype(bf16)
    dybt[...] = dyb[...].T
    for t in range(2):
        for part in range(2):
            cols = slice(part * 512, (part + 1) * 512)
            w_up = up(t, part)
            pre = dot(h2[...], w_up)
            hidden, tanh, square = gelu_parts(pre)
            slope = 0.5 * (1.0 + tanh) + (0.5 * gelu_coef) * pre * (1.0 - tanh * tanh) * (
                1.0 + (3 * 0.044715) * square
            )
            dhidden = dot(dyb[...], down(t, part))
            dpre = (dhidden * slope).astype(bf16)
            out_cols = slice(1024 + part * 512, 1024 + (part + 1) * 512)
            put_grad(grads, t, out_cols, dot(dybt[...], hidden.astype(bf16)).astype(bf16))
            put_grad(grads, t, cols, dot(h2t[...], dpre).astype(bf16))
            more = dot_nt(dpre, w_up)
            if t + part == 0:
                dh2[...] = more
            else:
                dh2[...] += more
    xhat, inv = ln_parts(x1[...])
    grad = dh2[...]
    small[0:1, :] = jnp.sum(grad * xhat, axis=0, keepdims=True)
    small[1:2, :] = jnp.sum(grad, axis=0, keepdims=True)
    dx1[...] = dy[...] + ln_back(grad, xhat, inv, gain_of(norms, at))


def heads_back(low, w, saved, lse, mask, put_out, scratch):
    qs, k, v, o, qst, kt = saved
    flip, do, dot_t, dqt, dq, dk, dv = scratch
    flip[...] = low.T
    for t in range(2):
        cols = slice(t * 256, (t + 1) * 256)
        do[:, cols] = dot(low, w_at(w, None, t, 768, 256)).astype(bf16)
        put_out(t, dot(flip[...], o[:, cols]).astype(bf16))
    dot_t[...] = do[...].T
    first = lax.broadcasted_iota(jnp.int32, (512, 128), 1) < HEAD_DIM
    for pair in range(4):
        lanes = slice(pair * 128, (pair + 1) * 128)
        dvs, dks = [], []
        for which in range(2):
            head = pair * 2 + which
            rows = pl.ds(head * HEAD_DIM, HEAD_DIM)
            scores = dot(k[:, lanes], head_rows(qst, pair, which)) + mask[...]
            probs = jnp.exp(scores - lse[head : head + 1, :])
            dprobs = dot(v[:, lanes], head_rows(dot_t, pair, which))
            shift = jnp.sum(probs * dprobs, axis=0, keepdims=True)
            dscore = (probs * (dprobs - shift)).astype(bf16)
            dvs.append(dot(probs.astype(bf16), do[:, lanes]))
            dks.append(dot(dscore, qs[:, lanes]))
            dqt[rows, :] = (dot(kt[rows, :], dscore) * HEAD_DIM ** (-0.5)).astype(bf16)
        dv[:, lanes] = jnp.where(first, dvs[0], dvs[1]).astype(bf16)
        dk[:, lanes] = jnp.where(first, dks[0], dks[1]).astype(bf16)
    dq[...] = dqt[...].T


def rows_back(at, xf, norms, w, parts, small, grads, h, flip):
    h[...] = (ln_parts(xf)[0] * gain_of(norms, at) + bias_of(norms, at)).astype(bf16)
    flip[...] = h[...].T
    grad = jnp.zeros((512, 512), f32)
    for t in range(2):
        cols = slice(t * 256, (t + 1) * 256)
        for index, part in enumerate(parts):
            w_cols = slice(index * 256, (index + 1) * 256)
            put_grad(grads, t, w_cols, dot(flip[...], part[:, cols]).astype(bf16))
            grad = grad + dot_nt(part[:, cols], w_at(w, None, t, index * 256, 256))
    xhat, inv = ln_parts(xf)
    small[0:1, :] = jnp.sum(grad * xhat, axis=0, keepdims=True)
    small[1:2, :] = jnp.sum(grad, axis=0, keepdims=True)
    return ln_back(grad, xhat, inv, gain_of(norms, at))


def take_saved(saved, held, sems):
    copies = [
        pltpu.make_async_copy(a, b, sems.at[i]) for i, (a, b) in enumerate(zip(saved, held))
    ]
    start_all(copies)
    return copies


def attn_bwd_kernel(at, own, other, dx1, norms, lse, *refs):
    w, saved, x, refs = refs[:4], refs[4:10], refs[10], refs[11:]
    dx, small, grads = refs[0], refs[1], refs[2:4]
    mask, h, held, scratch, sems = refs[4], refs[5], refs[6:12], refs[12:19], refs[19]
    copies = take_saved(saved, held, sems)
    mask[...] = segment_mask(own, other)
    low = dx1[...].astype(bf16)
    wait_all(copies)

    def put_out(t, value):
        put_grad(grads, t, slice(768, 1024), value)

    heads_back(low, w, held, lse, mask, put_out, scratch)
    dx[...] = dx1[...] + rows_back(
        at, x[...], norms, w, scratch[4:], small, grads, h, scratch[0]
    )


def heads_bwd_kernel(own, other, dx1, lse, *refs):
    w, saved, refs = refs[:4], refs[4:10], refs[10:]
    parts, grads, mask, held = refs[:3], refs[3:5], refs[5], refs[6:12]
    scratch, sems = (*refs[12:16], *parts), refs[16]
    copies = take_saved(saved, held, sems)
    mask[...] = segment_mask(own, other)
    low = dx1[...].astype(bf16)
    wait_all(copies)

    def put_out(t, value):
        put_grad(grads, t, slice(0, 256), value)

    heads_back(low, w, held, lse, mask, put_out, scratch)


def rows_bwd_kernel(
    ids, own, other, dx1, norms, dq, dk, dv, out_0, out_1, other_small, d_x1, *refs
):
    w, d_w, (dx, dx_low, y, y_low), grads, (small, h, flip) = (
        refs[:4],
        refs[4:12],
        refs[12:16],
        refs[16:18],
        refs[18:],
    )
    total = dx1[...] + rows_back(
        0, load_rows(None, own, other), norms, w, (dq, dk, dv), small, grads, h, flip
    )
    dx[...] = total[:256, :]
    dx_low[...] = total[256:, :].astype(bf16)
    rows = jnp.concatenate([small[0:2, :], other_small[0:2, :], jnp.zeros((4, 512), f32)], axis=0)
    packed = pack_rows(ordered(rows, order_matrix(ids[0], True)))
    for grad, part in zip(grads, (out_0, out_1)):
        for i in range(4):
            for z in range(4):
                grad[i, z, :, 768:1024] = part[i, z]
                grad[i, z, :, 1024:1152] = packed
    rows = mlp_rows(4, d_x1[...], norms, d_w, h)
    y[...] = rows[:256, :]
    y_low[...] = rows[256:, :].astype(bf16)


def pack_rows(rows):
    cut = [rows[i : i + 1, 128 * j : 128 * (j + 1)] for i in range(4) for j in range(4)]
    return jnp.concatenate(split2(jnp.concatenate(cut, axis=0)), axis=0)


def code_prep_kernel(book_t, stack, stack_t):
    def one_chunk(index, _):
        lanes = pl.ds(pl.multiple_of(index * 512, 512), 512)
        rows = book_t[:, lanes]
        unit = rows * lax.rsqrt(jnp.sum(rows * rows, axis=0, keepdims=True) + norm_eps)
        hi, mid, lo = split3(unit)
        stack_t[:, lanes] = jnp.concatenate([hi, mid, lo, jnp.ones((32, 512), bf16)], axis=0)
        tall = jnp.concatenate([hi, mid, lo, hi, mid, hi, jnp.zeros((64, 512), bf16)], axis=0)
        stack[lanes, :] = tall.T
        return 0

    lax.fori_loop(0, book_t.shape[1] // 512, one_chunk, 0)


def factor_stack(x):
    hi, mid, lo = split3(x)
    return jnp.concatenate([hi, hi, hi, mid, mid, lo, jnp.zeros((64, x.shape[1]), bf16)], axis=0)


def code_loads(pairs, sems):
    loads = []
    for piece in range(4):
        group = []
        for at, (held, to, by_row) in enumerate(pairs):
            size = held.shape[0 if by_row else 1] // 4
            part = pl.ds(piece * size, size)
            place = (part, slice(None)) if by_row else (slice(None), part)
            group.append(pltpu.make_async_copy(held.at[place], to.at[place], sems.at[at, piece]))
        start_all(group)
        loads.append(group)
    return loads


def mlp_vq_kernel(x1, norms, vq_w, stack_hbm, stack_t_hbm, *refs):
    w, (e, u, kept, numer_hbm, h2, acc, stack, stack_t, numer, sems, out_sems) = refs[:8], refs[8:]
    loads = code_loads([(stack_hbm, stack, True), (stack_t_hbm, stack_t, False)], sems)
    e[...] = mlp_rows(1, x1[...], norms, w, h2)
    lnv = ln_parts(e[...])[0] * gain_of(norms, 2) + bias_of(norms, 2)
    raw = dot_nt(vq_w[0:32, :], lnv, highest)
    inv = lax.rsqrt(jnp.sum(raw * raw, axis=0, keepdims=True) + norm_eps)
    latent = raw * inv
    right = factor_stack(latent * (temper * log2e))
    chunks, keeps = stack.shape[0] // 2048, []
    for piece, group in enumerate(loads):
        wait_all(group)
        for part in range(piece * chunks // 4, (piece + 1) * chunks // 4):
            numers = []
            for index in range(4 * part, 4 * part + 4):
                codes = slice(index * 512, (index + 1) * 512)
                numers.append(jnp.exp2(dot(stack[codes, :], right)).astype(bf16))
            if part > 1:
                keeps[part - 2].wait()
            keeps.append(
                pltpu.make_async_copy(
                    numer.at[part % 2],
                    numer_hbm.at[pl.ds(part * 2048, 2048), :],
                    out_sems.at[part % 2],
                )
            )
            numer[part % 2] = jnp.concatenate(numers, axis=0)
            keeps[part].start()
            sums = dot(stack_t[:, part * 2048 : (part + 1) * 2048], numer[part % 2])
            if part == 0:
                acc[...] = sums
            else:
                acc[...] += sums
    total = acc[96:97, :]
    soft = (acc[0:32, :] + acc[32:64, :] + acc[64:96, :]) / total
    kept[0:32, :] = latent
    kept[32:64, :] = soft
    kept[64:65, :] = total
    kept[65:66, :] = inv
    u[...] = dot_full(soft.T, vq_w[32:64, :])
    wait_all(keeps[-2:])


def vq_bwd_kernel(
    ids, e, du, norms, vq_w, stack_hbm, stack_t_hbm, book_hbm, numer_hbm, kept, *refs
):
    small0, small1, de, code_keep, code_send = refs[:5]
    acc, grads, small, tail, stack, stack_t, book_t, numer, load_sems, sems = refs[5:]
    loads = code_loads(
        [
            (stack_hbm, stack, True),
            (numer_hbm, numer, True),
            (stack_t_hbm, stack_t, False),
            (book_hbm, book_t, False),
        ],
        load_sems,
    )
    xhat, inv_ln = ln_parts(e[...])
    lnv = xhat * gain_of(norms, 2) + bias_of(norms, 2)
    latent, soft = kept[0:32, :], kept[32:64, :]
    total, inv = kept[64:65, :], kept[65:66, :]
    direct = (2.0 * 1.25 * commit_weight) * (latent - soft)
    dsoft = dot_nt(vq_w[32:64, :], du[...], highest) - direct
    small[32:64, :] = dot_full(soft, du[...])
    shift = jnp.sum(dsoft * soft, axis=0, keepdims=True) / total
    dsoft = dsoft / total
    right = factor_stack(dsoft)
    pads = jnp.zeros((64, 512), f32)

    def tall(x):
        hi, lo = split2(x)
        return jnp.concatenate([hi.astype(f32), lo.astype(f32), pads], axis=0).T.astype(bf16)

    sides = jnp.concatenate([tall(dsoft), tall(latent * temper)], axis=0)
    chunks = stack.shape[0] // 2048
    for piece, group in enumerate(loads):
        wait_all(group)
        for part in range(piece * chunks // 4, (piece + 1) * chunks // 4):
            dlogits = []
            for index in range(4 * part, 4 * part + 4):
                codes = slice(index * 512, (index + 1) * 512)
                held = numer[codes, :]
                dlogit = (held.astype(f32) * (dot(stack[codes, :], right) - shift)).astype(bf16)
                dlogits.append(dlogit)
                sums = jnp.concatenate([held, dlogit], axis=1)
                dcode = dot(sums, sides).T
                dcode = dcode[0:32, :] + dcode[32:64, :]
                rows = book_t[:, codes]
                scale = lax.rsqrt(jnp.sum(rows * rows, axis=0, keepdims=True) + norm_eps)
                unit = rows * scale
                grads[:, codes] = (
                    scale * (dcode - unit * jnp.sum(unit * dcode, axis=0, keepdims=True))
                ).astype(bf16)
            sums = dot(
                stack_t[0:96, part * 2048 : (part + 1) * 2048], jnp.concatenate(dlogits, axis=0)
            )
            if part == 0:
                acc[...] = sums
            else:
                acc[...] += sums
    dlatent = temper * (acc[0:32, :] + acc[32:64, :] + acc[64:96, :]) + direct
    draw = inv * (dlatent - latent * jnp.sum(latent * dlatent, axis=0, keepdims=True))
    small[0:32, :] = dot_full(draw, lnv)
    dln = dot_full(draw.T, vq_w[0:32, :])
    small[64:65, :] = jnp.sum(dln * xhat, axis=0, keepdims=True)
    small[65:66, :] = jnp.sum(dln, axis=0, keepdims=True)
    small[66:68, :] = small0[0:2, :]
    small[68:70, :] = small1[0:2, :]
    small[70:96, :] = jnp.zeros((26, 512), f32)
    small[...] = ordered(small[...], order_matrix(ids[0], True))
    for block in range(3):
        for at, part in enumerate(split2(small[block * 32 : (block + 1) * 32, :])):
            for side in range(2):
                tail[block * 2 + side, :, at * 256 : (at + 1) * 256] = part[
                    :, side * 256 : (side + 1) * 256
                ]
    tail[6:8] = jnp.zeros((2, 32, 512), bf16)
    core, z = ids[0] % 2, ids[0] // 4
    copies = []
    for slot, (at, to) in enumerate(((core, code_keep), (1 - core, code_send))):
        for k in range(4):
            part = at * 4 + (z ^ k)
            lanes = pl.ds(pl.multiple_of(part * 1024, 1024), 1024)
            copies += [
                pltpu.make_async_copy(
                    grads.at[:, lanes], to.at[k, :, pl.ds(0, 1024)], sems.at[0, slot, k]
                ),
                pltpu.make_async_copy(
                    tail.at[part], to.at[k, :, pl.ds(1024, 512)], sems.at[1, slot, k]
                ),
            ]
    for copy in copies:
        copy.start()
    de[...] = ln_back(dln, xhat, inv_ln, gain_of(norms, 2))
    for copy in copies:
        copy.wait()


SMEM = pl.BlockSpec(memory_space=pltpu.SMEM)
VMEM = pl.BlockSpec(memory_space=pltpu.VMEM)
ANY = pl.BlockSpec(memory_space=pl.ANY)


def shaped(*pairs):
    return [jax.ShapeDtypeStruct(shape, dtype) for shape, dtype in pairs]


def pin(array):
    return pltpu.with_memory_space_constraint(array, pltpu.HBM)


def call(kernel, name, in_specs, out_specs, outs, scratch, flops, after=(), carry=()):
    n_in, n_extra, n_out = len(in_specs), len(after) + len(carry), len(outs)

    def body(*refs):
        first = n_in + n_extra
        kernel(*refs[:n_in], *refs[first : first + n_out], *refs[first + n_out + len(carry) :])

    made = pl.pallas_call(
        body,
        name=name,
        in_specs=in_specs + [ANY] * n_extra,
        out_specs=out_specs + [ANY] * len(carry),
        out_shape=outs + [jax.ShapeDtypeStruct(a.shape, a.dtype) for a in carry],
        scratch_shapes=scratch,
        input_output_aliases={n_in + len(after) + i: n_out + i for i in range(len(carry))},
        compiler_params=pltpu.CompilerParams(vmem_limit_bytes=vmem_cap),
        cost_estimate=pl.CostEstimate(flops=flops, bytes_accessed=10**6, transcendentals=0),
    )

    def run(*args):
        res = made(*args, *after, *carry)
        return (*res[:n_out], list(res[n_out:]))

    return run


DMA = pltpu.SemaphoreType.DMA
ROWS2 = (512, 512)


def attn_fwd(at, marked, xs, norms, w, after=(), carry=()):
    outs = shaped((ROWS2, f32), ((8, 512), f32)) + [pltpu.HBM(ROWS2, bf16)] * 6
    scratch = [
        *[pltpu.VMEM(ROWS2, bf16)] * 3,
        pltpu.VMEM(ROWS2, f32),
        *[pltpu.VMEM(ROWS2, bf16)] * 6,
        DMA((6,)),
    ]
    x1, lse, *saved, carried = call(
        functools.partial(attn_fwd_kernel, bool(xs), at),
        "attn_fwd",
        [VMEM] * (7 + len(xs)),
        [VMEM] * 2 + [ANY] * 6,
        outs,
        scratch,
        10**10,
        after,
        carry,
    )(*marked, norms, *w[:4], *xs)
    return x1, (lse, *saved), carried


def mlp_bwd(at, ids, x1, dys, norms, w, after=(), carry=()):
    scratch = [
        *[pltpu.VMEM(ROWS2, bf16)] * 4,
        *[pltpu.VMEM(ROWS2, f32)] * len(dys),
    ]
    return call(
        functools.partial(mlp_bwd_kernel, len(dys) == 2, at),
        "mlp_bwd",
        [SMEM] + [VMEM] * (10 + len(dys)),
        [VMEM] * 4,
        shaped((ROWS2, f32), ((8, 512), f32), *[((4, 4, 32, 2048), bf16)] * 2),
        scratch,
        15 * 10**9,
        after,
        carry,
    )(ids, x1, norms, *w, *dys)


def attn_bwd(at, marked, x, dx1, norms, saved, w, after=(), carry=()):
    scratch = [pltpu.VMEM(ROWS2, f32), *[pltpu.VMEM(ROWS2, bf16)] * 14, DMA((6,))]
    outs = shaped((ROWS2, f32), ((8, 512), f32), *[((4, 4, 32, 1024), bf16)] * 2)
    return call(
        functools.partial(attn_bwd_kernel, at),
        "attn_bwd",
        [VMEM] * 9 + [ANY] * 6 + [VMEM],
        [VMEM] * 4,
        outs,
        scratch,
        15 * 10**9,
        after,
        carry,
    )(*marked, dx1, norms, saved[0], *w[:4], *map(pin, saved[1:]), x)


def heads_bwd(marked, dx1, saved, w, after=(), carry=()):
    scratch = [pltpu.VMEM(ROWS2, f32), *[pltpu.VMEM(ROWS2, bf16)] * 10, DMA((6,))]
    outs = shaped(*[(ROWS2, bf16)] * 3, *[((4, 4, 32, 256), bf16)] * 2)
    return call(
        heads_bwd_kernel,
        "heads_bwd",
        [VMEM] * 8 + [ANY] * 6,
        [VMEM] * 5,
        outs,
        scratch,
        10 * 10**9,
        after,
        carry,
    )(*marked, dx1, saved[0], *w[:4], *map(pin, saved[1:]))


def rows_bwd(ids, marked, dx1, norms, parts, other_small, d_x1, w, d_w, after=(), carry=()):
    scratch = [pltpu.VMEM((8, 512), f32), *[pltpu.VMEM(ROWS2, bf16)] * 2]
    outs = shaped(*[((256, 512), f32), ((256, 512), bf16)] * 2, *[((4, 4, 32, 1152), bf16)] * 2)
    return call(
        rows_bwd_kernel,
        "rows_bwd",
        [SMEM] + [VMEM] * 23,
        [VMEM] * 6,
        outs,
        scratch,
        10 * 10**9,
        after,
        carry,
    )(ids, *marked, dx1, norms, *parts, other_small, d_x1, *w[:4], *d_w)


def code_prep(book_t, after=(), carry=()):
    codes = book_t.shape[1]
    return call(
        code_prep_kernel,
        "code_prep",
        [VMEM],
        [VMEM] * 2,
        shaped(((codes, 256), bf16), ((128, codes), bf16)),
        [],
        6 * 10**9,
        after,
        carry,
    )(book_t)


def mlp_vq(x1, norms, vq_w, stack, stack_t, w, after=(), carry=()):
    return call(
        mlp_vq_kernel,
        "mlp_vq",
        [VMEM] * 3 + [ANY] * 2 + [VMEM] * 8,
        [VMEM] * 3 + [ANY],
        shaped((ROWS2, f32), (ROWS2, f32), ((72, 512), f32))
        + [pltpu.HBM((stack.shape[0], 512), bf16)],
        [
            pltpu.VMEM(ROWS2, bf16),
            pltpu.VMEM((128, 512), f32),
            pltpu.VMEM(stack.shape, bf16),
            pltpu.VMEM(stack_t.shape, bf16),
            pltpu.VMEM((2, 2048, 512), bf16),
            DMA((2, 4)),
            DMA((2,)),
        ],
        25 * 10**9,
        after,
        carry,
    )(x1, norms, vq_w, pin(stack), pin(stack_t), *w)


def vq_bwd(ids, e, du, norms, vq_w, codes, kept, smalls, after=(), carry=()):
    scratch = [
        pltpu.VMEM((96, 512), f32),
        pltpu.VMEM(codes[2].shape, bf16),
        pltpu.VMEM((96, 512), f32),
        pltpu.VMEM((8, 32, 512), bf16),
        *[pltpu.VMEM(a.shape, a.dtype) for a in codes],
        DMA((4, 4)),
        DMA((2, 2, 4)),
    ]
    return call(
        vq_bwd_kernel,
        "vq_bwd",
        [SMEM] + [VMEM] * 4 + [ANY] * 4 + [VMEM] * 3,
        [VMEM] + [ANY] * 2,
        shaped((ROWS2, f32), *[((4, 32, 1536), bf16)] * 2),
        scratch,
        25 * 10**9,
        after,
        carry,
    )(ids, e, du, norms, vq_w, *map(pin, codes), kept, *smalls)


def lines_kernel(cuts, *refs):
    first = 0
    for out, width in zip(refs[4:], cuts):
        for k in range(4):
            out[k] = refs[k][:, first : first + width]
        first += width


def stack_lines(shards, cuts, after=(), carry=()):
    return call(
        functools.partial(lines_kernel, cuts),
        "stack_lines",
        [VMEM] * 4,
        [VMEM] * len(cuts),
        shaped(*[((4, 32, width), bf16) for width in cuts]),
        [],
        1,
        after,
        carry,
    )(*shards)


def pack_kernel(*refs):
    hbm, outs, held, sems = refs[:4], refs[4:6], refs[6:10], refs[10]
    copies = [pltpu.make_async_copy(hbm[at], held[at], sems.at[at]) for at in range(4)]
    start_all(copies)
    wait_all(copies)
    qkv, out_t, up, down_t = held
    for layer, out in enumerate(outs):
        for index in range(3):
            out[:, index * 256 : (index + 1) * 256] = qkv[layer, index]
        out[:, 768:1024] = out_t[layer]
        out[:, 1024:2048] = up[layer]
        out[:, 2048:] = down_t[layer]


def pack_weights(*arrays):
    return call(
        pack_kernel,
        "pack_weights",
        [ANY] * 4,
        [VMEM] * 2,
        shaped(*[((32, 3072), bf16)] * 2),
        [*[pltpu.VMEM(a.shape, a.dtype) for a in arrays], DMA((4,))],
        1,
    )(*map(pin, arrays))[:-1]


def pairs_kernel(*refs):
    count = len(refs) // 3
    for at in range(count):
        refs[2 * count + at][0] = refs[2 * at][...]
        refs[2 * count + at][1] = refs[2 * at + 1][...]


def stack_pairs(pairs, after=(), carry=()):
    return call(
        pairs_kernel,
        "stack_pairs",
        [VMEM] * (2 * len(pairs)),
        [VMEM] * len(pairs),
        shaped(*[((2, *a.shape), bf16) for a, _ in pairs]),
        [],
        1,
        after,
        carry,
    )(*[array for pair in pairs for array in pair])


def gate(after, carry):
    def kernel(out):
        out[...] = jnp.zeros_like(out)

    return call(kernel, "gate", [], [VMEM], shaped(((8, 128), f32)), [], 1, after, carry)()[-1]


def rows_in_kernel(ids, *refs):
    hbm, (own, send, norms, vq_w), held, sems = refs[:7], refs[7:11], refs[11:18], refs[18]
    copies = [pltpu.make_async_copy(hbm[at], held[at], sems.at[at]) for at in range(7)]
    start_all(copies)
    matrix = order_matrix(ids[0], False)
    wait_all(copies)
    tokens, segs, cot, gains, biases, in_t, out_w = held
    for to, micro in ((send, 1 - ids[1]), (own, ids[1])):
        to[:, :512] = ordered(tokens[micro], matrix).astype(bf16)
        ids_row = segs[pl.ds(micro, 1), :].astype(f32)
        to[:, 512:640] = jnp.broadcast_to(ids_row, (128, 256)).T.astype(bf16)
    send[:, 640:] = ordered(cot[1 - ids[1]].astype(bf16), matrix).astype(bf16)
    pad = jnp.zeros((3, 512), f32)
    rows = jnp.concatenate([gains[...], pad, biases[...], pad], axis=0)
    norms[...] = ordered(rows, matrix)
    vq_w[...] = ordered(jnp.concatenate([in_t[...], out_w[...]], axis=0), matrix)


def rows_in(ids, *arrays):
    outs = shaped(
        ((256, 640), bf16), ((256, 1152), bf16), ((16, 512), f32), ((64, 512), f32)
    )
    return call(
        rows_in_kernel,
        "rows_in",
        [SMEM] + [ANY] * 7,
        [VMEM] * 4,
        outs,
        [*[pltpu.VMEM(a.shape, a.dtype) for a in arrays], DMA((7,))],
        1,
    )(ids, *map(pin, arrays))[:-1]


def joined(block):
    return block[0:16, 1024:].astype(f32) + block[16:32, 1024:].astype(f32)


def put_small(value, own, blocks):
    hi, lo = split2(value)
    own[0:16, 1024:] = hi.astype(f32) + lo.astype(f32)
    for block in blocks:
        block[0:16, 1024:] = hi
        block[16:32, 1024:] = lo


def near_kernel(ids, ins, outs):
    keep, other = ins
    for i in range(4):
        outs[i][...] = (keep[i].astype(f32) + other[i].astype(f32)).astype(outs[i].dtype)
    if keep.shape[3] == 1152:
        value = joined(keep.at[0, 0]) + joined(other.at[0, 0])
        put_small(value, outs[0].at[0], [out.at[0] for out in outs[1:]])


def near_task(keep, other):
    shape = keep.shape[1:]
    return near_kernel, [keep, other], shaped((shape, f32), *[(shape, bf16)] * 3)


def put_code(ref, first, code):
    for i in range(3):
        ref[first + i] = code[:, 1024 * i : 1024 * (i + 1)]


def get_code(ref, first):
    return jnp.concatenate([ref[first + i] for i in range(3)], axis=1)


def swapped(code):
    return jnp.concatenate([code[:, 1536:], code[:, :1536]], axis=1)


def code_sum(a, b):
    done = []
    for first in range(0, a.shape[1], 1536):
        total = a[:, first : first + 1024].astype(f32) + b[:, first : first + 1024].astype(f32)
        small = [
            x[:, first + 1024 : first + 1280].astype(f32) + x[:, first + 1280 : first + 1536].astype(f32)
            for x in (a, b)
        ]
        done += [total.astype(bf16), *split2(small[0] + small[1])]
    return jnp.concatenate(done, axis=1)


def fork_kernel(ids, ins, outs):
    keep, other = ins
    own_a, to_x, own_b, to_y = outs
    half = keep.shape[3] // 2
    for at, (own, send, kept, sent) in enumerate(
        ((own_a, to_x, (0, 2), (1, 3)), (own_b, to_y, (0, 1), (2, 3)))
    ):
        cols = slice(half * at, half * (at + 1))
        for j in range(2):
            own[j] = keep[kept[j], :, :, cols].astype(f32) + other[kept[j], :, :, cols].astype(f32)
            total = keep[sent[j], :, :, cols].astype(f32) + other[sent[j], :, :, cols].astype(f32)
            send[4 * j : 4 * (j + 1)] = total.astype(bf16)


def fork_task(keep, other):
    half = keep.shape[3] // 2
    outs = shaped(*[((2, 4, 32, half), f32), ((8, 32, half), bf16)] * 2)
    return fork_kernel, [keep, other], outs


def half_kernel(ids, ins, outs):
    own_a, from_x, own_b, from_y = ins[:4]
    kept_a, to_y, kept_b, to_x = outs[:4]
    for own, other, kept, send in (
        (own_a, from_x, kept_a, to_y),
        (own_b, from_y, kept_b, to_x),
    ):
        kept[...] = own[0] + other[0:4].astype(f32)
        send[0:4] = (own[1] + other[4:8].astype(f32)).astype(bf16)
    if len(ins) == 6:
        code, code_other = ins[4:]
        outs[4][...] = code_sum(code[...], swapped(code_other[...]))
        put_code(to_x, 4, outs[4])


def half_task(own_a, from_x, own_b, from_y, *codes):
    width = own_a.shape[3]
    outs = shaped(
        ((4, 32, width), f32),
        ((4, 32, width), bf16),
        ((4, 32, width), f32),
        ((7 if codes else 4, 32, width), bf16),
        *[(code.shape, bf16) for code in codes[:1]],
    )
    return half_kernel, [own_a, from_x, own_b, from_y, *codes], outs


def join_kernel(ids, ins, outs):
    kept, send = outs[:2]
    width = ins[0].shape[2]
    for at, (own, other) in enumerate((ins[0:2], ins[2:4])):
        cols = slice(width * at, width * (at + 1))
        for k in range(2):
            kept[k, :, cols] = own[2 * k] + other[2 * k].astype(f32)
            send[k, :, cols] = (own[2 * k + 1] + other[2 * k + 1].astype(f32)).astype(bf16)
    if len(ins) == 5:
        outs[2][...] = code_sum(ins[4][...], get_code(ins[3], 4))


def join_task(own_a, from_y, own_b, from_x, *codes):
    width = 2 * own_a.shape[2]
    outs = shaped(
        ((2, 32, width), f32),
        ((2, 32, width), bf16),
        *[(code.shape, bf16) for code in codes],
    )
    return join_kernel, [own_a, from_y, own_b, from_x, *codes], outs


def line_step_kernel(ids, ins, outs):
    kept, other = ins
    outs[0][...] = kept[0] + other[0].astype(f32)
    outs[1][...] = (kept[1] + other[1].astype(f32)).astype(bf16)


def line_step_task(kept, other):
    shape = kept.shape[1:]
    return line_step_kernel, [kept, other], shaped((shape, f32), (shape, bf16))


def line_pair_kernel(ids, ins, outs):
    kept, other, beside = ins
    width = kept.shape[2]
    outs[0][...] = kept[0] + other[0].astype(f32)
    outs[1][:, :width] = (kept[1] + other[1].astype(f32)).astype(bf16)
    outs[1][:, width:] = beside[...]


def line_pair_task(kept, other, beside):
    shape = kept.shape[1:]
    both = (shape[0], shape[1] + beside.shape[1])
    return line_pair_kernel, [kept, other, beside], shaped((shape, f32), (both, bf16))


def plane_line_kernel(ids, ins, outs):
    kept, send = outs
    for k in range(4):
        total = ins[0][k]
        for other in ins[1:]:
            total = total + other[k].astype(f32)
        to = send if k % 2 else kept
        to[k // 2] = total.astype(to.dtype)
    x, y, xy = [joined(other.at[0]) for other in ins[1:]]
    put_small((ins[0][0, 0:16, 1024:] + x) + (y + xy), kept.at[0], [send.at[0]])


def plane_line_task(own, others):
    outs = shaped(((2, 32, 1152), f32), ((2, 32, 1152), bf16))
    return plane_line_kernel, [own, *others], outs


def small_step_kernel(ids, ins, outs):
    kept, other = ins
    line_step_kernel(ids, ins, outs)
    put_small(kept[0, 0:16, 1024:] + joined(other.at[0]), outs[0], [outs[1]])


def small_step_task(kept, other):
    shape = kept.shape[1:]
    return small_step_kernel, [kept, other], shaped((shape, f32), (shape, bf16))


def line_total(ins, width):
    total = ins[0][:, :width]
    for other in ins[1:]:
        total = total + other[:, :width].astype(f32)
    return total


def rows_out_kernel(ids, ins, outs):
    y, y_low, dx, dx_low = ins
    matrix = order_matrix(ids[0], True)
    outs[0][...] = ordered(y[...], matrix)
    outs[1][...] = ordered(dx[...], matrix)
    outs[2][0:256, :] = ordered(y_low[...], matrix).astype(bf16)
    outs[2][256:, :] = ordered(dx_low[...], matrix).astype(bf16)


def rows_out_task(y, y_low, dx, dx_low):
    outs = shaped((y.shape, f32), (dx.shape, f32), (ROWS2, bf16))
    return rows_out_kernel, [y, y_low, dx, dx_low], outs


def rows_done_kernel(ids, y, dx, others, decoded, grad_tokens, held, sems):
    copies = []
    for at, (out, own) in enumerate(((decoded, y), (grad_tokens, dx))):
        held[at] = others[256 * at : 256 * (at + 1), :].astype(f32)
        copies.append(pltpu.make_async_copy(own, out.at[ids[1]], sems.at[at, 0]))
        copies.append(pltpu.make_async_copy(held.at[at], out.at[1 - ids[1]], sems.at[at, 1]))
    start_all(copies)
    wait_all(copies)


def rows_done(ids, y, dx, others, after):
    return call(
        rows_done_kernel,
        "rows_done",
        [SMEM] + [VMEM] * 3,
        [ANY] * 2,
        [pltpu.HBM((2, 256, 512), f32)] * 2,
        [pltpu.VMEM((2, 256, 512), f32), DMA((2, 2))],
        10**9,
        after,
    )(ids, y, dx, others)[:-1]


def code_near_kernel(ids, ins, outs):
    keep, other = ins
    for at, out in enumerate(outs):
        for i in range(2):
            out[:, 1536 * i : 1536 * (i + 1)] = code_sum(keep[2 * at + i], other[2 * at + i])


def code_near_task(keep, other):
    return code_near_kernel, [keep, other], shaped(*[((32, 3072), bf16)] * 2)


def code_add_kernel(ids, ins, outs):
    outs[0][...] = code_sum(ins[0][...], ins[1][...])


def code_add_task(a, b):
    return code_add_kernel, [a, b], shaped((a.shape, bf16))


def code_pair_kernel(ids, ins, outs):
    for at, part in enumerate(ins):
        outs[0][:, 3072 * at : 3072 * (at + 1)] = part[...]


def code_pair_task(a, b):
    return code_pair_kernel, [a, b], shaped(((32, 6144), bf16))


def finish_kernel(ids, ins, outs):
    mlp, attn, d_mlp = (ins[0], ins[1].at[:, pl.ds(0, 2048)]), ins[2:4], ins[4:6]
    d_attn, code, code_other = (ins[6], ins[1].at[:, pl.ds(2048, 1024)]), *ins[7:]
    qkv, out_t, up, down_t, book, vq_in, vq_out, gains, biases, dec_biases, small_ref = outs
    for layer, rows in enumerate((line_total(mlp, 2048), line_total(d_mlp, 2048))):
        up[layer] = rows[:, :1024]
        down_t[layer] = rows[:, 1024:]
    for layer, rows in enumerate((line_total(attn, 1024), line_total(d_attn, 1024))):
        for index in range(3):
            qkv[layer, index] = rows[:, index * 256 : (index + 1) * 256]
        out_t[layer] = rows[:, 768:]
    core, z = ids[0] % 2, ids[0] // 4
    for at, parts in ((core, code), (1 - core, code_other)):
        for k in range(4):
            part = at * 4 + (z ^ k)
            held = parts[:, 1536 * k : 1536 * (k + 1)].astype(f32)
            book[:, pl.ds(pl.multiple_of(part * 1024, 1024), 1024)] = held[:, :1024]
            small_ref[:, pl.ds(pl.multiple_of(part * 256, 256), 256)] = (
                held[:, 1024:1280] + held[:, 1280:1536]
            )
    small = small_ref[...]
    vq_in[...] = small[:, :512]
    vq_out[...] = small[:, 512:1024]
    rest = small[:, 1024:1536]
    packed = attn[0][0:16, 1024:] + joined(attn[1])
    for row, out in enumerate((gains.at[0:1], biases.at[0:1], gains.at[1:2], biases.at[1:2])):
        for j in range(4):
            out[:, 128 * j : 128 * (j + 1)] = packed[row * 4 + j : row * 4 + j + 1, :]
    gains[2:3, :] = rest[0:1, :]
    biases[2:3, :] = rest[1:2, :]
    gains[3:4, :] = rest[2:3, :]
    dec_biases[0:1, :] = rest[3:4, :]
    gains[4:5, :] = rest[4:5, :]
    dec_biases[1:2, :] = rest[5:6, :]


def finish_task(mlp, attn, d_mlp, d_attn, code, code_other):
    outs = shaped(
        ((2, 3, 32, 256), f32),
        ((2, 32, 256), f32),
        ((2, 32, 1024), f32),
        ((2, 32, 1024), f32),
        ((32, 8192), f32),
        ((32, 512), f32),
        ((32, 512), f32),
        ((5, 512), f32),
        ((3, 512), f32),
        ((2, 512), f32),
        ((32, 2048), f32),
    )
    ins = [*mlp, *attn, *d_mlp, d_attn, code, code_other]
    return finish_kernel, ins, outs


def run_tasks(ids, name, tasks, after=(), carry=()):
    sizes = [(len(ins), len(outs)) for _, ins, outs in tasks]
    n_in = sum(i for i, _ in sizes)

    def kernel(ids_ref, *refs):
        at_in, at_out = 0, n_in
        for (fn, _, _), (i, o) in zip(tasks, sizes):
            fn(ids_ref, refs[at_in : at_in + i], refs[at_out : at_out + o])
            at_in, at_out = at_in + i, at_out + o

    outs = [one for _, _, many in tasks for one in many]
    res = call(
        kernel, name, [SMEM] + [VMEM] * n_in, [VMEM] * len(outs), outs, [], 10**9, after, carry
    )(ids, *[one for _, many, _ in tasks for one in many])
    split, at = [], 0
    for _, o in sizes:
        split.append(res[at : at + o])
        at += o
    return (*split, res[-1])


def whole_groups(
    n_dp,
    tokens,
    segment_ids,
    norm_gains,
    norm_biases,
    w_qkv,
    w_attn_out,
    w_up,
    w_down,
    w_vq_in,
    w_vq_out,
    codebook,
    cotangent,
):
    dp_at, tp_at = lax.axis_index("dp"), lax.axis_index("tp")
    ids = jnp.stack([dp_at, tp_at]).astype(jnp.int32)

    def swap(values):
        return exchange(values, 0, 1, n_dp)

    def core(values):
        return [values, exchange(values, 1, 0, n_dp)]

    book_t = codebook.T
    enc_shard, dec_shard = pack_weights(
        w_qkv, w_attn_out.transpose(0, 2, 1), w_up, w_down.transpose(0, 2, 1)
    )
    enc_shards = spread_line(enc_shard, n_dp)
    own, send, norms, vq_w = rows_in(
        ids,
        tokens,
        segment_ids,
        cotangent,
        norm_gains,
        norm_biases,
        w_vq_in.T,
        w_vq_out,
    )
    marked = [own, swap(send)]

    line_a, line_b, (dec_shard,) = stack_lines(enc_shards, [1536] * 2, carry=[dec_shard])
    along_x, along_y = exchange(line_a, 0, 1, n_dp), exchange(line_b, 2, 0, n_dp)
    dec_shards = spread_line(dec_shard, n_dp)
    stack, stack_t, _ = code_prep(book_t, [line_a])
    codes = (stack, stack_t, book_t)
    a_0, b_0, _ = stack_pairs([(line_a, along_x), (line_b, along_y)], [stack_t, marked[1]])
    a_1, b_1 = exchange(a_0, 2, 0, n_dp), exchange(b_0, 0, 1, n_dp)
    line_a, line_b, (a_0, b_0) = stack_lines(dec_shards, [1536] * 2, [a_1, b_1], [a_0, b_0])
    enc_w = [a_0, a_1, exchange(a_0, 1, 0, n_dp), exchange(a_1, 1, 0, n_dp)]
    enc_w += [b_0, b_1, exchange(b_0, 1, 0, n_dp), exchange(b_1, 1, 0, n_dp)]
    along_x, along_y = exchange(line_a, 0, 1, n_dp), exchange(line_b, 2, 0, n_dp)
    e_x1, e_saved, _ = attn_fwd(0, marked, [], norms, enc_w)
    a_0, b_0, _ = stack_pairs([(line_a, along_x), (line_b, along_y)], [e_x1])
    a_1, b_1 = exchange(a_0, 2, 0, n_dp), exchange(b_0, 0, 1, n_dp)
    dec_w = [a_0, exchange(a_0, 1, 0, n_dp), b_0, exchange(b_0, 1, 0, n_dp)]
    e, u, kept, numer, _ = mlp_vq(e_x1, norms, vq_w, stack, stack_t, enc_w, [a_0, b_0])
    a_1, b_1 = gate([u], [a_1, b_1])
    a_1, b_1 = core(a_1), core(b_1)
    dec_w = [dec_w[0], a_1[0], dec_w[1], a_1[1], dec_w[2], b_1[0], dec_w[3], b_1[1]]
    d_x1, d_saved, _ = attn_fwd(3, marked, [u], norms, dec_w)

    dx1, d_small1, keep_m, send_m, _ = mlp_bwd(
        4, ids, d_x1, [cotangent, marked[1]], norms, dec_w
    )
    near_m = exchange(send_m, 1, 0, n_dp)
    du, d_small0, keep_a, send_a, (keep_m,) = attn_bwd(
        3, marked, u, dx1, norms, d_saved, dec_w, carry=[keep_m]
    )
    (m_a, to_x, m_b, to_y), (send_a,) = run_tasks(
        ids, "sums1", [fork_task(keep_m, near_m)], carry=[send_a]
    )
    from_x, from_y = exchange(to_x, 0, 1, n_dp), exchange(to_y, 2, 0, n_dp)
    near_a = exchange(send_a, 1, 0, n_dp)
    de, code, code_send, (m_a, m_b, keep_a) = vq_bwd(
        ids,
        e,
        du,
        norms,
        vq_w,
        [*codes, numer],
        kept,
        [d_small0, d_small1],
        [to_x, to_y],
        [m_a, m_b, keep_a],
    )
    (m_a, m_y, m_b, m_x), (a_a, to_x, a_b, to_y), (code, code_send) = run_tasks(
        ids,
        "sums2",
        [half_task(m_a, from_x, m_b, from_y), fork_task(keep_a, near_a)],
        carry=[code, code_send],
    )
    code_other = exchange(code_send, 1, 0, n_dp)
    from_m_y, from_m_x = exchange(m_y, 2, 0, n_dp), exchange(m_x, 0, 1, n_dp)
    from_x, from_y = exchange(to_x, 0, 1, n_dp), exchange(to_y, 2, 0, n_dp)
    (code, code_send), _ = run_tasks(ids, "sums2b", [code_near_task(code, code_other)])
    code_other = exchange(code_send, 8, 0, n_dp)
    ex1, e_small1, keep_m, send_m, (m_a, m_b, a_a, a_b, code) = mlp_bwd(
        1,
        ids,
        e_x1,
        [de],
        norms,
        enc_w,
        [m_y, m_x, to_x, to_y, code_send],
        [m_a, m_b, a_a, a_b, code],
    )
    (own_dm, send_dm), (a_a, to_y, a_b, to_x), (code,), (keep_m, send_m) = run_tasks(
        ids,
        "sums3",
        [
            join_task(m_a, from_m_y, m_b, from_m_x),
            half_task(a_a, from_x, a_b, from_y),
            code_add_task(code, code_other),
        ],
        carry=[keep_m, send_m],
    )
    near_m, code_other = exchange(send_m, 1, 0, n_dp), exchange(code, 2, 0, n_dp)
    from_y, from_x = exchange(to_y, 2, 0, n_dp), exchange(to_x, 0, 1, n_dp)
    other_dm = exchange(send_dm, 4, 0, n_dp)
    *parts, (a_a, a_b, own_dm) = heads_bwd(
        marked, ex1, e_saved, enc_w, [to_x, to_y, send_dm, code], [a_a, a_b, own_dm]
    )
    (m_a, to_x, m_b, to_y), (code,), (own_da, send_da), (own_dm, send_dm), _ = run_tasks(
        ids,
        "sums3b",
        [
            fork_task(keep_m, near_m),
            code_add_task(code, code_other),
            join_task(a_a, from_y, a_b, from_x),
            line_step_task(own_dm, other_dm),
        ],
        [parts[0]],
    )
    other_dm, code_other = exchange(send_dm, 8, 0, n_dp), exchange(code, 4, 0, n_dp)
    from_y, from_x = exchange(to_y, 2, 0, n_dp), exchange(to_x, 0, 1, n_dp)
    dx, dx_low, y, y_low, keep_a, send_a, (m_a, m_b, own_dm, own_da, send_da) = rows_bwd(
        ids,
        marked,
        ex1,
        norms,
        parts,
        e_small1,
        d_x1,
        enc_w,
        dec_w,
        [to_x, to_y, send_dm, code],
        [m_a, m_b, own_dm, own_da, send_da],
    )
    (m_a, to_y, m_b, to_x, code), (keep_a, send_a, send_da) = run_tasks(
        ids,
        "sums4",
        [half_task(m_a, from_x, m_b, from_y, code, code_other)],
        [other_dm],
        [keep_a, send_a, send_da],
    )
    near_a, other_da = exchange(send_a, 1, 0, n_dp), exchange(send_da, 4, 0, n_dp)
    from_y, from_x = exchange(to_y, 2, 0, n_dp), exchange(to_x, 0, 1, n_dp)
    (own_a, *lows_a), (own_da, send_da), (m_a, m_b, code) = run_tasks(
        ids,
        "sums4b",
        [near_task(keep_a, near_a), line_step_task(own_da, other_da)],
        carry=[m_a, m_b, code],
    )
    plane_a = plane_send(lows_a, n_dp)
    (own_m, send_m, code), (own_a,) = run_tasks(
        ids,
        "sums5",
        [join_task(m_a, from_y, m_b, from_x, code)],
        lows_a,
        [own_a],
    )
    other_m, code_other = exchange(send_m, 4, 0, n_dp), exchange(code, 8, 0, n_dp)
    (y, dx, rows), (own_a,) = run_tasks(
        ids, "rows_out", [rows_out_task(y, y_low, dx, dx_low)], [send_m, code], [own_a]
    )
    (own_a, send_a), (own_m, send_m), (code,), (rows,) = run_tasks(
        ids,
        "sums6",
        [
            plane_line_task(own_a, plane_a),
            line_pair_task(own_m, other_m, send_da),
            code_pair_task(code, code_other),
        ],
        carry=[rows],
    )
    other_a, other_m = exchange(send_a, 4, 0, n_dp), exchange(send_m, 8, 0, n_dp)
    code_other, rows = exchange(code, 1, 0, n_dp), swap(rows)
    (own_a, send_a), _ = run_tasks(ids, "sums7", [small_step_task(own_a, other_a)])
    other_a = exchange(send_a, 8, 0, n_dp)
    decoded, grad_tokens = rows_done(ids, y, dx, rows, [send_a])
    (qkv, out_t, up, down_t, book, vq_in, vq_out, *norm_grads, _), _ = run_tasks(
        ids,
        "finish",
        [
            finish_task(
                (own_m, other_m),
                (own_a, other_a),
                (own_dm, other_dm),
                own_da,
                code,
                code_other,
            )
        ],
        [decoded],
    )
    return (
        decoded,
        grad_tokens,
        *norm_grads,
        qkv,
        out_t.transpose(0, 2, 1),
        up,
        down_t.transpose(0, 2, 1),
        vq_in.T,
        vq_out,
        book.T,
    )


def layer_norm(values, norm_gain, norm_bias):
    centred = values - jnp.mean(values, axis=-1, keepdims=True)
    spread = jnp.mean(centred * centred, axis=-1, keepdims=True)
    return centred * lax.rsqrt(spread + ln_eps) * norm_gain + norm_bias


def gelu_tanh(values):
    return (
        0.5 * values * (1.0 + jnp.tanh(gelu_coef * (values + 0.044715 * values * values * values)))
    )


def matmul(former, latter):
    return jnp.dot(former, latter, precision=highest, preferred_element_type=jnp.float32)


def normalize(values):
    return values * lax.rsqrt(jnp.sum(values * values, axis=-1, keepdims=True) + norm_eps)


def quantize(in_rows, norm_gain, norm_bias, in_w, out_w, code_w):
    latent = normalize(matmul(layer_norm(in_rows, norm_gain, norm_bias), in_w))
    code_rows = normalize(code_w)
    logits = matmul(latent, code_rows.T) * temper
    row_max = jnp.max(logits, axis=-1, keepdims=True)
    numerator = jnp.exp(logits - row_max)
    assign = numerator / jnp.sum(numerator, axis=-1, keepdims=True)
    soft_code = matmul(assign, code_rows)
    offset = latent - soft_code
    vq_loss = commit_weight * 1.25 * jnp.sum(offset * offset)
    return (matmul(soft_code, out_w), vq_loss)


def product(former, latter):
    return jnp.dot(former, latter, preferred_element_type=jnp.float32)


def product_tn(former, latter):
    return lax.dot_general(
        former, latter, (((0,), (0,)), ((), ())), preferred_element_type=jnp.float32
    )


def product_nt(former, latter):
    return lax.dot_general(
        former, latter, (((1,), (1,)), ((), ())), preferred_element_type=jnp.float32
    )


def split_heads(values):
    return values.reshape(values.shape[0], values.shape[1] // HEAD_DIM, HEAD_DIM).transpose(1, 0, 2)


def join_heads(values):
    return values.transpose(1, 0, 2).reshape(values.shape[1], values.shape[0] * HEAD_DIM)


def masked_scores(query_blk, key_h, seg_blk, seg_keys):
    scores = jnp.einsum(
        "hqd,hkd->hqk", query_blk, key_h, preferred_element_type=jnp.float32
    ) * HEAD_DIM ** (-0.5)
    return jnp.where((seg_blk[:, None] == seg_keys[None, :])[None], scores, masked_score)


def attend(query_h, key_h, value_h, seg_keys):
    block_rows = min(512, query_h.shape[1])
    block_count = query_h.shape[1] // block_rows

    def one_block(begin_row):
        query_blk = lax.dynamic_slice_in_dim(query_h, begin_row, block_rows, 1)
        seg_blk = lax.dynamic_slice_in_dim(seg_keys, begin_row, block_rows, 0)
        scores = masked_scores(query_blk, key_h, seg_blk, seg_keys)
        row_max = jnp.max(scores, axis=-1, keepdims=True)
        numerator = jnp.exp(scores - row_max)
        row_total = jnp.sum(numerator, axis=-1, keepdims=True)
        prob_low = (numerator / row_total).astype(jnp.bfloat16)
        attended = jnp.einsum("hqk,hkd->hqd", prob_low, value_h, preferred_element_type=jnp.float32)
        return (attended.astype(jnp.bfloat16), (row_max + jnp.log(row_total))[..., 0])

    starts = jnp.arange(block_count, dtype=jnp.int32) * block_rows
    attended, log_sums = lax.map(one_block, starts)
    heads_out = attended.transpose(1, 0, 2, 3).reshape(query_h.shape)
    log_sums = log_sums.transpose(1, 0, 2).reshape(query_h.shape[0], query_h.shape[1])
    return (heads_out, log_sums)


def attend_back(query_h, key_h, value_h, seg_keys, log_sums, grad_out):
    block_rows = min(512, query_h.shape[1])
    block_count = query_h.shape[1] // block_rows

    def one_block(carry, begin_row):
        grad_key, grad_value = carry
        query_blk = lax.dynamic_slice_in_dim(query_h, begin_row, block_rows, 1)
        grad_blk = lax.dynamic_slice_in_dim(grad_out, begin_row, block_rows, 1)
        lse_blk = lax.dynamic_slice_in_dim(log_sums, begin_row, block_rows, 1)
        seg_blk = lax.dynamic_slice_in_dim(seg_keys, begin_row, block_rows, 0)
        scores = masked_scores(query_blk, key_h, seg_blk, seg_keys)
        probs = jnp.exp(scores - lse_blk[..., None])
        prob_low = probs.astype(jnp.bfloat16)
        grad_value = grad_value + jnp.einsum(
            "hqk,hqd->hkd", prob_low, grad_blk, preferred_element_type=jnp.float32
        )
        grad_prob = jnp.einsum(
            "hqd,hkd->hqk", grad_blk, value_h, preferred_element_type=jnp.float32
        )
        row_dot = jnp.sum(probs * grad_prob, axis=-1, keepdims=True)
        grad_score = (probs * (grad_prob - row_dot) * HEAD_DIM ** (-0.5)).astype(jnp.bfloat16)
        grad_query = jnp.einsum(
            "hqk,hkd->hqd", grad_score, key_h, preferred_element_type=jnp.float32
        )
        grad_key = grad_key + jnp.einsum(
            "hqk,hqd->hkd", grad_score, query_blk, preferred_element_type=jnp.float32
        )
        return ((grad_key, grad_value), grad_query)

    starts = jnp.arange(block_count, dtype=jnp.int32) * block_rows
    zeros_kv = jnp.zeros(key_h.shape, jnp.float32)
    (grad_key, grad_value), grad_query = lax.scan(one_block, (zeros_kv, zeros_kv), starts)
    grad_query = grad_query.transpose(1, 0, 2, 3).reshape(query_h.shape)
    return (
        grad_query.astype(jnp.bfloat16),
        grad_key.astype(jnp.bfloat16),
        grad_value.astype(jnp.bfloat16),
    )


def spread_rows(values):
    return lax.all_gather(values, "tp", axis=0, tiled=True)


def combine_rows(partial_value):
    return lax.psum_scatter(partial_value, "tp", scatter_dimension=0, tiled=True)


def spread_grads(values):
    return lax.all_gather(values, "tp", axis=0, tiled=True)


def combine_grads(partial_value):
    return lax.psum_scatter(
        partial_value.astype(jnp.bfloat16), "tp", scatter_dimension=0, tiled=True
    ).astype(jnp.float32)


def fetch_weights(w_qkv, w_attn_out, w_up, w_down, layer):
    return (
        lax.all_gather(w_qkv[layer], "dp", axis=1, tiled=True),
        lax.all_gather(w_attn_out[layer], "dp", axis=1, tiled=True),
        lax.all_gather(w_up[layer], "dp", axis=0, tiled=True),
        lax.all_gather(w_down[layer], "dp", axis=1, tiled=True),
    )


def reduce_weight_grads(grads):
    return (
        lax.psum_scatter(
            grads[0].astype(jnp.bfloat16), "dp", scatter_dimension=1, tiled=True
        ).astype(jnp.float32),
        lax.psum_scatter(
            grads[1].astype(jnp.bfloat16), "dp", scatter_dimension=1, tiled=True
        ).astype(jnp.float32),
        lax.psum_scatter(
            grads[2].astype(jnp.bfloat16), "dp", scatter_dimension=0, tiled=True
        ).astype(jnp.float32),
        lax.psum_scatter(
            grads[3].astype(jnp.bfloat16), "dp", scatter_dimension=1, tiled=True
        ).astype(jnp.float32),
    )


def block_forward(resid_in, seg_local, gains, biases, weights):
    qkv_w, attn_w, up_w, down_w = weights
    normed = layer_norm(resid_in, gains[0], biases[0]).astype(jnp.bfloat16)
    normed_all, seg_all = (
        lax.all_gather(normed, "tp", axis=0, tiled=True),
        lax.all_gather(seg_local, "tp", axis=0, tiled=True),
    )
    query_h = split_heads(product(normed_all, qkv_w[0]).astype(jnp.bfloat16))
    key_h = split_heads(product(normed_all, qkv_w[1]).astype(jnp.bfloat16))
    value_h = split_heads(product(normed_all, qkv_w[2]).astype(jnp.bfloat16))
    heads_out, log_sums = attend(query_h, key_h, value_h, seg_all)
    attn_rows = join_heads(heads_out)
    middle = resid_in + combine_rows(product(attn_rows, attn_w))
    normed_mid = spread_rows(layer_norm(middle, gains[1], biases[1]).astype(jnp.bfloat16))
    hidden_pre = product(normed_mid, up_w)
    hidden = gelu_tanh(hidden_pre).astype(jnp.bfloat16)
    result = middle + combine_rows(product(hidden, down_w))
    kept = (
        resid_in,
        middle,
        normed_all,
        seg_all,
        query_h,
        key_h,
        value_h,
        log_sums,
        attn_rows,
        normed_mid,
        hidden_pre,
        hidden,
    )
    return (result, kept)


def block_backward(kept, gains, biases, weights, grad_result):
    (
        resid_in,
        middle,
        normed_all,
        seg_all,
        query_h,
        key_h,
        value_h,
        log_sums,
        attn_rows,
        normed_mid,
        hidden_pre,
        hidden,
    ) = kept
    qkv_w, attn_w, up_w, down_w = weights
    grad_branch = spread_grads(grad_result.astype(jnp.bfloat16))
    grad_down = product_tn(hidden, grad_branch)
    grad_hidden = product_nt(grad_branch, down_w)
    _, gelu_back = jax.vjp(gelu_tanh, hidden_pre)
    grad_pre = gelu_back(grad_hidden)[0].astype(jnp.bfloat16)
    grad_up = product_tn(normed_mid, grad_pre)
    grad_norm_mid = combine_grads(product_nt(grad_pre, up_w))
    _, norm_back_mid = jax.vjp(layer_norm, middle, gains[1], biases[1])
    grad_mid_ln, grad_gain_mid, grad_bias_mid = norm_back_mid(grad_norm_mid)
    grad_middle = grad_result + grad_mid_ln
    grad_attn_all = spread_grads(grad_middle.astype(jnp.bfloat16))
    grad_attn = product_tn(attn_rows, grad_attn_all)
    grad_heads = split_heads(product_nt(grad_attn_all, attn_w).astype(jnp.bfloat16))
    grad_query, grad_key, grad_value = attend_back(
        query_h, key_h, value_h, seg_all, log_sums, grad_heads
    )
    grad_parts = [join_heads(grad_query), join_heads(grad_key), join_heads(grad_value)]
    grad_qkv = jnp.stack([product_tn(normed_all, grad_part) for grad_part in grad_parts])
    grad_normed_part = (
        product_nt(grad_parts[0], qkv_w[0])
        + product_nt(grad_parts[1], qkv_w[1])
        + product_nt(grad_parts[2], qkv_w[2])
    )
    grad_normed = combine_grads(grad_normed_part)
    _, norm_back_in = jax.vjp(layer_norm, resid_in, gains[0], biases[0])
    grad_in_ln, grad_gain_in, grad_bias_in = norm_back_in(grad_normed)
    gain_grads = jnp.stack([grad_gain_in, grad_gain_mid])
    bias_grads = jnp.stack([grad_bias_in, grad_bias_mid])
    return (
        grad_middle + grad_in_ln,
        gain_grads,
        bias_grads,
        (grad_qkv, grad_attn, grad_up, grad_down),
    )


def local(
    tokens,
    segment_ids,
    norm_gains,
    norm_biases,
    w_qkv,
    w_attn_out,
    w_up,
    w_down,
    w_vq_in,
    w_vq_out,
    codebook,
    cotangent,
):
    gain_sum = jnp.zeros(norm_gains.shape, jnp.float32)
    bias_sum = jnp.zeros(norm_biases.shape, jnp.float32)
    vq_in_sum = jnp.zeros(w_vq_in.shape, jnp.float32)
    vq_out_sum = jnp.zeros(w_vq_out.shape, jnp.float32)
    code_sum = jnp.zeros(codebook.shape, jnp.float32)
    layer_sums = [None, None]
    outputs = []
    input_grads = []
    for micro in range(MICRO):
        resid_in = tokens[micro].astype(jnp.float32)
        seg_local = segment_ids[micro]
        enc_weights = fetch_weights(w_qkv, w_attn_out, w_up, w_down, 0)
        encoded, enc_kept = block_forward(
            resid_in, seg_local, norm_gains[0:2], norm_biases[0:2], enc_weights
        )
        (decoder_in, _), vq_back = jax.vjp(
            quantize, encoded, norm_gains[2], norm_biases[2], w_vq_in, w_vq_out, codebook
        )
        dec_weights = fetch_weights(w_qkv, w_attn_out, w_up, w_down, 1)
        decoded, dec_kept = block_forward(
            decoder_in, seg_local, norm_gains[3:5], norm_biases[3:5], dec_weights
        )
        outputs.append(decoded)
        grad_dec_in, gains_dec, biases_dec, grads_dec = block_backward(
            dec_kept, norm_gains[3:5], norm_biases[3:5], dec_weights, cotangent[micro]
        )
        grad_encoded, grad_gain_vq, grad_bias_vq, grad_in_w, grad_out_w, grad_codes = vq_back(
            (grad_dec_in, jnp.ones((), jnp.float32))
        )
        grad_input, gains_enc, biases_enc, grads_enc = block_backward(
            enc_kept, norm_gains[0:2], norm_biases[0:2], enc_weights, grad_encoded
        )
        input_grads.append(grad_input)
        gain_sum = gain_sum + jnp.concatenate([gains_enc, grad_gain_vq[None], gains_dec], axis=0)
        bias_sum = bias_sum + jnp.concatenate([biases_enc, grad_bias_vq[None], biases_dec], axis=0)
        vq_in_sum = vq_in_sum + grad_in_w
        vq_out_sum = vq_out_sum + grad_out_w
        code_sum = code_sum + grad_codes
        for layer, grads in ((0, grads_enc), (1, grads_dec)):
            reduced = reduce_weight_grads(grads)
            if layer_sums[layer] is None:
                layer_sums[layer] = reduced
            else:
                layer_sums[layer] = jax.tree.map(jnp.add, layer_sums[layer], reduced)
    gain_tot, bias_tot, vq_in_tot, vq_out_tot, code_tot = lax.psum(
        (gain_sum, bias_sum, vq_in_sum, vq_out_sum, code_sum), ("dp", "tp")
    )
    return (
        jnp.stack(outputs),
        jnp.stack(input_grads),
        gain_tot,
        bias_tot[0:3],
        bias_tot[3:5],
        jnp.stack([layer_sums[0][0], layer_sums[1][0]]),
        jnp.stack([layer_sums[0][1], layer_sums[1][1]]),
        jnp.stack([layer_sums[0][2], layer_sums[1][2]]),
        jnp.stack([layer_sums[0][3], layer_sums[1][3]]),
        vq_in_tot,
        vq_out_tot,
        code_tot,
    )


def solution(mesh):
    n_dp, n_tp = mesh.shape["dp"], mesh.shape["tp"]
    fits = n_tp == MICRO and n_dp == 16
    return jax.shard_map(
        functools.partial(whole_groups, n_dp) if fits else local,
        mesh=mesh,
        in_specs=(
            P(None, ("dp", "tp"), None),
            P(None, ("dp", "tp")),
            P(),
            P(),
            P(None, None, "dp", "tp"),
            P(None, "tp", "dp"),
            P(None, "dp", "tp"),
            P(None, "tp", "dp"),
            P(),
            P(),
            P(),
            P(None, ("dp", "tp"), None),
        ),
        out_specs=(
            P(None, ("dp", "tp"), None),
            P(None, ("dp", "tp"), None),
            P(),
            P(),
            P(),
            P(None, None, "dp", "tp"),
            P(None, "tp", "dp"),
            P(None, "dp", "tp"),
            P(None, "tp", "dp"),
            P(),
            P(),
            P(),
        ),
        check_vma=False,
    )
```

```python
import functools

import jax
import jax.numpy as jnp
from jax import lax
from jax.experimental import pallas as pl
from jax.experimental.pallas import tpu as pltpu
from jax.sharding import PartitionSpec as P

HEAD_DIM = 64
MICRO = 2
bf16 = jnp.bfloat16
f32 = jnp.float32
highest = lax.Precision.HIGHEST
ln_eps = 1e-05
norm_eps = 1e-06
temper = 10.0
commit_weight = 64.0
gelu_coef = 0.7978845608028654
masked_score = -1e30
log2e = 1.4426950408889634
vmem_cap = 26 * 1024 * 1024


PLANE = ((0, 0), (0, 1), (1, 0), (1, 1))


def exchange(values, dp_xor, tp_xor, n_dp):
    pairs = [
        (d * 2 + t, (d ^ dp_xor) * 2 + (t ^ tp_xor)) for d in range(n_dp) for t in range(2)
    ]
    return lax.ppermute(values, ("dp", "tp"), pairs)


def spread_line(shard, n_dp):
    return [shard] + [exchange(shard, 4 * k, 0, n_dp) for k in range(1, 4)]


def plane_send(lows, n_dp):
    return [exchange(low, 2 * y, x, n_dp) for (y, x), low in zip(PLANE[1:], lows)]


def line_send(lows, n_dp):
    return [exchange(low, 4 * k, 0, n_dp) for k, low in zip(range(1, 4), lows)]


def dot(a, b):
    return jnp.dot(a, b, preferred_element_type=f32)


def dot_nt(a, b, precision=None):
    return lax.dot_general(
        a, b, (((1,), (1,)), ((), ())), preferred_element_type=f32, precision=precision
    )


def dot_full(a, b):
    return jnp.dot(a, b, preferred_element_type=f32, precision=highest)


def ln_parts(x):
    centred = x - jnp.mean(x, axis=-1, keepdims=True)
    inv = lax.rsqrt(jnp.mean(centred * centred, axis=-1, keepdims=True) + ln_eps)
    return centred * inv, inv


def ln_back(grad, xhat, inv, gain):
    scaled = grad * gain
    return inv * (
        scaled
        - jnp.mean(scaled, axis=-1, keepdims=True)
        - xhat * jnp.mean(scaled * xhat, axis=-1, keepdims=True)
    )


def split2(x):
    hi = x.astype(bf16)
    return hi, (x - hi.astype(f32)).astype(bf16)


def split3(x):
    hi, _ = split2(x)
    rest = x - hi.astype(f32)
    mid = rest.astype(bf16)
    return hi, mid, (rest - mid.astype(f32)).astype(bf16)


def order_matrix(dp, inverse):
    at = lax.broadcasted_iota(jnp.int32, (512, 512), 0 if inverse else 1)
    other = lax.broadcasted_iota(jnp.int32, (512, 512), 1 if inverse else 0)
    block = at >> 5
    bits = ((block & 3) << 2) | (((block >> 2) & 1) << 1) | (block >> 3)
    return jnp.where(other == (((dp ^ bits) << 5) | (at & 31)), 1.0, 0.0).astype(bf16)


def ordered(x, matrix):
    if x.dtype == bf16:
        return dot(x, matrix)
    hi, mid, lo = split3(x)
    return (dot(hi, matrix) + dot(mid, matrix)) + dot(lo, matrix)


def w_at(a, b, t, first, width):
    parts = []
    for core in range(2):
        for y in range(2):
            if first < 1536:
                part = a[2 * core + y][t, :, :, first : first + width]
            else:
                part = b[2 * core + t][y, :, :, first - 1536 : first - 1536 + width]
            parts.append(part.reshape(128, width))
    return jnp.concatenate(parts, axis=0)


def put_grad(refs, t, cols, value):
    for core, ref in enumerate(refs):
        for y in range(2):
            rows = value[core * 256 + y * 128 : core * 256 + (y + 1) * 128]
            ref[2 * y + t, :, :, cols] = rows.reshape(4, 32, rows.shape[1])


def start_all(copies):
    for copy in copies:
        copy.start()


def wait_all(copies):
    for copy in copies:
        copy.wait()


def head_rows(ref, pair, which):
    own = ref[pl.ds(pair * 128 + which * HEAD_DIM, HEAD_DIM), :]
    zero = jnp.zeros_like(own)
    return jnp.concatenate([own, zero] if which == 0 else [zero, own], axis=0)


def segment_mask(own, other):
    ids = jnp.concatenate([own[:, 512:640], other[:, 512:640]], axis=0).astype(f32)
    return jnp.where(ids[:, 0:1] == ids.T[0:1, :], 0.0, masked_score)


def load_rows(x, own, other):
    if x is None:
        return jnp.concatenate([own[:, :512], other[:, :512]], axis=0).astype(f32)
    return x[...]


def gain_of(norms, at):
    return norms[at : at + 1, :]


def bias_of(norms, at):
    return norms[8 + at : 9 + at, :]


def attn_fwd_kernel(with_x, at, own, other, norms, *refs):
    w, refs = refs[:4], refs[4:]
    x, refs = (refs[0], refs[1:]) if with_x else (None, refs)
    x1, lse, saved, refs = refs[0], refs[1], refs[2:8], refs[8:]
    h, vt, ot, mask, qs, k, v, o, qst, kt, out_sems = refs
    keeps = [
        pltpu.make_async_copy(held, to, out_sems.at[i])
        for i, (held, to) in enumerate(zip((qs, k, v, o, qst, kt), saved))
    ]
    xf = load_rows(x, own, other)
    h[...] = (ln_parts(xf)[0] * gain_of(norms, at) + bias_of(norms, at)).astype(bf16)
    mask[...] = segment_mask(own, other)
    for t in range(2):
        cols = slice(t * 256, (t + 1) * 256)
        q = dot(h[...], w_at(w, None, t, 0, 256)).astype(bf16)
        qs[:, cols] = (q * HEAD_DIM ** (-0.5)).astype(bf16)
        k[:, cols] = dot(h[...], w_at(w, None, t, 256, 256)).astype(bf16)
        v[:, cols] = dot(h[...], w_at(w, None, t, 512, 256)).astype(bf16)
    qst[...] = qs[...].T
    kt[...] = k[...].T
    vt[...] = v[...].T
    for i in (0, 1, 2, 4, 5):
        keeps[i].start()
    for pair in range(4):
        k_pair = k[:, pair * 128 : (pair + 1) * 128]
        for which in range(2):
            scores = dot(k_pair, head_rows(qst, pair, which)) + mask[...]
            top = jnp.max(scores, axis=0, keepdims=True)
            numer = jnp.exp(scores - top).astype(bf16)
            rows = pl.ds(pair * 128 + which * HEAD_DIM, HEAD_DIM)
            left = jnp.concatenate([vt[rows, :], jnp.ones((16, 512), bf16)], axis=0)
            both = dot(left, numer)
            total = both[HEAD_DIM : HEAD_DIM + 1, :]
            ot[rows, :] = (both[:HEAD_DIM, :] / total).astype(bf16)
            lse[pl.ds(pair * 2 + which, 1), :] = top + jnp.log(total)
    o[...] = ot[...].T
    keeps[3].start()
    acc = xf
    for t in range(2):
        acc = acc + dot_nt(o[:, t * 256 : (t + 1) * 256], w_at(w, None, t, 768, 256))
    x1[...] = acc
    wait_all(keeps)


def gelu_parts(u):
    square = u * u
    tanh = jnp.tanh(gelu_coef * u * (1.0 + 0.044715 * square))
    return 0.5 * u * (1.0 + tanh), tanh, square


def mlp_weights(w):
    def up(t, part):
        return w_at(w[:4], w[4:], t, 1024 + part * 512, 512)

    def down(t, part):
        return w_at(w[:4], w[4:], t, 2048 + part * 512, 512)

    return up, down


def mlp_rows(at, x, norms, w, h2):
    up, down = mlp_weights(w)
    h2[...] = (ln_parts(x)[0] * gain_of(norms, at) + bias_of(norms, at)).astype(bf16)
    for t in range(2):
        for part in range(2):
            hidden = gelu_parts(dot(h2[...], up(t, part)))[0].astype(bf16)
            x = x + dot_nt(hidden, down(t, part))
    return x


def mlp_bwd_kernel(split, at, ids, x1, norms, *refs):
    up, down = mlp_weights(refs[:8])
    refs = refs[8:]
    if split:
        own, other, refs = refs[0], refs[1], refs[2:]
    else:
        dy, refs = refs[0], refs[1:]
    dx1, small, grads = refs[0], refs[1], refs[2:4]
    h2, h2t, dyb, dybt, dh2 = refs[4:9]
    if split:
        dy = refs[9]
        dy[0:256, :] = ordered(own[ids[1]], order_matrix(ids[0], False))
        dy[256:, :] = other[:, 640:].astype(f32)
    h2[...] = (ln_parts(x1[...])[0] * gain_of(norms, at) + bias_of(norms, at)).astype(bf16)
    h2t[...] = h2[...].T
    dyb[...] = dy[...].astype(bf16)
    dybt[...] = dyb[...].T
    for t in range(2):
        for part in range(2):
            cols = slice(part * 512, (part + 1) * 512)
            w_up = up(t, part)
            pre = dot(h2[...], w_up)
            hidden, tanh, square = gelu_parts(pre)
            slope = 0.5 * (1.0 + tanh) + (0.5 * gelu_coef) * pre * (1.0 - tanh * tanh) * (
                1.0 + (3 * 0.044715) * square
            )
            dhidden = dot(dyb[...], down(t, part))
            dpre = (dhidden * slope).astype(bf16)
            out_cols = slice(1024 + part * 512, 1024 + (part + 1) * 512)
            put_grad(grads, t, out_cols, dot(dybt[...], hidden.astype(bf16)).astype(bf16))
            put_grad(grads, t, cols, dot(h2t[...], dpre).astype(bf16))
            more = dot_nt(dpre, w_up)
            if t + part == 0:
                dh2[...] = more
            else:
                dh2[...] += more
    xhat, inv = ln_parts(x1[...])
    grad = dh2[...]
    small[0:1, :] = jnp.sum(grad * xhat, axis=0, keepdims=True)
    small[1:2, :] = jnp.sum(grad, axis=0, keepdims=True)
    dx1[...] = dy[...] + ln_back(grad, xhat, inv, gain_of(norms, at))


def heads_back(low, w, saved, lse, mask, put_out, scratch):
    qs, k, v, o, qst, kt = saved
    flip, do, dot_t, dqt, dq, dk, dv = scratch
    flip[...] = low.T
    for t in range(2):
        cols = slice(t * 256, (t + 1) * 256)
        do[:, cols] = dot(low, w_at(w, None, t, 768, 256)).astype(bf16)
        put_out(t, dot(flip[...], o[:, cols]).astype(bf16))
    dot_t[...] = do[...].T
    first = lax.broadcasted_iota(jnp.int32, (512, 128), 1) < HEAD_DIM
    for pair in range(4):
        lanes = slice(pair * 128, (pair + 1) * 128)
        dvs, dks = [], []
        for which in range(2):
            head = pair * 2 + which
            rows = pl.ds(head * HEAD_DIM, HEAD_DIM)
            scores = dot(k[:, lanes], head_rows(qst, pair, which)) + mask[...]
            probs = jnp.exp(scores - lse[head : head + 1, :])
            dprobs = dot(v[:, lanes], head_rows(dot_t, pair, which))
            shift = jnp.sum(probs * dprobs, axis=0, keepdims=True)
            dscore = (probs * (dprobs - shift)).astype(bf16)
            dvs.append(dot(probs.astype(bf16), do[:, lanes]))
            dks.append(dot(dscore, qs[:, lanes]))
            dqt[rows, :] = (dot(kt[rows, :], dscore) * HEAD_DIM ** (-0.5)).astype(bf16)
        dv[:, lanes] = jnp.where(first, dvs[0], dvs[1]).astype(bf16)
        dk[:, lanes] = jnp.where(first, dks[0], dks[1]).astype(bf16)
    dq[...] = dqt[...].T


def rows_back(at, xf, norms, w, parts, small, grads, h, flip):
    h[...] = (ln_parts(xf)[0] * gain_of(norms, at) + bias_of(norms, at)).astype(bf16)
    flip[...] = h[...].T
    grad = jnp.zeros((512, 512), f32)
    for t in range(2):
        cols = slice(t * 256, (t + 1) * 256)
        for index, part in enumerate(parts):
            w_cols = slice(index * 256, (index + 1) * 256)
            put_grad(grads, t, w_cols, dot(flip[...], part[:, cols]).astype(bf16))
            grad = grad + dot_nt(part[:, cols], w_at(w, None, t, index * 256, 256))
    xhat, inv = ln_parts(xf)
    small[0:1, :] = jnp.sum(grad * xhat, axis=0, keepdims=True)
    small[1:2, :] = jnp.sum(grad, axis=0, keepdims=True)
    return ln_back(grad, xhat, inv, gain_of(norms, at))


def take_saved(saved, held, sems):
    copies = [
        pltpu.make_async_copy(a, b, sems.at[i]) for i, (a, b) in enumerate(zip(saved, held))
    ]
    start_all(copies)
    return copies


def attn_bwd_kernel(at, own, other, dx1, norms, lse, *refs):
    w, saved, x, refs = refs[:4], refs[4:10], refs[10], refs[11:]
    dx, small, grads = refs[0], refs[1], refs[2:4]
    mask, h, held, scratch, sems = refs[4], refs[5], refs[6:12], refs[12:19], refs[19]
    copies = take_saved(saved, held, sems)
    mask[...] = segment_mask(own, other)
    low = dx1[...].astype(bf16)
    wait_all(copies)

    def put_out(t, value):
        put_grad(grads, t, slice(768, 1024), value)

    heads_back(low, w, held, lse, mask, put_out, scratch)
    dx[...] = dx1[...] + rows_back(
        at, x[...], norms, w, scratch[4:], small, grads, h, scratch[0]
    )


def heads_bwd_kernel(own, other, dx1, lse, *refs):
    w, saved, refs = refs[:4], refs[4:10], refs[10:]
    parts, grads, mask, held = refs[:3], refs[3:5], refs[5], refs[6:12]
    scratch, sems = (*refs[12:16], *parts), refs[16]
    copies = take_saved(saved, held, sems)
    mask[...] = segment_mask(own, other)
    low = dx1[...].astype(bf16)
    wait_all(copies)

    def put_out(t, value):
        put_grad(grads, t, slice(0, 256), value)

    heads_back(low, w, held, lse, mask, put_out, scratch)


def rows_bwd_kernel(
    ids, own, other, dx1, norms, dq, dk, dv, out_0, out_1, other_small, d_x1, *refs
):
    w, d_w, (dx, dx_low, y, y_low), grads, (small, h, flip) = (
        refs[:4],
        refs[4:12],
        refs[12:16],
        refs[16:18],
        refs[18:],
    )
    total = dx1[...] + rows_back(
        0, load_rows(None, own, other), norms, w, (dq, dk, dv), small, grads, h, flip
    )
    dx[...] = total[:256, :]
    dx_low[...] = total[256:, :].astype(bf16)
    rows = jnp.concatenate([small[0:2, :], other_small[0:2, :], jnp.zeros((4, 512), f32)], axis=0)
    packed = pack_rows(ordered(rows, order_matrix(ids[0], True)))
    for grad, part in zip(grads, (out_0, out_1)):
        for i in range(4):
            for z in range(4):
                grad[i, z, :, 768:1024] = part[i, z]
                grad[i, z, :, 1024:1152] = packed
    rows = mlp_rows(4, d_x1[...], norms, d_w, h)
    y[...] = rows[:256, :]
    y_low[...] = rows[256:, :].astype(bf16)


def pack_rows(rows):
    cut = [rows[i : i + 1, 128 * j : 128 * (j + 1)] for i in range(4) for j in range(4)]
    return jnp.concatenate(split2(jnp.concatenate(cut, axis=0)), axis=0)


def code_prep_kernel(book_t, stack, stack_t):
    def one_chunk(index, _):
        lanes = pl.ds(pl.multiple_of(index * 512, 512), 512)
        rows = book_t[:, lanes]
        unit = rows * lax.rsqrt(jnp.sum(rows * rows, axis=0, keepdims=True) + norm_eps)
        hi, mid, lo = split3(unit)
        stack_t[:, lanes] = jnp.concatenate([hi, mid, lo, jnp.ones((32, 512), bf16)], axis=0)
        tall = jnp.concatenate([hi, mid, lo, hi, mid, hi, jnp.zeros((64, 512), bf16)], axis=0)
        stack[lanes, :] = tall.T
        return 0

    lax.fori_loop(0, book_t.shape[1] // 512, one_chunk, 0)


def factor_stack(x):
    hi, mid, lo = split3(x)
    return jnp.concatenate([hi, hi, hi, mid, mid, lo, jnp.zeros((64, x.shape[1]), bf16)], axis=0)


def code_loads(pairs, sems):
    loads = []
    for piece in range(4):
        group = []
        for at, (held, to, by_row) in enumerate(pairs):
            size = held.shape[0 if by_row else 1] // 4
            part = pl.ds(piece * size, size)
            place = (part, slice(None)) if by_row else (slice(None), part)
            group.append(pltpu.make_async_copy(held.at[place], to.at[place], sems.at[at, piece]))
        start_all(group)
        loads.append(group)
    return loads


def mlp_vq_kernel(x1, norms, vq_w, stack_hbm, stack_t_hbm, *refs):
    w, (e, u, kept, numer_hbm, h2, acc, stack, stack_t, numer, sems, out_sems) = refs[:8], refs[8:]
    loads = code_loads([(stack_hbm, stack, True), (stack_t_hbm, stack_t, False)], sems)
    e[...] = mlp_rows(1, x1[...], norms, w, h2)
    lnv = ln_parts(e[...])[0] * gain_of(norms, 2) + bias_of(norms, 2)
    raw = dot_nt(vq_w[0:32, :], lnv, highest)
    inv = lax.rsqrt(jnp.sum(raw * raw, axis=0, keepdims=True) + norm_eps)
    latent = raw * inv
    right = factor_stack(latent * (temper * log2e))
    chunks, keeps = stack.shape[0] // 2048, []
    for piece, group in enumerate(loads):
        wait_all(group)
        for part in range(piece * chunks // 4, (piece + 1) * chunks // 4):
            numers = []
            for index in range(4 * part, 4 * part + 4):
                codes = slice(index * 512, (index + 1) * 512)
                numers.append(jnp.exp2(dot(stack[codes, :], right)).astype(bf16))
            if part > 1:
                keeps[part - 2].wait()
            keeps.append(
                pltpu.make_async_copy(
                    numer.at[part % 2],
                    numer_hbm.at[pl.ds(part * 2048, 2048), :],
                    out_sems.at[part % 2],
                )
            )
            numer[part % 2] = jnp.concatenate(numers, axis=0)
            keeps[part].start()
            sums = dot(stack_t[:, part * 2048 : (part + 1) * 2048], numer[part % 2])
            if part == 0:
                acc[...] = sums
            else:
                acc[...] += sums
    total = acc[96:97, :]
    soft = (acc[0:32, :] + acc[32:64, :] + acc[64:96, :]) / total
    kept[0:32, :] = latent
    kept[32:64, :] = soft
    kept[64:65, :] = total
    kept[65:66, :] = inv
    u[...] = dot_full(soft.T, vq_w[32:64, :])
    wait_all(keeps[-2:])


def vq_bwd_kernel(
    ids, e, du, norms, vq_w, stack_hbm, stack_t_hbm, book_hbm, numer_hbm, kept, *refs
):
    small0, small1, de, code_keep, code_send = refs[:5]
    acc, grads, small, tail, stack, stack_t, book_t, numer, load_sems, sems = refs[5:]
    loads = code_loads(
        [
            (stack_hbm, stack, True),
            (numer_hbm, numer, True),
            (stack_t_hbm, stack_t, False),
            (book_hbm, book_t, False),
        ],
        load_sems,
    )
    xhat, inv_ln = ln_parts(e[...])
    lnv = xhat * gain_of(norms, 2) + bias_of(norms, 2)
    latent, soft = kept[0:32, :], kept[32:64, :]
    total, inv = kept[64:65, :], kept[65:66, :]
    direct = (2.0 * 1.25 * commit_weight) * (latent - soft)
    dsoft = dot_nt(vq_w[32:64, :], du[...], highest) - direct
    small[32:64, :] = dot_full(soft, du[...])
    shift = jnp.sum(dsoft * soft, axis=0, keepdims=True) / total
    dsoft = dsoft / total
    right = factor_stack(dsoft)
    pads = jnp.zeros((64, 512), f32)

    def tall(x):
        hi, lo = split2(x)
        return jnp.concatenate([hi.astype(f32), lo.astype(f32), pads], axis=0).T.astype(bf16)

    sides = jnp.concatenate([tall(dsoft), tall(latent * temper)], axis=0)
    chunks = stack.shape[0] // 2048
    for piece, group in enumerate(loads):
        wait_all(group)
        for part in range(piece * chunks // 4, (piece + 1) * chunks // 4):
            dlogits = []
            for index in range(4 * part, 4 * part + 4):
                codes = slice(index * 512, (index + 1) * 512)
                held = numer[codes, :]
                dlogit = (held.astype(f32) * (dot(stack[codes, :], right) - shift)).astype(bf16)
                dlogits.append(dlogit)
                sums = jnp.concatenate([held, dlogit], axis=1)
                dcode = dot(sums, sides).T
                dcode = dcode[0:32, :] + dcode[32:64, :]
                rows = book_t[:, codes]
                scale = lax.rsqrt(jnp.sum(rows * rows, axis=0, keepdims=True) + norm_eps)
                unit = rows * scale
                grads[:, codes] = (
                    scale * (dcode - unit * jnp.sum(unit * dcode, axis=0, keepdims=True))
                ).astype(bf16)
            sums = dot(
                stack_t[0:96, part * 2048 : (part + 1) * 2048], jnp.concatenate(dlogits, axis=0)
            )
            if part == 0:
                acc[...] = sums
            else:
                acc[...] += sums
    dlatent = temper * (acc[0:32, :] + acc[32:64, :] + acc[64:96, :]) + direct
    draw = inv * (dlatent - latent * jnp.sum(latent * dlatent, axis=0, keepdims=True))
    small[0:32, :] = dot_full(draw, lnv)
    dln = dot_full(draw.T, vq_w[0:32, :])
    small[64:65, :] = jnp.sum(dln * xhat, axis=0, keepdims=True)
    small[65:66, :] = jnp.sum(dln, axis=0, keepdims=True)
    small[66:68, :] = small0[0:2, :]
    small[68:70, :] = small1[0:2, :]
    small[70:96, :] = jnp.zeros((26, 512), f32)
    small[...] = ordered(small[...], order_matrix(ids[0], True))
    for block in range(3):
        for at, part in enumerate(split2(small[block * 32 : (block + 1) * 32, :])):
            for side in range(2):
                tail[block * 2 + side, :, at * 256 : (at + 1) * 256] = part[
                    :, side * 256 : (side + 1) * 256
                ]
    tail[6:8] = jnp.zeros((2, 32, 512), bf16)
    core, z = ids[0] % 2, ids[0] // 4
    copies = []
    for slot, (at, to) in enumerate(((core, code_keep), (1 - core, code_send))):
        for k in range(4):
            part = at * 4 + (z ^ k)
            lanes = pl.ds(pl.multiple_of(part * 1024, 1024), 1024)
            copies += [
                pltpu.make_async_copy(
                    grads.at[:, lanes], to.at[k, :, pl.ds(0, 1024)], sems.at[0, slot, k]
                ),
                pltpu.make_async_copy(
                    tail.at[part], to.at[k, :, pl.ds(1024, 512)], sems.at[1, slot, k]
                ),
            ]
    for copy in copies:
        copy.start()
    de[...] = ln_back(dln, xhat, inv_ln, gain_of(norms, 2))
    for copy in copies:
        copy.wait()


SMEM = pl.BlockSpec(memory_space=pltpu.SMEM)
VMEM = pl.BlockSpec(memory_space=pltpu.VMEM)
ANY = pl.BlockSpec(memory_space=pl.ANY)


def shaped(*pairs):
    return [jax.ShapeDtypeStruct(shape, dtype) for shape, dtype in pairs]


def pin(array):
    return pltpu.with_memory_space_constraint(array, pltpu.HBM)


def call(kernel, name, in_specs, out_specs, outs, scratch, flops, after=(), carry=()):
    n_in, n_extra, n_out = len(in_specs), len(after) + len(carry), len(outs)

    def body(*refs):
        first = n_in + n_extra
        kernel(*refs[:n_in], *refs[first : first + n_out], *refs[first + n_out + len(carry) :])

    made = pl.pallas_call(
        body,
        name=name,
        in_specs=in_specs + [ANY] * n_extra,
        out_specs=out_specs + [ANY] * len(carry),
        out_shape=outs + [jax.ShapeDtypeStruct(a.shape, a.dtype) for a in carry],
        scratch_shapes=scratch,
        input_output_aliases={n_in + len(after) + i: n_out + i for i in range(len(carry))},
        compiler_params=pltpu.CompilerParams(vmem_limit_bytes=vmem_cap),
        cost_estimate=pl.CostEstimate(flops=flops, bytes_accessed=10**6, transcendentals=0),
    )

    def run(*args):
        res = made(*args, *after, *carry)
        return (*res[:n_out], list(res[n_out:]))

    return run


DMA = pltpu.SemaphoreType.DMA
ROWS2 = (512, 512)


def attn_fwd(at, marked, xs, norms, w, after=(), carry=()):
    outs = shaped((ROWS2, f32), ((8, 512), f32)) + [pltpu.HBM(ROWS2, bf16)] * 6
    scratch = [
        *[pltpu.VMEM(ROWS2, bf16)] * 3,
        pltpu.VMEM(ROWS2, f32),
        *[pltpu.VMEM(ROWS2, bf16)] * 6,
        DMA((6,)),
    ]
    x1, lse, *saved, carried = call(
        functools.partial(attn_fwd_kernel, bool(xs), at),
        "attn_fwd",
        [VMEM] * (7 + len(xs)),
        [VMEM] * 2 + [ANY] * 6,
        outs,
        scratch,
        10**10,
        after,
        carry,
    )(*marked, norms, *w[:4], *xs)
    return x1, (lse, *saved), carried


def mlp_bwd(at, ids, x1, dys, norms, w, after=(), carry=()):
    scratch = [
        *[pltpu.VMEM(ROWS2, bf16)] * 4,
        *[pltpu.VMEM(ROWS2, f32)] * len(dys),
    ]
    return call(
        functools.partial(mlp_bwd_kernel, len(dys) == 2, at),
        "mlp_bwd",
        [SMEM] + [VMEM] * (10 + len(dys)),
        [VMEM] * 4,
        shaped((ROWS2, f32), ((8, 512), f32), *[((4, 4, 32, 2048), bf16)] * 2),
        scratch,
        15 * 10**9,
        after,
        carry,
    )(ids, x1, norms, *w, *dys)


def attn_bwd(at, marked, x, dx1, norms, saved, w, after=(), carry=()):
    scratch = [pltpu.VMEM(ROWS2, f32), *[pltpu.VMEM(ROWS2, bf16)] * 14, DMA((6,))]
    outs = shaped((ROWS2, f32), ((8, 512), f32), *[((4, 4, 32, 1024), bf16)] * 2)
    return call(
        functools.partial(attn_bwd_kernel, at),
        "attn_bwd",
        [VMEM] * 9 + [ANY] * 6 + [VMEM],
        [VMEM] * 4,
        outs,
        scratch,
        15 * 10**9,
        after,
        carry,
    )(*marked, dx1, norms, saved[0], *w[:4], *map(pin, saved[1:]), x)


def heads_bwd(marked, dx1, saved, w, after=(), carry=()):
    scratch = [pltpu.VMEM(ROWS2, f32), *[pltpu.VMEM(ROWS2, bf16)] * 10, DMA((6,))]
    outs = shaped(*[(ROWS2, bf16)] * 3, *[((4, 4, 32, 256), bf16)] * 2)
    return call(
        heads_bwd_kernel,
        "heads_bwd",
        [VMEM] * 8 + [ANY] * 6,
        [VMEM] * 5,
        outs,
        scratch,
        10 * 10**9,
        after,
        carry,
    )(*marked, dx1, saved[0], *w[:4], *map(pin, saved[1:]))


def rows_bwd(ids, marked, dx1, norms, parts, other_small, d_x1, w, d_w, after=(), carry=()):
    scratch = [pltpu.VMEM((8, 512), f32), *[pltpu.VMEM(ROWS2, bf16)] * 2]
    outs = shaped(*[((256, 512), f32), ((256, 512), bf16)] * 2, *[((4, 4, 32, 1152), bf16)] * 2)
    return call(
        rows_bwd_kernel,
        "rows_bwd",
        [SMEM] + [VMEM] * 23,
        [VMEM] * 6,
        outs,
        scratch,
        10 * 10**9,
        after,
        carry,
    )(ids, *marked, dx1, norms, *parts, other_small, d_x1, *w[:4], *d_w)


def code_prep(book_t, after=(), carry=()):
    codes = book_t.shape[1]
    return call(
        code_prep_kernel,
        "code_prep",
        [VMEM],
        [VMEM] * 2,
        shaped(((codes, 256), bf16), ((128, codes), bf16)),
        [],
        6 * 10**9,
        after,
        carry,
    )(book_t)


def mlp_vq(x1, norms, vq_w, stack, stack_t, w, after=(), carry=()):
    return call(
        mlp_vq_kernel,
        "mlp_vq",
        [VMEM] * 3 + [ANY] * 2 + [VMEM] * 8,
        [VMEM] * 3 + [ANY],
        shaped((ROWS2, f32), (ROWS2, f32), ((72, 512), f32))
        + [pltpu.HBM((stack.shape[0], 512), bf16)],
        [
            pltpu.VMEM(ROWS2, bf16),
            pltpu.VMEM((128, 512), f32),
            pltpu.VMEM(stack.shape, bf16),
            pltpu.VMEM(stack_t.shape, bf16),
            pltpu.VMEM((2, 2048, 512), bf16),
            DMA((2, 4)),
            DMA((2,)),
        ],
        25 * 10**9,
        after,
        carry,
    )(x1, norms, vq_w, pin(stack), pin(stack_t), *w)


def vq_bwd(ids, e, du, norms, vq_w, codes, kept, smalls, after=(), carry=()):
    scratch = [
        pltpu.VMEM((96, 512), f32),
        pltpu.VMEM(codes[2].shape, bf16),
        pltpu.VMEM((96, 512), f32),
        pltpu.VMEM((8, 32, 512), bf16),
        *[pltpu.VMEM(a.shape, a.dtype) for a in codes],
        DMA((4, 4)),
        DMA((2, 2, 4)),
    ]
    return call(
        vq_bwd_kernel,
        "vq_bwd",
        [SMEM] + [VMEM] * 4 + [ANY] * 4 + [VMEM] * 3,
        [VMEM] + [ANY] * 2,
        shaped((ROWS2, f32), *[((4, 32, 1536), bf16)] * 2),
        scratch,
        25 * 10**9,
        after,
        carry,
    )(ids, e, du, norms, vq_w, *map(pin, codes), kept, *smalls)


def lines_kernel(cuts, *refs):
    first = 0
    for out, width in zip(refs[4:], cuts):
        for k in range(4):
            out[k] = refs[k][:, first : first + width]
        first += width


def stack_lines(shards, cuts, after=(), carry=()):
    return call(
        functools.partial(lines_kernel, cuts),
        "stack_lines",
        [VMEM] * 4,
        [VMEM] * len(cuts),
        shaped(*[((4, 32, width), bf16) for width in cuts]),
        [],
        1,
        after,
        carry,
    )(*shards)


def pack_kernel(*refs):
    hbm, outs, held, sems = refs[:4], refs[4:6], refs[6:10], refs[10]
    copies = [pltpu.make_async_copy(hbm[at], held[at], sems.at[at]) for at in range(4)]
    start_all(copies)
    wait_all(copies)
    qkv, out_t, up, down_t = held
    for layer, out in enumerate(outs):
        for index in range(3):
            out[:, index * 256 : (index + 1) * 256] = qkv[layer, index]
        out[:, 768:1024] = out_t[layer]
        out[:, 1024:2048] = up[layer]
        out[:, 2048:] = down_t[layer]


def pack_weights(*arrays):
    return call(
        pack_kernel,
        "pack_weights",
        [ANY] * 4,
        [VMEM] * 2,
        shaped(*[((32, 3072), bf16)] * 2),
        [*[pltpu.VMEM(a.shape, a.dtype) for a in arrays], DMA((4,))],
        1,
    )(*map(pin, arrays))[:-1]


def pairs_kernel(*refs):
    count = len(refs) // 3
    for at in range(count):
        refs[2 * count + at][0] = refs[2 * at][...]
        refs[2 * count + at][1] = refs[2 * at + 1][...]


def stack_pairs(pairs, after=(), carry=()):
    return call(
        pairs_kernel,
        "stack_pairs",
        [VMEM] * (2 * len(pairs)),
        [VMEM] * len(pairs),
        shaped(*[((2, *a.shape), bf16) for a, _ in pairs]),
        [],
        1,
        after,
        carry,
    )(*[array for pair in pairs for array in pair])


def gate(after, carry):
    def kernel(out):
        out[...] = jnp.zeros_like(out)

    return call(kernel, "gate", [], [VMEM], shaped(((8, 128), f32)), [], 1, after, carry)()[-1]


def rows_in_kernel(ids, *refs):
    hbm, (own, send, norms, vq_w), held, sems = refs[:7], refs[7:11], refs[11:18], refs[18]
    copies = [pltpu.make_async_copy(hbm[at], held[at], sems.at[at]) for at in range(7)]
    start_all(copies)
    matrix = order_matrix(ids[0], False)
    wait_all(copies)
    tokens, segs, cot, gains, biases, in_t, out_w = held
    for to, micro in ((send, 1 - ids[1]), (own, ids[1])):
        to[:, :512] = ordered(tokens[micro], matrix).astype(bf16)
        ids_row = segs[pl.ds(micro, 1), :].astype(f32)
        to[:, 512:640] = jnp.broadcast_to(ids_row, (128, 256)).T.astype(bf16)
    send[:, 640:] = ordered(cot[1 - ids[1]].astype(bf16), matrix).astype(bf16)
    pad = jnp.zeros((3, 512), f32)
    rows = jnp.concatenate([gains[...], pad, biases[...], pad], axis=0)
    norms[...] = ordered(rows, matrix)
    vq_w[...] = ordered(jnp.concatenate([in_t[...], out_w[...]], axis=0), matrix)


def rows_in(ids, *arrays):
    outs = shaped(
        ((256, 640), bf16), ((256, 1152), bf16), ((16, 512), f32), ((64, 512), f32)
    )
    return call(
        rows_in_kernel,
        "rows_in",
        [SMEM] + [ANY] * 7,
        [VMEM] * 4,
        outs,
        [*[pltpu.VMEM(a.shape, a.dtype) for a in arrays], DMA((7,))],
        1,
    )(ids, *map(pin, arrays))[:-1]


def joined(block):
    return block[0:16, 1024:].astype(f32) + block[16:32, 1024:].astype(f32)


def put_small(value, own, blocks):
    hi, lo = split2(value)
    own[0:16, 1024:] = hi.astype(f32) + lo.astype(f32)
    for block in blocks:
        block[0:16, 1024:] = hi
        block[16:32, 1024:] = lo


def near_kernel(ids, ins, outs):
    keep, other = ins
    for i in range(4):
        outs[i][...] = (keep[i].astype(f32) + other[i].astype(f32)).astype(outs[i].dtype)
    if keep.shape[3] == 1152:
        value = joined(keep.at[0, 0]) + joined(other.at[0, 0])
        put_small(value, outs[0].at[0], [out.at[0] for out in outs[1:]])


def near_task(keep, other):
    shape = keep.shape[1:]
    return near_kernel, [keep, other], shaped((shape, f32), *[(shape, bf16)] * 3)


def put_code(ref, first, code):
    for i in range(3):
        ref[first + i] = code[:, 1024 * i : 1024 * (i + 1)]


def get_code(ref, first):
    return jnp.concatenate([ref[first + i] for i in range(3)], axis=1)


def swapped(code):
    return jnp.concatenate([code[:, 1536:], code[:, :1536]], axis=1)


def code_sum(a, b):
    done = []
    for first in range(0, a.shape[1], 1536):
        total = a[:, first : first + 1024].astype(f32) + b[:, first : first + 1024].astype(f32)
        small = [
            x[:, first + 1024 : first + 1280].astype(f32) + x[:, first + 1280 : first + 1536].astype(f32)
            for x in (a, b)
        ]
        done += [total.astype(bf16), *split2(small[0] + small[1])]
    return jnp.concatenate(done, axis=1)


def fork_kernel(ids, ins, outs):
    keep, other = ins
    own_a, to_x, own_b, to_y = outs
    half = keep.shape[3] // 2
    for at, (own, send, kept, sent) in enumerate(
        ((own_a, to_x, (0, 2), (1, 3)), (own_b, to_y, (0, 1), (2, 3)))
    ):
        cols = slice(half * at, half * (at + 1))
        for j in range(2):
            own[j] = keep[kept[j], :, :, cols].astype(f32) + other[kept[j], :, :, cols].astype(f32)
            total = keep[sent[j], :, :, cols].astype(f32) + other[sent[j], :, :, cols].astype(f32)
            send[4 * j : 4 * (j + 1)] = total.astype(bf16)


def fork_task(keep, other):
    half = keep.shape[3] // 2
    outs = shaped(*[((2, 4, 32, half), f32), ((8, 32, half), bf16)] * 2)
    return fork_kernel, [keep, other], outs


def half_kernel(ids, ins, outs):
    own_a, from_x, own_b, from_y = ins[:4]
    kept_a, to_y, kept_b, to_x = outs[:4]
    for own, other, kept, send in (
        (own_a, from_x, kept_a, to_y),
        (own_b, from_y, kept_b, to_x),
    ):
        kept[...] = own[0] + other[0:4].astype(f32)
        send[0:4] = (own[1] + other[4:8].astype(f32)).astype(bf16)
    if len(ins) == 6:
        code, from_z = ins[4:]
        outs[4][...] = code_sum(code[...], swapped(get_code(from_z, 2)))
        put_code(to_x, 4, outs[4])


def half_task(own_a, from_x, own_b, from_y, *codes):
    width = own_a.shape[3]
    outs = shaped(
        ((4, 32, width), f32),
        ((4, 32, width), bf16),
        ((4, 32, width), f32),
        ((7 if codes else 4, 32, width), bf16),
        *[(code.shape, bf16) for code in codes[:1]],
    )
    return half_kernel, [own_a, from_x, own_b, from_y, *codes], outs


def join_kernel(ids, ins, outs):
    kept, send = outs[:2]
    width = ins[0].shape[2]
    for at, (own, other) in enumerate((ins[0:2], ins[2:4])):
        cols = slice(width * at, width * (at + 1))
        for k in range(2):
            kept[k, :, cols] = own[2 * k] + other[2 * k].astype(f32)
            total = (own[2 * k + 1] + other[2 * k + 1].astype(f32)).astype(bf16)
            send[k, :, cols] = total
    if len(ins) == 5:
        outs[2][...] = code_sum(ins[4][...], get_code(ins[3], 4))


def join_task(own_a, from_y, own_b, from_x, *codes):
    width = 2 * own_a.shape[2]
    outs = shaped(
        ((2, 32, width), f32),
        ((2, 32, width), bf16),
        *[(code.shape, bf16) for code in codes],
    )
    return join_kernel, [own_a, from_y, own_b, from_x, *codes], outs


def line_step_kernel(ids, ins, outs):
    kept, other = ins
    outs[0][...] = kept[0] + other[0].astype(f32)
    outs[1][...] = (kept[1] + other[1].astype(f32)).astype(bf16)


def line_step_task(kept, other):
    shape = kept.shape[1:]
    return line_step_kernel, [kept, other], shaped((shape, f32), (shape, bf16))


def line_code_kernel(ids, ins, outs):
    kept, other, code, code_other = ins
    own, code_out, send = outs
    own[...] = kept[0] + other[0].astype(f32)
    for i in range(2):
        cols = slice(1024 * i, 1024 * (i + 1))
        send[i] = (kept[1, :, cols] + other[1, :, cols].astype(f32)).astype(bf16)
    code_out[...] = code_sum(code[...], code_other[...])
    put_code(send, 2, code_out)


def line_code_task(kept, other, code, code_other):
    outs = shaped((kept.shape[1:], f32), (code.shape, bf16), ((5, 32, 1024), bf16))
    return line_code_kernel, [kept, other, code, code_other], outs


def line_last_kernel(ids, ins, outs):
    kept, other, code, code_other = ins
    line_step_kernel(ids, ins[:2], outs[:2])
    outs[2][:, :3072] = code[...]
    outs[2][:, 3072:] = code_other[...]


def line_last_task(kept, other, code, code_other):
    shape = kept.shape[1:]
    outs = shaped((shape, f32), (shape, bf16), ((32, 6144), bf16))
    return line_last_kernel, [kept, other, code, code_other], outs


def plane_line_kernel(ids, ins, outs):
    kept, send = outs
    for k in range(4):
        total = ins[0][k]
        for other in ins[1:]:
            total = total + other[k].astype(f32)
        to = send if k % 2 else kept
        to[k // 2] = total.astype(to.dtype)
    x, y, xy = [joined(other.at[0]) for other in ins[1:]]
    put_small((ins[0][0, 0:16, 1024:] + x) + (y + xy), kept.at[0], [send.at[0]])


def plane_line_task(own, others):
    outs = shaped(((2, 32, 1152), f32), ((2, 32, 1152), bf16))
    return plane_line_kernel, [own, *others], outs


def small_step_kernel(ids, ins, outs):
    kept, other = ins
    line_step_kernel(ids, ins, outs)
    put_small(kept[0, 0:16, 1024:] + joined(other.at[0]), outs[0], [outs[1]])


def small_step_task(kept, other):
    shape = kept.shape[1:]
    return small_step_kernel, [kept, other], shaped((shape, f32), (shape, bf16))


def line_total(ins, width):
    total = ins[0][:, :width]
    for other in ins[1:]:
        total = total + other[:, :width].astype(f32)
    return total


def rows_out_kernel(ids, ins, outs):
    y, y_low, dx, dx_low = ins
    matrix = order_matrix(ids[0], True)
    outs[0][...] = ordered(y[...], matrix)
    outs[1][...] = ordered(dx[...], matrix)
    outs[2][0:256, :] = ordered(y_low[...], matrix).astype(bf16)
    outs[2][256:, :] = ordered(dx_low[...], matrix).astype(bf16)


def rows_out_task(y, y_low, dx, dx_low):
    outs = shaped((y.shape, f32), (dx.shape, f32), (ROWS2, bf16))
    return rows_out_kernel, [y, y_low, dx, dx_low], outs


def rows_done_kernel(ids, y, dx, others, decoded, grad_tokens, done, held, sems):
    copies = []
    done[...] = jnp.zeros_like(done)
    for at, (out, own) in enumerate(((decoded, y), (grad_tokens, dx))):
        held[at] = others[256 * at : 256 * (at + 1), :].astype(f32)
        copies.append(pltpu.make_async_copy(own, out.at[ids[1]], sems.at[at, 0]))
        copies.append(pltpu.make_async_copy(held.at[at], out.at[1 - ids[1]], sems.at[at, 1]))
    start_all(copies)
    wait_all(copies)


def rows_done(ids, y, dx, others, after):
    return call(
        rows_done_kernel,
        "rows_done",
        [SMEM] + [VMEM] * 3,
        [ANY] * 2 + [VMEM],
        [pltpu.HBM((2, 256, 512), f32)] * 2 + shaped(((8, 128), f32)),
        [pltpu.VMEM((2, 256, 512), f32), DMA((2, 2))],
        10**9,
        after,
    )(ids, y, dx, others)[:-1]


def code_near_kernel(ids, ins, outs):
    keep, other = ins
    for at, out in enumerate(outs):
        for i in range(2):
            out[:, 1536 * i : 1536 * (i + 1)] = code_sum(keep[2 * i + at], other[2 * i + at])


def code_near_task(keep, other):
    return code_near_kernel, [keep, other], shaped(*[((32, 3072), bf16)] * 2)


def code_add_kernel(ids, ins, outs):
    outs[0][...] = code_sum(ins[0][...], ins[1][...])


def code_add_task(a, b):
    return code_add_kernel, [a, b], shaped((a.shape, bf16))


def finish_kernel(ids, ins, outs):
    mlp, attn, d_mlp, d_attn, code, code_other = ins[:2], ins[2:4], ins[4:6], ins[6:8], *ins[8:]
    qkv, out_t, up, down_t, book, vq_in, vq_out, gains, biases, dec_biases, small_ref = outs
    rows = line_total(mlp, 2048)
    up[0] = rows[:, :1024]
    down_t[0] = rows[:, 1024:]
    for i, out in enumerate((up, down_t)):
        out[1] = d_mlp[0][:, 1024 * i : 1024 * (i + 1)] + d_mlp[1][i].astype(f32)
    for layer, rows in enumerate((line_total(attn, 1024), line_total(d_attn, 1024))):
        for index in range(3):
            qkv[layer, index] = rows[:, index * 256 : (index + 1) * 256]
        out_t[layer] = rows[:, 768:]
    core, z = ids[0] % 2, ids[0] // 4
    for at, parts in ((core, code), (1 - core, code_other)):
        for k in range(4):
            part = at * 4 + (z ^ k)
            place = k // 2 + 2 * (k % 2)
            held = parts[:, 1536 * place : 1536 * (place + 1)].astype(f32)
            book[:, pl.ds(pl.multiple_of(part * 1024, 1024), 1024)] = held[:, :1024]
            small_ref[:, pl.ds(pl.multiple_of(part * 256, 256), 256)] = (
                held[:, 1024:1280] + held[:, 1280:1536]
            )
    small = small_ref[...]
    vq_in[...] = small[:, :512]
    vq_out[...] = small[:, 512:1024]
    rest = small[:, 1024:1536]
    packed = attn[0][0:16, 1024:] + joined(attn[1])
    for row, out in enumerate((gains.at[0:1], biases.at[0:1], gains.at[1:2], biases.at[1:2])):
        for j in range(4):
            out[:, 128 * j : 128 * (j + 1)] = packed[row * 4 + j : row * 4 + j + 1, :]
    gains[2:3, :] = rest[0:1, :]
    biases[2:3, :] = rest[1:2, :]
    gains[3:4, :] = rest[2:3, :]
    dec_biases[0:1, :] = rest[3:4, :]
    gains[4:5, :] = rest[4:5, :]
    dec_biases[1:2, :] = rest[5:6, :]


def finish_task(mlp, attn, d_mlp, d_attn, code, code_other):
    outs = shaped(
        ((2, 3, 32, 256), f32),
        ((2, 32, 256), f32),
        ((2, 32, 1024), f32),
        ((2, 32, 1024), f32),
        ((32, 8192), f32),
        ((32, 512), f32),
        ((32, 512), f32),
        ((5, 512), f32),
        ((3, 512), f32),
        ((2, 512), f32),
        ((32, 2048), f32),
    )
    ins = [*mlp, *attn, *d_mlp, *d_attn, code, code_other]
    return finish_kernel, ins, outs


def run_tasks(ids, name, tasks, after=(), carry=()):
    sizes = [(len(ins), len(outs)) for _, ins, outs in tasks]
    n_in = sum(i for i, _ in sizes)

    def kernel(ids_ref, *refs):
        at_in, at_out = 0, n_in
        for (fn, _, _), (i, o) in zip(tasks, sizes):
            fn(ids_ref, refs[at_in : at_in + i], refs[at_out : at_out + o])
            at_in, at_out = at_in + i, at_out + o

    outs = [one for _, _, many in tasks for one in many]
    res = call(
        kernel, name, [SMEM] + [VMEM] * n_in, [VMEM] * len(outs), outs, [], 10**9, after, carry
    )(ids, *[one for _, many, _ in tasks for one in many])
    split, at = [], 0
    for _, o in sizes:
        split.append(res[at : at + o])
        at += o
    return (*split, res[-1])


def whole_groups(
    n_dp,
    tokens,
    segment_ids,
    norm_gains,
    norm_biases,
    w_qkv,
    w_attn_out,
    w_up,
    w_down,
    w_vq_in,
    w_vq_out,
    codebook,
    cotangent,
):
    dp_at, tp_at = lax.axis_index("dp"), lax.axis_index("tp")
    ids = jnp.stack([dp_at, tp_at]).astype(jnp.int32)

    def swap(values):
        return exchange(values, 0, 1, n_dp)

    def core(values):
        return [values, exchange(values, 1, 0, n_dp)]

    book_t = codebook.T
    enc_shard, dec_shard = pack_weights(
        w_qkv, w_attn_out.transpose(0, 2, 1), w_up, w_down.transpose(0, 2, 1)
    )
    enc_shards = spread_line(enc_shard, n_dp)
    own, send, norms, vq_w = rows_in(
        ids,
        tokens,
        segment_ids,
        cotangent,
        norm_gains,
        norm_biases,
        w_vq_in.T,
        w_vq_out,
    )
    marked = [own, swap(send)]

    line_a, line_b, (dec_shard,) = stack_lines(enc_shards, [1536] * 2, carry=[dec_shard])
    along_x, along_y = exchange(line_a, 0, 1, n_dp), exchange(line_b, 2, 0, n_dp)
    dec_shards = spread_line(dec_shard, n_dp)
    stack, stack_t, _ = code_prep(book_t, [line_a])
    codes = (stack, stack_t, book_t)
    a_0, b_0, _ = stack_pairs([(line_a, along_x), (line_b, along_y)], [stack_t, marked[1]])
    a_1, b_1 = exchange(a_0, 2, 0, n_dp), exchange(b_0, 0, 1, n_dp)
    line_a, line_b, (a_0, b_0) = stack_lines(dec_shards, [1536] * 2, [a_1, b_1], [a_0, b_0])
    enc_w = [a_0, a_1, exchange(a_0, 1, 0, n_dp), exchange(a_1, 1, 0, n_dp)]
    enc_w += [b_0, b_1, exchange(b_0, 1, 0, n_dp), exchange(b_1, 1, 0, n_dp)]
    along_x, along_y = exchange(line_a, 0, 1, n_dp), exchange(line_b, 2, 0, n_dp)
    e_x1, e_saved, _ = attn_fwd(0, marked, [], norms, enc_w)
    a_0, b_0, _ = stack_pairs([(line_a, along_x), (line_b, along_y)], [e_x1])
    a_1, b_1 = exchange(a_0, 2, 0, n_dp), exchange(b_0, 0, 1, n_dp)
    dec_w = [a_0, exchange(a_0, 1, 0, n_dp), b_0, exchange(b_0, 1, 0, n_dp)]
    e, u, kept, numer, _ = mlp_vq(e_x1, norms, vq_w, stack, stack_t, enc_w, [a_0, b_0])
    a_1, b_1 = gate([u], [a_1, b_1])
    a_1, b_1 = core(a_1), core(b_1)
    dec_w = [dec_w[0], a_1[0], dec_w[1], a_1[1], dec_w[2], b_1[0], dec_w[3], b_1[1]]
    d_x1, d_saved, _ = attn_fwd(3, marked, [u], norms, dec_w)

    dx1, d_small1, keep_m, send_m, _ = mlp_bwd(
        4, ids, d_x1, [cotangent, marked[1]], norms, dec_w
    )
    near_m = exchange(send_m, 1, 0, n_dp)
    du, d_small0, keep_a, send_a, (keep_m,) = attn_bwd(
        3, marked, u, dx1, norms, d_saved, dec_w, carry=[keep_m]
    )
    (m_a, to_x, m_b, to_y), (send_a,) = run_tasks(
        ids, "sums1", [fork_task(keep_m, near_m)], carry=[send_a]
    )
    from_x, from_y = exchange(to_x, 0, 1, n_dp), exchange(to_y, 2, 0, n_dp)
    near_a = exchange(send_a, 1, 0, n_dp)
    de, code, code_send, (m_a, m_b, keep_a) = vq_bwd(
        ids,
        e,
        du,
        norms,
        vq_w,
        [*codes, numer],
        kept,
        [d_small0, d_small1],
        [to_x, to_y],
        [m_a, m_b, keep_a],
    )
    (m_a, m_y, m_b, m_x), (a_a, to_x, a_b, to_y), (code, code_send) = run_tasks(
        ids,
        "sums2",
        [half_task(m_a, from_x, m_b, from_y), fork_task(keep_a, near_a)],
        carry=[code, code_send],
    )
    code_other = exchange(code_send, 1, 0, n_dp)
    from_m_y, from_m_x = exchange(m_y, 2, 0, n_dp), exchange(m_x, 0, 1, n_dp)
    from_x, from_y = exchange(to_x, 0, 1, n_dp), exchange(to_y, 2, 0, n_dp)
    (code, code_send), _ = run_tasks(ids, "sums2b", [code_near_task(code, code_other)])
    code_other = exchange(code_send, 4, 0, n_dp)
    ex1, e_small1, keep_m, send_m, (m_a, m_b, a_a, a_b, code) = mlp_bwd(
        1,
        ids,
        e_x1,
        [de],
        norms,
        enc_w,
        [m_y, m_x, to_x, to_y, code_send],
        [m_a, m_b, a_a, a_b, code],
    )
    (own_dm, send_dm), (a_a, to_y, a_b, to_x), (code,), (keep_m, send_m) = run_tasks(
        ids,
        "sums3",
        [
            join_task(m_a, from_m_y, m_b, from_m_x),
            half_task(a_a, from_x, a_b, from_y),
            code_add_task(code, code_other),
        ],
        carry=[keep_m, send_m],
    )
    near_m, code_other = exchange(send_m, 1, 0, n_dp), exchange(code, 2, 0, n_dp)
    from_y, from_x = exchange(to_y, 2, 0, n_dp), exchange(to_x, 0, 1, n_dp)
    other_dm = exchange(send_dm, 4, 0, n_dp)
    *parts, (a_a, a_b, own_dm) = heads_bwd(
        marked, ex1, e_saved, enc_w, [to_x, to_y, send_dm, code], [a_a, a_b, own_dm]
    )
    (m_a, to_x, m_b, to_y), (own_da, send_da), (own_dm, code, send_dm), _ = run_tasks(
        ids,
        "sums3b",
        [
            fork_task(keep_m, near_m),
            join_task(a_a, from_y, a_b, from_x),
            line_code_task(own_dm, other_dm, code, code_other),
        ],
        [parts[0]],
    )
    other_da, other_dm = exchange(send_da, 4, 0, n_dp), exchange(send_dm, 8, 0, n_dp)
    from_y, from_x = exchange(to_y, 2, 0, n_dp), exchange(to_x, 0, 1, n_dp)
    dx, dx_low, y, y_low, keep_a, send_a, (m_a, m_b, own_dm, own_da) = rows_bwd(
        ids,
        marked,
        ex1,
        norms,
        parts,
        e_small1,
        d_x1,
        enc_w,
        dec_w,
        [to_x, to_y, send_da, send_dm],
        [m_a, m_b, own_dm, own_da],
    )
    (m_a, to_y, m_b, to_x, code), (own_da, send_da), (keep_a, send_a) = run_tasks(
        ids,
        "sums4",
        [half_task(m_a, from_x, m_b, from_y, code, other_dm), line_step_task(own_da, other_da)],
        carry=[keep_a, send_a],
    )
    near_a = exchange(send_a, 1, 0, n_dp)
    from_y, from_x = exchange(to_y, 2, 0, n_dp), exchange(to_x, 0, 1, n_dp)
    (own_a, *lows_a), (m_a, m_b, code, send_da) = run_tasks(
        ids, "sums4b", [near_task(keep_a, near_a)], carry=[m_a, m_b, code, send_da]
    )
    plane_a = plane_send(lows_a, n_dp)
    (own_m, send_m, code), (own_a, send_da) = run_tasks(
        ids,
        "sums5",
        [join_task(m_a, from_y, m_b, from_x, code)],
        lows_a,
        [own_a, send_da],
    )
    other_m, code_other = exchange(send_m, 4, 0, n_dp), exchange(code, 4, 0, n_dp)
    (y, dx, rows), (own_a,) = run_tasks(
        ids, "rows_out", [rows_out_task(y, y_low, dx, dx_low)], [send_m, code], [own_a]
    )
    (own_a, send_a), (own_m, send_m, code), (rows, send_da) = run_tasks(
        ids,
        "sums6",
        [plane_line_task(own_a, plane_a), line_last_task(own_m, other_m, code, code_other)],
        carry=[rows, send_da],
    )
    other_da = exchange(send_da, 8, 0, n_dp)
    other_a, other_m = exchange(send_a, 4, 0, n_dp), exchange(send_m, 8, 0, n_dp)
    code_other, rows = exchange(code, 1, 0, n_dp), swap(rows)
    (own_a, send_a), _ = run_tasks(ids, "sums7", [small_step_task(own_a, other_a)])
    other_a = exchange(send_a, 8, 0, n_dp)
    decoded, grad_tokens, done = rows_done(ids, y, dx, rows, [send_a])
    (qkv, out_t, up, down_t, book, vq_in, vq_out, *norm_grads, _), _ = run_tasks(
        ids,
        "finish",
        [
            finish_task(
                (own_m, other_m),
                (own_a, other_a),
                (own_dm, other_dm),
                (own_da, other_da),
                code,
                code_other,
            )
        ],
        [done],
    )
    return (
        decoded,
        grad_tokens,
        *norm_grads,
        qkv,
        out_t.transpose(0, 2, 1),
        up,
        down_t.transpose(0, 2, 1),
        vq_in.T,
        vq_out,
        book.T,
    )


def layer_norm(values, norm_gain, norm_bias):
    centred = values - jnp.mean(values, axis=-1, keepdims=True)
    spread = jnp.mean(centred * centred, axis=-1, keepdims=True)
    return centred * lax.rsqrt(spread + ln_eps) * norm_gain + norm_bias


def gelu_tanh(values):
    return (
        0.5 * values * (1.0 + jnp.tanh(gelu_coef * (values + 0.044715 * values * values * values)))
    )


def matmul(former, latter):
    return jnp.dot(former, latter, precision=highest, preferred_element_type=jnp.float32)


def normalize(values):
    return values * lax.rsqrt(jnp.sum(values * values, axis=-1, keepdims=True) + norm_eps)


def quantize(in_rows, norm_gain, norm_bias, in_w, out_w, code_w):
    latent = normalize(matmul(layer_norm(in_rows, norm_gain, norm_bias), in_w))
    code_rows = normalize(code_w)
    logits = matmul(latent, code_rows.T) * temper
    row_max = jnp.max(logits, axis=-1, keepdims=True)
    numerator = jnp.exp(logits - row_max)
    assign = numerator / jnp.sum(numerator, axis=-1, keepdims=True)
    soft_code = matmul(assign, code_rows)
    offset = latent - soft_code
    vq_loss = commit_weight * 1.25 * jnp.sum(offset * offset)
    return (matmul(soft_code, out_w), vq_loss)


def product(former, latter):
    return jnp.dot(former, latter, preferred_element_type=jnp.float32)


def product_tn(former, latter):
    return lax.dot_general(
        former, latter, (((0,), (0,)), ((), ())), preferred_element_type=jnp.float32
    )


def product_nt(former, latter):
    return lax.dot_general(
        former, latter, (((1,), (1,)), ((), ())), preferred_element_type=jnp.float32
    )


def split_heads(values):
    return values.reshape(values.shape[0], values.shape[1] // HEAD_DIM, HEAD_DIM).transpose(1, 0, 2)


def join_heads(values):
    return values.transpose(1, 0, 2).reshape(values.shape[1], values.shape[0] * HEAD_DIM)


def masked_scores(query_blk, key_h, seg_blk, seg_keys):
    scores = jnp.einsum(
        "hqd,hkd->hqk", query_blk, key_h, preferred_element_type=jnp.float32
    ) * HEAD_DIM ** (-0.5)
    return jnp.where((seg_blk[:, None] == seg_keys[None, :])[None], scores, masked_score)


def attend(query_h, key_h, value_h, seg_keys):
    block_rows = min(512, query_h.shape[1])
    block_count = query_h.shape[1] // block_rows

    def one_block(begin_row):
        query_blk = lax.dynamic_slice_in_dim(query_h, begin_row, block_rows, 1)
        seg_blk = lax.dynamic_slice_in_dim(seg_keys, begin_row, block_rows, 0)
        scores = masked_scores(query_blk, key_h, seg_blk, seg_keys)
        row_max = jnp.max(scores, axis=-1, keepdims=True)
        numerator = jnp.exp(scores - row_max)
        row_total = jnp.sum(numerator, axis=-1, keepdims=True)
        prob_low = (numerator / row_total).astype(jnp.bfloat16)
        attended = jnp.einsum("hqk,hkd->hqd", prob_low, value_h, preferred_element_type=jnp.float32)
        return (attended.astype(jnp.bfloat16), (row_max + jnp.log(row_total))[..., 0])

    starts = jnp.arange(block_count, dtype=jnp.int32) * block_rows
    attended, log_sums = lax.map(one_block, starts)
    heads_out = attended.transpose(1, 0, 2, 3).reshape(query_h.shape)
    log_sums = log_sums.transpose(1, 0, 2).reshape(query_h.shape[0], query_h.shape[1])
    return (heads_out, log_sums)


def attend_back(query_h, key_h, value_h, seg_keys, log_sums, grad_out):
    block_rows = min(512, query_h.shape[1])
    block_count = query_h.shape[1] // block_rows

    def one_block(carry, begin_row):
        grad_key, grad_value = carry
        query_blk = lax.dynamic_slice_in_dim(query_h, begin_row, block_rows, 1)
        grad_blk = lax.dynamic_slice_in_dim(grad_out, begin_row, block_rows, 1)
        lse_blk = lax.dynamic_slice_in_dim(log_sums, begin_row, block_rows, 1)
        seg_blk = lax.dynamic_slice_in_dim(seg_keys, begin_row, block_rows, 0)
        scores = masked_scores(query_blk, key_h, seg_blk, seg_keys)
        probs = jnp.exp(scores - lse_blk[..., None])
        prob_low = probs.astype(jnp.bfloat16)
        grad_value = grad_value + jnp.einsum(
            "hqk,hqd->hkd", prob_low, grad_blk, preferred_element_type=jnp.float32
        )
        grad_prob = jnp.einsum(
            "hqd,hkd->hqk", grad_blk, value_h, preferred_element_type=jnp.float32
        )
        row_dot = jnp.sum(probs * grad_prob, axis=-1, keepdims=True)
        grad_score = (probs * (grad_prob - row_dot) * HEAD_DIM ** (-0.5)).astype(jnp.bfloat16)
        grad_query = jnp.einsum(
            "hqk,hkd->hqd", grad_score, key_h, preferred_element_type=jnp.float32
        )
        grad_key = grad_key + jnp.einsum(
            "hqk,hqd->hkd", grad_score, query_blk, preferred_element_type=jnp.float32
        )
        return ((grad_key, grad_value), grad_query)

    starts = jnp.arange(block_count, dtype=jnp.int32) * block_rows
    zeros_kv = jnp.zeros(key_h.shape, jnp.float32)
    (grad_key, grad_value), grad_query = lax.scan(one_block, (zeros_kv, zeros_kv), starts)
    grad_query = grad_query.transpose(1, 0, 2, 3).reshape(query_h.shape)
    return (
        grad_query.astype(jnp.bfloat16),
        grad_key.astype(jnp.bfloat16),
        grad_value.astype(jnp.bfloat16),
    )


def spread_rows(values):
    return lax.all_gather(values, "tp", axis=0, tiled=True)


def combine_rows(partial_value):
    return lax.psum_scatter(partial_value, "tp", scatter_dimension=0, tiled=True)


def spread_grads(values):
    return lax.all_gather(values, "tp", axis=0, tiled=True)


def combine_grads(partial_value):
    return lax.psum_scatter(
        partial_value.astype(jnp.bfloat16), "tp", scatter_dimension=0, tiled=True
    ).astype(jnp.float32)


def fetch_weights(w_qkv, w_attn_out, w_up, w_down, layer):
    return (
        lax.all_gather(w_qkv[layer], "dp", axis=1, tiled=True),
        lax.all_gather(w_attn_out[layer], "dp", axis=1, tiled=True),
        lax.all_gather(w_up[layer], "dp", axis=0, tiled=True),
        lax.all_gather(w_down[layer], "dp", axis=1, tiled=True),
    )


def reduce_weight_grads(grads):
    return (
        lax.psum_scatter(
            grads[0].astype(jnp.bfloat16), "dp", scatter_dimension=1, tiled=True
        ).astype(jnp.float32),
        lax.psum_scatter(
            grads[1].astype(jnp.bfloat16), "dp", scatter_dimension=1, tiled=True
        ).astype(jnp.float32),
        lax.psum_scatter(
            grads[2].astype(jnp.bfloat16), "dp", scatter_dimension=0, tiled=True
        ).astype(jnp.float32),
        lax.psum_scatter(
            grads[3].astype(jnp.bfloat16), "dp", scatter_dimension=1, tiled=True
        ).astype(jnp.float32),
    )


def block_forward(resid_in, seg_local, gains, biases, weights):
    qkv_w, attn_w, up_w, down_w = weights
    normed = layer_norm(resid_in, gains[0], biases[0]).astype(jnp.bfloat16)
    normed_all, seg_all = (
        lax.all_gather(normed, "tp", axis=0, tiled=True),
        lax.all_gather(seg_local, "tp", axis=0, tiled=True),
    )
    query_h = split_heads(product(normed_all, qkv_w[0]).astype(jnp.bfloat16))
    key_h = split_heads(product(normed_all, qkv_w[1]).astype(jnp.bfloat16))
    value_h = split_heads(product(normed_all, qkv_w[2]).astype(jnp.bfloat16))
    heads_out, log_sums = attend(query_h, key_h, value_h, seg_all)
    attn_rows = join_heads(heads_out)
    middle = resid_in + combine_rows(product(attn_rows, attn_w))
    normed_mid = spread_rows(layer_norm(middle, gains[1], biases[1]).astype(jnp.bfloat16))
    hidden_pre = product(normed_mid, up_w)
    hidden = gelu_tanh(hidden_pre).astype(jnp.bfloat16)
    result = middle + combine_rows(product(hidden, down_w))
    kept = (
        resid_in,
        middle,
        normed_all,
        seg_all,
        query_h,
        key_h,
        value_h,
        log_sums,
        attn_rows,
        normed_mid,
        hidden_pre,
        hidden,
    )
    return (result, kept)


def block_backward(kept, gains, biases, weights, grad_result):
    (
        resid_in,
        middle,
        normed_all,
        seg_all,
        query_h,
        key_h,
        value_h,
        log_sums,
        attn_rows,
        normed_mid,
        hidden_pre,
        hidden,
    ) = kept
    qkv_w, attn_w, up_w, down_w = weights
    grad_branch = spread_grads(grad_result.astype(jnp.bfloat16))
    grad_down = product_tn(hidden, grad_branch)
    grad_hidden = product_nt(grad_branch, down_w)
    _, gelu_back = jax.vjp(gelu_tanh, hidden_pre)
    grad_pre = gelu_back(grad_hidden)[0].astype(jnp.bfloat16)
    grad_up = product_tn(normed_mid, grad_pre)
    grad_norm_mid = combine_grads(product_nt(grad_pre, up_w))
    _, norm_back_mid = jax.vjp(layer_norm, middle, gains[1], biases[1])
    grad_mid_ln, grad_gain_mid, grad_bias_mid = norm_back_mid(grad_norm_mid)
    grad_middle = grad_result + grad_mid_ln
    grad_attn_all = spread_grads(grad_middle.astype(jnp.bfloat16))
    grad_attn = product_tn(attn_rows, grad_attn_all)
    grad_heads = split_heads(product_nt(grad_attn_all, attn_w).astype(jnp.bfloat16))
    grad_query, grad_key, grad_value = attend_back(
        query_h, key_h, value_h, seg_all, log_sums, grad_heads
    )
    grad_parts = [join_heads(grad_query), join_heads(grad_key), join_heads(grad_value)]
    grad_qkv = jnp.stack([product_tn(normed_all, grad_part) for grad_part in grad_parts])
    grad_normed_part = (
        product_nt(grad_parts[0], qkv_w[0])
        + product_nt(grad_parts[1], qkv_w[1])
        + product_nt(grad_parts[2], qkv_w[2])
    )
    grad_normed = combine_grads(grad_normed_part)
    _, norm_back_in = jax.vjp(layer_norm, resid_in, gains[0], biases[0])
    grad_in_ln, grad_gain_in, grad_bias_in = norm_back_in(grad_normed)
    gain_grads = jnp.stack([grad_gain_in, grad_gain_mid])
    bias_grads = jnp.stack([grad_bias_in, grad_bias_mid])
    return (
        grad_middle + grad_in_ln,
        gain_grads,
        bias_grads,
        (grad_qkv, grad_attn, grad_up, grad_down),
    )


def local(
    tokens,
    segment_ids,
    norm_gains,
    norm_biases,
    w_qkv,
    w_attn_out,
    w_up,
    w_down,
    w_vq_in,
    w_vq_out,
    codebook,
    cotangent,
):
    gain_sum = jnp.zeros(norm_gains.shape, jnp.float32)
    bias_sum = jnp.zeros(norm_biases.shape, jnp.float32)
    vq_in_sum = jnp.zeros(w_vq_in.shape, jnp.float32)
    vq_out_sum = jnp.zeros(w_vq_out.shape, jnp.float32)
    code_sum = jnp.zeros(codebook.shape, jnp.float32)
    layer_sums = [None, None]
    outputs = []
    input_grads = []
    for micro in range(MICRO):
        resid_in = tokens[micro].astype(jnp.float32)
        seg_local = segment_ids[micro]
        enc_weights = fetch_weights(w_qkv, w_attn_out, w_up, w_down, 0)
        encoded, enc_kept = block_forward(
            resid_in, seg_local, norm_gains[0:2], norm_biases[0:2], enc_weights
        )
        (decoder_in, _), vq_back = jax.vjp(
            quantize, encoded, norm_gains[2], norm_biases[2], w_vq_in, w_vq_out, codebook
        )
        dec_weights = fetch_weights(w_qkv, w_attn_out, w_up, w_down, 1)
        decoded, dec_kept = block_forward(
            decoder_in, seg_local, norm_gains[3:5], norm_biases[3:5], dec_weights
        )
        outputs.append(decoded)
        grad_dec_in, gains_dec, biases_dec, grads_dec = block_backward(
            dec_kept, norm_gains[3:5], norm_biases[3:5], dec_weights, cotangent[micro]
        )
        grad_encoded, grad_gain_vq, grad_bias_vq, grad_in_w, grad_out_w, grad_codes = vq_back(
            (grad_dec_in, jnp.ones((), jnp.float32))
        )
        grad_input, gains_enc, biases_enc, grads_enc = block_backward(
            enc_kept, norm_gains[0:2], norm_biases[0:2], enc_weights, grad_encoded
        )
        input_grads.append(grad_input)
        gain_sum = gain_sum + jnp.concatenate([gains_enc, grad_gain_vq[None], gains_dec], axis=0)
        bias_sum = bias_sum + jnp.concatenate([biases_enc, grad_bias_vq[None], biases_dec], axis=0)
        vq_in_sum = vq_in_sum + grad_in_w
        vq_out_sum = vq_out_sum + grad_out_w
        code_sum = code_sum + grad_codes
        for layer, grads in ((0, grads_enc), (1, grads_dec)):
            reduced = reduce_weight_grads(grads)
            if layer_sums[layer] is None:
                layer_sums[layer] = reduced
            else:
                layer_sums[layer] = jax.tree.map(jnp.add, layer_sums[layer], reduced)
    gain_tot, bias_tot, vq_in_tot, vq_out_tot, code_tot = lax.psum(
        (gain_sum, bias_sum, vq_in_sum, vq_out_sum, code_sum), ("dp", "tp")
    )
    return (
        jnp.stack(outputs),
        jnp.stack(input_grads),
        gain_tot,
        bias_tot[0:3],
        bias_tot[3:5],
        jnp.stack([layer_sums[0][0], layer_sums[1][0]]),
        jnp.stack([layer_sums[0][1], layer_sums[1][1]]),
        jnp.stack([layer_sums[0][2], layer_sums[1][2]]),
        jnp.stack([layer_sums[0][3], layer_sums[1][3]]),
        vq_in_tot,
        vq_out_tot,
        code_tot,
    )


def solution(mesh):
    n_dp, n_tp = mesh.shape["dp"], mesh.shape["tp"]
    fits = n_tp == MICRO and n_dp == 16
    return jax.shard_map(
        functools.partial(whole_groups, n_dp) if fits else local,
        mesh=mesh,
        in_specs=(
            P(None, ("dp", "tp"), None),
            P(None, ("dp", "tp")),
            P(),
            P(),
            P(None, None, "dp", "tp"),
            P(None, "tp", "dp"),
            P(None, "dp", "tp"),
            P(None, "tp", "dp"),
            P(),
            P(),
            P(),
            P(None, ("dp", "tp"), None),
        ),
        out_specs=(
            P(None, ("dp", "tp"), None),
            P(None, ("dp", "tp"), None),
            P(),
            P(),
            P(),
            P(None, None, "dp", "tp"),
            P(None, "tp", "dp"),
            P(None, "dp", "tp"),
            P(None, "tp", "dp"),
            P(),
            P(),
            P(),
        ),
        check_vma=False,
    )
```

```python
import functools

import jax
import jax.numpy as jnp
from jax import lax
from jax.experimental import pallas as pl
from jax.experimental.pallas import tpu as pltpu
from jax.sharding import PartitionSpec as P

HEAD_DIM = 64
MICRO = 2
bf16 = jnp.bfloat16
f32 = jnp.float32
highest = lax.Precision.HIGHEST
ln_eps = 1e-05
norm_eps = 1e-06
temper = 10.0
commit_weight = 64.0
gelu_coef = 0.7978845608028654
masked_score = -1e30
log2e = 1.4426950408889634
vmem_cap = 26 * 1024 * 1024


PLANE = ((0, 0), (0, 1), (1, 0), (1, 1))


def exchange(values, dp_xor, tp_xor, n_dp):
    pairs = [
        (d * 2 + t, (d ^ dp_xor) * 2 + (t ^ tp_xor)) for d in range(n_dp) for t in range(2)
    ]
    return lax.ppermute(values, ("dp", "tp"), pairs)


def spread_line(shard, n_dp):
    return [shard] + [exchange(shard, 4 * k, 0, n_dp) for k in range(1, 4)]


def plane_send(lows, n_dp):
    return [exchange(low, 2 * y, x, n_dp) for (y, x), low in zip(PLANE[1:], lows)]


def line_send(lows, n_dp):
    return [exchange(low, 4 * k, 0, n_dp) for k, low in zip(range(1, 4), lows)]


def dot(a, b):
    return jnp.dot(a, b, preferred_element_type=f32)


def dot_nt(a, b, precision=None):
    return lax.dot_general(
        a, b, (((1,), (1,)), ((), ())), preferred_element_type=f32, precision=precision
    )


def dot_full(a, b):
    return jnp.dot(a, b, preferred_element_type=f32, precision=highest)


def ln_parts(x):
    centred = x - jnp.mean(x, axis=-1, keepdims=True)
    inv = lax.rsqrt(jnp.mean(centred * centred, axis=-1, keepdims=True) + ln_eps)
    return centred * inv, inv


def ln_back(grad, xhat, inv, gain):
    scaled = grad * gain
    return inv * (
        scaled
        - jnp.mean(scaled, axis=-1, keepdims=True)
        - xhat * jnp.mean(scaled * xhat, axis=-1, keepdims=True)
    )


def split2(x):
    hi = x.astype(bf16)
    return hi, (x - hi.astype(f32)).astype(bf16)


def split3(x):
    hi, _ = split2(x)
    rest = x - hi.astype(f32)
    mid = rest.astype(bf16)
    return hi, mid, (rest - mid.astype(f32)).astype(bf16)


def order_matrix(dp, inverse):
    at = lax.broadcasted_iota(jnp.int32, (512, 512), 0 if inverse else 1)
    other = lax.broadcasted_iota(jnp.int32, (512, 512), 1 if inverse else 0)
    block = at >> 5
    bits = ((block & 3) << 2) | (((block >> 2) & 1) << 1) | (block >> 3)
    return jnp.where(other == (((dp ^ bits) << 5) | (at & 31)), 1.0, 0.0).astype(bf16)


def ordered(x, matrix):
    if x.dtype == bf16:
        return dot(x, matrix)
    hi, mid, lo = split3(x)
    return (dot(hi, matrix) + dot(mid, matrix)) + dot(lo, matrix)


def w_at(a, b, t, first, width):
    parts = []
    for core in range(2):
        for y in range(2):
            if first < 1536:
                part = a[2 * core + y][t, :, :, first : first + width]
            else:
                part = b[2 * core + t][y, :, :, first - 1536 : first - 1536 + width]
            parts.append(part.reshape(128, width))
    return jnp.concatenate(parts, axis=0)


def put_grad(refs, t, cols, value):
    for core, ref in enumerate(refs):
        for y in range(2):
            rows = value[core * 256 + y * 128 : core * 256 + (y + 1) * 128]
            ref[2 * y + t, :, :, cols] = rows.reshape(4, 32, rows.shape[1])


def start_all(copies):
    for copy in copies:
        copy.start()


def wait_all(copies):
    for copy in copies:
        copy.wait()


def head_rows(ref, pair, which):
    own = ref[pl.ds(pair * 128 + which * HEAD_DIM, HEAD_DIM), :]
    zero = jnp.zeros_like(own)
    return jnp.concatenate([own, zero] if which == 0 else [zero, own], axis=0)


def segment_mask(own, other):
    ids = jnp.concatenate([own[:, 512:640], other[:, 512:640]], axis=0).astype(f32)
    return jnp.where(ids[:, 0:1] == ids.T[0:1, :], 0.0, masked_score)


def load_rows(x, own, other):
    if x is None:
        return jnp.concatenate([own[:, :512], other[:, :512]], axis=0).astype(f32)
    return x[...]


def gain_of(norms, at):
    return norms[at : at + 1, :]


def bias_of(norms, at):
    return norms[8 + at : 9 + at, :]


def attn_fwd_kernel(with_x, at, own, other, norms, *refs):
    w, refs = refs[:4], refs[4:]
    x, refs = (refs[0], refs[1:]) if with_x else (None, refs)
    x1, lse, saved, refs = refs[0], refs[1], refs[2:8], refs[8:]
    h, vt, ot, mask, qs, k, v, o, qst, kt, out_sems = refs
    keeps = [
        pltpu.make_async_copy(held, to, out_sems.at[i])
        for i, (held, to) in enumerate(zip((qs, k, v, o, qst, kt), saved))
    ]
    xf = load_rows(x, own, other)
    h[...] = (ln_parts(xf)[0] * gain_of(norms, at) + bias_of(norms, at)).astype(bf16)
    mask[...] = segment_mask(own, other)
    for t in range(2):
        cols = slice(t * 256, (t + 1) * 256)
        q = dot(h[...], w_at(w, None, t, 0, 256)).astype(bf16)
        qs[:, cols] = (q * HEAD_DIM ** (-0.5)).astype(bf16)
        k[:, cols] = dot(h[...], w_at(w, None, t, 256, 256)).astype(bf16)
        v[:, cols] = dot(h[...], w_at(w, None, t, 512, 256)).astype(bf16)
    qst[...] = qs[...].T
    kt[...] = k[...].T
    vt[...] = v[...].T
    for i in (0, 1, 2, 4, 5):
        keeps[i].start()
    for pair in range(4):
        k_pair = k[:, pair * 128 : (pair + 1) * 128]
        for which in range(2):
            scores = dot(k_pair, head_rows(qst, pair, which)) + mask[...]
            top = jnp.max(scores, axis=0, keepdims=True)
            numer = jnp.exp(scores - top).astype(bf16)
            rows = pl.ds(pair * 128 + which * HEAD_DIM, HEAD_DIM)
            left = jnp.concatenate([vt[rows, :], jnp.ones((16, 512), bf16)], axis=0)
            both = dot(left, numer)
            total = both[HEAD_DIM : HEAD_DIM + 1, :]
            ot[rows, :] = (both[:HEAD_DIM, :] / total).astype(bf16)
            lse[pl.ds(pair * 2 + which, 1), :] = top + jnp.log(total)
    o[...] = ot[...].T
    keeps[3].start()
    acc = xf
    for t in range(2):
        acc = acc + dot_nt(o[:, t * 256 : (t + 1) * 256], w_at(w, None, t, 768, 256))
    x1[...] = acc
    wait_all(keeps)


def gelu_parts(u):
    square = u * u
    tanh = jnp.tanh(gelu_coef * u * (1.0 + 0.044715 * square))
    return 0.5 * u * (1.0 + tanh), tanh, square


def mlp_weights(w):
    def up(t, part):
        return w_at(w[:4], w[4:], t, 1024 + part * 512, 512)

    def down(t, part):
        return w_at(w[:4], w[4:], t, 2048 + part * 512, 512)

    return up, down


def mlp_rows(at, x, norms, w, h2):
    up, down = mlp_weights(w)
    h2[...] = (ln_parts(x)[0] * gain_of(norms, at) + bias_of(norms, at)).astype(bf16)
    for t in range(2):
        for part in range(2):
            hidden = gelu_parts(dot(h2[...], up(t, part)))[0].astype(bf16)
            x = x + dot_nt(hidden, down(t, part))
    return x


def mlp_bwd_kernel(split, at, ids, x1, norms, *refs):
    up, down = mlp_weights(refs[:8])
    refs = refs[8:]
    if split:
        own, other, refs = refs[0], refs[1], refs[2:]
    else:
        dy, refs = refs[0], refs[1:]
    dx1, small, grads = refs[0], refs[1], refs[2:4]
    h2, h2t, dyb, dybt, dh2 = refs[4:9]
    if split:
        dy = refs[9]
        dy[0:256, :] = ordered(own[ids[1]], order_matrix(ids[0], False))
        dy[256:, :] = other[:, 640:].astype(f32)
    h2[...] = (ln_parts(x1[...])[0] * gain_of(norms, at) + bias_of(norms, at)).astype(bf16)
    h2t[...] = h2[...].T
    dyb[...] = dy[...].astype(bf16)
    dybt[...] = dyb[...].T
    for t in range(2):
        for part in range(2):
            cols = slice(part * 512, (part + 1) * 512)
            w_up = up(t, part)
            pre = dot(h2[...], w_up)
            hidden, tanh, square = gelu_parts(pre)
            slope = 0.5 * (1.0 + tanh) + (0.5 * gelu_coef) * pre * (1.0 - tanh * tanh) * (
                1.0 + (3 * 0.044715) * square
            )
            dhidden = dot(dyb[...], down(t, part))
            dpre = (dhidden * slope).astype(bf16)
            out_cols = slice(1024 + part * 512, 1024 + (part + 1) * 512)
            put_grad(grads, t, out_cols, dot(dybt[...], hidden.astype(bf16)).astype(bf16))
            put_grad(grads, t, cols, dot(h2t[...], dpre).astype(bf16))
            more = dot_nt(dpre, w_up)
            if t + part == 0:
                dh2[...] = more
            else:
                dh2[...] += more
    xhat, inv = ln_parts(x1[...])
    grad = dh2[...]
    small[0:1, :] = jnp.sum(grad * xhat, axis=0, keepdims=True)
    small[1:2, :] = jnp.sum(grad, axis=0, keepdims=True)
    dx1[...] = dy[...] + ln_back(grad, xhat, inv, gain_of(norms, at))


def heads_back(low, w, saved, lse, mask, put_out, scratch):
    qs, k, v, o, qst, kt = saved
    flip, do, dot_t, dqt, dq, dk, dv = scratch
    flip[...] = low.T
    for t in range(2):
        cols = slice(t * 256, (t + 1) * 256)
        do[:, cols] = dot(low, w_at(w, None, t, 768, 256)).astype(bf16)
        put_out(t, dot(flip[...], o[:, cols]).astype(bf16))
    dot_t[...] = do[...].T
    first = lax.broadcasted_iota(jnp.int32, (512, 128), 1) < HEAD_DIM
    for pair in range(4):
        lanes = slice(pair * 128, (pair + 1) * 128)
        dvs, dks = [], []
        for which in range(2):
            head = pair * 2 + which
            rows = pl.ds(head * HEAD_DIM, HEAD_DIM)
            scores = dot(k[:, lanes], head_rows(qst, pair, which)) + mask[...]
            probs = jnp.exp(scores - lse[head : head + 1, :])
            dprobs = dot(v[:, lanes], head_rows(dot_t, pair, which))
            shift = jnp.sum(probs * dprobs, axis=0, keepdims=True)
            dscore = (probs * (dprobs - shift)).astype(bf16)
            dvs.append(dot(probs.astype(bf16), do[:, lanes]))
            dks.append(dot(dscore, qs[:, lanes]))
            dqt[rows, :] = (dot(kt[rows, :], dscore) * HEAD_DIM ** (-0.5)).astype(bf16)
        dv[:, lanes] = jnp.where(first, dvs[0], dvs[1]).astype(bf16)
        dk[:, lanes] = jnp.where(first, dks[0], dks[1]).astype(bf16)
    dq[...] = dqt[...].T


def rows_back(at, xf, norms, w, parts, small, grads, h, flip):
    h[...] = (ln_parts(xf)[0] * gain_of(norms, at) + bias_of(norms, at)).astype(bf16)
    flip[...] = h[...].T
    grad = jnp.zeros((512, 512), f32)
    for t in range(2):
        cols = slice(t * 256, (t + 1) * 256)
        for index, part in enumerate(parts):
            w_cols = slice(index * 256, (index + 1) * 256)
            put_grad(grads, t, w_cols, dot(flip[...], part[:, cols]).astype(bf16))
            grad = grad + dot_nt(part[:, cols], w_at(w, None, t, index * 256, 256))
    xhat, inv = ln_parts(xf)
    small[0:1, :] = jnp.sum(grad * xhat, axis=0, keepdims=True)
    small[1:2, :] = jnp.sum(grad, axis=0, keepdims=True)
    return ln_back(grad, xhat, inv, gain_of(norms, at))


def take_saved(saved, held, sems):
    copies = [
        pltpu.make_async_copy(a, b, sems.at[i]) for i, (a, b) in enumerate(zip(saved, held))
    ]
    start_all(copies)
    return copies


def attn_bwd_kernel(at, own, other, dx1, norms, lse, *refs):
    w, saved, x, refs = refs[:4], refs[4:10], refs[10], refs[11:]
    dx, small, grads = refs[0], refs[1], refs[2:4]
    mask, h, held, scratch, sems = refs[4], refs[5], refs[6:12], refs[12:19], refs[19]
    copies = take_saved(saved, held, sems)
    mask[...] = segment_mask(own, other)
    low = dx1[...].astype(bf16)
    wait_all(copies)

    def put_out(t, value):
        put_grad(grads, t, slice(768, 1024), value)

    heads_back(low, w, held, lse, mask, put_out, scratch)
    dx[...] = dx1[...] + rows_back(
        at, x[...], norms, w, scratch[4:], small, grads, h, scratch[0]
    )


def heads_bwd_kernel(own, other, dx1, lse, *refs):
    w, saved, refs = refs[:4], refs[4:10], refs[10:]
    parts, grads, mask, held = refs[:3], refs[3:5], refs[5], refs[6:12]
    scratch, sems = (*refs[12:16], *parts), refs[16]
    copies = take_saved(saved, held, sems)
    mask[...] = segment_mask(own, other)
    low = dx1[...].astype(bf16)
    wait_all(copies)

    def put_out(t, value):
        put_grad(grads, t, slice(0, 256), value)

    heads_back(low, w, held, lse, mask, put_out, scratch)


def rows_bwd_kernel(
    ids, own, other, dx1, norms, dq, dk, dv, out_0, out_1, other_small, d_x1, *refs
):
    w, d_w, (dx, dx_low, y, y_low), grads, (small, h, flip) = (
        refs[:4],
        refs[4:12],
        refs[12:16],
        refs[16:18],
        refs[18:],
    )
    total = dx1[...] + rows_back(
        0, load_rows(None, own, other), norms, w, (dq, dk, dv), small, grads, h, flip
    )
    dx[...] = total[:256, :]
    dx_low[...] = total[256:, :].astype(bf16)
    rows = jnp.concatenate([small[0:2, :], other_small[0:2, :], jnp.zeros((4, 512), f32)], axis=0)
    packed = pack_rows(ordered(rows, order_matrix(ids[0], True)))
    for grad, part in zip(grads, (out_0, out_1)):
        for i in range(4):
            for z in range(4):
                grad[i, z, :, 768:1024] = part[i, z]
                grad[i, z, :, 1024:1152] = packed
    rows = mlp_rows(4, d_x1[...], norms, d_w, h)
    y[...] = rows[:256, :]
    y_low[...] = rows[256:, :].astype(bf16)


def pack_rows(rows):
    cut = [rows[i : i + 1, 128 * j : 128 * (j + 1)] for i in range(4) for j in range(4)]
    return jnp.concatenate(split2(jnp.concatenate(cut, axis=0)), axis=0)


def code_prep_kernel(book_t, stack, stack_t):
    def one_chunk(index, _):
        lanes = pl.ds(pl.multiple_of(index * 512, 512), 512)
        rows = book_t[:, lanes]
        unit = rows * lax.rsqrt(jnp.sum(rows * rows, axis=0, keepdims=True) + norm_eps)
        hi, mid, lo = split3(unit)
        stack_t[:, lanes] = jnp.concatenate([hi, mid, lo, jnp.ones((32, 512), bf16)], axis=0)
        tall = jnp.concatenate([hi, mid, lo, hi, mid, hi, jnp.zeros((64, 512), bf16)], axis=0)
        stack[lanes, :] = tall.T
        return 0

    lax.fori_loop(0, book_t.shape[1] // 512, one_chunk, 0)


def factor_stack(x):
    hi, mid, lo = split3(x)
    return jnp.concatenate([hi, hi, hi, mid, mid, lo, jnp.zeros((64, x.shape[1]), bf16)], axis=0)


def code_loads(pairs, sems):
    loads = []
    for piece in range(4):
        group = []
        for at, (held, to, by_row) in enumerate(pairs):
            size = held.shape[0 if by_row else 1] // 4
            part = pl.ds(piece * size, size)
            place = (part, slice(None)) if by_row else (slice(None), part)
            group.append(pltpu.make_async_copy(held.at[place], to.at[place], sems.at[at, piece]))
        start_all(group)
        loads.append(group)
    return loads


def mlp_vq_kernel(x1, norms, vq_w, stack_hbm, stack_t_hbm, *refs):
    w, (e, u, kept, numer_hbm, h2, acc, stack, stack_t, numer, sems, out_sems) = refs[:8], refs[8:]
    loads = code_loads([(stack_hbm, stack, True), (stack_t_hbm, stack_t, False)], sems)
    e[...] = mlp_rows(1, x1[...], norms, w, h2)
    lnv = ln_parts(e[...])[0] * gain_of(norms, 2) + bias_of(norms, 2)
    raw = dot_nt(vq_w[0:32, :], lnv, highest)
    inv = lax.rsqrt(jnp.sum(raw * raw, axis=0, keepdims=True) + norm_eps)
    latent = raw * inv
    right = factor_stack(latent * (temper * log2e))
    chunks, keeps = stack.shape[0] // 2048, []
    for piece, group in enumerate(loads):
        wait_all(group)
        for part in range(piece * chunks // 4, (piece + 1) * chunks // 4):
            numers = []
            for index in range(4 * part, 4 * part + 4):
                codes = slice(index * 512, (index + 1) * 512)
                numers.append(jnp.exp2(dot(stack[codes, :], right)).astype(bf16))
            if part > 1:
                keeps[part - 2].wait()
            keeps.append(
                pltpu.make_async_copy(
                    numer.at[part % 2],
                    numer_hbm.at[pl.ds(part * 2048, 2048), :],
                    out_sems.at[part % 2],
                )
            )
            numer[part % 2] = jnp.concatenate(numers, axis=0)
            keeps[part].start()
            sums = dot(stack_t[:, part * 2048 : (part + 1) * 2048], numer[part % 2])
            if part == 0:
                acc[...] = sums
            else:
                acc[...] += sums
    total = acc[96:97, :]
    soft = (acc[0:32, :] + acc[32:64, :] + acc[64:96, :]) / total
    kept[0:32, :] = latent
    kept[32:64, :] = soft
    kept[64:65, :] = total
    kept[65:66, :] = inv
    u[...] = dot_full(soft.T, vq_w[32:64, :])
    wait_all(keeps[-2:])


def vq_bwd_kernel(
    ids, e, du, norms, vq_w, stack_hbm, stack_t_hbm, book_hbm, numer_hbm, kept, *refs
):
    small0, small1, de, code_keep, code_send = refs[:5]
    acc, grads, small, tail, stack, stack_t, book_t, numer, load_sems, sems = refs[5:]
    loads = code_loads(
        [
            (stack_hbm, stack, True),
            (numer_hbm, numer, True),
            (stack_t_hbm, stack_t, False),
            (book_hbm, book_t, False),
        ],
        load_sems,
    )
    xhat, inv_ln = ln_parts(e[...])
    lnv = xhat * gain_of(norms, 2) + bias_of(norms, 2)
    latent, soft = kept[0:32, :], kept[32:64, :]
    total, inv = kept[64:65, :], kept[65:66, :]
    direct = (2.0 * 1.25 * commit_weight) * (latent - soft)
    dsoft = dot_nt(vq_w[32:64, :], du[...], highest) - direct
    small[32:64, :] = dot_full(soft, du[...])
    shift = jnp.sum(dsoft * soft, axis=0, keepdims=True) / total
    dsoft = dsoft / total
    right = factor_stack(dsoft)
    pads = jnp.zeros((64, 512), f32)

    def tall(x):
        hi, lo = split2(x)
        return jnp.concatenate([hi.astype(f32), lo.astype(f32), pads], axis=0).T.astype(bf16)

    sides = jnp.concatenate([tall(dsoft), tall(latent * temper)], axis=0)
    chunks = stack.shape[0] // 2048
    for piece, group in enumerate(loads):
        wait_all(group)
        for part in range(piece * chunks // 4, (piece + 1) * chunks // 4):
            dlogits = []
            for index in range(4 * part, 4 * part + 4):
                codes = slice(index * 512, (index + 1) * 512)
                held = numer[codes, :]
                dlogit = (held.astype(f32) * (dot(stack[codes, :], right) - shift)).astype(bf16)
                dlogits.append(dlogit)
                sums = jnp.concatenate([held, dlogit], axis=1)
                dcode = dot(sums, sides).T
                dcode = dcode[0:32, :] + dcode[32:64, :]
                rows = book_t[:, codes]
                scale = lax.rsqrt(jnp.sum(rows * rows, axis=0, keepdims=True) + norm_eps)
                unit = rows * scale
                grads[:, codes] = (
                    scale * (dcode - unit * jnp.sum(unit * dcode, axis=0, keepdims=True))
                ).astype(bf16)
            sums = dot(
                stack_t[0:96, part * 2048 : (part + 1) * 2048], jnp.concatenate(dlogits, axis=0)
            )
            if part == 0:
                acc[...] = sums
            else:
                acc[...] += sums
    dlatent = temper * (acc[0:32, :] + acc[32:64, :] + acc[64:96, :]) + direct
    draw = inv * (dlatent - latent * jnp.sum(latent * dlatent, axis=0, keepdims=True))
    small[0:32, :] = dot_full(draw, lnv)
    dln = dot_full(draw.T, vq_w[0:32, :])
    small[64:65, :] = jnp.sum(dln * xhat, axis=0, keepdims=True)
    small[65:66, :] = jnp.sum(dln, axis=0, keepdims=True)
    small[66:68, :] = small0[0:2, :]
    small[68:70, :] = small1[0:2, :]
    small[70:96, :] = jnp.zeros((26, 512), f32)
    small[...] = ordered(small[...], order_matrix(ids[0], True))
    for block in range(3):
        for at, part in enumerate(split2(small[block * 32 : (block + 1) * 32, :])):
            for side in range(2):
                tail[block * 2 + side, :, at * 256 : (at + 1) * 256] = part[
                    :, side * 256 : (side + 1) * 256
                ]
    tail[6:8] = jnp.zeros((2, 32, 512), bf16)
    core, z = ids[0] % 2, ids[0] // 4
    copies = []
    for slot, (at, to) in enumerate(((core, code_keep), (1 - core, code_send))):
        for k in range(4):
            part = at * 4 + (z ^ k)
            lanes = pl.ds(pl.multiple_of(part * 1024, 1024), 1024)
            copies += [
                pltpu.make_async_copy(
                    grads.at[:, lanes], to.at[k, :, pl.ds(0, 1024)], sems.at[0, slot, k]
                ),
                pltpu.make_async_copy(
                    tail.at[part], to.at[k, :, pl.ds(1024, 512)], sems.at[1, slot, k]
                ),
            ]
    for copy in copies:
        copy.start()
    de[...] = ln_back(dln, xhat, inv_ln, gain_of(norms, 2))
    for copy in copies:
        copy.wait()


SMEM = pl.BlockSpec(memory_space=pltpu.SMEM)
VMEM = pl.BlockSpec(memory_space=pltpu.VMEM)
ANY = pl.BlockSpec(memory_space=pl.ANY)


def shaped(*pairs):
    return [jax.ShapeDtypeStruct(shape, dtype) for shape, dtype in pairs]


def pin(array):
    return pltpu.with_memory_space_constraint(array, pltpu.HBM)


def call(kernel, name, in_specs, out_specs, outs, scratch, flops, after=(), carry=()):
    n_in, n_extra, n_out = len(in_specs), len(after) + len(carry), len(outs)

    def body(*refs):
        first = n_in + n_extra
        kernel(*refs[:n_in], *refs[first : first + n_out], *refs[first + n_out + len(carry) :])

    made = pl.pallas_call(
        body,
        name=name,
        in_specs=in_specs + [ANY] * n_extra,
        out_specs=out_specs + [ANY] * len(carry),
        out_shape=outs + [jax.ShapeDtypeStruct(a.shape, a.dtype) for a in carry],
        scratch_shapes=scratch,
        input_output_aliases={n_in + len(after) + i: n_out + i for i in range(len(carry))},
        compiler_params=pltpu.CompilerParams(vmem_limit_bytes=vmem_cap),
        cost_estimate=pl.CostEstimate(flops=flops, bytes_accessed=10**6, transcendentals=0),
    )

    def run(*args):
        res = made(*args, *after, *carry)
        return (*res[:n_out], list(res[n_out:]))

    return run


DMA = pltpu.SemaphoreType.DMA
ROWS2 = (512, 512)


def attn_fwd(at, marked, xs, norms, w, after=(), carry=()):
    outs = shaped((ROWS2, f32), ((8, 512), f32)) + [pltpu.HBM(ROWS2, bf16)] * 6
    scratch = [
        *[pltpu.VMEM(ROWS2, bf16)] * 3,
        pltpu.VMEM(ROWS2, f32),
        *[pltpu.VMEM(ROWS2, bf16)] * 6,
        DMA((6,)),
    ]
    x1, lse, *saved, carried = call(
        functools.partial(attn_fwd_kernel, bool(xs), at),
        "attn_fwd",
        [VMEM] * (7 + len(xs)),
        [VMEM] * 2 + [ANY] * 6,
        outs,
        scratch,
        10**10,
        after,
        carry,
    )(*marked, norms, *w[:4], *xs)
    return x1, (lse, *saved), carried


def mlp_bwd(at, ids, x1, dys, norms, w, after=(), carry=()):
    scratch = [
        *[pltpu.VMEM(ROWS2, bf16)] * 4,
        *[pltpu.VMEM(ROWS2, f32)] * len(dys),
    ]
    return call(
        functools.partial(mlp_bwd_kernel, len(dys) == 2, at),
        "mlp_bwd",
        [SMEM] + [VMEM] * (10 + len(dys)),
        [VMEM] * 4,
        shaped((ROWS2, f32), ((8, 512), f32), *[((4, 4, 32, 2048), bf16)] * 2),
        scratch,
        15 * 10**9,
        after,
        carry,
    )(ids, x1, norms, *w, *dys)


def attn_bwd(at, marked, x, dx1, norms, saved, w, after=(), carry=()):
    scratch = [pltpu.VMEM(ROWS2, f32), *[pltpu.VMEM(ROWS2, bf16)] * 14, DMA((6,))]
    outs = shaped((ROWS2, f32), ((8, 512), f32), *[((4, 4, 32, 1024), bf16)] * 2)
    return call(
        functools.partial(attn_bwd_kernel, at),
        "attn_bwd",
        [VMEM] * 9 + [ANY] * 6 + [VMEM],
        [VMEM] * 4,
        outs,
        scratch,
        15 * 10**9,
        after,
        carry,
    )(*marked, dx1, norms, saved[0], *w[:4], *map(pin, saved[1:]), x)


def heads_bwd(marked, dx1, saved, w, after=(), carry=()):
    scratch = [pltpu.VMEM(ROWS2, f32), *[pltpu.VMEM(ROWS2, bf16)] * 10, DMA((6,))]
    outs = shaped(*[(ROWS2, bf16)] * 3, *[((4, 4, 32, 256), bf16)] * 2)
    return call(
        heads_bwd_kernel,
        "heads_bwd",
        [VMEM] * 8 + [ANY] * 6,
        [VMEM] * 5,
        outs,
        scratch,
        10 * 10**9,
        after,
        carry,
    )(*marked, dx1, saved[0], *w[:4], *map(pin, saved[1:]))


def rows_bwd(ids, marked, dx1, norms, parts, other_small, d_x1, w, d_w, after=(), carry=()):
    scratch = [pltpu.VMEM((8, 512), f32), *[pltpu.VMEM(ROWS2, bf16)] * 2]
    outs = shaped(*[((256, 512), f32), ((256, 512), bf16)] * 2, *[((4, 4, 32, 1152), bf16)] * 2)
    return call(
        rows_bwd_kernel,
        "rows_bwd",
        [SMEM] + [VMEM] * 23,
        [VMEM] * 6,
        outs,
        scratch,
        10 * 10**9,
        after,
        carry,
    )(ids, *marked, dx1, norms, *parts, other_small, d_x1, *w[:4], *d_w)


def code_prep(book_t, after=(), carry=()):
    codes = book_t.shape[1]
    return call(
        code_prep_kernel,
        "code_prep",
        [VMEM],
        [VMEM] * 2,
        shaped(((codes, 256), bf16), ((128, codes), bf16)),
        [],
        6 * 10**9,
        after,
        carry,
    )(book_t)


def mlp_vq(x1, norms, vq_w, stack, stack_t, w, after=(), carry=()):
    return call(
        mlp_vq_kernel,
        "mlp_vq",
        [VMEM] * 3 + [ANY] * 2 + [VMEM] * 8,
        [VMEM] * 3 + [ANY],
        shaped((ROWS2, f32), (ROWS2, f32), ((72, 512), f32))
        + [pltpu.HBM((stack.shape[0], 512), bf16)],
        [
            pltpu.VMEM(ROWS2, bf16),
            pltpu.VMEM((128, 512), f32),
            pltpu.VMEM(stack.shape, bf16),
            pltpu.VMEM(stack_t.shape, bf16),
            pltpu.VMEM((2, 2048, 512), bf16),
            DMA((2, 4)),
            DMA((2,)),
        ],
        25 * 10**9,
        after,
        carry,
    )(x1, norms, vq_w, pin(stack), pin(stack_t), *w)


def vq_bwd(ids, e, du, norms, vq_w, codes, kept, smalls, after=(), carry=()):
    scratch = [
        pltpu.VMEM((96, 512), f32),
        pltpu.VMEM(codes[2].shape, bf16),
        pltpu.VMEM((96, 512), f32),
        pltpu.VMEM((8, 32, 512), bf16),
        *[pltpu.VMEM(a.shape, a.dtype) for a in codes],
        DMA((4, 4)),
        DMA((2, 2, 4)),
    ]
    return call(
        vq_bwd_kernel,
        "vq_bwd",
        [SMEM] + [VMEM] * 4 + [ANY] * 4 + [VMEM] * 3,
        [VMEM] + [ANY] * 2,
        shaped((ROWS2, f32), *[((4, 32, 1536), bf16)] * 2),
        scratch,
        25 * 10**9,
        after,
        carry,
    )(ids, e, du, norms, vq_w, *map(pin, codes), kept, *smalls)


def lines_kernel(cuts, *refs):
    first = 0
    for out, width in zip(refs[4:], cuts):
        for k in range(4):
            out[k] = refs[k][:, first : first + width]
        first += width


def stack_lines(shards, cuts, after=(), carry=()):
    return call(
        functools.partial(lines_kernel, cuts),
        "stack_lines",
        [VMEM] * 4,
        [VMEM] * len(cuts),
        shaped(*[((4, 32, width), bf16) for width in cuts]),
        [],
        1,
        after,
        carry,
    )(*shards)


def pack_kernel(*refs):
    hbm, outs, held, sems = refs[:4], refs[4:6], refs[6:10], refs[10]
    copies = [pltpu.make_async_copy(hbm[at], held[at], sems.at[at]) for at in range(4)]
    start_all(copies)
    wait_all(copies)
    qkv, out_t, up, down_t = held
    for layer, out in enumerate(outs):
        for index in range(3):
            out[:, index * 256 : (index + 1) * 256] = qkv[layer, index]
        out[:, 768:1024] = out_t[layer]
        out[:, 1024:2048] = up[layer]
        out[:, 2048:] = down_t[layer]


def pack_weights(*arrays):
    return call(
        pack_kernel,
        "pack_weights",
        [ANY] * 4,
        [VMEM] * 2,
        shaped(*[((32, 3072), bf16)] * 2),
        [*[pltpu.VMEM(a.shape, a.dtype) for a in arrays], DMA((4,))],
        1,
    )(*map(pin, arrays))[:-1]


def pairs_kernel(*refs):
    count = len(refs) // 3
    for at in range(count):
        refs[2 * count + at][0] = refs[2 * at][...]
        refs[2 * count + at][1] = refs[2 * at + 1][...]


def stack_pairs(pairs, after=(), carry=()):
    return call(
        pairs_kernel,
        "stack_pairs",
        [VMEM] * (2 * len(pairs)),
        [VMEM] * len(pairs),
        shaped(*[((2, *a.shape), bf16) for a, _ in pairs]),
        [],
        1,
        after,
        carry,
    )(*[array for pair in pairs for array in pair])


def gate(after, carry):
    def kernel(out):
        out[...] = jnp.zeros_like(out)

    return call(kernel, "gate", [], [VMEM], shaped(((8, 128), f32)), [], 1, after, carry)()[-1]


def rows_in_kernel(ids, *refs):
    hbm, (own, send, norms, vq_w), held, sems = refs[:7], refs[7:11], refs[11:18], refs[18]
    copies = [pltpu.make_async_copy(hbm[at], held[at], sems.at[at]) for at in range(7)]
    start_all(copies)
    matrix = order_matrix(ids[0], False)
    wait_all(copies)
    tokens, segs, cot, gains, biases, in_t, out_w = held
    for to, micro in ((send, 1 - ids[1]), (own, ids[1])):
        to[:, :512] = ordered(tokens[micro], matrix).astype(bf16)
        ids_row = segs[pl.ds(micro, 1), :].astype(f32)
        to[:, 512:640] = jnp.broadcast_to(ids_row, (128, 256)).T.astype(bf16)
    send[:, 640:] = ordered(cot[1 - ids[1]].astype(bf16), matrix).astype(bf16)
    pad = jnp.zeros((3, 512), f32)
    rows = jnp.concatenate([gains[...], pad, biases[...], pad], axis=0)
    norms[...] = ordered(rows, matrix)
    vq_w[...] = ordered(jnp.concatenate([in_t[...], out_w[...]], axis=0), matrix)


def rows_in(ids, *arrays):
    outs = shaped(
        ((256, 640), bf16), ((256, 1152), bf16), ((16, 512), f32), ((64, 512), f32)
    )
    return call(
        rows_in_kernel,
        "rows_in",
        [SMEM] + [ANY] * 7,
        [VMEM] * 4,
        outs,
        [*[pltpu.VMEM(a.shape, a.dtype) for a in arrays], DMA((7,))],
        1,
    )(ids, *map(pin, arrays))[:-1]


def joined(block):
    return block[0:16, 1024:].astype(f32) + block[16:32, 1024:].astype(f32)


def put_small(value, own, blocks):
    hi, lo = split2(value)
    own[0:16, 1024:] = hi.astype(f32) + lo.astype(f32)
    for block in blocks:
        block[0:16, 1024:] = hi
        block[16:32, 1024:] = lo


def near_kernel(ids, ins, outs):
    keep, other = ins
    for i in range(4):
        outs[i][...] = (keep[i].astype(f32) + other[i].astype(f32)).astype(outs[i].dtype)
    if keep.shape[3] == 1152:
        value = joined(keep.at[0, 0]) + joined(other.at[0, 0])
        put_small(value, outs[0].at[0], [out.at[0] for out in outs[1:]])


def near_task(keep, other):
    shape = keep.shape[1:]
    return near_kernel, [keep, other], shaped((shape, f32), *[(shape, bf16)] * 3)


def put_code(ref, first, code):
    for i in range(3):
        ref[first + i] = code[:, 1024 * i : 1024 * (i + 1)]


def get_code(ref, first):
    return jnp.concatenate([ref[first + i] for i in range(3)], axis=1)


def swapped(code):
    return jnp.concatenate([code[:, 1536:], code[:, :1536]], axis=1)


def code_sum(a, b):
    done = []
    for first in range(0, a.shape[1], 1536):
        total = a[:, first : first + 1024].astype(f32) + b[:, first : first + 1024].astype(f32)
        small = [
            x[:, first + 1024 : first + 1280].astype(f32) + x[:, first + 1280 : first + 1536].astype(f32)
            for x in (a, b)
        ]
        done += [total.astype(bf16), *split2(small[0] + small[1])]
    return jnp.concatenate(done, axis=1)


def fork_kernel(ids, ins, outs):
    keep, other = ins
    own_a, to_x, own_b, to_y = outs
    half = keep.shape[3] // 2
    for at, (own, send, kept, sent) in enumerate(
        ((own_a, to_x, (0, 2), (1, 3)), (own_b, to_y, (0, 1), (2, 3)))
    ):
        cols = slice(half * at, half * (at + 1))
        for j in range(2):
            own[j] = keep[kept[j], :, :, cols].astype(f32) + other[kept[j], :, :, cols].astype(f32)
            total = keep[sent[j], :, :, cols].astype(f32) + other[sent[j], :, :, cols].astype(f32)
            send[4 * j : 4 * (j + 1)] = total.astype(bf16)


def fork_task(keep, other):
    half = keep.shape[3] // 2
    outs = shaped(*[((2, 4, 32, half), f32), ((8, 32, half), bf16)] * 2)
    return fork_kernel, [keep, other], outs


def half_kernel(ids, ins, outs):
    own_a, from_x, own_b, from_y = ins[:4]
    kept_a, to_y, kept_b, to_x = outs[:4]
    for own, other, kept, send in (
        (own_a, from_x, kept_a, to_y),
        (own_b, from_y, kept_b, to_x),
    ):
        kept[...] = own[0] + other[0:4].astype(f32)
        send[0:4] = (own[1] + other[4:8].astype(f32)).astype(bf16)
    if len(ins) == 6:
        code, code_other = ins[4:]
        outs[4][...] = code_sum(code[...], swapped(code_other[...]))
        put_code(to_x, 4, outs[4])


def half_task(own_a, from_x, own_b, from_y, *codes):
    width = own_a.shape[3]
    outs = shaped(
        ((4, 32, width), f32),
        ((4, 32, width), bf16),
        ((4, 32, width), f32),
        ((7 if codes else 4, 32, width), bf16),
        *[(code.shape, bf16) for code in codes[:1]],
    )
    return half_kernel, [own_a, from_x, own_b, from_y, *codes], outs


def join_kernel(ids, ins, outs):
    kept, send = outs[:2]
    width = ins[0].shape[2]
    for at, (own, other) in enumerate((ins[0:2], ins[2:4])):
        cols = slice(width * at, width * (at + 1))
        for k in range(2):
            kept[k, :, cols] = own[2 * k] + other[2 * k].astype(f32)
            send[k, :, cols] = (own[2 * k + 1] + other[2 * k + 1].astype(f32)).astype(bf16)
    if len(ins) == 5:
        outs[2][...] = code_sum(ins[4][...], get_code(ins[3], 4))


def join_task(own_a, from_y, own_b, from_x, *codes):
    width = 2 * own_a.shape[2]
    outs = shaped(
        ((2, 32, width), f32),
        ((2, 32, width), bf16),
        *[(code.shape, bf16) for code in codes],
    )
    return join_kernel, [own_a, from_y, own_b, from_x, *codes], outs


def far_kernel(ids, ins, outs):
    own_a, from_y, own_b, from_x, kept_dm, other_dm = ins
    kept, own_dm, send = outs
    for at, (own, other) in enumerate(((own_a, from_y), (own_b, from_x))):
        cols = slice(512 * at, 512 * (at + 1))
        for k in range(2):
            kept[k, :, cols] = own[k] + other[k].astype(f32)
            send[2 + k, :, cols] = (own[2 + k] + other[2 + k].astype(f32)).astype(bf16)
    own_dm[...] = kept_dm[0] + other_dm[0].astype(f32)
    for i in range(2):
        cols = slice(1024 * i, 1024 * (i + 1))
        send[i] = (kept_dm[1, :, cols] + other_dm[1, :, cols].astype(f32)).astype(bf16)


def far_task(own_a, from_y, own_b, from_x, kept_dm, other_dm):
    outs = shaped(((2, 32, 1024), f32), (kept_dm.shape[1:], f32), ((4, 32, 1024), bf16))
    return far_kernel, [own_a, from_y, own_b, from_x, kept_dm, other_dm], outs


def near_step_kernel(ids, ins, outs):
    kept, other = ins
    outs[0][...] = kept[0] + other[2].astype(f32)
    outs[1][...] = (kept[1] + other[3].astype(f32)).astype(bf16)


def near_step_task(kept, other):
    shape = kept.shape[1:]
    return near_step_kernel, [kept, other], shaped((shape, f32), (shape, bf16))


def line_step_kernel(ids, ins, outs):
    kept, other = ins
    outs[0][...] = kept[0] + other[0].astype(f32)
    outs[1][...] = (kept[1] + other[1].astype(f32)).astype(bf16)


def line_step_task(kept, other):
    shape = kept.shape[1:]
    return line_step_kernel, [kept, other], shaped((shape, f32), (shape, bf16))


def plane_line_kernel(ids, ins, outs):
    kept, send = outs
    for k in range(4):
        total = ins[0][k]
        for other in ins[1:]:
            total = total + other[k].astype(f32)
        to = send if k % 2 else kept
        to[k // 2] = total.astype(to.dtype)
    x, y, xy = [joined(other.at[0]) for other in ins[1:]]
    put_small((ins[0][0, 0:16, 1024:] + x) + (y + xy), kept.at[0], [send.at[0]])


def plane_line_task(own, others):
    outs = shaped(((2, 32, 1152), f32), ((2, 32, 1152), bf16))
    return plane_line_kernel, [own, *others], outs


def small_step_kernel(ids, ins, outs):
    kept, other = ins
    line_step_kernel(ids, ins, outs)
    put_small(kept[0, 0:16, 1024:] + joined(other.at[0]), outs[0], [outs[1]])


def small_step_task(kept, other):
    shape = kept.shape[1:]
    return small_step_kernel, [kept, other], shaped((shape, f32), (shape, bf16))


def line_total(ins, width):
    total = ins[0][:, :width]
    for other in ins[1:]:
        total = total + other[:, :width].astype(f32)
    return total


def rows_out_kernel(ids, ins, outs):
    y, y_low, dx, dx_low = ins
    matrix = order_matrix(ids[0], True)
    outs[0][...] = ordered(y[...], matrix)
    outs[1][...] = ordered(dx[...], matrix)
    outs[2][0:256, :] = ordered(y_low[...], matrix).astype(bf16)
    outs[2][256:, :] = ordered(dx_low[...], matrix).astype(bf16)


def rows_out_task(y, y_low, dx, dx_low):
    outs = shaped((y.shape, f32), (dx.shape, f32), (ROWS2, bf16))
    return rows_out_kernel, [y, y_low, dx, dx_low], outs


def rows_done_kernel(ids, y, dx, others, decoded, grad_tokens, done, held, sems):
    copies = []
    done[...] = jnp.zeros_like(done)
    for at, (out, own) in enumerate(((decoded, y), (grad_tokens, dx))):
        held[at] = others[256 * at : 256 * (at + 1), :].astype(f32)
        copies.append(pltpu.make_async_copy(own, out.at[ids[1]], sems.at[at, 0]))
        copies.append(pltpu.make_async_copy(held.at[at], out.at[1 - ids[1]], sems.at[at, 1]))
    start_all(copies)
    wait_all(copies)


def rows_done(ids, y, dx, others, after):
    return call(
        rows_done_kernel,
        "rows_done",
        [SMEM] + [VMEM] * 3,
        [ANY] * 2 + [VMEM],
        [pltpu.HBM((2, 256, 512), f32)] * 2 + shaped(((8, 128), f32)),
        [pltpu.VMEM((2, 256, 512), f32), DMA((2, 2))],
        10**9,
        after,
    )(ids, y, dx, others)[:-1]


def code_near_kernel(ids, ins, outs):
    keep, other = ins
    for at, out in enumerate(outs):
        for i in range(2):
            out[:, 1536 * i : 1536 * (i + 1)] = code_sum(keep[2 * at + i], other[2 * at + i])


def code_near_task(keep, other):
    return code_near_kernel, [keep, other], shaped(*[((32, 3072), bf16)] * 2)


def code_add_kernel(ids, ins, outs):
    outs[0][...] = code_sum(ins[0][...], ins[1][...])


def code_add_task(a, b):
    return code_add_kernel, [a, b], shaped((a.shape, bf16))


def code_pair_kernel(ids, ins, outs):
    for at, part in enumerate(ins):
        outs[0][:, 3072 * at : 3072 * (at + 1)] = part[...]


def code_pair_task(a, b):
    return code_pair_kernel, [a, b], shaped(((32, 6144), bf16))


def finish_kernel(ids, ins, outs):
    mlp, attn, d_mlp, d_attn, code, code_other = ins[:2], ins[2:4], ins[4:6], ins[6:8], *ins[8:]
    qkv, out_t, up, down_t, book, vq_in, vq_out, gains, biases, dec_biases, small_ref = outs
    rows = line_total(mlp, 2048)
    up[0] = rows[:, :1024]
    down_t[0] = rows[:, 1024:]
    for i, out in enumerate((up, down_t)):
        out[1] = d_mlp[0][:, 1024 * i : 1024 * (i + 1)] + d_mlp[1][i].astype(f32)
    d_rows = line_total(d_attn, 1024)
    for layer, rows in enumerate((line_total(attn, 1024), d_rows)):
        for index in range(3):
            qkv[layer, index] = rows[:, index * 256 : (index + 1) * 256]
        out_t[layer] = rows[:, 768:]
    core, z = ids[0] % 2, ids[0] // 4
    for at, parts in ((core, code), (1 - core, code_other)):
        for k in range(4):
            part = at * 4 + (z ^ k)
            held = parts[:, 1536 * k : 1536 * (k + 1)].astype(f32)
            book[:, pl.ds(pl.multiple_of(part * 1024, 1024), 1024)] = held[:, :1024]
            small_ref[:, pl.ds(pl.multiple_of(part * 256, 256), 256)] = (
                held[:, 1024:1280] + held[:, 1280:1536]
            )
    small = small_ref[...]
    vq_in[...] = small[:, :512]
    vq_out[...] = small[:, 512:1024]
    rest = small[:, 1024:1536]
    packed = attn[0][0:16, 1024:] + joined(attn[1])
    for row, out in enumerate((gains.at[0:1], biases.at[0:1], gains.at[1:2], biases.at[1:2])):
        for j in range(4):
            out[:, 128 * j : 128 * (j + 1)] = packed[row * 4 + j : row * 4 + j + 1, :]
    gains[2:3, :] = rest[0:1, :]
    biases[2:3, :] = rest[1:2, :]
    gains[3:4, :] = rest[2:3, :]
    dec_biases[0:1, :] = rest[3:4, :]
    gains[4:5, :] = rest[4:5, :]
    dec_biases[1:2, :] = rest[5:6, :]


def finish_task(mlp, attn, d_mlp, d_attn, code, code_other):
    outs = shaped(
        ((2, 3, 32, 256), f32),
        ((2, 32, 256), f32),
        ((2, 32, 1024), f32),
        ((2, 32, 1024), f32),
        ((32, 8192), f32),
        ((32, 512), f32),
        ((32, 512), f32),
        ((5, 512), f32),
        ((3, 512), f32),
        ((2, 512), f32),
        ((32, 2048), f32),
    )
    ins = [*mlp, *attn, *d_mlp, *d_attn, code, code_other]
    return finish_kernel, ins, outs


def run_tasks(ids, name, tasks, after=(), carry=()):
    sizes = [(len(ins), len(outs)) for _, ins, outs in tasks]
    n_in = sum(i for i, _ in sizes)

    def kernel(ids_ref, *refs):
        at_in, at_out = 0, n_in
        for (fn, _, _), (i, o) in zip(tasks, sizes):
            fn(ids_ref, refs[at_in : at_in + i], refs[at_out : at_out + o])
            at_in, at_out = at_in + i, at_out + o

    outs = [one for _, _, many in tasks for one in many]
    res = call(
        kernel, name, [SMEM] + [VMEM] * n_in, [VMEM] * len(outs), outs, [], 10**9, after, carry
    )(ids, *[one for _, many, _ in tasks for one in many])
    split, at = [], 0
    for _, o in sizes:
        split.append(res[at : at + o])
        at += o
    return (*split, res[-1])


def whole_groups(
    n_dp,
    tokens,
    segment_ids,
    norm_gains,
    norm_biases,
    w_qkv,
    w_attn_out,
    w_up,
    w_down,
    w_vq_in,
    w_vq_out,
    codebook,
    cotangent,
):
    dp_at, tp_at = lax.axis_index("dp"), lax.axis_index("tp")
    ids = jnp.stack([dp_at, tp_at]).astype(jnp.int32)

    def swap(values):
        return exchange(values, 0, 1, n_dp)

    def core(values):
        return [values, exchange(values, 1, 0, n_dp)]

    book_t = codebook.T
    enc_shard, dec_shard = pack_weights(
        w_qkv, w_attn_out.transpose(0, 2, 1), w_up, w_down.transpose(0, 2, 1)
    )
    enc_shards = spread_line(enc_shard, n_dp)
    own, send, norms, vq_w = rows_in(
        ids,
        tokens,
        segment_ids,
        cotangent,
        norm_gains,
        norm_biases,
        w_vq_in.T,
        w_vq_out,
    )
    marked = [own, swap(send)]

    line_a, line_b, (dec_shard,) = stack_lines(enc_shards, [1536] * 2, carry=[dec_shard])
    along_x, along_y = exchange(line_a, 0, 1, n_dp), exchange(line_b, 2, 0, n_dp)
    dec_shards = spread_line(dec_shard, n_dp)
    stack, stack_t, _ = code_prep(book_t, [line_a])
    codes = (stack, stack_t, book_t)
    a_0, b_0, _ = stack_pairs([(line_a, along_x), (line_b, along_y)], [stack_t, marked[1]])
    a_1, b_1 = exchange(a_0, 2, 0, n_dp), exchange(b_0, 0, 1, n_dp)
    line_a, line_b, (a_0, b_0) = stack_lines(dec_shards, [1536] * 2, [a_1, b_1], [a_0, b_0])
    enc_w = [a_0, a_1, exchange(a_0, 1, 0, n_dp), exchange(a_1, 1, 0, n_dp)]
    enc_w += [b_0, b_1, exchange(b_0, 1, 0, n_dp), exchange(b_1, 1, 0, n_dp)]
    along_x, along_y = exchange(line_a, 0, 1, n_dp), exchange(line_b, 2, 0, n_dp)
    e_x1, e_saved, _ = attn_fwd(0, marked, [], norms, enc_w)
    a_0, b_0, _ = stack_pairs([(line_a, along_x), (line_b, along_y)], [e_x1])
    a_1, b_1 = exchange(a_0, 2, 0, n_dp), exchange(b_0, 0, 1, n_dp)
    dec_w = [a_0, exchange(a_0, 1, 0, n_dp), b_0, exchange(b_0, 1, 0, n_dp)]
    e, u, kept, numer, _ = mlp_vq(e_x1, norms, vq_w, stack, stack_t, enc_w, [a_0, b_0])
    a_1, b_1 = gate([u], [a_1, b_1])
    a_1, b_1 = core(a_1), core(b_1)
    dec_w = [dec_w[0], a_1[0], dec_w[1], a_1[1], dec_w[2], b_1[0], dec_w[3], b_1[1]]
    d_x1, d_saved, _ = attn_fwd(3, marked, [u], norms, dec_w)

    dx1, d_small1, keep_m, send_m, _ = mlp_bwd(
        4, ids, d_x1, [cotangent, marked[1]], norms, dec_w
    )
    near_m = exchange(send_m, 1, 0, n_dp)
    du, d_small0, keep_a, send_a, (keep_m,) = attn_bwd(
        3, marked, u, dx1, norms, d_saved, dec_w, carry=[keep_m]
    )
    (m_a, to_x, m_b, to_y), (send_a,) = run_tasks(
        ids, "sums1", [fork_task(keep_m, near_m)], carry=[send_a]
    )
    from_x, from_y = exchange(to_x, 0, 1, n_dp), exchange(to_y, 2, 0, n_dp)
    near_a = exchange(send_a, 1, 0, n_dp)
    de, code, code_send, (m_a, m_b, keep_a) = vq_bwd(
        ids,
        e,
        du,
        norms,
        vq_w,
        [*codes, numer],
        kept,
        [d_small0, d_small1],
        [to_x, to_y],
        [m_a, m_b, keep_a],
    )
    (m_a, m_y, m_b, m_x), (a_a, to_x, a_b, to_y), (code, code_send) = run_tasks(
        ids,
        "sums2",
        [half_task(m_a, from_x, m_b, from_y), fork_task(keep_a, near_a)],
        carry=[code, code_send],
    )
    code_other = exchange(code_send, 1, 0, n_dp)
    from_m_y, from_m_x = exchange(m_y, 2, 0, n_dp), exchange(m_x, 0, 1, n_dp)
    from_x, from_y = exchange(to_x, 0, 1, n_dp), exchange(to_y, 2, 0, n_dp)
    (code, code_send), _ = run_tasks(ids, "sums2b", [code_near_task(code, code_other)])
    code_other = exchange(code_send, 8, 0, n_dp)
    ex1, e_small1, keep_m, send_m, (m_a, m_b, a_a, a_b, code) = mlp_bwd(
        1,
        ids,
        e_x1,
        [de],
        norms,
        enc_w,
        [m_y, m_x, to_x, to_y, code_send],
        [m_a, m_b, a_a, a_b, code],
    )
    (own_dm, send_dm), (a_a, to_y, a_b, to_x), (code,), (keep_m, send_m) = run_tasks(
        ids,
        "sums3",
        [
            join_task(m_a, from_m_y, m_b, from_m_x),
            half_task(a_a, from_x, a_b, from_y),
            code_add_task(code, code_other),
        ],
        carry=[keep_m, send_m],
    )
    near_m, code_other = exchange(send_m, 1, 0, n_dp), exchange(code, 2, 0, n_dp)
    from_y, from_x = exchange(to_y, 2, 0, n_dp), exchange(to_x, 0, 1, n_dp)
    other_dm = exchange(send_dm, 4, 0, n_dp)
    *parts, (a_a, a_b, own_dm) = heads_bwd(
        marked, ex1, e_saved, enc_w, [to_x, to_y, send_dm, code], [a_a, a_b, own_dm]
    )
    (m_a, to_x, m_b, to_y), (code,), (own_da, own_dm, send_d), _ = run_tasks(
        ids,
        "sums3b",
        [
            fork_task(keep_m, near_m),
            code_add_task(code, code_other),
            far_task(a_a, from_y, a_b, from_x, own_dm, other_dm),
        ],
        [parts[0]],
    )
    other_d, code_other = exchange(send_d, 8, 0, n_dp), exchange(code, 4, 0, n_dp)
    from_y, from_x = exchange(to_y, 2, 0, n_dp), exchange(to_x, 0, 1, n_dp)
    dx, dx_low, y, y_low, keep_a, send_a, (m_a, m_b, own_dm, own_da) = rows_bwd(
        ids,
        marked,
        ex1,
        norms,
        parts,
        e_small1,
        d_x1,
        enc_w,
        dec_w,
        [to_x, to_y, send_d, code],
        [m_a, m_b, own_dm, own_da],
    )
    (m_a, to_y, m_b, to_x, code), (own_da, send_da), (keep_a, send_a) = run_tasks(
        ids,
        "sums4",
        [
            half_task(m_a, from_x, m_b, from_y, code, code_other),
            near_step_task(own_da, other_d),
        ],
        carry=[keep_a, send_a],
    )
    near_a = exchange(send_a, 1, 0, n_dp)
    from_y, from_x = exchange(to_y, 2, 0, n_dp), exchange(to_x, 0, 1, n_dp)
    other_da = exchange(send_da, 4, 0, n_dp)
    (own_a, *lows_a), (m_a, m_b, code) = run_tasks(
        ids, "sums4b", [near_task(keep_a, near_a)], carry=[m_a, m_b, code]
    )
    plane_a = plane_send(lows_a, n_dp)
    (own_m, send_m, code), (own_a,) = run_tasks(
        ids,
        "sums5",
        [join_task(m_a, from_y, m_b, from_x, code)],
        lows_a,
        [own_a],
    )
    other_m, code_other = exchange(send_m, 4, 0, n_dp), exchange(code, 8, 0, n_dp)
    (y, dx, rows), (own_a,) = run_tasks(
        ids, "rows_out", [rows_out_task(y, y_low, dx, dx_low)], [send_m, code], [own_a]
    )
    (own_a, send_a), (own_m, send_m), (code,), (rows,) = run_tasks(
        ids,
        "sums6",
        [
            plane_line_task(own_a, plane_a),
            line_step_task(own_m, other_m),
            code_pair_task(code, code_other),
        ],
        carry=[rows],
    )
    other_a, other_m = exchange(send_a, 4, 0, n_dp), exchange(send_m, 8, 0, n_dp)
    code_other, rows = exchange(code, 1, 0, n_dp), swap(rows)
    (own_a, send_a), _ = run_tasks(ids, "sums7", [small_step_task(own_a, other_a)])
    other_a = exchange(send_a, 8, 0, n_dp)
    decoded, grad_tokens, done = rows_done(ids, y, dx, rows, [send_a])
    (qkv, out_t, up, down_t, book, vq_in, vq_out, *norm_grads, _), _ = run_tasks(
        ids,
        "finish",
        [
            finish_task(
                (own_m, other_m),
                (own_a, other_a),
                (own_dm, other_d),
                (own_da, other_da),
                code,
                code_other,
            )
        ],
        [done],
    )
    return (
        decoded,
        grad_tokens,
        *norm_grads,
        qkv,
        out_t.transpose(0, 2, 1),
        up,
        down_t.transpose(0, 2, 1),
        vq_in.T,
        vq_out,
        book.T,
    )


def layer_norm(values, norm_gain, norm_bias):
    centred = values - jnp.mean(values, axis=-1, keepdims=True)
    spread = jnp.mean(centred * centred, axis=-1, keepdims=True)
    return centred * lax.rsqrt(spread + ln_eps) * norm_gain + norm_bias


def gelu_tanh(values):
    return (
        0.5 * values * (1.0 + jnp.tanh(gelu_coef * (values + 0.044715 * values * values * values)))
    )


def matmul(former, latter):
    return jnp.dot(former, latter, precision=highest, preferred_element_type=jnp.float32)


def normalize(values):
    return values * lax.rsqrt(jnp.sum(values * values, axis=-1, keepdims=True) + norm_eps)


def quantize(in_rows, norm_gain, norm_bias, in_w, out_w, code_w):
    latent = normalize(matmul(layer_norm(in_rows, norm_gain, norm_bias), in_w))
    code_rows = normalize(code_w)
    logits = matmul(latent, code_rows.T) * temper
    row_max = jnp.max(logits, axis=-1, keepdims=True)
    numerator = jnp.exp(logits - row_max)
    assign = numerator / jnp.sum(numerator, axis=-1, keepdims=True)
    soft_code = matmul(assign, code_rows)
    offset = latent - soft_code
    vq_loss = commit_weight * 1.25 * jnp.sum(offset * offset)
    return (matmul(soft_code, out_w), vq_loss)


def product(former, latter):
    return jnp.dot(former, latter, preferred_element_type=jnp.float32)


def product_tn(former, latter):
    return lax.dot_general(
        former, latter, (((0,), (0,)), ((), ())), preferred_element_type=jnp.float32
    )


def product_nt(former, latter):
    return lax.dot_general(
        former, latter, (((1,), (1,)), ((), ())), preferred_element_type=jnp.float32
    )


def split_heads(values):
    return values.reshape(values.shape[0], values.shape[1] // HEAD_DIM, HEAD_DIM).transpose(1, 0, 2)


def join_heads(values):
    return values.transpose(1, 0, 2).reshape(values.shape[1], values.shape[0] * HEAD_DIM)


def masked_scores(query_blk, key_h, seg_blk, seg_keys):
    scores = jnp.einsum(
        "hqd,hkd->hqk", query_blk, key_h, preferred_element_type=jnp.float32
    ) * HEAD_DIM ** (-0.5)
    return jnp.where((seg_blk[:, None] == seg_keys[None, :])[None], scores, masked_score)


def attend(query_h, key_h, value_h, seg_keys):
    block_rows = min(512, query_h.shape[1])
    block_count = query_h.shape[1] // block_rows

    def one_block(begin_row):
        query_blk = lax.dynamic_slice_in_dim(query_h, begin_row, block_rows, 1)
        seg_blk = lax.dynamic_slice_in_dim(seg_keys, begin_row, block_rows, 0)
        scores = masked_scores(query_blk, key_h, seg_blk, seg_keys)
        row_max = jnp.max(scores, axis=-1, keepdims=True)
        numerator = jnp.exp(scores - row_max)
        row_total = jnp.sum(numerator, axis=-1, keepdims=True)
        prob_low = (numerator / row_total).astype(jnp.bfloat16)
        attended = jnp.einsum("hqk,hkd->hqd", prob_low, value_h, preferred_element_type=jnp.float32)
        return (attended.astype(jnp.bfloat16), (row_max + jnp.log(row_total))[..., 0])

    starts = jnp.arange(block_count, dtype=jnp.int32) * block_rows
    attended, log_sums = lax.map(one_block, starts)
    heads_out = attended.transpose(1, 0, 2, 3).reshape(query_h.shape)
    log_sums = log_sums.transpose(1, 0, 2).reshape(query_h.shape[0], query_h.shape[1])
    return (heads_out, log_sums)


def attend_back(query_h, key_h, value_h, seg_keys, log_sums, grad_out):
    block_rows = min(512, query_h.shape[1])
    block_count = query_h.shape[1] // block_rows

    def one_block(carry, begin_row):
        grad_key, grad_value = carry
        query_blk = lax.dynamic_slice_in_dim(query_h, begin_row, block_rows, 1)
        grad_blk = lax.dynamic_slice_in_dim(grad_out, begin_row, block_rows, 1)
        lse_blk = lax.dynamic_slice_in_dim(log_sums, begin_row, block_rows, 1)
        seg_blk = lax.dynamic_slice_in_dim(seg_keys, begin_row, block_rows, 0)
        scores = masked_scores(query_blk, key_h, seg_blk, seg_keys)
        probs = jnp.exp(scores - lse_blk[..., None])
        prob_low = probs.astype(jnp.bfloat16)
        grad_value = grad_value + jnp.einsum(
            "hqk,hqd->hkd", prob_low, grad_blk, preferred_element_type=jnp.float32
        )
        grad_prob = jnp.einsum(
            "hqd,hkd->hqk", grad_blk, value_h, preferred_element_type=jnp.float32
        )
        row_dot = jnp.sum(probs * grad_prob, axis=-1, keepdims=True)
        grad_score = (probs * (grad_prob - row_dot) * HEAD_DIM ** (-0.5)).astype(jnp.bfloat16)
        grad_query = jnp.einsum(
            "hqk,hkd->hqd", grad_score, key_h, preferred_element_type=jnp.float32
        )
        grad_key = grad_key + jnp.einsum(
            "hqk,hqd->hkd", grad_score, query_blk, preferred_element_type=jnp.float32
        )
        return ((grad_key, grad_value), grad_query)

    starts = jnp.arange(block_count, dtype=jnp.int32) * block_rows
    zeros_kv = jnp.zeros(key_h.shape, jnp.float32)
    (grad_key, grad_value), grad_query = lax.scan(one_block, (zeros_kv, zeros_kv), starts)
    grad_query = grad_query.transpose(1, 0, 2, 3).reshape(query_h.shape)
    return (
        grad_query.astype(jnp.bfloat16),
        grad_key.astype(jnp.bfloat16),
        grad_value.astype(jnp.bfloat16),
    )


def spread_rows(values):
    return lax.all_gather(values, "tp", axis=0, tiled=True)


def combine_rows(partial_value):
    return lax.psum_scatter(partial_value, "tp", scatter_dimension=0, tiled=True)


def spread_grads(values):
    return lax.all_gather(values, "tp", axis=0, tiled=True)


def combine_grads(partial_value):
    return lax.psum_scatter(
        partial_value.astype(jnp.bfloat16), "tp", scatter_dimension=0, tiled=True
    ).astype(jnp.float32)


def fetch_weights(w_qkv, w_attn_out, w_up, w_down, layer):
    return (
        lax.all_gather(w_qkv[layer], "dp", axis=1, tiled=True),
        lax.all_gather(w_attn_out[layer], "dp", axis=1, tiled=True),
        lax.all_gather(w_up[layer], "dp", axis=0, tiled=True),
        lax.all_gather(w_down[layer], "dp", axis=1, tiled=True),
    )


def reduce_weight_grads(grads):
    return (
        lax.psum_scatter(
            grads[0].astype(jnp.bfloat16), "dp", scatter_dimension=1, tiled=True
        ).astype(jnp.float32),
        lax.psum_scatter(
            grads[1].astype(jnp.bfloat16), "dp", scatter_dimension=1, tiled=True
        ).astype(jnp.float32),
        lax.psum_scatter(
            grads[2].astype(jnp.bfloat16), "dp", scatter_dimension=0, tiled=True
        ).astype(jnp.float32),
        lax.psum_scatter(
            grads[3].astype(jnp.bfloat16), "dp", scatter_dimension=1, tiled=True
        ).astype(jnp.float32),
    )


def block_forward(resid_in, seg_local, gains, biases, weights):
    qkv_w, attn_w, up_w, down_w = weights
    normed = layer_norm(resid_in, gains[0], biases[0]).astype(jnp.bfloat16)
    normed_all, seg_all = (
        lax.all_gather(normed, "tp", axis=0, tiled=True),
        lax.all_gather(seg_local, "tp", axis=0, tiled=True),
    )
    query_h = split_heads(product(normed_all, qkv_w[0]).astype(jnp.bfloat16))
    key_h = split_heads(product(normed_all, qkv_w[1]).astype(jnp.bfloat16))
    value_h = split_heads(product(normed_all, qkv_w[2]).astype(jnp.bfloat16))
    heads_out, log_sums = attend(query_h, key_h, value_h, seg_all)
    attn_rows = join_heads(heads_out)
    middle = resid_in + combine_rows(product(attn_rows, attn_w))
    normed_mid = spread_rows(layer_norm(middle, gains[1], biases[1]).astype(jnp.bfloat16))
    hidden_pre = product(normed_mid, up_w)
    hidden = gelu_tanh(hidden_pre).astype(jnp.bfloat16)
    result = middle + combine_rows(product(hidden, down_w))
    kept = (
        resid_in,
        middle,
        normed_all,
        seg_all,
        query_h,
        key_h,
        value_h,
        log_sums,
        attn_rows,
        normed_mid,
        hidden_pre,
        hidden,
    )
    return (result, kept)


def block_backward(kept, gains, biases, weights, grad_result):
    (
        resid_in,
        middle,
        normed_all,
        seg_all,
        query_h,
        key_h,
        value_h,
        log_sums,
        attn_rows,
        normed_mid,
        hidden_pre,
        hidden,
    ) = kept
    qkv_w, attn_w, up_w, down_w = weights
    grad_branch = spread_grads(grad_result.astype(jnp.bfloat16))
    grad_down = product_tn(hidden, grad_branch)
    grad_hidden = product_nt(grad_branch, down_w)
    _, gelu_back = jax.vjp(gelu_tanh, hidden_pre)
    grad_pre = gelu_back(grad_hidden)[0].astype(jnp.bfloat16)
    grad_up = product_tn(normed_mid, grad_pre)
    grad_norm_mid = combine_grads(product_nt(grad_pre, up_w))
    _, norm_back_mid = jax.vjp(layer_norm, middle, gains[1], biases[1])
    grad_mid_ln, grad_gain_mid, grad_bias_mid = norm_back_mid(grad_norm_mid)
    grad_middle = grad_result + grad_mid_ln
    grad_attn_all = spread_grads(grad_middle.astype(jnp.bfloat16))
    grad_attn = product_tn(attn_rows, grad_attn_all)
    grad_heads = split_heads(product_nt(grad_attn_all, attn_w).astype(jnp.bfloat16))
    grad_query, grad_key, grad_value = attend_back(
        query_h, key_h, value_h, seg_all, log_sums, grad_heads
    )
    grad_parts = [join_heads(grad_query), join_heads(grad_key), join_heads(grad_value)]
    grad_qkv = jnp.stack([product_tn(normed_all, grad_part) for grad_part in grad_parts])
    grad_normed_part = (
        product_nt(grad_parts[0], qkv_w[0])
        + product_nt(grad_parts[1], qkv_w[1])
        + product_nt(grad_parts[2], qkv_w[2])
    )
    grad_normed = combine_grads(grad_normed_part)
    _, norm_back_in = jax.vjp(layer_norm, resid_in, gains[0], biases[0])
    grad_in_ln, grad_gain_in, grad_bias_in = norm_back_in(grad_normed)
    gain_grads = jnp.stack([grad_gain_in, grad_gain_mid])
    bias_grads = jnp.stack([grad_bias_in, grad_bias_mid])
    return (
        grad_middle + grad_in_ln,
        gain_grads,
        bias_grads,
        (grad_qkv, grad_attn, grad_up, grad_down),
    )


def local(
    tokens,
    segment_ids,
    norm_gains,
    norm_biases,
    w_qkv,
    w_attn_out,
    w_up,
    w_down,
    w_vq_in,
    w_vq_out,
    codebook,
    cotangent,
):
    gain_sum = jnp.zeros(norm_gains.shape, jnp.float32)
    bias_sum = jnp.zeros(norm_biases.shape, jnp.float32)
    vq_in_sum = jnp.zeros(w_vq_in.shape, jnp.float32)
    vq_out_sum = jnp.zeros(w_vq_out.shape, jnp.float32)
    code_sum = jnp.zeros(codebook.shape, jnp.float32)
    layer_sums = [None, None]
    outputs = []
    input_grads = []
    for micro in range(MICRO):
        resid_in = tokens[micro].astype(jnp.float32)
        seg_local = segment_ids[micro]
        enc_weights = fetch_weights(w_qkv, w_attn_out, w_up, w_down, 0)
        encoded, enc_kept = block_forward(
            resid_in, seg_local, norm_gains[0:2], norm_biases[0:2], enc_weights
        )
        (decoder_in, _), vq_back = jax.vjp(
            quantize, encoded, norm_gains[2], norm_biases[2], w_vq_in, w_vq_out, codebook
        )
        dec_weights = fetch_weights(w_qkv, w_attn_out, w_up, w_down, 1)
        decoded, dec_kept = block_forward(
            decoder_in, seg_local, norm_gains[3:5], norm_biases[3:5], dec_weights
        )
        outputs.append(decoded)
        grad_dec_in, gains_dec, biases_dec, grads_dec = block_backward(
            dec_kept, norm_gains[3:5], norm_biases[3:5], dec_weights, cotangent[micro]
        )
        grad_encoded, grad_gain_vq, grad_bias_vq, grad_in_w, grad_out_w, grad_codes = vq_back(
            (grad_dec_in, jnp.ones((), jnp.float32))
        )
        grad_input, gains_enc, biases_enc, grads_enc = block_backward(
            enc_kept, norm_gains[0:2], norm_biases[0:2], enc_weights, grad_encoded
        )
        input_grads.append(grad_input)
        gain_sum = gain_sum + jnp.concatenate([gains_enc, grad_gain_vq[None], gains_dec], axis=0)
        bias_sum = bias_sum + jnp.concatenate([biases_enc, grad_bias_vq[None], biases_dec], axis=0)
        vq_in_sum = vq_in_sum + grad_in_w
        vq_out_sum = vq_out_sum + grad_out_w
        code_sum = code_sum + grad_codes
        for layer, grads in ((0, grads_enc), (1, grads_dec)):
            reduced = reduce_weight_grads(grads)
            if layer_sums[layer] is None:
                layer_sums[layer] = reduced
            else:
                layer_sums[layer] = jax.tree.map(jnp.add, layer_sums[layer], reduced)
    gain_tot, bias_tot, vq_in_tot, vq_out_tot, code_tot = lax.psum(
        (gain_sum, bias_sum, vq_in_sum, vq_out_sum, code_sum), ("dp", "tp")
    )
    return (
        jnp.stack(outputs),
        jnp.stack(input_grads),
        gain_tot,
        bias_tot[0:3],
        bias_tot[3:5],
        jnp.stack([layer_sums[0][0], layer_sums[1][0]]),
        jnp.stack([layer_sums[0][1], layer_sums[1][1]]),
        jnp.stack([layer_sums[0][2], layer_sums[1][2]]),
        jnp.stack([layer_sums[0][3], layer_sums[1][3]]),
        vq_in_tot,
        vq_out_tot,
        code_tot,
    )


def solution(mesh):
    n_dp, n_tp = mesh.shape["dp"], mesh.shape["tp"]
    fits = n_tp == MICRO and n_dp == 16
    return jax.shard_map(
        functools.partial(whole_groups, n_dp) if fits else local,
        mesh=mesh,
        in_specs=(
            P(None, ("dp", "tp"), None),
            P(None, ("dp", "tp")),
            P(),
            P(),
            P(None, None, "dp", "tp"),
            P(None, "tp", "dp"),
            P(None, "dp", "tp"),
            P(None, "tp", "dp"),
            P(),
            P(),
            P(),
            P(None, ("dp", "tp"), None),
        ),
        out_specs=(
            P(None, ("dp", "tp"), None),
            P(None, ("dp", "tp"), None),
            P(),
            P(),
            P(),
            P(None, None, "dp", "tp"),
            P(None, "tp", "dp"),
            P(None, "dp", "tp"),
            P(None, "tp", "dp"),
            P(),
            P(),
            P(),
        ),
        check_vma=False,
    )
```

```python
import functools

import jax
import jax.numpy as jnp
from jax import lax
from jax.experimental import pallas as pl
from jax.experimental.pallas import tpu as pltpu
from jax.sharding import PartitionSpec as P

HEAD_DIM = 64
MICRO = 2
bf16 = jnp.bfloat16
f32 = jnp.float32
highest = lax.Precision.HIGHEST
ln_eps = 1e-05
norm_eps = 1e-06
temper = 10.0
commit_weight = 64.0
gelu_coef = 0.7978845608028654
masked_score = -1e30
log2e = 1.4426950408889634
vmem_cap = 26 * 1024 * 1024


PLANE = ((0, 0), (0, 1), (1, 0), (1, 1))


def exchange(values, dp_xor, tp_xor, n_dp):
    pairs = [
        (d * 2 + t, (d ^ dp_xor) * 2 + (t ^ tp_xor)) for d in range(n_dp) for t in range(2)
    ]
    return lax.ppermute(values, ("dp", "tp"), pairs)


def spread_line(shard, n_dp):
    return [shard] + [exchange(shard, 4 * k, 0, n_dp) for k in range(1, 4)]


def plane_send(lows, n_dp):
    return [exchange(low, 2 * y, x, n_dp) for (y, x), low in zip(PLANE[1:], lows)]


def line_send(lows, n_dp):
    return [exchange(low, 4 * k, 0, n_dp) for k, low in zip(range(1, 4), lows)]


def dot(a, b):
    return jnp.dot(a, b, preferred_element_type=f32)


def dot_nt(a, b, precision=None):
    return lax.dot_general(
        a, b, (((1,), (1,)), ((), ())), preferred_element_type=f32, precision=precision
    )


def dot_full(a, b):
    return jnp.dot(a, b, preferred_element_type=f32, precision=highest)


def ln_parts(x):
    centred = x - jnp.mean(x, axis=-1, keepdims=True)
    inv = lax.rsqrt(jnp.mean(centred * centred, axis=-1, keepdims=True) + ln_eps)
    return centred * inv, inv


def ln_back(grad, xhat, inv, gain):
    scaled = grad * gain
    return inv * (
        scaled
        - jnp.mean(scaled, axis=-1, keepdims=True)
        - xhat * jnp.mean(scaled * xhat, axis=-1, keepdims=True)
    )


def split2(x):
    hi = x.astype(bf16)
    return hi, (x - hi.astype(f32)).astype(bf16)


def split3(x):
    hi, _ = split2(x)
    rest = x - hi.astype(f32)
    mid = rest.astype(bf16)
    return hi, mid, (rest - mid.astype(f32)).astype(bf16)


def order_matrix(dp, inverse):
    at = lax.broadcasted_iota(jnp.int32, (512, 512), 0 if inverse else 1)
    other = lax.broadcasted_iota(jnp.int32, (512, 512), 1 if inverse else 0)
    block = at >> 5
    bits = ((block & 3) << 2) | (((block >> 2) & 1) << 1) | (block >> 3)
    return jnp.where(other == (((dp ^ bits) << 5) | (at & 31)), 1.0, 0.0).astype(bf16)


def ordered(x, matrix):
    if x.dtype == bf16:
        return dot(x, matrix)
    hi, mid, lo = split3(x)
    return (dot(hi, matrix) + dot(mid, matrix)) + dot(lo, matrix)


def w_at(a, b, t, first, width):
    parts = []
    for core in range(2):
        for y in range(2):
            if first < 1536:
                part = a[2 * core + y][t, :, :, first : first + width]
            else:
                part = b[2 * core + t][y, :, :, first - 1536 : first - 1536 + width]
            parts.append(part.reshape(128, width))
    return jnp.concatenate(parts, axis=0)


def put_grad(refs, t, cols, value):
    for core, ref in enumerate(refs):
        for y in range(2):
            rows = value[core * 256 + y * 128 : core * 256 + (y + 1) * 128]
            ref[2 * y + t, :, :, cols] = rows.reshape(4, 32, rows.shape[1])


def start_all(copies):
    for copy in copies:
        copy.start()


def wait_all(copies):
    for copy in copies:
        copy.wait()


def head_rows(ref, pair, which):
    own = ref[pl.ds(pair * 128 + which * HEAD_DIM, HEAD_DIM), :]
    zero = jnp.zeros_like(own)
    return jnp.concatenate([own, zero] if which == 0 else [zero, own], axis=0)


def segment_mask(own, other):
    ids = jnp.concatenate([own[:, 512:640], other[:, 512:640]], axis=0).astype(f32)
    return jnp.where(ids[:, 0:1] == ids.T[0:1, :], 0.0, masked_score)


def load_rows(x, own, other):
    if x is None:
        return jnp.concatenate([own[:, :512], other[:, :512]], axis=0).astype(f32)
    return x[...]


def gain_of(norms, at):
    return norms[at : at + 1, :]


def bias_of(norms, at):
    return norms[8 + at : 9 + at, :]


def attn_fwd_kernel(with_x, at, own, other, norms, *refs):
    w, refs = refs[:4], refs[4:]
    x, refs = (refs[0], refs[1:]) if with_x else (None, refs)
    x1, lse, saved, refs = refs[0], refs[1], refs[2:8], refs[8:]
    h, vt, ot, mask, qs, k, v, o, qst, kt, out_sems = refs
    keeps = [
        pltpu.make_async_copy(held, to, out_sems.at[i])
        for i, (held, to) in enumerate(zip((qs, k, v, o, qst, kt), saved))
    ]
    xf = load_rows(x, own, other)
    h[...] = (ln_parts(xf)[0] * gain_of(norms, at) + bias_of(norms, at)).astype(bf16)
    mask[...] = segment_mask(own, other)
    for t in range(2):
        cols = slice(t * 256, (t + 1) * 256)
        q = dot(h[...], w_at(w, None, t, 0, 256)).astype(bf16)
        qs[:, cols] = (q * HEAD_DIM ** (-0.5)).astype(bf16)
        k[:, cols] = dot(h[...], w_at(w, None, t, 256, 256)).astype(bf16)
        v[:, cols] = dot(h[...], w_at(w, None, t, 512, 256)).astype(bf16)
    qst[...] = qs[...].T
    kt[...] = k[...].T
    vt[...] = v[...].T
    for i in (0, 1, 2, 4, 5):
        keeps[i].start()
    for pair in range(4):
        k_pair = k[:, pair * 128 : (pair + 1) * 128]
        for which in range(2):
            scores = dot(k_pair, head_rows(qst, pair, which)) + mask[...]
            top = jnp.max(scores, axis=0, keepdims=True)
            numer = jnp.exp(scores - top).astype(bf16)
            rows = pl.ds(pair * 128 + which * HEAD_DIM, HEAD_DIM)
            left = jnp.concatenate([vt[rows, :], jnp.ones((16, 512), bf16)], axis=0)
            both = dot(left, numer)
            total = both[HEAD_DIM : HEAD_DIM + 1, :]
            ot[rows, :] = (both[:HEAD_DIM, :] / total).astype(bf16)
            lse[pl.ds(pair * 2 + which, 1), :] = top + jnp.log(total)
    o[...] = ot[...].T
    keeps[3].start()
    x1[...] = xf + dot_nt(
        o[...], jnp.concatenate([w_at(w, None, t, 768, 256) for t in range(2)], axis=1)
    )
    wait_all(keeps)


def gelu_parts(u):
    square = u * u
    tanh = jnp.tanh(gelu_coef * u * (1.0 + 0.044715 * square))
    return 0.5 * u * (1.0 + tanh), tanh, square


def mlp_weights(w):
    def up(t, part):
        return w_at(w[:4], w[4:], t, 1024 + part * 512, 512)

    def down(t, part):
        return w_at(w[:4], w[4:], t, 2048 + part * 512, 512)

    return up, down


def mlp_rows(at, x, norms, w, h2):
    up, down = mlp_weights(w)
    h2[...] = (ln_parts(x)[0] * gain_of(norms, at) + bias_of(norms, at)).astype(bf16)
    places = [(t, part) for t in range(2) for part in range(2)]
    hidden = [gelu_parts(dot(h2[...], up(*place)))[0].astype(bf16) for place in places]
    return x + dot_nt(
        jnp.concatenate(hidden, axis=1),
        jnp.concatenate([down(*place) for place in places], axis=1),
    )


def mlp_bwd_kernel(split, at, ids, x1, norms, *refs):
    up, down = mlp_weights(refs[:8])
    refs = refs[8:]
    if split:
        own, other, refs = refs[0], refs[1], refs[2:]
    else:
        dy, refs = refs[0], refs[1:]
    dx1, small, grads = refs[0], refs[1], refs[2:4]
    h2, h2t, dyb, dybt = refs[4:8]
    if split:
        dy = refs[8]
        dy[0:256, :] = ordered(own[ids[1]], order_matrix(ids[0], False))
        dy[256:, :] = other[:, 640:].astype(f32)
    h2[...] = (ln_parts(x1[...])[0] * gain_of(norms, at) + bias_of(norms, at)).astype(bf16)
    h2t[...] = h2[...].T
    dyb[...] = dy[...].astype(bf16)
    dybt[...] = dyb[...].T
    dpres, w_ups = [], []
    for t in range(2):
        for part in range(2):
            cols = slice(part * 512, (part + 1) * 512)
            w_up = up(t, part)
            pre = dot(h2[...], w_up)
            hidden, tanh, square = gelu_parts(pre)
            slope = 0.5 * (1.0 + tanh) + (0.5 * gelu_coef) * pre * (1.0 - tanh * tanh) * (
                1.0 + (3 * 0.044715) * square
            )
            dhidden = dot(dyb[...], down(t, part))
            dpre = (dhidden * slope).astype(bf16)
            out_cols = slice(1024 + part * 512, 1024 + (part + 1) * 512)
            put_grad(grads, t, out_cols, dot(dybt[...], hidden.astype(bf16)).astype(bf16))
            put_grad(grads, t, cols, dot(h2t[...], dpre).astype(bf16))
            dpres.append(dpre)
            w_ups.append(w_up)
    xhat, inv = ln_parts(x1[...])
    grad = dot_nt(jnp.concatenate(dpres, axis=1), jnp.concatenate(w_ups, axis=1))
    small[0:1, :] = jnp.sum(grad * xhat, axis=0, keepdims=True)
    small[1:2, :] = jnp.sum(grad, axis=0, keepdims=True)
    dx1[...] = dy[...] + ln_back(grad, xhat, inv, gain_of(norms, at))


def heads_back(low, w, saved, lse, mask, put_out, scratch):
    qs, k, v, o, qst, kt = saved
    flip, do, dot_t, dqt, dq, dk, dv = scratch
    flip[...] = low.T
    for t in range(2):
        cols = slice(t * 256, (t + 1) * 256)
        do[:, cols] = dot(low, w_at(w, None, t, 768, 256)).astype(bf16)
        put_out(t, dot(flip[...], o[:, cols]).astype(bf16))
    dot_t[...] = do[...].T
    first = lax.broadcasted_iota(jnp.int32, (512, 128), 1) < HEAD_DIM
    for pair in range(4):
        lanes = slice(pair * 128, (pair + 1) * 128)
        dvs, dks = [], []
        for which in range(2):
            head = pair * 2 + which
            rows = pl.ds(head * HEAD_DIM, HEAD_DIM)
            scores = dot(k[:, lanes], head_rows(qst, pair, which)) + mask[...]
            probs = jnp.exp(scores - lse[head : head + 1, :])
            dprobs = dot(v[:, lanes], head_rows(dot_t, pair, which))
            shift = jnp.sum(probs * dprobs, axis=0, keepdims=True)
            dscore = (probs * (dprobs - shift)).astype(bf16)
            dvs.append(dot(probs.astype(bf16), do[:, lanes]))
            dks.append(dot(dscore, qs[:, lanes]))
            dqt[rows, :] = (dot(kt[rows, :], dscore) * HEAD_DIM ** (-0.5)).astype(bf16)
        dv[:, lanes] = jnp.where(first, dvs[0], dvs[1]).astype(bf16)
        dk[:, lanes] = jnp.where(first, dks[0], dks[1]).astype(bf16)
    dq[...] = dqt[...].T


def rows_back(at, xf, norms, w, parts, small, grads, h, flip):
    h[...] = (ln_parts(xf)[0] * gain_of(norms, at) + bias_of(norms, at)).astype(bf16)
    flip[...] = h[...].T
    halves = []
    for t in range(2):
        cols = slice(t * 256, (t + 1) * 256)
        halves.append(jnp.concatenate([part[:, cols] for part in parts], axis=1))
        put_grad(grads, t, slice(0, 768), dot(flip[...], halves[t]).astype(bf16))
    grad = dot_nt(
        jnp.concatenate(halves, axis=1),
        jnp.concatenate([w_at(w, None, t, 0, 768) for t in range(2)], axis=1),
    )
    xhat, inv = ln_parts(xf)
    small[0:1, :] = jnp.sum(grad * xhat, axis=0, keepdims=True)
    small[1:2, :] = jnp.sum(grad, axis=0, keepdims=True)
    return ln_back(grad, xhat, inv, gain_of(norms, at))


def take_saved(saved, held, sems):
    copies = [
        pltpu.make_async_copy(a, b, sems.at[i]) for i, (a, b) in enumerate(zip(saved, held))
    ]
    start_all(copies)
    return copies


def attn_bwd_kernel(at, own, other, dx1, norms, lse, *refs):
    w, saved, x, refs = refs[:4], refs[4:10], refs[10], refs[11:]
    dx, small, grads = refs[0], refs[1], refs[2:4]
    mask, h, held, scratch, sems = refs[4], refs[5], refs[6:12], refs[12:19], refs[19]
    copies = take_saved(saved, held, sems)
    mask[...] = segment_mask(own, other)
    low = dx1[...].astype(bf16)
    wait_all(copies)

    def put_out(t, value):
        put_grad(grads, t, slice(768, 1024), value)

    heads_back(low, w, held, lse, mask, put_out, scratch)
    dx[...] = dx1[...] + rows_back(
        at, x[...], norms, w, scratch[4:], small, grads, h, scratch[0]
    )


def heads_bwd_kernel(own, other, dx1, lse, *refs):
    w, saved, refs = refs[:4], refs[4:10], refs[10:]
    parts, grads, mask, held = refs[:3], refs[3:5], refs[5], refs[6:12]
    scratch, sems = (*refs[12:16], *parts), refs[16]
    copies = take_saved(saved, held, sems)
    mask[...] = segment_mask(own, other)
    low = dx1[...].astype(bf16)
    wait_all(copies)

    def put_out(t, value):
        put_grad(grads, t, slice(0, 256), value)

    heads_back(low, w, held, lse, mask, put_out, scratch)


def rows_bwd_kernel(
    ids, own, other, dx1, norms, dq, dk, dv, out_0, out_1, other_small, d_x1, *refs
):
    w, d_w, (dx, dx_low, y, y_low), grads, (small, h, flip) = (
        refs[:4],
        refs[4:12],
        refs[12:16],
        refs[16:18],
        refs[18:],
    )
    total = dx1[...] + rows_back(
        0, load_rows(None, own, other), norms, w, (dq, dk, dv), small, grads, h, flip
    )
    dx[...] = total[:256, :]
    dx_low[...] = total[256:, :].astype(bf16)
    rows = jnp.concatenate([small[0:2, :], other_small[0:2, :], jnp.zeros((4, 512), f32)], axis=0)
    packed = pack_rows(ordered(rows, order_matrix(ids[0], True)))
    for grad, part in zip(grads, (out_0, out_1)):
        for i in range(4):
            for z in range(4):
                grad[i, z, :, 768:1024] = part[i, z]
                grad[i, z, :, 1024:1152] = packed
    rows = mlp_rows(4, d_x1[...], norms, d_w, h)
    y[...] = rows[:256, :]
    y_low[...] = rows[256:, :].astype(bf16)


def pack_rows(rows):
    cut = [rows[i : i + 1, 128 * j : 128 * (j + 1)] for i in range(4) for j in range(4)]
    return jnp.concatenate(split2(jnp.concatenate(cut, axis=0)), axis=0)


def code_prep_kernel(book_t, stack, stack_t):
    def one_chunk(index, _):
        lanes = pl.ds(pl.multiple_of(index * 512, 512), 512)
        rows = book_t[:, lanes]
        unit = rows * lax.rsqrt(jnp.sum(rows * rows, axis=0, keepdims=True) + norm_eps)
        hi, mid, lo = split3(unit)
        stack_t[:, lanes] = jnp.concatenate([hi, mid, lo, jnp.ones((32, 512), bf16)], axis=0)
        tall = jnp.concatenate([hi, mid, lo, hi, mid, hi, jnp.zeros((64, 512), bf16)], axis=0)
        stack[lanes, :] = tall.T
        return 0

    lax.fori_loop(0, book_t.shape[1] // 512, one_chunk, 0)


def factor_stack(x):
    hi, mid, lo = split3(x)
    return jnp.concatenate([hi, hi, hi, mid, mid, lo, jnp.zeros((64, x.shape[1]), bf16)], axis=0)


def code_loads(pairs, sems):
    loads = []
    for piece in range(4):
        group = []
        for at, (held, to, by_row) in enumerate(pairs):
            size = held.shape[0 if by_row else 1] // 4
            part = pl.ds(piece * size, size)
            place = (part, slice(None)) if by_row else (slice(None), part)
            group.append(pltpu.make_async_copy(held.at[place], to.at[place], sems.at[at, piece]))
        start_all(group)
        loads.append(group)
    return loads


def mlp_vq_kernel(x1, norms, vq_w, stack_hbm, stack_t_hbm, *refs):
    w, (e, u, kept, numer_hbm, h2, acc, stack, stack_t, numer, sems, out_sems) = refs[:8], refs[8:]
    loads = code_loads([(stack_hbm, stack, True), (stack_t_hbm, stack_t, False)], sems)
    e[...] = mlp_rows(1, x1[...], norms, w, h2)
    lnv = ln_parts(e[...])[0] * gain_of(norms, 2) + bias_of(norms, 2)
    raw = dot_nt(vq_w[0:32, :], lnv, highest)
    inv = lax.rsqrt(jnp.sum(raw * raw, axis=0, keepdims=True) + norm_eps)
    latent = raw * inv
    right = factor_stack(latent * (temper * log2e))
    chunks, keeps = stack.shape[0] // 2048, []
    for piece, group in enumerate(loads):
        wait_all(group)
        for part in range(piece * chunks // 4, (piece + 1) * chunks // 4):
            numers = []
            for index in range(4 * part, 4 * part + 4):
                codes = slice(index * 512, (index + 1) * 512)
                numers.append(jnp.exp2(dot(stack[codes, :], right)).astype(bf16))
            if part > 1:
                keeps[part - 2].wait()
            keeps.append(
                pltpu.make_async_copy(
                    numer.at[part % 2],
                    numer_hbm.at[pl.ds(part * 2048, 2048), :],
                    out_sems.at[part % 2],
                )
            )
            numer[part % 2] = jnp.concatenate(numers, axis=0)
            keeps[part].start()
            sums = dot(stack_t[:, part * 2048 : (part + 1) * 2048], numer[part % 2])
            if part == 0:
                acc[...] = sums
            else:
                acc[...] += sums
    total = acc[96:97, :]
    soft = (acc[0:32, :] + acc[32:64, :] + acc[64:96, :]) / total
    kept[0:32, :] = latent
    kept[32:64, :] = soft
    kept[64:65, :] = total
    kept[65:66, :] = inv
    u[...] = dot_full(soft.T, vq_w[32:64, :])
    wait_all(keeps[-2:])


def vq_bwd_kernel(
    ids, e, du, norms, vq_w, stack_hbm, stack_t_hbm, book_hbm, numer_hbm, kept, *refs
):
    small0, small1, de, code_keep, code_send = refs[:5]
    acc, grads, small, tail, stack, stack_t, book_t, numer, load_sems, sems = refs[5:]
    loads = code_loads(
        [
            (stack_hbm, stack, True),
            (numer_hbm, numer, True),
            (stack_t_hbm, stack_t, False),
            (book_hbm, book_t, False),
        ],
        load_sems,
    )
    xhat, inv_ln = ln_parts(e[...])
    lnv = xhat * gain_of(norms, 2) + bias_of(norms, 2)
    latent, soft = kept[0:32, :], kept[32:64, :]
    total, inv = kept[64:65, :], kept[65:66, :]
    direct = (2.0 * 1.25 * commit_weight) * (latent - soft)
    dsoft = dot_nt(vq_w[32:64, :], du[...], highest) - direct
    small[32:64, :] = dot_full(soft, du[...])
    shift = jnp.sum(dsoft * soft, axis=0, keepdims=True) / total
    dsoft = dsoft / total
    right = factor_stack(dsoft)
    pads = jnp.zeros((64, 512), f32)

    def tall(x):
        hi, lo = split2(x)
        return jnp.concatenate([hi.astype(f32), lo.astype(f32), pads], axis=0).T.astype(bf16)

    sides = jnp.concatenate([tall(dsoft), tall(latent * temper)], axis=0)
    chunks = stack.shape[0] // 2048
    for piece, group in enumerate(loads):
        wait_all(group)
        for part in range(piece * chunks // 4, (piece + 1) * chunks // 4):
            dlogits = []
            for index in range(4 * part, 4 * part + 4):
                codes = slice(index * 512, (index + 1) * 512)
                held = numer[codes, :]
                dlogit = (held.astype(f32) * (dot(stack[codes, :], right) - shift)).astype(bf16)
                dlogits.append(dlogit)
                sums = jnp.concatenate([held, dlogit], axis=1)
                dcode = dot(sums, sides).T
                dcode = dcode[0:32, :] + dcode[32:64, :]
                rows = book_t[:, codes]
                scale = lax.rsqrt(jnp.sum(rows * rows, axis=0, keepdims=True) + norm_eps)
                unit = rows * scale
                grads[:, codes] = (
                    scale * (dcode - unit * jnp.sum(unit * dcode, axis=0, keepdims=True))
                ).astype(bf16)
            sums = dot(
                stack_t[0:96, part * 2048 : (part + 1) * 2048], jnp.concatenate(dlogits, axis=0)
            )
            if part == 0:
                acc[...] = sums
            else:
                acc[...] += sums
    dlatent = temper * (acc[0:32, :] + acc[32:64, :] + acc[64:96, :]) + direct
    draw = inv * (dlatent - latent * jnp.sum(latent * dlatent, axis=0, keepdims=True))
    small[0:32, :] = dot_full(draw, lnv)
    dln = dot_full(draw.T, vq_w[0:32, :])
    small[64:65, :] = jnp.sum(dln * xhat, axis=0, keepdims=True)
    small[65:66, :] = jnp.sum(dln, axis=0, keepdims=True)
    small[66:68, :] = small0[0:2, :]
    small[68:70, :] = small1[0:2, :]
    small[70:96, :] = jnp.zeros((26, 512), f32)
    small[...] = ordered(small[...], order_matrix(ids[0], True))
    for block in range(3):
        for at, part in enumerate(split2(small[block * 32 : (block + 1) * 32, :])):
            for side in range(2):
                tail[block * 2 + side, :, at * 256 : (at + 1) * 256] = part[
                    :, side * 256 : (side + 1) * 256
                ]
    tail[6:8] = jnp.zeros((2, 32, 512), bf16)
    core, z = ids[0] % 2, ids[0] // 4
    copies = []
    for slot, (at, to) in enumerate(((core, code_keep), (1 - core, code_send))):
        for k in range(4):
            part = at * 4 + (z ^ k)
            lanes = pl.ds(pl.multiple_of(part * 1024, 1024), 1024)
            copies += [
                pltpu.make_async_copy(
                    grads.at[:, lanes], to.at[k, :, pl.ds(0, 1024)], sems.at[0, slot, k]
                ),
                pltpu.make_async_copy(
                    tail.at[part], to.at[k, :, pl.ds(1024, 512)], sems.at[1, slot, k]
                ),
            ]
    for copy in copies:
        copy.start()
    de[...] = ln_back(dln, xhat, inv_ln, gain_of(norms, 2))
    for copy in copies:
        copy.wait()


SMEM = pl.BlockSpec(memory_space=pltpu.SMEM)
VMEM = pl.BlockSpec(memory_space=pltpu.VMEM)
ANY = pl.BlockSpec(memory_space=pl.ANY)


def shaped(*pairs):
    return [jax.ShapeDtypeStruct(shape, dtype) for shape, dtype in pairs]


def pin(array):
    return pltpu.with_memory_space_constraint(array, pltpu.HBM)


def call(kernel, name, in_specs, out_specs, outs, scratch, flops, after=(), carry=()):
    n_in, n_extra, n_out = len(in_specs), len(after) + len(carry), len(outs)

    def body(*refs):
        first = n_in + n_extra
        kernel(*refs[:n_in], *refs[first : first + n_out], *refs[first + n_out + len(carry) :])

    made = pl.pallas_call(
        body,
        name=name,
        in_specs=in_specs + [ANY] * n_extra,
        out_specs=out_specs + [ANY] * len(carry),
        out_shape=outs + [jax.ShapeDtypeStruct(a.shape, a.dtype) for a in carry],
        scratch_shapes=scratch,
        input_output_aliases={n_in + len(after) + i: n_out + i for i in range(len(carry))},
        compiler_params=pltpu.CompilerParams(vmem_limit_bytes=vmem_cap),
        cost_estimate=pl.CostEstimate(flops=flops, bytes_accessed=10**6, transcendentals=0),
    )

    def run(*args):
        res = made(*args, *after, *carry)
        return (*res[:n_out], list(res[n_out:]))

    return run


DMA = pltpu.SemaphoreType.DMA
ROWS2 = (512, 512)


def attn_fwd(at, marked, xs, norms, w, after=(), carry=()):
    outs = shaped((ROWS2, f32), ((8, 512), f32)) + [pltpu.HBM(ROWS2, bf16)] * 6
    scratch = [
        *[pltpu.VMEM(ROWS2, bf16)] * 3,
        pltpu.VMEM(ROWS2, f32),
        *[pltpu.VMEM(ROWS2, bf16)] * 6,
        DMA((6,)),
    ]
    x1, lse, *saved, carried = call(
        functools.partial(attn_fwd_kernel, bool(xs), at),
        "attn_fwd",
        [VMEM] * (7 + len(xs)),
        [VMEM] * 2 + [ANY] * 6,
        outs,
        scratch,
        10**10,
        after,
        carry,
    )(*marked, norms, *w[:4], *xs)
    return x1, (lse, *saved), carried


def mlp_bwd(at, ids, x1, dys, norms, w, after=(), carry=()):
    scratch = [
        *[pltpu.VMEM(ROWS2, bf16)] * 4,
        *[pltpu.VMEM(ROWS2, f32)] * (len(dys) - 1),
    ]
    return call(
        functools.partial(mlp_bwd_kernel, len(dys) == 2, at),
        "mlp_bwd",
        [SMEM] + [VMEM] * (10 + len(dys)),
        [VMEM] * 4,
        shaped((ROWS2, f32), ((8, 512), f32), *[((4, 4, 32, 2048), bf16)] * 2),
        scratch,
        15 * 10**9,
        after,
        carry,
    )(ids, x1, norms, *w, *dys)


def attn_bwd(at, marked, x, dx1, norms, saved, w, after=(), carry=()):
    scratch = [pltpu.VMEM(ROWS2, f32), *[pltpu.VMEM(ROWS2, bf16)] * 14, DMA((6,))]
    outs = shaped((ROWS2, f32), ((8, 512), f32), *[((4, 4, 32, 1024), bf16)] * 2)
    return call(
        functools.partial(attn_bwd_kernel, at),
        "attn_bwd",
        [VMEM] * 9 + [ANY] * 6 + [VMEM],
        [VMEM] * 4,
        outs,
        scratch,
        15 * 10**9,
        after,
        carry,
    )(*marked, dx1, norms, saved[0], *w[:4], *map(pin, saved[1:]), x)


def heads_bwd(marked, dx1, saved, w, after=(), carry=()):
    scratch = [pltpu.VMEM(ROWS2, f32), *[pltpu.VMEM(ROWS2, bf16)] * 10, DMA((6,))]
    outs = shaped(*[(ROWS2, bf16)] * 3, *[((4, 4, 32, 256), bf16)] * 2)
    return call(
        heads_bwd_kernel,
        "heads_bwd",
        [VMEM] * 8 + [ANY] * 6,
        [VMEM] * 5,
        outs,
        scratch,
        10 * 10**9,
        after,
        carry,
    )(*marked, dx1, saved[0], *w[:4], *map(pin, saved[1:]))


def rows_bwd(ids, marked, dx1, norms, parts, other_small, d_x1, w, d_w, after=(), carry=()):
    scratch = [pltpu.VMEM((8, 512), f32), *[pltpu.VMEM(ROWS2, bf16)] * 2]
    outs = shaped(*[((256, 512), f32), ((256, 512), bf16)] * 2, *[((4, 4, 32, 1152), bf16)] * 2)
    return call(
        rows_bwd_kernel,
        "rows_bwd",
        [SMEM] + [VMEM] * 23,
        [VMEM] * 6,
        outs,
        scratch,
        10 * 10**9,
        after,
        carry,
    )(ids, *marked, dx1, norms, *parts, other_small, d_x1, *w[:4], *d_w)


def code_prep(book_t, after=(), carry=()):
    codes = book_t.shape[1]
    return call(
        code_prep_kernel,
        "code_prep",
        [VMEM],
        [VMEM] * 2,
        shaped(((codes, 256), bf16), ((128, codes), bf16)),
        [],
        6 * 10**9,
        after,
        carry,
    )(book_t)


def mlp_vq(x1, norms, vq_w, stack, stack_t, w, after=(), carry=()):
    return call(
        mlp_vq_kernel,
        "mlp_vq",
        [VMEM] * 3 + [ANY] * 2 + [VMEM] * 8,
        [VMEM] * 3 + [ANY],
        shaped((ROWS2, f32), (ROWS2, f32), ((72, 512), f32))
        + [pltpu.HBM((stack.shape[0], 512), bf16)],
        [
            pltpu.VMEM(ROWS2, bf16),
            pltpu.VMEM((128, 512), f32),
            pltpu.VMEM(stack.shape, bf16),
            pltpu.VMEM(stack_t.shape, bf16),
            pltpu.VMEM((2, 2048, 512), bf16),
            DMA((2, 4)),
            DMA((2,)),
        ],
        25 * 10**9,
        after,
        carry,
    )(x1, norms, vq_w, pin(stack), pin(stack_t), *w)


def vq_bwd(ids, e, du, norms, vq_w, codes, kept, smalls, after=(), carry=()):
    scratch = [
        pltpu.VMEM((96, 512), f32),
        pltpu.VMEM(codes[2].shape, bf16),
        pltpu.VMEM((96, 512), f32),
        pltpu.VMEM((8, 32, 512), bf16),
        *[pltpu.VMEM(a.shape, a.dtype) for a in codes],
        DMA((4, 4)),
        DMA((2, 2, 4)),
    ]
    return call(
        vq_bwd_kernel,
        "vq_bwd",
        [SMEM] + [VMEM] * 4 + [ANY] * 4 + [VMEM] * 3,
        [VMEM] + [ANY] * 2,
        shaped((ROWS2, f32), *[((4, 32, 1536), bf16)] * 2),
        scratch,
        25 * 10**9,
        after,
        carry,
    )(ids, e, du, norms, vq_w, *map(pin, codes), kept, *smalls)


def lines_kernel(cuts, *refs):
    first = 0
    for out, width in zip(refs[4:], cuts):
        for k in range(4):
            out[k] = refs[k][:, first : first + width]
        first += width


def stack_lines(shards, cuts, after=(), carry=()):
    return call(
        functools.partial(lines_kernel, cuts),
        "stack_lines",
        [VMEM] * 4,
        [VMEM] * len(cuts),
        shaped(*[((4, 32, width), bf16) for width in cuts]),
        [],
        1,
        after,
        carry,
    )(*shards)


def pack_kernel(*refs):
    hbm, outs, held, sems = refs[:4], refs[4:6], refs[6:10], refs[10]
    copies = [pltpu.make_async_copy(hbm[at], held[at], sems.at[at]) for at in range(4)]
    start_all(copies)
    wait_all(copies)
    qkv, out_t, up, down_t = held
    for layer, out in enumerate(outs):
        for index in range(3):
            out[:, index * 256 : (index + 1) * 256] = qkv[layer, index]
        out[:, 768:1024] = out_t[layer]
        out[:, 1024:2048] = up[layer]
        out[:, 2048:] = down_t[layer]


def pack_weights(*arrays):
    return call(
        pack_kernel,
        "pack_weights",
        [ANY] * 4,
        [VMEM] * 2,
        shaped(*[((32, 3072), bf16)] * 2),
        [*[pltpu.VMEM(a.shape, a.dtype) for a in arrays], DMA((4,))],
        1,
    )(*map(pin, arrays))[:-1]


def pairs_kernel(*refs):
    count = len(refs) // 3
    for at in range(count):
        refs[2 * count + at][0] = refs[2 * at][...]
        refs[2 * count + at][1] = refs[2 * at + 1][...]


def stack_pairs(pairs, after=(), carry=()):
    return call(
        pairs_kernel,
        "stack_pairs",
        [VMEM] * (2 * len(pairs)),
        [VMEM] * len(pairs),
        shaped(*[((2, *a.shape), bf16) for a, _ in pairs]),
        [],
        1,
        after,
        carry,
    )(*[array for pair in pairs for array in pair])


def gate(after, carry):
    def kernel(out):
        out[...] = jnp.zeros_like(out)

    return call(kernel, "gate", [], [VMEM], shaped(((8, 128), f32)), [], 1, after, carry)()[-1]


def rows_in_kernel(ids, *refs):
    hbm, (own, send, norms, vq_w), held, sems = refs[:7], refs[7:11], refs[11:18], refs[18]
    copies = [pltpu.make_async_copy(hbm[at], held[at], sems.at[at]) for at in range(7)]
    start_all(copies)
    matrix = order_matrix(ids[0], False)
    wait_all(copies)
    tokens, segs, cot, gains, biases, in_t, out_w = held
    for to, micro in ((send, 1 - ids[1]), (own, ids[1])):
        to[:, :512] = ordered(tokens[micro], matrix).astype(bf16)
        ids_row = segs[pl.ds(micro, 1), :].astype(f32)
        to[:, 512:640] = jnp.broadcast_to(ids_row, (128, 256)).T.astype(bf16)
    send[:, 640:] = ordered(cot[1 - ids[1]].astype(bf16), matrix).astype(bf16)
    pad = jnp.zeros((3, 512), f32)
    rows = jnp.concatenate([gains[...], pad, biases[...], pad], axis=0)
    norms[...] = ordered(rows, matrix)
    vq_w[...] = ordered(jnp.concatenate([in_t[...], out_w[...]], axis=0), matrix)


def rows_in(ids, *arrays):
    outs = shaped(
        ((256, 640), bf16), ((256, 1152), bf16), ((16, 512), f32), ((64, 512), f32)
    )
    return call(
        rows_in_kernel,
        "rows_in",
        [SMEM] + [ANY] * 7,
        [VMEM] * 4,
        outs,
        [*[pltpu.VMEM(a.shape, a.dtype) for a in arrays], DMA((7,))],
        1,
    )(ids, *map(pin, arrays))[:-1]


def joined(block):
    return block[0:16, 1024:].astype(f32) + block[16:32, 1024:].astype(f32)


def put_small(value, own, blocks):
    hi, lo = split2(value)
    own[0:16, 1024:] = hi.astype(f32) + lo.astype(f32)
    for block in blocks:
        block[0:16, 1024:] = hi
        block[16:32, 1024:] = lo


def near_kernel(ids, ins, outs):
    keep, other = ins
    for i in range(4):
        outs[i][...] = (keep[i].astype(f32) + other[i].astype(f32)).astype(outs[i].dtype)
    if keep.shape[3] == 1152:
        value = joined(keep.at[0, 0]) + joined(other.at[0, 0])
        put_small(value, outs[0].at[0], [out.at[0] for out in outs[1:]])


def near_task(keep, other):
    shape = keep.shape[1:]
    return near_kernel, [keep, other], shaped((shape, f32), *[(shape, bf16)] * 3)


def put_code(ref, first, code):
    for i in range(3):
        ref[first + i] = code[:, 1024 * i : 1024 * (i + 1)]


def get_code(ref, first):
    return jnp.concatenate([ref[first + i] for i in range(3)], axis=1)


def swapped(code):
    return jnp.concatenate([code[:, 1536:], code[:, :1536]], axis=1)


def code_sum(a, b):
    done = []
    for first in range(0, a.shape[1], 1536):
        total = a[:, first : first + 1024].astype(f32) + b[:, first : first + 1024].astype(f32)
        small = [
            x[:, first + 1024 : first + 1280].astype(f32) + x[:, first + 1280 : first + 1536].astype(f32)
            for x in (a, b)
        ]
        done += [total.astype(bf16), *split2(small[0] + small[1])]
    return jnp.concatenate(done, axis=1)


def fork_kernel(ids, ins, outs):
    keep, other = ins
    own_a, to_x, own_b, to_y = outs
    half = keep.shape[3] // 2
    for at, (own, send, kept, sent) in enumerate(
        ((own_a, to_x, (0, 2), (1, 3)), (own_b, to_y, (0, 1), (2, 3)))
    ):
        cols = slice(half * at, half * (at + 1))
        for j in range(2):
            own[j] = keep[kept[j], :, :, cols].astype(f32) + other[kept[j], :, :, cols].astype(f32)
            total = keep[sent[j], :, :, cols].astype(f32) + other[sent[j], :, :, cols].astype(f32)
            send[4 * j : 4 * (j + 1)] = total.astype(bf16)


def fork_task(keep, other):
    half = keep.shape[3] // 2
    outs = shaped(*[((2, 4, 32, half), f32), ((8, 32, half), bf16)] * 2)
    return fork_kernel, [keep, other], outs


def half_kernel(ids, ins, outs):
    own_a, from_x, own_b, from_y = ins[:4]
    kept_a, to_y, kept_b, to_x = outs[:4]
    for own, other, kept, send in (
        (own_a, from_x, kept_a, to_y),
        (own_b, from_y, kept_b, to_x),
    ):
        kept[...] = own[0] + other[0:4].astype(f32)
        send[0:4] = (own[1] + other[4:8].astype(f32)).astype(bf16)
    if len(ins) == 6:
        code, code_other = ins[4:]
        outs[4][...] = code_sum(code[...], swapped(code_other[...]))
        put_code(to_x, 4, outs[4])


def half_task(own_a, from_x, own_b, from_y, *codes):
    width = own_a.shape[3]
    outs = shaped(
        ((4, 32, width), f32),
        ((4, 32, width), bf16),
        ((4, 32, width), f32),
        ((7 if codes else 4, 32, width), bf16),
        *[(code.shape, bf16) for code in codes[:1]],
    )
    return half_kernel, [own_a, from_x, own_b, from_y, *codes], outs


def join_kernel(ids, ins, outs):
    kept, send = outs[:2]
    width = ins[0].shape[2]
    for at, (own, other) in enumerate((ins[0:2], ins[2:4])):
        cols = slice(width * at, width * (at + 1))
        for k in range(2):
            kept[k, :, cols] = own[2 * k] + other[2 * k].astype(f32)
            send[k, :, cols] = (own[2 * k + 1] + other[2 * k + 1].astype(f32)).astype(bf16)
    if len(ins) == 5:
        outs[2][...] = code_sum(ins[4][...], get_code(ins[3], 4))


def join_task(own_a, from_y, own_b, from_x, *codes):
    width = 2 * own_a.shape[2]
    outs = shaped(
        ((2, 32, width), f32),
        ((2, 32, width), bf16),
        *[(code.shape, bf16) for code in codes],
    )
    return join_kernel, [own_a, from_y, own_b, from_x, *codes], outs


def far_kernel(ids, ins, outs):
    own_a, from_y, own_b, from_x, kept_dm, other_dm = ins
    kept, own_dm, send = outs
    for at, (own, other) in enumerate(((own_a, from_y), (own_b, from_x))):
        cols = slice(512 * at, 512 * (at + 1))
        for k in range(2):
            kept[k, :, cols] = own[k] + other[k].astype(f32)
            send[2 + k, :, cols] = (own[2 + k] + other[2 + k].astype(f32)).astype(bf16)
    own_dm[...] = kept_dm[0] + other_dm[0].astype(f32)
    for i in range(2):
        cols = slice(1024 * i, 1024 * (i + 1))
        send[i] = (kept_dm[1, :, cols] + other_dm[1, :, cols].astype(f32)).astype(bf16)


def far_task(own_a, from_y, own_b, from_x, kept_dm, other_dm):
    outs = shaped(((2, 32, 1024), f32), (kept_dm.shape[1:], f32), ((4, 32, 1024), bf16))
    return far_kernel, [own_a, from_y, own_b, from_x, kept_dm, other_dm], outs


def near_step_kernel(ids, ins, outs):
    kept, other = ins
    outs[0][...] = kept[0] + other[2].astype(f32)
    outs[1][...] = (kept[1] + other[3].astype(f32)).astype(bf16)


def near_step_task(kept, other):
    shape = kept.shape[1:]
    return near_step_kernel, [kept, other], shaped((shape, f32), (shape, bf16))


def line_step_kernel(ids, ins, outs):
    kept, other = ins
    outs[0][...] = kept[0] + other[0].astype(f32)
    outs[1][...] = (kept[1] + other[1].astype(f32)).astype(bf16)


def line_step_task(kept, other):
    shape = kept.shape[1:]
    return line_step_kernel, [kept, other], shaped((shape, f32), (shape, bf16))


def plane_line_kernel(ids, ins, outs):
    kept, send = outs
    for k in range(4):
        total = ins[0][k]
        for other in ins[1:]:
            total = total + other[k].astype(f32)
        to = send if k % 2 else kept
        to[k // 2] = total.astype(to.dtype)
    x, y, xy = [joined(other.at[0]) for other in ins[1:]]
    put_small((ins[0][0, 0:16, 1024:] + x) + (y + xy), kept.at[0], [send.at[0]])


def plane_line_task(own, others):
    outs = shaped(((2, 32, 1152), f32), ((2, 32, 1152), bf16))
    return plane_line_kernel, [own, *others], outs


def small_step_kernel(ids, ins, outs):
    kept, other = ins
    line_step_kernel(ids, ins, outs)
    put_small(kept[0, 0:16, 1024:] + joined(other.at[0]), outs[0], [outs[1]])


def small_step_task(kept, other):
    shape = kept.shape[1:]
    return small_step_kernel, [kept, other], shaped((shape, f32), (shape, bf16))


def line_total(ins, width):
    total = ins[0][:, :width]
    for other in ins[1:]:
        total = total + other[:, :width].astype(f32)
    return total


def rows_out_kernel(ids, ins, outs):
    y, y_low, dx, dx_low = ins
    matrix = order_matrix(ids[0], True)
    outs[0][...] = ordered(y[...], matrix)
    outs[1][...] = ordered(dx[...], matrix)
    outs[2][0:256, :] = ordered(y_low[...], matrix).astype(bf16)
    outs[2][256:, :] = ordered(dx_low[...], matrix).astype(bf16)


def rows_out_task(y, y_low, dx, dx_low):
    outs = shaped((y.shape, f32), (dx.shape, f32), (ROWS2, bf16))
    return rows_out_kernel, [y, y_low, dx, dx_low], outs


def rows_done_kernel(ids, y, dx, others, decoded, grad_tokens, done, held, sems):
    copies = []
    done[...] = jnp.zeros_like(done)
    for at, (out, own) in enumerate(((decoded, y), (grad_tokens, dx))):
        held[at] = others[256 * at : 256 * (at + 1), :].astype(f32)
        copies.append(pltpu.make_async_copy(own, out.at[ids[1]], sems.at[at, 0]))
        copies.append(pltpu.make_async_copy(held.at[at], out.at[1 - ids[1]], sems.at[at, 1]))
    start_all(copies)
    wait_all(copies)


def rows_done(ids, y, dx, others, after):
    return call(
        rows_done_kernel,
        "rows_done",
        [SMEM] + [VMEM] * 3,
        [ANY] * 2 + [VMEM],
        [pltpu.HBM((2, 256, 512), f32)] * 2 + shaped(((8, 128), f32)),
        [pltpu.VMEM((2, 256, 512), f32), DMA((2, 2))],
        10**9,
        after,
    )(ids, y, dx, others)[:-1]


def code_near_kernel(ids, ins, outs):
    keep, other = ins
    for at, out in enumerate(outs):
        for i in range(2):
            out[:, 1536 * i : 1536 * (i + 1)] = code_sum(keep[2 * at + i], other[2 * at + i])


def code_near_task(keep, other):
    return code_near_kernel, [keep, other], shaped(*[((32, 3072), bf16)] * 2)


def code_add_kernel(ids, ins, outs):
    outs[0][...] = code_sum(ins[0][...], ins[1][...])


def code_add_task(a, b):
    return code_add_kernel, [a, b], shaped((a.shape, bf16))


def code_pair_kernel(ids, ins, outs):
    for at, part in enumerate(ins):
        outs[0][:, 3072 * at : 3072 * (at + 1)] = part[...]


def code_pair_task(a, b):
    return code_pair_kernel, [a, b], shaped(((32, 6144), bf16))


def finish_kernel(ids, ins, outs):
    mlp, attn, d_mlp, d_attn, code, code_other = ins[:2], ins[2:4], ins[4:6], ins[6:8], *ins[8:]
    qkv, out_t, up, down_t, book, vq_in, vq_out, gains, biases, dec_biases, small_ref = outs
    rows = line_total(mlp, 2048)
    up[0] = rows[:, :1024]
    down_t[0] = rows[:, 1024:]
    for i, out in enumerate((up, down_t)):
        out[1] = d_mlp[0][:, 1024 * i : 1024 * (i + 1)] + d_mlp[1][i].astype(f32)
    d_rows = line_total(d_attn, 1024)
    for layer, rows in enumerate((line_total(attn, 1024), d_rows)):
        for index in range(3):
            qkv[layer, index] = rows[:, index * 256 : (index + 1) * 256]
        out_t[layer] = rows[:, 768:]
    core, z = ids[0] % 2, ids[0] // 4
    for at, parts in ((core, code), (1 - core, code_other)):
        for k in range(4):
            part = at * 4 + (z ^ k)
            held = parts[:, 1536 * k : 1536 * (k + 1)].astype(f32)
            book[:, pl.ds(pl.multiple_of(part * 1024, 1024), 1024)] = held[:, :1024]
            small_ref[:, pl.ds(pl.multiple_of(part * 256, 256), 256)] = (
                held[:, 1024:1280] + held[:, 1280:1536]
            )
    small = small_ref[...]
    vq_in[...] = small[:, :512]
    vq_out[...] = small[:, 512:1024]
    rest = small[:, 1024:1536]
    packed = attn[0][0:16, 1024:] + joined(attn[1])
    for row, out in enumerate((gains.at[0:1], biases.at[0:1], gains.at[1:2], biases.at[1:2])):
        for j in range(4):
            out[:, 128 * j : 128 * (j + 1)] = packed[row * 4 + j : row * 4 + j + 1, :]
    gains[2:3, :] = rest[0:1, :]
    biases[2:3, :] = rest[1:2, :]
    gains[3:4, :] = rest[2:3, :]
    dec_biases[0:1, :] = rest[3:4, :]
    gains[4:5, :] = rest[4:5, :]
    dec_biases[1:2, :] = rest[5:6, :]


def finish_task(mlp, attn, d_mlp, d_attn, code, code_other):
    outs = shaped(
        ((2, 3, 32, 256), f32),
        ((2, 32, 256), f32),
        ((2, 32, 1024), f32),
        ((2, 32, 1024), f32),
        ((32, 8192), f32),
        ((32, 512), f32),
        ((32, 512), f32),
        ((5, 512), f32),
        ((3, 512), f32),
        ((2, 512), f32),
        ((32, 2048), f32),
    )
    ins = [*mlp, *attn, *d_mlp, *d_attn, code, code_other]
    return finish_kernel, ins, outs


def run_tasks(ids, name, tasks, after=(), carry=()):
    sizes = [(len(ins), len(outs)) for _, ins, outs in tasks]
    n_in = sum(i for i, _ in sizes)

    def kernel(ids_ref, *refs):
        at_in, at_out = 0, n_in
        for (fn, _, _), (i, o) in zip(tasks, sizes):
            fn(ids_ref, refs[at_in : at_in + i], refs[at_out : at_out + o])
            at_in, at_out = at_in + i, at_out + o

    outs = [one for _, _, many in tasks for one in many]
    res = call(
        kernel, name, [SMEM] + [VMEM] * n_in, [VMEM] * len(outs), outs, [], 10**9, after, carry
    )(ids, *[one for _, many, _ in tasks for one in many])
    split, at = [], 0
    for _, o in sizes:
        split.append(res[at : at + o])
        at += o
    return (*split, res[-1])


def whole_groups(
    n_dp,
    tokens,
    segment_ids,
    norm_gains,
    norm_biases,
    w_qkv,
    w_attn_out,
    w_up,
    w_down,
    w_vq_in,
    w_vq_out,
    codebook,
    cotangent,
):
    dp_at, tp_at = lax.axis_index("dp"), lax.axis_index("tp")
    ids = jnp.stack([dp_at, tp_at]).astype(jnp.int32)

    def swap(values):
        return exchange(values, 0, 1, n_dp)

    def core(values):
        return [values, exchange(values, 1, 0, n_dp)]

    book_t = codebook.T
    enc_shard, dec_shard = pack_weights(
        w_qkv, w_attn_out.transpose(0, 2, 1), w_up, w_down.transpose(0, 2, 1)
    )
    enc_shards = spread_line(enc_shard, n_dp)
    own, send, norms, vq_w = rows_in(
        ids,
        tokens,
        segment_ids,
        cotangent,
        norm_gains,
        norm_biases,
        w_vq_in.T,
        w_vq_out,
    )
    marked = [own, swap(send)]

    line_a, line_b, (dec_shard,) = stack_lines(enc_shards, [1536] * 2, carry=[dec_shard])
    along_x, along_y = exchange(line_a, 0, 1, n_dp), exchange(line_b, 2, 0, n_dp)
    dec_shards = spread_line(dec_shard, n_dp)
    stack, stack_t, _ = code_prep(book_t, [line_a])
    codes = (stack, stack_t, book_t)
    a_0, b_0, _ = stack_pairs([(line_a, along_x), (line_b, along_y)], [stack_t, marked[1]])
    a_1, b_1 = exchange(a_0, 2, 0, n_dp), exchange(b_0, 0, 1, n_dp)
    line_a, line_b, (a_0, b_0) = stack_lines(dec_shards, [1536] * 2, [a_1, b_1], [a_0, b_0])
    enc_w = [a_0, a_1, exchange(a_0, 1, 0, n_dp), exchange(a_1, 1, 0, n_dp)]
    enc_w += [b_0, b_1, exchange(b_0, 1, 0, n_dp), exchange(b_1, 1, 0, n_dp)]
    along_x, along_y = exchange(line_a, 0, 1, n_dp), exchange(line_b, 2, 0, n_dp)
    e_x1, e_saved, _ = attn_fwd(0, marked, [], norms, enc_w)
    a_0, b_0, _ = stack_pairs([(line_a, along_x), (line_b, along_y)], [e_x1])
    a_1, b_1 = exchange(a_0, 2, 0, n_dp), exchange(b_0, 0, 1, n_dp)
    dec_w = [a_0, exchange(a_0, 1, 0, n_dp), b_0, exchange(b_0, 1, 0, n_dp)]
    e, u, kept, numer, _ = mlp_vq(e_x1, norms, vq_w, stack, stack_t, enc_w, [a_0, b_0])
    a_1, b_1 = gate([u], [a_1, b_1])
    a_1, b_1 = core(a_1), core(b_1)
    dec_w = [dec_w[0], a_1[0], dec_w[1], a_1[1], dec_w[2], b_1[0], dec_w[3], b_1[1]]
    d_x1, d_saved, _ = attn_fwd(3, marked, [u], norms, dec_w)

    dx1, d_small1, keep_m, send_m, _ = mlp_bwd(
        4, ids, d_x1, [cotangent, marked[1]], norms, dec_w
    )
    near_m = exchange(send_m, 1, 0, n_dp)
    du, d_small0, keep_a, send_a, (keep_m,) = attn_bwd(
        3, marked, u, dx1, norms, d_saved, dec_w, carry=[keep_m]
    )
    (m_a, to_x, m_b, to_y), (send_a,) = run_tasks(
        ids, "sums1", [fork_task(keep_m, near_m)], carry=[send_a]
    )
    from_x, from_y = exchange(to_x, 0, 1, n_dp), exchange(to_y, 2, 0, n_dp)
    near_a = exchange(send_a, 1, 0, n_dp)
    de, code, code_send, (m_a, m_b, keep_a) = vq_bwd(
        ids,
        e,
        du,
        norms,
        vq_w,
        [*codes, numer],
        kept,
        [d_small0, d_small1],
        [to_x, to_y],
        [m_a, m_b, keep_a],
    )
    (m_a, m_y, m_b, m_x), (a_a, to_x, a_b, to_y), (code, code_send) = run_tasks(
        ids,
        "sums2",
        [half_task(m_a, from_x, m_b, from_y), fork_task(keep_a, near_a)],
        carry=[code, code_send],
    )
    code_other = exchange(code_send, 1, 0, n_dp)
    from_m_y, from_m_x = exchange(m_y, 2, 0, n_dp), exchange(m_x, 0, 1, n_dp)
    from_x, from_y = exchange(to_x, 0, 1, n_dp), exchange(to_y, 2, 0, n_dp)
    (code, code_send), _ = run_tasks(ids, "sums2b", [code_near_task(code, code_other)])
    code_other = exchange(code_send, 8, 0, n_dp)
    ex1, e_small1, keep_m, send_m, (m_a, m_b, a_a, a_b, code) = mlp_bwd(
        1,
        ids,
        e_x1,
        [de],
        norms,
        enc_w,
        [m_y, m_x, to_x, to_y, code_send],
        [m_a, m_b, a_a, a_b, code],
    )
    (own_dm, send_dm), (a_a, to_y, a_b, to_x), (code,), (keep_m, send_m) = run_tasks(
        ids,
        "sums3",
        [
            join_task(m_a, from_m_y, m_b, from_m_x),
            half_task(a_a, from_x, a_b, from_y),
            code_add_task(code, code_other),
        ],
        carry=[keep_m, send_m],
    )
    near_m, code_other = exchange(send_m, 1, 0, n_dp), exchange(code, 2, 0, n_dp)
    from_y, from_x = exchange(to_y, 2, 0, n_dp), exchange(to_x, 0, 1, n_dp)
    other_dm = exchange(send_dm, 4, 0, n_dp)
    *parts, (a_a, a_b, own_dm) = heads_bwd(
        marked, ex1, e_saved, enc_w, [to_x, to_y, send_dm, code], [a_a, a_b, own_dm]
    )
    (m_a, to_x, m_b, to_y), (code,), (own_da, own_dm, send_d), _ = run_tasks(
        ids,
        "sums3b",
        [
            fork_task(keep_m, near_m),
            code_add_task(code, code_other),
            far_task(a_a, from_y, a_b, from_x, own_dm, other_dm),
        ],
        [parts[0]],
    )
    other_d, code_other = exchange(send_d, 8, 0, n_dp), exchange(code, 4, 0, n_dp)
    from_y, from_x = exchange(to_y, 2, 0, n_dp), exchange(to_x, 0, 1, n_dp)
    dx, dx_low, y, y_low, keep_a, send_a, (m_a, m_b, own_dm, own_da) = rows_bwd(
        ids,
        marked,
        ex1,
        norms,
        parts,
        e_small1,
        d_x1,
        enc_w,
        dec_w,
        [to_x, to_y, send_d, code],
        [m_a, m_b, own_dm, own_da],
    )
    (m_a, to_y, m_b, to_x, code), (own_da, send_da), (keep_a, send_a) = run_tasks(
        ids,
        "sums4",
        [
            half_task(m_a, from_x, m_b, from_y, code, code_other),
            near_step_task(own_da, other_d),
        ],
        carry=[keep_a, send_a],
    )
    near_a = exchange(send_a, 1, 0, n_dp)
    from_y, from_x = exchange(to_y, 2, 0, n_dp), exchange(to_x, 0, 1, n_dp)
    other_da = exchange(send_da, 4, 0, n_dp)
    (own_a, *lows_a), (m_a, m_b, code) = run_tasks(
        ids, "sums4b", [near_task(keep_a, near_a)], carry=[m_a, m_b, code]
    )
    plane_a = plane_send(lows_a, n_dp)
    (own_m, send_m, code), (own_a,) = run_tasks(
        ids,
        "sums5",
        [join_task(m_a, from_y, m_b, from_x, code)],
        lows_a,
        [own_a],
    )
    other_m, code_other = exchange(send_m, 4, 0, n_dp), exchange(code, 8, 0, n_dp)
    (y, dx, rows), (own_a,) = run_tasks(
        ids, "rows_out", [rows_out_task(y, y_low, dx, dx_low)], [send_m, code], [own_a]
    )
    (own_a, send_a), (own_m, send_m), (code,), (rows,) = run_tasks(
        ids,
        "sums6",
        [
            plane_line_task(own_a, plane_a),
            line_step_task(own_m, other_m),
            code_pair_task(code, code_other),
        ],
        carry=[rows],
    )
    other_a, other_m = exchange(send_a, 4, 0, n_dp), exchange(send_m, 8, 0, n_dp)
    code_other, rows = exchange(code, 1, 0, n_dp), swap(rows)
    (own_a, send_a), _ = run_tasks(ids, "sums7", [small_step_task(own_a, other_a)])
    other_a = exchange(send_a, 8, 0, n_dp)
    decoded, grad_tokens, done = rows_done(ids, y, dx, rows, [send_a])
    (qkv, out_t, up, down_t, book, vq_in, vq_out, *norm_grads, _), _ = run_tasks(
        ids,
        "finish",
        [
            finish_task(
                (own_m, other_m),
                (own_a, other_a),
                (own_dm, other_d),
                (own_da, other_da),
                code,
                code_other,
            )
        ],
        [done],
    )
    return (
        decoded,
        grad_tokens,
        *norm_grads,
        qkv,
        out_t.transpose(0, 2, 1),
        up,
        down_t.transpose(0, 2, 1),
        vq_in.T,
        vq_out,
        book.T,
    )


def layer_norm(values, norm_gain, norm_bias):
    centred = values - jnp.mean(values, axis=-1, keepdims=True)
    spread = jnp.mean(centred * centred, axis=-1, keepdims=True)
    return centred * lax.rsqrt(spread + ln_eps) * norm_gain + norm_bias


def gelu_tanh(values):
    return (
        0.5 * values * (1.0 + jnp.tanh(gelu_coef * (values + 0.044715 * values * values * values)))
    )


def matmul(former, latter):
    return jnp.dot(former, latter, precision=highest, preferred_element_type=jnp.float32)


def normalize(values):
    return values * lax.rsqrt(jnp.sum(values * values, axis=-1, keepdims=True) + norm_eps)


def quantize(in_rows, norm_gain, norm_bias, in_w, out_w, code_w):
    latent = normalize(matmul(layer_norm(in_rows, norm_gain, norm_bias), in_w))
    code_rows = normalize(code_w)
    logits = matmul(latent, code_rows.T) * temper
    row_max = jnp.max(logits, axis=-1, keepdims=True)
    numerator = jnp.exp(logits - row_max)
    assign = numerator / jnp.sum(numerator, axis=-1, keepdims=True)
    soft_code = matmul(assign, code_rows)
    offset = latent - soft_code
    vq_loss = commit_weight * 1.25 * jnp.sum(offset * offset)
    return (matmul(soft_code, out_w), vq_loss)


def product(former, latter):
    return jnp.dot(former, latter, preferred_element_type=jnp.float32)


def product_tn(former, latter):
    return lax.dot_general(
        former, latter, (((0,), (0,)), ((), ())), preferred_element_type=jnp.float32
    )


def product_nt(former, latter):
    return lax.dot_general(
        former, latter, (((1,), (1,)), ((), ())), preferred_element_type=jnp.float32
    )


def split_heads(values):
    return values.reshape(values.shape[0], values.shape[1] // HEAD_DIM, HEAD_DIM).transpose(1, 0, 2)


def join_heads(values):
    return values.transpose(1, 0, 2).reshape(values.shape[1], values.shape[0] * HEAD_DIM)


def masked_scores(query_blk, key_h, seg_blk, seg_keys):
    scores = jnp.einsum(
        "hqd,hkd->hqk", query_blk, key_h, preferred_element_type=jnp.float32
    ) * HEAD_DIM ** (-0.5)
    return jnp.where((seg_blk[:, None] == seg_keys[None, :])[None], scores, masked_score)


def attend(query_h, key_h, value_h, seg_keys):
    block_rows = min(512, query_h.shape[1])
    block_count = query_h.shape[1] // block_rows

    def one_block(begin_row):
        query_blk = lax.dynamic_slice_in_dim(query_h, begin_row, block_rows, 1)
        seg_blk = lax.dynamic_slice_in_dim(seg_keys, begin_row, block_rows, 0)
        scores = masked_scores(query_blk, key_h, seg_blk, seg_keys)
        row_max = jnp.max(scores, axis=-1, keepdims=True)
        numerator = jnp.exp(scores - row_max)
        row_total = jnp.sum(numerator, axis=-1, keepdims=True)
        prob_low = (numerator / row_total).astype(jnp.bfloat16)
        attended = jnp.einsum("hqk,hkd->hqd", prob_low, value_h, preferred_element_type=jnp.float32)
        return (attended.astype(jnp.bfloat16), (row_max + jnp.log(row_total))[..., 0])

    starts = jnp.arange(block_count, dtype=jnp.int32) * block_rows
    attended, log_sums = lax.map(one_block, starts)
    heads_out = attended.transpose(1, 0, 2, 3).reshape(query_h.shape)
    log_sums = log_sums.transpose(1, 0, 2).reshape(query_h.shape[0], query_h.shape[1])
    return (heads_out, log_sums)


def attend_back(query_h, key_h, value_h, seg_keys, log_sums, grad_out):
    block_rows = min(512, query_h.shape[1])
    block_count = query_h.shape[1] // block_rows

    def one_block(carry, begin_row):
        grad_key, grad_value = carry
        query_blk = lax.dynamic_slice_in_dim(query_h, begin_row, block_rows, 1)
        grad_blk = lax.dynamic_slice_in_dim(grad_out, begin_row, block_rows, 1)
        lse_blk = lax.dynamic_slice_in_dim(log_sums, begin_row, block_rows, 1)
        seg_blk = lax.dynamic_slice_in_dim(seg_keys, begin_row, block_rows, 0)
        scores = masked_scores(query_blk, key_h, seg_blk, seg_keys)
        probs = jnp.exp(scores - lse_blk[..., None])
        prob_low = probs.astype(jnp.bfloat16)
        grad_value = grad_value + jnp.einsum(
            "hqk,hqd->hkd", prob_low, grad_blk, preferred_element_type=jnp.float32
        )
        grad_prob = jnp.einsum(
            "hqd,hkd->hqk", grad_blk, value_h, preferred_element_type=jnp.float32
        )
        row_dot = jnp.sum(probs * grad_prob, axis=-1, keepdims=True)
        grad_score = (probs * (grad_prob - row_dot) * HEAD_DIM ** (-0.5)).astype(jnp.bfloat16)
        grad_query = jnp.einsum(
            "hqk,hkd->hqd", grad_score, key_h, preferred_element_type=jnp.float32
        )
        grad_key = grad_key + jnp.einsum(
            "hqk,hqd->hkd", grad_score, query_blk, preferred_element_type=jnp.float32
        )
        return ((grad_key, grad_value), grad_query)

    starts = jnp.arange(block_count, dtype=jnp.int32) * block_rows
    zeros_kv = jnp.zeros(key_h.shape, jnp.float32)
    (grad_key, grad_value), grad_query = lax.scan(one_block, (zeros_kv, zeros_kv), starts)
    grad_query = grad_query.transpose(1, 0, 2, 3).reshape(query_h.shape)
    return (
        grad_query.astype(jnp.bfloat16),
        grad_key.astype(jnp.bfloat16),
        grad_value.astype(jnp.bfloat16),
    )


def spread_rows(values):
    return lax.all_gather(values, "tp", axis=0, tiled=True)


def combine_rows(partial_value):
    return lax.psum_scatter(partial_value, "tp", scatter_dimension=0, tiled=True)


def spread_grads(values):
    return lax.all_gather(values, "tp", axis=0, tiled=True)


def combine_grads(partial_value):
    return lax.psum_scatter(
        partial_value.astype(jnp.bfloat16), "tp", scatter_dimension=0, tiled=True
    ).astype(jnp.float32)


def fetch_weights(w_qkv, w_attn_out, w_up, w_down, layer):
    return (
        lax.all_gather(w_qkv[layer], "dp", axis=1, tiled=True),
        lax.all_gather(w_attn_out[layer], "dp", axis=1, tiled=True),
        lax.all_gather(w_up[layer], "dp", axis=0, tiled=True),
        lax.all_gather(w_down[layer], "dp", axis=1, tiled=True),
    )


def reduce_weight_grads(grads):
    return (
        lax.psum_scatter(
            grads[0].astype(jnp.bfloat16), "dp", scatter_dimension=1, tiled=True
        ).astype(jnp.float32),
        lax.psum_scatter(
            grads[1].astype(jnp.bfloat16), "dp", scatter_dimension=1, tiled=True
        ).astype(jnp.float32),
        lax.psum_scatter(
            grads[2].astype(jnp.bfloat16), "dp", scatter_dimension=0, tiled=True
        ).astype(jnp.float32),
        lax.psum_scatter(
            grads[3].astype(jnp.bfloat16), "dp", scatter_dimension=1, tiled=True
        ).astype(jnp.float32),
    )


def block_forward(resid_in, seg_local, gains, biases, weights):
    qkv_w, attn_w, up_w, down_w = weights
    normed = layer_norm(resid_in, gains[0], biases[0]).astype(jnp.bfloat16)
    normed_all, seg_all = (
        lax.all_gather(normed, "tp", axis=0, tiled=True),
        lax.all_gather(seg_local, "tp", axis=0, tiled=True),
    )
    query_h = split_heads(product(normed_all, qkv_w[0]).astype(jnp.bfloat16))
    key_h = split_heads(product(normed_all, qkv_w[1]).astype(jnp.bfloat16))
    value_h = split_heads(product(normed_all, qkv_w[2]).astype(jnp.bfloat16))
    heads_out, log_sums = attend(query_h, key_h, value_h, seg_all)
    attn_rows = join_heads(heads_out)
    middle = resid_in + combine_rows(product(attn_rows, attn_w))
    normed_mid = spread_rows(layer_norm(middle, gains[1], biases[1]).astype(jnp.bfloat16))
    hidden_pre = product(normed_mid, up_w)
    hidden = gelu_tanh(hidden_pre).astype(jnp.bfloat16)
    result = middle + combine_rows(product(hidden, down_w))
    kept = (
        resid_in,
        middle,
        normed_all,
        seg_all,
        query_h,
        key_h,
        value_h,
        log_sums,
        attn_rows,
        normed_mid,
        hidden_pre,
        hidden,
    )
    return (result, kept)


def block_backward(kept, gains, biases, weights, grad_result):
    (
        resid_in,
        middle,
        normed_all,
        seg_all,
        query_h,
        key_h,
        value_h,
        log_sums,
        attn_rows,
        normed_mid,
        hidden_pre,
        hidden,
    ) = kept
    qkv_w, attn_w, up_w, down_w = weights
    grad_branch = spread_grads(grad_result.astype(jnp.bfloat16))
    grad_down = product_tn(hidden, grad_branch)
    grad_hidden = product_nt(grad_branch, down_w)
    _, gelu_back = jax.vjp(gelu_tanh, hidden_pre)
    grad_pre = gelu_back(grad_hidden)[0].astype(jnp.bfloat16)
    grad_up = product_tn(normed_mid, grad_pre)
    grad_norm_mid = combine_grads(product_nt(grad_pre, up_w))
    _, norm_back_mid = jax.vjp(layer_norm, middle, gains[1], biases[1])
    grad_mid_ln, grad_gain_mid, grad_bias_mid = norm_back_mid(grad_norm_mid)
    grad_middle = grad_result + grad_mid_ln
    grad_attn_all = spread_grads(grad_middle.astype(jnp.bfloat16))
    grad_attn = product_tn(attn_rows, grad_attn_all)
    grad_heads = split_heads(product_nt(grad_attn_all, attn_w).astype(jnp.bfloat16))
    grad_query, grad_key, grad_value = attend_back(
        query_h, key_h, value_h, seg_all, log_sums, grad_heads
    )
    grad_parts = [join_heads(grad_query), join_heads(grad_key), join_heads(grad_value)]
    grad_qkv = jnp.stack([product_tn(normed_all, grad_part) for grad_part in grad_parts])
    grad_normed_part = (
        product_nt(grad_parts[0], qkv_w[0])
        + product_nt(grad_parts[1], qkv_w[1])
        + product_nt(grad_parts[2], qkv_w[2])
    )
    grad_normed = combine_grads(grad_normed_part)
    _, norm_back_in = jax.vjp(layer_norm, resid_in, gains[0], biases[0])
    grad_in_ln, grad_gain_in, grad_bias_in = norm_back_in(grad_normed)
    gain_grads = jnp.stack([grad_gain_in, grad_gain_mid])
    bias_grads = jnp.stack([grad_bias_in, grad_bias_mid])
    return (
        grad_middle + grad_in_ln,
        gain_grads,
        bias_grads,
        (grad_qkv, grad_attn, grad_up, grad_down),
    )


def local(
    tokens,
    segment_ids,
    norm_gains,
    norm_biases,
    w_qkv,
    w_attn_out,
    w_up,
    w_down,
    w_vq_in,
    w_vq_out,
    codebook,
    cotangent,
):
    gain_sum = jnp.zeros(norm_gains.shape, jnp.float32)
    bias_sum = jnp.zeros(norm_biases.shape, jnp.float32)
    vq_in_sum = jnp.zeros(w_vq_in.shape, jnp.float32)
    vq_out_sum = jnp.zeros(w_vq_out.shape, jnp.float32)
    code_sum = jnp.zeros(codebook.shape, jnp.float32)
    layer_sums = [None, None]
    outputs = []
    input_grads = []
    for micro in range(MICRO):
        resid_in = tokens[micro].astype(jnp.float32)
        seg_local = segment_ids[micro]
        enc_weights = fetch_weights(w_qkv, w_attn_out, w_up, w_down, 0)
        encoded, enc_kept = block_forward(
            resid_in, seg_local, norm_gains[0:2], norm_biases[0:2], enc_weights
        )
        (decoder_in, _), vq_back = jax.vjp(
            quantize, encoded, norm_gains[2], norm_biases[2], w_vq_in, w_vq_out, codebook
        )
        dec_weights = fetch_weights(w_qkv, w_attn_out, w_up, w_down, 1)
        decoded, dec_kept = block_forward(
            decoder_in, seg_local, norm_gains[3:5], norm_biases[3:5], dec_weights
        )
        outputs.append(decoded)
        grad_dec_in, gains_dec, biases_dec, grads_dec = block_backward(
            dec_kept, norm_gains[3:5], norm_biases[3:5], dec_weights, cotangent[micro]
        )
        grad_encoded, grad_gain_vq, grad_bias_vq, grad_in_w, grad_out_w, grad_codes = vq_back(
            (grad_dec_in, jnp.ones((), jnp.float32))
        )
        grad_input, gains_enc, biases_enc, grads_enc = block_backward(
            enc_kept, norm_gains[0:2], norm_biases[0:2], enc_weights, grad_encoded
        )
        input_grads.append(grad_input)
        gain_sum = gain_sum + jnp.concatenate([gains_enc, grad_gain_vq[None], gains_dec], axis=0)
        bias_sum = bias_sum + jnp.concatenate([biases_enc, grad_bias_vq[None], biases_dec], axis=0)
        vq_in_sum = vq_in_sum + grad_in_w
        vq_out_sum = vq_out_sum + grad_out_w
        code_sum = code_sum + grad_codes
        for layer, grads in ((0, grads_enc), (1, grads_dec)):
            reduced = reduce_weight_grads(grads)
            if layer_sums[layer] is None:
                layer_sums[layer] = reduced
            else:
                layer_sums[layer] = jax.tree.map(jnp.add, layer_sums[layer], reduced)
    gain_tot, bias_tot, vq_in_tot, vq_out_tot, code_tot = lax.psum(
        (gain_sum, bias_sum, vq_in_sum, vq_out_sum, code_sum), ("dp", "tp")
    )
    return (
        jnp.stack(outputs),
        jnp.stack(input_grads),
        gain_tot,
        bias_tot[0:3],
        bias_tot[3:5],
        jnp.stack([layer_sums[0][0], layer_sums[1][0]]),
        jnp.stack([layer_sums[0][1], layer_sums[1][1]]),
        jnp.stack([layer_sums[0][2], layer_sums[1][2]]),
        jnp.stack([layer_sums[0][3], layer_sums[1][3]]),
        vq_in_tot,
        vq_out_tot,
        code_tot,
    )


def solution(mesh):
    n_dp, n_tp = mesh.shape["dp"], mesh.shape["tp"]
    fits = n_tp == MICRO and n_dp == 16
    return jax.shard_map(
        functools.partial(whole_groups, n_dp) if fits else local,
        mesh=mesh,
        in_specs=(
            P(None, ("dp", "tp"), None),
            P(None, ("dp", "tp")),
            P(),
            P(),
            P(None, None, "dp", "tp"),
            P(None, "tp", "dp"),
            P(None, "dp", "tp"),
            P(None, "tp", "dp"),
            P(),
            P(),
            P(),
            P(None, ("dp", "tp"), None),
        ),
        out_specs=(
            P(None, ("dp", "tp"), None),
            P(None, ("dp", "tp"), None),
            P(),
            P(),
            P(),
            P(None, None, "dp", "tp"),
            P(None, "tp", "dp"),
            P(None, "dp", "tp"),
            P(None, "tp", "dp"),
            P(),
            P(),
            P(),
        ),
        check_vma=False,
    )
```

```python
import functools

import jax
import jax.numpy as jnp
from jax import lax
from jax.experimental import pallas as pl
from jax.experimental.pallas import tpu as pltpu
from jax.sharding import PartitionSpec as P

HEAD_DIM = 64
MICRO = 2
bf16 = jnp.bfloat16
f32 = jnp.float32
highest = lax.Precision.HIGHEST
ln_eps = 1e-05
norm_eps = 1e-06
temper = 10.0
commit_weight = 64.0
gelu_coef = 0.7978845608028654
masked_score = -1e30
log2e = 1.4426950408889634
vmem_cap = 26 * 1024 * 1024


PLANE = ((0, 0), (0, 1), (1, 0), (1, 1))


def exchange(values, dp_xor, tp_xor, n_dp):
    pairs = [
        (d * 2 + t, (d ^ dp_xor) * 2 + (t ^ tp_xor)) for d in range(n_dp) for t in range(2)
    ]
    return lax.ppermute(values, ("dp", "tp"), pairs)


def spread_line(shard, n_dp):
    return [shard] + [exchange(shard, 4 * k, 0, n_dp) for k in range(1, 4)]


def plane_send(lows, n_dp):
    return [exchange(low, 2 * y, x, n_dp) for (y, x), low in zip(PLANE[1:], lows)]


def line_send(lows, n_dp):
    return [exchange(low, 4 * k, 0, n_dp) for k, low in zip(range(1, 4), lows)]


def dot(a, b):
    return jnp.dot(a, b, preferred_element_type=f32)


def dot_nt(a, b, precision=None):
    return lax.dot_general(
        a, b, (((1,), (1,)), ((), ())), preferred_element_type=f32, precision=precision
    )


def dot_full(a, b):
    return jnp.dot(a, b, preferred_element_type=f32, precision=highest)


def ln_parts(x):
    centred = x - jnp.mean(x, axis=-1, keepdims=True)
    inv = lax.rsqrt(jnp.mean(centred * centred, axis=-1, keepdims=True) + ln_eps)
    return centred * inv, inv


def ln_back(grad, xhat, inv, gain):
    scaled = grad * gain
    return inv * (
        scaled
        - jnp.mean(scaled, axis=-1, keepdims=True)
        - xhat * jnp.mean(scaled * xhat, axis=-1, keepdims=True)
    )


def split2(x):
    hi = x.astype(bf16)
    return hi, (x - hi.astype(f32)).astype(bf16)


def split3(x):
    hi, _ = split2(x)
    rest = x - hi.astype(f32)
    mid = rest.astype(bf16)
    return hi, mid, (rest - mid.astype(f32)).astype(bf16)


def order_matrix(dp, inverse):
    at = lax.broadcasted_iota(jnp.int32, (512, 512), 0 if inverse else 1)
    other = lax.broadcasted_iota(jnp.int32, (512, 512), 1 if inverse else 0)
    block = at >> 5
    bits = ((block & 3) << 2) | (((block >> 2) & 1) << 1) | (block >> 3)
    return jnp.where(other == (((dp ^ bits) << 5) | (at & 31)), 1.0, 0.0).astype(bf16)


def ordered(x, matrix):
    if x.dtype == bf16:
        return dot(x, matrix)
    hi, mid, lo = split3(x)
    return (dot(hi, matrix) + dot(mid, matrix)) + dot(lo, matrix)


def w_at(a, b, t, first, width):
    parts = []
    for core in range(2):
        for y in range(2):
            if first < 1536:
                part = a[2 * core + y][t, :, :, first : first + width]
            else:
                part = b[2 * core + t][y, :, :, first - 1536 : first - 1536 + width]
            parts.append(part.reshape(128, width))
    return jnp.concatenate(parts, axis=0)


def put_grad(refs, t, cols, value):
    for core, ref in enumerate(refs):
        for y in range(2):
            rows = value[core * 256 + y * 128 : core * 256 + (y + 1) * 128]
            ref[2 * y + t, :, :, cols] = rows.reshape(4, 32, rows.shape[1])


def start_all(copies):
    for copy in copies:
        copy.start()


def wait_all(copies):
    for copy in copies:
        copy.wait()


def head_rows(ref, pair, which):
    own = ref[pl.ds(pair * 128 + which * HEAD_DIM, HEAD_DIM), :]
    zero = jnp.zeros_like(own)
    return jnp.concatenate([own, zero] if which == 0 else [zero, own], axis=0)


def segment_mask(own, other):
    ids = jnp.concatenate([own[:, 512:640], other[:, 512:640]], axis=0).astype(f32)
    return jnp.where(ids[:, 0:1] == ids.T[0:1, :], 0.0, masked_score)


def load_rows(x, own, other):
    if x is None:
        return jnp.concatenate([own[:, :512], other[:, :512]], axis=0).astype(f32)
    return x[...]


def gain_of(norms, at):
    return norms[at : at + 1, :]


def bias_of(norms, at):
    return norms[8 + at : 9 + at, :]


def attn_fwd_kernel(with_x, at, own, other, norms, *refs):
    w, refs = refs[:4], refs[4:]
    x, refs = (refs[0], refs[1:]) if with_x else (None, refs)
    x1, lse, saved, refs = refs[0], refs[1], refs[2:8], refs[8:]
    h, vt, ot, mask, qs, k, v, o, qst, kt, out_sems = refs
    keeps = [
        pltpu.make_async_copy(held, to, out_sems.at[i])
        for i, (held, to) in enumerate(zip((qs, k, v, o, qst, kt), saved))
    ]
    xf = load_rows(x, own, other)
    h[...] = (ln_parts(xf)[0] * gain_of(norms, at) + bias_of(norms, at)).astype(bf16)
    mask[...] = segment_mask(own, other)
    for t in range(2):
        cols = slice(t * 256, (t + 1) * 256)
        q = dot(h[...], w_at(w, None, t, 0, 256)).astype(bf16)
        qs[:, cols] = (q * HEAD_DIM ** (-0.5)).astype(bf16)
        k[:, cols] = dot(h[...], w_at(w, None, t, 256, 256)).astype(bf16)
        v[:, cols] = dot(h[...], w_at(w, None, t, 512, 256)).astype(bf16)
    qst[...] = qs[...].T
    kt[...] = k[...].T
    vt[...] = v[...].T
    for i in (0, 1, 2, 4, 5):
        keeps[i].start()
    for pair in range(4):
        k_pair = k[:, pair * 128 : (pair + 1) * 128]
        for which in range(2):
            scores = dot(k_pair, head_rows(qst, pair, which)) + mask[...]
            top = jnp.max(scores, axis=0, keepdims=True)
            numer = jnp.exp(scores - top).astype(bf16)
            rows = pl.ds(pair * 128 + which * HEAD_DIM, HEAD_DIM)
            left = jnp.concatenate([vt[rows, :], jnp.ones((16, 512), bf16)], axis=0)
            both = dot(left, numer)
            total = both[HEAD_DIM : HEAD_DIM + 1, :]
            ot[rows, :] = (both[:HEAD_DIM, :] / total).astype(bf16)
            lse[pl.ds(pair * 2 + which, 1), :] = top + jnp.log(total)
    o[...] = ot[...].T
    keeps[3].start()
    x1[...] = xf + dot_nt(
        o[...], jnp.concatenate([w_at(w, None, t, 768, 256) for t in range(2)], axis=1)
    )
    wait_all(keeps)


def gelu_parts(u):
    square = u * u
    tanh = jnp.tanh(gelu_coef * u * (1.0 + 0.044715 * square))
    return 0.5 * u * (1.0 + tanh), tanh, square


def mlp_weights(w):
    def up(t, part):
        return w_at(w[:4], w[4:], t, 1024 + part * 512, 512)

    def down(t, part):
        return w_at(w[:4], w[4:], t, 2048 + part * 512, 512)

    return up, down


def mlp_rows(at, x, norms, w, h2):
    up, down = mlp_weights(w)
    h2[...] = (ln_parts(x)[0] * gain_of(norms, at) + bias_of(norms, at)).astype(bf16)
    places = [(t, part) for t in range(2) for part in range(2)]
    hidden = [gelu_parts(dot(h2[...], up(*place)))[0].astype(bf16) for place in places]
    return x + dot_nt(
        jnp.concatenate(hidden, axis=1),
        jnp.concatenate([down(*place) for place in places], axis=1),
    )


def mlp_bwd_kernel(split, at, ids, x1, norms, *refs):
    up, down = mlp_weights(refs[:8])
    refs = refs[8:]
    if split:
        own, other, refs = refs[0], refs[1], refs[2:]
    else:
        dy, refs = refs[0], refs[1:]
    dx1, small, grads = refs[0], refs[1], refs[2:4]
    h2, h2t, dyb, dybt = refs[4:8]
    if split:
        dy = refs[8]
        dy[0:256, :] = own[...]
        dy[256:, :] = other[:, 640:].astype(f32)
    h2[...] = (ln_parts(x1[...])[0] * gain_of(norms, at) + bias_of(norms, at)).astype(bf16)
    h2t[...] = h2[...].T
    dyb[...] = dy[...].astype(bf16)
    dybt[...] = dyb[...].T
    dpres, w_ups = [], []
    for t in range(2):
        for part in range(2):
            cols = slice(part * 512, (part + 1) * 512)
            w_up = up(t, part)
            pre = dot(h2[...], w_up)
            hidden, tanh, square = gelu_parts(pre)
            slope = 0.5 * (1.0 + tanh) + (0.5 * gelu_coef) * pre * (1.0 - tanh * tanh) * (
                1.0 + (3 * 0.044715) * square
            )
            dhidden = dot(dyb[...], down(t, part))
            dpre = (dhidden * slope).astype(bf16)
            out_cols = slice(1024 + part * 512, 1024 + (part + 1) * 512)
            put_grad(grads, t, out_cols, dot(dybt[...], hidden.astype(bf16)).astype(bf16))
            put_grad(grads, t, cols, dot(h2t[...], dpre).astype(bf16))
            dpres.append(dpre)
            w_ups.append(w_up)
    xhat, inv = ln_parts(x1[...])
    grad = dot_nt(jnp.concatenate(dpres, axis=1), jnp.concatenate(w_ups, axis=1))
    small[0:1, :] = jnp.sum(grad * xhat, axis=0, keepdims=True)
    small[1:2, :] = jnp.sum(grad, axis=0, keepdims=True)
    dx1[...] = dy[...] + ln_back(grad, xhat, inv, gain_of(norms, at))


def heads_back(low, w, saved, lse, mask, put_out, scratch):
    qs, k, v, o, qst, kt = saved
    flip, do, dot_t, dqt, dq, dk, dv = scratch
    flip[...] = low.T
    for t in range(2):
        cols = slice(t * 256, (t + 1) * 256)
        do[:, cols] = dot(low, w_at(w, None, t, 768, 256)).astype(bf16)
        put_out(t, dot(flip[...], o[:, cols]).astype(bf16))
    dot_t[...] = do[...].T
    first = lax.broadcasted_iota(jnp.int32, (512, 128), 1) < HEAD_DIM
    for pair in range(4):
        lanes = slice(pair * 128, (pair + 1) * 128)
        dvs, dks = [], []
        for which in range(2):
            head = pair * 2 + which
            rows = pl.ds(head * HEAD_DIM, HEAD_DIM)
            scores = dot(k[:, lanes], head_rows(qst, pair, which)) + mask[...]
            probs = jnp.exp(scores - lse[head : head + 1, :])
            dprobs = dot(v[:, lanes], head_rows(dot_t, pair, which))
            shift = jnp.sum(probs * dprobs, axis=0, keepdims=True)
            dscore = (probs * (dprobs - shift)).astype(bf16)
            dvs.append(dot(probs.astype(bf16), do[:, lanes]))
            dks.append(dot(dscore, qs[:, lanes]))
            dqt[rows, :] = (dot(kt[rows, :], dscore) * HEAD_DIM ** (-0.5)).astype(bf16)
        dv[:, lanes] = jnp.where(first, dvs[0], dvs[1]).astype(bf16)
        dk[:, lanes] = jnp.where(first, dks[0], dks[1]).astype(bf16)
    dq[...] = dqt[...].T


def rows_back(at, xf, norms, w, parts, small, grads, h, flip):
    h[...] = (ln_parts(xf)[0] * gain_of(norms, at) + bias_of(norms, at)).astype(bf16)
    flip[...] = h[...].T
    halves = []
    for t in range(2):
        cols = slice(t * 256, (t + 1) * 256)
        halves.append(jnp.concatenate([part[:, cols] for part in parts], axis=1))
        put_grad(grads, t, slice(0, 768), dot(flip[...], halves[t]).astype(bf16))
    grad = dot_nt(
        jnp.concatenate(halves, axis=1),
        jnp.concatenate([w_at(w, None, t, 0, 768) for t in range(2)], axis=1),
    )
    xhat, inv = ln_parts(xf)
    small[0:1, :] = jnp.sum(grad * xhat, axis=0, keepdims=True)
    small[1:2, :] = jnp.sum(grad, axis=0, keepdims=True)
    return ln_back(grad, xhat, inv, gain_of(norms, at))


def take_saved(saved, held, sems):
    copies = [
        pltpu.make_async_copy(a, b, sems.at[i]) for i, (a, b) in enumerate(zip(saved, held))
    ]
    start_all(copies)
    return copies


def attn_bwd_kernel(at, own, other, dx1, norms, lse, *refs):
    w, saved, x, refs = refs[:4], refs[4:10], refs[10], refs[11:]
    dx, small, grads = refs[0], refs[1], refs[2:4]
    mask, h, held, scratch, sems = refs[4], refs[5], refs[6:12], refs[12:19], refs[19]
    copies = take_saved(saved, held, sems)
    mask[...] = segment_mask(own, other)
    low = dx1[...].astype(bf16)
    wait_all(copies)

    def put_out(t, value):
        put_grad(grads, t, slice(768, 1024), value)

    heads_back(low, w, held, lse, mask, put_out, scratch)
    dx[...] = dx1[...] + rows_back(
        at, x[...], norms, w, scratch[4:], small, grads, h, scratch[0]
    )


def heads_bwd_kernel(own, other, dx1, lse, *refs):
    w, saved, refs = refs[:4], refs[4:10], refs[10:]
    parts, grads, mask, held = refs[:3], refs[3:5], refs[5], refs[6:12]
    scratch, sems = (*refs[12:16], *parts), refs[16]
    copies = take_saved(saved, held, sems)
    mask[...] = segment_mask(own, other)
    low = dx1[...].astype(bf16)
    wait_all(copies)

    def put_out(t, value):
        put_grad(grads, t, slice(0, 256), value)

    heads_back(low, w, held, lse, mask, put_out, scratch)


def rows_bwd_kernel(
    ids, own, other, dx1, norms, dq, dk, dv, out_0, out_1, other_small, d_x1, *refs
):
    w, d_w, (dx, dx_low, y, y_low), grads, (small, h, flip) = (
        refs[:4],
        refs[4:12],
        refs[12:16],
        refs[16:18],
        refs[18:],
    )
    total = dx1[...] + rows_back(
        0, load_rows(None, own, other), norms, w, (dq, dk, dv), small, grads, h, flip
    )
    dx[...] = total[:256, :]
    dx_low[...] = total[256:, :].astype(bf16)
    rows = jnp.concatenate([small[0:2, :], other_small[0:2, :], jnp.zeros((4, 512), f32)], axis=0)
    packed = pack_rows(ordered(rows, order_matrix(ids[0], True)))
    for grad, part in zip(grads, (out_0, out_1)):
        for i in range(4):
            for z in range(4):
                grad[i, z, :, 768:1024] = part[i, z]
                grad[i, z, :, 1024:1152] = packed
    rows = mlp_rows(4, d_x1[...], norms, d_w, h)
    y[...] = rows[:256, :]
    y_low[...] = rows[256:, :].astype(bf16)


def pack_rows(rows):
    cut = [rows[i : i + 1, 128 * j : 128 * (j + 1)] for i in range(4) for j in range(4)]
    return jnp.concatenate(split2(jnp.concatenate(cut, axis=0)), axis=0)


def code_prep_kernel(book_t, stack, stack_t):
    def one_chunk(index, _):
        lanes = pl.ds(pl.multiple_of(index * 512, 512), 512)
        rows = book_t[:, lanes]
        unit = rows * lax.rsqrt(jnp.sum(rows * rows, axis=0, keepdims=True) + norm_eps)
        hi, mid, lo = split3(unit)
        stack_t[:, lanes] = jnp.concatenate([hi, mid, lo, jnp.ones((32, 512), bf16)], axis=0)
        tall = jnp.concatenate([hi, mid, lo, hi, mid, hi, jnp.zeros((64, 512), bf16)], axis=0)
        stack[lanes, :] = tall.T
        return 0

    lax.fori_loop(0, book_t.shape[1] // 512, one_chunk, 0)


def factor_stack(x):
    hi, mid, lo = split3(x)
    return jnp.concatenate([hi, hi, hi, mid, mid, lo, jnp.zeros((64, x.shape[1]), bf16)], axis=0)


def code_loads(pairs, sems):
    loads = []
    for piece in range(4):
        group = []
        for at, (held, to, by_row) in enumerate(pairs):
            size = held.shape[0 if by_row else 1] // 4
            part = pl.ds(piece * size, size)
            place = (part, slice(None)) if by_row else (slice(None), part)
            group.append(pltpu.make_async_copy(held.at[place], to.at[place], sems.at[at, piece]))
        start_all(group)
        loads.append(group)
    return loads


def mlp_vq_kernel(x1, norms, vq_w, stack_hbm, stack_t_hbm, *refs):
    w, (e, u, kept, numer_hbm, h2, acc, stack, stack_t, numer, sems, out_sems) = refs[:8], refs[8:]
    loads = code_loads([(stack_hbm, stack, True), (stack_t_hbm, stack_t, False)], sems)
    e[...] = mlp_rows(1, x1[...], norms, w, h2)
    lnv = ln_parts(e[...])[0] * gain_of(norms, 2) + bias_of(norms, 2)
    raw = dot_nt(vq_w[0:32, :], lnv, highest)
    inv = lax.rsqrt(jnp.sum(raw * raw, axis=0, keepdims=True) + norm_eps)
    latent = raw * inv
    right = factor_stack(latent * (temper * log2e))
    chunks, keeps = stack.shape[0] // 2048, []
    for piece, group in enumerate(loads):
        wait_all(group)
        for part in range(piece * chunks // 4, (piece + 1) * chunks // 4):
            numers = []
            for index in range(4 * part, 4 * part + 4):
                codes = slice(index * 512, (index + 1) * 512)
                numers.append(jnp.exp2(dot(stack[codes, :], right)).astype(bf16))
            if part > 1:
                keeps[part - 2].wait()
            keeps.append(
                pltpu.make_async_copy(
                    numer.at[part % 2],
                    numer_hbm.at[pl.ds(part * 2048, 2048), :],
                    out_sems.at[part % 2],
                )
            )
            numer[part % 2] = jnp.concatenate(numers, axis=0)
            keeps[part].start()
            sums = dot(stack_t[:, part * 2048 : (part + 1) * 2048], numer[part % 2])
            if part == 0:
                acc[...] = sums
            else:
                acc[...] += sums
    total = acc[96:97, :]
    soft = (acc[0:32, :] + acc[32:64, :] + acc[64:96, :]) / total
    kept[0:32, :] = latent
    kept[32:64, :] = soft
    kept[64:65, :] = total
    kept[65:66, :] = inv
    u[...] = dot_full(soft.T, vq_w[32:64, :])
    wait_all(keeps[-2:])


def vq_bwd_kernel(
    ids, e, du, norms, vq_w, stack_hbm, stack_t_hbm, book_hbm, numer_hbm, kept, *refs
):
    small0, small1, de, code_keep, code_send = refs[:5]
    acc, grads, small, tail, stack, stack_t, book_t, numer, load_sems, sems = refs[5:]
    loads = code_loads(
        [
            (stack_hbm, stack, True),
            (numer_hbm, numer, True),
            (stack_t_hbm, stack_t, False),
            (book_hbm, book_t, False),
        ],
        load_sems,
    )
    xhat, inv_ln = ln_parts(e[...])
    lnv = xhat * gain_of(norms, 2) + bias_of(norms, 2)
    latent, soft = kept[0:32, :], kept[32:64, :]
    total, inv = kept[64:65, :], kept[65:66, :]
    direct = (2.0 * 1.25 * commit_weight) * (latent - soft)
    dsoft = dot_nt(vq_w[32:64, :], du[...], highest) - direct
    small[32:64, :] = dot_full(soft, du[...])
    shift = jnp.sum(dsoft * soft, axis=0, keepdims=True) / total
    dsoft = dsoft / total
    right = factor_stack(dsoft)
    pads = jnp.zeros((64, 512), f32)

    def tall(x):
        hi, lo = split2(x)
        return jnp.concatenate([hi.astype(f32), lo.astype(f32), pads], axis=0).T.astype(bf16)

    sides = jnp.concatenate([tall(dsoft), tall(latent * temper)], axis=0)
    chunks = stack.shape[0] // 2048
    for piece, group in enumerate(loads):
        wait_all(group)
        for part in range(piece * chunks // 4, (piece + 1) * chunks // 4):
            dlogits = []
            for index in range(4 * part, 4 * part + 4):
                codes = slice(index * 512, (index + 1) * 512)
                held = numer[codes, :]
                dlogit = (held.astype(f32) * (dot(stack[codes, :], right) - shift)).astype(bf16)
                dlogits.append(dlogit)
                sums = jnp.concatenate([held, dlogit], axis=1)
                dcode = dot(sums, sides).T
                dcode = dcode[0:32, :] + dcode[32:64, :]
                rows = book_t[:, codes]
                scale = lax.rsqrt(jnp.sum(rows * rows, axis=0, keepdims=True) + norm_eps)
                unit = rows * scale
                grads[:, codes] = (
                    scale * (dcode - unit * jnp.sum(unit * dcode, axis=0, keepdims=True))
                ).astype(bf16)
            sums = dot(
                stack_t[0:96, part * 2048 : (part + 1) * 2048], jnp.concatenate(dlogits, axis=0)
            )
            if part == 0:
                acc[...] = sums
            else:
                acc[...] += sums
    dlatent = temper * (acc[0:32, :] + acc[32:64, :] + acc[64:96, :]) + direct
    draw = inv * (dlatent - latent * jnp.sum(latent * dlatent, axis=0, keepdims=True))
    small[0:32, :] = dot_full(draw, lnv)
    dln = dot_full(draw.T, vq_w[0:32, :])
    small[64:65, :] = jnp.sum(dln * xhat, axis=0, keepdims=True)
    small[65:66, :] = jnp.sum(dln, axis=0, keepdims=True)
    small[66:68, :] = small0[0:2, :]
    small[68:70, :] = small1[0:2, :]
    small[70:96, :] = jnp.zeros((26, 512), f32)
    small[...] = ordered(small[...], order_matrix(ids[0], True))
    for block in range(3):
        for at, part in enumerate(split2(small[block * 32 : (block + 1) * 32, :])):
            for side in range(2):
                tail[block * 2 + side, :, at * 256 : (at + 1) * 256] = part[
                    :, side * 256 : (side + 1) * 256
                ]
    tail[6:8] = jnp.zeros((2, 32, 512), bf16)
    core, z = ids[0] % 2, ids[0] // 4
    copies = []
    for slot, (at, to) in enumerate(((core, code_keep), (1 - core, code_send))):
        for k in range(4):
            part = at * 4 + (z ^ k)
            lanes = pl.ds(pl.multiple_of(part * 1024, 1024), 1024)
            copies += [
                pltpu.make_async_copy(
                    grads.at[:, lanes], to.at[k, :, pl.ds(0, 1024)], sems.at[0, slot, k]
                ),
                pltpu.make_async_copy(
                    tail.at[part], to.at[k, :, pl.ds(1024, 512)], sems.at[1, slot, k]
                ),
            ]
    for copy in copies:
        copy.start()
    de[...] = ln_back(dln, xhat, inv_ln, gain_of(norms, 2))
    for copy in copies:
        copy.wait()


SMEM = pl.BlockSpec(memory_space=pltpu.SMEM)
VMEM = pl.BlockSpec(memory_space=pltpu.VMEM)
ANY = pl.BlockSpec(memory_space=pl.ANY)


def shaped(*pairs):
    return [jax.ShapeDtypeStruct(shape, dtype) for shape, dtype in pairs]


def pin(array):
    return pltpu.with_memory_space_constraint(array, pltpu.HBM)


def call(kernel, name, in_specs, out_specs, outs, scratch, flops, after=(), carry=()):
    n_in, n_extra, n_out = len(in_specs), len(after) + len(carry), len(outs)

    def body(*refs):
        first = n_in + n_extra
        kernel(*refs[:n_in], *refs[first : first + n_out], *refs[first + n_out + len(carry) :])

    made = pl.pallas_call(
        body,
        name=name,
        in_specs=in_specs + [ANY] * n_extra,
        out_specs=out_specs + [ANY] * len(carry),
        out_shape=outs + [jax.ShapeDtypeStruct(a.shape, a.dtype) for a in carry],
        scratch_shapes=scratch,
        input_output_aliases={n_in + len(after) + i: n_out + i for i in range(len(carry))},
        compiler_params=pltpu.CompilerParams(vmem_limit_bytes=vmem_cap),
        cost_estimate=pl.CostEstimate(flops=flops, bytes_accessed=10**6, transcendentals=0),
    )

    def run(*args):
        res = made(*args, *after, *carry)
        return (*res[:n_out], list(res[n_out:]))

    return run


DMA = pltpu.SemaphoreType.DMA
ROWS2 = (512, 512)


def attn_fwd(at, marked, xs, norms, w, after=(), carry=()):
    outs = shaped((ROWS2, f32), ((8, 512), f32)) + [pltpu.HBM(ROWS2, bf16)] * 6
    scratch = [
        *[pltpu.VMEM(ROWS2, bf16)] * 3,
        pltpu.VMEM(ROWS2, f32),
        *[pltpu.VMEM(ROWS2, bf16)] * 6,
        DMA((6,)),
    ]
    x1, lse, *saved, carried = call(
        functools.partial(attn_fwd_kernel, bool(xs), at),
        "attn_fwd",
        [VMEM] * (7 + len(xs)),
        [VMEM] * 2 + [ANY] * 6,
        outs,
        scratch,
        10**10,
        after,
        carry,
    )(*marked, norms, *w[:4], *xs)
    return x1, (lse, *saved), carried


def mlp_bwd(at, ids, x1, dys, norms, w, after=(), carry=()):
    scratch = [
        *[pltpu.VMEM(ROWS2, bf16)] * 4,
        *[pltpu.VMEM(ROWS2, f32)] * (len(dys) - 1),
    ]
    return call(
        functools.partial(mlp_bwd_kernel, len(dys) == 2, at),
        "mlp_bwd",
        [SMEM] + [VMEM] * (10 + len(dys)),
        [VMEM] * 4,
        shaped((ROWS2, f32), ((8, 512), f32), *[((4, 4, 32, 2048), bf16)] * 2),
        scratch,
        15 * 10**9,
        after,
        carry,
    )(ids, x1, norms, *w, *dys)


def attn_bwd(at, marked, x, dx1, norms, saved, w, after=(), carry=()):
    scratch = [pltpu.VMEM(ROWS2, f32), *[pltpu.VMEM(ROWS2, bf16)] * 14, DMA((6,))]
    outs = shaped((ROWS2, f32), ((8, 512), f32), *[((4, 4, 32, 1024), bf16)] * 2)
    return call(
        functools.partial(attn_bwd_kernel, at),
        "attn_bwd",
        [VMEM] * 9 + [ANY] * 6 + [VMEM],
        [VMEM] * 4,
        outs,
        scratch,
        15 * 10**9,
        after,
        carry,
    )(*marked, dx1, norms, saved[0], *w[:4], *map(pin, saved[1:]), x)


def heads_bwd(marked, dx1, saved, w, after=(), carry=()):
    scratch = [pltpu.VMEM(ROWS2, f32), *[pltpu.VMEM(ROWS2, bf16)] * 10, DMA((6,))]
    outs = shaped(*[(ROWS2, bf16)] * 3, *[((4, 4, 32, 256), bf16)] * 2)
    return call(
        heads_bwd_kernel,
        "heads_bwd",
        [VMEM] * 8 + [ANY] * 6,
        [VMEM] * 5,
        outs,
        scratch,
        10 * 10**9,
        after,
        carry,
    )(*marked, dx1, saved[0], *w[:4], *map(pin, saved[1:]))


def rows_bwd(ids, marked, dx1, norms, parts, other_small, d_x1, w, d_w, after=(), carry=()):
    scratch = [pltpu.VMEM((8, 512), f32), *[pltpu.VMEM(ROWS2, bf16)] * 2]
    outs = shaped(*[((256, 512), f32), ((256, 512), bf16)] * 2, *[((4, 4, 32, 1152), bf16)] * 2)
    return call(
        rows_bwd_kernel,
        "rows_bwd",
        [SMEM] + [VMEM] * 23,
        [VMEM] * 6,
        outs,
        scratch,
        10 * 10**9,
        after,
        carry,
    )(ids, *marked, dx1, norms, *parts, other_small, d_x1, *w[:4], *d_w)


def code_prep(book_t, after=(), carry=()):
    codes = book_t.shape[1]
    return call(
        code_prep_kernel,
        "code_prep",
        [VMEM],
        [VMEM] * 2,
        shaped(((codes, 256), bf16), ((128, codes), bf16)),
        [],
        6 * 10**9,
        after,
        carry,
    )(book_t)


def mlp_vq(x1, norms, vq_w, stack, stack_t, w, after=(), carry=()):
    return call(
        mlp_vq_kernel,
        "mlp_vq",
        [VMEM] * 3 + [ANY] * 2 + [VMEM] * 8,
        [VMEM] * 3 + [ANY],
        shaped((ROWS2, f32), (ROWS2, f32), ((72, 512), f32))
        + [pltpu.HBM((stack.shape[0], 512), bf16)],
        [
            pltpu.VMEM(ROWS2, bf16),
            pltpu.VMEM((128, 512), f32),
            pltpu.VMEM(stack.shape, bf16),
            pltpu.VMEM(stack_t.shape, bf16),
            pltpu.VMEM((2, 2048, 512), bf16),
            DMA((2, 4)),
            DMA((2,)),
        ],
        25 * 10**9,
        after,
        carry,
    )(x1, norms, vq_w, pin(stack), pin(stack_t), *w)


def vq_bwd(ids, e, du, norms, vq_w, codes, kept, smalls, after=(), carry=()):
    scratch = [
        pltpu.VMEM((96, 512), f32),
        pltpu.VMEM(codes[2].shape, bf16),
        pltpu.VMEM((96, 512), f32),
        pltpu.VMEM((8, 32, 512), bf16),
        *[pltpu.VMEM(a.shape, a.dtype) for a in codes],
        DMA((4, 4)),
        DMA((2, 2, 4)),
    ]
    return call(
        vq_bwd_kernel,
        "vq_bwd",
        [SMEM] + [VMEM] * 4 + [ANY] * 4 + [VMEM] * 3,
        [VMEM] + [ANY] * 2,
        shaped((ROWS2, f32), *[((4, 32, 1536), bf16)] * 2),
        scratch,
        25 * 10**9,
        after,
        carry,
    )(ids, e, du, norms, vq_w, *map(pin, codes), kept, *smalls)


def lines_kernel(cuts, *refs):
    first = 0
    for out, width in zip(refs[4:], cuts):
        for k in range(4):
            out[k] = refs[k][:, first : first + width]
        first += width


def stack_lines(shards, cuts, after=(), carry=()):
    return call(
        functools.partial(lines_kernel, cuts),
        "stack_lines",
        [VMEM] * 4,
        [VMEM] * len(cuts),
        shaped(*[((4, 32, width), bf16) for width in cuts]),
        [],
        1,
        after,
        carry,
    )(*shards)


def pack_kernel(*refs):
    hbm, outs, held, sems = refs[:4], refs[4:6], refs[6:10], refs[10]
    copies = [pltpu.make_async_copy(hbm[at], held[at], sems.at[at]) for at in range(4)]
    start_all(copies)
    wait_all(copies)
    qkv, out_t, up, down_t = held
    for layer, out in enumerate(outs):
        for index in range(3):
            out[:, index * 256 : (index + 1) * 256] = qkv[layer, index]
        out[:, 768:1024] = out_t[layer]
        out[:, 1024:2048] = up[layer]
        out[:, 2048:] = down_t[layer]


def pack_weights(*arrays):
    return call(
        pack_kernel,
        "pack_weights",
        [ANY] * 4,
        [VMEM] * 2,
        shaped(*[((32, 3072), bf16)] * 2),
        [*[pltpu.VMEM(a.shape, a.dtype) for a in arrays], DMA((4,))],
        1,
    )(*map(pin, arrays))[:-1]


def pairs_kernel(*refs):
    count = len(refs) // 3
    for at in range(count):
        refs[2 * count + at][0] = refs[2 * at][...]
        refs[2 * count + at][1] = refs[2 * at + 1][...]


def stack_pairs(pairs, after=(), carry=()):
    return call(
        pairs_kernel,
        "stack_pairs",
        [VMEM] * (2 * len(pairs)),
        [VMEM] * len(pairs),
        shaped(*[((2, *a.shape), bf16) for a, _ in pairs]),
        [],
        1,
        after,
        carry,
    )(*[array for pair in pairs for array in pair])


def gate(after, carry):
    def kernel(out):
        out[...] = jnp.zeros_like(out)

    return call(kernel, "gate", [], [VMEM], shaped(((8, 128), f32)), [], 1, after, carry)()[-1]


def rows_in_kernel(ids, *refs):
    hbm, (own, send, norms, vq_w, cot_own), held, sems = refs[:7], refs[7:12], refs[12:19], refs[19]
    copies = [pltpu.make_async_copy(hbm[at], held[at], sems.at[at]) for at in range(7)]
    start_all(copies)
    matrix = order_matrix(ids[0], False)
    wait_all(copies)
    tokens, segs, cot, gains, biases, in_t, out_w = held
    for to, micro in ((send, 1 - ids[1]), (own, ids[1])):
        to[:, :512] = ordered(tokens[micro], matrix).astype(bf16)
        ids_row = segs[pl.ds(micro, 1), :].astype(f32)
        to[:, 512:640] = jnp.broadcast_to(ids_row, (128, 256)).T.astype(bf16)
    send[:, 640:] = ordered(cot[1 - ids[1]].astype(bf16), matrix).astype(bf16)
    pad = jnp.zeros((3, 512), f32)
    rows = jnp.concatenate([gains[...], pad, biases[...], pad], axis=0)
    norms[...] = ordered(rows, matrix)
    vq_w[...] = ordered(jnp.concatenate([in_t[...], out_w[...]], axis=0), matrix)
    cot_own[...] = ordered(cot[ids[1]], matrix)


def rows_in(ids, *arrays):
    outs = shaped(
        ((256, 640), bf16),
        ((256, 1152), bf16),
        ((16, 512), f32),
        ((64, 512), f32),
        ((256, 512), f32),
    )
    return call(
        rows_in_kernel,
        "rows_in",
        [SMEM] + [ANY] * 7,
        [VMEM] * 5,
        outs,
        [*[pltpu.VMEM(a.shape, a.dtype) for a in arrays], DMA((7,))],
        1,
    )(ids, *map(pin, arrays))[:-1]


def joined(block):
    return block[0:16, 1024:].astype(f32) + block[16:32, 1024:].astype(f32)


def put_small(value, own, blocks):
    hi, lo = split2(value)
    own[0:16, 1024:] = hi.astype(f32) + lo.astype(f32)
    for block in blocks:
        block[0:16, 1024:] = hi
        block[16:32, 1024:] = lo


def near_kernel(ids, ins, outs):
    keep, other = ins
    for i in range(4):
        outs[i][...] = (keep[i].astype(f32) + other[i].astype(f32)).astype(outs[i].dtype)
    if keep.shape[3] == 1152:
        value = joined(keep.at[0, 0]) + joined(other.at[0, 0])
        put_small(value, outs[0].at[0], [out.at[0] for out in outs[1:]])


def near_task(keep, other):
    shape = keep.shape[1:]
    return near_kernel, [keep, other], shaped((shape, f32), *[(shape, bf16)] * 3)


def put_code(ref, first, code):
    for i in range(3):
        ref[first + i] = code[:, 1024 * i : 1024 * (i + 1)]


def get_code(ref, first):
    return jnp.concatenate([ref[first + i] for i in range(3)], axis=1)


def swapped(code):
    return jnp.concatenate([code[:, 1536:], code[:, :1536]], axis=1)


def code_sum(a, b):
    done = []
    for first in range(0, a.shape[1], 1536):
        total = a[:, first : first + 1024].astype(f32) + b[:, first : first + 1024].astype(f32)
        small = [
            x[:, first + 1024 : first + 1280].astype(f32) + x[:, first + 1280 : first + 1536].astype(f32)
            for x in (a, b)
        ]
        done += [total.astype(bf16), *split2(small[0] + small[1])]
    return jnp.concatenate(done, axis=1)


def fork_kernel(ids, ins, outs):
    keep, other = ins
    own_a, to_x, own_b, to_y = outs
    half = keep.shape[3] // 2
    for at, (own, send, kept, sent) in enumerate(
        ((own_a, to_x, (0, 2), (1, 3)), (own_b, to_y, (0, 1), (2, 3)))
    ):
        cols = slice(half * at, half * (at + 1))
        for j in range(2):
            own[j] = keep[kept[j], :, :, cols].astype(f32) + other[kept[j], :, :, cols].astype(f32)
            total = keep[sent[j], :, :, cols].astype(f32) + other[sent[j], :, :, cols].astype(f32)
            send[4 * j : 4 * (j + 1)] = total.astype(bf16)


def fork_task(keep, other):
    half = keep.shape[3] // 2
    outs = shaped(*[((2, 4, 32, half), f32), ((8, 32, half), bf16)] * 2)
    return fork_kernel, [keep, other], outs


def half_kernel(ids, ins, outs):
    own_a, from_x, own_b, from_y = ins[:4]
    kept_a, to_y, kept_b, to_x = outs[:4]
    for own, other, kept, send in (
        (own_a, from_x, kept_a, to_y),
        (own_b, from_y, kept_b, to_x),
    ):
        kept[...] = own[0] + other[0:4].astype(f32)
        send[0:4] = (own[1] + other[4:8].astype(f32)).astype(bf16)
    if len(ins) == 6:
        code, code_other = ins[4:]
        outs[4][...] = code_sum(code[...], swapped(code_other[...]))
        put_code(to_x, 4, outs[4])


def half_task(own_a, from_x, own_b, from_y, *codes):
    width = own_a.shape[3]
    outs = shaped(
        ((4, 32, width), f32),
        ((4, 32, width), bf16),
        ((4, 32, width), f32),
        ((7 if codes else 4, 32, width), bf16),
        *[(code.shape, bf16) for code in codes[:1]],
    )
    return half_kernel, [own_a, from_x, own_b, from_y, *codes], outs


def join_kernel(ids, ins, outs):
    kept, send = outs[:2]
    width = ins[0].shape[2]
    for at, (own, other) in enumerate((ins[0:2], ins[2:4])):
        cols = slice(width * at, width * (at + 1))
        for k in range(2):
            kept[k, :, cols] = own[2 * k] + other[2 * k].astype(f32)
            send[k, :, cols] = (own[2 * k + 1] + other[2 * k + 1].astype(f32)).astype(bf16)
    if len(ins) == 5:
        outs[2][...] = code_sum(ins[4][...], get_code(ins[3], 4))


def join_task(own_a, from_y, own_b, from_x, *codes):
    width = 2 * own_a.shape[2]
    outs = shaped(
        ((2, 32, width), f32),
        ((2, 32, width), bf16),
        *[(code.shape, bf16) for code in codes],
    )
    return join_kernel, [own_a, from_y, own_b, from_x, *codes], outs


def far_kernel(ids, ins, outs):
    own_a, from_y, own_b, from_x, kept_dm, other_dm = ins
    kept, own_dm, send = outs
    for at, (own, other) in enumerate(((own_a, from_y), (own_b, from_x))):
        cols = slice(512 * at, 512 * (at + 1))
        for k in range(2):
            kept[k, :, cols] = own[k] + other[k].astype(f32)
            send[2 + k, :, cols] = (own[2 + k] + other[2 + k].astype(f32)).astype(bf16)
    own_dm[...] = kept_dm[0] + other_dm[0].astype(f32)
    for i in range(2):
        cols = slice(1024 * i, 1024 * (i + 1))
        send[i] = (kept_dm[1, :, cols] + other_dm[1, :, cols].astype(f32)).astype(bf16)


def far_task(own_a, from_y, own_b, from_x, kept_dm, other_dm):
    outs = shaped(((2, 32, 1024), f32), (kept_dm.shape[1:], f32), ((4, 32, 1024), bf16))
    return far_kernel, [own_a, from_y, own_b, from_x, kept_dm, other_dm], outs


def near_step_kernel(ids, ins, outs):
    kept, other = ins
    outs[0][...] = kept[0] + other[2].astype(f32)
    outs[1][...] = (kept[1] + other[3].astype(f32)).astype(bf16)


def near_step_task(kept, other):
    shape = kept.shape[1:]
    return near_step_kernel, [kept, other], shaped((shape, f32), (shape, bf16))


def line_step_kernel(ids, ins, outs):
    kept, other = ins
    outs[0][...] = kept[0] + other[0].astype(f32)
    outs[1][...] = (kept[1] + other[1].astype(f32)).astype(bf16)


def line_step_task(kept, other):
    shape = kept.shape[1:]
    return line_step_kernel, [kept, other], shaped((shape, f32), (shape, bf16))


def plane_line_kernel(ids, ins, outs):
    kept, send = outs
    for k in range(4):
        total = ins[0][k]
        for other in ins[1:]:
            total = total + other[k].astype(f32)
        to = send if k % 2 else kept
        to[k // 2] = total.astype(to.dtype)
    x, y, xy = [joined(other.at[0]) for other in ins[1:]]
    put_small((ins[0][0, 0:16, 1024:] + x) + (y + xy), kept.at[0], [send.at[0]])


def plane_line_task(own, others):
    outs = shaped(((2, 32, 1152), f32), ((2, 32, 1152), bf16))
    return plane_line_kernel, [own, *others], outs


def small_step_kernel(ids, ins, outs):
    kept, other = ins
    line_step_kernel(ids, ins, outs)
    put_small(kept[0, 0:16, 1024:] + joined(other.at[0]), outs[0], [outs[1]])


def small_step_task(kept, other):
    shape = kept.shape[1:]
    return small_step_kernel, [kept, other], shaped((shape, f32), (shape, bf16))


def line_total(ins, width):
    total = ins[0][:, :width]
    for other in ins[1:]:
        total = total + other[:, :width].astype(f32)
    return total


def rows_out_kernel(ids, ins, outs):
    y, y_low, dx, dx_low = ins
    matrix = order_matrix(ids[0], True)
    outs[0][...] = ordered(y[...], matrix)
    outs[1][...] = ordered(dx[...], matrix)
    outs[2][0:256, :] = ordered(y_low[...], matrix).astype(bf16)
    outs[2][256:, :] = ordered(dx_low[...], matrix).astype(bf16)


def rows_out_task(y, y_low, dx, dx_low):
    outs = shaped((y.shape, f32), (dx.shape, f32), (ROWS2, bf16))
    return rows_out_kernel, [y, y_low, dx, dx_low], outs


def rows_done_kernel(ids, y, dx, others, decoded, grad_tokens, done, held, sems):
    copies = []
    done[...] = jnp.zeros_like(done)
    for at, (out, own) in enumerate(((decoded, y), (grad_tokens, dx))):
        held[at] = others[256 * at : 256 * (at + 1), :].astype(f32)
        copies.append(pltpu.make_async_copy(own, out.at[ids[1]], sems.at[at, 0]))
        copies.append(pltpu.make_async_copy(held.at[at], out.at[1 - ids[1]], sems.at[at, 1]))
    start_all(copies)
    wait_all(copies)


def rows_done(ids, y, dx, others, after):
    return call(
        rows_done_kernel,
        "rows_done",
        [SMEM] + [VMEM] * 3,
        [ANY] * 2 + [VMEM],
        [pltpu.HBM((2, 256, 512), f32)] * 2 + shaped(((8, 128), f32)),
        [pltpu.VMEM((2, 256, 512), f32), DMA((2, 2))],
        10**9,
        after,
    )(ids, y, dx, others)[:-1]


def code_near_kernel(ids, ins, outs):
    keep, other = ins
    for at, out in enumerate(outs):
        for i in range(2):
            out[:, 1536 * i : 1536 * (i + 1)] = code_sum(keep[2 * at + i], other[2 * at + i])


def code_near_task(keep, other):
    return code_near_kernel, [keep, other], shaped(*[((32, 3072), bf16)] * 2)


def code_add_kernel(ids, ins, outs):
    outs[0][...] = code_sum(ins[0][...], ins[1][...])


def code_add_task(a, b):
    return code_add_kernel, [a, b], shaped((a.shape, bf16))


def code_pair_kernel(ids, ins, outs):
    for at, part in enumerate(ins):
        outs[0][:, 3072 * at : 3072 * (at + 1)] = part[...]


def code_pair_task(a, b):
    return code_pair_kernel, [a, b], shaped(((32, 6144), bf16))


def finish_kernel(ids, ins, outs):
    mlp, attn, d_mlp, d_attn, code, code_other = ins[:2], ins[2:4], ins[4:6], ins[6:8], *ins[8:]
    qkv, out_t, up, down_t, book, vq_in, vq_out, gains, biases, dec_biases, small_ref = outs
    rows = line_total(mlp, 2048)
    up[0] = rows[:, :1024]
    down_t[0] = rows[:, 1024:]
    for i, out in enumerate((up, down_t)):
        out[1] = d_mlp[0][:, 1024 * i : 1024 * (i + 1)] + d_mlp[1][i].astype(f32)
    d_rows = line_total(d_attn, 1024)
    for layer, rows in enumerate((line_total(attn, 1024), d_rows)):
        for index in range(3):
            qkv[layer, index] = rows[:, index * 256 : (index + 1) * 256]
        out_t[layer] = rows[:, 768:]
    core, z = ids[0] % 2, ids[0] // 4
    for at, parts in ((core, code), (1 - core, code_other)):
        for k in range(4):
            part = at * 4 + (z ^ k)
            held = parts[:, 1536 * k : 1536 * (k + 1)].astype(f32)
            book[:, pl.ds(pl.multiple_of(part * 1024, 1024), 1024)] = held[:, :1024]
            small_ref[:, pl.ds(pl.multiple_of(part * 256, 256), 256)] = (
                held[:, 1024:1280] + held[:, 1280:1536]
            )
    small = small_ref[...]
    vq_in[...] = small[:, :512]
    vq_out[...] = small[:, 512:1024]
    rest = small[:, 1024:1536]
    packed = attn[0][0:16, 1024:] + joined(attn[1])
    for row, out in enumerate((gains.at[0:1], biases.at[0:1], gains.at[1:2], biases.at[1:2])):
        for j in range(4):
            out[:, 128 * j : 128 * (j + 1)] = packed[row * 4 + j : row * 4 + j + 1, :]
    gains[2:3, :] = rest[0:1, :]
    biases[2:3, :] = rest[1:2, :]
    gains[3:4, :] = rest[2:3, :]
    dec_biases[0:1, :] = rest[3:4, :]
    gains[4:5, :] = rest[4:5, :]
    dec_biases[1:2, :] = rest[5:6, :]


def finish_task(mlp, attn, d_mlp, d_attn, code, code_other):
    outs = shaped(
        ((2, 3, 32, 256), f32),
        ((2, 32, 256), f32),
        ((2, 32, 1024), f32),
        ((2, 32, 1024), f32),
        ((32, 8192), f32),
        ((32, 512), f32),
        ((32, 512), f32),
        ((5, 512), f32),
        ((3, 512), f32),
        ((2, 512), f32),
        ((32, 2048), f32),
    )
    ins = [*mlp, *attn, *d_mlp, *d_attn, code, code_other]
    return finish_kernel, ins, outs


def run_tasks(ids, name, tasks, after=(), carry=()):
    sizes = [(len(ins), len(outs)) for _, ins, outs in tasks]
    n_in = sum(i for i, _ in sizes)

    def kernel(ids_ref, *refs):
        at_in, at_out = 0, n_in
        for (fn, _, _), (i, o) in zip(tasks, sizes):
            fn(ids_ref, refs[at_in : at_in + i], refs[at_out : at_out + o])
            at_in, at_out = at_in + i, at_out + o

    outs = [one for _, _, many in tasks for one in many]
    res = call(
        kernel, name, [SMEM] + [VMEM] * n_in, [VMEM] * len(outs), outs, [], 10**9, after, carry
    )(ids, *[one for _, many, _ in tasks for one in many])
    split, at = [], 0
    for _, o in sizes:
        split.append(res[at : at + o])
        at += o
    return (*split, res[-1])


def whole_groups(
    n_dp,
    tokens,
    segment_ids,
    norm_gains,
    norm_biases,
    w_qkv,
    w_attn_out,
    w_up,
    w_down,
    w_vq_in,
    w_vq_out,
    codebook,
    cotangent,
):
    dp_at, tp_at = lax.axis_index("dp"), lax.axis_index("tp")
    ids = jnp.stack([dp_at, tp_at]).astype(jnp.int32)

    def swap(values):
        return exchange(values, 0, 1, n_dp)

    def core(values):
        return [values, exchange(values, 1, 0, n_dp)]

    book_t = codebook.T
    enc_shard, dec_shard = pack_weights(
        w_qkv, w_attn_out.transpose(0, 2, 1), w_up, w_down.transpose(0, 2, 1)
    )
    enc_shards = spread_line(enc_shard, n_dp)
    own, send, norms, vq_w, cot_own = rows_in(
        ids,
        tokens,
        segment_ids,
        cotangent,
        norm_gains,
        norm_biases,
        w_vq_in.T,
        w_vq_out,
    )
    marked = [own, swap(send)]

    line_a, line_b, (dec_shard,) = stack_lines(enc_shards, [1536] * 2, carry=[dec_shard])
    along_x, along_y = exchange(line_a, 0, 1, n_dp), exchange(line_b, 2, 0, n_dp)
    dec_shards = spread_line(dec_shard, n_dp)
    stack, stack_t, _ = code_prep(book_t, [line_a])
    codes = (stack, stack_t, book_t)
    a_0, b_0, _ = stack_pairs([(line_a, along_x), (line_b, along_y)], [stack_t, marked[1]])
    a_1, b_1 = exchange(a_0, 2, 0, n_dp), exchange(b_0, 0, 1, n_dp)
    line_a, line_b, (a_0, b_0) = stack_lines(dec_shards, [1536] * 2, [a_1, b_1], [a_0, b_0])
    enc_w = [a_0, a_1, exchange(a_0, 1, 0, n_dp), exchange(a_1, 1, 0, n_dp)]
    enc_w += [b_0, b_1, exchange(b_0, 1, 0, n_dp), exchange(b_1, 1, 0, n_dp)]
    along_x, along_y = exchange(line_a, 0, 1, n_dp), exchange(line_b, 2, 0, n_dp)
    e_x1, e_saved, _ = attn_fwd(0, marked, [], norms, enc_w)
    a_0, b_0, _ = stack_pairs([(line_a, along_x), (line_b, along_y)], [e_x1])
    a_1, b_1 = exchange(a_0, 2, 0, n_dp), exchange(b_0, 0, 1, n_dp)
    dec_w = [a_0, exchange(a_0, 1, 0, n_dp), b_0, exchange(b_0, 1, 0, n_dp)]
    e, u, kept, numer, _ = mlp_vq(e_x1, norms, vq_w, stack, stack_t, enc_w, [a_0, b_0])
    a_1, b_1 = gate([u], [a_1, b_1])
    a_1, b_1 = core(a_1), core(b_1)
    dec_w = [dec_w[0], a_1[0], dec_w[1], a_1[1], dec_w[2], b_1[0], dec_w[3], b_1[1]]
    d_x1, d_saved, _ = attn_fwd(3, marked, [u], norms, dec_w)

    dx1, d_small1, keep_m, send_m, _ = mlp_bwd(
        4, ids, d_x1, [cot_own, marked[1]], norms, dec_w
    )
    near_m = exchange(send_m, 1, 0, n_dp)
    du, d_small0, keep_a, send_a, (keep_m,) = attn_bwd(
        3, marked, u, dx1, norms, d_saved, dec_w, carry=[keep_m]
    )
    (m_a, to_x, m_b, to_y), (send_a,) = run_tasks(
        ids, "sums1", [fork_task(keep_m, near_m)], carry=[send_a]
    )
    from_x, from_y = exchange(to_x, 0, 1, n_dp), exchange(to_y, 2, 0, n_dp)
    near_a = exchange(send_a, 1, 0, n_dp)
    de, code, code_send, (m_a, m_b, keep_a) = vq_bwd(
        ids,
        e,
        du,
        norms,
        vq_w,
        [*codes, numer],
        kept,
        [d_small0, d_small1],
        [to_x, to_y],
        [m_a, m_b, keep_a],
    )
    (m_a, m_y, m_b, m_x), (a_a, to_x, a_b, to_y), (code, code_send) = run_tasks(
        ids,
        "sums2",
        [half_task(m_a, from_x, m_b, from_y), fork_task(keep_a, near_a)],
        carry=[code, code_send],
    )
    code_other = exchange(code_send, 1, 0, n_dp)
    from_m_y, from_m_x = exchange(m_y, 2, 0, n_dp), exchange(m_x, 0, 1, n_dp)
    from_x, from_y = exchange(to_x, 0, 1, n_dp), exchange(to_y, 2, 0, n_dp)
    (code, code_send), _ = run_tasks(ids, "sums2b", [code_near_task(code, code_other)])
    code_other = exchange(code_send, 8, 0, n_dp)
    ex1, e_small1, keep_m, send_m, (m_a, m_b, a_a, a_b, code) = mlp_bwd(
        1,
        ids,
        e_x1,
        [de],
        norms,
        enc_w,
        [m_y, m_x, to_x, to_y, code_send],
        [m_a, m_b, a_a, a_b, code],
    )
    (own_dm, send_dm), (a_a, to_y, a_b, to_x), (code,), (keep_m, send_m) = run_tasks(
        ids,
        "sums3",
        [
            join_task(m_a, from_m_y, m_b, from_m_x),
            half_task(a_a, from_x, a_b, from_y),
            code_add_task(code, code_other),
        ],
        carry=[keep_m, send_m],
    )
    near_m, code_other = exchange(send_m, 1, 0, n_dp), exchange(code, 2, 0, n_dp)
    from_y, from_x = exchange(to_y, 2, 0, n_dp), exchange(to_x, 0, 1, n_dp)
    other_dm = exchange(send_dm, 4, 0, n_dp)
    *parts, (a_a, a_b, own_dm) = heads_bwd(
        marked, ex1, e_saved, enc_w, [to_x, to_y, send_dm, code], [a_a, a_b, own_dm]
    )
    (m_a, to_x, m_b, to_y), (code,), (own_da, own_dm, send_d), _ = run_tasks(
        ids,
        "sums3b",
        [
            fork_task(keep_m, near_m),
            code_add_task(code, code_other),
            far_task(a_a, from_y, a_b, from_x, own_dm, other_dm),
        ],
        [parts[0]],
    )
    other_d, code_other = exchange(send_d, 8, 0, n_dp), exchange(code, 4, 0, n_dp)
    from_y, from_x = exchange(to_y, 2, 0, n_dp), exchange(to_x, 0, 1, n_dp)
    dx, dx_low, y, y_low, keep_a, send_a, (m_a, m_b, own_dm, own_da) = rows_bwd(
        ids,
        marked,
        ex1,
        norms,
        parts,
        e_small1,
        d_x1,
        enc_w,
        dec_w,
        [to_x, to_y, send_d, code],
        [m_a, m_b, own_dm, own_da],
    )
    (m_a, to_y, m_b, to_x, code), (own_da, send_da), (keep_a, send_a) = run_tasks(
        ids,
        "sums4",
        [
            half_task(m_a, from_x, m_b, from_y, code, code_other),
            near_step_task(own_da, other_d),
        ],
        carry=[keep_a, send_a],
    )
    near_a = exchange(send_a, 1, 0, n_dp)
    from_y, from_x = exchange(to_y, 2, 0, n_dp), exchange(to_x, 0, 1, n_dp)
    other_da = exchange(send_da, 4, 0, n_dp)
    (own_a, *lows_a), (m_a, m_b, code) = run_tasks(
        ids, "sums4b", [near_task(keep_a, near_a)], carry=[m_a, m_b, code]
    )
    plane_a = plane_send(lows_a, n_dp)
    (own_m, send_m, code), (own_a,) = run_tasks(
        ids,
        "sums5",
        [join_task(m_a, from_y, m_b, from_x, code)],
        lows_a,
        [own_a],
    )
    other_m, code_other = exchange(send_m, 4, 0, n_dp), exchange(code, 8, 0, n_dp)
    (y, dx, rows), (own_a,) = run_tasks(
        ids, "rows_out", [rows_out_task(y, y_low, dx, dx_low)], [send_m, code], [own_a]
    )
    (own_a, send_a), (own_m, send_m), (code,), (rows,) = run_tasks(
        ids,
        "sums6",
        [
            plane_line_task(own_a, plane_a),
            line_step_task(own_m, other_m),
            code_pair_task(code, code_other),
        ],
        carry=[rows],
    )
    other_a, other_m = exchange(send_a, 4, 0, n_dp), exchange(send_m, 8, 0, n_dp)
    code_other, rows = exchange(code, 1, 0, n_dp), swap(rows)
    (own_a, send_a), _ = run_tasks(ids, "sums7", [small_step_task(own_a, other_a)])
    other_a = exchange(send_a, 8, 0, n_dp)
    decoded, grad_tokens, done = rows_done(ids, y, dx, rows, [send_a])
    (qkv, out_t, up, down_t, book, vq_in, vq_out, *norm_grads, _), _ = run_tasks(
        ids,
        "finish",
        [
            finish_task(
                (own_m, other_m),
                (own_a, other_a),
                (own_dm, other_d),
                (own_da, other_da),
                code,
                code_other,
            )
        ],
        [done],
    )
    return (
        decoded,
        grad_tokens,
        *norm_grads,
        qkv,
        out_t.transpose(0, 2, 1),
        up,
        down_t.transpose(0, 2, 1),
        vq_in.T,
        vq_out,
        book.T,
    )


def layer_norm(values, norm_gain, norm_bias):
    centred = values - jnp.mean(values, axis=-1, keepdims=True)
    spread = jnp.mean(centred * centred, axis=-1, keepdims=True)
    return centred * lax.rsqrt(spread + ln_eps) * norm_gain + norm_bias


def gelu_tanh(values):
    return (
        0.5 * values * (1.0 + jnp.tanh(gelu_coef * (values + 0.044715 * values * values * values)))
    )


def matmul(former, latter):
    return jnp.dot(former, latter, precision=highest, preferred_element_type=jnp.float32)


def normalize(values):
    return values * lax.rsqrt(jnp.sum(values * values, axis=-1, keepdims=True) + norm_eps)


def quantize(in_rows, norm_gain, norm_bias, in_w, out_w, code_w):
    latent = normalize(matmul(layer_norm(in_rows, norm_gain, norm_bias), in_w))
    code_rows = normalize(code_w)
    logits = matmul(latent, code_rows.T) * temper
    row_max = jnp.max(logits, axis=-1, keepdims=True)
    numerator = jnp.exp(logits - row_max)
    assign = numerator / jnp.sum(numerator, axis=-1, keepdims=True)
    soft_code = matmul(assign, code_rows)
    offset = latent - soft_code
    vq_loss = commit_weight * 1.25 * jnp.sum(offset * offset)
    return (matmul(soft_code, out_w), vq_loss)


def product(former, latter):
    return jnp.dot(former, latter, preferred_element_type=jnp.float32)


def product_tn(former, latter):
    return lax.dot_general(
        former, latter, (((0,), (0,)), ((), ())), preferred_element_type=jnp.float32
    )


def product_nt(former, latter):
    return lax.dot_general(
        former, latter, (((1,), (1,)), ((), ())), preferred_element_type=jnp.float32
    )


def split_heads(values):
    return values.reshape(values.shape[0], values.shape[1] // HEAD_DIM, HEAD_DIM).transpose(1, 0, 2)


def join_heads(values):
    return values.transpose(1, 0, 2).reshape(values.shape[1], values.shape[0] * HEAD_DIM)


def masked_scores(query_blk, key_h, seg_blk, seg_keys):
    scores = jnp.einsum(
        "hqd,hkd->hqk", query_blk, key_h, preferred_element_type=jnp.float32
    ) * HEAD_DIM ** (-0.5)
    return jnp.where((seg_blk[:, None] == seg_keys[None, :])[None], scores, masked_score)


def attend(query_h, key_h, value_h, seg_keys):
    block_rows = min(512, query_h.shape[1])
    block_count = query_h.shape[1] // block_rows

    def one_block(begin_row):
        query_blk = lax.dynamic_slice_in_dim(query_h, begin_row, block_rows, 1)
        seg_blk = lax.dynamic_slice_in_dim(seg_keys, begin_row, block_rows, 0)
        scores = masked_scores(query_blk, key_h, seg_blk, seg_keys)
        row_max = jnp.max(scores, axis=-1, keepdims=True)
        numerator = jnp.exp(scores - row_max)
        row_total = jnp.sum(numerator, axis=-1, keepdims=True)
        prob_low = (numerator / row_total).astype(jnp.bfloat16)
        attended = jnp.einsum("hqk,hkd->hqd", prob_low, value_h, preferred_element_type=jnp.float32)
        return (attended.astype(jnp.bfloat16), (row_max + jnp.log(row_total))[..., 0])

    starts = jnp.arange(block_count, dtype=jnp.int32) * block_rows
    attended, log_sums = lax.map(one_block, starts)
    heads_out = attended.transpose(1, 0, 2, 3).reshape(query_h.shape)
    log_sums = log_sums.transpose(1, 0, 2).reshape(query_h.shape[0], query_h.shape[1])
    return (heads_out, log_sums)


def attend_back(query_h, key_h, value_h, seg_keys, log_sums, grad_out):
    block_rows = min(512, query_h.shape[1])
    block_count = query_h.shape[1] // block_rows

    def one_block(carry, begin_row):
        grad_key, grad_value = carry
        query_blk = lax.dynamic_slice_in_dim(query_h, begin_row, block_rows, 1)
        grad_blk = lax.dynamic_slice_in_dim(grad_out, begin_row, block_rows, 1)
        lse_blk = lax.dynamic_slice_in_dim(log_sums, begin_row, block_rows, 1)
        seg_blk = lax.dynamic_slice_in_dim(seg_keys, begin_row, block_rows, 0)
        scores = masked_scores(query_blk, key_h, seg_blk, seg_keys)
        probs = jnp.exp(scores - lse_blk[..., None])
        prob_low = probs.astype(jnp.bfloat16)
        grad_value = grad_value + jnp.einsum(
            "hqk,hqd->hkd", prob_low, grad_blk, preferred_element_type=jnp.float32
        )
        grad_prob = jnp.einsum(
            "hqd,hkd->hqk", grad_blk, value_h, preferred_element_type=jnp.float32
        )
        row_dot = jnp.sum(probs * grad_prob, axis=-1, keepdims=True)
        grad_score = (probs * (grad_prob - row_dot) * HEAD_DIM ** (-0.5)).astype(jnp.bfloat16)
        grad_query = jnp.einsum(
            "hqk,hkd->hqd", grad_score, key_h, preferred_element_type=jnp.float32
        )
        grad_key = grad_key + jnp.einsum(
            "hqk,hqd->hkd", grad_score, query_blk, preferred_element_type=jnp.float32
        )
        return ((grad_key, grad_value), grad_query)

    starts = jnp.arange(block_count, dtype=jnp.int32) * block_rows
    zeros_kv = jnp.zeros(key_h.shape, jnp.float32)
    (grad_key, grad_value), grad_query = lax.scan(one_block, (zeros_kv, zeros_kv), starts)
    grad_query = grad_query.transpose(1, 0, 2, 3).reshape(query_h.shape)
    return (
        grad_query.astype(jnp.bfloat16),
        grad_key.astype(jnp.bfloat16),
        grad_value.astype(jnp.bfloat16),
    )


def spread_rows(values):
    return lax.all_gather(values, "tp", axis=0, tiled=True)


def combine_rows(partial_value):
    return lax.psum_scatter(partial_value, "tp", scatter_dimension=0, tiled=True)


def spread_grads(values):
    return lax.all_gather(values, "tp", axis=0, tiled=True)


def combine_grads(partial_value):
    return lax.psum_scatter(
        partial_value.astype(jnp.bfloat16), "tp", scatter_dimension=0, tiled=True
    ).astype(jnp.float32)


def fetch_weights(w_qkv, w_attn_out, w_up, w_down, layer):
    return (
        lax.all_gather(w_qkv[layer], "dp", axis=1, tiled=True),
        lax.all_gather(w_attn_out[layer], "dp", axis=1, tiled=True),
        lax.all_gather(w_up[layer], "dp", axis=0, tiled=True),
        lax.all_gather(w_down[layer], "dp", axis=1, tiled=True),
    )


def reduce_weight_grads(grads):
    return (
        lax.psum_scatter(
            grads[0].astype(jnp.bfloat16), "dp", scatter_dimension=1, tiled=True
        ).astype(jnp.float32),
        lax.psum_scatter(
            grads[1].astype(jnp.bfloat16), "dp", scatter_dimension=1, tiled=True
        ).astype(jnp.float32),
        lax.psum_scatter(
            grads[2].astype(jnp.bfloat16), "dp", scatter_dimension=0, tiled=True
        ).astype(jnp.float32),
        lax.psum_scatter(
            grads[3].astype(jnp.bfloat16), "dp", scatter_dimension=1, tiled=True
        ).astype(jnp.float32),
    )


def block_forward(resid_in, seg_local, gains, biases, weights):
    qkv_w, attn_w, up_w, down_w = weights
    normed = layer_norm(resid_in, gains[0], biases[0]).astype(jnp.bfloat16)
    normed_all, seg_all = (
        lax.all_gather(normed, "tp", axis=0, tiled=True),
        lax.all_gather(seg_local, "tp", axis=0, tiled=True),
    )
    query_h = split_heads(product(normed_all, qkv_w[0]).astype(jnp.bfloat16))
    key_h = split_heads(product(normed_all, qkv_w[1]).astype(jnp.bfloat16))
    value_h = split_heads(product(normed_all, qkv_w[2]).astype(jnp.bfloat16))
    heads_out, log_sums = attend(query_h, key_h, value_h, seg_all)
    attn_rows = join_heads(heads_out)
    middle = resid_in + combine_rows(product(attn_rows, attn_w))
    normed_mid = spread_rows(layer_norm(middle, gains[1], biases[1]).astype(jnp.bfloat16))
    hidden_pre = product(normed_mid, up_w)
    hidden = gelu_tanh(hidden_pre).astype(jnp.bfloat16)
    result = middle + combine_rows(product(hidden, down_w))
    kept = (
        resid_in,
        middle,
        normed_all,
        seg_all,
        query_h,
        key_h,
        value_h,
        log_sums,
        attn_rows,
        normed_mid,
        hidden_pre,
        hidden,
    )
    return (result, kept)


def block_backward(kept, gains, biases, weights, grad_result):
    (
        resid_in,
        middle,
        normed_all,
        seg_all,
        query_h,
        key_h,
        value_h,
        log_sums,
        attn_rows,
        normed_mid,
        hidden_pre,
        hidden,
    ) = kept
    qkv_w, attn_w, up_w, down_w = weights
    grad_branch = spread_grads(grad_result.astype(jnp.bfloat16))
    grad_down = product_tn(hidden, grad_branch)
    grad_hidden = product_nt(grad_branch, down_w)
    _, gelu_back = jax.vjp(gelu_tanh, hidden_pre)
    grad_pre = gelu_back(grad_hidden)[0].astype(jnp.bfloat16)
    grad_up = product_tn(normed_mid, grad_pre)
    grad_norm_mid = combine_grads(product_nt(grad_pre, up_w))
    _, norm_back_mid = jax.vjp(layer_norm, middle, gains[1], biases[1])
    grad_mid_ln, grad_gain_mid, grad_bias_mid = norm_back_mid(grad_norm_mid)
    grad_middle = grad_result + grad_mid_ln
    grad_attn_all = spread_grads(grad_middle.astype(jnp.bfloat16))
    grad_attn = product_tn(attn_rows, grad_attn_all)
    grad_heads = split_heads(product_nt(grad_attn_all, attn_w).astype(jnp.bfloat16))
    grad_query, grad_key, grad_value = attend_back(
        query_h, key_h, value_h, seg_all, log_sums, grad_heads
    )
    grad_parts = [join_heads(grad_query), join_heads(grad_key), join_heads(grad_value)]
    grad_qkv = jnp.stack([product_tn(normed_all, grad_part) for grad_part in grad_parts])
    grad_normed_part = (
        product_nt(grad_parts[0], qkv_w[0])
        + product_nt(grad_parts[1], qkv_w[1])
        + product_nt(grad_parts[2], qkv_w[2])
    )
    grad_normed = combine_grads(grad_normed_part)
    _, norm_back_in = jax.vjp(layer_norm, resid_in, gains[0], biases[0])
    grad_in_ln, grad_gain_in, grad_bias_in = norm_back_in(grad_normed)
    gain_grads = jnp.stack([grad_gain_in, grad_gain_mid])
    bias_grads = jnp.stack([grad_bias_in, grad_bias_mid])
    return (
        grad_middle + grad_in_ln,
        gain_grads,
        bias_grads,
        (grad_qkv, grad_attn, grad_up, grad_down),
    )


def local(
    tokens,
    segment_ids,
    norm_gains,
    norm_biases,
    w_qkv,
    w_attn_out,
    w_up,
    w_down,
    w_vq_in,
    w_vq_out,
    codebook,
    cotangent,
):
    gain_sum = jnp.zeros(norm_gains.shape, jnp.float32)
    bias_sum = jnp.zeros(norm_biases.shape, jnp.float32)
    vq_in_sum = jnp.zeros(w_vq_in.shape, jnp.float32)
    vq_out_sum = jnp.zeros(w_vq_out.shape, jnp.float32)
    code_sum = jnp.zeros(codebook.shape, jnp.float32)
    layer_sums = [None, None]
    outputs = []
    input_grads = []
    for micro in range(MICRO):
        resid_in = tokens[micro].astype(jnp.float32)
        seg_local = segment_ids[micro]
        enc_weights = fetch_weights(w_qkv, w_attn_out, w_up, w_down, 0)
        encoded, enc_kept = block_forward(
            resid_in, seg_local, norm_gains[0:2], norm_biases[0:2], enc_weights
        )
        (decoder_in, _), vq_back = jax.vjp(
            quantize, encoded, norm_gains[2], norm_biases[2], w_vq_in, w_vq_out, codebook
        )
        dec_weights = fetch_weights(w_qkv, w_attn_out, w_up, w_down, 1)
        decoded, dec_kept = block_forward(
            decoder_in, seg_local, norm_gains[3:5], norm_biases[3:5], dec_weights
        )
        outputs.append(decoded)
        grad_dec_in, gains_dec, biases_dec, grads_dec = block_backward(
            dec_kept, norm_gains[3:5], norm_biases[3:5], dec_weights, cotangent[micro]
        )
        grad_encoded, grad_gain_vq, grad_bias_vq, grad_in_w, grad_out_w, grad_codes = vq_back(
            (grad_dec_in, jnp.ones((), jnp.float32))
        )
        grad_input, gains_enc, biases_enc, grads_enc = block_backward(
            enc_kept, norm_gains[0:2], norm_biases[0:2], enc_weights, grad_encoded
        )
        input_grads.append(grad_input)
        gain_sum = gain_sum + jnp.concatenate([gains_enc, grad_gain_vq[None], gains_dec], axis=0)
        bias_sum = bias_sum + jnp.concatenate([biases_enc, grad_bias_vq[None], biases_dec], axis=0)
        vq_in_sum = vq_in_sum + grad_in_w
        vq_out_sum = vq_out_sum + grad_out_w
        code_sum = code_sum + grad_codes
        for layer, grads in ((0, grads_enc), (1, grads_dec)):
            reduced = reduce_weight_grads(grads)
            if layer_sums[layer] is None:
                layer_sums[layer] = reduced
            else:
                layer_sums[layer] = jax.tree.map(jnp.add, layer_sums[layer], reduced)
    gain_tot, bias_tot, vq_in_tot, vq_out_tot, code_tot = lax.psum(
        (gain_sum, bias_sum, vq_in_sum, vq_out_sum, code_sum), ("dp", "tp")
    )
    return (
        jnp.stack(outputs),
        jnp.stack(input_grads),
        gain_tot,
        bias_tot[0:3],
        bias_tot[3:5],
        jnp.stack([layer_sums[0][0], layer_sums[1][0]]),
        jnp.stack([layer_sums[0][1], layer_sums[1][1]]),
        jnp.stack([layer_sums[0][2], layer_sums[1][2]]),
        jnp.stack([layer_sums[0][3], layer_sums[1][3]]),
        vq_in_tot,
        vq_out_tot,
        code_tot,
    )


def solution(mesh):
    n_dp, n_tp = mesh.shape["dp"], mesh.shape["tp"]
    fits = n_tp == MICRO and n_dp == 16
    return jax.shard_map(
        functools.partial(whole_groups, n_dp) if fits else local,
        mesh=mesh,
        in_specs=(
            P(None, ("dp", "tp"), None),
            P(None, ("dp", "tp")),
            P(),
            P(),
            P(None, None, "dp", "tp"),
            P(None, "tp", "dp"),
            P(None, "dp", "tp"),
            P(None, "tp", "dp"),
            P(),
            P(),
            P(),
            P(None, ("dp", "tp"), None),
        ),
        out_specs=(
            P(None, ("dp", "tp"), None),
            P(None, ("dp", "tp"), None),
            P(),
            P(),
            P(),
            P(None, None, "dp", "tp"),
            P(None, "tp", "dp"),
            P(None, "dp", "tp"),
            P(None, "tp", "dp"),
            P(),
            P(),
            P(),
        ),
        check_vma=False,
    )
```
